32 devices in a mesh: dp: 8 (over y, x, core), ctx: 4 (over z).
Axes of the slice: x: 2, y: 2, z: 4, core: 2. Of those that a mesh axis runs over, the one named last changes fastest.
Arguments:
- tokens: bfloat16 [24, 1024, 768], P('dp', 'ctx'), may hold values from -6 to 6
- out_grad: bfloat16 [24, 1024, 768], P('dp', 'ctx'), may hold values from -6 to 6
- block_order: int32 [24, 8], P('dp'), may hold values from 0 to 7, each once within a row
- qkv_weight: float32 [768, 2304], P('ctx'), may hold values from -0.21875 to 0.21875
- out_weight: float32 [768, 768], P('ctx'), may hold values from -3 to 3
- up_weight: float32 [768, 3072], P('ctx'), may hold values from -0.21875 to 0.21875
- down_weight: float32 [3072, 768], P('ctx'), may hold values from -0.109375 to 0.109375
- norm_params: float32 [4, 768], P(None, 'ctx'), may hold values from -0.6 to 1.3
- bias_params: float32 [5376], P('ctx'), may hold values from -1 to 1
- qkv_first: float32 [768, 2304], P('ctx'), may hold values from -112 to 112
- qkv_second: float32 [768, 2304], P('ctx'), may hold values from 646.7368 to 10347.789
- out_first: float32 [768, 768], P('ctx'), may hold values from -7 to 7
- out_second: float32 [768, 768], P('ctx'), may hold values from 3.1578948 to 50.526318
- up_first: float32 [768, 3072], P('ctx'), may hold values from -32 to 32
- up_second: float32 [768, 3072], P('ctx'), may hold values from 71.14105 to 1138.2568
- down_first: float32 [3072, 768], P('ctx'), may hold values from -64 to 64
- down_second: float32 [3072, 768], P('ctx'), may hold values from 271.6295 to 4397.8105
- norm_first: float32 [4, 768], P(None, 'ctx'), may hold values from -119.14318 to 119.14318
- norm_second: float32 [4, 768], P(None, 'ctx'), may hold values from 270.336 to 29982.72
- bias_first: float32 [5376], P('ctx'), may hold values from -70.5453 to 70.5453
- bias_second: float32 [5376], P('ctx'), may hold values from 68.8128 to 10567.68
Outputs:
- layer_out: bfloat16 [24, 1024, 768], P('dp', 'ctx')
- input_grad: float32 [24, 1024, 768], P('dp', 'ctx')
- qkv_first_new: float32 [768, 2304], P('ctx')
- qkv_second_new: float32 [768, 2304], P('ctx')
- qkv_weight_new: float32 [768, 2304], P('ctx')
- out_first_new: float32 [768, 768], P('ctx')
- out_second_new: float32 [768, 768], P('ctx')
- out_weight_new: float32 [768, 768], P('ctx')
- up_first_new: float32 [768, 3072], P('ctx')
- up_second_new: float32 [768, 3072], P('ctx')
- up_weight_new: float32 [768, 3072], P('ctx')
- down_first_new: float32 [3072, 768], P('ctx')
- down_second_new: float32 [3072, 768], P('ctx')
- down_weight_new: float32 [3072, 768], P('ctx')
- norm_first_new: float32 [4, 768], P(None, 'ctx')
- norm_second_new: float32 [2, 768], P(None, 'ctx')
- feed_norm_second_new: float32 [2, 768], P(None, 'ctx')
- norm_params_new: float32 [4, 768], P(None, 'ctx')
- bias_first_new: float32 [5376], P('ctx')
- bias_second_new: float32 [5376], P('ctx')
- bias_params_new: float32 [5376], P('ctx')
The draws below stay inside these ranges and needn't reach their ends.
Inputs may be any that keep to these rules, and one draw needn't show every extreme that they name: `block_order`: each row holds every number below 8 once.
All inputs are finite; a program needn't handle non-finite values.
Results may differ from the reference program's by a relative error of at most 0.015.
Values may be sent and summed in bfloat16 or wider, within the bound.
A program may use at most 768 MiB of HBM per device.

```python
import math
import jax
import jax.numpy as jnp
from jax import lax

D = 768
HEADS = 12
HD = 64
FF = 3072
SEQS = 3
STEP = 10
ROT = 16
LEN = 1024
BLOCK = 128
BLOCKS = 8
BATCH = 24
ALL_TOK = 24576
QKV = 2304
BIAS = 5376


def norm_levels():
    return jnp.array([1.7, 1.7, 0.66, 0.66], jnp.float32)[:, None] * math.sqrt(ALL_TOK)


def bias_levels():
    place = jnp.arange(BIAS)
    up_part = (place >= 2 * D) & (place < 2 * D + FF)
    return jnp.where(up_part, 0.33, 1.0).astype(jnp.float32) * math.sqrt(ALL_TOK)


def first_moment(key, levels, shape):
    noise = jnp.clip(jax.random.normal(key, shape, jnp.float32), -4.0, 4.0)
    return noise * levels / 9.0


def second_moment(key, levels, shape):
    factor = jnp.exp(jax.random.uniform(key, shape, jnp.float32, math.log(0.5), math.log(8.0)))
    return factor * levels * levels / 19.0


def draw_norm_params(key, part):
    key = jax.random.fold_in(key, 1)
    noise = jnp.clip(jax.random.normal(key, (4, D), jnp.float32), -3.0, 3.0)
    spread = jnp.array([0.1, 0.2, 0.1, 0.2], jnp.float32)[:, None]
    centre = jnp.array([1.0, 0.0, 1.0, 0.0], jnp.float32)[:, None]
    return centre + spread * noise


def draw_norm_first(key, part):
    key = jax.random.fold_in(key, 2)
    return first_moment(key, norm_levels(), (4, D))


def draw_norm_second(key, part):
    key = jax.random.fold_in(key, 3)
    return second_moment(key, norm_levels(), (4, D))


def draw_bias_first(key, part):
    key = jax.random.fold_in(key, 4)
    return first_moment(key, bias_levels(), (BIAS,))


def draw_bias_second(key, part):
    key = jax.random.fold_in(key, 5)
    return second_moment(key, bias_levels(), (BIAS,))


def steps_of(key, dims, shards, smallest, high):
    level, own = 1.0, jax.random.fold_in(key, 6)
    for axis_at, shards_of in shards:
        draws = jnp.exp(jax.random.uniform(jax.random.fold_in(own, axis_at), (shards_of,), jnp.float32, smallest / len(shards), high / len(shards)))
        level = level * jnp.repeat(draws, dims[axis_at] // shards_of).reshape([-1 if axis == axis_at else 1 for axis in range(len(dims))])
    return level


def bell_draw(own_key, dims, width, bound, pieces=(), held_as=jnp.bfloat16):
    values = width * jax.random.normal(own_key, dims, jnp.float32)
    if pieces:
        values = values * steps_of(own_key, dims, pieces, -0.22, 0.18)
    return jnp.clip(values, -bound, bound).astype(held_as)


def setup_inputs(seed: int = 0) -> dict:
    key_list = jax.random.split(jax.random.key(seed), 22)
    return {
        "tokens": bell_draw(key_list[0], (BATCH, LEN, D), 1.0, 6.0, ((0, 8), (1, 4))),
        "out_grad": bell_draw(key_list[1], (BATCH, LEN, D), 1.0, 6.0, ((0, 8), (1, 4))),
        "block_order": jax.vmap(lambda own: jax.random.permutation(own, BLOCKS))(jax.random.split(key_list[2], BATCH)).reshape((BATCH, BLOCKS)).astype(jnp.int32),
        "qkv_weight": bell_draw(key_list[3], (D, QKV), D ** -0.5, 0.21875, ((0, 4),), jnp.float32),
        "out_weight": bell_draw(key_list[4], (D, D), (max(11 * D // (2 * LEN), 1)) ** -0.5, 3.0, ((0, 4),), jnp.float32),
        "up_weight": bell_draw(key_list[5], (D, FF), D ** -0.5, 0.21875, ((0, 4),), jnp.float32),
        "down_weight": bell_draw(key_list[6], (FF, D), FF ** -0.5, 0.109375, ((0, 4),), jnp.float32),
        "norm_params": draw_norm_params(jax.random.fold_in(key_list[21], 71), 0),
        "bias_params": bell_draw(key_list[8], (BIAS,), 0.2, 1.0, ((0, 4),), jnp.float32),
        "qkv_first": bell_draw(key_list[9], (D, QKV), (ALL_TOK ** 0.5 / 9), 112.0, ((0, 4),), jnp.float32),
        "qkv_second": jnp.clip(jnp.exp(math.log(10347.789) - 2.7725887 * jax.random.uniform(key_list[10], (D, QKV), jnp.float32) ** steps_of(key_list[10], (D, QKV), ((0, 4),), -0.2, 0.2)), 646.7368, 10347.789),
        "out_first": bell_draw(key_list[11], (D, D), ((5 * BATCH) ** 0.5 / 9), 7.0, ((0, 4),), jnp.float32),
        "out_second": jnp.clip(jnp.exp(math.log(50.526318) - 2.7725887 * jax.random.uniform(key_list[12], (D, D), jnp.float32) ** steps_of(key_list[12], (D, D), ((0, 4),), -0.2, 0.2)), 3.1578948, 50.526318),
        "up_first": bell_draw(key_list[13], (D, FF), (0.33 * ALL_TOK ** 0.5 / 9), 32.0, ((0, 4),), jnp.float32),
        "up_second": jnp.clip(jnp.exp(math.log(1138.2568) - 2.7725887 * jax.random.uniform(key_list[14], (D, FF), jnp.float32) ** steps_of(key_list[14], (D, FF), ((0, 4),), -0.2, 0.2)), 71.14105, 1138.2568),
        "down_first": bell_draw(key_list[15], (FF, D), (0.65 * ALL_TOK ** 0.5 / 9), 64.0, ((0, 4),), jnp.float32),
        "down_second": jnp.clip(jnp.exp(math.log(4397.8105) - 2.784423 * jax.random.uniform(key_list[16], (FF, D), jnp.float32) ** steps_of(key_list[16], (FF, D), ((0, 4),), -0.2, 0.2)), 271.6295, 4397.8105),
        "norm_first": draw_norm_first(jax.random.fold_in(key_list[21], 71), 0),
        "norm_second": draw_norm_second(jax.random.fold_in(key_list[21], 71), 0),
        "bias_first": draw_bias_first(jax.random.fold_in(key_list[21], 71), 0),
        "bias_second": draw_bias_second(jax.random.fold_in(key_list[21], 71), 0),
    }


@jax.custom_vjp
def low(v):
    return lax.optimization_barrier(v.astype(jnp.bfloat16)).astype(jnp.float32)

@jax.custom_vjp
def low_back(v):
    return v

def low_keep(v):
    return (low(v), None)

def low_pass(kept, grad):
    return (grad,)

def back_keep(v):
    return (v, None)

def back_low(kept, grad):
    return (low(grad),)
low.defvjp(low_keep, low_pass)
low_back.defvjp(back_keep, back_low)
EPS_NORM = 1e-05
BETA_ONE = 0.9
BETA_TWO = 0.95
EPS_ADAM = 1e-08
DECAY = 0.01
ROPE_BASE = 10000.0
HIGHEST = lax.Precision.HIGHEST

def multiply(left, right):
    return jnp.dot(left, right, precision=HIGHEST)

def layer_norm(values, gain, shift):
    mean = lax.optimization_barrier(jnp.mean(values, axis=-1, keepdims=True))
    centred = values - mean
    variance = lax.optimization_barrier(jnp.mean(centred * centred, axis=-1, keepdims=True))
    return centred * lax.rsqrt(variance + EPS_NORM) * gain + shift

def rotary_tables(positions):
    half = ROT // 2
    frequency = ROPE_BASE ** (-(jnp.arange(half, dtype=jnp.float32) * 2.0 / ROT))
    angle = positions.astype(jnp.float32)[:, None] * frequency[None, :]
    return (jnp.cos(angle), jnp.sin(angle))

def rotate(values, cosine, sine):
    half = ROT // 2
    first = values[..., :half]
    second = values[..., half:ROT]
    rest = values[..., ROT:]
    cos_b = cosine[:, None, :]
    sin_b = sine[:, None, :]
    return jnp.concatenate([first * cos_b - second * sin_b, second * cos_b + first * sin_b, rest], axis=-1)

def seq_positions(order):
    place = jnp.arange(LEN, dtype=jnp.int32)
    return jnp.repeat(order, BLOCK, axis=1) * BLOCK + place % BLOCK

def attend(items):
    query, keys, values, query_pos, key_pos = items
    scores = jnp.einsum('qgd,kgd->gqk', query, keys, precision=HIGHEST) * (1.0 / math.sqrt(HD))
    scores = low_back(scores)
    admitted = key_pos[None, None, :] <= query_pos[None, :, None]
    scores = jnp.where(admitted, scores, -1e+30)
    top = lax.optimization_barrier(jnp.max(scores, axis=-1, keepdims=True))
    expo = jnp.exp(scores - top)
    probs = expo / lax.optimization_barrier(jnp.sum(expo, axis=-1, keepdims=True))
    return jnp.einsum('gqk,kgd->qgd', low(probs), values, precision=HIGHEST)

def to_blocks(values):
    grouped = values.reshape(SEQS, LEN, HEADS // 2, 2, HD).transpose(0, 2, 1, 3, 4)
    return grouped.reshape(SEQS * (HEADS // 2), LEN, 2, HD)

def from_blocks(values):
    grouped = values.reshape(SEQS, HEADS // 2, LEN, 2, HD).transpose(0, 2, 1, 3, 4)
    return grouped.reshape(SEQS * LEN, D)

def layer(inputs, order, qkv_matrix, out_matrix, up_matrix, down_matrix, norms, biases):
    rows = inputs.reshape(SEQS * LEN, D)
    first = low(layer_norm(rows, norms[0], norms[1]))
    second = low(layer_norm(rows, norms[2], norms[3]))
    projected = multiply(first, qkv_matrix)
    query_pre = projected[:, :D] + biases[:D]
    key_pre = projected[:, D:2 * D]
    value_pre = projected[:, 2 * D:]
    positions = seq_positions(order)
    cosine, sine = rotary_tables(positions.reshape(SEQS * LEN))
    query = low(rotate(low_back(query_pre).reshape(SEQS * LEN, HEADS, HD), cosine, sine))
    keys = low(rotate(low_back(key_pre).reshape(SEQS * LEN, HEADS, HD), cosine, sine))
    values = low(low_back(value_pre)).reshape(SEQS * LEN, HEADS, HD)
    pos_blocks = jnp.repeat(positions, HEADS // 2, axis=0)
    mixed = lax.map(jax.checkpoint(attend), (to_blocks(query), to_blocks(keys), to_blocks(values), pos_blocks, pos_blocks))
    heads_out = low(low_back(from_blocks(mixed)))
    attend_out = multiply(heads_out, out_matrix) + biases[D:2 * D]
    up_value = low_back(multiply(second, up_matrix) + biases[2 * D:2 * D + FF])
    hidden = low(jax.nn.gelu(up_value, approximate=False))
    feed_out = multiply(hidden, down_matrix) + biases[2 * D + FF:]
    return (rows + attend_out + feed_out).reshape(SEQS, LEN, D)

def adamw(weight, grad, first, second, rate, decay):
    first_new = BETA_ONE * first + (1.0 - BETA_ONE) * grad
    second_new = BETA_TWO * second + (1.0 - BETA_TWO) * grad * grad
    first_hat = first_new / (1.0 - BETA_ONE ** STEP)
    second_hat = second_new / (1.0 - BETA_TWO ** STEP)
    weight_new = weight - rate * (first_hat / (jnp.sqrt(second_hat) + EPS_ADAM) + decay * weight)
    return (first_new, second_new, weight_new)

def copy_low(values):
    return lax.optimization_barrier(values.astype(jnp.bfloat16)).astype(jnp.float32)

def reference(tokens, out_grad, block_order, qkv_weight, out_weight, up_weight, down_weight, norm_params, bias_params, qkv_first, qkv_second, out_first, out_second, up_first, up_second, down_first, down_second, norm_first, norm_second, bias_first, bias_second):
    params = (copy_low(qkv_weight), copy_low(out_weight), copy_low(up_weight), copy_low(down_weight), copy_low(norm_params), copy_low(bias_params))
    groups = BATCH // SEQS
    inputs = tokens.reshape(groups, SEQS, LEN, D)
    cotangents = out_grad.reshape(groups, SEQS, LEN, D)
    orders = block_order.reshape(groups, SEQS, BLOCKS)
    zeros = tuple((jnp.zeros(p.shape, jnp.float32) for p in params))

    def group_step(totals, item):
        group_in, group_cot, group_order = item

        def forward(x_in, qkv_matrix, out_matrix, up_matrix, down_matrix, norms, biases):
            return layer(x_in, group_order, qkv_matrix, out_matrix, up_matrix, down_matrix, norms, biases)
        result, pullback = jax.vjp(forward, group_in.astype(jnp.float32), params[0], params[1], params[2], params[3], params[4], params[5])
        grads = pullback(group_cot.astype(jnp.float32))
        totals = tuple((t + g for t, g in zip(totals, grads[1:])))
        return (totals, (result.astype(jnp.bfloat16), grads[0]))
    totals, (outputs, input_grads) = lax.scan(group_step, zeros, (inputs, cotangents, orders))
    layer_out = outputs.reshape(BATCH, LEN, D)
    input_grad = input_grads.reshape(BATCH, LEN, D)
    qkv_new = adamw(qkv_weight, totals[0], qkv_first, qkv_second, 0.1, DECAY)
    out_new = adamw(out_weight, totals[1], out_first, out_second, 0.6, DECAY)
    up_new = adamw(up_weight, totals[2], up_first, up_second, 0.1, DECAY)
    down_new = adamw(down_weight, totals[3], down_first, down_second, 0.05, DECAY)
    norm_new = adamw(norm_params, totals[4], norm_first, norm_second, 0.6, 0.0)
    bias_new = adamw(bias_params, totals[5], bias_first, bias_second, 0.6, 0.0)
    return (layer_out, input_grad, qkv_new[0], qkv_new[1], qkv_new[2], out_new[0], out_new[1], out_new[2], up_new[0], up_new[1], up_new[2], down_new[0], down_new[1], down_new[2], norm_new[0], norm_new[1][:2], norm_new[1][2:], norm_new[2], bias_new[0], bias_new[1], bias_new[2])
```

```python
import functools
import math

import jax
import jax.numpy as jnp
from jax import lax
from jax.experimental import pallas as pl
from jax.experimental.pallas import tpu as pltpu
from jax.sharding import PartitionSpec as P

HEADS = 12
HD = 64
STEP = 10
ROT = 16
BLOCK = 128
QUAD = 4

EPS_NORM = 1e-05
BETA_ONE = 0.9
BETA_TWO = 0.95
EPS_ADAM = 1e-08
DECAY = 0.01
ROPE_BASE = 10000.0
F32 = jnp.float32
BF16 = jnp.bfloat16
MIB = 1024 * 1024


def dot(left, right, dims=((1,), (0,))):
    return lax.dot_general(left, right, (dims, ((), ())), preferred_element_type=F32)


NN = ((1,), (0,))
NT = ((1,), (1,))
TN = ((0,), (0,))


def normalized(values):
    mean = jnp.mean(values, axis=-1, keepdims=True)
    centred = values - mean
    variance = jnp.mean(centred * centred, axis=-1, keepdims=True)
    scale = lax.rsqrt(variance + EPS_NORM)
    return centred * scale, scale


def feed_kernel(
    x_ref, g_ref, norm_ref, bias_ref, up_ref, down_ref,
    out_ref, h_ref, dup_ref, ddown_ref, dbias_ref, small_ref,
    m_ref, hid_ref, dup_in_ref, acc_ref, dm_ref,
):
    step = pl.program_id(0)
    last = pl.num_programs(0) - 1
    rows, width = x_ref.shape
    tile = 256
    tiles = rows // tile

    @pl.when(step == 0)
    def _():
        for t in range(tiles):
            at = pl.ds(t * tile, tile)
            xh, _ = normalized(x_ref[at, :].astype(F32))
            m_ref[at, :] = (xh * norm_ref[2:3, :] + norm_ref[3:4, :]).astype(BF16)
        acc_ref[...] = jnp.zeros_like(acc_ref)
        dm_ref[...] = jnp.zeros_like(dm_ref)

    up = up_ref[...]
    down = down_ref[...]
    total = jnp.zeros(dbias_ref.shape, F32)
    for t in range(tiles):
        at = pl.ds(t * tile, tile)
        u = dot(m_ref[at, :], up) + bias_ref[...]
        cdf = 0.5 * (1.0 + lax.erf(u * (1.0 / math.sqrt(2.0))))
        hidden = (u * cdf).astype(BF16)
        slope = cdf + u * jnp.exp(-0.5 * u * u) * (1.0 / math.sqrt(2.0 * math.pi))
        back = (dot(g_ref[at, :], down, NT) * slope).astype(BF16)
        hid_ref[at, :] = hidden
        dup_in_ref[at, :] = back
        total += jnp.sum(back.astype(F32), axis=0, keepdims=True)
        acc_ref[at, :] += dot(hidden, down)
        dm_ref[at, :] += dot(back, up, NT)
    dbias_ref[...] = total
    ddown_ref[...] = dot(hid_ref[...], g_ref[...], TN).astype(BF16)
    dup_ref[...] = dot(m_ref[...], dup_in_ref[...], TN).astype(BF16)

    @pl.when(step == last)
    def _():
        gain = jnp.zeros((1, width), F32)
        shift = jnp.zeros((1, width), F32)
        sums = jnp.zeros((1, width), F32)
        for t in range(tiles):
            at = pl.ds(t * tile, tile)
            xh, _ = normalized(x_ref[at, :].astype(F32))
            dm = dm_ref[at, :]
            gain += jnp.sum(dm * xh, axis=0, keepdims=True)
            shift += jnp.sum(dm, axis=0, keepdims=True)
            sums += jnp.sum(g_ref[at, :].astype(F32), axis=0, keepdims=True)
            h_ref[at, :] = dm * norm_ref[2:3, :]
            out_ref[at, :] = acc_ref[at, :]
        small_ref[0:1, :] = gain
        small_ref[1:2, :] = shift
        small_ref[2:3, :] = sums


def feed(x, g, norms, bias_up, up, down):
    rows, width = x.shape
    ff = up.shape[1]
    chunk = 512
    whole = lambda shape: pl.BlockSpec(shape, lambda i: (0,) * len(shape))
    return pl.pallas_call(
        feed_kernel,
        grid=(ff // chunk,),
        in_specs=[
            whole((rows, width)),
            whole((rows, width)),
            whole(norms.shape),
            pl.BlockSpec((1, chunk), lambda i: (0, i)),
            pl.BlockSpec((width, chunk), lambda i: (0, i)),
            pl.BlockSpec((chunk, width), lambda i: (i, 0)),
        ],
        out_specs=[
            whole((rows, width)),
            whole((rows, width)),
            pl.BlockSpec((width, chunk), lambda i: (0, i)),
            pl.BlockSpec((chunk, width), lambda i: (i, 0)),
            pl.BlockSpec((1, chunk), lambda i: (0, i)),
            whole((8, width)),
        ],
        out_shape=[
            jax.ShapeDtypeStruct((rows, width), F32),
            jax.ShapeDtypeStruct((rows, width), F32),
            jax.ShapeDtypeStruct((width, ff), BF16),
            jax.ShapeDtypeStruct((ff, width), BF16),
            jax.ShapeDtypeStruct((1, ff), F32),
            jax.ShapeDtypeStruct((8, width), F32),
        ],
        scratch_shapes=[
            pltpu.VMEM((rows, width), BF16),
            pltpu.VMEM((rows, chunk), BF16),
            pltpu.VMEM((rows, chunk), BF16),
            pltpu.VMEM((rows, width), F32),
            pltpu.VMEM((rows, width), F32),
        ],
        compiler_params=pltpu.CompilerParams(vmem_limit_bytes=56 * MIB),
        cost_estimate=pl.CostEstimate(
            flops=12 * rows * width * ff, bytes_accessed=8 * width * ff, transcendentals=rows * ff
        ),
        name="feed",
    )(x, g, norms, bias_up, up, down)


def attend_kernel(
    x_ref, g_ref, norm_ref, bias_ref, cos_ref, low_ref, high_ref, wq_ref, wk_ref, wv_ref, wo_ref,
    out_ref, h_ref, dq_ref, dk_ref, dv_ref, dwo_ref, dbias_ref, small_ref,
    a_ref, acc_ref, da_ref, q_ref, k_ref, v_ref, do_ref, o_ref, dqs_ref, dks_ref, dvs_ref,
):
    step = pl.program_id(0)
    last = pl.num_programs(0) - 1
    rows, width = x_ref.shape
    lanes = QUAD * HD
    tile = 256
    half = ROT // 2
    scale = 1.0 / math.sqrt(HD)

    @pl.when(step == 0)
    def _():
        for t in range(rows // tile):
            at = pl.ds(t * tile, tile)
            xh, _ = normalized(x_ref[at, :].astype(F32))
            a_ref[at, :] = (xh * norm_ref[0:1, :] + norm_ref[1:2, :]).astype(BF16)
        acc_ref[...] = jnp.zeros_like(acc_ref)
        da_ref[...] = jnp.zeros_like(da_ref)

    def turn(values, at):
        low = pltpu.roll(values, lanes - half, 1) * low_ref[at, :]
        high = pltpu.roll(values, half, 1) * high_ref[at, :]
        return values * cos_ref[at, :], low + high

    for t in range(rows // tile):
        at = pl.ds(t * tile, tile)
        a = a_ref[at, :]
        same, cross = turn(dot(a, wq_ref[...]) + bias_ref[...], at)
        q_ref[at, :] = ((same + cross).astype(BF16) * scale).astype(BF16)
        same, cross = turn(dot(a, wk_ref[...]), at)
        k_ref[at, :] = (same + cross).astype(BF16)
        v_ref[at, :] = dot(a, wv_ref[...]).astype(BF16)
        do_ref[at, :] = dot(g_ref[at, :], wo_ref[...], NT).astype(BF16)

    dks_ref[...] = jnp.zeros_like(dks_ref)
    dvs_ref[...] = jnp.zeros_like(dvs_ref)
    head_of = lax.broadcasted_iota(jnp.int32, (BLOCK, lanes), 1) // HD

    def stack(values):
        zero = jnp.zeros_like(values)
        return jnp.concatenate([jnp.where(head_of == e, values, zero) for e in range(QUAD)], axis=0)

    def merge(values):
        out = values[:BLOCK]
        for e in range(1, QUAD):
            out = jnp.where(head_of == e, values[e * BLOCK : (e + 1) * BLOCK], out)
        return out

    spot = lax.broadcasted_iota(jnp.int32, (QUAD * BLOCK, BLOCK), 0) % BLOCK
    admitted = lax.broadcasted_iota(jnp.int32, (QUAD * BLOCK, BLOCK), 1) <= spot
    for b in range(rows // BLOCK):
        at = pl.ds(b * BLOCK, BLOCK)
        seen = pl.ds(0, (b + 1) * BLOCK)
        q = stack(q_ref[at, :])
        do_block = do_ref[at, :]
        do = stack(do_block)
        keys = k_ref[seen, :]
        values = v_ref[seen, :]
        scores = dot(q, keys, NT)
        edge = jnp.where(admitted, scores[:, b * BLOCK :], -1e30)
        scores = edge if b == 0 else jnp.concatenate([scores[:, : b * BLOCK], edge], axis=1)
        top = jnp.max(scores, axis=-1, keepdims=True)
        expo = jnp.exp(scores - top)
        probs = expo * (1.0 / jnp.sum(expo, axis=-1, keepdims=True))
        low = probs.astype(BF16)
        mixed = dot(low, values)
        o_ref[at, :] = merge(mixed).astype(BF16)
        share = jnp.sum(mixed * do.astype(F32), axis=-1, keepdims=True)
        back = (probs * (dot(do, values, NT) - share)).astype(BF16)
        dqs_ref[at, :] = merge(dot(back, keys)) * scale
        dks_ref[seen, :] += dot(back, q, TN)
        dvs_ref[seen, :] += dot(low, do, TN)

    total = jnp.zeros((1, lanes), F32)
    for t in range(rows // tile):
        at = pl.ds(t * tile, tile)
        same, cross = turn(dqs_ref[at, :], at)
        dq = (same - cross).astype(BF16)
        same, cross = turn(dks_ref[at, :], at)
        dk = (same - cross).astype(BF16)
        dv = dvs_ref[at, :].astype(BF16)
        total += jnp.sum(dq.astype(F32), axis=0, keepdims=True)
        q_ref[at, :] = dq
        k_ref[at, :] = dk
        v_ref[at, :] = dv
        acc_ref[at, :] += dot(o_ref[at, :], wo_ref[...])
        da_ref[at, :] += dot(dq, wq_ref[...], NT) + dot(dk, wk_ref[...], NT) + dot(dv, wv_ref[...], NT)
    dbias_ref[...] = total
    dwo_ref[...] = dot(o_ref[...], g_ref[...], TN).astype(BF16)
    dq_ref[...] = dot(a_ref[...], q_ref[...], TN).astype(BF16)
    dk_ref[...] = dot(a_ref[...], k_ref[...], TN).astype(BF16)
    dv_ref[...] = dot(a_ref[...], v_ref[...], TN).astype(BF16)

    @pl.when(step == last)
    def _():
        gain = jnp.zeros((1, width), F32)
        shift = jnp.zeros((1, width), F32)
        for t in range(rows // tile):
            at = pl.ds(t * tile, tile)
            xh, _ = normalized(x_ref[at, :].astype(F32))
            da = da_ref[at, :]
            gain += jnp.sum(da * xh, axis=0, keepdims=True)
            shift += jnp.sum(da, axis=0, keepdims=True)
            h_ref[at, :] = (da * norm_ref[0:1, :]).astype(BF16)
            out_ref[at, :] = acc_ref[at, :].astype(BF16)
        small_ref[0:1, :] = gain
        small_ref[1:2, :] = shift


def attend(x, g, norms, bias_q, tables, qkv, out_w):
    rows, width = x.shape
    lanes = QUAD * HD
    groups = width // lanes
    whole = lambda shape: pl.BlockSpec(shape, lambda i: (0,) * len(shape))
    column = pl.BlockSpec((width, lanes), lambda i: (0, i))
    small = jax.ShapeDtypeStruct((rows, width), BF16)
    return pl.pallas_call(
        attend_kernel,
        grid=(groups,),
        in_specs=[
            whole((rows, width)),
            whole((rows, width)),
            whole(norms.shape),
            pl.BlockSpec((1, lanes), lambda i: (0, i)),
            whole((rows, lanes)),
            whole((rows, lanes)),
            whole((rows, lanes)),
            pl.BlockSpec((width, lanes), lambda i: (0, i)),
            pl.BlockSpec((width, lanes), lambda i: (0, groups + i)),
            pl.BlockSpec((width, lanes), lambda i: (0, 2 * groups + i)),
            pl.BlockSpec((lanes, width), lambda i: (i, 0)),
        ],
        out_specs=[
            whole((rows, width)),
            whole((rows, width)),
            column,
            column,
            column,
            pl.BlockSpec((lanes, width), lambda i: (i, 0)),
            pl.BlockSpec((1, lanes), lambda i: (0, i)),
            whole((8, width)),
        ],
        out_shape=[
            small,
            small,
            jax.ShapeDtypeStruct((width, width), BF16),
            jax.ShapeDtypeStruct((width, width), BF16),
            jax.ShapeDtypeStruct((width, width), BF16),
            jax.ShapeDtypeStruct((width, width), BF16),
            jax.ShapeDtypeStruct((1, width), F32),
            jax.ShapeDtypeStruct((8, width), F32),
        ],
        scratch_shapes=[
            pltpu.VMEM((rows, width), BF16),
            pltpu.VMEM((rows, width), F32),
            pltpu.VMEM((rows, width), F32),
        ]
        + [pltpu.VMEM((rows, lanes), BF16)] * 5
        + [pltpu.VMEM((rows, lanes), F32)] * 3,
        compiler_params=pltpu.CompilerParams(vmem_limit_bytes=56 * MIB),
        cost_estimate=pl.CostEstimate(
            flops=24 * rows * width * width + 8 * rows * rows * width,
            bytes_accessed=16 * width * width + 8 * rows * width,
            transcendentals=HEADS * rows * rows // 2,
        ),
        name="attend",
    )(x, g, norms, bias_q, *tables, qkv, qkv, qkv, out_w)


def rotary_tables(length):
    half = ROT // 2
    frequency = ROPE_BASE ** (-(jnp.arange(half, dtype=F32) * 2.0 / ROT))
    angle = jnp.arange(length, dtype=F32)[:, None] * frequency[None, :]
    cosine, sine = jnp.cos(angle), jnp.sin(angle)
    rest = jnp.zeros((length, HD - ROT), F32)
    none = jnp.zeros_like(sine)
    cos_full = jnp.concatenate([cosine, cosine, rest + 1.0], axis=1)
    low = jnp.concatenate([-sine, none, rest], axis=1)
    high = jnp.concatenate([none, sine, rest], axis=1)
    return tuple(jnp.tile(table, (1, QUAD)) for table in (cos_full, low, high))


def adamw(weight, grad, first, second, rate, decay):
    first_new = BETA_ONE * first + (1.0 - BETA_ONE) * grad
    second_new = BETA_TWO * second + (1.0 - BETA_TWO) * grad * grad
    first_hat = first_new / (1.0 - BETA_ONE**STEP)
    second_hat = second_new / (1.0 - BETA_TWO**STEP)
    weight_new = weight - rate * (first_hat / (jnp.sqrt(second_hat) + EPS_ADAM) + decay * weight)
    return (first_new, second_new, weight_new)


def shards(
    tokens, out_grad, block_order, qkv_weight, out_weight, up_weight, down_weight, norm_params, bias_params,
    qkv_first, qkv_second, out_first, out_second, up_first, up_second, down_first, down_second,
    norm_first, norm_second, bias_first, bias_second,
):
    groups, ring = lax.axis_size("dp"), lax.axis_size("ctx")
    group, rank = lax.axis_index("dp"), lax.axis_index("ctx")
    batch, piece, width = tokens.shape
    length = piece * ring
    count = batch * piece
    ff = up_weight.shape[1]

    def gather(values, axis=0):
        return lax.all_gather(values.astype(BF16), "ctx", axis=axis, tiled=True)

    qkv_copy, out_copy, up_copy, down_copy = map(gather, (qkv_weight, out_weight, up_weight, down_weight))
    small = jnp.concatenate([norm_params.reshape(-1), bias_params]).astype(BF16)
    small_all = lax.all_gather(small, "ctx", axis=0, tiled=False).astype(F32)
    norms = small_all[:, : 4 * width // ring].reshape(ring, 4, width // ring).transpose(1, 0, 2).reshape(4, width)
    biases = small_all[:, 4 * width // ring :].reshape(1, -1)

    odd = group % 2
    both = jnp.stack([tokens, out_grad], axis=1)

    def shift_pairs(k):
        pairs = []
        for d in range(groups):
            for r in range(ring):
                if 0 <= (r + k) % ring - d % 2 < batch:
                    pairs.append((d * ring + r, d * ring + (r + k) % ring))
        return pairs

    def piece_for(home):
        return jnp.clip(home - odd, 0, batch - 1)

    mine = rank - odd
    is_home = (mine >= 0) & (mine < batch)
    own = both[piece_for(rank)]
    parts = [jnp.where(is_home, own, jnp.zeros_like(own))]
    for k in range(1, ring):
        send = both[piece_for((rank + k) % ring)]
        parts.append(lax.ppermute(send, ("dp", "ctx"), shift_pairs(k)))
    stored = jnp.stack(parts)[(rank - jnp.arange(ring)) % ring]
    per = piece // BLOCK
    stored = stored.reshape(ring, 2, per, BLOCK, width).transpose(1, 0, 2, 3, 4).reshape(2, ring * per, BLOCK, width)
    order = block_order[piece_for(rank)]
    place = jnp.argsort(order)
    stored = jnp.take(stored, place, axis=1)
    home_x = stored[0].reshape(length, width)
    home_g = stored[1].reshape(length, width)

    x_rows, g_rows = tokens.reshape(count, width), out_grad.reshape(count, width)
    feed_out, h_feed, dup, ddown, dbias_up, small_feed = feed(
        x_rows, g_rows, norms, biases[:, 2 * width : 2 * width + ff], up_copy, down_copy
    )
    attend_out, h_attend, dq, dk, dv, dout, dbias_q, small_attend = attend(
        home_x, home_g, norms, biases[:, :width], rotary_tables(length), qkv_copy, out_copy
    )

    results = jnp.stack([attend_out, h_attend]).reshape(2, ring * per, BLOCK, width)
    results = jnp.take(results, order, axis=1).reshape(2, ring, per * BLOCK, width)
    kept = [results[:, rank]]
    for k in range(1, ring):
        send = results[:, (rank - k) % ring]
        kept.append(lax.ppermute(send, ("dp", "ctx"), [(b, a) for a, b in shift_pairs(k)]))
    returned = jnp.stack(kept)[(jnp.arange(batch) + odd - rank) % ring]
    returned = returned.transpose(1, 0, 2, 3).reshape(2, count, width).astype(F32)

    rows = x_rows.astype(F32)
    bias_rows = biases[:, width : 2 * width] + biases[:, 2 * width + ff :]
    layer_out = (rows + returned[0] + feed_out + bias_rows).astype(BF16).reshape(batch, piece, width)
    xh, scale = normalized(rows)
    h = returned[1] + h_feed
    inner = jnp.mean(h * xh, axis=-1, keepdims=True)
    input_grad = g_rows.astype(F32) + scale * (h - jnp.mean(h, axis=-1, keepdims=True) - xh * inner)
    input_grad = input_grad.reshape(batch, piece, width)

    def reduce(grad):
        part = lax.psum_scatter(grad.reshape(ring, -1, grad.shape[1]), "dp", scatter_dimension=1, tiled=True)
        part = lax.psum_scatter(part, "ctx", scatter_dimension=0, tiled=False)
        return lax.all_gather(part, "dp", axis=0, tiled=True).astype(F32)

    dqkv = jnp.concatenate([dq, dk, dv], axis=1)
    owned = tuple(map(reduce, (dqkv, dout, dup, ddown)))
    tail = jnp.concatenate(
        [small_attend[:2].reshape(-1), small_feed[:2].reshape(-1), dbias_q[0], small_feed[2], dbias_up[0], small_feed[2]]
    )
    tail = lax.psum(tail, ("dp", "ctx"))
    norm_grad = lax.dynamic_slice_in_dim(tail[: 4 * width].reshape(4, width), rank * (width // ring), width // ring, 1)
    share = bias_params.shape[0]
    bias_grad = lax.dynamic_slice_in_dim(tail[4 * width :], rank * share, share, 0)

    qkv_new = adamw(qkv_weight, owned[0], qkv_first, qkv_second, 0.1, DECAY)
    out_new = adamw(out_weight, owned[1], out_first, out_second, 0.6, DECAY)
    up_new = adamw(up_weight, owned[2], up_first, up_second, 0.1, DECAY)
    down_new = adamw(down_weight, owned[3], down_first, down_second, 0.05, DECAY)
    norm_new = adamw(norm_params, norm_grad, norm_first, norm_second, 0.6, 0.0)
    bias_new = adamw(bias_params, bias_grad, bias_first, bias_second, 0.6, 0.0)
    return (
        layer_out, input_grad, *qkv_new, *out_new, *up_new, *down_new,
        norm_new[0], norm_new[1][:2], norm_new[1][2:], norm_new[2], *bias_new,
    )


def solution(mesh):
    rows, columns, token = P("ctx", None), P(None, "ctx"), P("dp", "ctx", None)
    in_specs = (token, token, P("dp", None)) + (rows,) * 4 + (columns, P("ctx")) + (rows,) * 8
    in_specs += (columns, columns, P("ctx"), P("ctx"))
    out_specs = (token, token) + (rows,) * 12 + (columns,) * 4 + (P("ctx"),) * 3
    return jax.shard_map(shards, mesh=mesh, in_specs=in_specs, out_specs=out_specs, check_vma=False)
```

```python
import functools
import math

import jax
import jax.numpy as jnp
from jax import lax
from jax.experimental import pallas as pl
from jax.experimental.pallas import tpu as pltpu
from jax.sharding import PartitionSpec as P

HEADS = 12
HD = 64
STEP = 10
ROT = 16
BLOCK = 128
QUAD = 4

EPS_NORM = 1e-05
BETA_ONE = 0.9
BETA_TWO = 0.95
EPS_ADAM = 1e-08
DECAY = 0.01
ROPE_BASE = 10000.0
F32 = jnp.float32
BF16 = jnp.bfloat16
MIB = 1024 * 1024


def dot(left, right, dims=((1,), (0,))):
    return lax.dot_general(left, right, (dims, ((), ())), preferred_element_type=F32)


NN = ((1,), (0,))
NT = ((1,), (1,))
TN = ((0,), (0,))


def normalized(values):
    mean = jnp.mean(values, axis=-1, keepdims=True)
    centred = values - mean
    variance = jnp.mean(centred * centred, axis=-1, keepdims=True)
    scale = lax.rsqrt(variance + EPS_NORM)
    return centred * scale, scale


MESH = pl.DeviceIdType.MESH


def plane(d):
    core, x, y = d % 2, d // 2 % 2, d // 4 % 2
    return core, x, y, d + 1 - 2 * core, d + 2 - 4 * x, d + 4 - 8 * y


def gather_kernel(
    up, down, att, small, tokens, cotangents,
    up_all, down_all, att_all, small_all, home_x, home_g,
    z_send, z_recv, p_send, p_recv, s_send, s_recv, t_send, t_recv, local,
):
    ring = lax.axis_size("ctx")
    d, z = lax.axis_index("dp"), lax.axis_index("ctx")
    core, x, y, core_id, x_id, y_id = plane(d)
    own = x + 2 * y
    own_x, own_y, far = own + 1 - 2 * x, own + 2 - 4 * y, 3 - own
    batch, piece = tokens.shape[:2]
    arrays = ((up, up_all, False), (down, down_all, True), (att, att_all, False))

    def slot(a, base, place, half=None):
        source, whole, tall = arrays[a]
        ref = source if base is None else whole
        rows, columns = source.shape
        at = 0 if base is None else base * rows
        height, span = rows // 4, columns // 2
        at = at + place * height
        column = core * span
        if half is not None:
            if tall:
                height = height // 2
                at = at + half * height
            else:
                span = span // 2
                column = column + half * span
        return ref.at[pl.ds(pl.multiple_of(at, 16), height), pl.ds(pl.multiple_of(column, 128), span)]

    def other_slot(a, base, place):
        source, whole, tall = arrays[a]
        rows, columns = source.shape
        at = pl.multiple_of(base * rows + place * (rows // 4), 16)
        column = pl.multiple_of((1 - core) * (columns // 2), 128)
        return whole.at[pl.ds(at, rows // 4), pl.ds(column, columns // 2)]

    def remote(src, dst, send, recv, dp, ctx):
        return pltpu.make_async_remote_copy(
            src_ref=src, dst_ref=dst, send_sem=send, recv_sem=recv, device_id=(dp, ctx), device_id_type=MESH
        )

    barrier = pltpu.get_barrier_semaphore()
    for k in range(1, ring):
        pl.semaphore_signal(barrier, inc=1, device_id=(d, (z + k) % ring), device_id_type=MESH)
    for other in (core_id, x_id, y_id):
        pl.semaphore_signal(barrier, inc=1, device_id=(other, z), device_id_type=MESH)
    pl.semaphore_wait(barrier, ring + 2)

    def hop(a, way, h):
        shard = z - h if way == 0 else z + h
        target = z + 1 if way == 0 else z - 1
        src = slot(a, None, own) if h == 0 else slot(a, shard, own)
        return remote(src, slot(a, shard, own), z_send.at[a, way, h], z_recv.at[a, way, h], d, target)

    def can_send(way, h):
        shard = z - h if way == 0 else z + h
        target = z + 1 if way == 0 else z - 1
        return (shard >= 0) & (shard < ring) & (target >= 0) & (target < ring)

    def in_range(way, h):
        shard = z - h if way == 0 else z + h
        return (shard >= 0) & (shard < ring)

    def cast(a, shard, j):
        send, recv = p_send.at[a, shard, j], p_recv.at[a, shard, j]
        if j == 0:
            ref = slot(a, shard, own)
            return remote(ref, ref, send, recv, x_id, z)
        if j == 1:
            ref = slot(a, shard, own)
            return remote(ref, ref, send, recv, y_id, z)
        if j == 2:
            ref = slot(a, shard, own_x, 0)
            return remote(ref, ref, send, recv, y_id, z)
        if j == 3:
            ref = slot(a, shard, own_y, 1)
            return remote(ref, ref, send, recv, x_id, z)
        ref = slot(a, shard, (own, own_x, own_y, far)[j - 4])
        return remote(ref, ref, send, recv, core_id, z)

    def arrived(a, shard, j):
        send, recv = p_send.at[a, shard, j], p_recv.at[a, shard, j]
        ref = {0: lambda: slot(a, shard, own_x), 1: lambda: slot(a, shard, own_y),
               2: lambda: slot(a, shard, far, 0), 3: lambda: slot(a, shard, far, 1)}.get(
            j, lambda: other_slot(a, shard, (own, own_x, own_y, far)[j - 4]))()
        remote(ref, ref, send, recv, core_id, z).wait_recv()

    for k in range(1, ring):
        to = (z + k) % ring
        remote(small, small_all.at[z], s_send.at[k], s_recv.at[k], d, to).start()
    for a in range(3):
        for way in range(2):
            @pl.when(can_send(way, 0))
            def _(a=a, way=way):
                hop(a, way, 0).start()
    own_copies = [pltpu.make_async_copy(small, small_all.at[z], local.at[0])]
    for a in range(3):
        source, whole, _ = arrays[a]
        rows = source.shape[0]
        at = pl.ds(pl.multiple_of(z * rows, 16), rows)
        own_copies.append(pltpu.make_async_copy(source, whole.at[at, :], local.at[1 + a]))
    for copy in own_copies:
        copy.start()

    def stage_a(a, h):
        for way in range(2):
            @pl.when(in_range(way, h))
            def _(way=way):
                shard = z - h if way == 0 else z + h
                ref = slot(a, shard, own)
                remote(ref, ref, z_send.at[a, way, h - 1], z_recv.at[a, way, h - 1], core_id, z).wait_recv()

                @pl.when(can_send(way, h))
                def _():
                    hop(a, way, h).start()

                cast(a, shard, 0).start()
                cast(a, shard, 1).start()
                cast(a, shard, 4).start()

    def stage_b(a, h):
        for way in range(2):
            @pl.when(in_range(way, h))
            def _(way=way):
                shard = z - h if way == 0 else z + h
                arrived(a, shard, 0)
                cast(a, shard, 2).start()
                cast(a, shard, 5).start()
                arrived(a, shard, 1)
                cast(a, shard, 3).start()
                cast(a, shard, 6).start()

    def stage_c(a, h):
        for way in range(2):
            @pl.when(in_range(way, h))
            def _(way=way):
                shard = z - h if way == 0 else z + h
                arrived(a, shard, 2)
                arrived(a, shard, 3)
                cast(a, shard, 7).start()

    def moved(i, which, to_home):
        source, whole = ((tokens, home_x), (cotangents, home_g))[which]
        target = i + core
        at = pl.ds(pl.multiple_of(z * piece, 16), piece)
        return source.at[i], whole.at[at, :], target

    def start_moves():
        for which in range(2):
            for i in range(batch):
                src, dst, target = moved(i, which, True)

                @pl.when(target != z)
                def _(src=src, dst=dst, target=target, which=which, i=i):
                    remote(src, dst, t_send.at[which, i], t_recv.at[which, z], d, target).start()

                @pl.when(target == z)
                def _(src=src, dst=dst, which=which):
                    pltpu.make_async_copy(src, dst, local.at[4 + which]).start()

    work = [(a, h) for a in range(3) for h in range(1, ring)]
    for n in range(len(work) + 2):
        if n == 2 * (ring - 1):
            start_moves()
        if n < len(work):
            stage_a(*work[n])
        if 1 <= n <= len(work):
            stage_b(*work[n - 1])
        if n >= 2:
            stage_c(*work[n - 2])

    for a, h in work:
        for way in range(2):
            @pl.when(in_range(way, h))
            def _(a=a, h=h, way=way):
                shard = z - h if way == 0 else z + h
                for j in range(4, 8):
                    arrived(a, shard, j)
    mine = z - core
    for which in range(2):
        for k in range(1, ring):
            @pl.when((mine >= 0) & (mine < batch))
            def _(which=which, k=k):
                source, whole = ((tokens, home_x), (cotangents, home_g))[which]
                other = (z + k) % ring
                ref = whole.at[pl.ds(pl.multiple_of(other * piece, 16), piece), :]
                remote(ref, ref, t_send.at[which, 0], t_recv.at[which, other], core_id, z).wait_recv()
    for k in range(1, ring):
        ref = small_all.at[(z + ring - k) % ring]
        remote(ref, ref, s_send.at[k], s_recv.at[k], core_id, z).wait_recv()
    for k in range(1, ring):
        remote(small, small_all.at[z], s_send.at[k], s_recv.at[k], d, (z + k) % ring).wait_send()
    for a in range(3):
        for way in range(2):
            for h in range(ring - 1):
                @pl.when(can_send(way, h))
                def _(a=a, way=way, h=h):
                    hop(a, way, h).wait_send()
    for a, h in work:
        for way in range(2):
            @pl.when(in_range(way, h))
            def _(a=a, h=h, way=way):
                shard = z - h if way == 0 else z + h
                for j in range(8):
                    cast(a, shard, j).wait_send()
    for which in range(2):
        for i in range(batch):
            src, dst, target = moved(i, which, True)

            @pl.when(target != z)
            def _(src=src, dst=dst, target=target, which=which, i=i):
                remote(src, dst, t_send.at[which, i], t_recv.at[which, z], d, target).wait_send()

            @pl.when(target == z)
            def _(src=src, dst=dst, which=which):
                pltpu.make_async_copy(src, dst, local.at[4 + which]).wait()
    for copy in own_copies:
        copy.wait()


def gather_all(up, down, att, small, tokens, cotangents):
    ring = lax.axis_size("ctx")
    batch, piece, width = tokens.shape
    full = lambda v: jax.ShapeDtypeStruct((ring * v.shape[0], v.shape[1]), v.dtype)
    home = jax.ShapeDtypeStruct((ring * piece, width), tokens.dtype)
    dma = pltpu.SemaphoreType.DMA
    anywhere = pl.BlockSpec(memory_space=pl.ANY)
    return pl.pallas_call(
        gather_kernel,
        in_specs=[anywhere] * 6,
        out_specs=[anywhere] * 6,
        out_shape=[full(up), full(down), full(att), jax.ShapeDtypeStruct((ring, *small.shape), small.dtype), home, home],
        scratch_shapes=[
            dma((3, 2, ring)), dma((3, 2, ring)), dma((3, ring, 8)), dma((3, ring, 8)),
            dma((ring,)), dma((ring,)), dma((2, batch)), dma((2, ring)), dma((6,)),
        ],
        compiler_params=pltpu.CompilerParams(collective_id=0, has_side_effects=True),
        cost_estimate=pl.CostEstimate(flops=0, bytes_accessed=60 * MIB, transcendentals=0),
        name="gather",
    )(up, down, att, small, tokens, cotangents)


def feed_kernel(
    x_ref, g_ref, norm_ref, bias_ref, up_ref, down_ref,
    out_ref, h_ref, dup_ref, ddown_ref, dbias_ref, small_ref,
    m_ref, hid_ref, dup_in_ref, acc_ref, dm_ref,
):
    step = pl.program_id(0)
    last = pl.num_programs(0) - 1
    rows, width = x_ref.shape
    tile = 256
    tiles = rows // tile

    @pl.when(step == 0)
    def _():
        for t in range(tiles):
            at = pl.ds(t * tile, tile)
            xh, _ = normalized(x_ref[at, :].astype(F32))
            m_ref[at, :] = (xh * norm_ref[2:3, :] + norm_ref[3:4, :]).astype(BF16)
        acc_ref[...] = jnp.zeros_like(acc_ref)
        dm_ref[...] = jnp.zeros_like(dm_ref)

    up = up_ref[...]
    down = down_ref[...]
    total = jnp.zeros(dbias_ref.shape, F32)
    for t in range(tiles):
        at = pl.ds(t * tile, tile)
        u = dot(m_ref[at, :], up) + bias_ref[...]
        cdf = 0.5 * (1.0 + lax.erf(u * (1.0 / math.sqrt(2.0))))
        hidden = (u * cdf).astype(BF16)
        slope = cdf + u * jnp.exp(-0.5 * u * u) * (1.0 / math.sqrt(2.0 * math.pi))
        back = (dot(g_ref[at, :], down, NT) * slope).astype(BF16)
        hid_ref[at, :] = hidden
        dup_in_ref[at, :] = back
        total += jnp.sum(back.astype(F32), axis=0, keepdims=True)
        acc_ref[at, :] += dot(hidden, down)
        dm_ref[at, :] += dot(back, up, NT)
    dbias_ref[...] = total
    ddown_ref[...] = dot(hid_ref[...], g_ref[...], TN).astype(BF16)
    dup_ref[...] = dot(m_ref[...], dup_in_ref[...], TN).astype(BF16)

    @pl.when(step == last)
    def _():
        gain = jnp.zeros((1, width), F32)
        shift = jnp.zeros((1, width), F32)
        sums = jnp.zeros((1, width), F32)
        for t in range(tiles):
            at = pl.ds(t * tile, tile)
            xh, _ = normalized(x_ref[at, :].astype(F32))
            dm = dm_ref[at, :]
            gain += jnp.sum(dm * xh, axis=0, keepdims=True)
            shift += jnp.sum(dm, axis=0, keepdims=True)
            sums += jnp.sum(g_ref[at, :].astype(F32), axis=0, keepdims=True)
            h_ref[at, :] = dm * norm_ref[2:3, :]
            out_ref[at, :] = acc_ref[at, :]
        small_ref[0:1, :] = gain
        small_ref[1:2, :] = shift
        small_ref[2:3, :] = sums


def feed(x, g, norms, bias_up, up, down):
    rows, width = x.shape
    ff = up.shape[1]
    chunk = 512
    whole = lambda shape: pl.BlockSpec(shape, lambda i: (0,) * len(shape))
    return pl.pallas_call(
        feed_kernel,
        grid=(ff // chunk,),
        in_specs=[
            whole((rows, width)),
            whole((rows, width)),
            whole(norms.shape),
            pl.BlockSpec((1, chunk), lambda i: (0, i)),
            pl.BlockSpec((width, chunk), lambda i: (0, i)),
            pl.BlockSpec((chunk, width), lambda i: (i, 0)),
        ],
        out_specs=[
            whole((rows, width)),
            whole((rows, width)),
            pl.BlockSpec((width, chunk), lambda i: (0, i)),
            pl.BlockSpec((chunk, width), lambda i: (i, 0)),
            pl.BlockSpec((1, chunk), lambda i: (0, i)),
            whole((8, width)),
        ],
        out_shape=[
            jax.ShapeDtypeStruct((rows, width), F32),
            jax.ShapeDtypeStruct((rows, width), F32),
            jax.ShapeDtypeStruct((width, ff), BF16),
            jax.ShapeDtypeStruct((ff, width), BF16),
            jax.ShapeDtypeStruct((1, ff), F32),
            jax.ShapeDtypeStruct((8, width), F32),
        ],
        scratch_shapes=[
            pltpu.VMEM((rows, width), BF16),
            pltpu.VMEM((rows, chunk), BF16),
            pltpu.VMEM((rows, chunk), BF16),
            pltpu.VMEM((rows, width), F32),
            pltpu.VMEM((rows, width), F32),
        ],
        compiler_params=pltpu.CompilerParams(vmem_limit_bytes=56 * MIB),
        cost_estimate=pl.CostEstimate(
            flops=12 * rows * width * ff, bytes_accessed=8 * width * ff, transcendentals=rows * ff
        ),
        name="feed",
    )(x, g, norms, bias_up, up, down)


def attend_kernel(
    x_ref, g_ref, norm_ref, bias_ref, cos_ref, low_ref, high_ref, wq_ref, wk_ref, wv_ref, wo_ref,
    out_ref, h_ref, dq_ref, dk_ref, dv_ref, dwo_ref, dbias_ref, small_ref,
    a_ref, acc_ref, da_ref, q_ref, k_ref, v_ref, do_ref, o_ref, dqs_ref, dks_ref, dvs_ref,
):
    step = pl.program_id(0)
    last = pl.num_programs(0) - 1
    rows, width = x_ref.shape
    lanes = QUAD * HD
    tile = 256
    half = ROT // 2
    scale = 1.0 / math.sqrt(HD)

    @pl.when(step == 0)
    def _():
        for t in range(rows // tile):
            at = pl.ds(t * tile, tile)
            xh, _ = normalized(x_ref[at, :].astype(F32))
            a_ref[at, :] = (xh * norm_ref[0:1, :] + norm_ref[1:2, :]).astype(BF16)
        acc_ref[...] = jnp.zeros_like(acc_ref)
        da_ref[...] = jnp.zeros_like(da_ref)

    def turn(values, at):
        low = pltpu.roll(values, lanes - half, 1) * low_ref[at, :]
        high = pltpu.roll(values, half, 1) * high_ref[at, :]
        return values * cos_ref[at, :], low + high

    for t in range(rows // tile):
        at = pl.ds(t * tile, tile)
        a = a_ref[at, :]
        same, cross = turn(dot(a, wq_ref[...]) + bias_ref[...], at)
        q_ref[at, :] = ((same + cross).astype(BF16) * scale).astype(BF16)
        same, cross = turn(dot(a, wk_ref[...]), at)
        k_ref[at, :] = (same + cross).astype(BF16)
        v_ref[at, :] = dot(a, wv_ref[...]).astype(BF16)
        do_ref[at, :] = dot(g_ref[at, :], wo_ref[...], NT).astype(BF16)

    dks_ref[...] = jnp.zeros_like(dks_ref)
    dvs_ref[...] = jnp.zeros_like(dvs_ref)
    head_of = lax.broadcasted_iota(jnp.int32, (BLOCK, lanes), 1) // HD

    def stack(values):
        zero = jnp.zeros_like(values)
        return jnp.concatenate([jnp.where(head_of == e, values, zero) for e in range(QUAD)], axis=0)

    def merge(values):
        out = values[:BLOCK]
        for e in range(1, QUAD):
            out = jnp.where(head_of == e, values[e * BLOCK : (e + 1) * BLOCK], out)
        return out

    spot = lax.broadcasted_iota(jnp.int32, (QUAD * BLOCK, BLOCK), 0) % BLOCK
    admitted = lax.broadcasted_iota(jnp.int32, (QUAD * BLOCK, BLOCK), 1) <= spot
    for b in range(rows // BLOCK):
        at = pl.ds(b * BLOCK, BLOCK)
        seen = pl.ds(0, (b + 1) * BLOCK)
        q = stack(q_ref[at, :])
        do_block = do_ref[at, :]
        do = stack(do_block)
        keys = k_ref[seen, :]
        values = v_ref[seen, :]
        scores = dot(q, keys, NT)
        edge = jnp.where(admitted, scores[:, b * BLOCK :], -1e30)
        scores = edge if b == 0 else jnp.concatenate([scores[:, : b * BLOCK], edge], axis=1)
        top = jnp.max(scores, axis=-1, keepdims=True)
        expo = jnp.exp(scores - top)
        probs = expo * (1.0 / jnp.sum(expo, axis=-1, keepdims=True))
        low = probs.astype(BF16)
        mixed = dot(low, values)
        o_ref[at, :] = merge(mixed).astype(BF16)
        share = jnp.sum(mixed * do.astype(F32), axis=-1, keepdims=True)
        back = (probs * (dot(do, values, NT) - share)).astype(BF16)
        dqs_ref[at, :] = merge(dot(back, keys)) * scale
        dks_ref[seen, :] += dot(back, q, TN)
        dvs_ref[seen, :] += dot(low, do, TN)

    total = jnp.zeros((1, lanes), F32)
    for t in range(rows // tile):
        at = pl.ds(t * tile, tile)
        same, cross = turn(dqs_ref[at, :], at)
        dq = (same - cross).astype(BF16)
        same, cross = turn(dks_ref[at, :], at)
        dk = (same - cross).astype(BF16)
        dv = dvs_ref[at, :].astype(BF16)
        total += jnp.sum(dq.astype(F32), axis=0, keepdims=True)
        q_ref[at, :] = dq
        k_ref[at, :] = dk
        v_ref[at, :] = dv
        acc_ref[at, :] += dot(o_ref[at, :], wo_ref[...])
        da_ref[at, :] += dot(dq, wq_ref[...], NT) + dot(dk, wk_ref[...], NT) + dot(dv, wv_ref[...], NT)
    dbias_ref[...] = total
    dwo_ref[...] = dot(o_ref[...], g_ref[...], TN).astype(BF16)
    dq_ref[...] = dot(a_ref[...], q_ref[...], TN).astype(BF16)
    dk_ref[...] = dot(a_ref[...], k_ref[...], TN).astype(BF16)
    dv_ref[...] = dot(a_ref[...], v_ref[...], TN).astype(BF16)

    @pl.when(step == last)
    def _():
        gain = jnp.zeros((1, width), F32)
        shift = jnp.zeros((1, width), F32)
        for t in range(rows // tile):
            at = pl.ds(t * tile, tile)
            xh, _ = normalized(x_ref[at, :].astype(F32))
            da = da_ref[at, :]
            gain += jnp.sum(da * xh, axis=0, keepdims=True)
            shift += jnp.sum(da, axis=0, keepdims=True)
            h_ref[at, :] = (da * norm_ref[0:1, :]).astype(BF16)
            out_ref[at, :] = acc_ref[at, :].astype(BF16)
        small_ref[0:1, :] = gain
        small_ref[1:2, :] = shift


def attend(x, g, norms, bias_q, tables, weights):
    rows, width = x.shape
    lanes = QUAD * HD
    groups = width // lanes
    whole = lambda shape: pl.BlockSpec(shape, lambda i: (0,) * len(shape))
    column = pl.BlockSpec((width, lanes), lambda i: (0, i))
    small = jax.ShapeDtypeStruct((rows, width), BF16)
    return pl.pallas_call(
        attend_kernel,
        grid=(groups,),
        in_specs=[
            whole((rows, width)),
            whole((rows, width)),
            whole(norms.shape),
            pl.BlockSpec((1, lanes), lambda i: (0, i)),
            whole((rows, lanes)),
            whole((rows, lanes)),
            whole((rows, lanes)),
            pl.BlockSpec((width, lanes), lambda i: (0, i)),
            pl.BlockSpec((width, lanes), lambda i: (0, groups + i)),
            pl.BlockSpec((width, lanes), lambda i: (0, 2 * groups + i)),
            pl.BlockSpec((lanes, width), lambda i: (i, 3)),
        ],
        out_specs=[
            whole((rows, width)),
            whole((rows, width)),
            column,
            column,
            column,
            pl.BlockSpec((lanes, width), lambda i: (i, 0)),
            pl.BlockSpec((1, lanes), lambda i: (0, i)),
            whole((8, width)),
        ],
        out_shape=[
            small,
            small,
            jax.ShapeDtypeStruct((width, width), BF16),
            jax.ShapeDtypeStruct((width, width), BF16),
            jax.ShapeDtypeStruct((width, width), BF16),
            jax.ShapeDtypeStruct((width, width), BF16),
            jax.ShapeDtypeStruct((1, width), F32),
            jax.ShapeDtypeStruct((8, width), F32),
        ],
        scratch_shapes=[
            pltpu.VMEM((rows, width), BF16),
            pltpu.VMEM((rows, width), F32),
            pltpu.VMEM((rows, width), F32),
        ]
        + [pltpu.VMEM((rows, lanes), BF16)] * 5
        + [pltpu.VMEM((rows, lanes), F32)] * 3,
        compiler_params=pltpu.CompilerParams(vmem_limit_bytes=56 * MIB),
        cost_estimate=pl.CostEstimate(
            flops=24 * rows * width * width + 8 * rows * rows * width,
            bytes_accessed=16 * width * width + 8 * rows * width,
            transcendentals=HEADS * rows * rows // 2,
        ),
        name="attend",
    )(x, g, norms, bias_q, *tables, weights, weights, weights, weights)


def rotary_tables(length):
    half = ROT // 2
    frequency = ROPE_BASE ** (-(jnp.arange(half, dtype=F32) * 2.0 / ROT))
    angle = jnp.arange(length, dtype=F32)[:, None] * frequency[None, :]
    cosine, sine = jnp.cos(angle), jnp.sin(angle)
    rest = jnp.zeros((length, HD - ROT), F32)
    none = jnp.zeros_like(sine)
    cos_full = jnp.concatenate([cosine, cosine, rest + 1.0], axis=1)
    low = jnp.concatenate([-sine, none, rest], axis=1)
    high = jnp.concatenate([none, sine, rest], axis=1)
    return tuple(jnp.tile(table, (1, QUAD)) for table in (cos_full, low, high))


def adamw(weight, grad, first, second, rate, decay):
    first_new = BETA_ONE * first + (1.0 - BETA_ONE) * grad
    second_new = BETA_TWO * second + (1.0 - BETA_TWO) * grad * grad
    first_hat = first_new / (1.0 - BETA_ONE**STEP)
    second_hat = second_new / (1.0 - BETA_TWO**STEP)
    weight_new = weight - rate * (first_hat / (jnp.sqrt(second_hat) + EPS_ADAM) + decay * weight)
    return (first_new, second_new, weight_new)


def shards(
    tokens, out_grad, block_order, qkv_weight, out_weight, up_weight, down_weight, norm_params, bias_params,
    qkv_first, qkv_second, out_first, out_second, up_first, up_second, down_first, down_second,
    norm_first, norm_second, bias_first, bias_second,
):
    groups, ring = lax.axis_size("dp"), lax.axis_size("ctx")
    group, rank = lax.axis_index("dp"), lax.axis_index("ctx")
    batch, piece, width = tokens.shape
    length = piece * ring
    count = batch * piece
    ff = up_weight.shape[1]

    att_weight = jnp.concatenate([qkv_weight, out_weight], axis=1).astype(BF16)
    small = jnp.concatenate([norm_params.reshape(-1), bias_params]).astype(BF16).astype(F32)
    entries = small.shape[0]
    small = jnp.pad(small, (0, -entries % 1024)).reshape(-1, 128)
    up_copy, down_copy, att_copy, small_all, home_x, home_g = gather_all(
        up_weight.astype(BF16), down_weight.astype(BF16), att_weight, small, tokens, out_grad
    )
    small_all = small_all.reshape(ring, -1)[:, :entries]
    norms = small_all[:, : 4 * width // ring].reshape(ring, 4, width // ring).transpose(1, 0, 2).reshape(4, width)
    biases = small_all[:, 4 * width // ring :].reshape(1, -1)

    odd = group % 2

    def shift_pairs(k):
        pairs = []
        for d in range(groups):
            for r in range(ring):
                if 0 <= (r + k) % ring - d % 2 < batch:
                    pairs.append((d * ring + r, d * ring + (r + k) % ring))
        return pairs

    def piece_for(home):
        return jnp.clip(home - odd, 0, batch - 1)

    mine = rank - odd
    is_home = (mine >= 0) & (mine < batch)
    per = piece // BLOCK
    order = block_order[piece_for(rank)]
    place = jnp.argsort(order)

    def sorted_rows(values):
        values = jnp.take(values.reshape(ring * per, BLOCK, width), place, axis=0).reshape(length, width)
        return jnp.where(is_home, values, jnp.zeros_like(values))

    home_x, home_g = sorted_rows(home_x), sorted_rows(home_g)

    x_rows, g_rows = tokens.reshape(count, width), out_grad.reshape(count, width)
    feed_out, h_feed, dup, ddown, dbias_up, small_feed = feed(
        x_rows, g_rows, norms, biases[:, 2 * width : 2 * width + ff], up_copy, down_copy
    )
    attend_out, h_attend, dq, dk, dv, dout, dbias_q, small_attend = attend(
        home_x, home_g, norms, biases[:, :width], rotary_tables(length), att_copy
    )

    results = jnp.stack([attend_out, h_attend]).reshape(2, ring * per, BLOCK, width)
    results = jnp.take(results, order, axis=1).reshape(2, ring, per * BLOCK, width)
    kept = [results[:, rank]]
    for k in range(1, ring):
        send = results[:, (rank - k) % ring]
        kept.append(lax.ppermute(send, ("dp", "ctx"), [(b, a) for a, b in shift_pairs(k)]))
    returned = jnp.stack(kept)[(jnp.arange(batch) + odd - rank) % ring]
    returned = returned.transpose(1, 0, 2, 3).reshape(2, count, width).astype(F32)

    rows = x_rows.astype(F32)
    bias_rows = biases[:, width : 2 * width] + biases[:, 2 * width + ff :]
    layer_out = (rows + returned[0] + feed_out + bias_rows).astype(BF16).reshape(batch, piece, width)
    xh, scale = normalized(rows)
    h = returned[1] + h_feed
    inner = jnp.mean(h * xh, axis=-1, keepdims=True)
    input_grad = g_rows.astype(F32) + scale * (h - jnp.mean(h, axis=-1, keepdims=True) - xh * inner)
    input_grad = input_grad.reshape(batch, piece, width)

    def reduce(grad):
        part = lax.psum_scatter(grad.reshape(ring, -1, grad.shape[1]), "dp", scatter_dimension=1, tiled=True)
        part = lax.psum_scatter(part, "ctx", scatter_dimension=0, tiled=False)
        return lax.all_gather(part, "dp", axis=0, tiled=True).astype(F32)

    dqkv = jnp.concatenate([dq, dk, dv], axis=1)
    owned = tuple(map(reduce, (dqkv, dout, dup, ddown)))
    tail = jnp.concatenate(
        [small_attend[:2].reshape(-1), small_feed[:2].reshape(-1), dbias_q[0], small_feed[2], dbias_up[0], small_feed[2]]
    )
    tail = lax.psum(tail, ("dp", "ctx"))
    norm_grad = lax.dynamic_slice_in_dim(tail[: 4 * width].reshape(4, width), rank * (width // ring), width // ring, 1)
    share = bias_params.shape[0]
    bias_grad = lax.dynamic_slice_in_dim(tail[4 * width :], rank * share, share, 0)

    qkv_new = adamw(qkv_weight, owned[0], qkv_first, qkv_second, 0.1, DECAY)
    out_new = adamw(out_weight, owned[1], out_first, out_second, 0.6, DECAY)
    up_new = adamw(up_weight, owned[2], up_first, up_second, 0.1, DECAY)
    down_new = adamw(down_weight, owned[3], down_first, down_second, 0.05, DECAY)
    norm_new = adamw(norm_params, norm_grad, norm_first, norm_second, 0.6, 0.0)
    bias_new = adamw(bias_params, bias_grad, bias_first, bias_second, 0.6, 0.0)
    return (
        layer_out, input_grad, *qkv_new, *out_new, *up_new, *down_new,
        norm_new[0], norm_new[1][:2], norm_new[1][2:], norm_new[2], *bias_new,
    )


def solution(mesh):
    rows, columns, token = P("ctx", None), P(None, "ctx"), P("dp", "ctx", None)
    in_specs = (token, token, P("dp", None)) + (rows,) * 4 + (columns, P("ctx")) + (rows,) * 8
    in_specs += (columns, columns, P("ctx"), P("ctx"))
    out_specs = (token, token) + (rows,) * 12 + (columns,) * 4 + (P("ctx"),) * 3
    return jax.shard_map(shards, mesh=mesh, in_specs=in_specs, out_specs=out_specs, check_vma=False)
```

```python
import functools
import math

import jax
import jax.numpy as jnp
import numpy as np
from jax import lax
from jax.experimental import pallas as pl
from jax.experimental.pallas import tpu as pltpu
from jax.sharding import PartitionSpec as P

HEADS = 12
HD = 64
STEP = 10
ROT = 16
SEQS = 3
BLOCK = 128
QUAD = 4

EPS_NORM = 1e-05
BETA_ONE = 0.9
BETA_TWO = 0.95
EPS_ADAM = 1e-08
DECAY = 0.01
ROPE_BASE = 10000.0
F32 = jnp.float32
BF16 = jnp.bfloat16
MIB = 1024 * 1024


def dot(left, right, dims=((1,), (0,))):
    return lax.dot_general(left, right, (dims, ((), ())), preferred_element_type=F32)


NN = ((1,), (0,))
NT = ((1,), (1,))
TN = ((0,), (0,))


def normalized(values):
    mean = jnp.mean(values, axis=-1, keepdims=True)
    centred = values - mean
    variance = jnp.mean(centred * centred, axis=-1, keepdims=True)
    scale = lax.rsqrt(variance + EPS_NORM)
    return centred * scale, scale


MESH = pl.DeviceIdType.MESH


def plane(d):
    core, x, y = d % 2, d // 2 % 2, d // 4 % 2
    return core, x, y, d + 1 - 2 * core, d + 2 - 4 * x, d + 4 - 8 * y


def gather_kernel(
    up, down, att, small, tokens, cotangents,
    up_all, down_all, att_all, small_all, home_x, home_g,
    z_send, z_recv, p_send, p_recv, s_send, s_recv, t_send, t_recv, local,
):
    ring = lax.axis_size("ctx")
    d, z = lax.axis_index("dp"), lax.axis_index("ctx")
    core, x, y, core_id, x_id, y_id = plane(d)
    own = x + 2 * y
    own_x, own_y, far = own + 1 - 2 * x, own + 2 - 4 * y, 3 - own
    batch, piece = tokens.shape[:2]
    arrays = ((up, up_all, False), (down, down_all, True), (att, att_all, False))

    def slot(a, base, place, half=None):
        source, whole, tall = arrays[a]
        ref = source if base is None else whole
        rows, columns = source.shape
        at = 0 if base is None else base * rows
        height, span = rows // 4, columns // 2
        at = at + place * height
        column = core * span
        if half is not None:
            if tall:
                height = height // 2
                at = at + half * height
            else:
                span = span // 2
                column = column + half * span
        return ref.at[pl.ds(pl.multiple_of(at, 16), height), pl.ds(pl.multiple_of(column, 128), span)]

    def other_slot(a, base, place):
        source, whole, tall = arrays[a]
        rows, columns = source.shape
        at = pl.multiple_of(base * rows + place * (rows // 4), 16)
        column = pl.multiple_of((1 - core) * (columns // 2), 128)
        return whole.at[pl.ds(at, rows // 4), pl.ds(column, columns // 2)]

    def remote(src, dst, send, recv, dp, ctx):
        return pltpu.make_async_remote_copy(
            src_ref=src, dst_ref=dst, send_sem=send, recv_sem=recv, device_id=(dp, ctx), device_id_type=MESH
        )

    barrier = pltpu.get_barrier_semaphore()
    for k in range(1, ring):
        pl.semaphore_signal(barrier, inc=1, device_id=(d, (z + k) % ring), device_id_type=MESH)
    for other in (core_id, x_id, y_id):
        pl.semaphore_signal(barrier, inc=1, device_id=(other, z), device_id_type=MESH)
    pl.semaphore_wait(barrier, ring + 2)

    def hop(a, way, h):
        shard = z - h if way == 0 else z + h
        target = z + 1 if way == 0 else z - 1
        src = slot(a, None, own) if h == 0 else slot(a, shard, own)
        return remote(src, slot(a, shard, own), z_send.at[a, way, h], z_recv.at[a, way, h], d, target)

    def can_send(way, h):
        shard = z - h if way == 0 else z + h
        target = z + 1 if way == 0 else z - 1
        return (shard >= 0) & (shard < ring) & (target >= 0) & (target < ring)

    def in_range(way, h):
        shard = z - h if way == 0 else z + h
        return (shard >= 0) & (shard < ring)

    def cast(a, shard, j):
        send, recv = p_send.at[a, shard, j], p_recv.at[a, shard, j]
        if j == 0:
            ref = slot(a, shard, own)
            return remote(ref, ref, send, recv, x_id, z)
        if j == 1:
            ref = slot(a, shard, own)
            return remote(ref, ref, send, recv, y_id, z)
        if j == 2:
            ref = slot(a, shard, own_x, 0)
            return remote(ref, ref, send, recv, y_id, z)
        if j == 3:
            ref = slot(a, shard, own_y, 1)
            return remote(ref, ref, send, recv, x_id, z)
        ref = slot(a, shard, (own, own_x, own_y, far)[j - 4])
        return remote(ref, ref, send, recv, core_id, z)

    def arrived(a, shard, j):
        send, recv = p_send.at[a, shard, j], p_recv.at[a, shard, j]
        ref = {0: lambda: slot(a, shard, own_x), 1: lambda: slot(a, shard, own_y),
               2: lambda: slot(a, shard, far, 0), 3: lambda: slot(a, shard, far, 1)}.get(
            j, lambda: other_slot(a, shard, (own, own_x, own_y, far)[j - 4]))()
        remote(ref, ref, send, recv, core_id, z).wait_recv()

    for k in range(1, ring):
        to = (z + k) % ring
        remote(small, small_all.at[z], s_send.at[k], s_recv.at[k], d, to).start()
    for a in range(3):
        for way in range(2):
            @pl.when(can_send(way, 0))
            def _(a=a, way=way):
                hop(a, way, 0).start()
    own_copies = [pltpu.make_async_copy(small, small_all.at[z], local.at[0])]
    for a in range(3):
        source, whole, _ = arrays[a]
        rows = source.shape[0]
        at = pl.ds(pl.multiple_of(z * rows, 16), rows)
        own_copies.append(pltpu.make_async_copy(source, whole.at[at, :], local.at[1 + a]))
    for copy in own_copies:
        copy.start()

    def stage_a(a, h):
        for way in range(2):
            @pl.when(in_range(way, h))
            def _(way=way):
                shard = z - h if way == 0 else z + h
                ref = slot(a, shard, own)
                remote(ref, ref, z_send.at[a, way, h - 1], z_recv.at[a, way, h - 1], core_id, z).wait_recv()

                @pl.when(can_send(way, h))
                def _():
                    hop(a, way, h).start()

                cast(a, shard, 0).start()
                cast(a, shard, 1).start()
                cast(a, shard, 4).start()

    def stage_b(a, h):
        for way in range(2):
            @pl.when(in_range(way, h))
            def _(way=way):
                shard = z - h if way == 0 else z + h
                arrived(a, shard, 0)
                cast(a, shard, 2).start()
                cast(a, shard, 5).start()
                arrived(a, shard, 1)
                cast(a, shard, 3).start()
                cast(a, shard, 6).start()

    def stage_c(a, h):
        for way in range(2):
            @pl.when(in_range(way, h))
            def _(way=way):
                shard = z - h if way == 0 else z + h
                arrived(a, shard, 2)
                arrived(a, shard, 3)
                cast(a, shard, 7).start()

    def moved(i, which, to_home):
        source, whole = ((tokens, home_x), (cotangents, home_g))[which]
        target = i + core
        at = pl.ds(pl.multiple_of(z * piece, 16), piece)
        return source.at[i], whole.at[at, :], target

    def start_moves():
        for which in range(2):
            for i in range(batch):
                src, dst, target = moved(i, which, True)

                @pl.when(target != z)
                def _(src=src, dst=dst, target=target, which=which, i=i):
                    remote(src, dst, t_send.at[which, i], t_recv.at[which, z], d, target).start()

                @pl.when(target == z)
                def _(src=src, dst=dst, which=which):
                    pltpu.make_async_copy(src, dst, local.at[4 + which]).start()

    work = [(a, h) for a in range(3) for h in range(1, ring)]
    for n in range(len(work) + 2):
        if n == 2 * (ring - 1):
            start_moves()
        if n < len(work):
            stage_a(*work[n])
        if 1 <= n <= len(work):
            stage_b(*work[n - 1])
        if n >= 2:
            stage_c(*work[n - 2])

    for a, h in work:
        for way in range(2):
            @pl.when(in_range(way, h))
            def _(a=a, h=h, way=way):
                shard = z - h if way == 0 else z + h
                for j in range(4, 8):
                    arrived(a, shard, j)
    mine = z - core
    for which in range(2):
        for k in range(1, ring):
            @pl.when((mine >= 0) & (mine < batch))
            def _(which=which, k=k):
                source, whole = ((tokens, home_x), (cotangents, home_g))[which]
                other = (z + k) % ring
                ref = whole.at[pl.ds(pl.multiple_of(other * piece, 16), piece), :]
                remote(ref, ref, t_send.at[which, 0], t_recv.at[which, other], core_id, z).wait_recv()
    for k in range(1, ring):
        ref = small_all.at[(z + ring - k) % ring]
        remote(ref, ref, s_send.at[k], s_recv.at[k], core_id, z).wait_recv()
    for k in range(1, ring):
        remote(small, small_all.at[z], s_send.at[k], s_recv.at[k], d, (z + k) % ring).wait_send()
    for a in range(3):
        for way in range(2):
            for h in range(ring - 1):
                @pl.when(can_send(way, h))
                def _(a=a, way=way, h=h):
                    hop(a, way, h).wait_send()
    for a, h in work:
        for way in range(2):
            @pl.when(in_range(way, h))
            def _(a=a, h=h, way=way):
                shard = z - h if way == 0 else z + h
                for j in range(8):
                    cast(a, shard, j).wait_send()
    for which in range(2):
        for i in range(batch):
            src, dst, target = moved(i, which, True)

            @pl.when(target != z)
            def _(src=src, dst=dst, target=target, which=which, i=i):
                remote(src, dst, t_send.at[which, i], t_recv.at[which, z], d, target).wait_send()

            @pl.when(target == z)
            def _(src=src, dst=dst, which=which):
                pltpu.make_async_copy(src, dst, local.at[4 + which]).wait()
    for copy in own_copies:
        copy.wait()


def gather_all(up, down, att, small, tokens, cotangents):
    ring = lax.axis_size("ctx")
    batch, piece, width = tokens.shape
    full = lambda v: jax.ShapeDtypeStruct((ring * v.shape[0], v.shape[1]), v.dtype)
    home = jax.ShapeDtypeStruct((ring * piece, width), tokens.dtype)
    dma = pltpu.SemaphoreType.DMA
    anywhere = pl.BlockSpec(memory_space=pl.ANY)
    return pl.pallas_call(
        gather_kernel,
        in_specs=[anywhere] * 6,
        out_specs=[anywhere] * 6,
        out_shape=[full(up), full(down), full(att), jax.ShapeDtypeStruct((ring, *small.shape), small.dtype), home, home],
        scratch_shapes=[
            dma((3, 2, ring)), dma((3, 2, ring)), dma((3, ring, 8)), dma((3, ring, 8)),
            dma((ring,)), dma((ring,)), dma((2, batch)), dma((2, ring)), dma((6,)),
        ],
        compiler_params=pltpu.CompilerParams(collective_id=0, has_side_effects=True),
        cost_estimate=pl.CostEstimate(flops=0, bytes_accessed=60 * MIB, transcendentals=0),
        name="gather",
    )(up, down, att, small, tokens, cotangents)


def fold(into, rows, term):
    owners, height, _ = term.shape
    tile = 48

    def body(n, _):
        o, t = n // (height // tile), n % (height // tile)
        at = pl.ds(pl.multiple_of(rows + t * tile, 16), tile)
        into[o, at, :] = (
            into[o, at, :].astype(F32) + term[o, pl.ds(pl.multiple_of(t * tile, 16), tile), :].astype(F32)
        ).astype(BF16)
        return 0

    lax.fori_loop(0, owners * (height // tile), body, 0)


def reduce_kernel(count, teams, *refs):
    ring = lax.axis_size("ctx")
    d, z = lax.axis_index("dp"), lax.axis_index("ctx")
    core, x, y, core_id, x_id, y_id = plane(d)
    far_id = x_id + y_id - d
    half = ring // 2
    grads, (small, mixed, back) = refs[:count], refs[count : count + 3]
    refs = refs[count + 3 :]
    sums, (small_out, ret_mixed, ret_back) = refs[:count], refs[count : count + 3]
    refs = refs[count + 3 :]
    bufs = [refs[6 * a : 6 * a + 6] for a in range(count)]
    small_acc, small_in = refs[6 * count : 6 * count + 2]
    send, recv, load, s_send, s_recv, r_send, r_recv, r_local = refs[6 * count + 2 :]
    batch, piece = ret_mixed.shape[:2]

    def remote(src, dst, send_sem, recv_sem, dp, ctx):
        return pltpu.make_async_remote_copy(
            src_ref=src, dst_ref=dst, send_sem=send_sem, recv_sem=recv_sem, device_id=(dp, ctx), device_id_type=MESH
        )

    def team_id(t):
        bit = d // (8 << t) % 2
        return d + (8 << t) * (1 - 2 * bit)

    barrier = pltpu.get_barrier_semaphore()
    partners = [core_id, x_id, y_id, far_id] + [team_id(t) for t in range(teams)]
    for k in range(1, ring):
        pl.semaphore_signal(barrier, inc=1, device_id=(d, (z + k) % ring), device_id_type=MESH)
    for other in partners:
        pl.semaphore_signal(barrier, inc=1, device_id=(other, z), device_id_type=MESH)
    pl.semaphore_wait(barrier, ring - 1 + len(partners))

    def returned(which, i, to):
        source, target = ((mixed, ret_mixed), (back, ret_back))[which]
        return source.at[pl.ds(pl.multiple_of(to * piece, 16), piece), :], target.at[i]

    mine = z - core
    is_home = (mine >= 0) & (mine < batch)

    def start_returns():
        for which in range(2):
            for i in range(batch):
                @pl.when(mine == i)
                def _(which=which, i=i):
                    for k in range(1, ring):
                        to = (z + k) % ring
                        src, dst = returned(which, i, to)
                        remote(src, dst, r_send.at[which, k], r_recv.at[which, i], d, to).start()
                    src, dst = returned(which, i, z)
                    pltpu.make_async_copy(src, dst, r_local.at[which]).start()

    def wait_returns():
        for which in range(2):
            for i in range(batch):
                src, dst = returned(which, i, z)

                @pl.when(mine == i)
                def _(which=which, i=i, src=src, dst=dst):
                    for k in range(1, ring):
                        to = (z + k) % ring
                        remote(*returned(which, i, to), r_send.at[which, k], r_recv.at[which, i], d, to).wait_send()
                    pltpu.make_async_copy(src, dst, r_local.at[which]).wait()

                @pl.when(mine != i)
                def _(which=which, i=i, src=src, dst=dst):
                    remote(src, dst, r_send.at[which, 0], r_recv.at[which, i], core_id, z).wait_recv()

    def sizes(a):
        rows, columns = sums[a].shape
        return rows, columns // 2

    def slice_of(order, xx, yy):
        return (1 - order) * (2 * xx + yy) + order * (2 * yy + xx)

    bits = ((x, y), (y, x))
    ids = ((x_id, y_id), (y_id, x_id))

    def core_copy(a):
        rows, span = sizes(a)
        away = pl.ds(pl.multiple_of((1 - core) * span, 128), span)
        return remote(grads[a].at[:, :, away], bufs[a][1], send.at[a, 0], recv.at[a, 0], core_id, z)

    def core_load(a):
        rows, span = sizes(a)
        keep = pl.ds(pl.multiple_of(core * span, 128), span)
        return pltpu.make_async_copy(grads[a].at[:, :, keep], bufs[a][0], load.at[a])

    def first_copy(a, order):
        rows, span = sizes(a)
        own = pl.ds(order * half, half)
        away = pl.ds(pl.multiple_of((1 - bits[order][0]) * (rows // 2), 16), rows // 2)
        return remote(
            bufs[a][0].at[own, away, :], bufs[a][2].at[own], send.at[a, 1 + order], recv.at[a, 1 + order],
            ids[order][0], z,
        )

    def second_copy(a, order):
        rows, span = sizes(a)
        own = pl.ds(order * half, half)
        away = bits[order][0] * (rows // 2) + (1 - bits[order][1]) * (rows // 4)
        return remote(
            bufs[a][0].at[own, pl.ds(pl.multiple_of(away, 16), rows // 4), :], bufs[a][3].at[own],
            send.at[a, 3 + order], recv.at[a, 3 + order], ids[order][1], z,
        )

    def quarter(a, owner):
        rows, span = sizes(a)
        at = slice_of(owner // half, x, y) * (rows // 4)
        return bufs[a][0].at[owner, pl.ds(pl.multiple_of(at, 16), rows // 4), :]

    def owner_copy(a, k):
        to = (z + k) % ring
        return remote(quarter(a, to), bufs[a][4].at[k - 1], send.at[a, 4 + k], recv.at[a, 4 + k], d, to)

    def team_copy(a, t):
        j = 4 + ring + 7 + t
        return remote(bufs[a][5].at[0], bufs[a][5].at[1 + t], send.at[a, j], recv.at[a, j], team_id(t), z)

    spots = ((x, y), (1 - x, y), (x, 1 - y), (1 - x, 1 - y))

    def final(a, spot, side):
        rows, span = sizes(a)
        at = slice_of(z // half, *spots[spot]) * (rows // 4)
        return sums[a].at[
            pl.ds(pl.multiple_of(at, 16), rows // 4), pl.ds(pl.multiple_of(side * span, 128), span)
        ]

    def spread(a, j):
        s, r = send.at[a, 4 + ring + j - 1], recv.at[a, 4 + ring + j - 1]
        if j < 4:
            return remote(bufs[a][5].at[0], final(a, 0, core), s, r, (x_id, y_id, far_id)[j - 1], z)
        src = bufs[a][5].at[0] if j == 4 else final(a, j - 4, core)
        return remote(src, final(a, j - 4, core), s, r, core_id, z)

    def spread_here(a, j):
        s, r = send.at[a, 4 + ring + j - 1], recv.at[a, 4 + ring + j - 1]
        ref = final(a, j, core) if j < 4 else final(a, j - 4, 1 - core)
        remote(ref, ref, s, r, core_id, z).wait_recv()

    def keep(a):
        return pltpu.make_async_copy(bufs[a][5].at[0], final(a, 0, core), load.at[count + a])

    def add_slices(target, terms):
        rows = target.shape[0]
        for t in range(rows // 48):
            at = pl.ds(t * 48, 48)
            total = terms[0][at, :].astype(F32)
            for term in terms[1:]:
                total += term[at, :].astype(F32)
            target[at, :] = total.astype(BF16)

    def stage_0(a):
        core_copy(a).start()
        core_load(a).start()

    def stage_1(a):
        core_load(a).wait()
        core_copy(a).wait_recv()
        fold(bufs[a][0], 0, bufs[a][1])
        for order in range(2):
            first_copy(a, order).start()

    def stage_2(a):
        rows, span = sizes(a)
        for order in range(2):
            own = pl.ds(order * half, half)
            first_copy(a, order).wait_recv()
            fold(bufs[a][0].at[own], bits[order][0] * (rows // 2), bufs[a][2].at[own])
            second_copy(a, order).start()

    def stage_3(a):
        rows, span = sizes(a)
        for order in range(2):
            own = pl.ds(order * half, half)
            second_copy(a, order).wait_recv()
            at = slice_of(order, x, y) * (rows // 4)
            fold(bufs[a][0].at[own], at, bufs[a][3].at[own])
        for k in range(1, ring):
            owner_copy(a, k).start()

    def stage_4(a):
        for k in range(1, ring):
            owner_copy(a, k).wait_recv()
        result = bufs[a][5].at[0]
        add_slices(result, [quarter(a, z)] + [bufs[a][4].at[k] for k in range(ring - 1)])
        for t in range(teams):
            team_copy(a, t).start()
            team_copy(a, t).wait()
            add_slices(result, [result, bufs[a][5].at[1 + t]])
        keep(a).start()
        for j in range(1, 5):
            spread(a, j).start()

    def stage_5(a):
        for j in range(1, 4):
            spread_here(a, j)
            spread(a, 4 + j).start()

    def stage_6(a):
        for j in range(4, 8):
            spread_here(a, j)
        core_copy(a).wait_send()
        for order in range(2):
            first_copy(a, order).wait_send()
            second_copy(a, order).wait_send()
        for k in range(1, ring):
            owner_copy(a, k).wait_send()
        for j in range(1, 8):
            spread(a, j).wait_send()
        keep(a).wait()

    steps = [core_id, x_id, y_id] + [team_id(t) for t in range(teams)]

    def small_copy(n):
        return remote(small_acc, small_in.at[n], s_send.at[n], s_recv.at[n], steps[n], z)

    def small_owner(k):
        n = len(steps) + k - 1
        return remote(small_acc, small_in.at[n], s_send.at[n], s_recv.at[n], d, (z + k) % ring)

    def small_step(n):
        if n < len(steps):
            if n == 0:
                small_acc[...] = small[...]
            small_copy(n).start()
        elif n == len(steps):
            for k in range(1, ring):
                small_owner(k).start()

    def small_close(n):
        if n < len(steps):
            small_copy(n).wait()
            small_acc[...] += small_in[n]
        elif n == len(steps):
            for k in range(1, ring):
                small_owner(k).wait()
            total = small_acc[...]
            for k in range(ring - 1):
                total += small_in[len(steps) + k]
            small_out[...] = total

    stages = (stage_0, stage_1, stage_2, stage_3, stage_4, stage_5, stage_6)
    for a in range(count):
        stage_0(a)
    start_returns()
    for n in range(1, max(len(stages), len(steps) + 2)):
        small_step(n - 1)
        if n < len(stages):
            for a in range(count):
                stages[n](a)
        small_close(n - 1)
    wait_returns()


def reduce_all(grads, small, mixed, back, batch):
    ring, groups = lax.axis_size("ctx"), lax.axis_size("dp")
    teams = (groups // 8).bit_length() - 1
    count = len(grads)
    grads = [g.reshape(ring, -1, g.shape[1]) for g in grads]
    length, width = mixed.shape
    dma = pltpu.SemaphoreType.DMA
    anywhere = pl.BlockSpec(memory_space=pl.ANY)
    vmem = pl.BlockSpec(memory_space=pltpu.VMEM)
    scratch = []
    for g in grads:
        _, rows, columns = g.shape
        span = columns // 2
        scratch += [
            pltpu.VMEM((ring, rows, span), BF16),
            pltpu.VMEM((ring, rows, span), BF16),
            pltpu.VMEM((ring, rows // 2, span), BF16),
            pltpu.VMEM((ring, rows // 4, span), BF16),
            pltpu.VMEM((ring - 1, rows // 4, span), BF16),
            pltpu.VMEM((1 + teams, rows // 4, span), BF16),
        ]
    rounds = 3 + teams + ring - 1
    scratch += [pltpu.VMEM(small.shape, F32), pltpu.VMEM((rounds, *small.shape), F32)]
    copies = 4 + ring + 7 + teams
    scratch += [
        dma((count, copies)), dma((count, copies)), dma((2 * count,)), dma((rounds,)), dma((rounds,)),
        dma((2, ring)), dma((2, batch)), dma((2,)),
    ]
    token = jax.ShapeDtypeStruct((batch, length // ring, width), BF16)
    return pl.pallas_call(
        functools.partial(reduce_kernel, count, teams),
        in_specs=[anywhere] * count + [vmem, anywhere, anywhere],
        out_specs=[anywhere] * count + [vmem, anywhere, anywhere],
        out_shape=[jax.ShapeDtypeStruct(g.shape[1:], BF16) for g in grads]
        + [jax.ShapeDtypeStruct(small.shape, F32), token, token],
        scratch_shapes=scratch,
        compiler_params=pltpu.CompilerParams(collective_id=1, has_side_effects=True, vmem_limit_bytes=56 * MIB),
        cost_estimate=pl.CostEstimate(flops=0, bytes_accessed=60 * MIB, transcendentals=0),
        name="reduce",
    )(*grads, small, mixed, back)


def feed_kernel(
    x_ref, g_ref, norm_ref, bias_ref, up_ref, down_ref,
    out_ref, h_ref, dup_ref, ddown_ref, dbias_ref, small_ref,
    m_ref, hid_ref, dup_in_ref, acc_ref, dm_ref,
):
    step = pl.program_id(0)
    last = pl.num_programs(0) - 1
    rows, width = x_ref.shape
    tile = 256
    tiles = rows // tile

    @pl.when(step == 0)
    def _():
        for t in range(tiles):
            at = pl.ds(t * tile, tile)
            xh, _ = normalized(x_ref[at, :].astype(F32))
            m_ref[at, :] = (xh * norm_ref[2:3, :] + norm_ref[3:4, :]).astype(BF16)
        acc_ref[...] = jnp.zeros_like(acc_ref)
        dm_ref[...] = jnp.zeros_like(dm_ref)

    up = up_ref[...]
    down = down_ref[...]
    total = jnp.zeros(dbias_ref.shape, F32)
    for t in range(tiles):
        at = pl.ds(t * tile, tile)
        u = dot(m_ref[at, :], up) + bias_ref[...]
        cdf = 0.5 * (1.0 + lax.erf(u * (1.0 / math.sqrt(2.0))))
        hidden = (u * cdf).astype(BF16)
        slope = cdf + u * jnp.exp(-0.5 * u * u) * (1.0 / math.sqrt(2.0 * math.pi))
        back = (dot(g_ref[at, :], down, NT) * slope).astype(BF16)
        hid_ref[at, :] = hidden
        dup_in_ref[at, :] = back
        total += jnp.sum(back.astype(F32), axis=0, keepdims=True)
        acc_ref[at, :] += dot(hidden, down)
        dm_ref[at, :] += dot(back, up, NT)
    dbias_ref[...] = total
    ddown_ref[...] = dot(hid_ref[...], g_ref[...], TN).astype(BF16)
    dup_ref[...] = dot(m_ref[...], dup_in_ref[...], TN).astype(BF16)

    @pl.when(step == last)
    def _():
        gain = jnp.zeros((1, width), F32)
        shift = jnp.zeros((1, width), F32)
        sums = jnp.zeros((1, width), F32)
        for t in range(tiles):
            at = pl.ds(t * tile, tile)
            xh, _ = normalized(x_ref[at, :].astype(F32))
            dm = dm_ref[at, :]
            gain += jnp.sum(dm * xh, axis=0, keepdims=True)
            shift += jnp.sum(dm, axis=0, keepdims=True)
            sums += jnp.sum(g_ref[at, :].astype(F32), axis=0, keepdims=True)
            h_ref[at, :] = dm * norm_ref[2:3, :]
            out_ref[at, :] = acc_ref[at, :]
        small_ref[0:1, :] = gain
        small_ref[1:2, :] = shift
        small_ref[2:3, :] = sums


def feed(x, g, norms, bias_up, up, down):
    rows, width = x.shape
    ff = up.shape[1]
    chunk = 512
    whole = lambda shape: pl.BlockSpec(shape, lambda i: (0,) * len(shape))
    return pl.pallas_call(
        feed_kernel,
        grid=(ff // chunk,),
        in_specs=[
            whole((rows, width)),
            whole((rows, width)),
            whole(norms.shape),
            pl.BlockSpec((1, chunk), lambda i: (0, i)),
            pl.BlockSpec((width, chunk), lambda i: (0, i)),
            pl.BlockSpec((chunk, width), lambda i: (i, 0)),
        ],
        out_specs=[
            whole((rows, width)),
            whole((rows, width)),
            pl.BlockSpec((width, chunk), lambda i: (0, i)),
            pl.BlockSpec((chunk, width), lambda i: (i, 0)),
            pl.BlockSpec((1, chunk), lambda i: (0, i)),
            whole((8, width)),
        ],
        out_shape=[
            jax.ShapeDtypeStruct((rows, width), F32),
            jax.ShapeDtypeStruct((rows, width), F32),
            jax.ShapeDtypeStruct((width, ff), BF16),
            jax.ShapeDtypeStruct((ff, width), BF16),
            jax.ShapeDtypeStruct((1, ff), F32),
            jax.ShapeDtypeStruct((8, width), F32),
        ],
        scratch_shapes=[
            pltpu.VMEM((rows, width), BF16),
            pltpu.VMEM((rows, chunk), BF16),
            pltpu.VMEM((rows, chunk), BF16),
            pltpu.VMEM((rows, width), F32),
            pltpu.VMEM((rows, width), F32),
        ],
        compiler_params=pltpu.CompilerParams(vmem_limit_bytes=56 * MIB),
        cost_estimate=pl.CostEstimate(
            flops=12 * rows * width * ff, bytes_accessed=8 * width * ff, transcendentals=rows * ff
        ),
        name="feed",
    )(x, g, norms, bias_up, up, down)


def attend_kernel(
    order_ref, x_ref, stored_g_ref, norm_ref, bias_ref, cos_ref, low_ref, high_ref, wq_ref, wk_ref, wv_ref, wo_ref,
    out_ref, h_ref, dq_ref, dk_ref, dv_ref, dwo_ref, dbias_ref, small_ref,
    g_ref, a_ref, acc_ref, da_ref, q_ref, k_ref, v_ref, do_ref, o_ref, dqs_ref, dks_ref, dvs_ref,
):
    step = pl.program_id(0)
    last = pl.num_programs(0) - 1
    rows, width = x_ref.shape
    lanes = QUAD * HD
    tile = 256
    half = ROT // 2
    scale = 1.0 / math.sqrt(HD)
    blocks = rows // BLOCK
    mine = lax.axis_index("ctx") - lax.axis_index("dp") % 2
    is_home = (mine >= 0) & (mine < SEQS)

    def stored(ref, at):
        values = ref[pl.ds(pl.multiple_of(at * BLOCK, BLOCK), BLOCK), :]
        return jnp.where(is_home, values, jnp.zeros_like(values))

    @pl.when(step == 0)
    def _():
        for j in range(blocks):
            place = 0
            for s in range(blocks):
                place = place + jnp.where(order_ref[s] == j, s, 0)
            at = pl.ds(j * BLOCK, BLOCK)
            xh, _ = normalized(stored(x_ref, place).astype(F32))
            a_ref[at, :] = (xh * norm_ref[0:1, :] + norm_ref[1:2, :]).astype(BF16)
            g_ref[at, :] = stored(stored_g_ref, place)
        acc_ref[...] = jnp.zeros_like(acc_ref)
        da_ref[...] = jnp.zeros_like(da_ref)

    def table(ref, at):
        values = ref[at, :]
        return jnp.concatenate([values] * (lanes // values.shape[1]), axis=1)

    def turn(values, at):
        low = pltpu.roll(values, lanes - half, 1) * table(low_ref, at)
        high = pltpu.roll(values, half, 1) * table(high_ref, at)
        return values * table(cos_ref, at), low + high

    for t in range(rows // tile):
        at = pl.ds(t * tile, tile)
        a = a_ref[at, :]
        same, cross = turn(dot(a, wq_ref[...]) + bias_ref[...], at)
        q_ref[at, :] = ((same + cross).astype(BF16) * scale).astype(BF16)
        same, cross = turn(dot(a, wk_ref[...]), at)
        k_ref[at, :] = (same + cross).astype(BF16)
        v_ref[at, :] = dot(a, wv_ref[...]).astype(BF16)
        do_ref[at, :] = dot(g_ref[at, :], wo_ref[...], NT).astype(BF16)

    dks_ref[...] = jnp.zeros_like(dks_ref)
    dvs_ref[...] = jnp.zeros_like(dvs_ref)
    head_of = lax.broadcasted_iota(jnp.int32, (BLOCK, lanes), 1) // HD

    def stack(values):
        zero = jnp.zeros_like(values)
        return jnp.concatenate([jnp.where(head_of == e, values, zero) for e in range(QUAD)], axis=0)

    def merge(values):
        out = values[:BLOCK]
        for e in range(1, QUAD):
            out = jnp.where(head_of == e, values[e * BLOCK : (e + 1) * BLOCK], out)
        return out

    spot = lax.broadcasted_iota(jnp.int32, (QUAD * BLOCK, BLOCK), 0) % BLOCK
    admitted = lax.broadcasted_iota(jnp.int32, (QUAD * BLOCK, BLOCK), 1) <= spot
    for b in range(rows // BLOCK):
        at = pl.ds(b * BLOCK, BLOCK)
        seen = pl.ds(0, (b + 1) * BLOCK)
        q = stack(q_ref[at, :])
        do_block = do_ref[at, :]
        do = stack(do_block)
        keys = k_ref[seen, :]
        values = v_ref[seen, :]
        scores = dot(q, keys, NT)
        edge = jnp.where(admitted, scores[:, b * BLOCK :], -1e30)
        scores = edge if b == 0 else jnp.concatenate([scores[:, : b * BLOCK], edge], axis=1)
        top = jnp.max(scores, axis=-1, keepdims=True)
        expo = jnp.exp(scores - top)
        probs = expo * (1.0 / jnp.sum(expo, axis=-1, keepdims=True))
        low = probs.astype(BF16)
        mixed = dot(low, values)
        o_ref[at, :] = merge(mixed).astype(BF16)
        share = jnp.sum(mixed * do.astype(F32), axis=-1, keepdims=True)
        back = (probs * (dot(do, values, NT) - share)).astype(BF16)
        dqs_ref[at, :] = merge(dot(back, keys)) * scale
        dks_ref[seen, :] += dot(back, q, TN)
        dvs_ref[seen, :] += dot(low, do, TN)

    total = jnp.zeros((1, lanes), F32)
    for t in range(rows // tile):
        at = pl.ds(t * tile, tile)
        same, cross = turn(dqs_ref[at, :], at)
        dq = (same - cross).astype(BF16)
        same, cross = turn(dks_ref[at, :], at)
        dk = (same - cross).astype(BF16)
        dv = dvs_ref[at, :].astype(BF16)
        total += jnp.sum(dq.astype(F32), axis=0, keepdims=True)
        q_ref[at, :] = dq
        k_ref[at, :] = dk
        v_ref[at, :] = dv
        acc_ref[at, :] += dot(o_ref[at, :], wo_ref[...])
        da_ref[at, :] += dot(dq, wq_ref[...], NT) + dot(dk, wk_ref[...], NT) + dot(dv, wv_ref[...], NT)
    dbias_ref[...] = total
    dwo_ref[...] = dot(o_ref[...], g_ref[...], TN).astype(BF16)
    dq_ref[...] = dot(a_ref[...], q_ref[...], TN).astype(BF16)
    dk_ref[...] = dot(a_ref[...], k_ref[...], TN).astype(BF16)
    dv_ref[...] = dot(a_ref[...], v_ref[...], TN).astype(BF16)

    @pl.when(step == last)
    def _():
        gain = jnp.zeros((1, width), F32)
        shift = jnp.zeros((1, width), F32)
        for s in range(blocks):
            at = pl.ds(s * BLOCK, BLOCK)
            sorted_at = pl.ds(pl.multiple_of(order_ref[s] * BLOCK, BLOCK), BLOCK)
            xh, _ = normalized(stored(x_ref, s).astype(F32))
            da = da_ref[sorted_at, :]
            gain += jnp.sum(da * xh, axis=0, keepdims=True)
            shift += jnp.sum(da, axis=0, keepdims=True)
            h_ref[at, :] = (da * norm_ref[0:1, :]).astype(BF16)
            out_ref[at, :] = acc_ref[sorted_at, :].astype(BF16)
        small_ref[0:1, :] = gain
        small_ref[1:2, :] = shift


def attend(order, x, g, norms, bias_q, tables, weights):
    rows, width = x.shape
    lanes = QUAD * HD
    groups = width // lanes
    whole = lambda shape: pl.BlockSpec(shape, lambda i: (0,) * len(shape))
    column = pl.BlockSpec((width, lanes), lambda i: (0, i))
    small = jax.ShapeDtypeStruct((rows, width), BF16)
    return pl.pallas_call(
        attend_kernel,
        grid=(groups,),
        in_specs=[
            pl.BlockSpec(memory_space=pltpu.SMEM),
            whole((rows, width)),
            whole((rows, width)),
            whole(norms.shape),
            pl.BlockSpec((1, lanes), lambda i: (0, i)),
            whole(tables[0].shape),
            whole(tables[0].shape),
            whole(tables[0].shape),
            pl.BlockSpec((width, lanes), lambda i: (0, i)),
            pl.BlockSpec((width, lanes), lambda i: (0, groups + i)),
            pl.BlockSpec((width, lanes), lambda i: (0, 2 * groups + i)),
            pl.BlockSpec((lanes, width), lambda i: (i, 3)),
        ],
        out_specs=[
            whole((rows, width)),
            whole((rows, width)),
            column,
            column,
            column,
            pl.BlockSpec((lanes, width), lambda i: (i, 0)),
            pl.BlockSpec((1, lanes), lambda i: (0, i)),
            whole((8, width)),
        ],
        out_shape=[
            small,
            small,
            jax.ShapeDtypeStruct((width, width), BF16),
            jax.ShapeDtypeStruct((width, width), BF16),
            jax.ShapeDtypeStruct((width, width), BF16),
            jax.ShapeDtypeStruct((width, width), BF16),
            jax.ShapeDtypeStruct((1, width), F32),
            jax.ShapeDtypeStruct((8, width), F32),
        ],
        scratch_shapes=[
            pltpu.VMEM((rows, width), BF16),
            pltpu.VMEM((rows, width), BF16),
            pltpu.VMEM((rows, width), F32),
            pltpu.VMEM((rows, width), F32),
        ]
        + [pltpu.VMEM((rows, lanes), BF16)] * 5
        + [pltpu.VMEM((rows, lanes), F32)] * 3,
        compiler_params=pltpu.CompilerParams(vmem_limit_bytes=56 * MIB),
        cost_estimate=pl.CostEstimate(
            flops=24 * rows * width * width + 8 * rows * rows * width,
            bytes_accessed=16 * width * width + 8 * rows * width,
            transcendentals=HEADS * rows * rows // 2,
        ),
        name="attend",
    )(order, x, g, norms, bias_q, *tables, weights, weights, weights, weights)


def rotary_tables(length):
    half = ROT // 2
    frequency = ROPE_BASE ** (-(np.arange(half) * 2.0 / ROT))
    angle = np.arange(length)[:, None] * frequency[None, :]
    cosine, sine = np.cos(angle), np.sin(angle)
    rest = np.zeros((length, HD - ROT))
    none = np.zeros_like(sine)
    cos_full = np.concatenate([cosine, cosine, rest + 1.0], axis=1)
    low = np.concatenate([-sine, none, rest], axis=1)
    high = np.concatenate([none, sine, rest], axis=1)
    return tuple(jnp.asarray(np.tile(t, (1, 2)).astype(np.float32)) for t in (cos_full, low, high))


def adamw(weight, grad, first, second, rate, decay):
    first_new = BETA_ONE * first + (1.0 - BETA_ONE) * grad
    second_new = BETA_TWO * second + (1.0 - BETA_TWO) * grad * grad
    first_hat = first_new / (1.0 - BETA_ONE**STEP)
    second_hat = second_new / (1.0 - BETA_TWO**STEP)
    weight_new = weight - rate * (first_hat / (jnp.sqrt(second_hat) + EPS_ADAM) + decay * weight)
    return (first_new, second_new, weight_new)


def shards(
    tokens, out_grad, block_order, qkv_weight, out_weight, up_weight, down_weight, norm_params, bias_params,
    qkv_first, qkv_second, out_first, out_second, up_first, up_second, down_first, down_second,
    norm_first, norm_second, bias_first, bias_second,
):
    groups, ring = lax.axis_size("dp"), lax.axis_size("ctx")
    group, rank = lax.axis_index("dp"), lax.axis_index("ctx")
    batch, piece, width = tokens.shape
    length = piece * ring
    count = batch * piece
    ff = up_weight.shape[1]

    att_weight = jnp.concatenate([qkv_weight, out_weight], axis=1).astype(BF16)
    small = jnp.concatenate([norm_params.reshape(-1), bias_params]).astype(BF16).astype(F32)
    entries = small.shape[0]
    small = jnp.pad(small, (0, -entries % 1024)).reshape(-1, 128)
    up_copy, down_copy, att_copy, small_all, home_x, home_g = gather_all(
        up_weight.astype(BF16), down_weight.astype(BF16), att_weight, small, tokens, out_grad
    )
    small_all = small_all.reshape(ring, -1)[:, :entries]
    norms = small_all[:, : 4 * width // ring].reshape(ring, 4, width // ring).transpose(1, 0, 2).reshape(4, width)
    biases = small_all[:, 4 * width // ring :].reshape(1, -1)

    odd = group % 2

    order = block_order[jnp.clip(rank - odd, 0, batch - 1)]

    x_rows, g_rows = tokens.reshape(count, width), out_grad.reshape(count, width)
    feed_out, h_feed, dup, ddown, dbias_up, small_feed = feed(
        x_rows, g_rows, norms, biases[:, 2 * width : 2 * width + ff], up_copy, down_copy
    )
    attend_out, h_attend, dq, dk, dv, dout, dbias_q, small_attend = attend(
        order, home_x, home_g, norms, biases[:, :width], rotary_tables(length), att_copy
    )

    dqkv = jnp.concatenate([dq, dk, dv], axis=1)
    tail = jnp.concatenate(
        [small_attend[:2].reshape(-1), small_feed[:2].reshape(-1), dbias_q[0], small_feed[2], dbias_up[0], small_feed[2]]
    )
    entries = tail.shape[0]
    tail = jnp.pad(tail, (0, -entries % 1024)).reshape(-1, 128)
    *owned, tail, ret_mixed, ret_back = reduce_all((dup, ddown, dqkv, dout), tail, attend_out, h_attend, batch)
    up_grad, down_grad, qkv_grad, out_grads = (g.astype(F32) for g in owned)
    tail = tail.reshape(-1)[:entries]
    returned = [v.reshape(count, width).astype(F32) for v in (ret_mixed, ret_back)]

    rows = x_rows.astype(F32)
    bias_rows = biases[:, width : 2 * width] + biases[:, 2 * width + ff :]
    layer_out = (rows + returned[0] + feed_out + bias_rows).astype(BF16).reshape(batch, piece, width)
    xh, scale = normalized(rows)
    h = returned[1] + h_feed
    inner = jnp.mean(h * xh, axis=-1, keepdims=True)
    input_grad = g_rows.astype(F32) + scale * (h - jnp.mean(h, axis=-1, keepdims=True) - xh * inner)
    input_grad = input_grad.reshape(batch, piece, width)

    norm_grad = lax.dynamic_slice_in_dim(tail[: 4 * width].reshape(4, width), rank * (width // ring), width // ring, 1)
    share = bias_params.shape[0]
    bias_grad = lax.dynamic_slice_in_dim(tail[4 * width :], rank * share, share, 0)

    qkv_new = adamw(qkv_weight, qkv_grad, qkv_first, qkv_second, 0.1, DECAY)
    out_new = adamw(out_weight, out_grads, out_first, out_second, 0.6, DECAY)
    up_new = adamw(up_weight, up_grad, up_first, up_second, 0.1, DECAY)
    down_new = adamw(down_weight, down_grad, down_first, down_second, 0.05, DECAY)
    norm_new = adamw(norm_params, norm_grad, norm_first, norm_second, 0.6, 0.0)
    bias_new = adamw(bias_params, bias_grad, bias_first, bias_second, 0.6, 0.0)
    return (
        layer_out, input_grad, *qkv_new, *out_new, *up_new, *down_new,
        norm_new[0], norm_new[1][:2], norm_new[1][2:], norm_new[2], *bias_new,
    )


def solution(mesh):
    rows, columns, token = P("ctx", None), P(None, "ctx"), P("dp", "ctx", None)
    in_specs = (token, token, P("dp", None)) + (rows,) * 4 + (columns, P("ctx")) + (rows,) * 8
    in_specs += (columns, columns, P("ctx"), P("ctx"))
    out_specs = (token, token) + (rows,) * 12 + (columns,) * 4 + (P("ctx"),) * 3
    return jax.shard_map(shards, mesh=mesh, in_specs=in_specs, out_specs=out_specs, check_vma=False)
```

```python
import functools
import math

import jax
import jax.numpy as jnp
import numpy as np
from jax import lax
from jax.experimental import pallas as pl
from jax.experimental.pallas import tpu as pltpu
from jax.sharding import PartitionSpec as P

HEADS = 12
HD = 64
STEP = 10
ROT = 16
SEQS = 3
BLOCK = 128
QUAD = 4

EPS_NORM = 1e-05
BETA_ONE = 0.9
BETA_TWO = 0.95
EPS_ADAM = 1e-08
DECAY = 0.01
ROPE_BASE = 10000.0
F32 = jnp.float32
BF16 = jnp.bfloat16
MIB = 1024 * 1024


def dot(left, right, dims=((1,), (0,))):
    return lax.dot_general(left, right, (dims, ((), ())), preferred_element_type=F32)


NN = ((1,), (0,))
NT = ((1,), (1,))
TN = ((0,), (0,))


def normalized(values):
    mean = jnp.mean(values, axis=-1, keepdims=True)
    centred = values - mean
    variance = jnp.mean(centred * centred, axis=-1, keepdims=True)
    scale = lax.rsqrt(variance + EPS_NORM)
    return centred * scale, scale


MESH = pl.DeviceIdType.MESH


def plane(d):
    core, x, y = d % 2, d // 2 % 2, d // 4 % 2
    return core, x, y, d + 1 - 2 * core, d + 2 - 4 * x, d + 4 - 8 * y


def gather_kernel(
    up, down, att, small, tokens, cotangents,
    att_all, small_all, home_x, home_g, out_ref, h_ref, dup_all, ddown_all, dbias_ref, sums_ref,
    up_all, down_all, small_in, x_ref, g_ref, m_ref, hid_ref, dup_in_ref, dup_ref, ddown_ref,
    z_send, z_recv, p_send, p_recv, s_send, s_recv, t_send, t_recv, local, out_sem,
):
    ring = lax.axis_size("ctx")
    d, z = lax.axis_index("dp"), lax.axis_index("ctx")
    core, x, y, core_id, x_id, y_id = plane(d)
    own = x + 2 * y
    own_x, own_y, far = own + 1 - 2 * x, own + 2 - 4 * y, 3 - own
    count, width = tokens.shape
    piece = home_x.shape[0] // ring
    batch = count // piece
    arrays = ((up, up_all, False), (down, down_all, True), (att, att_all, False))

    def slot(a, base, place, half=None):
        source, whole, tall = arrays[a]
        ref = source if base is None else whole
        rows, columns = source.shape
        at = 0 if base is None else base * rows
        height, span = rows // 4, columns // 2
        at = at + place * height
        column = core * span
        if half is not None:
            if tall:
                height = height // 2
                at = at + half * height
            else:
                span = span // 2
                column = column + half * span
        return ref.at[pl.ds(pl.multiple_of(at, 16), height), pl.ds(pl.multiple_of(column, 128), span)]

    def other_slot(a, base, place):
        source, whole, tall = arrays[a]
        rows, columns = source.shape
        at = pl.multiple_of(base * rows + place * (rows // 4), 16)
        column = pl.multiple_of((1 - core) * (columns // 2), 128)
        return whole.at[pl.ds(at, rows // 4), pl.ds(column, columns // 2)]

    def remote(src, dst, send, recv, dp, ctx):
        return pltpu.make_async_remote_copy(
            src_ref=src, dst_ref=dst, send_sem=send, recv_sem=recv, device_id=(dp, ctx), device_id_type=MESH
        )

    barrier = pltpu.get_barrier_semaphore()
    for k in range(1, ring):
        pl.semaphore_signal(barrier, inc=1, device_id=(d, (z + k) % ring), device_id_type=MESH)
    for other in (core_id, x_id, y_id):
        pl.semaphore_signal(barrier, inc=1, device_id=(other, z), device_id_type=MESH)
    pl.semaphore_wait(barrier, ring + 2)

    def hop(a, way, h):
        shard = z - h if way == 0 else z + h
        target = z + 1 if way == 0 else z - 1
        src = slot(a, None, own) if h == 0 else slot(a, shard, own)
        return remote(src, slot(a, shard, own), z_send.at[a, way, h], z_recv.at[a, way, h], d, target)

    def can_send(way, h):
        shard = z - h if way == 0 else z + h
        target = z + 1 if way == 0 else z - 1
        return (shard >= 0) & (shard < ring) & (target >= 0) & (target < ring)

    def in_range(way, h):
        shard = z - h if way == 0 else z + h
        return (shard >= 0) & (shard < ring)

    def cast(a, shard, j):
        send, recv = p_send.at[a, shard, j], p_recv.at[a, shard, j]
        if j == 0:
            ref = slot(a, shard, own)
            return remote(ref, ref, send, recv, x_id, z)
        if j == 1:
            ref = slot(a, shard, own)
            return remote(ref, ref, send, recv, y_id, z)
        if j == 2:
            ref = slot(a, shard, own_x, 0)
            return remote(ref, ref, send, recv, y_id, z)
        if j == 3:
            ref = slot(a, shard, own_y, 1)
            return remote(ref, ref, send, recv, x_id, z)
        ref = slot(a, shard, (own, own_x, own_y, far)[j - 4])
        return remote(ref, ref, send, recv, core_id, z)

    def arrived(a, shard, j):
        send, recv = p_send.at[a, shard, j], p_recv.at[a, shard, j]
        ref = {0: lambda: slot(a, shard, own_x), 1: lambda: slot(a, shard, own_y),
               2: lambda: slot(a, shard, far, 0), 3: lambda: slot(a, shard, far, 1)}.get(
            j, lambda: other_slot(a, shard, (own, own_x, own_y, far)[j - 4]))()
        remote(ref, ref, send, recv, core_id, z).wait_recv()

    def start_hops(a):
        for way in range(2):
            @pl.when(can_send(way, 0))
            def _(way=way):
                hop(a, way, 0).start()

    def small_copy(k):
        return remote(small, small_in.at[ring - k], s_send.at[k], s_recv.at[k], d, (z + k) % ring)

    def stage_a(a, h):
        for way in range(2):
            @pl.when(in_range(way, h))
            def _(way=way):
                shard = z - h if way == 0 else z + h
                ref = slot(a, shard, own)
                remote(ref, ref, z_send.at[a, way, h - 1], z_recv.at[a, way, h - 1], core_id, z).wait_recv()

                @pl.when(can_send(way, h))
                def _():
                    hop(a, way, h).start()

                cast(a, shard, 0).start()
                cast(a, shard, 1).start()
                cast(a, shard, 4).start()

    def stage_b(a, h):
        for way in range(2):
            @pl.when(in_range(way, h))
            def _(way=way):
                shard = z - h if way == 0 else z + h
                arrived(a, shard, 0)
                cast(a, shard, 2).start()
                cast(a, shard, 5).start()
                arrived(a, shard, 1)
                cast(a, shard, 3).start()
                cast(a, shard, 6).start()

    def stage_c(a, h):
        for way in range(2):
            @pl.when(in_range(way, h))
            def _(way=way):
                shard = z - h if way == 0 else z + h
                arrived(a, shard, 2)
                arrived(a, shard, 3)
                cast(a, shard, 7).start()

    def stage_d(a, h):
        for way in range(2):
            @pl.when(in_range(way, h))
            def _(way=way):
                shard = z - h if way == 0 else z + h
                for j in range(4, 8):
                    arrived(a, shard, j)

    pairs = ((tokens, home_x), (cotangents, home_g))

    def move(which, i):
        source, whole = pairs[which]
        src = source.at[pl.ds(i * piece, piece), :]
        dst = whole.at[pl.ds(pl.multiple_of(z * piece, 16), piece), :]
        return src, dst, i + core

    def start_moves(which):
        for i in range(batch):
            src, dst, target = move(which, i)

            @pl.when(target != z)
            def _(src=src, dst=dst, target=target, i=i):
                remote(src, dst, t_send.at[which, i], t_recv.at[which, z], d, target).start()

            @pl.when(target == z)
            def _(src=src, dst=dst):
                pltpu.make_async_copy(src, dst, local.at[6 + which]).start()

    own_copies = []
    for a in range(3):
        source, whole, _ = arrays[a]
        rows = source.shape[0]
        at = pl.ds(pl.multiple_of(z * rows, 16), rows)
        own_copies.append(pltpu.make_async_copy(source, whole.at[at, :], local.at[a]))
    x_load = pltpu.make_async_copy(tokens, x_ref, local.at[3])
    g_load = pltpu.make_async_copy(cotangents, g_ref, local.at[4])
    own_small = pltpu.make_async_copy(small, small_in.at[0], local.at[5])

    start_hops(0)
    start_hops(1)
    for k in range(1, ring):
        small_copy(k).start()
    for copy in own_copies + [x_load, g_load, own_small]:
        copy.start()
    hops = range(1, ring)
    work = [(a, h) for a in range(2) for h in hops]
    for n in range(len(work) + 2):
        if n < len(work):
            stage_a(*work[n])
        if n == len(work) - 1:
            start_moves(0)
            start_hops(2)
        if 1 <= n <= len(work):
            stage_b(*work[n - 1])
        if n >= 2:
            stage_c(*work[n - 2])
    start_moves(1)

    own_small.wait()
    for k in range(1, ring):
        ref = small_in.at[ring - k]
        remote(ref, ref, s_send.at[k], s_recv.at[k], core_id, z).wait_recv()
    x_load.wait()
    g_load.wait()
    total = small_in[0]
    for k in range(1, ring):
        total += small_in[k]
    small_all[...] = total
    ff = up_all.shape[1]
    gain_2, shift_2 = small_all[2:3, 2 * width : 3 * width], small_all[2:3, 3 * width : 4 * width]
    tile = 256
    tiles = count // tile
    for t in range(tiles):
        at = pl.ds(t * tile, tile)
        xh, _ = normalized(x_ref[at, :].astype(F32))
        m_ref[at, :] = (xh * gain_2 + shift_2).astype(BF16)
        out_ref[at, :] = jnp.zeros((tile, width), F32)
        h_ref[at, :] = jnp.zeros((tile, width), F32)
    own_copies[0].wait()
    own_copies[1].wait()
    for h in hops:
        stage_d(0, h)
        stage_d(1, h)

    chunk = dup_ref.shape[2]
    steps = ff // chunk

    def grads_out(step, which):
        at = pl.ds(pl.multiple_of(step * chunk, 128), chunk)
        spot = step % 2
        if which == 0:
            return pltpu.make_async_copy(dup_ref.at[spot], dup_all.at[:, at], out_sem.at[0, spot])
        return pltpu.make_async_copy(ddown_ref.at[spot], ddown_all.at[at, :], out_sem.at[1, spot])

    def feed_step(step, _):
        spot = step % 2
        for h in hops:
            @pl.when(step == h - 1)
            def _(h=h):
                stage_a(2, h)

            @pl.when(step == h)
            def _(h=h):
                stage_b(2, h)

            @pl.when(step == h + 1)
            def _(h=h):
                stage_c(2, h)

        @pl.when(step >= 2)
        def _():
            grads_out(step - 2, 0).wait()
            grads_out(step - 2, 1).wait()

        at_ff = pl.ds(pl.multiple_of(step * chunk, 128), chunk)
        up_part = up_all[:, at_ff]
        down_part = down_all[at_ff, :]
        bias = small_all[0:1, at_ff]
        total = jnp.zeros((1, chunk), F32)
        for t in range(tiles):
            at = pl.ds(t * tile, tile)
            u = dot(m_ref[at, :], up_part) + bias
            cdf = 0.5 * (1.0 + lax.erf(u * (1.0 / math.sqrt(2.0))))
            hidden = (u * cdf).astype(BF16)
            slope = cdf + u * jnp.exp(-0.5 * u * u) * (1.0 / math.sqrt(2.0 * math.pi))
            back = (dot(g_ref[at, :], down_part, NT) * slope).astype(BF16)
            hid_ref[at, :] = hidden
            dup_in_ref[at, :] = back
            total += jnp.sum(back.astype(F32), axis=0, keepdims=True)
            out_ref[at, :] += dot(hidden, down_part)
            h_ref[at, :] += dot(back, up_part, NT)
        dbias_ref[0:1, at_ff] = total
        ddown_ref[spot] = dot(hid_ref[...], g_ref[...], TN).astype(BF16)
        dup_ref[spot] = dot(m_ref[...], dup_in_ref[...], TN).astype(BF16)
        grads_out(step, 0).start()
        grads_out(step, 1).start()
        return 0

    lax.fori_loop(0, steps, feed_step, 0)

    gain = jnp.zeros((1, width), F32)
    shift = jnp.zeros((1, width), F32)
    sums = jnp.zeros((1, width), F32)
    for t in range(tiles):
        at = pl.ds(t * tile, tile)
        xh, _ = normalized(x_ref[at, :].astype(F32))
        dm = h_ref[at, :]
        gain += jnp.sum(dm * xh, axis=0, keepdims=True)
        shift += jnp.sum(dm, axis=0, keepdims=True)
        sums += jnp.sum(g_ref[at, :].astype(F32), axis=0, keepdims=True)
        h_ref[at, :] = dm * gain_2
    sums_ref[...] = jnp.concatenate([gain, shift, sums, jnp.zeros((5, width), F32)], axis=0)

    mine = z - core
    for which in range(2):
        for k in range(1, ring):
            @pl.when((mine >= 0) & (mine < batch))
            def _(which=which, k=k):
                other = (z + k) % ring
                ref = pairs[which][1].at[pl.ds(pl.multiple_of(other * piece, 16), piece), :]
                remote(ref, ref, t_send.at[which, 0], t_recv.at[which, other], core_id, z).wait_recv()
    for h in hops:
        stage_d(2, h)
    for k in range(1, ring):
        small_copy(k).wait_send()
    for a in range(3):
        for way in range(2):
            for h in range(ring - 1):
                @pl.when(can_send(way, h))
                def _(a=a, way=way, h=h):
                    hop(a, way, h).wait_send()
        for h in hops:
            for way in range(2):
                @pl.when(in_range(way, h))
                def _(a=a, h=h, way=way):
                    shard = z - h if way == 0 else z + h
                    for j in range(8):
                        cast(a, shard, j).wait_send()
    for which in range(2):
        for i in range(batch):
            src, dst, target = move(which, i)

            @pl.when(target != z)
            def _(src=src, dst=dst, target=target, which=which, i=i):
                remote(src, dst, t_send.at[which, i], t_recv.at[which, z], d, target).wait_send()

            @pl.when(target == z)
            def _(src=src, dst=dst, which=which):
                pltpu.make_async_copy(src, dst, local.at[6 + which]).wait()
    own_copies[2].wait()
    for step in range(steps - 2, steps):
        grads_out(step, 0).wait()
        grads_out(step, 1).wait()


def gather_feed(up, down, att, small, tokens, cotangents, piece):
    ring = lax.axis_size("ctx")
    count, width = tokens.shape
    ff = up.shape[1]
    chunk = 512
    full = lambda v: jax.ShapeDtypeStruct((ring * v.shape[0], v.shape[1]), v.dtype)
    home = jax.ShapeDtypeStruct((ring * piece, width), tokens.dtype)
    rows = jax.ShapeDtypeStruct((count, width), F32)
    dma = pltpu.SemaphoreType.DMA
    anywhere = pl.BlockSpec(memory_space=pl.ANY)
    vmem = pl.BlockSpec(memory_space=pltpu.VMEM)
    return pl.pallas_call(
        gather_kernel,
        in_specs=[anywhere] * 6,
        out_specs=[anywhere, vmem, anywhere, anywhere, vmem, vmem, anywhere, anywhere, vmem, vmem],
        out_shape=[
            full(att), jax.ShapeDtypeStruct(small.shape, F32), home, home, rows, rows, full(up), full(down),
            jax.ShapeDtypeStruct((8, ff), F32), jax.ShapeDtypeStruct((8, width), F32),
        ],
        scratch_shapes=[
            pltpu.VMEM(full(up).shape, BF16), pltpu.VMEM(full(down).shape, BF16),
            pltpu.VMEM((ring, *small.shape), F32),
            pltpu.VMEM((count, width), BF16), pltpu.VMEM((count, width), BF16), pltpu.VMEM((count, width), BF16),
            pltpu.VMEM((count, chunk), BF16), pltpu.VMEM((count, chunk), BF16),
            pltpu.VMEM((2, width, chunk), BF16), pltpu.VMEM((2, chunk, width), BF16),
            dma((3, 2, ring)), dma((3, 2, ring)), dma((3, ring, 8)), dma((3, ring, 8)),
            dma((ring,)), dma((ring,)), dma((2, count // piece)), dma((2, ring)), dma((8,)), dma((2, 2)),
        ],
        compiler_params=pltpu.CompilerParams(
            collective_id=0, has_side_effects=True, vmem_limit_bytes=56 * MIB
        ),
        cost_estimate=pl.CostEstimate(
            flops=12 * count * width * ff, bytes_accessed=60 * MIB, transcendentals=count * ff
        ),
        name="gather_feed",
    )(up, down, att, small, tokens, cotangents)


def fold(into, rows, term):
    owners, height, _ = term.shape
    tile = 48

    def body(n, _):
        o, t = n // (height // tile), n % (height // tile)
        at = pl.ds(pl.multiple_of(rows + t * tile, 16), tile)
        into[o, at, :] = (
            into[o, at, :].astype(F32) + term[o, pl.ds(pl.multiple_of(t * tile, 16), tile), :].astype(F32)
        ).astype(BF16)
        return 0

    lax.fori_loop(0, owners * (height // tile), body, 0)


def reduce_kernel(count, teams, *refs):
    ring = lax.axis_size("ctx")
    d, z = lax.axis_index("dp"), lax.axis_index("ctx")
    core, x, y, core_id, x_id, y_id = plane(d)
    far_id = x_id + y_id - d
    half = ring // 2
    grads, (small, mixed, back) = refs[:count], refs[count : count + 3]
    refs = refs[count + 3 :]
    sums, (small_out, ret_mixed, ret_back) = refs[:count], refs[count : count + 3]
    refs = refs[count + 3 :]
    bufs = [refs[6 * a : 6 * a + 6] for a in range(count)]
    small_acc, small_in = refs[6 * count : 6 * count + 2]
    send, recv, load, s_send, s_recv, r_send, r_recv, r_local = refs[6 * count + 2 :]
    batch, piece = ret_mixed.shape[:2]

    def remote(src, dst, send_sem, recv_sem, dp, ctx):
        return pltpu.make_async_remote_copy(
            src_ref=src, dst_ref=dst, send_sem=send_sem, recv_sem=recv_sem, device_id=(dp, ctx), device_id_type=MESH
        )

    def team_id(t):
        bit = d // (8 << t) % 2
        return d + (8 << t) * (1 - 2 * bit)

    barrier = pltpu.get_barrier_semaphore()
    partners = [core_id, x_id, y_id, far_id] + [team_id(t) for t in range(teams)]
    for k in range(1, ring):
        pl.semaphore_signal(barrier, inc=1, device_id=(d, (z + k) % ring), device_id_type=MESH)
    for other in partners:
        pl.semaphore_signal(barrier, inc=1, device_id=(other, z), device_id_type=MESH)
    pl.semaphore_wait(barrier, ring - 1 + len(partners))

    def returned(which, i, to):
        source, target = ((mixed, ret_mixed), (back, ret_back))[which]
        return source.at[pl.ds(pl.multiple_of(to * piece, 16), piece), :], target.at[i]

    mine = z - core
    is_home = (mine >= 0) & (mine < batch)

    def start_returns():
        for which in range(2):
            for i in range(batch):
                @pl.when(mine == i)
                def _(which=which, i=i):
                    for k in range(1, ring):
                        to = (z + k) % ring
                        src, dst = returned(which, i, to)
                        remote(src, dst, r_send.at[which, k], r_recv.at[which, i], d, to).start()
                    src, dst = returned(which, i, z)
                    pltpu.make_async_copy(src, dst, r_local.at[which]).start()

    def wait_returns():
        for which in range(2):
            for i in range(batch):
                src, dst = returned(which, i, z)

                @pl.when(mine == i)
                def _(which=which, i=i, src=src, dst=dst):
                    for k in range(1, ring):
                        to = (z + k) % ring
                        remote(*returned(which, i, to), r_send.at[which, k], r_recv.at[which, i], d, to).wait_send()
                    pltpu.make_async_copy(src, dst, r_local.at[which]).wait()

                @pl.when(mine != i)
                def _(which=which, i=i, src=src, dst=dst):
                    remote(src, dst, r_send.at[which, 0], r_recv.at[which, i], core_id, z).wait_recv()

    def sizes(a):
        rows, columns = sums[a].shape
        return rows, columns // 2

    def slice_of(order, xx, yy):
        return (1 - order) * (2 * xx + yy) + order * (2 * yy + xx)

    bits = ((x, y), (y, x))
    ids = ((x_id, y_id), (y_id, x_id))

    def core_copy(a):
        rows, span = sizes(a)
        away = pl.ds(pl.multiple_of((1 - core) * span, 128), span)
        return remote(grads[a].at[:, :, away], bufs[a][1], send.at[a, 0], recv.at[a, 0], core_id, z)

    def core_load(a):
        rows, span = sizes(a)
        keep = pl.ds(pl.multiple_of(core * span, 128), span)
        return pltpu.make_async_copy(grads[a].at[:, :, keep], bufs[a][0], load.at[a])

    def first_copy(a, order):
        rows, span = sizes(a)
        own = pl.ds(order * half, half)
        away = pl.ds(pl.multiple_of((1 - bits[order][0]) * (rows // 2), 16), rows // 2)
        return remote(
            bufs[a][0].at[own, away, :], bufs[a][2].at[own], send.at[a, 1 + order], recv.at[a, 1 + order],
            ids[order][0], z,
        )

    def second_copy(a, order):
        rows, span = sizes(a)
        own = pl.ds(order * half, half)
        away = bits[order][0] * (rows // 2) + (1 - bits[order][1]) * (rows // 4)
        return remote(
            bufs[a][0].at[own, pl.ds(pl.multiple_of(away, 16), rows // 4), :], bufs[a][3].at[own],
            send.at[a, 3 + order], recv.at[a, 3 + order], ids[order][1], z,
        )

    def quarter(a, owner):
        rows, span = sizes(a)
        at = slice_of(owner // half, x, y) * (rows // 4)
        return bufs[a][0].at[owner, pl.ds(pl.multiple_of(at, 16), rows // 4), :]

    def owner_copy(a, k):
        to = (z + k) % ring
        return remote(quarter(a, to), bufs[a][4].at[k - 1], send.at[a, 4 + k], recv.at[a, 4 + k], d, to)

    def team_copy(a, t):
        j = 4 + ring + 7 + t
        return remote(bufs[a][5].at[0], bufs[a][5].at[1 + t], send.at[a, j], recv.at[a, j], team_id(t), z)

    spots = ((x, y), (1 - x, y), (x, 1 - y), (1 - x, 1 - y))

    def final(a, spot, side):
        rows, span = sizes(a)
        at = slice_of(z // half, *spots[spot]) * (rows // 4)
        return sums[a].at[
            pl.ds(pl.multiple_of(at, 16), rows // 4), pl.ds(pl.multiple_of(side * span, 128), span)
        ]

    def spread(a, j):
        s, r = send.at[a, 4 + ring + j - 1], recv.at[a, 4 + ring + j - 1]
        if j < 4:
            return remote(bufs[a][5].at[0], final(a, 0, core), s, r, (x_id, y_id, far_id)[j - 1], z)
        src = bufs[a][5].at[0] if j == 4 else final(a, j - 4, core)
        return remote(src, final(a, j - 4, core), s, r, core_id, z)

    def spread_here(a, j):
        s, r = send.at[a, 4 + ring + j - 1], recv.at[a, 4 + ring + j - 1]
        ref = final(a, j, core) if j < 4 else final(a, j - 4, 1 - core)
        remote(ref, ref, s, r, core_id, z).wait_recv()

    def keep(a):
        return pltpu.make_async_copy(bufs[a][5].at[0], final(a, 0, core), load.at[count + a])

    def add_slices(target, terms):
        rows = target.shape[0]
        for t in range(rows // 48):
            at = pl.ds(t * 48, 48)
            total = terms[0][at, :].astype(F32)
            for term in terms[1:]:
                total += term[at, :].astype(F32)
            target[at, :] = total.astype(BF16)

    def stage_0(a):
        core_copy(a).start()
        core_load(a).start()

    def stage_1(a):
        core_load(a).wait()
        core_copy(a).wait_recv()
        fold(bufs[a][0], 0, bufs[a][1])
        for order in range(2):
            first_copy(a, order).start()

    def stage_2(a):
        rows, span = sizes(a)
        for order in range(2):
            own = pl.ds(order * half, half)
            first_copy(a, order).wait_recv()
            fold(bufs[a][0].at[own], bits[order][0] * (rows // 2), bufs[a][2].at[own])
            second_copy(a, order).start()

    def stage_3(a):
        rows, span = sizes(a)
        for order in range(2):
            own = pl.ds(order * half, half)
            second_copy(a, order).wait_recv()
            at = slice_of(order, x, y) * (rows // 4)
            fold(bufs[a][0].at[own], at, bufs[a][3].at[own])
        for k in range(1, ring):
            owner_copy(a, k).start()

    def stage_4(a):
        for k in range(1, ring):
            owner_copy(a, k).wait_recv()
        result = bufs[a][5].at[0]
        add_slices(result, [quarter(a, z)] + [bufs[a][4].at[k] for k in range(ring - 1)])
        for t in range(teams):
            team_copy(a, t).start()
            team_copy(a, t).wait()
            add_slices(result, [result, bufs[a][5].at[1 + t]])
        keep(a).start()
        for j in range(1, 5):
            spread(a, j).start()

    def stage_5(a):
        for j in range(1, 4):
            spread_here(a, j)
            spread(a, 4 + j).start()

    def stage_6(a):
        for j in range(4, 8):
            spread_here(a, j)
        core_copy(a).wait_send()
        for order in range(2):
            first_copy(a, order).wait_send()
            second_copy(a, order).wait_send()
        for k in range(1, ring):
            owner_copy(a, k).wait_send()
        for j in range(1, 8):
            spread(a, j).wait_send()
        keep(a).wait()

    steps = [core_id, x_id, y_id] + [team_id(t) for t in range(teams)]

    def small_copy(n):
        return remote(small_acc, small_in.at[n], s_send.at[n], s_recv.at[n], steps[n], z)

    def small_owner(k):
        n = len(steps) + k - 1
        return remote(small_acc, small_in.at[n], s_send.at[n], s_recv.at[n], d, (z + k) % ring)

    def small_step(n):
        if n < len(steps):
            if n == 0:
                small_acc[...] = small[...]
            small_copy(n).start()
        elif n == len(steps):
            for k in range(1, ring):
                small_owner(k).start()

    def small_close(n):
        if n < len(steps):
            small_copy(n).wait()
            small_acc[...] += small_in[n]
        elif n == len(steps):
            for k in range(1, ring):
                small_owner(k).wait()
            total = small_acc[...]
            for k in range(ring - 1):
                total += small_in[len(steps) + k]
            small_out[...] = total

    stages = (stage_0, stage_1, stage_2, stage_3, stage_4, stage_5, stage_6)
    for a in range(count):
        stage_0(a)
    start_returns()
    for n in range(1, max(len(stages), len(steps) + 2)):
        small_step(n - 1)
        if n < len(stages):
            for a in range(count):
                stages[n](a)
        small_close(n - 1)
    wait_returns()


def reduce_all(grads, small, mixed, back, batch):
    ring, groups = lax.axis_size("ctx"), lax.axis_size("dp")
    teams = (groups // 8).bit_length() - 1
    count = len(grads)
    grads = [g.reshape(ring, -1, g.shape[1]) for g in grads]
    length, width = mixed.shape
    dma = pltpu.SemaphoreType.DMA
    anywhere = pl.BlockSpec(memory_space=pl.ANY)
    vmem = pl.BlockSpec(memory_space=pltpu.VMEM)
    scratch = []
    for g in grads:
        _, rows, columns = g.shape
        span = columns // 2
        scratch += [
            pltpu.VMEM((ring, rows, span), BF16),
            pltpu.VMEM((ring, rows, span), BF16),
            pltpu.VMEM((ring, rows // 2, span), BF16),
            pltpu.VMEM((ring, rows // 4, span), BF16),
            pltpu.VMEM((ring - 1, rows // 4, span), BF16),
            pltpu.VMEM((1 + teams, rows // 4, span), BF16),
        ]
    rounds = 3 + teams + ring - 1
    scratch += [pltpu.VMEM(small.shape, F32), pltpu.VMEM((rounds, *small.shape), F32)]
    copies = 4 + ring + 7 + teams
    scratch += [
        dma((count, copies)), dma((count, copies)), dma((2 * count,)), dma((rounds,)), dma((rounds,)),
        dma((2, ring)), dma((2, batch)), dma((2,)),
    ]
    token = jax.ShapeDtypeStruct((batch, length // ring, width), BF16)
    return pl.pallas_call(
        functools.partial(reduce_kernel, count, teams),
        in_specs=[anywhere] * count + [vmem, anywhere, anywhere],
        out_specs=[anywhere] * count + [vmem, anywhere, anywhere],
        out_shape=[jax.ShapeDtypeStruct(g.shape[1:], BF16) for g in grads]
        + [jax.ShapeDtypeStruct(small.shape, F32), token, token],
        scratch_shapes=scratch,
        compiler_params=pltpu.CompilerParams(collective_id=1, has_side_effects=True, vmem_limit_bytes=56 * MIB),
        cost_estimate=pl.CostEstimate(flops=0, bytes_accessed=60 * MIB, transcendentals=0),
        name="reduce",
    )(*grads, small, mixed, back)


def attend_kernel(
    order_ref, x_ref, stored_g_ref, norm_ref, bias_ref, cos_ref, low_ref, high_ref, wq_ref, wk_ref, wv_ref, wo_ref,
    out_ref, h_ref, dq_ref, dk_ref, dv_ref, dwo_ref, dbias_ref, small_ref,
    g_ref, a_ref, acc_ref, da_ref, q_ref, k_ref, v_ref, do_ref, o_ref, dqs_ref, dks_ref, dvs_ref,
):
    step = pl.program_id(0)
    last = pl.num_programs(0) - 1
    rows, width = x_ref.shape
    lanes = QUAD * HD
    tile = 256
    half = ROT // 2
    scale = 1.0 / math.sqrt(HD)
    blocks = rows // BLOCK
    mine = lax.axis_index("ctx") - lax.axis_index("dp") % 2
    is_home = (mine >= 0) & (mine < SEQS)

    def stored(ref, at):
        values = ref[pl.ds(pl.multiple_of(at * BLOCK, BLOCK), BLOCK), :]
        return jnp.where(is_home, values, jnp.zeros_like(values))

    @pl.when(step == 0)
    def _():
        for j in range(blocks):
            place = 0
            for s in range(blocks):
                place = place + jnp.where(order_ref[s] == j, s, 0)
            at = pl.ds(j * BLOCK, BLOCK)
            xh, _ = normalized(stored(x_ref, place).astype(F32))
            a_ref[at, :] = (xh * norm_ref[0:1, :] + norm_ref[1:2, :]).astype(BF16)
            g_ref[at, :] = stored(stored_g_ref, place)
        acc_ref[...] = jnp.zeros_like(acc_ref)
        da_ref[...] = jnp.zeros_like(da_ref)

    def table(ref, at):
        values = ref[at, :]
        return jnp.concatenate([values] * (lanes // values.shape[1]), axis=1)

    def turn(values, at):
        low = pltpu.roll(values, lanes - half, 1) * table(low_ref, at)
        high = pltpu.roll(values, half, 1) * table(high_ref, at)
        return values * table(cos_ref, at), low + high

    for t in range(rows // tile):
        at = pl.ds(t * tile, tile)
        a = a_ref[at, :]
        same, cross = turn(dot(a, wq_ref[...]) + bias_ref[...], at)
        q_ref[at, :] = ((same + cross).astype(BF16) * scale).astype(BF16)
        same, cross = turn(dot(a, wk_ref[...]), at)
        k_ref[at, :] = (same + cross).astype(BF16)
        v_ref[at, :] = dot(a, wv_ref[...]).astype(BF16)
        do_ref[at, :] = dot(g_ref[at, :], wo_ref[...], NT).astype(BF16)

    dks_ref[...] = jnp.zeros_like(dks_ref)
    dvs_ref[...] = jnp.zeros_like(dvs_ref)
    head_of = lax.broadcasted_iota(jnp.int32, (BLOCK, lanes), 1) // HD

    def stack(values):
        zero = jnp.zeros_like(values)
        return jnp.concatenate([jnp.where(head_of == e, values, zero) for e in range(QUAD)], axis=0)

    def merge(values):
        out = values[:BLOCK]
        for e in range(1, QUAD):
            out = jnp.where(head_of == e, values[e * BLOCK : (e + 1) * BLOCK], out)
        return out

    spot = lax.broadcasted_iota(jnp.int32, (QUAD * BLOCK, BLOCK), 0) % BLOCK
    admitted = lax.broadcasted_iota(jnp.int32, (QUAD * BLOCK, BLOCK), 1) <= spot
    for b in range(rows // BLOCK):
        at = pl.ds(b * BLOCK, BLOCK)
        seen = pl.ds(0, (b + 1) * BLOCK)
        q = stack(q_ref[at, :])
        do_block = do_ref[at, :]
        do = stack(do_block)
        keys = k_ref[seen, :]
        values = v_ref[seen, :]
        scores = dot(q, keys, NT)
        edge = jnp.where(admitted, scores[:, b * BLOCK :], -1e30)
        scores = edge if b == 0 else jnp.concatenate([scores[:, : b * BLOCK], edge], axis=1)
        top = jnp.max(scores, axis=-1, keepdims=True)
        expo = jnp.exp(scores - top)
        probs = expo * (1.0 / jnp.sum(expo, axis=-1, keepdims=True))
        low = probs.astype(BF16)
        mixed = dot(low, values)
        o_ref[at, :] = merge(mixed).astype(BF16)
        share = jnp.sum(mixed * do.astype(F32), axis=-1, keepdims=True)
        back = (probs * (dot(do, values, NT) - share)).astype(BF16)
        dqs_ref[at, :] = merge(dot(back, keys)) * scale
        dks_ref[seen, :] += dot(back, q, TN)
        dvs_ref[seen, :] += dot(low, do, TN)

    total = jnp.zeros((1, lanes), F32)
    for t in range(rows // tile):
        at = pl.ds(t * tile, tile)
        same, cross = turn(dqs_ref[at, :], at)
        dq = (same - cross).astype(BF16)
        same, cross = turn(dks_ref[at, :], at)
        dk = (same - cross).astype(BF16)
        dv = dvs_ref[at, :].astype(BF16)
        total += jnp.sum(dq.astype(F32), axis=0, keepdims=True)
        q_ref[at, :] = dq
        k_ref[at, :] = dk
        v_ref[at, :] = dv
        acc_ref[at, :] += dot(o_ref[at, :], wo_ref[...])
        da_ref[at, :] += dot(dq, wq_ref[...], NT) + dot(dk, wk_ref[...], NT) + dot(dv, wv_ref[...], NT)
    dbias_ref[...] = total
    dwo_ref[...] = dot(o_ref[...], g_ref[...], TN).astype(BF16)
    dq_ref[...] = dot(a_ref[...], q_ref[...], TN).astype(BF16)
    dk_ref[...] = dot(a_ref[...], k_ref[...], TN).astype(BF16)
    dv_ref[...] = dot(a_ref[...], v_ref[...], TN).astype(BF16)

    @pl.when(step == last)
    def _():
        gain = jnp.zeros((1, width), F32)
        shift = jnp.zeros((1, width), F32)
        for s in range(blocks):
            at = pl.ds(s * BLOCK, BLOCK)
            sorted_at = pl.ds(pl.multiple_of(order_ref[s] * BLOCK, BLOCK), BLOCK)
            xh, _ = normalized(stored(x_ref, s).astype(F32))
            da = da_ref[sorted_at, :]
            gain += jnp.sum(da * xh, axis=0, keepdims=True)
            shift += jnp.sum(da, axis=0, keepdims=True)
            h_ref[at, :] = (da * norm_ref[0:1, :]).astype(BF16)
            out_ref[at, :] = acc_ref[sorted_at, :].astype(BF16)
        small_ref[0:1, :] = gain
        small_ref[1:2, :] = shift


def attend(order, x, g, norms, bias_q, tables, weights):
    rows, width = x.shape
    lanes = QUAD * HD
    groups = width // lanes
    whole = lambda shape: pl.BlockSpec(shape, lambda i: (0,) * len(shape))
    column = pl.BlockSpec((width, lanes), lambda i: (0, i))
    small = jax.ShapeDtypeStruct((rows, width), BF16)
    return pl.pallas_call(
        attend_kernel,
        grid=(groups,),
        in_specs=[
            pl.BlockSpec(memory_space=pltpu.SMEM),
            whole((rows, width)),
            whole((rows, width)),
            whole(norms.shape),
            pl.BlockSpec((1, lanes), lambda i: (0, i)),
            whole(tables[0].shape),
            whole(tables[0].shape),
            whole(tables[0].shape),
            pl.BlockSpec((width, lanes), lambda i: (0, i)),
            pl.BlockSpec((width, lanes), lambda i: (0, groups + i)),
            pl.BlockSpec((width, lanes), lambda i: (0, 2 * groups + i)),
            pl.BlockSpec((lanes, width), lambda i: (i, 3)),
        ],
        out_specs=[
            whole((rows, width)),
            whole((rows, width)),
            column,
            column,
            column,
            pl.BlockSpec((lanes, width), lambda i: (i, 0)),
            pl.BlockSpec((1, lanes), lambda i: (0, i)),
            whole((8, width)),
        ],
        out_shape=[
            small,
            small,
            jax.ShapeDtypeStruct((width, width), BF16),
            jax.ShapeDtypeStruct((width, width), BF16),
            jax.ShapeDtypeStruct((width, width), BF16),
            jax.ShapeDtypeStruct((width, width), BF16),
            jax.ShapeDtypeStruct((1, width), F32),
            jax.ShapeDtypeStruct((8, width), F32),
        ],
        scratch_shapes=[
            pltpu.VMEM((rows, width), BF16),
            pltpu.VMEM((rows, width), BF16),
            pltpu.VMEM((rows, width), F32),
            pltpu.VMEM((rows, width), F32),
        ]
        + [pltpu.VMEM((rows, lanes), BF16)] * 5
        + [pltpu.VMEM((rows, lanes), F32)] * 3,
        compiler_params=pltpu.CompilerParams(vmem_limit_bytes=56 * MIB),
        cost_estimate=pl.CostEstimate(
            flops=24 * rows * width * width + 8 * rows * rows * width,
            bytes_accessed=16 * width * width + 8 * rows * width,
            transcendentals=HEADS * rows * rows // 2,
        ),
        name="attend",
    )(order, x, g, norms, bias_q, *tables, weights, weights, weights, weights)


def rotary_tables(length):
    half = ROT // 2
    frequency = ROPE_BASE ** (-(np.arange(half) * 2.0 / ROT))
    angle = np.arange(length)[:, None] * frequency[None, :]
    cosine, sine = np.cos(angle), np.sin(angle)
    rest = np.zeros((length, HD - ROT))
    none = np.zeros_like(sine)
    cos_full = np.concatenate([cosine, cosine, rest + 1.0], axis=1)
    low = np.concatenate([-sine, none, rest], axis=1)
    high = np.concatenate([none, sine, rest], axis=1)
    return tuple(jnp.asarray(np.tile(t, (1, 2)).astype(np.float32)) for t in (cos_full, low, high))


def adamw(weight, grad, first, second, rate, decay):
    first_new = BETA_ONE * first + (1.0 - BETA_ONE) * grad
    second_new = BETA_TWO * second + (1.0 - BETA_TWO) * grad * grad
    first_hat = first_new / (1.0 - BETA_ONE**STEP)
    second_hat = second_new / (1.0 - BETA_TWO**STEP)
    weight_new = weight - rate * (first_hat / (jnp.sqrt(second_hat) + EPS_ADAM) + decay * weight)
    return (first_new, second_new, weight_new)


def shards(
    tokens, out_grad, block_order, qkv_weight, out_weight, up_weight, down_weight, norm_params, bias_params,
    qkv_first, qkv_second, out_first, out_second, up_first, up_second, down_first, down_second,
    norm_first, norm_second, bias_first, bias_second,
):
    groups, ring = lax.axis_size("dp"), lax.axis_size("ctx")
    group, rank = lax.axis_index("dp"), lax.axis_index("ctx")
    batch, piece, width = tokens.shape
    length = piece * ring
    count = batch * piece
    ff = up_weight.shape[1]

    att_weight = jnp.concatenate([qkv_weight, out_weight], axis=1).astype(BF16)
    share = bias_params.shape[0]
    wide = jnp.zeros((4, width), F32)
    own_norms = lax.dynamic_update_slice(wide, norm_params.astype(BF16).astype(F32), (0, rank * (width // ring)))
    own_biases = jnp.zeros((ring * share,), F32)
    own_biases = lax.dynamic_update_slice(own_biases, bias_params.astype(BF16).astype(F32), (rank * share,))
    others = jnp.concatenate([own_biases[: 2 * width], own_biases[2 * width + ff :], jnp.zeros((ff - 3 * width,), F32)])
    small = jnp.stack([own_biases[2 * width : 2 * width + ff], others, own_norms.reshape(-1)])
    small = jnp.pad(small, ((0, 5), (0, 0)))
    x_rows, g_rows = tokens.reshape(count, width), out_grad.reshape(count, width)
    att_copy, small, home_x, home_g, feed_out, h_feed, dup, ddown, dbias_up, small_feed = gather_feed(
        up_weight.astype(BF16), down_weight.astype(BF16), att_weight, small, x_rows, g_rows, piece
    )
    norms = small[2].reshape(4, width)
    bias_q = small[1:2, :width]

    odd = group % 2

    order = block_order[jnp.clip(rank - odd, 0, batch - 1)]

    attend_out, h_attend, dq, dk, dv, dout, dbias_q, small_attend = attend(
        order, home_x, home_g, norms, bias_q, rotary_tables(length), att_copy
    )

    dqkv = jnp.concatenate([dq, dk, dv], axis=1)
    tail = jnp.concatenate(
        [small_attend[:2].reshape(-1), small_feed[:2].reshape(-1), dbias_q[0], small_feed[2], dbias_up[0], small_feed[2]]
    )
    entries = tail.shape[0]
    tail = jnp.pad(tail, (0, -entries % 1024)).reshape(-1, 128)
    *owned, tail, ret_mixed, ret_back = reduce_all((dup, ddown, dqkv, dout), tail, attend_out, h_attend, batch)
    up_grad, down_grad, qkv_grad, out_grads = (g.astype(F32) for g in owned)
    tail = tail.reshape(-1)[:entries]
    returned = [v.reshape(count, width).astype(F32) for v in (ret_mixed, ret_back)]

    rows = x_rows.astype(F32)
    bias_rows = small[1:2, width : 2 * width] + small[1:2, 2 * width : 3 * width]
    layer_out = (rows + returned[0] + feed_out + bias_rows).astype(BF16).reshape(batch, piece, width)
    xh, scale = normalized(rows)
    h = returned[1] + h_feed
    inner = jnp.mean(h * xh, axis=-1, keepdims=True)
    input_grad = g_rows.astype(F32) + scale * (h - jnp.mean(h, axis=-1, keepdims=True) - xh * inner)
    input_grad = input_grad.reshape(batch, piece, width)

    norm_grad = lax.dynamic_slice_in_dim(tail[: 4 * width].reshape(4, width), rank * (width // ring), width // ring, 1)
    bias_grad = lax.dynamic_slice_in_dim(tail[4 * width :], rank * share, share, 0)

    qkv_new = adamw(qkv_weight, qkv_grad, qkv_first, qkv_second, 0.1, DECAY)
    out_new = adamw(out_weight, out_grads, out_first, out_second, 0.6, DECAY)
    up_new = adamw(up_weight, up_grad, up_first, up_second, 0.1, DECAY)
    down_new = adamw(down_weight, down_grad, down_first, down_second, 0.05, DECAY)
    norm_new = adamw(norm_params, norm_grad, norm_first, norm_second, 0.6, 0.0)
    bias_new = adamw(bias_params, bias_grad, bias_first, bias_second, 0.6, 0.0)
    return (
        layer_out, input_grad, *qkv_new, *out_new, *up_new, *down_new,
        norm_new[0], norm_new[1][:2], norm_new[1][2:], norm_new[2], *bias_new,
    )


def solution(mesh):
    rows, columns, token = P("ctx", None), P(None, "ctx"), P("dp", "ctx", None)
    in_specs = (token, token, P("dp", None)) + (rows,) * 4 + (columns, P("ctx")) + (rows,) * 8
    in_specs += (columns, columns, P("ctx"), P("ctx"))
    out_specs = (token, token) + (rows,) * 12 + (columns,) * 4 + (P("ctx"),) * 3
    return jax.shard_map(shards, mesh=mesh, in_specs=in_specs, out_specs=out_specs, check_vma=False)
```

```python
import functools
import math

import jax
import jax.numpy as jnp
import numpy as np
from jax import lax
from jax.experimental import pallas as pl
from jax.experimental.pallas import tpu as pltpu
from jax.sharding import PartitionSpec as P

HEADS = 12
HD = 64
STEP = 10
ROT = 16
SEQS = 3
BLOCK = 128
QUAD = 4

EPS_NORM = 1e-05
BETA_ONE = 0.9
BETA_TWO = 0.95
EPS_ADAM = 1e-08
DECAY = 0.01
ROPE_BASE = 10000.0
F32 = jnp.float32
BF16 = jnp.bfloat16
MIB = 1024 * 1024


def dot(left, right, dims=((1,), (0,))):
    return lax.dot_general(left, right, (dims, ((), ())), preferred_element_type=F32)


NN = ((1,), (0,))
NT = ((1,), (1,))
TN = ((0,), (0,))


def normalized(values):
    mean = jnp.mean(values, axis=-1, keepdims=True)
    centred = values - mean
    variance = jnp.mean(centred * centred, axis=-1, keepdims=True)
    scale = lax.rsqrt(variance + EPS_NORM)
    return centred * scale, scale


MESH = pl.DeviceIdType.MESH


def plane(d):
    core, x, y = d % 2, d // 2 % 2, d // 4 % 2
    return core, x, y, d + 1 - 2 * core, d + 2 - 4 * x, d + 4 - 8 * y


def gather_kernel(
    up, down, att, small, tokens, cotangents,
    att_all, small_all, home_x, home_g, out_ref, h_ref, dup_all, ddown_all, dbias_ref, sums_ref,
    up_all, down_all, small_in, x_ref, g_ref, m_ref, hid_ref, dup_in_ref, dup_ref, ddown_ref,
    z_send, z_recv, p_send, p_recv, s_send, s_recv, t_send, t_recv, local, out_sem,
):
    ring = lax.axis_size("ctx")
    d, z = lax.axis_index("dp"), lax.axis_index("ctx")
    core, x, y, core_id, x_id, y_id = plane(d)
    own = x + 2 * y
    own_x, own_y, far = own + 1 - 2 * x, own + 2 - 4 * y, 3 - own
    count, width = tokens.shape
    piece = home_x.shape[0] // ring
    batch = count // piece
    arrays = ((up, up_all, False), (down, down_all, True), (att, att_all, False))

    def slot(a, base, place, half=None):
        source, whole, tall = arrays[a]
        ref = source if base is None else whole
        rows, columns = source.shape
        at = 0 if base is None else base * rows
        height, span = rows // 4, columns // 2
        at = at + place * height
        column = core * span
        if half is not None:
            if tall:
                height = height // 2
                at = at + half * height
            else:
                span = span // 2
                column = column + half * span
        return ref.at[pl.ds(pl.multiple_of(at, 16), height), pl.ds(pl.multiple_of(column, 128), span)]

    def other_slot(a, base, place):
        source, whole, tall = arrays[a]
        rows, columns = source.shape
        at = pl.multiple_of(base * rows + place * (rows // 4), 16)
        column = pl.multiple_of((1 - core) * (columns // 2), 128)
        return whole.at[pl.ds(at, rows // 4), pl.ds(column, columns // 2)]

    def remote(src, dst, send, recv, dp, ctx):
        return pltpu.make_async_remote_copy(
            src_ref=src, dst_ref=dst, send_sem=send, recv_sem=recv, device_id=(dp, ctx), device_id_type=MESH
        )

    barrier = pltpu.get_barrier_semaphore()
    for k in range(1, ring):
        pl.semaphore_signal(barrier, inc=1, device_id=(d, (z + k) % ring), device_id_type=MESH)
    for other in (core_id, x_id, y_id):
        pl.semaphore_signal(barrier, inc=1, device_id=(other, z), device_id_type=MESH)
    pl.semaphore_wait(barrier, ring + 2)

    def hop(a, way, h):
        shard = z - h if way == 0 else z + h
        target = z + 1 if way == 0 else z - 1
        src = slot(a, None, own) if h == 0 else slot(a, shard, own)
        return remote(src, slot(a, shard, own), z_send.at[a, way, h], z_recv.at[a, way, h], d, target)

    def can_send(way, h):
        shard = z - h if way == 0 else z + h
        target = z + 1 if way == 0 else z - 1
        return (shard >= 0) & (shard < ring) & (target >= 0) & (target < ring)

    def in_range(way, h):
        shard = z - h if way == 0 else z + h
        return (shard >= 0) & (shard < ring)

    def cast(a, shard, j):
        send, recv = p_send.at[a, shard, j], p_recv.at[a, shard, j]
        if j == 0:
            ref = slot(a, shard, own)
            return remote(ref, ref, send, recv, x_id, z)
        if j == 1:
            ref = slot(a, shard, own)
            return remote(ref, ref, send, recv, y_id, z)
        if j == 2:
            ref = slot(a, shard, own_x, 0)
            return remote(ref, ref, send, recv, y_id, z)
        if j == 3:
            ref = slot(a, shard, own_y, 1)
            return remote(ref, ref, send, recv, x_id, z)
        ref = slot(a, shard, (own, own_x, own_y, far)[j - 4])
        return remote(ref, ref, send, recv, core_id, z)

    def arrived(a, shard, j):
        send, recv = p_send.at[a, shard, j], p_recv.at[a, shard, j]
        ref = {0: lambda: slot(a, shard, own_x), 1: lambda: slot(a, shard, own_y),
               2: lambda: slot(a, shard, far, 0), 3: lambda: slot(a, shard, far, 1)}.get(
            j, lambda: other_slot(a, shard, (own, own_x, own_y, far)[j - 4]))()
        remote(ref, ref, send, recv, core_id, z).wait_recv()

    def start_hops(a):
        for way in range(2):
            @pl.when(can_send(way, 0))
            def _(way=way):
                hop(a, way, 0).start()

    def small_copy(k):
        return remote(small, small_in.at[ring - k], s_send.at[k], s_recv.at[k], d, (z + k) % ring)

    def stage_a(a, h):
        for way in range(2):
            @pl.when(in_range(way, h))
            def _(way=way):
                shard = z - h if way == 0 else z + h
                ref = slot(a, shard, own)
                remote(ref, ref, z_send.at[a, way, h - 1], z_recv.at[a, way, h - 1], core_id, z).wait_recv()

                @pl.when(can_send(way, h))
                def _():
                    hop(a, way, h).start()

                cast(a, shard, 0).start()
                cast(a, shard, 1).start()
                cast(a, shard, 4).start()

    def stage_b(a, h):
        for way in range(2):
            @pl.when(in_range(way, h))
            def _(way=way):
                shard = z - h if way == 0 else z + h
                arrived(a, shard, 0)
                cast(a, shard, 2).start()
                cast(a, shard, 5).start()
                arrived(a, shard, 1)
                cast(a, shard, 3).start()
                cast(a, shard, 6).start()

    def stage_c(a, h):
        for way in range(2):
            @pl.when(in_range(way, h))
            def _(way=way):
                shard = z - h if way == 0 else z + h
                arrived(a, shard, 2)
                arrived(a, shard, 3)
                cast(a, shard, 7).start()

    def stage_d(a, h):
        for way in range(2):
            @pl.when(in_range(way, h))
            def _(way=way):
                shard = z - h if way == 0 else z + h
                for j in range(4, 8):
                    arrived(a, shard, j)

    pairs = ((tokens, home_x), (cotangents, home_g))

    def move(which, i):
        source, whole = pairs[which]
        src = source.at[pl.ds(i * piece, piece), :]
        dst = whole.at[pl.ds(pl.multiple_of(z * piece, 16), piece), :]
        return src, dst, i + core

    def start_moves(which):
        for i in range(batch):
            src, dst, target = move(which, i)

            @pl.when(target != z)
            def _(src=src, dst=dst, target=target, i=i):
                remote(src, dst, t_send.at[which, i], t_recv.at[which, z], d, target).start()

            @pl.when(target == z)
            def _(src=src, dst=dst):
                pltpu.make_async_copy(src, dst, local.at[6 + which]).start()

    own_copies = []
    for a in range(3):
        source, whole, _ = arrays[a]
        rows = source.shape[0]
        at = pl.ds(pl.multiple_of(z * rows, 16), rows)
        own_copies.append(pltpu.make_async_copy(source, whole.at[at, :], local.at[a]))
    x_load = pltpu.make_async_copy(tokens, x_ref, local.at[3])
    g_load = pltpu.make_async_copy(cotangents, g_ref, local.at[4])
    own_small = pltpu.make_async_copy(small, small_in.at[0], local.at[5])

    start_hops(0)
    start_hops(1)
    for k in range(1, ring):
        small_copy(k).start()
    start_moves(0)
    start_hops(2)
    for copy in own_copies + [x_load, g_load, own_small]:
        copy.start()
    hops = range(1, ring)
    work = [(a, h) for a in range(2) for h in hops]
    for n in range(len(work) + 2):
        if n < len(work):
            stage_a(*work[n])
        if 1 <= n <= len(work):
            stage_b(*work[n - 1])
        if n >= 2:
            stage_c(*work[n - 2])
    start_moves(1)
    stage_a(2, 1)

    own_small.wait()
    for k in range(1, ring):
        ref = small_in.at[ring - k]
        remote(ref, ref, s_send.at[k], s_recv.at[k], core_id, z).wait_recv()
    x_load.wait()
    g_load.wait()
    total = small_in[0]
    for k in range(1, ring):
        total += small_in[k]
    small_all[...] = total
    ff = up_all.shape[1]
    gain_2, shift_2 = small_all[2:3, 2 * width : 3 * width], small_all[2:3, 3 * width : 4 * width]
    tile = 256
    tiles = count // tile
    for t in range(tiles):
        at = pl.ds(t * tile, tile)
        xh, _ = normalized(x_ref[at, :].astype(F32))
        m_ref[at, :] = (xh * gain_2 + shift_2).astype(BF16)
        out_ref[at, :] = jnp.zeros((tile, width), F32)
        h_ref[at, :] = jnp.zeros((tile, width), F32)
    own_copies[0].wait()
    own_copies[1].wait()
    for h in hops:
        stage_d(0, h)
        stage_d(1, h)

    chunk = dup_ref.shape[2]
    steps = ff // chunk

    def grads_out(step, which):
        at = pl.ds(pl.multiple_of(step * chunk, 128), chunk)
        spot = step % 2
        if which == 0:
            return pltpu.make_async_copy(dup_ref.at[spot], dup_all.at[:, at], out_sem.at[0, spot])
        return pltpu.make_async_copy(ddown_ref.at[spot], ddown_all.at[at, :], out_sem.at[1, spot])

    def feed_step(step, _):
        spot = step % 2
        for h in hops:
            @pl.when((step == 2 * h - 3) & (h > 1))
            def _(h=h):
                stage_a(2, h)

            @pl.when(step == 2 * h - 2)
            def _(h=h):
                stage_b(2, h)

            @pl.when(step == jnp.minimum(2 * h - 1, steps - 1))
            def _(h=h):
                stage_c(2, h)

        @pl.when(step >= 2)
        def _():
            grads_out(step - 2, 0).wait()
            grads_out(step - 2, 1).wait()

        at_ff = pl.ds(pl.multiple_of(step * chunk, 128), chunk)
        up_part = up_all[:, at_ff]
        down_part = down_all[at_ff, :]
        bias = small_all[0:1, at_ff]
        total = jnp.zeros((1, chunk), F32)
        for t in range(tiles):
            at = pl.ds(t * tile, tile)
            u = dot(m_ref[at, :], up_part) + bias
            cdf = 0.5 * (1.0 + lax.erf(u * (1.0 / math.sqrt(2.0))))
            hidden = (u * cdf).astype(BF16)
            slope = cdf + u * jnp.exp(-0.5 * u * u) * (1.0 / math.sqrt(2.0 * math.pi))
            back = (dot(g_ref[at, :], down_part, NT) * slope).astype(BF16)
            hid_ref[at, :] = hidden
            dup_in_ref[at, :] = back
            total += jnp.sum(back.astype(F32), axis=0, keepdims=True)
            out_ref[at, :] += dot(hidden, down_part)
            h_ref[at, :] += dot(back, up_part, NT)
        dbias_ref[0:1, at_ff] = total
        ddown_ref[spot] = dot(hid_ref[...], g_ref[...], TN).astype(BF16)
        dup_ref[spot] = dot(m_ref[...], dup_in_ref[...], TN).astype(BF16)
        grads_out(step, 0).start()
        grads_out(step, 1).start()
        return 0

    lax.fori_loop(0, steps, feed_step, 0)

    gain = jnp.zeros((1, width), F32)
    shift = jnp.zeros((1, width), F32)
    sums = jnp.zeros((1, width), F32)
    for t in range(tiles):
        at = pl.ds(t * tile, tile)
        xh, _ = normalized(x_ref[at, :].astype(F32))
        dm = h_ref[at, :]
        gain += jnp.sum(dm * xh, axis=0, keepdims=True)
        shift += jnp.sum(dm, axis=0, keepdims=True)
        sums += jnp.sum(g_ref[at, :].astype(F32), axis=0, keepdims=True)
        h_ref[at, :] = dm * gain_2
    sums_ref[...] = jnp.concatenate([gain, shift, sums, jnp.zeros((5, width), F32)], axis=0)

    mine = z - core
    for which in range(2):
        for k in range(1, ring):
            @pl.when((mine >= 0) & (mine < batch))
            def _(which=which, k=k):
                other = (z + k) % ring
                ref = pairs[which][1].at[pl.ds(pl.multiple_of(other * piece, 16), piece), :]
                remote(ref, ref, t_send.at[which, 0], t_recv.at[which, other], core_id, z).wait_recv()
    for h in hops:
        stage_d(2, h)
    for k in range(1, ring):
        small_copy(k).wait_send()
    for a in range(3):
        for way in range(2):
            for h in range(ring - 1):
                @pl.when(can_send(way, h))
                def _(a=a, way=way, h=h):
                    hop(a, way, h).wait_send()
        for h in hops:
            for way in range(2):
                @pl.when(in_range(way, h))
                def _(a=a, h=h, way=way):
                    shard = z - h if way == 0 else z + h
                    for j in range(8):
                        cast(a, shard, j).wait_send()
    for which in range(2):
        for i in range(batch):
            src, dst, target = move(which, i)

            @pl.when(target != z)
            def _(src=src, dst=dst, target=target, which=which, i=i):
                remote(src, dst, t_send.at[which, i], t_recv.at[which, z], d, target).wait_send()

            @pl.when(target == z)
            def _(src=src, dst=dst, which=which):
                pltpu.make_async_copy(src, dst, local.at[6 + which]).wait()
    own_copies[2].wait()
    for step in range(steps - 2, steps):
        grads_out(step, 0).wait()
        grads_out(step, 1).wait()


def gather_feed(up, down, att, small, tokens, cotangents, piece):
    ring = lax.axis_size("ctx")
    count, width = tokens.shape
    ff = up.shape[1]
    chunk = 512
    full = lambda v: jax.ShapeDtypeStruct((ring * v.shape[0], v.shape[1]), v.dtype)
    home = jax.ShapeDtypeStruct((ring * piece, width), tokens.dtype)
    rows = jax.ShapeDtypeStruct((count, width), F32)
    dma = pltpu.SemaphoreType.DMA
    anywhere = pl.BlockSpec(memory_space=pl.ANY)
    vmem = pl.BlockSpec(memory_space=pltpu.VMEM)
    return pl.pallas_call(
        gather_kernel,
        in_specs=[anywhere] * 6,
        out_specs=[anywhere, vmem, anywhere, anywhere, vmem, vmem, anywhere, anywhere, vmem, vmem],
        out_shape=[
            full(att), jax.ShapeDtypeStruct(small.shape, F32), home, home, rows, rows, full(up), full(down),
            jax.ShapeDtypeStruct((8, ff), F32), jax.ShapeDtypeStruct((8, width), F32),
        ],
        scratch_shapes=[
            pltpu.VMEM(full(up).shape, BF16), pltpu.VMEM(full(down).shape, BF16),
            pltpu.VMEM((ring, *small.shape), F32),
            pltpu.VMEM((count, width), BF16), pltpu.VMEM((count, width), BF16), pltpu.VMEM((count, width), BF16),
            pltpu.VMEM((count, chunk), BF16), pltpu.VMEM((count, chunk), BF16),
            pltpu.VMEM((2, width, chunk), BF16), pltpu.VMEM((2, chunk, width), BF16),
            dma((3, 2, ring)), dma((3, 2, ring)), dma((3, ring, 8)), dma((3, ring, 8)),
            dma((ring,)), dma((ring,)), dma((2, count // piece)), dma((2, ring)), dma((8,)), dma((2, 2)),
        ],
        compiler_params=pltpu.CompilerParams(
            collective_id=0, has_side_effects=True, vmem_limit_bytes=56 * MIB
        ),
        cost_estimate=pl.CostEstimate(
            flops=12 * count * width * ff, bytes_accessed=60 * MIB, transcendentals=count * ff
        ),
        name="gather_feed",
    )(up, down, att, small, tokens, cotangents)


def fold(into, rows, term):
    owners, height, _ = term.shape
    tile = 48

    def body(n, _):
        o, t = n // (height // tile), n % (height // tile)
        at = pl.ds(pl.multiple_of(rows + t * tile, 16), tile)
        into[o, at, :] = (
            into[o, at, :].astype(F32) + term[o, pl.ds(pl.multiple_of(t * tile, 16), tile), :].astype(F32)
        ).astype(BF16)
        return 0

    lax.fori_loop(0, owners * (height // tile), body, 0)


def remote(src, dst, send_sem, recv_sem, dp, ctx):
    return pltpu.make_async_remote_copy(
        src_ref=src, dst_ref=dst, send_sem=send_sem, recv_sem=recv_sem, device_id=(dp, ctx), device_id_type=MESH
    )


def team_id(d, t):
    return d + (8 << t) * (1 - 2 * (d // (8 << t) % 2))


def greet(teams):
    ring = lax.axis_size("ctx")
    d, z = lax.axis_index("dp"), lax.axis_index("ctx")
    core, x, y, core_id, x_id, y_id = plane(d)
    barrier = pltpu.get_barrier_semaphore()
    partners = [core_id, x_id, y_id, x_id + y_id - d] + [team_id(d, t) for t in range(teams)]
    for k in range(1, ring):
        pl.semaphore_signal(barrier, inc=1, device_id=(d, (z + k) % ring), device_id_type=MESH)
    for other in partners:
        pl.semaphore_signal(barrier, inc=1, device_id=(other, z), device_id_type=MESH)
    pl.semaphore_wait(barrier, ring - 1 + len(partners))


def reducer(teams, grads, sums, bufs, send, recv, load):
    count = len(grads)
    ring = lax.axis_size("ctx")
    d, z = lax.axis_index("dp"), lax.axis_index("ctx")
    core, x, y, core_id, x_id, y_id = plane(d)
    far_id = x_id + y_id - d
    half = ring // 2

    def sizes(a):
        rows, columns = sums[a].shape
        return rows, columns // 2

    def slice_of(order, xx, yy):
        return (1 - order) * (2 * xx + yy) + order * (2 * yy + xx)

    bits = ((x, y), (y, x))
    ids = ((x_id, y_id), (y_id, x_id))

    def core_copy(a):
        rows, span = sizes(a)
        away = pl.ds(pl.multiple_of((1 - core) * span, 128), span)
        return remote(grads[a].at[:, :, away], bufs[a][1], send.at[a, 0], recv.at[a, 0], core_id, z)

    def core_load(a):
        rows, span = sizes(a)
        keep = pl.ds(pl.multiple_of(core * span, 128), span)
        return pltpu.make_async_copy(grads[a].at[:, :, keep], bufs[a][0], load.at[a])

    def first_copy(a, order):
        rows, span = sizes(a)
        own = pl.ds(order * half, half)
        away = pl.ds(pl.multiple_of((1 - bits[order][0]) * (rows // 2), 16), rows // 2)
        return remote(
            bufs[a][0].at[own, away, :], bufs[a][2].at[own], send.at[a, 1 + order], recv.at[a, 1 + order],
            ids[order][0], z,
        )

    def second_copy(a, order):
        rows, span = sizes(a)
        own = pl.ds(order * half, half)
        away = bits[order][0] * (rows // 2) + (1 - bits[order][1]) * (rows // 4)
        return remote(
            bufs[a][0].at[own, pl.ds(pl.multiple_of(away, 16), rows // 4), :], bufs[a][3].at[own],
            send.at[a, 3 + order], recv.at[a, 3 + order], ids[order][1], z,
        )

    def quarter(a, owner):
        rows, span = sizes(a)
        at = slice_of(owner // half, x, y) * (rows // 4)
        return bufs[a][0].at[owner, pl.ds(pl.multiple_of(at, 16), rows // 4), :]

    def owner_copy(a, k):
        to = (z + k) % ring
        return remote(quarter(a, to), bufs[a][4].at[k - 1], send.at[a, 4 + k], recv.at[a, 4 + k], d, to)

    def team_copy(a, t):
        j = 4 + ring + 7 + t
        return remote(bufs[a][5].at[0], bufs[a][5].at[1 + t], send.at[a, j], recv.at[a, j], team_id(d, t), z)

    spots = ((x, y), (1 - x, y), (x, 1 - y), (1 - x, 1 - y))

    def final(a, spot, side):
        rows, span = sizes(a)
        at = slice_of(z // half, *spots[spot]) * (rows // 4)
        return sums[a].at[
            pl.ds(pl.multiple_of(at, 16), rows // 4), pl.ds(pl.multiple_of(side * span, 128), span)
        ]

    def spread(a, j):
        s, r = send.at[a, 4 + ring + j - 1], recv.at[a, 4 + ring + j - 1]
        if j < 4:
            return remote(bufs[a][5].at[0], final(a, 0, core), s, r, (x_id, y_id, far_id)[j - 1], z)
        src = bufs[a][5].at[0] if j == 4 else final(a, j - 4, core)
        return remote(src, final(a, j - 4, core), s, r, core_id, z)

    def spread_here(a, j):
        s, r = send.at[a, 4 + ring + j - 1], recv.at[a, 4 + ring + j - 1]
        ref = final(a, j, core) if j < 4 else final(a, j - 4, 1 - core)
        remote(ref, ref, s, r, core_id, z).wait_recv()

    def keep(a):
        return pltpu.make_async_copy(bufs[a][5].at[0], final(a, 0, core), load.at[count + a])

    def add_slices(target, terms):
        rows = target.shape[0]
        for t in range(rows // 48):
            at = pl.ds(t * 48, 48)
            total = terms[0][at, :].astype(F32)
            for term in terms[1:]:
                total += term[at, :].astype(F32)
            target[at, :] = total.astype(BF16)

    def stage_0(a):
        core_copy(a).start()
        core_load(a).start()

    def stage_1(a):
        core_load(a).wait()
        core_copy(a).wait_recv()
        fold(bufs[a][0], 0, bufs[a][1])
        for order in range(2):
            first_copy(a, order).start()

    def stage_2(a):
        rows, span = sizes(a)
        for order in range(2):
            own = pl.ds(order * half, half)
            first_copy(a, order).wait_recv()
            fold(bufs[a][0].at[own], bits[order][0] * (rows // 2), bufs[a][2].at[own])
            second_copy(a, order).start()

    def stage_3(a):
        rows, span = sizes(a)
        for order in range(2):
            own = pl.ds(order * half, half)
            second_copy(a, order).wait_recv()
            at = slice_of(order, x, y) * (rows // 4)
            fold(bufs[a][0].at[own], at, bufs[a][3].at[own])
        for k in range(1, ring):
            owner_copy(a, k).start()

    def stage_4(a):
        for k in range(1, ring):
            owner_copy(a, k).wait_recv()
        result = bufs[a][5].at[0]
        add_slices(result, [quarter(a, z)] + [bufs[a][4].at[k] for k in range(ring - 1)])
        for t in range(teams):
            team_copy(a, t).start()
            team_copy(a, t).wait()
            add_slices(result, [result, bufs[a][5].at[1 + t]])
        keep(a).start()
        for j in range(1, 5):
            spread(a, j).start()

    def stage_5(a):
        for j in range(1, 4):
            spread_here(a, j)
            spread(a, 4 + j).start()

    def stage_6(a):
        for j in range(4, 8):
            spread_here(a, j)
        core_copy(a).wait_send()
        for order in range(2):
            first_copy(a, order).wait_send()
            second_copy(a, order).wait_send()
        for k in range(1, ring):
            owner_copy(a, k).wait_send()
        for j in range(1, 8):
            spread(a, j).wait_send()
        keep(a).wait()

    return stage_0, stage_1, stage_2, stage_3, stage_4, stage_5, stage_6


def reducer_scratch(grads, teams, ring):
    scratch = []
    for g in grads:
        rows, span = g[1], g[2] // 2
        scratch += [
            pltpu.VMEM((ring, rows, span), BF16),
            pltpu.VMEM((ring, rows, span), BF16),
            pltpu.VMEM((ring, rows // 2, span), BF16),
            pltpu.VMEM((ring, rows // 4, span), BF16),
            pltpu.VMEM((ring - 1, rows // 4, span), BF16),
            pltpu.VMEM((1 + teams, rows // 4, span), BF16),
        ]
    copies = 4 + ring + 7 + teams
    dma = pltpu.SemaphoreType.DMA
    return scratch + [dma((len(grads), copies)), dma((len(grads), copies)), dma((2 * len(grads),))]


def reduce_kernel(count, teams, *refs):
    ring = lax.axis_size("ctx")
    d, z = lax.axis_index("dp"), lax.axis_index("ctx")
    core, x, y, core_id, x_id, y_id = plane(d)
    grads, (small, mixed, back) = refs[:count], refs[count : count + 3]
    refs = refs[count + 3 :]
    sums, (small_out, ret_mixed, ret_back) = refs[:count], refs[count : count + 3]
    refs = refs[count + 3 :]
    bufs = [refs[6 * a : 6 * a + 6] for a in range(count)]
    send, recv, load, small_acc, small_in, s_send, s_recv, r_send, r_recv, r_local = refs[6 * count :]
    batch, piece = ret_mixed.shape[:2]
    greet(teams)
    stages = reducer(teams, grads, sums, bufs, send, recv, load)

    def returned(which, i, to):
        source, target = ((mixed, ret_mixed), (back, ret_back))[which]
        return source.at[pl.ds(pl.multiple_of(to * piece, 16), piece), :], target.at[i]

    mine = z - core
    is_home = (mine >= 0) & (mine < batch)

    def start_returns():
        for which in range(2):
            for i in range(batch):
                @pl.when(mine == i)
                def _(which=which, i=i):
                    for k in range(1, ring):
                        to = (z + k) % ring
                        src, dst = returned(which, i, to)
                        remote(src, dst, r_send.at[which, k], r_recv.at[which, i], d, to).start()
                    src, dst = returned(which, i, z)
                    pltpu.make_async_copy(src, dst, r_local.at[which]).start()

    def wait_returns():
        for which in range(2):
            for i in range(batch):
                src, dst = returned(which, i, z)

                @pl.when(mine == i)
                def _(which=which, i=i, src=src, dst=dst):
                    for k in range(1, ring):
                        to = (z + k) % ring
                        remote(*returned(which, i, to), r_send.at[which, k], r_recv.at[which, i], d, to).wait_send()
                    pltpu.make_async_copy(src, dst, r_local.at[which]).wait()

                @pl.when(mine != i)
                def _(which=which, i=i, src=src, dst=dst):
                    remote(src, dst, r_send.at[which, 0], r_recv.at[which, i], core_id, z).wait_recv()

    steps = [core_id, x_id, y_id] + [team_id(d, t) for t in range(teams)]

    def small_copy(n):
        return remote(small_acc, small_in.at[n], s_send.at[n], s_recv.at[n], steps[n], z)

    def small_owner(k):
        n = len(steps) + k - 1
        return remote(small_acc, small_in.at[n], s_send.at[n], s_recv.at[n], d, (z + k) % ring)

    def small_step(n):
        if n < len(steps):
            if n == 0:
                small_acc[...] = small[...]
            small_copy(n).start()
        elif n == len(steps):
            for k in range(1, ring):
                small_owner(k).start()

    def small_close(n):
        if n < len(steps):
            small_copy(n).wait()
            small_acc[...] += small_in[n]
        elif n == len(steps):
            for k in range(1, ring):
                small_owner(k).wait()
            total = small_acc[...]
            for k in range(ring - 1):
                total += small_in[len(steps) + k]
            small_out[...] = total

    for a in range(count):
        stages[0](a)
    start_returns()
    for n in range(1, max(len(stages), len(steps) + 2)):
        small_step(n - 1)
        if n < len(stages):
            for a in range(count):
                stages[n](a)
        small_close(n - 1)
    wait_returns()


def reduce_all(grads, small, mixed, back, batch):
    ring, groups = lax.axis_size("ctx"), lax.axis_size("dp")
    teams = (groups // 8).bit_length() - 1
    count = len(grads)
    grads = [g.reshape(ring, -1, g.shape[1]) for g in grads]
    length, width = mixed.shape
    dma = pltpu.SemaphoreType.DMA
    anywhere = pl.BlockSpec(memory_space=pl.ANY)
    vmem = pl.BlockSpec(memory_space=pltpu.VMEM)
    rounds = 3 + teams + ring - 1
    scratch = reducer_scratch([g.shape for g in grads], teams, ring)
    scratch += [
        pltpu.VMEM(small.shape, F32), pltpu.VMEM((rounds, *small.shape), F32), dma((rounds,)), dma((rounds,)),
        dma((2, ring)), dma((2, batch)), dma((2,)),
    ]
    token = jax.ShapeDtypeStruct((batch, length // ring, width), BF16)
    return pl.pallas_call(
        functools.partial(reduce_kernel, count, teams),
        in_specs=[anywhere] * count + [vmem, anywhere, anywhere],
        out_specs=[anywhere] * count + [vmem, anywhere, anywhere],
        out_shape=[jax.ShapeDtypeStruct(g.shape[1:], BF16) for g in grads]
        + [jax.ShapeDtypeStruct(small.shape, F32), token, token],
        scratch_shapes=scratch,
        compiler_params=pltpu.CompilerParams(collective_id=1, has_side_effects=True, vmem_limit_bytes=56 * MIB),
        cost_estimate=pl.CostEstimate(flops=0, bytes_accessed=60 * MIB, transcendentals=0),
        name="reduce",
    )(*grads, small, mixed, back)


def attend_kernel(
    teams, order_ref, x_ref, stored_g_ref, norm_ref, bias_ref, cos_ref, low_ref, high_ref, wq_ref, wk_ref, wv_ref,
    wo_ref, up_ref, down_ref, out_ref, h_ref, dq_ref, dk_ref, dv_ref, dwo_ref, dbias_ref, small_ref, up_sum, down_sum,
    g_ref, a_ref, acc_ref, da_ref, q_ref, k_ref, v_ref, do_ref, o_ref, dqs_ref, dks_ref, dvs_ref, *reduce_refs,
):
    step = pl.program_id(0)
    bufs = (reduce_refs[:6], reduce_refs[6:12])
    stages = reducer(teams, (up_ref, down_ref), (up_sum, down_sum), bufs, *reduce_refs[12:])

    plan = {
        (0, 2): ((1, 0),), (0, 4): ((1, 1),), (1, 0): ((2, 0),), (1, 3): ((2, 1),), (1, 5): ((3, 0),),
        (1, 7): ((3, 1),), (2, 2): ((4, 0),), (2, 4): ((4, 1),), (2, 6): ((5, 0), (5, 1)),
    }

    @pl.when(step == 0)
    def _():
        greet(teams)
        stages[0](0)
        stages[0](1)

    last = pl.num_programs(0) - 1
    rows, width = x_ref.shape
    lanes = QUAD * HD
    tile = 256
    half = ROT // 2
    scale = 1.0 / math.sqrt(HD)
    blocks = rows // BLOCK
    mine = lax.axis_index("ctx") - lax.axis_index("dp") % 2
    is_home = (mine >= 0) & (mine < SEQS)

    def stored(ref, at):
        values = ref[pl.ds(at * BLOCK, BLOCK), :]
        return jnp.where(is_home, values, jnp.zeros_like(values))

    @pl.when(step == 0)
    def _():
        for j in range(blocks):
            place = order_ref[1, j]
            at = pl.ds(j * BLOCK, BLOCK)
            xh, _ = normalized(stored(x_ref, place).astype(F32))
            a_ref[at, :] = (xh * norm_ref[0:1, :] + norm_ref[1:2, :]).astype(BF16)
            g_ref[at, :] = stored(stored_g_ref, place)
        acc_ref[...] = jnp.zeros_like(acc_ref)
        da_ref[...] = jnp.zeros_like(da_ref)

    def table(ref, at):
        values = ref[at, :]
        return jnp.concatenate([values] * (lanes // values.shape[1]), axis=1)

    def turn(values, at):
        low = pltpu.roll(values, lanes - half, 1) * table(low_ref, at)
        high = pltpu.roll(values, half, 1) * table(high_ref, at)
        return values * table(cos_ref, at), low + high

    for t in range(rows // tile):
        at = pl.ds(t * tile, tile)
        a = a_ref[at, :]
        same, cross = turn(dot(a, wq_ref[...]) + bias_ref[...], at)
        q_ref[at, :] = ((same + cross).astype(BF16) * scale).astype(BF16)
        same, cross = turn(dot(a, wk_ref[...]), at)
        k_ref[at, :] = (same + cross).astype(BF16)
        v_ref[at, :] = dot(a, wv_ref[...]).astype(BF16)
        do_ref[at, :] = dot(g_ref[at, :], wo_ref[...], NT).astype(BF16)

    dks_ref[...] = jnp.zeros_like(dks_ref)
    dvs_ref[...] = jnp.zeros_like(dvs_ref)
    head_of = lax.broadcasted_iota(jnp.int32, (BLOCK, lanes), 1) // HD

    def stack(values):
        zero = jnp.zeros_like(values)
        return jnp.concatenate([jnp.where(head_of == e, values, zero) for e in range(QUAD)], axis=0)

    def merge(values):
        out = values[:BLOCK]
        for e in range(1, QUAD):
            out = jnp.where(head_of == e, values[e * BLOCK : (e + 1) * BLOCK], out)
        return out

    spot = lax.broadcasted_iota(jnp.int32, (QUAD * BLOCK, BLOCK), 0) % BLOCK
    admitted = lax.broadcasted_iota(jnp.int32, (QUAD * BLOCK, BLOCK), 1) <= spot
    for b in range(rows // BLOCK):
        for (when, block), work in plan.items():
            if block == b:
                @pl.when(step == when)
                def _(work=work):
                    for n, a in work:
                        stages[n](a)
        at = pl.ds(b * BLOCK, BLOCK)
        seen = pl.ds(0, (b + 1) * BLOCK)
        q = stack(q_ref[at, :])
        do_block = do_ref[at, :]
        do = stack(do_block)
        keys = k_ref[seen, :]
        values = v_ref[seen, :]
        scores = dot(q, keys, NT)
        edge = jnp.where(admitted, scores[:, b * BLOCK :], -1e30)
        scores = edge if b == 0 else jnp.concatenate([scores[:, : b * BLOCK], edge], axis=1)
        top = jnp.max(scores, axis=-1, keepdims=True)
        expo = jnp.exp(scores - top)
        probs = expo * (1.0 / jnp.sum(expo, axis=-1, keepdims=True))
        low = probs.astype(BF16)
        mixed = dot(low, values)
        o_ref[at, :] = merge(mixed).astype(BF16)
        share = jnp.sum(mixed * do.astype(F32), axis=-1, keepdims=True)
        back = (probs * (dot(do, values, NT) - share)).astype(BF16)
        dqs_ref[at, :] = merge(dot(back, keys)) * scale
        dks_ref[seen, :] += dot(back, q, TN)
        dvs_ref[seen, :] += dot(low, do, TN)

    total = jnp.zeros((1, lanes), F32)
    for t in range(rows // tile):
        at = pl.ds(t * tile, tile)
        same, cross = turn(dqs_ref[at, :], at)
        dq = (same - cross).astype(BF16)
        same, cross = turn(dks_ref[at, :], at)
        dk = (same - cross).astype(BF16)
        dv = dvs_ref[at, :].astype(BF16)
        total += jnp.sum(dq.astype(F32), axis=0, keepdims=True)
        q_ref[at, :] = dq
        k_ref[at, :] = dk
        v_ref[at, :] = dv
        acc_ref[at, :] += dot(o_ref[at, :], wo_ref[...])
        da_ref[at, :] += dot(dq, wq_ref[...], NT) + dot(dk, wk_ref[...], NT) + dot(dv, wv_ref[...], NT)
    dbias_ref[...] = total
    dwo_ref[...] = dot(o_ref[...], g_ref[...], TN).astype(BF16)
    dq_ref[...] = dot(a_ref[...], q_ref[...], TN).astype(BF16)
    dk_ref[...] = dot(a_ref[...], k_ref[...], TN).astype(BF16)
    dv_ref[...] = dot(a_ref[...], v_ref[...], TN).astype(BF16)

    @pl.when(step == last)
    def _():
        gain = jnp.zeros((1, width), F32)
        shift = jnp.zeros((1, width), F32)
        for s in range(blocks):
            at = pl.ds(s * BLOCK, BLOCK)
            sorted_at = pl.ds(order_ref[0, s] * BLOCK, BLOCK)
            xh, _ = normalized(stored(x_ref, s).astype(F32))
            da = da_ref[sorted_at, :]
            gain += jnp.sum(da * xh, axis=0, keepdims=True)
            shift += jnp.sum(da, axis=0, keepdims=True)
            h_ref[at, :] = (da * norm_ref[0:1, :]).astype(BF16)
            out_ref[at, :] = acc_ref[sorted_at, :].astype(BF16)
        small_ref[0:1, :] = gain
        small_ref[1:2, :] = shift
        stages[6](0)
        stages[6](1)


def attend(order, x, g, norms, bias_q, tables, weights, up, down):
    ring, groups_dp = lax.axis_size("ctx"), lax.axis_size("dp")
    teams = (groups_dp // 8).bit_length() - 1
    up, down = (g_.reshape(ring, -1, g_.shape[1]) for g_ in (up, down))
    anywhere = pl.BlockSpec(memory_space=pl.ANY)
    rows, width = x.shape
    lanes = QUAD * HD
    groups = width // lanes
    whole = lambda shape: pl.BlockSpec(shape, lambda i: (0,) * len(shape))
    column = pl.BlockSpec((width, lanes), lambda i: (0, i))
    once = lambda shape: pl.BlockSpec(shape, lambda i: (0,) * len(shape), pipeline_mode=pl.Buffered(1))
    small = jax.ShapeDtypeStruct((rows, width), BF16)
    return pl.pallas_call(
        functools.partial(attend_kernel, teams),
        grid=(groups,),
        in_specs=[
            pl.BlockSpec(memory_space=pltpu.SMEM),
            once((rows, width)),
            once((rows, width)),
            once(norms.shape),
            pl.BlockSpec((1, lanes), lambda i: (0, i)),
            once(tables[0].shape),
            once(tables[0].shape),
            once(tables[0].shape),
            pl.BlockSpec((width, lanes), lambda i: (0, i)),
            pl.BlockSpec((width, lanes), lambda i: (0, groups + i)),
            pl.BlockSpec((width, lanes), lambda i: (0, 2 * groups + i)),
            pl.BlockSpec((lanes, width), lambda i: (i, 3)),
            anywhere,
            anywhere,
        ],
        out_specs=[
            whole((rows, width)),
            whole((rows, width)),
            column,
            column,
            column,
            pl.BlockSpec((lanes, width), lambda i: (i, 0)),
            pl.BlockSpec((1, lanes), lambda i: (0, i)),
            whole((8, width)),
            anywhere,
            anywhere,
        ],
        out_shape=[
            small,
            small,
            jax.ShapeDtypeStruct((width, width), BF16),
            jax.ShapeDtypeStruct((width, width), BF16),
            jax.ShapeDtypeStruct((width, width), BF16),
            jax.ShapeDtypeStruct((width, width), BF16),
            jax.ShapeDtypeStruct((1, width), F32),
            jax.ShapeDtypeStruct((8, width), F32),
            jax.ShapeDtypeStruct(up.shape[1:], BF16),
            jax.ShapeDtypeStruct(down.shape[1:], BF16),
        ],
        scratch_shapes=[
            pltpu.VMEM((rows, width), BF16),
            pltpu.VMEM((rows, width), BF16),
            pltpu.VMEM((rows, width), F32),
            pltpu.VMEM((rows, width), F32),
        ]
        + [pltpu.VMEM((rows, lanes), BF16)] * 5
        + [pltpu.VMEM((rows, lanes), F32)] * 3
        + reducer_scratch((up.shape, down.shape), teams, ring),
        compiler_params=pltpu.CompilerParams(
            collective_id=2, has_side_effects=True, vmem_limit_bytes=60 * MIB
        ),
        cost_estimate=pl.CostEstimate(
            flops=24 * rows * width * width + 8 * rows * rows * width,
            bytes_accessed=16 * width * width + 8 * rows * width,
            transcendentals=HEADS * rows * rows // 2,
        ),
        name="attend",
    )(order, x, g, norms, bias_q, *tables, weights, weights, weights, weights, up, down)


def rotary_tables(length):
    half = ROT // 2
    frequency = ROPE_BASE ** (-(np.arange(half) * 2.0 / ROT))
    angle = np.arange(length)[:, None] * frequency[None, :]
    cosine, sine = np.cos(angle), np.sin(angle)
    rest = np.zeros((length, HD - ROT))
    none = np.zeros_like(sine)
    cos_full = np.concatenate([cosine, cosine, rest + 1.0], axis=1)
    low = np.concatenate([-sine, none, rest], axis=1)
    high = np.concatenate([none, sine, rest], axis=1)
    return tuple(jnp.asarray(np.tile(t, (1, 2)).astype(np.float32)) for t in (cos_full, low, high))


def adamw(weight, grad, first, second, rate, decay):
    first_new = BETA_ONE * first + (1.0 - BETA_ONE) * grad
    second_new = BETA_TWO * second + (1.0 - BETA_TWO) * grad * grad
    first_hat = first_new / (1.0 - BETA_ONE**STEP)
    second_hat = second_new / (1.0 - BETA_TWO**STEP)
    weight_new = weight - rate * (first_hat / (jnp.sqrt(second_hat) + EPS_ADAM) + decay * weight)
    return (first_new, second_new, weight_new)


def shards(
    tokens, out_grad, block_order, qkv_weight, out_weight, up_weight, down_weight, norm_params, bias_params,
    qkv_first, qkv_second, out_first, out_second, up_first, up_second, down_first, down_second,
    norm_first, norm_second, bias_first, bias_second,
):
    groups, ring = lax.axis_size("dp"), lax.axis_size("ctx")
    group, rank = lax.axis_index("dp"), lax.axis_index("ctx")
    batch, piece, width = tokens.shape
    length = piece * ring
    count = batch * piece
    ff = up_weight.shape[1]

    att_weight = jnp.concatenate([qkv_weight, out_weight], axis=1).astype(BF16)
    share = bias_params.shape[0]
    wide = jnp.zeros((4, width), F32)
    own_norms = lax.dynamic_update_slice(wide, norm_params.astype(BF16).astype(F32), (0, rank * (width // ring)))
    own_biases = jnp.zeros((ring * share,), F32)
    own_biases = lax.dynamic_update_slice(own_biases, bias_params.astype(BF16).astype(F32), (rank * share,))
    others = jnp.concatenate([own_biases[: 2 * width], own_biases[2 * width + ff :], jnp.zeros((ff - 3 * width,), F32)])
    small = jnp.stack([own_biases[2 * width : 2 * width + ff], others, own_norms.reshape(-1)])
    small = jnp.pad(small, ((0, 5), (0, 0)))
    x_rows, g_rows = tokens.reshape(count, width), out_grad.reshape(count, width)
    att_copy, small, home_x, home_g, feed_out, h_feed, dup, ddown, dbias_up, small_feed = gather_feed(
        up_weight.astype(BF16), down_weight.astype(BF16), att_weight, small, x_rows, g_rows, piece
    )
    norms = small[2].reshape(4, width)
    bias_q = small[1:2, :width]

    odd = group % 2

    order = block_order[jnp.clip(rank - odd, 0, batch - 1)]
    spots = jnp.arange(order.shape[0])
    order = jnp.stack([order, jnp.sum(jnp.where(order[None, :] == spots[:, None], spots[None, :], 0), axis=1)])

    attend_out, h_attend, dq, dk, dv, dout, dbias_q, small_attend, up_grad, down_grad = attend(
        order, home_x, home_g, norms, bias_q, rotary_tables(length), att_copy, dup, ddown
    )

    dqkv = jnp.concatenate([dq, dk, dv], axis=1)
    tail = jnp.concatenate(
        [small_attend[:2].reshape(-1), small_feed[:2].reshape(-1), dbias_q[0], small_feed[2], dbias_up[0], small_feed[2]]
    )
    entries = tail.shape[0]
    tail = jnp.pad(tail, (0, -entries % 1024)).reshape(-1, 128)
    *owned, tail, ret_mixed, ret_back = reduce_all((dqkv, dout), tail, attend_out, h_attend, batch)
    up_grad, down_grad, qkv_grad, out_grads = (g.astype(F32) for g in (up_grad, down_grad, *owned))
    tail = tail.reshape(-1)[:entries]
    returned = [v.reshape(count, width).astype(F32) for v in (ret_mixed, ret_back)]

    rows = x_rows.astype(F32)
    bias_rows = small[1:2, width : 2 * width] + small[1:2, 2 * width : 3 * width]
    layer_out = (rows + returned[0] + feed_out + bias_rows).astype(BF16).reshape(batch, piece, width)
    xh, scale = normalized(rows)
    h = returned[1] + h_feed
    inner = jnp.mean(h * xh, axis=-1, keepdims=True)
    input_grad = g_rows.astype(F32) + scale * (h - jnp.mean(h, axis=-1, keepdims=True) - xh * inner)
    input_grad = input_grad.reshape(batch, piece, width)

    norm_grad = lax.dynamic_slice_in_dim(tail[: 4 * width].reshape(4, width), rank * (width // ring), width // ring, 1)
    bias_grad = lax.dynamic_slice_in_dim(tail[4 * width :], rank * share, share, 0)

    qkv_new = adamw(qkv_weight, qkv_grad, qkv_first, qkv_second, 0.1, DECAY)
    out_new = adamw(out_weight, out_grads, out_first, out_second, 0.6, DECAY)
    up_new = adamw(up_weight, up_grad, up_first, up_second, 0.1, DECAY)
    down_new = adamw(down_weight, down_grad, down_first, down_second, 0.05, DECAY)
    norm_new = adamw(norm_params, norm_grad, norm_first, norm_second, 0.6, 0.0)
    bias_new = adamw(bias_params, bias_grad, bias_first, bias_second, 0.6, 0.0)
    return (
        layer_out, input_grad, *qkv_new, *out_new, *up_new, *down_new,
        norm_new[0], norm_new[1][:2], norm_new[1][2:], norm_new[2], *bias_new,
    )


def solution(mesh):
    rows, columns, token = P("ctx", None), P(None, "ctx"), P("dp", "ctx", None)
    in_specs = (token, token, P("dp", None)) + (rows,) * 4 + (columns, P("ctx")) + (rows,) * 8
    in_specs += (columns, columns, P("ctx"), P("ctx"))
    out_specs = (token, token) + (rows,) * 12 + (columns,) * 4 + (P("ctx"),) * 3
    return jax.shard_map(shards, mesh=mesh, in_specs=in_specs, out_specs=out_specs, check_vma=False)
```

```python
import functools
import math

import jax
import jax.numpy as jnp
import numpy as np
from jax import lax
from jax.experimental import pallas as pl
from jax.experimental.pallas import tpu as pltpu
from jax.sharding import PartitionSpec as P

HEADS = 12
HD = 64
STEP = 10
ROT = 16
SEQS = 3
BLOCK = 128
QUAD = 4

EPS_NORM = 1e-05
BETA_ONE = 0.9
BETA_TWO = 0.95
EPS_ADAM = 1e-08
DECAY = 0.01
ROPE_BASE = 10000.0
F32 = jnp.float32
BF16 = jnp.bfloat16
MIB = 1024 * 1024


def dot(left, right, dims=((1,), (0,))):
    return lax.dot_general(left, right, (dims, ((), ())), preferred_element_type=F32)


NN = ((1,), (0,))
NT = ((1,), (1,))
TN = ((0,), (0,))


def normalized(values):
    mean = jnp.mean(values, axis=-1, keepdims=True)
    centred = values - mean
    variance = jnp.mean(centred * centred, axis=-1, keepdims=True)
    scale = lax.rsqrt(variance + EPS_NORM)
    return centred * scale, scale


MESH = pl.DeviceIdType.MESH


def plane(d):
    core, x, y = d % 2, d // 2 % 2, d // 4 % 2
    return core, x, y, d + 1 - 2 * core, d + 2 - 4 * x, d + 4 - 8 * y


def gather_kernel(
    up, down, att, small, tokens, cotangents,
    att_all, small_all, home_x, home_g, out_ref, h_ref, up_part, down_part, dbias_ref, sums_ref,
    up_all, down_all, small_in, x_ref, g_ref, m_ref, hid_ref, dup_in_ref,
    dup_ref, up_core, up_first, up_second, ddown_ref, down_core, down_first, down_second,
    z_send, z_recv, p_send, p_recv, s_send, s_recv, t_send, t_recv, local, out_sem, c_send, c_recv,
):
    ring = lax.axis_size("ctx")
    d, z = lax.axis_index("dp"), lax.axis_index("ctx")
    core, x, y, core_id, x_id, y_id = plane(d)
    own = x + 2 * y
    own_x, own_y, far = own + 1 - 2 * x, own + 2 - 4 * y, 3 - own
    count, width = tokens.shape
    piece = home_x.shape[0] // ring
    batch = count // piece
    arrays = ((up, up_all, False), (down, down_all, True), (att, att_all, False))

    def slot(a, base, place, half=None):
        source, whole, tall = arrays[a]
        ref = source if base is None else whole
        rows, columns = source.shape
        at = 0 if base is None else base * rows
        height, span = rows // 4, columns // 2
        at = at + place * height
        column = core * span
        if half is not None:
            if tall:
                height = height // 2
                at = at + half * height
            else:
                span = span // 2
                column = column + half * span
        return ref.at[pl.ds(pl.multiple_of(at, 16), height), pl.ds(pl.multiple_of(column, 128), span)]

    def other_slot(a, base, place):
        source, whole, tall = arrays[a]
        rows, columns = source.shape
        at = pl.multiple_of(base * rows + place * (rows // 4), 16)
        column = pl.multiple_of((1 - core) * (columns // 2), 128)
        return whole.at[pl.ds(at, rows // 4), pl.ds(column, columns // 2)]

    def remote(src, dst, send, recv, dp, ctx):
        return pltpu.make_async_remote_copy(
            src_ref=src, dst_ref=dst, send_sem=send, recv_sem=recv, device_id=(dp, ctx), device_id_type=MESH
        )

    barrier = pltpu.get_barrier_semaphore()
    for k in range(1, ring):
        pl.semaphore_signal(barrier, inc=1, device_id=(d, (z + k) % ring), device_id_type=MESH)
    for other in (core_id, x_id, y_id):
        pl.semaphore_signal(barrier, inc=1, device_id=(other, z), device_id_type=MESH)
    pl.semaphore_wait(barrier, ring + 2)

    def hop(a, way, h):
        shard = z - h if way == 0 else z + h
        target = z + 1 if way == 0 else z - 1
        src = slot(a, None, own) if h == 0 else slot(a, shard, own)
        return remote(src, slot(a, shard, own), z_send.at[a, way, h], z_recv.at[a, way, h], d, target)

    def can_send(way, h):
        shard = z - h if way == 0 else z + h
        target = z + 1 if way == 0 else z - 1
        return (shard >= 0) & (shard < ring) & (target >= 0) & (target < ring)

    def in_range(way, h):
        shard = z - h if way == 0 else z + h
        return (shard >= 0) & (shard < ring)

    def cast(a, shard, j):
        send, recv = p_send.at[a, shard, j], p_recv.at[a, shard, j]
        if j == 0:
            ref = slot(a, shard, own)
            return remote(ref, ref, send, recv, x_id, z)
        if j == 1:
            ref = slot(a, shard, own)
            return remote(ref, ref, send, recv, y_id, z)
        if j == 2:
            ref = slot(a, shard, own_x, 0)
            return remote(ref, ref, send, recv, y_id, z)
        if j == 3:
            ref = slot(a, shard, own_y, 1)
            return remote(ref, ref, send, recv, x_id, z)
        ref = slot(a, shard, (own, own_x, own_y, far)[j - 4])
        return remote(ref, ref, send, recv, core_id, z)

    def arrived(a, shard, j):
        send, recv = p_send.at[a, shard, j], p_recv.at[a, shard, j]
        ref = {0: lambda: slot(a, shard, own_x), 1: lambda: slot(a, shard, own_y),
               2: lambda: slot(a, shard, far, 0), 3: lambda: slot(a, shard, far, 1)}.get(
            j, lambda: other_slot(a, shard, (own, own_x, own_y, far)[j - 4]))()
        remote(ref, ref, send, recv, core_id, z).wait_recv()

    def start_hops(a):
        for way in range(2):
            @pl.when(can_send(way, 0))
            def _(way=way):
                hop(a, way, 0).start()

    def small_copy(k):
        return remote(small, small_in.at[ring - k], s_send.at[k], s_recv.at[k], d, (z + k) % ring)

    def stage_a(a, h):
        for way in range(2):
            @pl.when(in_range(way, h))
            def _(way=way):
                shard = z - h if way == 0 else z + h
                ref = slot(a, shard, own)
                remote(ref, ref, z_send.at[a, way, h - 1], z_recv.at[a, way, h - 1], core_id, z).wait_recv()

                @pl.when(can_send(way, h))
                def _():
                    hop(a, way, h).start()

                cast(a, shard, 0).start()
                cast(a, shard, 1).start()
                cast(a, shard, 4).start()

    def stage_b(a, h):
        for way in range(2):
            @pl.when(in_range(way, h))
            def _(way=way):
                shard = z - h if way == 0 else z + h
                arrived(a, shard, 0)
                cast(a, shard, 2).start()
                cast(a, shard, 5).start()
                arrived(a, shard, 1)
                cast(a, shard, 3).start()
                cast(a, shard, 6).start()

    def stage_c(a, h):
        for way in range(2):
            @pl.when(in_range(way, h))
            def _(way=way):
                shard = z - h if way == 0 else z + h
                arrived(a, shard, 2)
                arrived(a, shard, 3)
                cast(a, shard, 7).start()

    def stage_d(a, h):
        for way in range(2):
            @pl.when(in_range(way, h))
            def _(way=way):
                shard = z - h if way == 0 else z + h
                for j in range(4, 8):
                    arrived(a, shard, j)

    pairs = ((tokens, home_x), (cotangents, home_g))

    def move(which, i):
        source, whole = pairs[which]
        src = source.at[pl.ds(i * piece, piece), :]
        dst = whole.at[pl.ds(pl.multiple_of(z * piece, 16), piece), :]
        return src, dst, i + core

    def start_moves(which):
        for i in range(batch):
            src, dst, target = move(which, i)

            @pl.when(target != z)
            def _(src=src, dst=dst, target=target, i=i):
                remote(src, dst, t_send.at[which, i], t_recv.at[which, z], d, target).start()

            @pl.when(target == z)
            def _(src=src, dst=dst):
                pltpu.make_async_copy(src, dst, local.at[6 + which]).start()

    own_copies = []
    for a in range(3):
        source, whole, _ = arrays[a]
        rows = source.shape[0]
        at = pl.ds(pl.multiple_of(z * rows, 16), rows)
        own_copies.append(pltpu.make_async_copy(source, whole.at[at, :], local.at[a]))
    x_load = pltpu.make_async_copy(tokens, x_ref, local.at[3])
    g_load = pltpu.make_async_copy(cotangents, g_ref, local.at[4])
    own_small = pltpu.make_async_copy(small, small_in.at[0], local.at[5])

    for a in range(3):
        start_hops(a)
    for k in range(1, ring):
        small_copy(k).start()
    for copy in own_copies + [x_load, g_load, own_small]:
        copy.start()
    hops = range(1, ring)
    work = [(a, h) for a in range(3) for h in hops]
    early = 2 * (ring - 1)
    for n in range(len(work)):
        stage_a(*work[n])
        if 1 <= n <= early:
            stage_b(*work[n - 1])
        if 2 <= n <= early + 1:
            stage_c(*work[n - 2])
    start_moves(0)
    start_moves(1)

    own_small.wait()
    for k in range(1, ring):
        ref = small_in.at[ring - k]
        remote(ref, ref, s_send.at[k], s_recv.at[k], core_id, z).wait_recv()
    x_load.wait()
    g_load.wait()
    total = small_in[0]
    for k in range(1, ring):
        total += small_in[k]
    small_all[...] = total
    ff = up_all.shape[1]
    gain_2, shift_2 = small_all[2:3, 2 * width : 3 * width], small_all[2:3, 3 * width : 4 * width]
    tile = 256
    tiles = count // tile
    for t in range(tiles):
        at = pl.ds(t * tile, tile)
        xh, _ = normalized(x_ref[at, :].astype(F32))
        m_ref[at, :] = (xh * gain_2 + shift_2).astype(BF16)
        out_ref[at, :] = jnp.zeros((tile, width), F32)
        h_ref[at, :] = jnp.zeros((tile, width), F32)
    own_copies[0].wait()
    own_copies[1].wait()
    for h in hops:
        stage_d(0, h)
        stage_d(1, h)

    strip = dup_ref.shape[3] // ring
    steps = ff // (ring * strip)
    half = ring // 2
    big, by_core = (dup_ref, ddown_ref), (up_core, down_core)
    by_first, by_second = (up_first, down_first), (up_second, down_second)
    bits, ids = ((x, y), (y, x)), ((x_id, y_id), (y_id, x_id))

    def sizes(a):
        return by_core[a].shape[2], by_core[a].shape[3]

    def slice_of(order):
        return 2 * bits[order][0] + bits[order][1]

    def core_copy(a, i):
        _, span = sizes(a)
        away = pl.ds(pl.multiple_of((1 - core) * span, 128), span)
        return remote(big[a].at[i, :, :, away], by_core[a].at[i], c_send.at[a, i, 0], c_recv.at[a, i, 0], core_id, z)

    def first_copy(a, i, order):
        height, _ = sizes(a)
        own = pl.ds(order * half, half)
        away = pl.ds(pl.multiple_of((1 - bits[order][0]) * (height // 2), 16), height // 2)
        return remote(
            by_core[a].at[i, own, away, :], by_first[a].at[i, own], c_send.at[a, i, 1 + order],
            c_recv.at[a, i, 1 + order], ids[order][0], z,
        )

    def second_copy(a, i, order):
        height, _ = sizes(a)
        own = pl.ds(order * half, half)
        away = bits[order][0] * (height // 2) + (1 - bits[order][1]) * (height // 4)
        return remote(
            by_core[a].at[i, own, pl.ds(pl.multiple_of(away, 16), height // 4), :], by_second[a].at[i, own],
            c_send.at[a, i, 3 + order], c_recv.at[a, i, 3 + order], ids[order][1], z,
        )

    def add(into, at, term, owners):
        height = term(0).shape[0]
        tile = 32 if height % 48 else 48

        def body(n, _):
            o, t = n // (height // tile), n % (height // tile)
            spot = pl.ds(pl.multiple_of(at + t * tile, 16), tile)
            value = term(o)[pl.ds(pl.multiple_of(t * tile, 16), tile), :]
            into[o, spot, :] = (into[o, spot, :].astype(F32) + value.astype(F32)).astype(BF16)
            return 0

        lax.fori_loop(0, owners * (height // tile), body, 0)

    def chunk_1(a, i):
        _, span = sizes(a)
        core_copy(a, i).wait_recv()
        keep = pl.ds(pl.multiple_of(core * span, 128), span)
        add(by_core[a].at[i], 0, lambda o: big[a].at[i, o, :, keep], ring)
        for order in range(2):
            first_copy(a, i, order).start()

    def chunk_2(a, i):
        height, _ = sizes(a)
        for order in range(2):
            own = pl.ds(order * half, half)
            first_copy(a, i, order).wait_recv()
            at = bits[order][0] * (height // 2)
            add(by_core[a].at[i, own], at, lambda o: by_first[a].at[i, order * half + o], half)
            second_copy(a, i, order).start()

    def parts_out(a, i, order):
        height, span = sizes(a)
        own = pl.ds(order * half, half)
        rows = pl.ds(pl.multiple_of(slice_of(order) * (height // 4), 16), height // 4)
        if a == 1:
            return [pltpu.make_async_copy(
                by_core[1].at[i, own, rows, :], down_part.at[own, i], out_sem.at[i, 2 * half + order]
            )]
        return [
            pltpu.make_async_copy(
                by_core[0].at[i, own, rows, pl.ds(n * strip, strip)],
                up_part.at[own, :, pl.ds(pl.multiple_of(n * steps * strip + i * strip, 128), strip)],
                out_sem.at[i, half * order + n],
            )
            for n in range(half)
        ]

    def chunk_3(a, i):
        height, _ = sizes(a)
        for order in range(2):
            own = pl.ds(order * half, half)
            second_copy(a, i, order).wait_recv()
            at = slice_of(order) * (height // 4)
            add(by_core[a].at[i, own], at, lambda o: by_second[a].at[i, order * half + o], half)
            for copy in parts_out(a, i, order):
                copy.start()

    def feed_step(step, _):
        for h in hops:
            @pl.when(step == h - 1)
            def _(h=h):
                stage_b(2, h)

            @pl.when(step == h)
            def _(h=h):
                stage_c(2, h)

        @pl.when(step < steps)
        def _():
            spots = [pl.ds(pl.multiple_of(r * (ff // ring) + step * strip, 128), strip) for r in range(ring)]
            up_part_ = jnp.concatenate([up_all[:, at] for at in spots], axis=1)
            down_part_ = jnp.concatenate([down_all[at, :] for at in spots], axis=0)
            bias = jnp.concatenate([small_all[0:1, at] for at in spots], axis=1)
            total = jnp.zeros((1, ring * strip), F32)
            for t in range(tiles):
                at = pl.ds(t * tile, tile)
                u = dot(m_ref[at, :], up_part_) + bias
                cdf = 0.5 * (1.0 + lax.erf(u * (1.0 / math.sqrt(2.0))))
                hidden = (u * cdf).astype(BF16)
                slope = cdf + u * jnp.exp(-0.5 * u * u) * (1.0 / math.sqrt(2.0 * math.pi))
                back = (dot(g_ref[at, :], down_part_, NT) * slope).astype(BF16)
                hid_ref[at, :] = hidden
                dup_in_ref[at, :] = back
                total += jnp.sum(back.astype(F32), axis=0, keepdims=True)
                out_ref[at, :] += dot(hidden, down_part_)
                h_ref[at, :] += dot(back, up_part_, NT)
            for r in range(ring):
                dbias_ref[0:1, spots[r]] = total[:, r * strip : (r + 1) * strip]
            ddown = dot(hid_ref[...], g_ref[...], TN).astype(BF16)
            dup = dot(m_ref[...], dup_in_ref[...], TN).astype(BF16)
            for r in range(ring):
                ddown_ref[step, r] = ddown[r * strip : (r + 1) * strip, :]
                dup_ref[step, r] = dup[r * (width // ring) : (r + 1) * (width // ring), :]
            core_copy(0, step).start()
            core_copy(1, step).start()

        for lag, stage in ((1, chunk_1), (3, chunk_2), (5, chunk_3)):
            @pl.when((step >= lag) & (step < steps + lag))
            def _(lag=lag, stage=stage):
                stage(0, step - lag)
                stage(1, step - lag)

        return 0

    lax.fori_loop(0, steps + 5, feed_step, 0)

    gain = jnp.zeros((1, width), F32)
    shift = jnp.zeros((1, width), F32)
    sums = jnp.zeros((1, width), F32)
    for t in range(tiles):
        at = pl.ds(t * tile, tile)
        xh, _ = normalized(x_ref[at, :].astype(F32))
        dm = h_ref[at, :]
        gain += jnp.sum(dm * xh, axis=0, keepdims=True)
        shift += jnp.sum(dm, axis=0, keepdims=True)
        sums += jnp.sum(g_ref[at, :].astype(F32), axis=0, keepdims=True)
        h_ref[at, :] = dm * gain_2
    sums_ref[...] = jnp.concatenate([gain, shift, sums, jnp.zeros((5, width), F32)], axis=0)

    mine = z - core
    for which in range(2):
        for k in range(1, ring):
            @pl.when((mine >= 0) & (mine < batch))
            def _(which=which, k=k):
                other = (z + k) % ring
                ref = pairs[which][1].at[pl.ds(pl.multiple_of(other * piece, 16), piece), :]
                remote(ref, ref, t_send.at[which, 0], t_recv.at[which, other], core_id, z).wait_recv()
    for h in hops:
        stage_d(2, h)
    for k in range(1, ring):
        small_copy(k).wait_send()
    for a in range(3):
        for way in range(2):
            for h in range(ring - 1):
                @pl.when(can_send(way, h))
                def _(a=a, way=way, h=h):
                    hop(a, way, h).wait_send()
        for h in hops:
            for way in range(2):
                @pl.when(in_range(way, h))
                def _(a=a, h=h, way=way):
                    shard = z - h if way == 0 else z + h
                    for j in range(8):
                        cast(a, shard, j).wait_send()
    for which in range(2):
        for i in range(batch):
            src, dst, target = move(which, i)

            @pl.when(target != z)
            def _(src=src, dst=dst, target=target, which=which, i=i):
                remote(src, dst, t_send.at[which, i], t_recv.at[which, z], d, target).wait_send()

            @pl.when(target == z)
            def _(src=src, dst=dst, which=which):
                pltpu.make_async_copy(src, dst, local.at[6 + which]).wait()
    own_copies[2].wait()

    def close(i, _):
        for a in range(2):
            core_copy(a, i).wait_send()
            for order in range(2):
                first_copy(a, i, order).wait_send()
                second_copy(a, i, order).wait_send()
                for copy in parts_out(a, i, order):
                    copy.wait()
        return 0

    lax.fori_loop(0, steps, close, 0)


def gather_feed(up, down, att, small, tokens, cotangents, piece):
    ring = lax.axis_size("ctx")
    count, width = tokens.shape
    ff = up.shape[1]
    strip = 128
    chunk = ring * strip
    steps = ff // chunk
    shard = up.shape[0]
    full = lambda v: jax.ShapeDtypeStruct((ring * v.shape[0], v.shape[1]), v.dtype)
    home = jax.ShapeDtypeStruct((ring * piece, width), tokens.dtype)
    rows = jax.ShapeDtypeStruct((count, width), F32)
    dma = pltpu.SemaphoreType.DMA
    anywhere = pl.BlockSpec(memory_space=pl.ANY)
    vmem = pl.BlockSpec(memory_space=pltpu.VMEM)
    return pl.pallas_call(
        gather_kernel,
        in_specs=[anywhere] * 6,
        out_specs=[anywhere, vmem, anywhere, anywhere, vmem, vmem, anywhere, anywhere, vmem, vmem],
        out_shape=[
            full(att), jax.ShapeDtypeStruct(small.shape, F32), home, home, rows, rows,
            jax.ShapeDtypeStruct((ring, shard // 4, ff // 2), BF16),
            jax.ShapeDtypeStruct((ring, steps, strip // 4, width // 2), BF16),
            jax.ShapeDtypeStruct((8, ff), F32), jax.ShapeDtypeStruct((8, width), F32),
        ],
        scratch_shapes=[
            pltpu.VMEM(full(up).shape, BF16), pltpu.VMEM(full(down).shape, BF16),
            pltpu.VMEM((ring, *small.shape), F32),
            pltpu.VMEM((count, width), BF16), pltpu.VMEM((count, width), BF16), pltpu.VMEM((count, width), BF16),
            pltpu.VMEM((count, chunk), BF16), pltpu.VMEM((count, chunk), BF16),
            pltpu.VMEM((steps, ring, shard, chunk), BF16), pltpu.VMEM((steps, ring, shard, chunk // 2), BF16),
            pltpu.VMEM((steps, ring, shard // 2, chunk // 2), BF16),
            pltpu.VMEM((steps, ring, shard // 4, chunk // 2), BF16),
            pltpu.VMEM((steps, ring, strip, width), BF16), pltpu.VMEM((steps, ring, strip, width // 2), BF16),
            pltpu.VMEM((steps, ring, strip // 2, width // 2), BF16),
            pltpu.VMEM((steps, ring, strip // 4, width // 2), BF16),
            dma((3, 2, ring)), dma((3, 2, ring)), dma((3, ring, 8)), dma((3, ring, 8)),
            dma((ring,)), dma((ring,)), dma((2, count // piece)), dma((2, ring)), dma((8,)), dma((steps, ring + 2)),
            dma((2, steps, 5)), dma((2, steps, 5)),
        ],
        compiler_params=pltpu.CompilerParams(
            collective_id=0, has_side_effects=True, vmem_limit_bytes=56 * MIB
        ),
        cost_estimate=pl.CostEstimate(
            flops=12 * count * width * ff, bytes_accessed=60 * MIB, transcendentals=count * ff
        ),
        name="gather_feed",
    )(up, down, att, small, tokens, cotangents)


def fold(into, rows, term):
    owners, height, _ = term.shape
    tile = 48

    def body(n, _):
        o, t = n // (height // tile), n % (height // tile)
        at = pl.ds(pl.multiple_of(rows + t * tile, 16), tile)
        into[o, at, :] = (
            into[o, at, :].astype(F32) + term[o, pl.ds(pl.multiple_of(t * tile, 16), tile), :].astype(F32)
        ).astype(BF16)
        return 0

    lax.fori_loop(0, owners * (height // tile), body, 0)


def remote(src, dst, send_sem, recv_sem, dp, ctx):
    return pltpu.make_async_remote_copy(
        src_ref=src, dst_ref=dst, send_sem=send_sem, recv_sem=recv_sem, device_id=(dp, ctx), device_id_type=MESH
    )


def team_id(d, t):
    return d + (8 << t) * (1 - 2 * (d // (8 << t) % 2))


def greet(teams):
    ring = lax.axis_size("ctx")
    d, z = lax.axis_index("dp"), lax.axis_index("ctx")
    core, x, y, core_id, x_id, y_id = plane(d)
    barrier = pltpu.get_barrier_semaphore()
    partners = [core_id, x_id, y_id, x_id + y_id - d] + [team_id(d, t) for t in range(teams)]
    for k in range(1, ring):
        pl.semaphore_signal(barrier, inc=1, device_id=(d, (z + k) % ring), device_id_type=MESH)
    for other in partners:
        pl.semaphore_signal(barrier, inc=1, device_id=(other, z), device_id_type=MESH)
    pl.semaphore_wait(barrier, ring - 1 + len(partners))


def reducer(teams, grads, sums, bufs, send, recv, load):
    count = len(grads)
    ring = lax.axis_size("ctx")
    d, z = lax.axis_index("dp"), lax.axis_index("ctx")
    core, x, y, core_id, x_id, y_id = plane(d)
    far_id = x_id + y_id - d
    half = ring // 2

    def sizes(a):
        rows, columns = sums[a].shape
        return rows, columns // 2

    def slice_of(order, xx, yy):
        return (1 - order) * (2 * xx + yy) + order * (2 * yy + xx)

    bits = ((x, y), (y, x))
    ids = ((x_id, y_id), (y_id, x_id))

    def core_copy(a):
        rows, span = sizes(a)
        away = pl.ds(pl.multiple_of((1 - core) * span, 128), span)
        return remote(grads[a].at[:, :, away], bufs[a][1], send.at[a, 0], recv.at[a, 0], core_id, z)

    def core_load(a):
        rows, span = sizes(a)
        keep = pl.ds(pl.multiple_of(core * span, 128), span)
        return pltpu.make_async_copy(grads[a].at[:, :, keep], bufs[a][0], load.at[a])

    def first_copy(a, order):
        rows, span = sizes(a)
        own = pl.ds(order * half, half)
        away = pl.ds(pl.multiple_of((1 - bits[order][0]) * (rows // 2), 16), rows // 2)
        return remote(
            bufs[a][0].at[own, away, :], bufs[a][2].at[own], send.at[a, 1 + order], recv.at[a, 1 + order],
            ids[order][0], z,
        )

    def second_copy(a, order):
        rows, span = sizes(a)
        own = pl.ds(order * half, half)
        away = bits[order][0] * (rows // 2) + (1 - bits[order][1]) * (rows // 4)
        return remote(
            bufs[a][0].at[own, pl.ds(pl.multiple_of(away, 16), rows // 4), :], bufs[a][3].at[own],
            send.at[a, 3 + order], recv.at[a, 3 + order], ids[order][1], z,
        )

    def quarter(a, owner):
        rows, span = sizes(a)
        at = slice_of(owner // half, x, y) * (rows // 4)
        return bufs[a][0].at[owner, pl.ds(pl.multiple_of(at, 16), rows // 4), :]

    def owner_copy(a, k):
        to = (z + k) % ring
        return remote(quarter(a, to), bufs[a][4].at[k - 1], send.at[a, 4 + k], recv.at[a, 4 + k], d, to)

    def team_copy(a, t):
        j = 4 + ring + 7 + t
        return remote(bufs[a][5].at[0], bufs[a][5].at[1 + t], send.at[a, j], recv.at[a, j], team_id(d, t), z)

    spots = ((x, y), (1 - x, y), (x, 1 - y), (1 - x, 1 - y))

    def final(a, spot, side):
        rows, span = sizes(a)
        at = slice_of(z // half, *spots[spot]) * (rows // 4)
        return sums[a].at[
            pl.ds(pl.multiple_of(at, 16), rows // 4), pl.ds(pl.multiple_of(side * span, 128), span)
        ]

    def spread(a, j):
        s, r = send.at[a, 4 + ring + j - 1], recv.at[a, 4 + ring + j - 1]
        if j < 4:
            return remote(bufs[a][5].at[0], final(a, 0, core), s, r, (x_id, y_id, far_id)[j - 1], z)
        src = bufs[a][5].at[0] if j == 4 else final(a, j - 4, core)
        return remote(src, final(a, j - 4, core), s, r, core_id, z)

    def spread_here(a, j):
        s, r = send.at[a, 4 + ring + j - 1], recv.at[a, 4 + ring + j - 1]
        ref = final(a, j, core) if j < 4 else final(a, j - 4, 1 - core)
        remote(ref, ref, s, r, core_id, z).wait_recv()

    def keep(a):
        return pltpu.make_async_copy(bufs[a][5].at[0], final(a, 0, core), load.at[count + a])

    def add_slices(target, terms):
        rows = target.shape[0]
        for t in range(rows // 48):
            at = pl.ds(t * 48, 48)
            total = terms[0][at, :].astype(F32)
            for term in terms[1:]:
                total += term[at, :].astype(F32)
            target[at, :] = total.astype(BF16)

    def stage_0(a):
        core_copy(a).start()
        core_load(a).start()

    def stage_1(a):
        core_load(a).wait()
        core_copy(a).wait_recv()
        fold(bufs[a][0], 0, bufs[a][1])
        for order in range(2):
            first_copy(a, order).start()

    def stage_2(a):
        rows, span = sizes(a)
        for order in range(2):
            own = pl.ds(order * half, half)
            first_copy(a, order).wait_recv()
            fold(bufs[a][0].at[own], bits[order][0] * (rows // 2), bufs[a][2].at[own])
            second_copy(a, order).start()

    def stage_3(a):
        rows, span = sizes(a)
        for order in range(2):
            own = pl.ds(order * half, half)
            second_copy(a, order).wait_recv()
            at = slice_of(order, x, y) * (rows // 4)
            fold(bufs[a][0].at[own], at, bufs[a][3].at[own])
        for k in range(1, ring):
            owner_copy(a, k).start()

    def stage_4(a):
        for k in range(1, ring):
            owner_copy(a, k).wait_recv()
        result = bufs[a][5].at[0]
        add_slices(result, [quarter(a, z)] + [bufs[a][4].at[k] for k in range(ring - 1)])
        for t in range(teams):
            team_copy(a, t).start()
            team_copy(a, t).wait()
            add_slices(result, [result, bufs[a][5].at[1 + t]])
        keep(a).start()
        for j in range(1, 5):
            spread(a, j).start()

    def stage_5(a):
        for j in range(1, 4):
            spread_here(a, j)
            spread(a, 4 + j).start()

    def stage_6(a):
        for j in range(4, 8):
            spread_here(a, j)
        core_copy(a).wait_send()
        for order in range(2):
            first_copy(a, order).wait_send()
            second_copy(a, order).wait_send()
        for k in range(1, ring):
            owner_copy(a, k).wait_send()
        for j in range(1, 8):
            spread(a, j).wait_send()
        keep(a).wait()

    return stage_0, stage_1, stage_2, stage_3, stage_4, stage_5, stage_6


def finisher(teams, parts, sums, bufs, send, recv, load):
    count = len(parts)
    ring = lax.axis_size("ctx")
    d, z = lax.axis_index("dp"), lax.axis_index("ctx")
    core, x, y, core_id, x_id, y_id = plane(d)
    ids = (x_id, y_id, x_id + y_id - d)
    order = z // (ring // 2)
    spots = ((x, y), (1 - x, y), (x, 1 - y), (1 - x, 1 - y))

    def owner_copy(a, k):
        to = (z + k) % ring
        return remote(parts[a].at[to], bufs[a][0].at[k - 1], send.at[a, k], recv.at[a, k], d, to)

    def own_load(a):
        return pltpu.make_async_copy(parts[a].at[z], bufs[a][1].at[0], load.at[a])

    def team_copy(a, t):
        j = ring + 7 + t
        return remote(bufs[a][1].at[0], bufs[a][1].at[1 + t], send.at[a, j], recv.at[a, j], team_id(d, t), z)

    def final(a, spot, side):
        xx, yy = spots[spot]
        quarter = (1 - order) * (2 * xx + yy) + order * (2 * yy + xx)
        height, span = bufs[a][1].shape[-2:]
        rows = pl.ds(pl.multiple_of(quarter * height, 16), height)
        columns = pl.ds(pl.multiple_of(side * span, 128), span)
        return sums[a].at[rows, columns] if len(sums[a].shape) == 2 else sums[a].at[:, rows, columns]

    def spread(a, j):
        s, r = send.at[a, ring + j - 1], recv.at[a, ring + j - 1]
        if j < 4:
            return remote(bufs[a][1].at[0], final(a, 0, core), s, r, ids[j - 1], z)
        src = bufs[a][1].at[0] if j == 4 else final(a, j - 4, core)
        return remote(src, final(a, j - 4, core), s, r, core_id, z)

    def spread_here(a, j):
        ref = final(a, j, core) if j < 4 else final(a, j - 4, 1 - core)
        remote(ref, ref, send.at[a, ring + j - 1], recv.at[a, ring + j - 1], core_id, z).wait_recv()

    def keep(a):
        return pltpu.make_async_copy(bufs[a][1].at[0], final(a, 0, core), load.at[count + a])

    def stage_0(a):
        own_load(a).start()
        for k in range(1, ring):
            owner_copy(a, k).start()

    def stage_1(a):
        own_load(a).wait()
        for k in range(1, ring):
            owner_copy(a, k).wait_recv()
        result = bufs[a][1].at[0]
        result[...] = sum((bufs[a][0][k].astype(F32) for k in range(ring - 1)), result[...].astype(F32)).astype(BF16)
        for t in range(teams):
            team_copy(a, t).start()
            team_copy(a, t).wait()
            result[...] = (result[...].astype(F32) + bufs[a][1][1 + t].astype(F32)).astype(BF16)
        keep(a).start()
        for j in range(1, 5):
            spread(a, j).start()

    def stage_2(a):
        for j in range(1, 4):
            spread_here(a, j)
            spread(a, 4 + j).start()

    def stage_3(a):
        for j in range(4, 8):
            spread_here(a, j)
        for k in range(1, ring):
            owner_copy(a, k).wait_send()
        for j in range(1, 8):
            spread(a, j).wait_send()
        keep(a).wait()

    return stage_0, stage_1, stage_2, stage_3


def finisher_scratch(parts, teams, ring):
    scratch = []
    for p in parts:
        scratch += [pltpu.VMEM((ring - 1, *p[1:]), BF16), pltpu.VMEM((1 + teams, *p[1:]), BF16)]
    copies = ring + 7 + teams
    dma = pltpu.SemaphoreType.DMA
    return scratch + [dma((len(parts), copies)), dma((len(parts), copies)), dma((2 * len(parts),))]


def reducer_scratch(grads, teams, ring):
    scratch = []
    for g in grads:
        rows, span = g[1], g[2] // 2
        scratch += [
            pltpu.VMEM((ring, rows, span), BF16),
            pltpu.VMEM((ring, rows, span), BF16),
            pltpu.VMEM((ring, rows // 2, span), BF16),
            pltpu.VMEM((ring, rows // 4, span), BF16),
            pltpu.VMEM((ring - 1, rows // 4, span), BF16),
            pltpu.VMEM((1 + teams, rows // 4, span), BF16),
        ]
    copies = 4 + ring + 7 + teams
    dma = pltpu.SemaphoreType.DMA
    return scratch + [dma((len(grads), copies)), dma((len(grads), copies)), dma((2 * len(grads),))]


def reduce_kernel(count, teams, *refs):
    ring = lax.axis_size("ctx")
    d, z = lax.axis_index("dp"), lax.axis_index("ctx")
    core, x, y, core_id, x_id, y_id = plane(d)
    grads, (small, mixed, back) = refs[:count], refs[count : count + 3]
    refs = refs[count + 3 :]
    sums, (small_out, ret_mixed, ret_back) = refs[:count], refs[count : count + 3]
    refs = refs[count + 3 :]
    bufs = [refs[6 * a : 6 * a + 6] for a in range(count)]
    send, recv, load, small_acc, small_in, s_send, s_recv, r_send, r_recv, r_local = refs[6 * count :]
    batch, piece = ret_mixed.shape[:2]
    greet(teams)
    stages = reducer(teams, grads, sums, bufs, send, recv, load)

    def returned(which, i, to):
        source, target = ((mixed, ret_mixed), (back, ret_back))[which]
        return source.at[pl.ds(pl.multiple_of(to * piece, 16), piece), :], target.at[i]

    mine = z - core
    is_home = (mine >= 0) & (mine < batch)

    def start_returns():
        for which in range(2):
            for i in range(batch):
                @pl.when(mine == i)
                def _(which=which, i=i):
                    for k in range(1, ring):
                        to = (z + k) % ring
                        src, dst = returned(which, i, to)
                        remote(src, dst, r_send.at[which, k], r_recv.at[which, i], d, to).start()
                    src, dst = returned(which, i, z)
                    pltpu.make_async_copy(src, dst, r_local.at[which]).start()

    def wait_returns():
        for which in range(2):
            for i in range(batch):
                src, dst = returned(which, i, z)

                @pl.when(mine == i)
                def _(which=which, i=i, src=src, dst=dst):
                    for k in range(1, ring):
                        to = (z + k) % ring
                        remote(*returned(which, i, to), r_send.at[which, k], r_recv.at[which, i], d, to).wait_send()
                    pltpu.make_async_copy(src, dst, r_local.at[which]).wait()

                @pl.when(mine != i)
                def _(which=which, i=i, src=src, dst=dst):
                    remote(src, dst, r_send.at[which, 0], r_recv.at[which, i], core_id, z).wait_recv()

    steps = [core_id, x_id, y_id] + [team_id(d, t) for t in range(teams)]

    def small_copy(n):
        return remote(small_acc, small_in.at[n], s_send.at[n], s_recv.at[n], steps[n], z)

    def small_owner(k):
        n = len(steps) + k - 1
        return remote(small_acc, small_in.at[n], s_send.at[n], s_recv.at[n], d, (z + k) % ring)

    def small_step(n):
        if n < len(steps):
            if n == 0:
                small_acc[...] = small[...]
            small_copy(n).start()
        elif n == len(steps):
            for k in range(1, ring):
                small_owner(k).start()

    def small_close(n):
        if n < len(steps):
            small_copy(n).wait()
            small_acc[...] += small_in[n]
        elif n == len(steps):
            for k in range(1, ring):
                small_owner(k).wait()
            total = small_acc[...]
            for k in range(ring - 1):
                total += small_in[len(steps) + k]
            small_out[...] = total

    for a in range(count):
        stages[0](a)
    start_returns()
    for n in range(1, max(len(stages), len(steps) + 2)):
        small_step(n - 1)
        if n < len(stages):
            for a in range(count):
                stages[n](a)
        small_close(n - 1)
    wait_returns()


def reduce_all(grads, small, mixed, back, batch):
    ring, groups = lax.axis_size("ctx"), lax.axis_size("dp")
    teams = (groups // 8).bit_length() - 1
    count = len(grads)
    grads = [g.reshape(ring, -1, g.shape[1]) for g in grads]
    length, width = mixed.shape
    dma = pltpu.SemaphoreType.DMA
    anywhere = pl.BlockSpec(memory_space=pl.ANY)
    vmem = pl.BlockSpec(memory_space=pltpu.VMEM)
    rounds = 3 + teams + ring - 1
    scratch = reducer_scratch([g.shape for g in grads], teams, ring)
    scratch += [
        pltpu.VMEM(small.shape, F32), pltpu.VMEM((rounds, *small.shape), F32), dma((rounds,)), dma((rounds,)),
        dma((2, ring)), dma((2, batch)), dma((2,)),
    ]
    token = jax.ShapeDtypeStruct((batch, length // ring, width), BF16)
    return pl.pallas_call(
        functools.partial(reduce_kernel, count, teams),
        in_specs=[anywhere] * count + [vmem, anywhere, anywhere],
        out_specs=[anywhere] * count + [vmem, anywhere, anywhere],
        out_shape=[jax.ShapeDtypeStruct(g.shape[1:], BF16) for g in grads]
        + [jax.ShapeDtypeStruct(small.shape, F32), token, token],
        scratch_shapes=scratch,
        compiler_params=pltpu.CompilerParams(collective_id=1, has_side_effects=True, vmem_limit_bytes=56 * MIB),
        cost_estimate=pl.CostEstimate(flops=0, bytes_accessed=60 * MIB, transcendentals=0),
        name="reduce",
    )(*grads, small, mixed, back)


def attend_kernel(
    teams, order_ref, x_ref, stored_g_ref, norm_ref, bias_ref, cos_ref, low_ref, high_ref, wq_ref, wk_ref, wv_ref,
    wo_ref, up_ref, down_ref, out_ref, h_ref, dq_ref, dk_ref, dv_ref, dwo_ref, dbias_ref, small_ref, up_sum, down_sum,
    g_ref, a_ref, acc_ref, da_ref, q_ref, k_ref, v_ref, do_ref, o_ref, dqs_ref, dks_ref, dvs_ref, *reduce_refs,
):
    step = pl.program_id(0)
    bufs = (reduce_refs[:2], reduce_refs[2:4])
    stages = finisher(teams, (up_ref, down_ref), (up_sum, down_sum), bufs, *reduce_refs[4:])

    plan = {(0, 6): ((1, 0),), (1, 1): ((1, 1),), (1, 5): ((2, 0),), (2, 1): ((2, 1),)}

    @pl.when(step == 0)
    def _():
        greet(teams)
        stages[0](0)
        stages[0](1)

    last = pl.num_programs(0) - 1
    rows, width = x_ref.shape
    lanes = QUAD * HD
    tile = 256
    half = ROT // 2
    scale = 1.0 / math.sqrt(HD)
    blocks = rows // BLOCK
    mine = lax.axis_index("ctx") - lax.axis_index("dp") % 2
    is_home = (mine >= 0) & (mine < SEQS)

    def stored(ref, at):
        values = ref[pl.ds(at * BLOCK, BLOCK), :]
        return jnp.where(is_home, values, jnp.zeros_like(values))

    @pl.when(step == 0)
    def _():
        for j in range(blocks):
            place = order_ref[1, j]
            at = pl.ds(j * BLOCK, BLOCK)
            xh, _ = normalized(stored(x_ref, place).astype(F32))
            a_ref[at, :] = (xh * norm_ref[0:1, :] + norm_ref[1:2, :]).astype(BF16)
            g_ref[at, :] = stored(stored_g_ref, place)
        acc_ref[...] = jnp.zeros_like(acc_ref)
        da_ref[...] = jnp.zeros_like(da_ref)

    def table(ref, at):
        values = ref[at, :]
        return jnp.concatenate([values] * (lanes // values.shape[1]), axis=1)

    def turn(values, at):
        low = pltpu.roll(values, lanes - half, 1) * table(low_ref, at)
        high = pltpu.roll(values, half, 1) * table(high_ref, at)
        return values * table(cos_ref, at), low + high

    for t in range(rows // tile):
        at = pl.ds(t * tile, tile)
        a = a_ref[at, :]
        same, cross = turn(dot(a, wq_ref[...]) + bias_ref[...], at)
        q_ref[at, :] = ((same + cross).astype(BF16) * scale).astype(BF16)
        same, cross = turn(dot(a, wk_ref[...]), at)
        k_ref[at, :] = (same + cross).astype(BF16)
        v_ref[at, :] = dot(a, wv_ref[...]).astype(BF16)
        do_ref[at, :] = dot(g_ref[at, :], wo_ref[...], NT).astype(BF16)

    dks_ref[...] = jnp.zeros_like(dks_ref)
    dvs_ref[...] = jnp.zeros_like(dvs_ref)
    head_of = lax.broadcasted_iota(jnp.int32, (BLOCK, lanes), 1) // HD

    def stack(values):
        zero = jnp.zeros_like(values)
        return jnp.concatenate([jnp.where(head_of == e, values, zero) for e in range(QUAD)], axis=0)

    def merge(values):
        out = values[:BLOCK]
        for e in range(1, QUAD):
            out = jnp.where(head_of == e, values[e * BLOCK : (e + 1) * BLOCK], out)
        return out

    spot = lax.broadcasted_iota(jnp.int32, (QUAD * BLOCK, BLOCK), 0) % BLOCK
    admitted = lax.broadcasted_iota(jnp.int32, (QUAD * BLOCK, BLOCK), 1) <= spot
    for b in range(rows // BLOCK):
        for (when, block), work in plan.items():
            if block == b:
                @pl.when(step == when)
                def _(work=work):
                    for n, a in work:
                        stages[n](a)
        at = pl.ds(b * BLOCK, BLOCK)
        seen = pl.ds(0, (b + 1) * BLOCK)
        q = stack(q_ref[at, :])
        do_block = do_ref[at, :]
        do = stack(do_block)
        keys = k_ref[seen, :]
        values = v_ref[seen, :]
        scores = dot(q, keys, NT)
        edge = jnp.where(admitted, scores[:, b * BLOCK :], -1e30)
        scores = edge if b == 0 else jnp.concatenate([scores[:, : b * BLOCK], edge], axis=1)
        top = jnp.max(scores, axis=-1, keepdims=True)
        expo = jnp.exp(scores - top)
        probs = expo * (1.0 / jnp.sum(expo, axis=-1, keepdims=True))
        low = probs.astype(BF16)
        mixed = dot(low, values)
        o_ref[at, :] = merge(mixed).astype(BF16)
        share = jnp.sum(mixed * do.astype(F32), axis=-1, keepdims=True)
        back = (probs * (dot(do, values, NT) - share)).astype(BF16)
        dqs_ref[at, :] = merge(dot(back, keys)) * scale
        dks_ref[seen, :] += dot(back, q, TN)
        dvs_ref[seen, :] += dot(low, do, TN)

    total = jnp.zeros((1, lanes), F32)
    for t in range(rows // tile):
        at = pl.ds(t * tile, tile)
        same, cross = turn(dqs_ref[at, :], at)
        dq = (same - cross).astype(BF16)
        same, cross = turn(dks_ref[at, :], at)
        dk = (same - cross).astype(BF16)
        dv = dvs_ref[at, :].astype(BF16)
        total += jnp.sum(dq.astype(F32), axis=0, keepdims=True)
        q_ref[at, :] = dq
        k_ref[at, :] = dk
        v_ref[at, :] = dv
        acc_ref[at, :] += dot(o_ref[at, :], wo_ref[...])
        da_ref[at, :] += dot(dq, wq_ref[...], NT) + dot(dk, wk_ref[...], NT) + dot(dv, wv_ref[...], NT)
    dbias_ref[...] = total
    dwo_ref[...] = dot(o_ref[...], g_ref[...], TN).astype(BF16)
    dq_ref[...] = dot(a_ref[...], q_ref[...], TN).astype(BF16)
    dk_ref[...] = dot(a_ref[...], k_ref[...], TN).astype(BF16)
    dv_ref[...] = dot(a_ref[...], v_ref[...], TN).astype(BF16)

    @pl.when(step == last)
    def _():
        gain = jnp.zeros((1, width), F32)
        shift = jnp.zeros((1, width), F32)
        for s in range(blocks):
            at = pl.ds(s * BLOCK, BLOCK)
            sorted_at = pl.ds(order_ref[0, s] * BLOCK, BLOCK)
            xh, _ = normalized(stored(x_ref, s).astype(F32))
            da = da_ref[sorted_at, :]
            gain += jnp.sum(da * xh, axis=0, keepdims=True)
            shift += jnp.sum(da, axis=0, keepdims=True)
            h_ref[at, :] = (da * norm_ref[0:1, :]).astype(BF16)
            out_ref[at, :] = acc_ref[sorted_at, :].astype(BF16)
        small_ref[0:1, :] = gain
        small_ref[1:2, :] = shift
        stages[3](0)
        stages[3](1)


def attend(order, x, g, norms, bias_q, tables, weights, up, down):
    ring, groups_dp = lax.axis_size("ctx"), lax.axis_size("dp")
    teams = (groups_dp // 8).bit_length() - 1
    anywhere = pl.BlockSpec(memory_space=pl.ANY)
    rows, width = x.shape
    lanes = QUAD * HD
    groups = width // lanes
    whole = lambda shape: pl.BlockSpec(shape, lambda i: (0,) * len(shape))
    column = pl.BlockSpec((width, lanes), lambda i: (0, i))
    once = lambda shape: pl.BlockSpec(shape, lambda i: (0,) * len(shape), pipeline_mode=pl.Buffered(1))
    small = jax.ShapeDtypeStruct((rows, width), BF16)
    return pl.pallas_call(
        functools.partial(attend_kernel, teams),
        grid=(groups,),
        in_specs=[
            pl.BlockSpec(memory_space=pltpu.SMEM),
            once((rows, width)),
            once((rows, width)),
            once(norms.shape),
            pl.BlockSpec((1, lanes), lambda i: (0, i)),
            once(tables[0].shape),
            once(tables[0].shape),
            once(tables[0].shape),
            pl.BlockSpec((width, lanes), lambda i: (0, i)),
            pl.BlockSpec((width, lanes), lambda i: (0, groups + i)),
            pl.BlockSpec((width, lanes), lambda i: (0, 2 * groups + i)),
            pl.BlockSpec((lanes, width), lambda i: (i, 3)),
            anywhere,
            anywhere,
        ],
        out_specs=[
            whole((rows, width)),
            whole((rows, width)),
            column,
            column,
            column,
            pl.BlockSpec((lanes, width), lambda i: (i, 0)),
            pl.BlockSpec((1, lanes), lambda i: (0, i)),
            whole((8, width)),
            anywhere,
            anywhere,
        ],
        out_shape=[
            small,
            small,
            jax.ShapeDtypeStruct((width, width), BF16),
            jax.ShapeDtypeStruct((width, width), BF16),
            jax.ShapeDtypeStruct((width, width), BF16),
            jax.ShapeDtypeStruct((width, width), BF16),
            jax.ShapeDtypeStruct((1, width), F32),
            jax.ShapeDtypeStruct((8, width), F32),
            jax.ShapeDtypeStruct((4 * up.shape[1], 2 * up.shape[2]), BF16),
            jax.ShapeDtypeStruct((down.shape[1], 4 * down.shape[2], 2 * down.shape[3]), BF16),
        ],
        scratch_shapes=[
            pltpu.VMEM((rows, width), BF16),
            pltpu.VMEM((rows, width), BF16),
            pltpu.VMEM((rows, width), F32),
            pltpu.VMEM((rows, width), F32),
        ]
        + [pltpu.VMEM((rows, lanes), BF16)] * 5
        + [pltpu.VMEM((rows, lanes), F32)] * 3
        + finisher_scratch((up.shape, down.shape), teams, ring),
        compiler_params=pltpu.CompilerParams(
            collective_id=2, has_side_effects=True, vmem_limit_bytes=60 * MIB
        ),
        cost_estimate=pl.CostEstimate(
            flops=24 * rows * width * width + 8 * rows * rows * width,
            bytes_accessed=16 * width * width + 8 * rows * width,
            transcendentals=HEADS * rows * rows // 2,
        ),
        name="attend",
    )(order, x, g, norms, bias_q, *tables, weights, weights, weights, weights, up, down)


def rotary_tables(length):
    half = ROT // 2
    frequency = ROPE_BASE ** (-(np.arange(half) * 2.0 / ROT))
    angle = np.arange(length)[:, None] * frequency[None, :]
    cosine, sine = np.cos(angle), np.sin(angle)
    rest = np.zeros((length, HD - ROT))
    none = np.zeros_like(sine)
    cos_full = np.concatenate([cosine, cosine, rest + 1.0], axis=1)
    low = np.concatenate([-sine, none, rest], axis=1)
    high = np.concatenate([none, sine, rest], axis=1)
    return tuple(jnp.asarray(np.tile(t, (1, 2)).astype(np.float32)) for t in (cos_full, low, high))


def adamw(weight, grad, first, second, rate, decay):
    first_new = BETA_ONE * first + (1.0 - BETA_ONE) * grad
    second_new = BETA_TWO * second + (1.0 - BETA_TWO) * grad * grad
    first_hat = first_new / (1.0 - BETA_ONE**STEP)
    second_hat = second_new / (1.0 - BETA_TWO**STEP)
    weight_new = weight - rate * (first_hat / (jnp.sqrt(second_hat) + EPS_ADAM) + decay * weight)
    return (first_new, second_new, weight_new)


def shards(
    tokens, out_grad, block_order, qkv_weight, out_weight, up_weight, down_weight, norm_params, bias_params,
    qkv_first, qkv_second, out_first, out_second, up_first, up_second, down_first, down_second,
    norm_first, norm_second, bias_first, bias_second,
):
    groups, ring = lax.axis_size("dp"), lax.axis_size("ctx")
    group, rank = lax.axis_index("dp"), lax.axis_index("ctx")
    batch, piece, width = tokens.shape
    length = piece * ring
    count = batch * piece
    ff = up_weight.shape[1]

    att_weight = jnp.concatenate([qkv_weight, out_weight], axis=1).astype(BF16)
    share = bias_params.shape[0]
    wide = jnp.zeros((4, width), F32)
    own_norms = lax.dynamic_update_slice(wide, norm_params.astype(BF16).astype(F32), (0, rank * (width // ring)))
    own_biases = jnp.zeros((ring * share,), F32)
    own_biases = lax.dynamic_update_slice(own_biases, bias_params.astype(BF16).astype(F32), (rank * share,))
    others = jnp.concatenate([own_biases[: 2 * width], own_biases[2 * width + ff :], jnp.zeros((ff - 3 * width,), F32)])
    small = jnp.stack([own_biases[2 * width : 2 * width + ff], others, own_norms.reshape(-1)])
    small = jnp.pad(small, ((0, 5), (0, 0)))
    x_rows, g_rows = tokens.reshape(count, width), out_grad.reshape(count, width)
    att_copy, small, home_x, home_g, feed_out, h_feed, dup, ddown, dbias_up, small_feed = gather_feed(
        up_weight.astype(BF16), down_weight.astype(BF16), att_weight, small, x_rows, g_rows, piece
    )
    norms = small[2].reshape(4, width)
    bias_q = small[1:2, :width]

    odd = group % 2

    order = block_order[jnp.clip(rank - odd, 0, batch - 1)]
    spots = jnp.arange(order.shape[0])
    order = jnp.stack([order, jnp.sum(jnp.where(order[None, :] == spots[:, None], spots[None, :], 0), axis=1)])

    attend_out, h_attend, dq, dk, dv, dout, dbias_q, small_attend, up_grad, down_grad = attend(
        order, home_x, home_g, norms, bias_q, rotary_tables(length), att_copy, dup, ddown
    )

    dqkv = jnp.concatenate([dq, dk, dv], axis=1)
    tail = jnp.concatenate(
        [small_attend[:2].reshape(-1), small_feed[:2].reshape(-1), dbias_q[0], small_feed[2], dbias_up[0], small_feed[2]]
    )
    entries = tail.shape[0]
    tail = jnp.pad(tail, (0, -entries % 1024)).reshape(-1, 128)
    *owned, tail, ret_mixed, ret_back = reduce_all((dqkv, dout), tail, attend_out, h_attend, batch)
    up_grad, down_grad, qkv_grad, out_grads = (g.astype(F32) for g in (up_grad, down_grad.reshape(down_weight.shape), *owned))
    tail = tail.reshape(-1)[:entries]
    returned = [v.reshape(count, width).astype(F32) for v in (ret_mixed, ret_back)]

    rows = x_rows.astype(F32)
    bias_rows = small[1:2, width : 2 * width] + small[1:2, 2 * width : 3 * width]
    layer_out = (rows + returned[0] + feed_out + bias_rows).astype(BF16).reshape(batch, piece, width)
    xh, scale = normalized(rows)
    h = returned[1] + h_feed
    inner = jnp.mean(h * xh, axis=-1, keepdims=True)
    input_grad = g_rows.astype(F32) + scale * (h - jnp.mean(h, axis=-1, keepdims=True) - xh * inner)
    input_grad = input_grad.reshape(batch, piece, width)

    norm_grad = lax.dynamic_slice_in_dim(tail[: 4 * width].reshape(4, width), rank * (width // ring), width // ring, 1)
    bias_grad = lax.dynamic_slice_in_dim(tail[4 * width :], rank * share, share, 0)

    qkv_new = adamw(qkv_weight, qkv_grad, qkv_first, qkv_second, 0.1, DECAY)
    out_new = adamw(out_weight, out_grads, out_first, out_second, 0.6, DECAY)
    up_new = adamw(up_weight, up_grad, up_first, up_second, 0.1, DECAY)
    down_new = adamw(down_weight, down_grad, down_first, down_second, 0.05, DECAY)
    norm_new = adamw(norm_params, norm_grad, norm_first, norm_second, 0.6, 0.0)
    bias_new = adamw(bias_params, bias_grad, bias_first, bias_second, 0.6, 0.0)
    return (
        layer_out, input_grad, *qkv_new, *out_new, *up_new, *down_new,
        norm_new[0], norm_new[1][:2], norm_new[1][2:], norm_new[2], *bias_new,
    )


def solution(mesh):
    rows, columns, token = P("ctx", None), P(None, "ctx"), P("dp", "ctx", None)
    in_specs = (token, token, P("dp", None)) + (rows,) * 4 + (columns, P("ctx")) + (rows,) * 8
    in_specs += (columns, columns, P("ctx"), P("ctx"))
    out_specs = (token, token) + (rows,) * 12 + (columns,) * 4 + (P("ctx"),) * 3
    return jax.shard_map(shards, mesh=mesh, in_specs=in_specs, out_specs=out_specs, check_vma=False)
```

```python
import functools
import math

import jax
import jax.numpy as jnp
import numpy as np
from jax import lax
from jax.experimental import pallas as pl
from jax.experimental.pallas import tpu as pltpu
from jax.sharding import PartitionSpec as P

HEADS = 12
HD = 64
STEP = 10
ROT = 16
SEQS = 3
BLOCK = 128
QUAD = 4
MLP_LEVELS = (2, 1)

EPS_NORM = 1e-05
BETA_ONE = 0.9
BETA_TWO = 0.95
EPS_ADAM = 1e-08
DECAY = 0.01
ROPE_BASE = 10000.0
F32 = jnp.float32
BF16 = jnp.bfloat16
MIB = 1024 * 1024


def dot(left, right, dims=((1,), (0,))):
    return lax.dot_general(left, right, (dims, ((), ())), preferred_element_type=F32)


NN = ((1,), (0,))
NT = ((1,), (1,))
TN = ((0,), (0,))


def normalized(values):
    mean = jnp.mean(values, axis=-1, keepdims=True)
    centred = values - mean
    variance = jnp.mean(centred * centred, axis=-1, keepdims=True)
    scale = lax.rsqrt(variance + EPS_NORM)
    return centred * scale, scale


MESH = pl.DeviceIdType.MESH


def plane(d):
    core, x, y = d % 2, d // 2 % 2, d // 4 % 2
    return core, x, y, d + 1 - 2 * core, d + 2 - 4 * x, d + 4 - 8 * y


def gather_kernel(
    up, down, qkv, out, small, tokens, cotangents,
    att_all, small_all, norm_all, home_x, home_g, out_ref, h_ref, up_part, down_part, dbias_ref, sums_ref,
    up_all, down_all, att_own, up_wide, down_wide, att_wide, small_in, x_ref, g_ref, m_ref, hid_ref, dup_in_ref,
    dup_ref, up_core, up_first, ddown_ref, down_core,
    z_send, z_recv, p_send, p_recv, s_send, s_recv, t_send, t_recv, local, out_sem, c_send, c_recv,
):
    ring = lax.axis_size("ctx")
    d, z = lax.axis_index("dp"), lax.axis_index("ctx")
    core, x, y, core_id, x_id, y_id = plane(d)
    own = x + 2 * y
    own_x, own_y, far = own + 1 - 2 * x, own + 2 - 4 * y, 3 - own
    count, width = tokens.shape
    piece = home_x.shape[0] // ring
    batch = count // piece
    arrays = ((up_wide, up_all, False), (down_wide, down_all, True), (att_own, att_all, False))

    def slot(a, base, place, half=None):
        source, whole, tall = arrays[a]
        ref = source if base is None else whole
        rows, columns = source.shape
        at = 0 if base is None else base * rows
        height, span = rows // 4, columns // 2
        at = at + place * height
        column = core * span
        if half is not None:
            if tall:
                height = height // 2
                at = at + half * height
            else:
                span = span // 2
                column = column + half * span
        return ref.at[pl.ds(pl.multiple_of(at, 16), height), pl.ds(pl.multiple_of(column, 128), span)]

    def other_slot(a, base, place):
        source, whole, tall = arrays[a]
        rows, columns = source.shape
        at = pl.multiple_of(base * rows + place * (rows // 4), 16)
        column = pl.multiple_of((1 - core) * (columns // 2), 128)
        return whole.at[pl.ds(at, rows // 4), pl.ds(column, columns // 2)]

    def remote(src, dst, send, recv, dp, ctx):
        return pltpu.make_async_remote_copy(
            src_ref=src, dst_ref=dst, send_sem=send, recv_sem=recv, device_id=(dp, ctx), device_id_type=MESH
        )

    columns = qkv.shape[1]
    wide_loads = [
        [pltpu.make_async_copy(up, up_wide, local.at[0])],
        [pltpu.make_async_copy(down, down_wide, local.at[1])],
        [
            pltpu.make_async_copy(qkv, att_wide.at[:, pl.ds(0, columns)], local.at[2]),
            pltpu.make_async_copy(out, att_wide.at[:, pl.ds(columns, out.shape[1])], local.at[8]),
        ],
    ]
    for loads in wide_loads:
        for copy in loads:
            copy.start()

    def cast_own(a):
        for copy in wide_loads[a]:
            copy.wait()
        wide, target = ((up_wide, up_all), (down_wide, down_all), (att_wide, att_own))[a]
        rows = wide.shape[0]
        tile = 64
        base = 0 if a == 2 else z * rows

        def body(t, _):
            value = wide[pl.ds(pl.multiple_of(t * tile, 16), tile), :].astype(BF16)
            target[pl.ds(pl.multiple_of(base + t * tile, 16), tile), :] = value
            return 0

        lax.fori_loop(0, rows // tile, body, 0)

    barrier = pltpu.get_barrier_semaphore()
    for k in range(1, ring):
        pl.semaphore_signal(barrier, inc=1, device_id=(d, (z + k) % ring), device_id_type=MESH)
    for other in (core_id, x_id, y_id):
        pl.semaphore_signal(barrier, inc=1, device_id=(other, z), device_id_type=MESH)
    cast_own(0)
    pl.semaphore_wait(barrier, ring + 2)

    def hop(a, way, h):
        shard = z - h if way == 0 else z + h
        target = z + 1 if way == 0 else z - 1
        src = slot(a, None, own) if h == 0 and a == 2 else slot(a, shard, own)
        return remote(src, slot(a, shard, own), z_send.at[a, way, h], z_recv.at[a, way, h], d, target)

    def can_send(way, h):
        shard = z - h if way == 0 else z + h
        target = z + 1 if way == 0 else z - 1
        return (shard >= 0) & (shard < ring) & (target >= 0) & (target < ring)

    def in_range(way, h):
        shard = z - h if way == 0 else z + h
        return (shard >= 0) & (shard < ring)

    def cast(a, shard, j):
        send, recv = p_send.at[a, shard, j], p_recv.at[a, shard, j]
        if j == 0:
            ref = slot(a, shard, own)
            return remote(ref, ref, send, recv, x_id, z)
        if j == 1:
            ref = slot(a, shard, own)
            return remote(ref, ref, send, recv, y_id, z)
        if j == 2:
            ref = slot(a, shard, own_x, 0)
            return remote(ref, ref, send, recv, y_id, z)
        if j == 3:
            ref = slot(a, shard, own_y, 1)
            return remote(ref, ref, send, recv, x_id, z)
        ref = slot(a, shard, (own, own_x, own_y, far)[j - 4])
        return remote(ref, ref, send, recv, core_id, z)

    def arrived(a, shard, j):
        send, recv = p_send.at[a, shard, j], p_recv.at[a, shard, j]
        ref = {0: lambda: slot(a, shard, own_x), 1: lambda: slot(a, shard, own_y),
               2: lambda: slot(a, shard, far, 0), 3: lambda: slot(a, shard, far, 1)}.get(
            j, lambda: other_slot(a, shard, (own, own_x, own_y, far)[j - 4]))()
        remote(ref, ref, send, recv, core_id, z).wait_recv()

    def start_hops(a):
        for way in range(2):
            @pl.when(can_send(way, 0))
            def _(way=way):
                hop(a, way, 0).start()

    def small_copy(k):
        return remote(small, small_in.at[z], s_send.at[k], s_recv.at[k], d, (z + k) % ring)

    def stage_a(a, h):
        for way in range(2):
            @pl.when(in_range(way, h))
            def _(way=way):
                shard = z - h if way == 0 else z + h
                ref = slot(a, shard, own)
                remote(ref, ref, z_send.at[a, way, h - 1], z_recv.at[a, way, h - 1], core_id, z).wait_recv()

                @pl.when(can_send(way, h))
                def _():
                    hop(a, way, h).start()

                cast(a, shard, 0).start()
                cast(a, shard, 1).start()
                cast(a, shard, 4).start()

    def stage_b(a, h):
        for way in range(2):
            @pl.when(in_range(way, h))
            def _(way=way):
                shard = z - h if way == 0 else z + h
                arrived(a, shard, 0)
                cast(a, shard, 2).start()
                cast(a, shard, 5).start()
                arrived(a, shard, 1)
                cast(a, shard, 3).start()
                cast(a, shard, 6).start()

    def stage_c(a, h):
        for way in range(2):
            @pl.when(in_range(way, h))
            def _(way=way):
                shard = z - h if way == 0 else z + h
                arrived(a, shard, 2)
                arrived(a, shard, 3)
                cast(a, shard, 7).start()

    def stage_d(a, h):
        for way in range(2):
            @pl.when(in_range(way, h))
            def _(way=way):
                shard = z - h if way == 0 else z + h
                for j in range(4, 8):
                    arrived(a, shard, j)

    pairs = ((tokens, home_x), (cotangents, home_g))

    def move(which, i):
        source, whole = pairs[which]
        src = source.at[pl.ds(i * piece, piece), :]
        dst = whole.at[pl.ds(pl.multiple_of(z * piece, 16), piece), :]
        return src, dst, i + core

    def start_moves(which):
        for i in range(batch):
            src, dst, target = move(which, i)

            @pl.when(target != z)
            def _(src=src, dst=dst, target=target, i=i):
                remote(src, dst, t_send.at[which, i], t_recv.at[which, z], d, target).start()

            @pl.when(target == z)
            def _(src=src, dst=dst):
                pltpu.make_async_copy(src, dst, local.at[6 + which]).start()

    own_rows = pl.ds(pl.multiple_of(z * att_own.shape[0], 16), att_own.shape[0])
    own_att = pltpu.make_async_copy(att_own, att_all.at[own_rows, :], local.at[9])
    x_load = pltpu.make_async_copy(tokens, x_ref, local.at[3])
    g_load = pltpu.make_async_copy(cotangents, g_ref, local.at[4])
    own_small = pltpu.make_async_copy(small, small_in.at[z], local.at[5])

    start_hops(0)
    cast_own(1)
    start_hops(1)
    cast_own(2)
    start_hops(2)
    for k in range(1, ring):
        small_copy(k).start()
    for copy in (own_att, x_load, g_load, own_small):
        copy.start()
    hops = range(1, ring)
    work = [(a, h) for a in range(3) for h in hops]
    early = 2 * (ring - 1)
    for n in range(len(work)):
        stage_a(*work[n])
        if 1 <= n <= early:
            stage_b(*work[n - 1])
        if 2 <= n <= early + 1:
            stage_c(*work[n - 2])
    start_moves(0)
    start_moves(1)

    own_small.wait()
    for k in range(1, ring):
        ref = small_in.at[(z + ring - k) % ring]
        remote(ref, ref, s_send.at[k], s_recv.at[k], core_id, z).wait_recv()
    x_load.wait()
    g_load.wait()
    entries = small_all.shape[1]
    biases = jnp.zeros((8, entries), F32)
    norms = jnp.zeros((8, width), F32)
    for r in range(ring):
        block = small_in[r].astype(BF16).astype(F32)
        full = jnp.concatenate([block, jnp.zeros((8, entries - block.shape[1]), F32)], axis=1)
        biases += pltpu.roll(full, r * (entries // ring), 1) if r else full
        norms += pltpu.roll(block[:, :width], r * (width // ring), 1) if r else block[:, :width]
    small_all[...] = biases
    norm_all[...] = norms
    ff = up_all.shape[1]
    gain_2, shift_2 = norm_all[3:4, :], norm_all[4:5, :]
    tile = 256
    tiles = count // tile
    for t in range(tiles):
        at = pl.ds(t * tile, tile)
        xh, _ = normalized(x_ref[at, :].astype(F32))
        m_ref[at, :] = (xh * gain_2 + shift_2).astype(BF16)
        out_ref[at, :] = jnp.zeros((tile, width), F32)
        h_ref[at, :] = jnp.zeros((tile, width), F32)
    for h in hops:
        stage_d(0, h)
        stage_d(1, h)

    strip = dup_ref.shape[3] // ring
    steps = ff // (ring * strip)
    half = ring // 2
    big, by_core = (dup_ref, ddown_ref), (up_core, down_core)
    bits, ids = ((x, y), (y, x)), ((x_id, y_id), (y_id, x_id))

    def sizes(a):
        return by_core[a].shape[2], by_core[a].shape[3]

    def slice_of(order):
        return 2 * bits[order][0] + bits[order][1]

    def core_copy(a, i):
        _, span = sizes(a)
        away = pl.ds(pl.multiple_of((1 - core) * span, 128), span)
        return remote(big[a].at[i, :, :, away], by_core[a].at[i], c_send.at[a, i, 0], c_recv.at[a, i, 0], core_id, z)

    def first_copy(a, i, order):
        height, _ = sizes(a)
        own = pl.ds(order * half, half)
        away = pl.ds(pl.multiple_of((1 - bits[order][0]) * (height // 2), 16), height // 2)
        return remote(
            by_core[a].at[i, own, away, :], up_first.at[i, own], c_send.at[a, i, 1 + order],
            c_recv.at[a, i, 1 + order], ids[order][0], z,
        )

    def add(into, at, term, owners):
        height = term(0).shape[0]
        tile = 32 if height % 48 else 48

        def body(n, _):
            o, t = n // (height // tile), n % (height // tile)
            spot = pl.ds(pl.multiple_of(at + t * tile, 16), tile)
            value = term(o)[pl.ds(pl.multiple_of(t * tile, 16), tile), :]
            into[o, spot, :] = (into[o, spot, :].astype(F32) + value.astype(F32)).astype(BF16)
            return 0

        lax.fori_loop(0, owners * (height // tile), body, 0)

    def chunk_1(i):
        for a in range(2):
            _, span = sizes(a)
            core_copy(a, i).wait_recv()
            keep = pl.ds(pl.multiple_of(core * span, 128), span)
            add(by_core[a].at[i], 0, lambda o: big[a].at[i, o, :, keep], ring)
        for order in range(2):
            first_copy(0, i, order).start()
        parts_out(1, i)[0].start()

    def chunk_2(i):
        height, _ = sizes(0)
        for order in range(2):
            own = pl.ds(order * half, half)
            first_copy(0, i, order).wait_recv()
            at = bits[order][0] * (height // 2)
            add(by_core[0].at[i, own], at, lambda o: up_first.at[i, order * half + o], half)
        for copy in parts_out(0, i):
            copy.start()

    def parts_out(a, i):
        height, span = sizes(a)
        if a == 1:
            return [pltpu.make_async_copy(by_core[1].at[i], down_part.at[:, i], out_sem.at[i, 2 * half])]
        copies = []
        for order in range(2):
            own = pl.ds(order * half, half)
            rows = pl.ds(pl.multiple_of(bits[order][0] * (height // 2), 16), height // 2)
            for n in range(half):
                copies.append(pltpu.make_async_copy(
                    by_core[0].at[i, own, rows, pl.ds(n * strip, strip)],
                    up_part.at[own, :, pl.ds(pl.multiple_of(n * steps * strip + i * strip, 128), strip)],
                    out_sem.at[i, half * order + n],
                ))
        return copies

    def feed_step(step, _):
        for h in hops:
            @pl.when(step == h - 1)
            def _(h=h):
                stage_b(2, h)

            @pl.when(step == h)
            def _(h=h):
                stage_c(2, h)

        @pl.when(step < steps)
        def _():
            spots = [pl.ds(pl.multiple_of(r * (ff // ring) + step * strip, 128), strip) for r in range(ring)]
            bias_spots = [
                pl.ds(pl.multiple_of(2 * width + r * (ff // ring) + step * strip, 128), strip) for r in range(ring)
            ]
            up_part_ = jnp.concatenate([up_all[:, at] for at in spots], axis=1)
            down_part_ = jnp.concatenate([down_all[at, :] for at in spots], axis=0)
            bias = jnp.concatenate([small_all[0:1, at] for at in bias_spots], axis=1)
            total = jnp.zeros((1, ring * strip), F32)
            for t in range(tiles):
                at = pl.ds(t * tile, tile)
                u = dot(m_ref[at, :], up_part_) + bias
                cdf = 0.5 * (1.0 + lax.erf(u * (1.0 / math.sqrt(2.0))))
                hidden = (u * cdf).astype(BF16)
                slope = cdf + u * jnp.exp(-0.5 * u * u) * (1.0 / math.sqrt(2.0 * math.pi))
                back = (dot(g_ref[at, :], down_part_, NT) * slope).astype(BF16)
                hid_ref[at, :] = hidden
                dup_in_ref[at, :] = back
                total += jnp.sum(back.astype(F32), axis=0, keepdims=True)
                out_ref[at, :] += dot(hidden, down_part_)
                h_ref[at, :] += dot(back, up_part_, NT)
            for r in range(ring):
                dbias_ref[0:1, spots[r]] = total[:, r * strip : (r + 1) * strip]
            ddown = dot(hid_ref[...], g_ref[...], TN).astype(BF16)
            dup = dot(m_ref[...], dup_in_ref[...], TN).astype(BF16)
            for r in range(ring):
                ddown_ref[step, r] = ddown[r * strip : (r + 1) * strip, :]
                dup_ref[step, r] = dup[r * (width // ring) : (r + 1) * (width // ring), :]
            core_copy(0, step).start()
            core_copy(1, step).start()

        for lag, stage in ((1, chunk_1), (3, chunk_2)):
            @pl.when((step >= lag) & (step < steps + lag))
            def _(lag=lag, stage=stage):
                stage(step - lag)

        return 0

    lax.fori_loop(0, steps + 3, feed_step, 0)

    gain = jnp.zeros((1, width), F32)
    shift = jnp.zeros((1, width), F32)
    sums = jnp.zeros((1, width), F32)
    for t in range(tiles):
        at = pl.ds(t * tile, tile)
        xh, _ = normalized(x_ref[at, :].astype(F32))
        dm = h_ref[at, :]
        gain += jnp.sum(dm * xh, axis=0, keepdims=True)
        shift += jnp.sum(dm, axis=0, keepdims=True)
        sums += jnp.sum(g_ref[at, :].astype(F32), axis=0, keepdims=True)
        h_ref[at, :] = dm * gain_2
    sums_ref[...] = jnp.concatenate([gain, shift, sums, jnp.zeros((5, width), F32)], axis=0)

    mine = z - core
    for which in range(2):
        for k in range(1, ring):
            @pl.when((mine >= 0) & (mine < batch))
            def _(which=which, k=k):
                other = (z + k) % ring
                ref = pairs[which][1].at[pl.ds(pl.multiple_of(other * piece, 16), piece), :]
                remote(ref, ref, t_send.at[which, 0], t_recv.at[which, other], core_id, z).wait_recv()
    for h in hops:
        stage_d(2, h)
    for k in range(1, ring):
        small_copy(k).wait_send()
    for a in range(3):
        for way in range(2):
            for h in range(ring - 1):
                @pl.when(can_send(way, h))
                def _(a=a, way=way, h=h):
                    hop(a, way, h).wait_send()
        for h in hops:
            for way in range(2):
                @pl.when(in_range(way, h))
                def _(a=a, h=h, way=way):
                    shard = z - h if way == 0 else z + h
                    for j in range(8):
                        cast(a, shard, j).wait_send()
    for which in range(2):
        for i in range(batch):
            src, dst, target = move(which, i)

            @pl.when(target != z)
            def _(src=src, dst=dst, target=target, which=which, i=i):
                remote(src, dst, t_send.at[which, i], t_recv.at[which, z], d, target).wait_send()

            @pl.when(target == z)
            def _(src=src, dst=dst, which=which):
                pltpu.make_async_copy(src, dst, local.at[6 + which]).wait()
    own_att.wait()

    def close(i, _):
        for a in range(2):
            core_copy(a, i).wait_send()
            for copy in parts_out(a, i):
                copy.wait()
        for order in range(2):
            first_copy(0, i, order).wait_send()
        return 0

    lax.fori_loop(0, steps, close, 0)


def gather_feed(up, down, qkv, out, small, tokens, cotangents, piece, entries):
    ring = lax.axis_size("ctx")
    count, width = tokens.shape
    ff = up.shape[1]
    strip = 128
    chunk = ring * strip
    steps = ff // chunk
    shard = up.shape[0]
    columns = qkv.shape[1] + out.shape[1]
    home = jax.ShapeDtypeStruct((ring * piece, width), tokens.dtype)
    rows = jax.ShapeDtypeStruct((count, width), F32)
    dma = pltpu.SemaphoreType.DMA
    anywhere = pl.BlockSpec(memory_space=pl.ANY)
    vmem = pl.BlockSpec(memory_space=pltpu.VMEM)
    return pl.pallas_call(
        gather_kernel,
        in_specs=[anywhere] * 7,
        out_specs=[anywhere, vmem, vmem, anywhere, anywhere, vmem, vmem, anywhere, anywhere, vmem, vmem],
        out_shape=[
            jax.ShapeDtypeStruct((ring * shard, columns), BF16),
            jax.ShapeDtypeStruct((8, entries), F32), jax.ShapeDtypeStruct((8, width), F32), home, home, rows, rows,
            jax.ShapeDtypeStruct((ring, shard // 2, ff // 2), BF16),
            jax.ShapeDtypeStruct((ring, steps, strip, width // 2), BF16),
            jax.ShapeDtypeStruct((8, ff), F32), jax.ShapeDtypeStruct((8, width), F32),
        ],
        scratch_shapes=[
            pltpu.VMEM((ring * shard, ff), BF16), pltpu.VMEM((ring * down.shape[0], width), BF16),
            pltpu.VMEM((shard, columns), BF16),
            pltpu.VMEM(up.shape, F32), pltpu.VMEM(down.shape, F32), pltpu.VMEM((shard, columns), F32),
            pltpu.VMEM((ring, *small.shape), F32),
            pltpu.VMEM((count, width), BF16), pltpu.VMEM((count, width), BF16), pltpu.VMEM((count, width), BF16),
            pltpu.VMEM((count, chunk), BF16), pltpu.VMEM((count, chunk), BF16),
            pltpu.VMEM((steps, ring, shard, chunk), BF16), pltpu.VMEM((steps, ring, shard, chunk // 2), BF16),
            pltpu.VMEM((steps, ring, shard // 2, chunk // 2), BF16),
            pltpu.VMEM((steps, ring, strip, width), BF16), pltpu.VMEM((steps, ring, strip, width // 2), BF16),
            dma((3, 2, ring)), dma((3, 2, ring)), dma((3, ring, 8)), dma((3, ring, 8)),
            dma((ring,)), dma((ring,)), dma((2, count // piece)), dma((2, ring)), dma((10,)), dma((steps, ring + 1)),
            dma((2, steps, 3)), dma((2, steps, 3)),
        ],
        compiler_params=pltpu.CompilerParams(
            collective_id=0, has_side_effects=True, vmem_limit_bytes=60 * MIB
        ),
        cost_estimate=pl.CostEstimate(
            flops=12 * count * width * ff, bytes_accessed=60 * MIB, transcendentals=count * ff
        ),
        name="gather_feed",
    )(up, down, qkv, out, small, tokens, cotangents)


def remote(src, dst, send_sem, recv_sem, dp, ctx):
    return pltpu.make_async_remote_copy(
        src_ref=src, dst_ref=dst, send_sem=send_sem, recv_sem=recv_sem, device_id=(dp, ctx), device_id_type=MESH
    )


def team_id(d, t):
    return d + (8 << t) * (1 - 2 * (d // (8 << t) % 2))


def greet(teams):
    ring = lax.axis_size("ctx")
    d, z = lax.axis_index("dp"), lax.axis_index("ctx")
    core, x, y, core_id, x_id, y_id = plane(d)
    barrier = pltpu.get_barrier_semaphore()
    partners = [core_id, x_id, y_id, x_id + y_id - d] + [team_id(d, t) for t in range(teams)]
    for k in range(1, ring):
        pl.semaphore_signal(barrier, inc=1, device_id=(d, (z + k) % ring), device_id_type=MESH)
    for other in partners:
        pl.semaphore_signal(barrier, inc=1, device_id=(other, z), device_id_type=MESH)
    pl.semaphore_wait(barrier, ring - 1 + len(partners))


def reducer(teams, levels, ins, sums, bufs, send, recv, load):
    count = len(ins)
    ring = lax.axis_size("ctx")
    d, z = lax.axis_index("dp"), lax.axis_index("ctx")
    core, x, y, core_id, x_id, y_id = plane(d)
    far_id = x_id + y_id - d
    bits, ids = ((x, y), (y, x)), ((x_id, y_id), (y_id, x_id))
    spots = ((x, y), (1 - x, y), (x, 1 - y), (1 - x, 1 - y))

    def sizes(a):
        _, strips, quarter, span = bufs[a][-1].shape
        return strips, quarter, span

    def owners(a, order):
        strips = sizes(a)[0]
        return pl.ds(order * ring // 2 * strips, ring // 2 * strips)

    def rows_at(at, height):
        return pl.ds(pl.multiple_of(at, 16), height)

    def kept(a, order):
        return 0 if levels[a] == 2 else bits[order][0] * 2 * sizes(a)[1]

    def core_copy(a):
        span = sizes(a)[2]
        away = pl.ds(pl.multiple_of((1 - core) * span, 128), span)
        return remote(ins[a].at[:, :, away], bufs[a][1], send.at[a, 0], recv.at[a, 0], core_id, z)

    def own_load(a):
        span = sizes(a)[2]
        keep = pl.ds(pl.multiple_of(core * span, 128), span)
        src = ins[a].at[:, :, keep] if levels[a] == 0 else ins[a]
        return pltpu.make_async_copy(src, bufs[a][0], load.at[a])

    def first_copy(a, order):
        quarter = sizes(a)[1]
        away = rows_at((1 - bits[order][0]) * 2 * quarter, 2 * quarter)
        return remote(
            bufs[a][0].at[owners(a, order), away, :], bufs[a][2].at[owners(a, order)], send.at[a, 1 + order],
            recv.at[a, 1 + order], ids[order][0], z,
        )

    def second_copy(a, order):
        quarter = sizes(a)[1]
        away = rows_at(kept(a, order) + (1 - bits[order][1]) * quarter, quarter)
        return remote(
            bufs[a][0].at[owners(a, order), away, :], bufs[a][3].at[owners(a, order)], send.at[a, 3 + order],
            recv.at[a, 3 + order], ids[order][1], z,
        )

    def own_quarter(a, owner):
        strips, quarter, _ = sizes(a)
        order = owner // (ring // 2)
        first, second = (1 - order) * x + order * y, (1 - order) * y + order * x
        at = second * quarter if levels[a] == 2 else (2 * first + second) * quarter
        return bufs[a][0].at[pl.ds(owner * strips, strips), rows_at(at, quarter), :]

    def owner_copy(a, k):
        to = (z + k) % ring
        return remote(own_quarter(a, to), bufs[a][4].at[k - 1], send.at[a, 4 + k], recv.at[a, 4 + k], d, to)

    def team_copy(a, t):
        j = 4 + ring + 7 + t
        return remote(bufs[a][5].at[0], bufs[a][5].at[1 + t], send.at[a, j], recv.at[a, j], team_id(d, t), z)

    def final(a, spot, side):
        strips, quarter, span = sizes(a)
        order = z // (ring // 2)
        xx, yy = spots[spot]
        at = ((1 - order) * (2 * xx + yy) + order * (2 * yy + xx)) * quarter
        return sums[a].at[:, rows_at(at, quarter), pl.ds(pl.multiple_of(side * span, 128), span)]

    def spread(a, j):
        s, r = send.at[a, 4 + ring + j - 1], recv.at[a, 4 + ring + j - 1]
        if j < 4:
            return remote(bufs[a][5].at[0], final(a, 0, core), s, r, (x_id, y_id, far_id)[j - 1], z)
        src = bufs[a][5].at[0] if j == 4 else final(a, j - 4, core)
        return remote(src, final(a, j - 4, core), s, r, core_id, z)

    def spread_here(a, j):
        s, r = send.at[a, 4 + ring + j - 1], recv.at[a, 4 + ring + j - 1]
        ref = final(a, j, core) if j < 4 else final(a, j - 4, 1 - core)
        remote(ref, ref, s, r, core_id, z).wait_recv()

    def keep_own(a):
        return pltpu.make_async_copy(bufs[a][5].at[0], final(a, 0, core), load.at[count + a])

    def add(into, at, term, blocks):
        height = term.shape[1]
        tile = 32 if height % 48 else 48

        def body(n, _):
            o, t = n // (height // tile), n % (height // tile)
            spot = rows_at(at + t * tile, tile)
            value = term[o, rows_at(t * tile, tile), :]
            into[o, spot, :] = (into[o, spot, :].astype(F32) + value.astype(F32)).astype(BF16)
            return 0

        lax.fori_loop(0, blocks * (height // tile), body, 0)

    def enter(a):
        if levels[a] == 0:
            core_copy(a).start()
        own_load(a).start()

    def first(a):
        own_load(a).wait()
        if levels[a] == 0:
            core_copy(a).wait_recv()
            add(bufs[a][0], 0, bufs[a][1], bufs[a][0].shape[0])
        if levels[a] < 2:
            for order in range(2):
                first_copy(a, order).start()

    def second(a):
        for order in range(2):
            if levels[a] < 2:
                first_copy(a, order).wait_recv()
                own = owners(a, order)
                add(bufs[a][0].at[own], kept(a, order), bufs[a][2].at[own], ring // 2 * sizes(a)[0])
            second_copy(a, order).start()

    def to_owner(a):
        for order in range(2):
            second_copy(a, order).wait_recv()
            own = owners(a, order)
            at = kept(a, order) + bits[order][1] * sizes(a)[1]
            add(bufs[a][0].at[own], at, bufs[a][3].at[own], ring // 2 * sizes(a)[0])
        for k in range(1, ring):
            owner_copy(a, k).start()

    def total(a):
        for k in range(1, ring):
            owner_copy(a, k).wait_recv()
        mine = own_quarter(a, z)
        for s in range(sizes(a)[0]):
            terms = [mine[s]] + [bufs[a][4][k, s] for k in range(ring - 1)]
            bufs[a][5][0, s] = sum((t.astype(F32) for t in terms[1:]), terms[0].astype(F32)).astype(BF16)
        for t in range(teams):
            team_copy(a, t).start()
            team_copy(a, t).wait()
            bufs[a][5][0] = (bufs[a][5][0].astype(F32) + bufs[a][5][1 + t].astype(F32)).astype(BF16)
        keep_own(a).start()
        for j in range(1, 5):
            spread(a, j).start()

    def share(a):
        for j in range(1, 4):
            spread_here(a, j)
            spread(a, 4 + j).start()

    def close(a):
        for j in range(4, 8):
            spread_here(a, j)
        if levels[a] == 0:
            core_copy(a).wait_send()
        for order in range(2):
            if levels[a] < 2:
                first_copy(a, order).wait_send()
            second_copy(a, order).wait_send()
        for k in range(1, ring):
            owner_copy(a, k).wait_send()
        for j in range(1, 8):
            spread(a, j).wait_send()
        keep_own(a).wait()

    return enter, first, second, to_owner, total, share, close


def reducer_scratch(levels, shapes, teams, ring):
    scratch = []
    for level, (strips, rows, columns) in zip(levels, shapes):
        blocks, span = ring * strips, columns // 2
        none = (1, 16, 128)
        scratch += [
            pltpu.VMEM((blocks, rows // 2 if level == 2 else rows, span), BF16),
            pltpu.VMEM((blocks, rows, span) if level == 0 else none, BF16),
            pltpu.VMEM((blocks, rows // 2, span) if level < 2 else none, BF16),
            pltpu.VMEM((blocks, rows // 4, span), BF16),
            pltpu.VMEM((ring - 1, strips, rows // 4, span), BF16),
            pltpu.VMEM((1 + teams, strips, rows // 4, span), BF16),
        ]
    copies = 4 + ring + 7 + teams
    dma = pltpu.SemaphoreType.DMA
    return scratch + [dma((len(levels), copies)), dma((len(levels), copies)), dma((2 * len(levels),))]


def reduce_kernel(count, teams, *refs):
    ring = lax.axis_size("ctx")
    d, z = lax.axis_index("dp"), lax.axis_index("ctx")
    core, x, y, core_id, x_id, y_id = plane(d)
    grads, (small, mixed, back) = refs[:count], refs[count : count + 3]
    refs = refs[count + 3 :]
    sums, (small_out, ret_mixed, ret_back) = refs[:count], refs[count : count + 3]
    refs = refs[count + 3 :]
    bufs = [refs[6 * a : 6 * a + 6] for a in range(count)]
    send, recv, load, small_acc, small_in, s_send, s_recv, r_send, r_recv, r_local = refs[6 * count :]
    batch, piece = ret_mixed.shape[:2]
    greet(teams)
    stages = reducer(teams, (0,) * count, grads, sums, bufs, send, recv, load)

    def returned(which, i, to):
        source, target = ((mixed, ret_mixed), (back, ret_back))[which]
        return source.at[pl.ds(pl.multiple_of(to * piece, 16), piece), :], target.at[i]

    mine = z - core
    is_home = (mine >= 0) & (mine < batch)

    def start_returns():
        for which in range(2):
            for i in range(batch):
                @pl.when(mine == i)
                def _(which=which, i=i):
                    for k in range(1, ring):
                        to = (z + k) % ring
                        src, dst = returned(which, i, to)
                        remote(src, dst, r_send.at[which, k], r_recv.at[which, i], d, to).start()
                    src, dst = returned(which, i, z)
                    pltpu.make_async_copy(src, dst, r_local.at[which]).start()

    def wait_returns():
        for which in range(2):
            for i in range(batch):
                src, dst = returned(which, i, z)

                @pl.when(mine == i)
                def _(which=which, i=i, src=src, dst=dst):
                    for k in range(1, ring):
                        to = (z + k) % ring
                        remote(*returned(which, i, to), r_send.at[which, k], r_recv.at[which, i], d, to).wait_send()
                    pltpu.make_async_copy(src, dst, r_local.at[which]).wait()

                @pl.when(mine != i)
                def _(which=which, i=i, src=src, dst=dst):
                    remote(src, dst, r_send.at[which, 0], r_recv.at[which, i], core_id, z).wait_recv()

    steps = [core_id, x_id, y_id] + [team_id(d, t) for t in range(teams)]

    def small_copy(n):
        return remote(small_acc, small_in.at[n], s_send.at[n], s_recv.at[n], steps[n], z)

    def small_owner(k):
        n = len(steps) + k - 1
        return remote(small_acc, small_in.at[n], s_send.at[n], s_recv.at[n], d, (z + k) % ring)

    def small_step(n):
        if n < len(steps):
            if n == 0:
                small_acc[...] = small[...]
            small_copy(n).start()
        elif n == len(steps):
            for k in range(1, ring):
                small_owner(k).start()

    def small_close(n):
        if n < len(steps):
            small_copy(n).wait()
            small_acc[...] += small_in[n]
        elif n == len(steps):
            for k in range(1, ring):
                small_owner(k).wait()
            total = small_acc[...]
            for k in range(ring - 1):
                total += small_in[len(steps) + k]
            small_out[...] = total

    for a in range(count):
        stages[0](a)
    start_returns()
    for n in range(1, max(len(stages), len(steps) + 2)):
        small_step(n - 1)
        if n < len(stages):
            for a in range(count):
                stages[n](a)
        small_close(n - 1)
    wait_returns()


def reduce_all(grads, small, mixed, back, batch):
    ring, groups = lax.axis_size("ctx"), lax.axis_size("dp")
    teams = (groups // 8).bit_length() - 1
    count = len(grads)
    grads = [g.reshape(ring, -1, g.shape[1]) for g in grads]
    length, width = mixed.shape
    dma = pltpu.SemaphoreType.DMA
    anywhere = pl.BlockSpec(memory_space=pl.ANY)
    vmem = pl.BlockSpec(memory_space=pltpu.VMEM)
    rounds = 3 + teams + ring - 1
    scratch = reducer_scratch((0,) * count, [(1, *g.shape[1:]) for g in grads], teams, ring)
    scratch += [
        pltpu.VMEM(small.shape, F32), pltpu.VMEM((rounds, *small.shape), F32), dma((rounds,)), dma((rounds,)),
        dma((2, ring)), dma((2, batch)), dma((2,)),
    ]
    token = jax.ShapeDtypeStruct((batch, length // ring, width), BF16)
    return pl.pallas_call(
        functools.partial(reduce_kernel, count, teams),
        in_specs=[anywhere] * count + [vmem, anywhere, anywhere],
        out_specs=[anywhere] * count + [vmem, anywhere, anywhere],
        out_shape=[jax.ShapeDtypeStruct((1, *g.shape[1:]), BF16) for g in grads]
        + [jax.ShapeDtypeStruct(small.shape, F32), token, token],
        scratch_shapes=scratch,
        compiler_params=pltpu.CompilerParams(collective_id=1, has_side_effects=True, vmem_limit_bytes=56 * MIB),
        cost_estimate=pl.CostEstimate(flops=0, bytes_accessed=60 * MIB, transcendentals=0),
        name="reduce",
    )(*grads, small, mixed, back)


def attend_kernel(
    teams, order_ref, x_ref, stored_g_ref, norm_ref, bias_ref, cos_ref, low_ref, high_ref, wq_ref, wk_ref, wv_ref,
    wo_ref, up_ref, down_ref, out_ref, h_ref, dq_ref, dk_ref, dv_ref, dwo_ref, dbias_ref, small_ref, up_sum, down_sum,
    g_ref, a_ref, acc_ref, da_ref, q_ref, k_ref, v_ref, do_ref, o_ref, dqs_ref, dks_ref, dvs_ref, *reduce_refs,
):
    step = pl.program_id(0)
    bufs = (reduce_refs[:6], reduce_refs[6:12])
    stages = reducer(teams, MLP_LEVELS, (up_ref, down_ref), (up_sum, down_sum), bufs, *reduce_refs[12:])

    plan = {
        (0, 6): ((3, 0),), (1, 0): ((2, 1),), (1, 3): ((3, 1),), (1, 5): ((4, 0),), (2, 0): ((5, 0),),
        (2, 2): ((4, 1),), (2, 6): ((5, 1),),
    }

    @pl.when(step == 0)
    def _():
        stages[0](1)
        stages[0](0)
        greet(teams)
        stages[1](1)
        stages[1](0)
        stages[2](0)

    last = pl.num_programs(0) - 1
    rows, width = x_ref.shape
    lanes = QUAD * HD
    tile = 256
    half = ROT // 2
    scale = 1.0 / math.sqrt(HD)
    blocks = rows // BLOCK
    mine = lax.axis_index("ctx") - lax.axis_index("dp") % 2
    is_home = (mine >= 0) & (mine < SEQS)

    def stored(ref, at):
        values = ref[pl.ds(at * BLOCK, BLOCK), :]
        return jnp.where(is_home, values, jnp.zeros_like(values))

    @pl.when(step == 0)
    def _():
        for j in range(blocks):
            place = order_ref[1, j]
            at = pl.ds(j * BLOCK, BLOCK)
            xh, _ = normalized(stored(x_ref, place).astype(F32))
            a_ref[at, :] = (xh * norm_ref[1:2, :] + norm_ref[2:3, :]).astype(BF16)
            g_ref[at, :] = stored(stored_g_ref, place)
        acc_ref[...] = jnp.zeros_like(acc_ref)
        da_ref[...] = jnp.zeros_like(da_ref)

    def table(ref, at):
        values = ref[at, :]
        return jnp.concatenate([values] * (lanes // values.shape[1]), axis=1)

    def turn(values, at):
        low = pltpu.roll(values, lanes - half, 1) * table(low_ref, at)
        high = pltpu.roll(values, half, 1) * table(high_ref, at)
        return values * table(cos_ref, at), low + high

    for t in range(rows // tile):
        at = pl.ds(t * tile, tile)
        a = a_ref[at, :]
        same, cross = turn(dot(a, wq_ref[...]) + bias_ref[0:1, :], at)
        q_ref[at, :] = ((same + cross).astype(BF16) * scale).astype(BF16)
        same, cross = turn(dot(a, wk_ref[...]), at)
        k_ref[at, :] = (same + cross).astype(BF16)
        v_ref[at, :] = dot(a, wv_ref[...]).astype(BF16)
        do_ref[at, :] = dot(g_ref[at, :], wo_ref[...], NT).astype(BF16)

    dks_ref[...] = jnp.zeros_like(dks_ref)
    dvs_ref[...] = jnp.zeros_like(dvs_ref)
    head_of = lax.broadcasted_iota(jnp.int32, (BLOCK, lanes), 1) // HD

    def stack(values):
        zero = jnp.zeros_like(values)
        return jnp.concatenate([jnp.where(head_of == e, values, zero) for e in range(QUAD)], axis=0)

    def merge(values):
        out = values[:BLOCK]
        for e in range(1, QUAD):
            out = jnp.where(head_of == e, values[e * BLOCK : (e + 1) * BLOCK], out)
        return out

    spot = lax.broadcasted_iota(jnp.int32, (QUAD * BLOCK, BLOCK), 0) % BLOCK
    admitted = lax.broadcasted_iota(jnp.int32, (QUAD * BLOCK, BLOCK), 1) <= spot
    for b in range(rows // BLOCK):
        for (when, block), work in plan.items():
            if block == b:
                @pl.when(step == when)
                def _(work=work):
                    for n, a in work:
                        stages[n](a)
        at = pl.ds(b * BLOCK, BLOCK)
        seen = pl.ds(0, (b + 1) * BLOCK)
        q = stack(q_ref[at, :])
        do_block = do_ref[at, :]
        do = stack(do_block)
        keys = k_ref[seen, :]
        values = v_ref[seen, :]
        scores = dot(q, keys, NT)
        edge = jnp.where(admitted, scores[:, b * BLOCK :], -1e30)
        scores = edge if b == 0 else jnp.concatenate([scores[:, : b * BLOCK], edge], axis=1)
        top = jnp.max(scores, axis=-1, keepdims=True)
        expo = jnp.exp(scores - top)
        probs = expo * (1.0 / jnp.sum(expo, axis=-1, keepdims=True))
        low = probs.astype(BF16)
        mixed = dot(low, values)
        o_ref[at, :] = merge(mixed).astype(BF16)
        share = jnp.sum(mixed * do.astype(F32), axis=-1, keepdims=True)
        back = (probs * (dot(do, values, NT) - share)).astype(BF16)
        dqs_ref[at, :] = merge(dot(back, keys)) * scale
        dks_ref[seen, :] += dot(back, q, TN)
        dvs_ref[seen, :] += dot(low, do, TN)

    total = jnp.zeros((1, lanes), F32)
    for t in range(rows // tile):
        at = pl.ds(t * tile, tile)
        same, cross = turn(dqs_ref[at, :], at)
        dq = (same - cross).astype(BF16)
        same, cross = turn(dks_ref[at, :], at)
        dk = (same - cross).astype(BF16)
        dv = dvs_ref[at, :].astype(BF16)
        total += jnp.sum(dq.astype(F32), axis=0, keepdims=True)
        q_ref[at, :] = dq
        k_ref[at, :] = dk
        v_ref[at, :] = dv
        acc_ref[at, :] += dot(o_ref[at, :], wo_ref[...])
        da_ref[at, :] += dot(dq, wq_ref[...], NT) + dot(dk, wk_ref[...], NT) + dot(dv, wv_ref[...], NT)
    dbias_ref[...] = total
    dwo_ref[...] = dot(o_ref[...], g_ref[...], TN).astype(BF16)
    dq_ref[...] = dot(a_ref[...], q_ref[...], TN).astype(BF16)
    dk_ref[...] = dot(a_ref[...], k_ref[...], TN).astype(BF16)
    dv_ref[...] = dot(a_ref[...], v_ref[...], TN).astype(BF16)

    @pl.when(step == last)
    def _():
        gain = jnp.zeros((1, width), F32)
        shift = jnp.zeros((1, width), F32)
        for s in range(blocks):
            at = pl.ds(s * BLOCK, BLOCK)
            sorted_at = pl.ds(order_ref[0, s] * BLOCK, BLOCK)
            xh, _ = normalized(stored(x_ref, s).astype(F32))
            da = da_ref[sorted_at, :]
            gain += jnp.sum(da * xh, axis=0, keepdims=True)
            shift += jnp.sum(da, axis=0, keepdims=True)
            h_ref[at, :] = (da * norm_ref[1:2, :]).astype(BF16)
            out_ref[at, :] = acc_ref[sorted_at, :].astype(BF16)
        small_ref[0:1, :] = gain
        small_ref[1:2, :] = shift
        stages[6](0)
        stages[6](1)


def attend(order, x, g, norms, bias_q, tables, weights, up, down):
    ring, groups_dp = lax.axis_size("ctx"), lax.axis_size("dp")
    teams = (groups_dp // 8).bit_length() - 1
    anywhere = pl.BlockSpec(memory_space=pl.ANY)
    shapes = ((1, 2 * up.shape[1], 2 * up.shape[2]), (down.shape[1], down.shape[2], 2 * down.shape[3]))
    down = down.reshape(-1, *down.shape[2:])
    rows, width = x.shape
    lanes = QUAD * HD
    groups = width // lanes
    whole = lambda shape: pl.BlockSpec(shape, lambda i: (0,) * len(shape))
    column = pl.BlockSpec((width, lanes), lambda i: (0, i))
    once = lambda shape: pl.BlockSpec(shape, lambda i: (0,) * len(shape), pipeline_mode=pl.Buffered(1))
    small = jax.ShapeDtypeStruct((rows, width), BF16)
    return pl.pallas_call(
        functools.partial(attend_kernel, teams),
        grid=(groups,),
        in_specs=[
            pl.BlockSpec(memory_space=pltpu.SMEM),
            once((rows, width)),
            once((rows, width)),
            once(norms.shape),
            pl.BlockSpec((8, lanes), lambda i: (0, i)),
            once(tables[0].shape),
            once(tables[0].shape),
            once(tables[0].shape),
            pl.BlockSpec((width, lanes), lambda i: (0, i)),
            pl.BlockSpec((width, lanes), lambda i: (0, groups + i)),
            pl.BlockSpec((width, lanes), lambda i: (0, 2 * groups + i)),
            pl.BlockSpec((lanes, width), lambda i: (i, 3)),
            anywhere,
            anywhere,
        ],
        out_specs=[
            whole((rows, width)),
            whole((rows, width)),
            column,
            column,
            column,
            pl.BlockSpec((lanes, width), lambda i: (i, 0)),
            pl.BlockSpec((1, lanes), lambda i: (0, i)),
            whole((8, width)),
            anywhere,
            anywhere,
        ],
        out_shape=[
            small,
            small,
            jax.ShapeDtypeStruct((width, width), BF16),
            jax.ShapeDtypeStruct((width, width), BF16),
            jax.ShapeDtypeStruct((width, width), BF16),
            jax.ShapeDtypeStruct((width, width), BF16),
            jax.ShapeDtypeStruct((1, width), F32),
            jax.ShapeDtypeStruct((8, width), F32),
            jax.ShapeDtypeStruct(shapes[0], BF16),
            jax.ShapeDtypeStruct(shapes[1], BF16),
        ],
        scratch_shapes=[
            pltpu.VMEM((rows, width), BF16),
            pltpu.VMEM((rows, width), BF16),
            pltpu.VMEM((rows, width), F32),
            pltpu.VMEM((rows, width), F32),
        ]
        + [pltpu.VMEM((rows, lanes), BF16)] * 5
        + [pltpu.VMEM((rows, lanes), F32)] * 3
        + reducer_scratch(MLP_LEVELS, shapes, teams, ring),
        compiler_params=pltpu.CompilerParams(
            collective_id=2, has_side_effects=True, vmem_limit_bytes=60 * MIB
        ),
        cost_estimate=pl.CostEstimate(
            flops=24 * rows * width * width + 8 * rows * rows * width,
            bytes_accessed=16 * width * width + 8 * rows * width,
            transcendentals=HEADS * rows * rows // 2,
        ),
        name="attend",
    )(order, x, g, norms, bias_q, *tables, weights, weights, weights, weights, up, down)


def rotary_tables(length):
    half = ROT // 2
    frequency = ROPE_BASE ** (-(np.arange(half) * 2.0 / ROT))
    angle = np.arange(length)[:, None] * frequency[None, :]
    cosine, sine = np.cos(angle), np.sin(angle)
    rest = np.zeros((length, HD - ROT))
    none = np.zeros_like(sine)
    cos_full = np.concatenate([cosine, cosine, rest + 1.0], axis=1)
    low = np.concatenate([-sine, none, rest], axis=1)
    high = np.concatenate([none, sine, rest], axis=1)
    return tuple(jnp.asarray(np.tile(t, (1, 2)).astype(np.float32)) for t in (cos_full, low, high))


def adamw(weight, grad, first, second, rate, decay):
    first_new = BETA_ONE * first + (1.0 - BETA_ONE) * grad
    second_new = BETA_TWO * second + (1.0 - BETA_TWO) * grad * grad
    first_hat = first_new / (1.0 - BETA_ONE**STEP)
    second_hat = second_new / (1.0 - BETA_TWO**STEP)
    weight_new = weight - rate * (first_hat / (jnp.sqrt(second_hat) + EPS_ADAM) + decay * weight)
    return (first_new, second_new, weight_new)


def shards(
    tokens, out_grad, block_order, qkv_weight, out_weight, up_weight, down_weight, norm_params, bias_params,
    qkv_first, qkv_second, out_first, out_second, up_first, up_second, down_first, down_second,
    norm_first, norm_second, bias_first, bias_second,
):
    groups, ring = lax.axis_size("dp"), lax.axis_size("ctx")
    group, rank = lax.axis_index("dp"), lax.axis_index("ctx")
    batch, piece, width = tokens.shape
    length = piece * ring
    count = batch * piece
    ff = up_weight.shape[1]

    share = bias_params.shape[0]
    lanes = share + -share % 128
    small = jnp.concatenate([
        jnp.pad(bias_params[None, :], ((0, 0), (0, lanes - share))),
        jnp.pad(norm_params, ((0, 3), (0, lanes - norm_params.shape[1]))),
    ])
    x_rows, g_rows = tokens.reshape(count, width), out_grad.reshape(count, width)
    att_copy, biases, norms, home_x, home_g, feed_out, h_feed, dup, ddown, dbias_up, small_feed = gather_feed(
        up_weight, down_weight, qkv_weight, out_weight, small, x_rows, g_rows, piece, ring * share
    )

    odd = group % 2

    order = block_order[jnp.clip(rank - odd, 0, batch - 1)]
    spots = jnp.arange(order.shape[0])
    order = jnp.stack([order, jnp.sum(jnp.where(order[None, :] == spots[:, None], spots[None, :], 0), axis=1)])

    attend_out, h_attend, dq, dk, dv, dout, dbias_q, small_attend, up_grad, down_grad = attend(
        order, home_x, home_g, norms, biases, rotary_tables(length), att_copy, dup, ddown
    )

    dqkv = jnp.concatenate([dq, dk, dv], axis=1)
    tail = jnp.concatenate(
        [small_attend[:2].reshape(-1), small_feed[:2].reshape(-1), dbias_q[0], small_feed[2], dbias_up[0], small_feed[2]]
    )
    entries = tail.shape[0]
    tail = jnp.pad(tail, (0, -entries % 1024)).reshape(-1, 128)
    *owned, tail, ret_mixed, ret_back = reduce_all((dqkv, dout), tail, attend_out, h_attend, batch)
    up_grad, down_grad, qkv_grad, out_grads = (
        g.reshape(w.shape).astype(F32)
        for g, w in zip((up_grad, down_grad, *owned), (up_weight, down_weight, qkv_weight, out_weight))
    )
    tail = tail.reshape(-1)[:entries]
    returned = [v.reshape(count, width).astype(F32) for v in (ret_mixed, ret_back)]

    rows = x_rows.astype(F32)
    bias_rows = biases[0:1, width : 2 * width] + biases[0:1, 2 * width + ff :]
    layer_out = (rows + returned[0] + feed_out + bias_rows).astype(BF16).reshape(batch, piece, width)
    xh, scale = normalized(rows)
    h = returned[1] + h_feed
    inner = jnp.mean(h * xh, axis=-1, keepdims=True)
    input_grad = g_rows.astype(F32) + scale * (h - jnp.mean(h, axis=-1, keepdims=True) - xh * inner)
    input_grad = input_grad.reshape(batch, piece, width)

    norm_grad = lax.dynamic_slice_in_dim(tail[: 4 * width].reshape(4, width), rank * (width // ring), width // ring, 1)
    bias_grad = lax.dynamic_slice_in_dim(tail[4 * width :], rank * share, share, 0)

    qkv_new = adamw(qkv_weight, qkv_grad, qkv_first, qkv_second, 0.1, DECAY)
    out_new = adamw(out_weight, out_grads, out_first, out_second, 0.6, DECAY)
    up_new = adamw(up_weight, up_grad, up_first, up_second, 0.1, DECAY)
    down_new = adamw(down_weight, down_grad, down_first, down_second, 0.05, DECAY)
    norm_new = adamw(norm_params, norm_grad, norm_first, norm_second, 0.6, 0.0)
    bias_new = adamw(bias_params, bias_grad, bias_first, bias_second, 0.6, 0.0)
    return (
        layer_out, input_grad, *qkv_new, *out_new, *up_new, *down_new,
        norm_new[0], norm_new[1][:2], norm_new[1][2:], norm_new[2], *bias_new,
    )


def solution(mesh):
    rows, columns, token = P("ctx", None), P(None, "ctx"), P("dp", "ctx", None)
    in_specs = (token, token, P("dp", None)) + (rows,) * 4 + (columns, P("ctx")) + (rows,) * 8
    in_specs += (columns, columns, P("ctx"), P("ctx"))
    out_specs = (token, token) + (rows,) * 12 + (columns,) * 4 + (P("ctx"),) * 3
    return jax.shard_map(shards, mesh=mesh, in_specs=in_specs, out_specs=out_specs, check_vma=False)
```

```python
import functools
import math

import jax
import jax.numpy as jnp
import numpy as np
from jax import lax
from jax.experimental import pallas as pl
from jax.experimental.pallas import tpu as pltpu
from jax.sharding import PartitionSpec as P

HEADS = 12
HD = 64
STEP = 10
ROT = 16
SEQS = 3
BLOCK = 128
QUAD = 4
MLP_LEVELS = (2, 1)

EPS_NORM = 1e-05
BETA_ONE = 0.9
BETA_TWO = 0.95
EPS_ADAM = 1e-08
DECAY = 0.01
ROPE_BASE = 10000.0
F32 = jnp.float32
BF16 = jnp.bfloat16
MIB = 1024 * 1024


def dot(left, right, dims=((1,), (0,))):
    return lax.dot_general(left, right, (dims, ((), ())), preferred_element_type=F32)


NN = ((1,), (0,))
NT = ((1,), (1,))
TN = ((0,), (0,))


def normalized(values):
    mean = jnp.mean(values, axis=-1, keepdims=True)
    centred = values - mean
    variance = jnp.mean(centred * centred, axis=-1, keepdims=True)
    scale = lax.rsqrt(variance + EPS_NORM)
    return centred * scale, scale


MESH = pl.DeviceIdType.MESH


def plane(d):
    core, x, y = d % 2, d // 2 % 2, d // 4 % 2
    return core, x, y, d + 1 - 2 * core, d + 2 - 4 * x, d + 4 - 8 * y


def gather_kernel(
    up, down, qkv, out, small, tokens, cotangents,
    att_all, small_all, norm_all, home_x, home_g, out_ref, h_ref, up_part, down_part, dbias_ref, sums_ref,
    up_all, down_all, att_own, up_wide, down_wide, att_wide, small_in, x_ref, g_ref, m_ref, mt_ref, hid_ref, dup_in_ref,
    dup_ref, up_core, up_first, ddown_ref, down_core,
    z_send, z_recv, p_send, p_recv, s_send, s_recv, t_send, t_recv, local, out_sem, c_send, c_recv,
):
    ring = lax.axis_size("ctx")
    d, z = lax.axis_index("dp"), lax.axis_index("ctx")
    core, x, y, core_id, x_id, y_id = plane(d)
    own = x + 2 * y
    own_x, own_y, far = own + 1 - 2 * x, own + 2 - 4 * y, 3 - own
    count, width = tokens.shape
    piece = home_x.shape[0] // ring
    batch = count // piece
    arrays = ((up_wide, up_all, False), (down_wide, down_all, True), (att_own, att_all, False))

    def slot(a, base, place, half=None):
        source, whole, tall = arrays[a]
        ref = source if base is None else whole
        rows, columns = source.shape
        at = 0 if base is None else base * rows
        height, span = rows // 4, columns // 2
        at = at + place * height
        column = core * span
        if half is not None:
            if tall:
                height = height // 2
                at = at + half * height
            else:
                span = span // 2
                column = column + half * span
        return ref.at[pl.ds(pl.multiple_of(at, 16), height), pl.ds(pl.multiple_of(column, 128), span)]

    def other_slot(a, base, place):
        source, whole, tall = arrays[a]
        rows, columns = source.shape
        at = pl.multiple_of(base * rows + place * (rows // 4), 16)
        column = pl.multiple_of((1 - core) * (columns // 2), 128)
        return whole.at[pl.ds(at, rows // 4), pl.ds(column, columns // 2)]

    def remote(src, dst, send, recv, dp, ctx):
        return pltpu.make_async_remote_copy(
            src_ref=src, dst_ref=dst, send_sem=send, recv_sem=recv, device_id=(dp, ctx), device_id_type=MESH
        )

    columns = qkv.shape[1]
    wide_loads = [
        [pltpu.make_async_copy(up, up_wide, local.at[0])],
        [pltpu.make_async_copy(down, down_wide, local.at[1])],
        [
            pltpu.make_async_copy(qkv, att_wide.at[:, pl.ds(0, columns)], local.at[2]),
            pltpu.make_async_copy(out, att_wide.at[:, pl.ds(columns, out.shape[1])], local.at[8]),
        ],
    ]
    for loads in wide_loads:
        for copy in loads:
            copy.start()

    def cast_own(a):
        for copy in wide_loads[a]:
            copy.wait()
        wide, target = ((up_wide, up_all), (down_wide, down_all), (att_wide, att_own))[a]
        rows = wide.shape[0]
        tile = 64
        base = 0 if a == 2 else z * rows

        def body(t, _):
            value = wide[pl.ds(pl.multiple_of(t * tile, 16), tile), :].astype(BF16)
            target[pl.ds(pl.multiple_of(base + t * tile, 16), tile), :] = value
            return 0

        lax.fori_loop(0, rows // tile, body, 0)

    barrier = pltpu.get_barrier_semaphore()
    for k in range(1, ring):
        pl.semaphore_signal(barrier, inc=1, device_id=(d, (z + k) % ring), device_id_type=MESH)
    for other in (core_id, x_id, y_id):
        pl.semaphore_signal(barrier, inc=1, device_id=(other, z), device_id_type=MESH)
    cast_own(0)
    pl.semaphore_wait(barrier, ring + 2)

    def hop(a, way, h):
        shard = z - h if way == 0 else z + h
        target = z + 1 if way == 0 else z - 1
        src = slot(a, None, own) if h == 0 and a == 2 else slot(a, shard, own)
        return remote(src, slot(a, shard, own), z_send.at[a, way, h], z_recv.at[a, way, h], d, target)

    def can_send(way, h):
        shard = z - h if way == 0 else z + h
        target = z + 1 if way == 0 else z - 1
        return (shard >= 0) & (shard < ring) & (target >= 0) & (target < ring)

    def in_range(way, h):
        shard = z - h if way == 0 else z + h
        return (shard >= 0) & (shard < ring)

    def cast(a, shard, j):
        send, recv = p_send.at[a, shard, j], p_recv.at[a, shard, j]
        if j == 0:
            ref = slot(a, shard, own)
            return remote(ref, ref, send, recv, x_id, z)
        if j == 1:
            ref = slot(a, shard, own)
            return remote(ref, ref, send, recv, y_id, z)
        if j == 2:
            ref = slot(a, shard, own_x, 0)
            return remote(ref, ref, send, recv, y_id, z)
        if j == 3:
            ref = slot(a, shard, own_y, 1)
            return remote(ref, ref, send, recv, x_id, z)
        ref = slot(a, shard, (own, own_x, own_y, far)[j - 4])
        return remote(ref, ref, send, recv, core_id, z)

    def arrived(a, shard, j):
        send, recv = p_send.at[a, shard, j], p_recv.at[a, shard, j]
        ref = {0: lambda: slot(a, shard, own_x), 1: lambda: slot(a, shard, own_y),
               2: lambda: slot(a, shard, far, 0), 3: lambda: slot(a, shard, far, 1)}.get(
            j, lambda: other_slot(a, shard, (own, own_x, own_y, far)[j - 4]))()
        remote(ref, ref, send, recv, core_id, z).wait_recv()

    def start_hops(a):
        for way in range(2):
            @pl.when(can_send(way, 0))
            def _(way=way):
                hop(a, way, 0).start()

    def small_copy(k):
        return remote(small, small_in.at[z], s_send.at[k], s_recv.at[k], d, (z + k) % ring)

    def stage_a(a, h):
        for way in range(2):
            @pl.when(in_range(way, h))
            def _(way=way):
                shard = z - h if way == 0 else z + h
                ref = slot(a, shard, own)
                remote(ref, ref, z_send.at[a, way, h - 1], z_recv.at[a, way, h - 1], core_id, z).wait_recv()

                @pl.when(can_send(way, h))
                def _():
                    hop(a, way, h).start()

                cast(a, shard, 0).start()
                cast(a, shard, 1).start()
                cast(a, shard, 4).start()

    def stage_b(a, h):
        for way in range(2):
            @pl.when(in_range(way, h))
            def _(way=way):
                shard = z - h if way == 0 else z + h
                arrived(a, shard, 0)
                cast(a, shard, 2).start()
                cast(a, shard, 5).start()
                arrived(a, shard, 1)
                cast(a, shard, 3).start()
                cast(a, shard, 6).start()

    def stage_c(a, h):
        for way in range(2):
            @pl.when(in_range(way, h))
            def _(way=way):
                shard = z - h if way == 0 else z + h
                arrived(a, shard, 2)
                arrived(a, shard, 3)
                cast(a, shard, 7).start()

    def stage_d(a, h):
        for way in range(2):
            @pl.when(in_range(way, h))
            def _(way=way):
                shard = z - h if way == 0 else z + h
                for j in range(4, 8):
                    arrived(a, shard, j)

    pairs = ((tokens, home_x), (cotangents, home_g))

    def move(which, i):
        source, whole = pairs[which]
        src = source.at[pl.ds(i * piece, piece), :]
        dst = whole.at[pl.ds(pl.multiple_of(z * piece, 16), piece), :]
        return src, dst, i + core

    def start_moves(which):
        for i in range(batch):
            src, dst, target = move(which, i)

            @pl.when(target != z)
            def _(src=src, dst=dst, target=target, i=i):
                remote(src, dst, t_send.at[which, i], t_recv.at[which, z], d, target).start()

            @pl.when(target == z)
            def _(src=src, dst=dst):
                pltpu.make_async_copy(src, dst, local.at[6 + which]).start()

    own_rows = pl.ds(pl.multiple_of(z * att_own.shape[0], 16), att_own.shape[0])
    own_att = pltpu.make_async_copy(att_own, att_all.at[own_rows, :], local.at[9])
    x_load = pltpu.make_async_copy(tokens, x_ref, local.at[3])
    g_load = pltpu.make_async_copy(cotangents, g_ref, local.at[4])
    own_small = pltpu.make_async_copy(small, small_in.at[z], local.at[5])

    start_hops(0)
    cast_own(1)
    start_hops(1)
    cast_own(2)
    start_hops(2)
    for k in range(1, ring):
        small_copy(k).start()
    for copy in (own_att, x_load, g_load, own_small):
        copy.start()
    hops = range(1, ring)
    work = [(a, h) for a in range(3) for h in hops]
    early = 2 * (ring - 1)
    for n in range(len(work)):
        stage_a(*work[n])
        if 1 <= n <= early:
            stage_b(*work[n - 1])
        if 2 <= n <= early + 1:
            stage_c(*work[n - 2])
    start_moves(0)
    start_moves(1)

    own_small.wait()
    for k in range(1, ring):
        ref = small_in.at[(z + ring - k) % ring]
        remote(ref, ref, s_send.at[k], s_recv.at[k], core_id, z).wait_recv()
    x_load.wait()
    g_load.wait()
    entries = small_all.shape[1]
    biases = jnp.zeros((8, entries), F32)
    norms = jnp.zeros((8, width), F32)
    for r in range(ring):
        block = small_in[r].astype(BF16).astype(F32)
        full = jnp.concatenate([block, jnp.zeros((8, entries - block.shape[1]), F32)], axis=1)
        biases += pltpu.roll(full, r * (entries // ring), 1) if r else full
        norms += pltpu.roll(block[:, :width], r * (width // ring), 1) if r else block[:, :width]
    small_all[...] = biases
    norm_all[...] = norms
    ff = up_all.shape[1]
    gain_2, shift_2 = norm_all[3:4, :], norm_all[4:5, :]
    tile = 256
    tiles = count // tile
    for t in range(tiles):
        at = pl.ds(t * tile, tile)
        xh, _ = normalized(x_ref[at, :].astype(F32))
        m = xh * gain_2 + shift_2
        m_ref[at, :] = m.astype(BF16)
        mt_ref[:, at] = m.T.astype(BF16)
        out_ref[at, :] = jnp.zeros((tile, width), F32)
        h_ref[at, :] = jnp.zeros((tile, width), F32)
    for h in hops:
        stage_d(0, h)
        stage_d(1, h)

    strip = dup_ref.shape[3] // ring
    steps = ff // (ring * strip)
    half = ring // 2
    big, by_core = (dup_ref, ddown_ref), (up_core, down_core)
    bits, ids = ((x, y), (y, x)), ((x_id, y_id), (y_id, x_id))

    def sizes(a):
        return by_core[a].shape[2], by_core[a].shape[3]

    def slice_of(order):
        return 2 * bits[order][0] + bits[order][1]

    def core_copy(a, i):
        _, span = sizes(a)
        away = pl.ds(pl.multiple_of((1 - core) * span, 128), span)
        return remote(big[a].at[i, :, :, away], by_core[a].at[i], c_send.at[a, i, 0], c_recv.at[a, i, 0], core_id, z)

    def first_copy(a, i, order):
        height, _ = sizes(a)
        own = pl.ds(order * half, half)
        away = pl.ds(pl.multiple_of((1 - bits[order][0]) * (height // 2), 16), height // 2)
        return remote(
            by_core[a].at[i, own, away, :], up_first.at[i, own], c_send.at[a, i, 1 + order],
            c_recv.at[a, i, 1 + order], ids[order][0], z,
        )

    def add(into, at, term, owners):
        height = term(0).shape[0]
        tile = 32 if height % 48 else 48

        def body(n, _):
            o, t = n // (height // tile), n % (height // tile)
            spot = pl.ds(pl.multiple_of(at + t * tile, 16), tile)
            value = term(o)[pl.ds(pl.multiple_of(t * tile, 16), tile), :]
            into[o, spot, :] = (into[o, spot, :].astype(F32) + value.astype(F32)).astype(BF16)
            return 0

        lax.fori_loop(0, owners * (height // tile), body, 0)

    def chunk_1(i):
        for a in range(2):
            _, span = sizes(a)
            core_copy(a, i).wait_recv()
            keep = pl.ds(pl.multiple_of(core * span, 128), span)
            add(by_core[a].at[i], 0, lambda o: big[a].at[i, o, :, keep], ring)
        for order in range(2):
            first_copy(0, i, order).start()
        parts_out(1, i)[0].start()

    def chunk_2(i):
        height, _ = sizes(0)
        for order in range(2):
            own = pl.ds(order * half, half)
            first_copy(0, i, order).wait_recv()
            at = bits[order][0] * (height // 2)
            add(by_core[0].at[i, own], at, lambda o: up_first.at[i, order * half + o], half)
        for copy in parts_out(0, i):
            copy.start()

    def parts_out(a, i):
        height, span = sizes(a)
        if a == 1:
            return [pltpu.make_async_copy(by_core[1].at[i], down_part.at[:, i], out_sem.at[i, 2 * half])]
        copies = []
        for order in range(2):
            own = pl.ds(order * half, half)
            rows = pl.ds(pl.multiple_of(bits[order][0] * (height // 2), 16), height // 2)
            for n in range(half):
                copies.append(pltpu.make_async_copy(
                    by_core[0].at[i, own, rows, pl.ds(n * strip, strip)],
                    up_part.at[own, :, pl.ds(pl.multiple_of(n * steps * strip + i * strip, 128), strip)],
                    out_sem.at[i, half * order + n],
                ))
        return copies

    def feed_step(step, _):
        for h in hops:
            @pl.when(step == h - 1)
            def _(h=h):
                stage_b(2, h)

            @pl.when(step == h)
            def _(h=h):
                stage_c(2, h)

        @pl.when(step < steps)
        def _():
            spots = [pl.ds(pl.multiple_of(r * (ff // ring) + step * strip, 128), strip) for r in range(ring)]
            bias_spots = [
                pl.ds(pl.multiple_of(2 * width + r * (ff // ring) + step * strip, 128), strip) for r in range(ring)
            ]
            up_part_ = jnp.concatenate([up_all[:, at] for at in spots], axis=1)
            down_part_ = jnp.concatenate([down_all[at, :] for at in spots], axis=0)
            bias = jnp.concatenate([small_all[0:1, at] for at in bias_spots], axis=1)
            total = jnp.zeros((1, ring * strip), F32)
            for t in range(tiles):
                at = pl.ds(t * tile, tile)
                u = dot(m_ref[at, :], up_part_) + bias
                cdf = 0.5 * (1.0 + lax.erf(u * (1.0 / math.sqrt(2.0))))
                hidden = (u * cdf).astype(BF16)
                slope = cdf + u * jnp.exp(-0.5 * u * u) * (1.0 / math.sqrt(2.0 * math.pi))
                back = (dot(g_ref[at, :], down_part_, NT) * slope).astype(BF16)
                hid_ref[at, :] = hidden
                dup_in_ref[at, :] = back
                total += jnp.sum(back.astype(F32), axis=0, keepdims=True)
                out_ref[at, :] += dot(hidden, down_part_)
                h_ref[at, :] += dot(back, up_part_, NT)
            for r in range(ring):
                dbias_ref[0:1, spots[r]] = total[:, r * strip : (r + 1) * strip]
            ddown = dot(hid_ref[...], g_ref[...], TN).astype(BF16)
            dup = dot(mt_ref[...], dup_in_ref[...]).astype(BF16)
            for r in range(ring):
                ddown_ref[step, r] = ddown[r * strip : (r + 1) * strip, :]
                dup_ref[step, r] = dup[r * (width // ring) : (r + 1) * (width // ring), :]
            core_copy(0, step).start()
            core_copy(1, step).start()

        for lag, stage in ((1, chunk_1), (3, chunk_2)):
            @pl.when((step >= lag) & (step < steps + lag))
            def _(lag=lag, stage=stage):
                stage(step - lag)

        return 0

    lax.fori_loop(0, steps + 3, feed_step, 0)

    gain = jnp.zeros((1, width), F32)
    shift = jnp.zeros((1, width), F32)
    sums = jnp.zeros((1, width), F32)
    for t in range(tiles):
        at = pl.ds(t * tile, tile)
        xh, _ = normalized(x_ref[at, :].astype(F32))
        dm = h_ref[at, :]
        gain += jnp.sum(dm * xh, axis=0, keepdims=True)
        shift += jnp.sum(dm, axis=0, keepdims=True)
        sums += jnp.sum(g_ref[at, :].astype(F32), axis=0, keepdims=True)
        h_ref[at, :] = dm * gain_2
    sums_ref[...] = jnp.concatenate([gain, shift, sums, jnp.zeros((5, width), F32)], axis=0)

    mine = z - core
    for which in range(2):
        for k in range(1, ring):
            @pl.when((mine >= 0) & (mine < batch))
            def _(which=which, k=k):
                other = (z + k) % ring
                ref = pairs[which][1].at[pl.ds(pl.multiple_of(other * piece, 16), piece), :]
                remote(ref, ref, t_send.at[which, 0], t_recv.at[which, other], core_id, z).wait_recv()
    for h in hops:
        stage_d(2, h)
    for k in range(1, ring):
        small_copy(k).wait_send()
    for a in range(3):
        for way in range(2):
            for h in range(ring - 1):
                @pl.when(can_send(way, h))
                def _(a=a, way=way, h=h):
                    hop(a, way, h).wait_send()
        for h in hops:
            for way in range(2):
                @pl.when(in_range(way, h))
                def _(a=a, h=h, way=way):
                    shard = z - h if way == 0 else z + h
                    for j in range(8):
                        cast(a, shard, j).wait_send()
    for which in range(2):
        for i in range(batch):
            src, dst, target = move(which, i)

            @pl.when(target != z)
            def _(src=src, dst=dst, target=target, which=which, i=i):
                remote(src, dst, t_send.at[which, i], t_recv.at[which, z], d, target).wait_send()

            @pl.when(target == z)
            def _(src=src, dst=dst, which=which):
                pltpu.make_async_copy(src, dst, local.at[6 + which]).wait()
    own_att.wait()

    def close(i, _):
        for a in range(2):
            core_copy(a, i).wait_send()
            for copy in parts_out(a, i):
                copy.wait()
        for order in range(2):
            first_copy(0, i, order).wait_send()
        return 0

    lax.fori_loop(0, steps, close, 0)


def gather_feed(up, down, qkv, out, small, tokens, cotangents, piece, entries):
    ring = lax.axis_size("ctx")
    count, width = tokens.shape
    ff = up.shape[1]
    strip = 128
    chunk = ring * strip
    steps = ff // chunk
    shard = up.shape[0]
    columns = qkv.shape[1] + out.shape[1]
    home = jax.ShapeDtypeStruct((ring * piece, width), tokens.dtype)
    rows = jax.ShapeDtypeStruct((count, width), F32)
    dma = pltpu.SemaphoreType.DMA
    anywhere = pl.BlockSpec(memory_space=pl.ANY)
    vmem = pl.BlockSpec(memory_space=pltpu.VMEM)
    return pl.pallas_call(
        gather_kernel,
        in_specs=[anywhere] * 7,
        out_specs=[anywhere, vmem, vmem, anywhere, anywhere, vmem, vmem, anywhere, anywhere, vmem, vmem],
        out_shape=[
            jax.ShapeDtypeStruct((ring * shard, columns), BF16),
            jax.ShapeDtypeStruct((8, entries), F32), jax.ShapeDtypeStruct((8, width), F32), home, home, rows, rows,
            jax.ShapeDtypeStruct((ring, shard // 2, ff // 2), BF16),
            jax.ShapeDtypeStruct((ring, steps, strip, width // 2), BF16),
            jax.ShapeDtypeStruct((8, ff), F32), jax.ShapeDtypeStruct((8, width), F32),
        ],
        scratch_shapes=[
            pltpu.VMEM((ring * shard, ff), BF16), pltpu.VMEM((ring * down.shape[0], width), BF16),
            pltpu.VMEM((shard, columns), BF16),
            pltpu.VMEM(up.shape, F32), pltpu.VMEM(down.shape, F32), pltpu.VMEM((shard, columns), F32),
            pltpu.VMEM((ring, *small.shape), F32),
            pltpu.VMEM((count, width), BF16), pltpu.VMEM((count, width), BF16), pltpu.VMEM((count, width), BF16),
            pltpu.VMEM((width, count), BF16),
            pltpu.VMEM((count, chunk), BF16), pltpu.VMEM((count, chunk), BF16),
            pltpu.VMEM((steps, ring, shard, chunk), BF16), pltpu.VMEM((steps, ring, shard, chunk // 2), BF16),
            pltpu.VMEM((steps, ring, shard // 2, chunk // 2), BF16),
            pltpu.VMEM((steps, ring, strip, width), BF16), pltpu.VMEM((steps, ring, strip, width // 2), BF16),
            dma((3, 2, ring)), dma((3, 2, ring)), dma((3, ring, 8)), dma((3, ring, 8)),
            dma((ring,)), dma((ring,)), dma((2, count // piece)), dma((2, ring)), dma((10,)), dma((steps, ring + 1)),
            dma((2, steps, 3)), dma((2, steps, 3)),
        ],
        compiler_params=pltpu.CompilerParams(
            collective_id=0, has_side_effects=True, vmem_limit_bytes=60 * MIB
        ),
        cost_estimate=pl.CostEstimate(
            flops=12 * count * width * ff, bytes_accessed=60 * MIB, transcendentals=count * ff
        ),
        name="gather_feed",
    )(up, down, qkv, out, small, tokens, cotangents)


def remote(src, dst, send_sem, recv_sem, dp, ctx):
    return pltpu.make_async_remote_copy(
        src_ref=src, dst_ref=dst, send_sem=send_sem, recv_sem=recv_sem, device_id=(dp, ctx), device_id_type=MESH
    )


def team_id(d, t):
    return d + (8 << t) * (1 - 2 * (d // (8 << t) % 2))


def greet(teams):
    ring = lax.axis_size("ctx")
    d, z = lax.axis_index("dp"), lax.axis_index("ctx")
    core, x, y, core_id, x_id, y_id = plane(d)
    barrier = pltpu.get_barrier_semaphore()
    partners = [core_id, x_id, y_id, x_id + y_id - d] + [team_id(d, t) for t in range(teams)]
    for k in range(1, ring):
        pl.semaphore_signal(barrier, inc=1, device_id=(d, (z + k) % ring), device_id_type=MESH)
    for other in partners:
        pl.semaphore_signal(barrier, inc=1, device_id=(other, z), device_id_type=MESH)
    pl.semaphore_wait(barrier, ring - 1 + len(partners))


def reducer(teams, levels, ins, sums, bufs, send, recv, load):
    count = len(ins)
    ring = lax.axis_size("ctx")
    d, z = lax.axis_index("dp"), lax.axis_index("ctx")
    core, x, y, core_id, x_id, y_id = plane(d)
    far_id = x_id + y_id - d
    bits, ids = ((x, y), (y, x)), ((x_id, y_id), (y_id, x_id))
    spots = ((x, y), (1 - x, y), (x, 1 - y), (1 - x, 1 - y))

    def sizes(a):
        _, strips, quarter, span = bufs[a][-1].shape
        return strips, quarter, span

    def owners(a, order):
        strips = sizes(a)[0]
        return pl.ds(order * ring // 2 * strips, ring // 2 * strips)

    def rows_at(at, height):
        return pl.ds(pl.multiple_of(at, 16), height)

    def kept(a, order):
        return 0 if levels[a] == 2 else bits[order][0] * 2 * sizes(a)[1]

    def core_copy(a):
        span = sizes(a)[2]
        away = pl.ds(pl.multiple_of((1 - core) * span, 128), span)
        return remote(ins[a].at[:, :, away], bufs[a][1], send.at[a, 0], recv.at[a, 0], core_id, z)

    def own_load(a):
        span = sizes(a)[2]
        keep = pl.ds(pl.multiple_of(core * span, 128), span)
        src = ins[a].at[:, :, keep] if levels[a] == 0 else ins[a]
        return pltpu.make_async_copy(src, bufs[a][0], load.at[a])

    def first_copy(a, order):
        quarter = sizes(a)[1]
        away = rows_at((1 - bits[order][0]) * 2 * quarter, 2 * quarter)
        return remote(
            bufs[a][0].at[owners(a, order), away, :], bufs[a][2].at[owners(a, order)], send.at[a, 1 + order],
            recv.at[a, 1 + order], ids[order][0], z,
        )

    def second_copy(a, order):
        quarter = sizes(a)[1]
        away = rows_at(kept(a, order) + (1 - bits[order][1]) * quarter, quarter)
        return remote(
            bufs[a][0].at[owners(a, order), away, :], bufs[a][3].at[owners(a, order)], send.at[a, 3 + order],
            recv.at[a, 3 + order], ids[order][1], z,
        )

    def own_quarter(a, owner):
        strips, quarter, _ = sizes(a)
        order = owner // (ring // 2)
        first, second = (1 - order) * x + order * y, (1 - order) * y + order * x
        at = second * quarter if levels[a] == 2 else (2 * first + second) * quarter
        return bufs[a][0].at[pl.ds(owner * strips, strips), rows_at(at, quarter), :]

    def owner_copy(a, k):
        to = (z + k) % ring
        return remote(own_quarter(a, to), bufs[a][4].at[k - 1], send.at[a, 4 + k], recv.at[a, 4 + k], d, to)

    def team_copy(a, t):
        j = 4 + ring + 7 + t
        return remote(bufs[a][5].at[0], bufs[a][5].at[1 + t], send.at[a, j], recv.at[a, j], team_id(d, t), z)

    def final(a, spot, side):
        strips, quarter, span = sizes(a)
        order = z // (ring // 2)
        xx, yy = spots[spot]
        at = ((1 - order) * (2 * xx + yy) + order * (2 * yy + xx)) * quarter
        return sums[a].at[:, rows_at(at, quarter), pl.ds(pl.multiple_of(side * span, 128), span)]

    def spread(a, j):
        s, r = send.at[a, 4 + ring + j - 1], recv.at[a, 4 + ring + j - 1]
        if j < 4:
            return remote(bufs[a][5].at[0], final(a, 0, core), s, r, (x_id, y_id, far_id)[j - 1], z)
        src = bufs[a][5].at[0] if j == 4 else final(a, j - 4, core)
        return remote(src, final(a, j - 4, core), s, r, core_id, z)

    def spread_here(a, j):
        s, r = send.at[a, 4 + ring + j - 1], recv.at[a, 4 + ring + j - 1]
        ref = final(a, j, core) if j < 4 else final(a, j - 4, 1 - core)
        remote(ref, ref, s, r, core_id, z).wait_recv()

    def keep_own(a):
        return pltpu.make_async_copy(bufs[a][5].at[0], final(a, 0, core), load.at[count + a])

    def add(into, at, term, blocks):
        height = term.shape[1]
        tile = 32 if height % 48 else 48

        def body(n, _):
            o, t = n // (height // tile), n % (height // tile)
            spot = rows_at(at + t * tile, tile)
            value = term[o, rows_at(t * tile, tile), :]
            into[o, spot, :] = (into[o, spot, :].astype(F32) + value.astype(F32)).astype(BF16)
            return 0

        lax.fori_loop(0, blocks * (height // tile), body, 0)

    def enter(a):
        if levels[a] == 0:
            core_copy(a).start()
        own_load(a).start()

    def first(a):
        own_load(a).wait()
        if levels[a] == 0:
            core_copy(a).wait_recv()
            add(bufs[a][0], 0, bufs[a][1], bufs[a][0].shape[0])
        if levels[a] < 2:
            for order in range(2):
                first_copy(a, order).start()

    def second(a):
        for order in range(2):
            if levels[a] < 2:
                first_copy(a, order).wait_recv()
                own = owners(a, order)
                add(bufs[a][0].at[own], kept(a, order), bufs[a][2].at[own], ring // 2 * sizes(a)[0])
            second_copy(a, order).start()

    def to_owner(a):
        for order in range(2):
            second_copy(a, order).wait_recv()
            own = owners(a, order)
            at = kept(a, order) + bits[order][1] * sizes(a)[1]
            add(bufs[a][0].at[own], at, bufs[a][3].at[own], ring // 2 * sizes(a)[0])
        for k in range(1, ring):
            owner_copy(a, k).start()

    def total(a):
        for k in range(1, ring):
            owner_copy(a, k).wait_recv()
        mine = own_quarter(a, z)
        for s in range(sizes(a)[0]):
            terms = [mine[s]] + [bufs[a][4][k, s] for k in range(ring - 1)]
            bufs[a][5][0, s] = sum((t.astype(F32) for t in terms[1:]), terms[0].astype(F32)).astype(BF16)
        for t in range(teams):
            team_copy(a, t).start()
            team_copy(a, t).wait()
            bufs[a][5][0] = (bufs[a][5][0].astype(F32) + bufs[a][5][1 + t].astype(F32)).astype(BF16)
        keep_own(a).start()
        for j in range(1, 5):
            spread(a, j).start()

    def share(a):
        for j in range(1, 4):
            spread_here(a, j)
            spread(a, 4 + j).start()

    def close(a):
        for j in range(4, 8):
            spread_here(a, j)
        if levels[a] == 0:
            core_copy(a).wait_send()
        for order in range(2):
            if levels[a] < 2:
                first_copy(a, order).wait_send()
            second_copy(a, order).wait_send()
        for k in range(1, ring):
            owner_copy(a, k).wait_send()
        for j in range(1, 8):
            spread(a, j).wait_send()
        keep_own(a).wait()

    return enter, first, second, to_owner, total, share, close


def reducer_scratch(levels, shapes, teams, ring):
    scratch = []
    for level, (strips, rows, columns) in zip(levels, shapes):
        blocks, span = ring * strips, columns // 2
        none = (1, 16, 128)
        scratch += [
            pltpu.VMEM((blocks, rows // 2 if level == 2 else rows, span), BF16),
            pltpu.VMEM((blocks, rows, span) if level == 0 else none, BF16),
            pltpu.VMEM((blocks, rows // 2, span) if level < 2 else none, BF16),
            pltpu.VMEM((blocks, rows // 4, span), BF16),
            pltpu.VMEM((ring - 1, strips, rows // 4, span), BF16),
            pltpu.VMEM((1 + teams, strips, rows // 4, span), BF16),
        ]
    copies = 4 + ring + 7 + teams
    dma = pltpu.SemaphoreType.DMA
    return scratch + [dma((len(levels), copies)), dma((len(levels), copies)), dma((2 * len(levels),))]


def reduce_kernel(count, teams, *refs):
    ring = lax.axis_size("ctx")
    d, z = lax.axis_index("dp"), lax.axis_index("ctx")
    core, x, y, core_id, x_id, y_id = plane(d)
    grads, (small, mixed, back) = refs[:count], refs[count : count + 3]
    refs = refs[count + 3 :]
    sums, (small_out, ret_mixed, ret_back) = refs[:count], refs[count : count + 3]
    refs = refs[count + 3 :]
    bufs = [refs[6 * a : 6 * a + 6] for a in range(count)]
    send, recv, load, small_acc, small_in, s_send, s_recv, r_send, r_recv, r_local = refs[6 * count :]
    batch, piece = ret_mixed.shape[:2]
    greet(teams)
    stages = reducer(teams, (0,) * count, grads, sums, bufs, send, recv, load)

    def returned(which, i, to):
        source, target = ((mixed, ret_mixed), (back, ret_back))[which]
        return source.at[pl.ds(pl.multiple_of(to * piece, 16), piece), :], target.at[i]

    mine = z - core
    is_home = (mine >= 0) & (mine < batch)

    def start_returns():
        for which in range(2):
            for i in range(batch):
                @pl.when(mine == i)
                def _(which=which, i=i):
                    for k in range(1, ring):
                        to = (z + k) % ring
                        src, dst = returned(which, i, to)
                        remote(src, dst, r_send.at[which, k], r_recv.at[which, i], d, to).start()
                    src, dst = returned(which, i, z)
                    pltpu.make_async_copy(src, dst, r_local.at[which]).start()

    def wait_returns():
        for which in range(2):
            for i in range(batch):
                src, dst = returned(which, i, z)

                @pl.when(mine == i)
                def _(which=which, i=i, src=src, dst=dst):
                    for k in range(1, ring):
                        to = (z + k) % ring
                        remote(*returned(which, i, to), r_send.at[which, k], r_recv.at[which, i], d, to).wait_send()
                    pltpu.make_async_copy(src, dst, r_local.at[which]).wait()

                @pl.when(mine != i)
                def _(which=which, i=i, src=src, dst=dst):
                    remote(src, dst, r_send.at[which, 0], r_recv.at[which, i], core_id, z).wait_recv()

    steps = [core_id, x_id, y_id] + [team_id(d, t) for t in range(teams)]

    def small_copy(n):
        return remote(small_acc, small_in.at[n], s_send.at[n], s_recv.at[n], steps[n], z)

    def small_owner(k):
        n = len(steps) + k - 1
        return remote(small_acc, small_in.at[n], s_send.at[n], s_recv.at[n], d, (z + k) % ring)

    def small_step(n):
        if n < len(steps):
            if n == 0:
                small_acc[...] = small[...]
            small_copy(n).start()
        elif n == len(steps):
            for k in range(1, ring):
                small_owner(k).start()

    def small_close(n):
        if n < len(steps):
            small_copy(n).wait()
            small_acc[...] += small_in[n]
        elif n == len(steps):
            for k in range(1, ring):
                small_owner(k).wait()
            total = small_acc[...]
            for k in range(ring - 1):
                total += small_in[len(steps) + k]
            small_out[...] = total

    for a in range(count):
        stages[0](a)
    start_returns()
    for n in range(1, max(len(stages), len(steps) + 2)):
        small_step(n - 1)
        if n < len(stages):
            for a in range(count):
                stages[n](a)
        small_close(n - 1)
    wait_returns()


def reduce_all(grads, small, mixed, back, batch):
    ring, groups = lax.axis_size("ctx"), lax.axis_size("dp")
    teams = (groups // 8).bit_length() - 1
    count = len(grads)
    grads = [g.reshape(ring, -1, g.shape[1]) for g in grads]
    length, width = mixed.shape
    dma = pltpu.SemaphoreType.DMA
    anywhere = pl.BlockSpec(memory_space=pl.ANY)
    vmem = pl.BlockSpec(memory_space=pltpu.VMEM)
    rounds = 3 + teams + ring - 1
    scratch = reducer_scratch((0,) * count, [(1, *g.shape[1:]) for g in grads], teams, ring)
    scratch += [
        pltpu.VMEM(small.shape, F32), pltpu.VMEM((rounds, *small.shape), F32), dma((rounds,)), dma((rounds,)),
        dma((2, ring)), dma((2, batch)), dma((2,)),
    ]
    token = jax.ShapeDtypeStruct((batch, length // ring, width), BF16)
    return pl.pallas_call(
        functools.partial(reduce_kernel, count, teams),
        in_specs=[anywhere] * count + [vmem, anywhere, anywhere],
        out_specs=[anywhere] * count + [vmem, anywhere, anywhere],
        out_shape=[jax.ShapeDtypeStruct((1, *g.shape[1:]), BF16) for g in grads]
        + [jax.ShapeDtypeStruct(small.shape, F32), token, token],
        scratch_shapes=scratch,
        compiler_params=pltpu.CompilerParams(collective_id=1, has_side_effects=True, vmem_limit_bytes=56 * MIB),
        cost_estimate=pl.CostEstimate(flops=0, bytes_accessed=60 * MIB, transcendentals=0),
        name="reduce",
    )(*grads, small, mixed, back)


def attend_kernel(
    teams, order_ref, x_ref, stored_g_ref, norm_ref, bias_ref, cos_ref, low_ref, high_ref, wq_ref, wk_ref, wv_ref,
    wo_ref, up_ref, down_ref, out_ref, h_ref, dq_ref, dk_ref, dv_ref, dwo_ref, dbias_ref, small_ref, up_sum, down_sum,
    g_ref, a_ref, at_ref, acc_ref, da_ref, q_ref, k_ref, v_ref, do_ref, o_ref, kt_ref, vt_ref, dot_ref, ot_ref,
    dqs_ref, dks_ref, dvs_ref, *reduce_refs,
):
    step = pl.program_id(0)
    bufs = (reduce_refs[:6], reduce_refs[6:12])
    stages = reducer(teams, MLP_LEVELS, (up_ref, down_ref), (up_sum, down_sum), bufs, *reduce_refs[12:])

    plan = {
        (0, 2): ((3, 0),), (1, 0): ((2, 1),), (1, 2): ((3, 1), (4, 0)), (2, 1): ((5, 0),), (2, 2): ((4, 1),),
    }

    def between(phase):
        for (when, at), work in plan.items():
            if at == phase:
                @pl.when(step == when)
                def _(work=work):
                    for n, a in work:
                        stages[n](a)

    @pl.when(step == 0)
    def _():
        stages[0](1)
        stages[0](0)
        greet(teams)
        stages[1](1)
        stages[1](0)
        stages[2](0)

    between(0)

    last = pl.num_programs(0) - 1
    rows, width = x_ref.shape
    lanes = QUAD * HD
    tile = 256
    half = ROT // 2
    scale = 1.0 / math.sqrt(HD)
    blocks = rows // BLOCK
    mine = lax.axis_index("ctx") - lax.axis_index("dp") % 2
    is_home = (mine >= 0) & (mine < SEQS)

    def stored(ref, at):
        values = ref[pl.ds(at * BLOCK, BLOCK), :]
        return jnp.where(is_home, values, jnp.zeros_like(values))

    @pl.when(step == 0)
    def _():
        for j in range(blocks):
            place = order_ref[1, j]
            at = pl.ds(j * BLOCK, BLOCK)
            xh, _ = normalized(stored(x_ref, place).astype(F32))
            a = xh * norm_ref[1:2, :] + norm_ref[2:3, :]
            a_ref[at, :] = a.astype(BF16)
            at_ref[:, at] = a.T.astype(BF16)
            g_ref[at, :] = stored(stored_g_ref, place)
        acc_ref[...] = jnp.zeros_like(acc_ref)
        da_ref[...] = jnp.zeros_like(da_ref)

    def table(ref, at):
        values = ref[at, :]
        return jnp.concatenate([values] * (lanes // values.shape[1]), axis=1)

    def turn(values, at):
        low = pltpu.roll(values, lanes - half, 1) * table(low_ref, at)
        high = pltpu.roll(values, half, 1) * table(high_ref, at)
        return values * table(cos_ref, at), low + high

    for t in range(rows // tile):
        at = pl.ds(t * tile, tile)
        a = a_ref[at, :]
        same, cross = turn(dot(a, wq_ref[...]) + bias_ref[0:1, :], at)
        q_ref[at, :] = ((same + cross).astype(BF16) * scale).astype(BF16)
        same, cross = turn(dot(a, wk_ref[...]), at)
        keys = same + cross
        k_ref[at, :] = keys.astype(BF16)
        kt_ref[:, at] = keys.T.astype(BF16)
        values = dot(a, wv_ref[...])
        v_ref[at, :] = values.astype(BF16)
        vt_ref[:, at] = values.T.astype(BF16)
        mixed_back = dot(g_ref[at, :], wo_ref[...], NT)
        do_ref[at, :] = mixed_back.astype(BF16)
        dot_ref[:, at] = mixed_back.T.astype(BF16)

    dks_ref[...] = jnp.zeros_like(dks_ref)
    dvs_ref[...] = jnp.zeros_like(dvs_ref)
    head_of = lax.broadcasted_iota(jnp.int32, (BLOCK, lanes), 1) // HD

    def stack(values):
        zero = jnp.zeros_like(values)
        return jnp.concatenate([jnp.where(head_of == e, values, zero) for e in range(QUAD)], axis=0)

    def diagonal(values):
        return [values[e * HD : (e + 1) * HD, e * BLOCK : (e + 1) * BLOCK] for e in range(QUAD)]

    between(1)
    spot = lax.broadcasted_iota(jnp.int32, (BLOCK, QUAD * BLOCK), 1) % BLOCK
    admitted = lax.broadcasted_iota(jnp.int32, (BLOCK, QUAD * BLOCK), 0) <= spot
    for b in range(rows // BLOCK):
        at = pl.ds(b * BLOCK, BLOCK)
        seen = pl.ds(0, (b + 1) * BLOCK)
        q = stack(q_ref[at, :])
        do = stack(do_ref[at, :])
        scores = dot(k_ref[seen, :], q, NT)
        edge = jnp.where(admitted, scores[b * BLOCK :], -1e30)
        scores = edge if b == 0 else jnp.concatenate([scores[: b * BLOCK], edge], axis=0)
        top = jnp.max(scores, axis=0, keepdims=True)
        expo = jnp.exp(scores - top)
        probs = expo * (1.0 / jnp.sum(expo, axis=0, keepdims=True))
        low = probs.astype(BF16)
        mixed = diagonal(dot(vt_ref[:, seen], low))
        mixed_back = [dot_ref[e * HD : (e + 1) * HD, at].astype(F32) for e in range(QUAD)]
        share = jnp.concatenate(
            [jnp.sum(m * mb, axis=0, keepdims=True) for m, mb in zip(mixed, mixed_back)], axis=1
        )
        mixed = jnp.concatenate(mixed, axis=0)
        ot_ref[:, at] = mixed.astype(BF16)
        o_ref[at, :] = mixed.T.astype(BF16)
        back = (probs * (dot(v_ref[seen, :], do, NT) - share)).astype(BF16)
        dqs_ref[at, :] = jnp.concatenate(diagonal(dot(kt_ref[:, seen], back)), axis=0).T * scale
        dks_ref[seen, :] += dot(back, q)
        dvs_ref[seen, :] += dot(low, do)
    between(2)

    total = jnp.zeros((1, lanes), F32)
    for t in range(rows // tile):
        at = pl.ds(t * tile, tile)
        same, cross = turn(dqs_ref[at, :], at)
        dq = (same - cross).astype(BF16)
        same, cross = turn(dks_ref[at, :], at)
        dk = (same - cross).astype(BF16)
        dv = dvs_ref[at, :].astype(BF16)
        total += jnp.sum(dq.astype(F32), axis=0, keepdims=True)
        q_ref[at, :] = dq
        k_ref[at, :] = dk
        v_ref[at, :] = dv
        acc_ref[at, :] += dot(o_ref[at, :], wo_ref[...])
        da_ref[at, :] += dot(dq, wq_ref[...], NT) + dot(dk, wk_ref[...], NT) + dot(dv, wv_ref[...], NT)
    dbias_ref[...] = total
    dwo_ref[...] = dot(ot_ref[...], g_ref[...]).astype(BF16)
    dq_ref[...] = dot(at_ref[...], q_ref[...]).astype(BF16)
    dk_ref[...] = dot(at_ref[...], k_ref[...]).astype(BF16)
    dv_ref[...] = dot(at_ref[...], v_ref[...]).astype(BF16)

    @pl.when(step == last)
    def _():
        gain = jnp.zeros((1, width), F32)
        shift = jnp.zeros((1, width), F32)
        for s in range(blocks):
            at = pl.ds(s * BLOCK, BLOCK)
            sorted_at = pl.ds(order_ref[0, s] * BLOCK, BLOCK)
            xh, _ = normalized(stored(x_ref, s).astype(F32))
            da = da_ref[sorted_at, :]
            gain += jnp.sum(da * xh, axis=0, keepdims=True)
            shift += jnp.sum(da, axis=0, keepdims=True)
            h_ref[at, :] = (da * norm_ref[1:2, :]).astype(BF16)
            out_ref[at, :] = acc_ref[sorted_at, :].astype(BF16)
        small_ref[0:1, :] = gain
        small_ref[1:2, :] = shift
        stages[5](1)
        stages[6](0)
        stages[6](1)


def attend(order, x, g, norms, bias_q, tables, weights, up, down):
    ring, groups_dp = lax.axis_size("ctx"), lax.axis_size("dp")
    teams = (groups_dp // 8).bit_length() - 1
    anywhere = pl.BlockSpec(memory_space=pl.ANY)
    shapes = ((1, 2 * up.shape[1], 2 * up.shape[2]), (down.shape[1], down.shape[2], 2 * down.shape[3]))
    down = down.reshape(-1, *down.shape[2:])
    rows, width = x.shape
    lanes = QUAD * HD
    groups = width // lanes
    whole = lambda shape: pl.BlockSpec(shape, lambda i: (0,) * len(shape))
    column = pl.BlockSpec((width, lanes), lambda i: (0, i))
    once = lambda shape: pl.BlockSpec(shape, lambda i: (0,) * len(shape), pipeline_mode=pl.Buffered(1))
    small = jax.ShapeDtypeStruct((rows, width), BF16)
    return pl.pallas_call(
        functools.partial(attend_kernel, teams),
        grid=(groups,),
        in_specs=[
            pl.BlockSpec(memory_space=pltpu.SMEM),
            once((rows, width)),
            once((rows, width)),
            once(norms.shape),
            pl.BlockSpec((8, lanes), lambda i: (0, i)),
            once(tables[0].shape),
            once(tables[0].shape),
            once(tables[0].shape),
            pl.BlockSpec((width, lanes), lambda i: (0, i)),
            pl.BlockSpec((width, lanes), lambda i: (0, groups + i)),
            pl.BlockSpec((width, lanes), lambda i: (0, 2 * groups + i)),
            pl.BlockSpec((lanes, width), lambda i: (i, 3)),
            anywhere,
            anywhere,
        ],
        out_specs=[
            whole((rows, width)),
            whole((rows, width)),
            column,
            column,
            column,
            pl.BlockSpec((lanes, width), lambda i: (i, 0)),
            pl.BlockSpec((1, lanes), lambda i: (0, i)),
            whole((8, width)),
            anywhere,
            anywhere,
        ],
        out_shape=[
            small,
            small,
            jax.ShapeDtypeStruct((width, width), BF16),
            jax.ShapeDtypeStruct((width, width), BF16),
            jax.ShapeDtypeStruct((width, width), BF16),
            jax.ShapeDtypeStruct((width, width), BF16),
            jax.ShapeDtypeStruct((1, width), F32),
            jax.ShapeDtypeStruct((8, width), F32),
            jax.ShapeDtypeStruct(shapes[0], BF16),
            jax.ShapeDtypeStruct(shapes[1], BF16),
        ],
        scratch_shapes=[
            pltpu.VMEM((rows, width), BF16),
            pltpu.VMEM((rows, width), BF16),
            pltpu.VMEM((width, rows), BF16),
            pltpu.VMEM((rows, width), F32),
            pltpu.VMEM((rows, width), F32),
        ]
        + [pltpu.VMEM((rows, lanes), BF16)] * 5
        + [pltpu.VMEM((lanes, rows), BF16)] * 4
        + [pltpu.VMEM((rows, lanes), F32)] * 3
        + reducer_scratch(MLP_LEVELS, shapes, teams, ring),
        compiler_params=pltpu.CompilerParams(
            collective_id=2, has_side_effects=True, vmem_limit_bytes=60 * MIB
        ),
        cost_estimate=pl.CostEstimate(
            flops=24 * rows * width * width + 8 * rows * rows * width,
            bytes_accessed=16 * width * width + 8 * rows * width,
            transcendentals=HEADS * rows * rows // 2,
        ),
        name="attend",
    )(order, x, g, norms, bias_q, *tables, weights, weights, weights, weights, up, down)


def rotary_tables(length):
    half = ROT // 2
    frequency = ROPE_BASE ** (-(np.arange(half) * 2.0 / ROT))
    angle = np.arange(length)[:, None] * frequency[None, :]
    cosine, sine = np.cos(angle), np.sin(angle)
    rest = np.zeros((length, HD - ROT))
    none = np.zeros_like(sine)
    cos_full = np.concatenate([cosine, cosine, rest + 1.0], axis=1)
    low = np.concatenate([-sine, none, rest], axis=1)
    high = np.concatenate([none, sine, rest], axis=1)
    return tuple(jnp.asarray(np.tile(t, (1, 2)).astype(np.float32)) for t in (cos_full, low, high))


def adamw(weight, grad, first, second, rate, decay):
    first_new = BETA_ONE * first + (1.0 - BETA_ONE) * grad
    second_new = BETA_TWO * second + (1.0 - BETA_TWO) * grad * grad
    first_hat = first_new / (1.0 - BETA_ONE**STEP)
    second_hat = second_new / (1.0 - BETA_TWO**STEP)
    weight_new = weight - rate * (first_hat / (jnp.sqrt(second_hat) + EPS_ADAM) + decay * weight)
    return (first_new, second_new, weight_new)


def shards(
    tokens, out_grad, block_order, qkv_weight, out_weight, up_weight, down_weight, norm_params, bias_params,
    qkv_first, qkv_second, out_first, out_second, up_first, up_second, down_first, down_second,
    norm_first, norm_second, bias_first, bias_second,
):
    groups, ring = lax.axis_size("dp"), lax.axis_size("ctx")
    group, rank = lax.axis_index("dp"), lax.axis_index("ctx")
    batch, piece, width = tokens.shape
    length = piece * ring
    count = batch * piece
    ff = up_weight.shape[1]

    share = bias_params.shape[0]
    lanes = share + -share % 128
    small = jnp.concatenate([
        jnp.pad(bias_params[None, :], ((0, 0), (0, lanes - share))),
        jnp.pad(norm_params, ((0, 3), (0, lanes - norm_params.shape[1]))),
    ])
    x_rows, g_rows = tokens.reshape(count, width), out_grad.reshape(count, width)
    att_copy, biases, norms, home_x, home_g, feed_out, h_feed, dup, ddown, dbias_up, small_feed = gather_feed(
        up_weight, down_weight, qkv_weight, out_weight, small, x_rows, g_rows, piece, ring * share
    )

    odd = group % 2

    order = block_order[jnp.clip(rank - odd, 0, batch - 1)]
    spots = jnp.arange(order.shape[0])
    order = jnp.stack([order, jnp.sum(jnp.where(order[None, :] == spots[:, None], spots[None, :], 0), axis=1)])

    attend_out, h_attend, dq, dk, dv, dout, dbias_q, small_attend, up_grad, down_grad = attend(
        order, home_x, home_g, norms, biases, rotary_tables(length), att_copy, dup, ddown
    )

    dqkv = jnp.concatenate([dq, dk, dv], axis=1)
    tail = jnp.concatenate(
        [small_attend[:2].reshape(-1), small_feed[:2].reshape(-1), dbias_q[0], small_feed[2], dbias_up[0], small_feed[2]]
    )
    entries = tail.shape[0]
    tail = jnp.pad(tail, (0, -entries % 1024)).reshape(-1, 128)
    *owned, tail, ret_mixed, ret_back = reduce_all((dqkv, dout), tail, attend_out, h_attend, batch)
    up_grad, down_grad, qkv_grad, out_grads = (
        g.reshape(w.shape).astype(F32)
        for g, w in zip((up_grad, down_grad, *owned), (up_weight, down_weight, qkv_weight, out_weight))
    )
    tail = tail.reshape(-1)[:entries]
    returned = [v.reshape(count, width).astype(F32) for v in (ret_mixed, ret_back)]

    rows = x_rows.astype(F32)
    bias_rows = biases[0:1, width : 2 * width] + biases[0:1, 2 * width + ff :]
    layer_out = (rows + returned[0] + feed_out + bias_rows).astype(BF16).reshape(batch, piece, width)
    xh, scale = normalized(rows)
    h = returned[1] + h_feed
    inner = jnp.mean(h * xh, axis=-1, keepdims=True)
    input_grad = g_rows.astype(F32) + scale * (h - jnp.mean(h, axis=-1, keepdims=True) - xh * inner)
    input_grad = input_grad.reshape(batch, piece, width)

    norm_grad = lax.dynamic_slice_in_dim(tail[: 4 * width].reshape(4, width), rank * (width // ring), width // ring, 1)
    bias_grad = lax.dynamic_slice_in_dim(tail[4 * width :], rank * share, share, 0)

    qkv_new = adamw(qkv_weight, qkv_grad, qkv_first, qkv_second, 0.1, DECAY)
    out_new = adamw(out_weight, out_grads, out_first, out_second, 0.6, DECAY)
    up_new = adamw(up_weight, up_grad, up_first, up_second, 0.1, DECAY)
    down_new = adamw(down_weight, down_grad, down_first, down_second, 0.05, DECAY)
    norm_new = adamw(norm_params, norm_grad, norm_first, norm_second, 0.6, 0.0)
    bias_new = adamw(bias_params, bias_grad, bias_first, bias_second, 0.6, 0.0)
    return (
        layer_out, input_grad, *qkv_new, *out_new, *up_new, *down_new,
        norm_new[0], norm_new[1][:2], norm_new[1][2:], norm_new[2], *bias_new,
    )


def solution(mesh):
    rows, columns, token = P("ctx", None), P(None, "ctx"), P("dp", "ctx", None)
    in_specs = (token, token, P("dp", None)) + (rows,) * 4 + (columns, P("ctx")) + (rows,) * 8
    in_specs += (columns, columns, P("ctx"), P("ctx"))
    out_specs = (token, token) + (rows,) * 12 + (columns,) * 4 + (P("ctx"),) * 3
    return jax.shard_map(shards, mesh=mesh, in_specs=in_specs, out_specs=out_specs, check_vma=False)
```

```python
import functools
import math

import jax
import jax.numpy as jnp
import numpy as np
from jax import lax
from jax.experimental import pallas as pl
from jax.experimental.pallas import tpu as pltpu
from jax.sharding import PartitionSpec as P

HEADS = 12
HD = 64
STEP = 10
ROT = 16
SEQS = 3
BLOCK = 128
QUAD = 4
LEVELS = (2, 1, 0, 0)

EPS_NORM = 1e-05
BETA_ONE = 0.9
BETA_TWO = 0.95
EPS_ADAM = 1e-08
DECAY = 0.01
ROPE_BASE = 10000.0
F32 = jnp.float32
BF16 = jnp.bfloat16
MIB = 1024 * 1024


def dot(left, right, dims=((1,), (0,))):
    return lax.dot_general(left, right, (dims, ((), ())), preferred_element_type=F32)


NN = ((1,), (0,))
NT = ((1,), (1,))
TN = ((0,), (0,))


def normalized(values):
    mean = jnp.mean(values, axis=-1, keepdims=True)
    centred = values - mean
    variance = jnp.mean(centred * centred, axis=-1, keepdims=True)
    scale = lax.rsqrt(variance + EPS_NORM)
    return centred * scale, scale


MESH = pl.DeviceIdType.MESH


def plane(d):
    core, x, y = d % 2, d // 2 % 2, d // 4 % 2
    return core, x, y, d + 1 - 2 * core, d + 2 - 4 * x, d + 4 - 8 * y


def gather_kernel(
    up, down, qkv, out, small, tokens, cotangents,
    att_all, small_all, norm_all, home_x, home_g, out_ref, h_ref, up_part, down_part, dbias_ref, sums_ref,
    up_all, down_all, att_own, up_wide, down_wide, att_wide, small_in, x_ref, g_ref, m_ref, mt_ref, hid_ref, dup_in_ref,
    dup_ref, up_core, up_first, ddown_ref, down_core,
    z_send, z_recv, p_send, p_recv, s_send, s_recv, t_send, t_recv, local, out_sem, c_send, c_recv,
):
    ring = lax.axis_size("ctx")
    d, z = lax.axis_index("dp"), lax.axis_index("ctx")
    core, x, y, core_id, x_id, y_id = plane(d)
    own = x + 2 * y
    own_x, own_y, far = own + 1 - 2 * x, own + 2 - 4 * y, 3 - own
    count, width = tokens.shape
    piece = home_x.shape[0] // ring
    batch = count // piece
    arrays = ((up_wide, up_all, False), (down_wide, down_all, True), (att_own, att_all, False))

    def slot(a, base, place, half=None):
        source, whole, tall = arrays[a]
        ref = source if base is None else whole
        rows, columns = source.shape
        at = 0 if base is None else base * rows
        height, span = rows // 4, columns // 2
        at = at + place * height
        column = core * span
        if half is not None:
            if tall:
                height = height // 2
                at = at + half * height
            else:
                span = span // 2
                column = column + half * span
        return ref.at[pl.ds(pl.multiple_of(at, 16), height), pl.ds(pl.multiple_of(column, 128), span)]

    def other_slot(a, base, place):
        source, whole, tall = arrays[a]
        rows, columns = source.shape
        at = pl.multiple_of(base * rows + place * (rows // 4), 16)
        column = pl.multiple_of((1 - core) * (columns // 2), 128)
        return whole.at[pl.ds(at, rows // 4), pl.ds(column, columns // 2)]

    def remote(src, dst, send, recv, dp, ctx):
        return pltpu.make_async_remote_copy(
            src_ref=src, dst_ref=dst, send_sem=send, recv_sem=recv, device_id=(dp, ctx), device_id_type=MESH
        )

    columns = qkv.shape[1]
    wide_loads = [
        [pltpu.make_async_copy(up, up_wide, local.at[0])],
        [pltpu.make_async_copy(down, down_wide, local.at[1])],
        [
            pltpu.make_async_copy(qkv, att_wide.at[:, pl.ds(0, columns)], local.at[2]),
            pltpu.make_async_copy(out, att_wide.at[:, pl.ds(columns, out.shape[1])], local.at[8]),
        ],
    ]
    for loads in wide_loads:
        for copy in loads:
            copy.start()

    def cast_own(a):
        for copy in wide_loads[a]:
            copy.wait()
        wide, target = ((up_wide, up_all), (down_wide, down_all), (att_wide, att_own))[a]
        rows = wide.shape[0]
        tile = 64
        base = 0 if a == 2 else z * rows

        def body(t, _):
            value = wide[pl.ds(pl.multiple_of(t * tile, 16), tile), :].astype(BF16)
            target[pl.ds(pl.multiple_of(base + t * tile, 16), tile), :] = value
            return 0

        lax.fori_loop(0, rows // tile, body, 0)

    barrier = pltpu.get_barrier_semaphore()
    for k in range(1, ring):
        pl.semaphore_signal(barrier, inc=1, device_id=(d, (z + k) % ring), device_id_type=MESH)
    for other in (core_id, x_id, y_id):
        pl.semaphore_signal(barrier, inc=1, device_id=(other, z), device_id_type=MESH)
    cast_own(0)
    pl.semaphore_wait(barrier, ring + 2)

    def hop(a, way, h):
        shard = z - h if way == 0 else z + h
        target = z + 1 if way == 0 else z - 1
        src = slot(a, None, own) if h == 0 and a == 2 else slot(a, shard, own)
        return remote(src, slot(a, shard, own), z_send.at[a, way, h], z_recv.at[a, way, h], d, target)

    def can_send(way, h):
        shard = z - h if way == 0 else z + h
        target = z + 1 if way == 0 else z - 1
        return (shard >= 0) & (shard < ring) & (target >= 0) & (target < ring)

    def in_range(way, h):
        shard = z - h if way == 0 else z + h
        return (shard >= 0) & (shard < ring)

    def cast(a, shard, j):
        send, recv = p_send.at[a, shard, j], p_recv.at[a, shard, j]
        if j == 0:
            ref = slot(a, shard, own)
            return remote(ref, ref, send, recv, x_id, z)
        if j == 1:
            ref = slot(a, shard, own)
            return remote(ref, ref, send, recv, y_id, z)
        if j == 2:
            ref = slot(a, shard, own_x, 0)
            return remote(ref, ref, send, recv, y_id, z)
        if j == 3:
            ref = slot(a, shard, own_y, 1)
            return remote(ref, ref, send, recv, x_id, z)
        ref = slot(a, shard, (own, own_x, own_y, far)[j - 4])
        return remote(ref, ref, send, recv, core_id, z)

    def arrived(a, shard, j):
        send, recv = p_send.at[a, shard, j], p_recv.at[a, shard, j]
        ref = {0: lambda: slot(a, shard, own_x), 1: lambda: slot(a, shard, own_y),
               2: lambda: slot(a, shard, far, 0), 3: lambda: slot(a, shard, far, 1)}.get(
            j, lambda: other_slot(a, shard, (own, own_x, own_y, far)[j - 4]))()
        remote(ref, ref, send, recv, core_id, z).wait_recv()

    def start_hops(a):
        for way in range(2):
            @pl.when(can_send(way, 0))
            def _(way=way):
                hop(a, way, 0).start()

    def small_copy(k):
        return remote(small, small_in.at[z], s_send.at[k], s_recv.at[k], d, (z + k) % ring)

    def stage_a(a, h):
        for way in range(2):
            @pl.when(in_range(way, h))
            def _(way=way):
                shard = z - h if way == 0 else z + h
                ref = slot(a, shard, own)
                remote(ref, ref, z_send.at[a, way, h - 1], z_recv.at[a, way, h - 1], core_id, z).wait_recv()

                @pl.when(can_send(way, h))
                def _():
                    hop(a, way, h).start()

                cast(a, shard, 0).start()
                cast(a, shard, 1).start()
                cast(a, shard, 4).start()

    def stage_b(a, h):
        for way in range(2):
            @pl.when(in_range(way, h))
            def _(way=way):
                shard = z - h if way == 0 else z + h
                arrived(a, shard, 0)
                cast(a, shard, 2).start()
                cast(a, shard, 5).start()
                arrived(a, shard, 1)
                cast(a, shard, 3).start()
                cast(a, shard, 6).start()

    def stage_c(a, h):
        for way in range(2):
            @pl.when(in_range(way, h))
            def _(way=way):
                shard = z - h if way == 0 else z + h
                arrived(a, shard, 2)
                arrived(a, shard, 3)
                cast(a, shard, 7).start()

    def stage_d(a, h):
        for way in range(2):
            @pl.when(in_range(way, h))
            def _(way=way):
                shard = z - h if way == 0 else z + h
                for j in range(4, 8):
                    arrived(a, shard, j)

    pairs = ((tokens, home_x), (cotangents, home_g))

    def move(which, i):
        source, whole = pairs[which]
        src = source.at[pl.ds(i * piece, piece), :]
        dst = whole.at[pl.ds(pl.multiple_of(z * piece, 16), piece), :]
        return src, dst, i + core

    def start_moves(which):
        for i in range(batch):
            src, dst, target = move(which, i)

            @pl.when(target != z)
            def _(src=src, dst=dst, target=target, i=i):
                remote(src, dst, t_send.at[which, i], t_recv.at[which, z], d, target).start()

            @pl.when(target == z)
            def _(src=src, dst=dst):
                pltpu.make_async_copy(src, dst, local.at[6 + which]).start()

    own_rows = pl.ds(pl.multiple_of(z * att_own.shape[0], 16), att_own.shape[0])
    own_att = pltpu.make_async_copy(att_own, att_all.at[own_rows, :], local.at[9])
    x_load = pltpu.make_async_copy(tokens, x_ref, local.at[3])
    g_load = pltpu.make_async_copy(cotangents, g_ref, local.at[4])
    own_small = pltpu.make_async_copy(small, small_in.at[z], local.at[5])

    start_hops(0)
    cast_own(1)
    start_hops(1)
    cast_own(2)
    start_hops(2)
    for k in range(1, ring):
        small_copy(k).start()
    for copy in (own_att, x_load, g_load, own_small):
        copy.start()
    hops = range(1, ring)
    work = [(a, h) for a in range(3) for h in hops]
    early = 2 * (ring - 1)
    for n in range(len(work)):
        stage_a(*work[n])
        if 1 <= n <= early:
            stage_b(*work[n - 1])
        if 2 <= n <= early + 1:
            stage_c(*work[n - 2])
    start_moves(0)
    start_moves(1)

    own_small.wait()
    for k in range(1, ring):
        ref = small_in.at[(z + ring - k) % ring]
        remote(ref, ref, s_send.at[k], s_recv.at[k], core_id, z).wait_recv()
    x_load.wait()
    g_load.wait()
    entries = small_all.shape[1]
    biases = jnp.zeros((8, entries), F32)
    norms = jnp.zeros((8, width), F32)
    for r in range(ring):
        block = small_in[r].astype(BF16).astype(F32)
        full = jnp.concatenate([block, jnp.zeros((8, entries - block.shape[1]), F32)], axis=1)
        biases += pltpu.roll(full, r * (entries // ring), 1) if r else full
        norms += pltpu.roll(block[:, :width], r * (width // ring), 1) if r else block[:, :width]
    small_all[...] = biases
    norm_all[...] = norms
    ff = up_all.shape[1]
    gain_2, shift_2 = norm_all[3:4, :], norm_all[4:5, :]
    tile = 256
    tiles = count // tile
    for t in range(tiles):
        at = pl.ds(t * tile, tile)
        xh, _ = normalized(x_ref[at, :].astype(F32))
        m = xh * gain_2 + shift_2
        m_ref[at, :] = m.astype(BF16)
        mt_ref[:, at] = m.T.astype(BF16)
        out_ref[at, :] = jnp.zeros((tile, width), F32)
        h_ref[at, :] = jnp.zeros((tile, width), F32)
    for h in hops:
        stage_d(0, h)
        stage_d(1, h)

    strip = dup_ref.shape[3] // ring
    steps = ff // (ring * strip)
    half = ring // 2
    big, by_core = (dup_ref, ddown_ref), (up_core, down_core)
    bits, ids = ((x, y), (y, x)), ((x_id, y_id), (y_id, x_id))

    def sizes(a):
        return by_core[a].shape[2], by_core[a].shape[3]

    def slice_of(order):
        return 2 * bits[order][0] + bits[order][1]

    def core_copy(a, i):
        _, span = sizes(a)
        away = pl.ds(pl.multiple_of((1 - core) * span, 128), span)
        return remote(big[a].at[i, :, :, away], by_core[a].at[i], c_send.at[a, i, 0], c_recv.at[a, i, 0], core_id, z)

    def first_copy(a, i, order):
        height, _ = sizes(a)
        own = pl.ds(order * half, half)
        away = pl.ds(pl.multiple_of((1 - bits[order][0]) * (height // 2), 16), height // 2)
        return remote(
            by_core[a].at[i, own, away, :], up_first.at[i, own], c_send.at[a, i, 1 + order],
            c_recv.at[a, i, 1 + order], ids[order][0], z,
        )

    def add(into, at, term, owners):
        height = term(0).shape[0]
        tile = 32 if height % 48 else 48

        def body(n, _):
            o, t = n // (height // tile), n % (height // tile)
            spot = pl.ds(pl.multiple_of(at + t * tile, 16), tile)
            value = term(o)[pl.ds(pl.multiple_of(t * tile, 16), tile), :]
            into[o, spot, :] = (into[o, spot, :].astype(F32) + value.astype(F32)).astype(BF16)
            return 0

        lax.fori_loop(0, owners * (height // tile), body, 0)

    def chunk_1(i):
        for a in range(2):
            _, span = sizes(a)
            core_copy(a, i).wait_recv()
            keep = pl.ds(pl.multiple_of(core * span, 128), span)
            add(by_core[a].at[i], 0, lambda o: big[a].at[i, o, :, keep], ring)
        for order in range(2):
            first_copy(0, i, order).start()
        parts_out(1, i)[0].start()

    def chunk_2(i):
        height, _ = sizes(0)
        for order in range(2):
            own = pl.ds(order * half, half)
            first_copy(0, i, order).wait_recv()
            at = bits[order][0] * (height // 2)
            add(by_core[0].at[i, own], at, lambda o: up_first.at[i, order * half + o], half)
        for copy in parts_out(0, i):
            copy.start()

    def parts_out(a, i):
        height, span = sizes(a)
        if a == 1:
            return [pltpu.make_async_copy(by_core[1].at[i], down_part.at[:, i], out_sem.at[i, 2 * half])]
        copies = []
        for order in range(2):
            own = pl.ds(order * half, half)
            rows = pl.ds(pl.multiple_of(bits[order][0] * (height // 2), 16), height // 2)
            for n in range(half):
                copies.append(pltpu.make_async_copy(
                    by_core[0].at[i, own, rows, pl.ds(n * strip, strip)],
                    up_part.at[own, :, pl.ds(pl.multiple_of(n * steps * strip + i * strip, 128), strip)],
                    out_sem.at[i, half * order + n],
                ))
        return copies

    def feed_step(step, _):
        for h in hops:
            @pl.when(step == h - 1)
            def _(h=h):
                stage_b(2, h)

            @pl.when(step == h)
            def _(h=h):
                stage_c(2, h)

        @pl.when(step < steps)
        def _():
            spots = [pl.ds(pl.multiple_of(r * (ff // ring) + step * strip, 128), strip) for r in range(ring)]
            bias_spots = [
                pl.ds(pl.multiple_of(2 * width + r * (ff // ring) + step * strip, 128), strip) for r in range(ring)
            ]
            up_part_ = jnp.concatenate([up_all[:, at] for at in spots], axis=1)
            down_part_ = jnp.concatenate([down_all[at, :] for at in spots], axis=0)
            bias = jnp.concatenate([small_all[0:1, at] for at in bias_spots], axis=1)
            total = jnp.zeros((1, ring * strip), F32)
            for t in range(tiles):
                at = pl.ds(t * tile, tile)
                u = dot(m_ref[at, :], up_part_) + bias
                cdf = 0.5 * (1.0 + lax.erf(u * (1.0 / math.sqrt(2.0))))
                hidden = (u * cdf).astype(BF16)
                slope = cdf + u * jnp.exp(-0.5 * u * u) * (1.0 / math.sqrt(2.0 * math.pi))
                back = (dot(g_ref[at, :], down_part_, NT) * slope).astype(BF16)
                hid_ref[at, :] = hidden
                dup_in_ref[at, :] = back
                total += jnp.sum(back.astype(F32), axis=0, keepdims=True)
                out_ref[at, :] += dot(hidden, down_part_)
                h_ref[at, :] += dot(back, up_part_, NT)
            for r in range(ring):
                dbias_ref[0:1, spots[r]] = total[:, r * strip : (r + 1) * strip]
            ddown = dot(hid_ref[...], g_ref[...], TN).astype(BF16)
            dup = dot(mt_ref[...], dup_in_ref[...]).astype(BF16)
            for r in range(ring):
                ddown_ref[step, r] = ddown[r * strip : (r + 1) * strip, :]
                dup_ref[step, r] = dup[r * (width // ring) : (r + 1) * (width // ring), :]
            core_copy(0, step).start()
            core_copy(1, step).start()

        for lag, stage in ((1, chunk_1), (3, chunk_2)):
            @pl.when((step >= lag) & (step < steps + lag))
            def _(lag=lag, stage=stage):
                stage(step - lag)

        return 0

    lax.fori_loop(0, steps + 3, feed_step, 0)

    gain = jnp.zeros((1, width), F32)
    shift = jnp.zeros((1, width), F32)
    sums = jnp.zeros((1, width), F32)
    for t in range(tiles):
        at = pl.ds(t * tile, tile)
        xh, _ = normalized(x_ref[at, :].astype(F32))
        dm = h_ref[at, :]
        gain += jnp.sum(dm * xh, axis=0, keepdims=True)
        shift += jnp.sum(dm, axis=0, keepdims=True)
        sums += jnp.sum(g_ref[at, :].astype(F32), axis=0, keepdims=True)
        h_ref[at, :] = dm * gain_2
    sums_ref[...] = jnp.concatenate([gain, shift, sums, jnp.zeros((5, width), F32)], axis=0)

    mine = z - core
    for which in range(2):
        for k in range(1, ring):
            @pl.when((mine >= 0) & (mine < batch))
            def _(which=which, k=k):
                other = (z + k) % ring
                ref = pairs[which][1].at[pl.ds(pl.multiple_of(other * piece, 16), piece), :]
                remote(ref, ref, t_send.at[which, 0], t_recv.at[which, other], core_id, z).wait_recv()
    for h in hops:
        stage_d(2, h)
    for k in range(1, ring):
        small_copy(k).wait_send()
    for a in range(3):
        for way in range(2):
            for h in range(ring - 1):
                @pl.when(can_send(way, h))
                def _(a=a, way=way, h=h):
                    hop(a, way, h).wait_send()
        for h in hops:
            for way in range(2):
                @pl.when(in_range(way, h))
                def _(a=a, h=h, way=way):
                    shard = z - h if way == 0 else z + h
                    for j in range(8):
                        cast(a, shard, j).wait_send()
    for which in range(2):
        for i in range(batch):
            src, dst, target = move(which, i)

            @pl.when(target != z)
            def _(src=src, dst=dst, target=target, which=which, i=i):
                remote(src, dst, t_send.at[which, i], t_recv.at[which, z], d, target).wait_send()

            @pl.when(target == z)
            def _(src=src, dst=dst, which=which):
                pltpu.make_async_copy(src, dst, local.at[6 + which]).wait()
    own_att.wait()

    def close(i, _):
        for a in range(2):
            core_copy(a, i).wait_send()
            for copy in parts_out(a, i):
                copy.wait()
        for order in range(2):
            first_copy(0, i, order).wait_send()
        return 0

    lax.fori_loop(0, steps, close, 0)


def gather_feed(up, down, qkv, out, small, tokens, cotangents, piece, entries):
    ring = lax.axis_size("ctx")
    count, width = tokens.shape
    ff = up.shape[1]
    strip = 128
    chunk = ring * strip
    steps = ff // chunk
    shard = up.shape[0]
    columns = qkv.shape[1] + out.shape[1]
    home = jax.ShapeDtypeStruct((ring * piece, width), tokens.dtype)
    rows = jax.ShapeDtypeStruct((count, width), F32)
    dma = pltpu.SemaphoreType.DMA
    anywhere = pl.BlockSpec(memory_space=pl.ANY)
    vmem = pl.BlockSpec(memory_space=pltpu.VMEM)
    return pl.pallas_call(
        gather_kernel,
        in_specs=[anywhere] * 7,
        out_specs=[anywhere, vmem, vmem, anywhere, anywhere, vmem, vmem, anywhere, anywhere, vmem, vmem],
        out_shape=[
            jax.ShapeDtypeStruct((ring * shard, columns), BF16),
            jax.ShapeDtypeStruct((8, entries), F32), jax.ShapeDtypeStruct((8, width), F32), home, home, rows, rows,
            jax.ShapeDtypeStruct((ring, shard // 2, ff // 2), BF16),
            jax.ShapeDtypeStruct((ring, steps, strip, width // 2), BF16),
            jax.ShapeDtypeStruct((8, ff), F32), jax.ShapeDtypeStruct((8, width), F32),
        ],
        scratch_shapes=[
            pltpu.VMEM((ring * shard, ff), BF16), pltpu.VMEM((ring * down.shape[0], width), BF16),
            pltpu.VMEM((shard, columns), BF16),
            pltpu.VMEM(up.shape, F32), pltpu.VMEM(down.shape, F32), pltpu.VMEM((shard, columns), F32),
            pltpu.VMEM((ring, *small.shape), F32),
            pltpu.VMEM((count, width), BF16), pltpu.VMEM((count, width), BF16), pltpu.VMEM((count, width), BF16),
            pltpu.VMEM((width, count), BF16),
            pltpu.VMEM((count, chunk), BF16), pltpu.VMEM((count, chunk), BF16),
            pltpu.VMEM((steps, ring, shard, chunk), BF16), pltpu.VMEM((steps, ring, shard, chunk // 2), BF16),
            pltpu.VMEM((steps, ring, shard // 2, chunk // 2), BF16),
            pltpu.VMEM((steps, ring, strip, width), BF16), pltpu.VMEM((steps, ring, strip, width // 2), BF16),
            dma((3, 2, ring)), dma((3, 2, ring)), dma((3, ring, 8)), dma((3, ring, 8)),
            dma((ring,)), dma((ring,)), dma((2, count // piece)), dma((2, ring)), dma((10,)), dma((steps, ring + 1)),
            dma((2, steps, 3)), dma((2, steps, 3)),
        ],
        compiler_params=pltpu.CompilerParams(
            collective_id=0, has_side_effects=True, vmem_limit_bytes=60 * MIB
        ),
        cost_estimate=pl.CostEstimate(
            flops=12 * count * width * ff, bytes_accessed=60 * MIB, transcendentals=count * ff
        ),
        name="gather_feed",
    )(up, down, qkv, out, small, tokens, cotangents)


def remote(src, dst, send_sem, recv_sem, dp, ctx):
    return pltpu.make_async_remote_copy(
        src_ref=src, dst_ref=dst, send_sem=send_sem, recv_sem=recv_sem, device_id=(dp, ctx), device_id_type=MESH
    )


def team_id(d, t):
    return d + (8 << t) * (1 - 2 * (d // (8 << t) % 2))


def greet(teams):
    ring = lax.axis_size("ctx")
    d, z = lax.axis_index("dp"), lax.axis_index("ctx")
    core, x, y, core_id, x_id, y_id = plane(d)
    barrier = pltpu.get_barrier_semaphore()
    partners = [core_id, x_id, y_id, x_id + y_id - d] + [team_id(d, t) for t in range(teams)]
    for k in range(1, ring):
        pl.semaphore_signal(barrier, inc=1, device_id=(d, (z + k) % ring), device_id_type=MESH)
    for other in partners:
        pl.semaphore_signal(barrier, inc=1, device_id=(other, z), device_id_type=MESH)
    pl.semaphore_wait(barrier, ring - 1 + len(partners))


def reducer(teams, levels, ins, sums, bufs, send, recv, load):
    count = len(ins)
    ring = lax.axis_size("ctx")
    d, z = lax.axis_index("dp"), lax.axis_index("ctx")
    core, x, y, core_id, x_id, y_id = plane(d)
    far_id = x_id + y_id - d
    bits, ids = ((x, y), (y, x)), ((x_id, y_id), (y_id, x_id))
    spots = ((x, y), (1 - x, y), (x, 1 - y), (1 - x, 1 - y))

    def sizes(a):
        _, strips, quarter, span = bufs[a][-1].shape
        return strips, quarter, span

    def owners(a, order):
        strips = sizes(a)[0]
        return pl.ds(order * ring // 2 * strips, ring // 2 * strips)

    def rows_at(at, height):
        return pl.ds(pl.multiple_of(at, 16), height)

    def kept(a, order):
        return 0 if levels[a] == 2 else bits[order][0] * 2 * sizes(a)[1]

    def core_copy(a):
        span = sizes(a)[2]
        away = pl.ds(pl.multiple_of((1 - core) * span, 128), span)
        return remote(ins[a].at[:, :, away], bufs[a][1], send.at[a, 0], recv.at[a, 0], core_id, z)

    def own_load(a):
        span = sizes(a)[2]
        keep = pl.ds(pl.multiple_of(core * span, 128), span)
        src = ins[a].at[:, :, keep] if levels[a] == 0 else ins[a]
        return pltpu.make_async_copy(src, bufs[a][0], load.at[a])

    def first_copy(a, order):
        quarter = sizes(a)[1]
        away = rows_at((1 - bits[order][0]) * 2 * quarter, 2 * quarter)
        return remote(
            bufs[a][0].at[owners(a, order), away, :], bufs[a][2].at[owners(a, order)], send.at[a, 1 + order],
            recv.at[a, 1 + order], ids[order][0], z,
        )

    def second_copy(a, order):
        quarter = sizes(a)[1]
        away = rows_at(kept(a, order) + (1 - bits[order][1]) * quarter, quarter)
        return remote(
            bufs[a][0].at[owners(a, order), away, :], bufs[a][3].at[owners(a, order)], send.at[a, 3 + order],
            recv.at[a, 3 + order], ids[order][1], z,
        )

    def own_quarter(a, owner):
        strips, quarter, _ = sizes(a)
        order = owner // (ring // 2)
        first, second = (1 - order) * x + order * y, (1 - order) * y + order * x
        at = second * quarter if levels[a] == 2 else (2 * first + second) * quarter
        return bufs[a][0].at[pl.ds(owner * strips, strips), rows_at(at, quarter), :]

    def owner_copy(a, k):
        to = (z + k) % ring
        return remote(own_quarter(a, to), bufs[a][4].at[k - 1], send.at[a, 4 + k], recv.at[a, 4 + k], d, to)

    def team_copy(a, t):
        j = 4 + ring + 7 + t
        return remote(bufs[a][5].at[0], bufs[a][5].at[1 + t], send.at[a, j], recv.at[a, j], team_id(d, t), z)

    def final(a, spot, side):
        strips, quarter, span = sizes(a)
        order = z // (ring // 2)
        xx, yy = spots[spot]
        at = ((1 - order) * (2 * xx + yy) + order * (2 * yy + xx)) * quarter
        return sums[a].at[:, rows_at(at, quarter), pl.ds(pl.multiple_of(side * span, 128), span)]

    def spread(a, j):
        s, r = send.at[a, 4 + ring + j - 1], recv.at[a, 4 + ring + j - 1]
        if j < 4:
            return remote(bufs[a][5].at[0], final(a, 0, core), s, r, (x_id, y_id, far_id)[j - 1], z)
        src = bufs[a][5].at[0] if j == 4 else final(a, j - 4, core)
        return remote(src, final(a, j - 4, core), s, r, core_id, z)

    def spread_here(a, j):
        s, r = send.at[a, 4 + ring + j - 1], recv.at[a, 4 + ring + j - 1]
        ref = final(a, j, core) if j < 4 else final(a, j - 4, 1 - core)
        remote(ref, ref, s, r, core_id, z).wait_recv()

    def keep_own(a):
        return pltpu.make_async_copy(bufs[a][5].at[0], final(a, 0, core), load.at[count + a])

    def add(into, at, term, blocks):
        height = term.shape[1]
        tile = 32 if height % 48 else 48

        def body(n, _):
            o, t = n // (height // tile), n % (height // tile)
            spot = rows_at(at + t * tile, tile)
            value = term[o, rows_at(t * tile, tile), :]
            into[o, spot, :] = (into[o, spot, :].astype(F32) + value.astype(F32)).astype(BF16)
            return 0

        lax.fori_loop(0, blocks * (height // tile), body, 0)

    def enter(a):
        if levels[a] == 0:
            core_copy(a).start()
        own_load(a).start()

    def first(a):
        own_load(a).wait()
        if levels[a] == 0:
            core_copy(a).wait_recv()
            add(bufs[a][0], 0, bufs[a][1], bufs[a][0].shape[0])
        if levels[a] < 2:
            for order in range(2):
                first_copy(a, order).start()

    def second(a):
        for order in range(2):
            if levels[a] < 2:
                first_copy(a, order).wait_recv()
                own = owners(a, order)
                add(bufs[a][0].at[own], kept(a, order), bufs[a][2].at[own], ring // 2 * sizes(a)[0])
            second_copy(a, order).start()

    def to_owner(a):
        for order in range(2):
            second_copy(a, order).wait_recv()
            own = owners(a, order)
            at = kept(a, order) + bits[order][1] * sizes(a)[1]
            add(bufs[a][0].at[own], at, bufs[a][3].at[own], ring // 2 * sizes(a)[0])
        for k in range(1, ring):
            owner_copy(a, k).start()

    def total(a):
        for k in range(1, ring):
            owner_copy(a, k).wait_recv()
        mine = own_quarter(a, z)
        for s in range(sizes(a)[0]):
            terms = [mine[s]] + [bufs[a][4][k, s] for k in range(ring - 1)]
            bufs[a][5][0, s] = sum((t.astype(F32) for t in terms[1:]), terms[0].astype(F32)).astype(BF16)
        for t in range(teams):
            team_copy(a, t).start()
            team_copy(a, t).wait()
            bufs[a][5][0] = (bufs[a][5][0].astype(F32) + bufs[a][5][1 + t].astype(F32)).astype(BF16)
        keep_own(a).start()
        for j in range(1, 5):
            spread(a, j).start()

    def share(a):
        for j in range(1, 4):
            spread_here(a, j)
            spread(a, 4 + j).start()

    def close(a):
        for j in range(4, 8):
            spread_here(a, j)
        if levels[a] == 0:
            core_copy(a).wait_send()
        for order in range(2):
            if levels[a] < 2:
                first_copy(a, order).wait_send()
            second_copy(a, order).wait_send()
        for k in range(1, ring):
            owner_copy(a, k).wait_send()
        for j in range(1, 8):
            spread(a, j).wait_send()
        keep_own(a).wait()

    return enter, first, second, to_owner, total, share, close


def reducer_scratch(levels, shapes, teams, ring):
    scratch = []
    for level, (strips, rows, columns) in zip(levels, shapes):
        blocks, span = ring * strips, columns // 2
        none = (1, 16, 128)
        scratch += [
            pltpu.VMEM((blocks, rows // 2 if level == 2 else rows, span), BF16),
            pltpu.VMEM((blocks, rows, span) if level == 0 else none, BF16),
            pltpu.VMEM((blocks, rows // 2, span) if level < 2 else none, BF16),
            pltpu.VMEM((blocks, rows // 4, span), BF16),
            pltpu.VMEM((ring - 1, strips, rows // 4, span), BF16),
            pltpu.VMEM((1 + teams, strips, rows // 4, span), BF16),
        ]
    copies = 4 + ring + 7 + teams
    dma = pltpu.SemaphoreType.DMA
    return scratch + [dma((len(levels), copies)), dma((len(levels), copies)), dma((2 * len(levels),))]


def reduce_kernel(count, teams, *refs):
    ring = lax.axis_size("ctx")
    d, z = lax.axis_index("dp"), lax.axis_index("ctx")
    core, x, y, core_id, x_id, y_id = plane(d)
    grads, (small, mixed, back) = refs[:count], refs[count : count + 3]
    refs = refs[count + 3 :]
    sums, (small_out, ret_mixed, ret_back) = refs[:count], refs[count : count + 3]
    refs = refs[count + 3 :]
    bufs = [refs[6 * a : 6 * a + 6] for a in range(count)]
    send, recv, load, small_acc, small_in, s_send, s_recv, r_send, r_recv, r_local = refs[6 * count :]
    batch, piece = ret_mixed.shape[:2]
    greet(teams)
    stages = reducer(teams, LEVELS, grads, sums, bufs, send, recv, load)

    def returned(which, i, to):
        source, target = ((mixed, ret_mixed), (back, ret_back))[which]
        return source.at[pl.ds(pl.multiple_of(to * piece, 16), piece), :], target.at[i]

    mine = z - core
    is_home = (mine >= 0) & (mine < batch)

    def start_returns():
        for which in range(2):
            for i in range(batch):
                @pl.when(mine == i)
                def _(which=which, i=i):
                    for k in range(1, ring):
                        to = (z + k) % ring
                        src, dst = returned(which, i, to)
                        remote(src, dst, r_send.at[which, k], r_recv.at[which, i], d, to).start()
                    src, dst = returned(which, i, z)
                    pltpu.make_async_copy(src, dst, r_local.at[which]).start()

    def wait_returns():
        for which in range(2):
            for i in range(batch):
                src, dst = returned(which, i, z)

                @pl.when(mine == i)
                def _(which=which, i=i, src=src, dst=dst):
                    for k in range(1, ring):
                        to = (z + k) % ring
                        remote(*returned(which, i, to), r_send.at[which, k], r_recv.at[which, i], d, to).wait_send()
                    pltpu.make_async_copy(src, dst, r_local.at[which]).wait()

                @pl.when(mine != i)
                def _(which=which, i=i, src=src, dst=dst):
                    remote(src, dst, r_send.at[which, 0], r_recv.at[which, i], core_id, z).wait_recv()

    steps = [core_id, x_id, y_id] + [team_id(d, t) for t in range(teams)]

    def small_copy(n):
        return remote(small_acc, small_in.at[n], s_send.at[n], s_recv.at[n], steps[n], z)

    def small_owner(k):
        n = len(steps) + k - 1
        return remote(small_acc, small_in.at[n], s_send.at[n], s_recv.at[n], d, (z + k) % ring)

    def small_step(n):
        if n < len(steps):
            if n == 0:
                small_acc[...] = small[...]
            small_copy(n).start()
        elif n == len(steps):
            for k in range(1, ring):
                small_owner(k).start()

    def small_close(n):
        if n < len(steps):
            small_copy(n).wait()
            small_acc[...] += small_in[n]
        elif n == len(steps):
            for k in range(1, ring):
                small_owner(k).wait()
            total = small_acc[...]
            for k in range(ring - 1):
                total += small_in[len(steps) + k]
            small_out[...] = total

    for a in range(count):
        stages[0](a)
    start_returns()
    for n in range(1, max(len(stages), len(steps) + 2)):
        small_step(n - 1)
        if n < len(stages):
            for a in range(count):
                stages[n](a)
        small_close(n - 1)
    wait_returns()


def reduce_all(grads, small, mixed, back, batch):
    ring, groups = lax.axis_size("ctx"), lax.axis_size("dp")
    teams = (groups // 8).bit_length() - 1
    count = len(grads)
    up, down, qkv, out = grads
    shapes = [(1, 2 * up.shape[1], 2 * up.shape[2]), (down.shape[1], down.shape[2], 2 * down.shape[3])]
    shapes += [(1, g.shape[0] // ring, g.shape[1]) for g in (qkv, out)]
    grads = [up, down.reshape(-1, *down.shape[2:])] + [g.reshape(ring, -1, g.shape[1]) for g in (qkv, out)]
    length, width = mixed.shape
    dma = pltpu.SemaphoreType.DMA
    anywhere = pl.BlockSpec(memory_space=pl.ANY)
    vmem = pl.BlockSpec(memory_space=pltpu.VMEM)
    rounds = 3 + teams + ring - 1
    scratch = reducer_scratch(LEVELS, shapes, teams, ring)
    scratch += [
        pltpu.VMEM(small.shape, F32), pltpu.VMEM((rounds, *small.shape), F32), dma((rounds,)), dma((rounds,)),
        dma((2, ring)), dma((2, batch)), dma((2,)),
    ]
    token = jax.ShapeDtypeStruct((batch, length // ring, width), BF16)
    return pl.pallas_call(
        functools.partial(reduce_kernel, count, teams),
        in_specs=[anywhere] * count + [vmem, anywhere, anywhere],
        out_specs=[anywhere] * count + [vmem, anywhere, anywhere],
        out_shape=[jax.ShapeDtypeStruct(shape, BF16) for shape in shapes]
        + [jax.ShapeDtypeStruct(small.shape, F32), token, token],
        scratch_shapes=scratch,
        compiler_params=pltpu.CompilerParams(collective_id=1, has_side_effects=True, vmem_limit_bytes=56 * MIB),
        cost_estimate=pl.CostEstimate(flops=0, bytes_accessed=60 * MIB, transcendentals=0),
        name="reduce",
    )(*grads, small, mixed, back)


def attend_kernel(
    order_ref, x_ref, stored_g_ref, norm_ref, bias_ref, cos_ref, low_ref, high_ref, wq_ref, wk_ref, wv_ref, wo_ref,
    out_ref, h_ref, dq_ref, dk_ref, dv_ref, dwo_ref, dbias_ref, small_ref,
    g_ref, a_ref, at_ref, acc_ref, da_ref, q_ref, k_ref, v_ref, do_ref, o_ref, kt_ref, vt_ref, dot_ref, ot_ref,
    dqs_ref, dks_ref, dvs_ref,
):
    step = pl.program_id(0)
    last = pl.num_programs(0) - 1
    rows, width = x_ref.shape
    lanes = QUAD * HD
    tile = 256
    half = ROT // 2
    scale = 1.0 / math.sqrt(HD)
    blocks = rows // BLOCK
    mine = lax.axis_index("ctx") - lax.axis_index("dp") % 2
    is_home = (mine >= 0) & (mine < SEQS)

    def stored(ref, at):
        values = ref[pl.ds(at * BLOCK, BLOCK), :]
        return jnp.where(is_home, values, jnp.zeros_like(values))

    @pl.when(step == 0)
    def _():
        for j in range(blocks):
            place = order_ref[1, j]
            at = pl.ds(j * BLOCK, BLOCK)
            xh, _ = normalized(stored(x_ref, place).astype(F32))
            a = xh * norm_ref[1:2, :] + norm_ref[2:3, :]
            a_ref[at, :] = a.astype(BF16)
            at_ref[:, at] = a.T.astype(BF16)
            g_ref[at, :] = stored(stored_g_ref, place)
        acc_ref[...] = jnp.zeros_like(acc_ref)
        da_ref[...] = jnp.zeros_like(da_ref)

    def table(ref, at):
        values = ref[at, :]
        return jnp.concatenate([values] * (lanes // values.shape[1]), axis=1)

    def turn(values, at):
        low = pltpu.roll(values, lanes - half, 1) * table(low_ref, at)
        high = pltpu.roll(values, half, 1) * table(high_ref, at)
        return values * table(cos_ref, at), low + high

    for t in range(rows // tile):
        at = pl.ds(t * tile, tile)
        a = a_ref[at, :]
        same, cross = turn(dot(a, wq_ref[...]) + bias_ref[0:1, :], at)
        q_ref[at, :] = ((same + cross).astype(BF16) * scale).astype(BF16)
        same, cross = turn(dot(a, wk_ref[...]), at)
        keys = same + cross
        k_ref[at, :] = keys.astype(BF16)
        kt_ref[:, at] = keys.T.astype(BF16)
        values = dot(a, wv_ref[...])
        v_ref[at, :] = values.astype(BF16)
        vt_ref[:, at] = values.T.astype(BF16)
        mixed_back = dot(g_ref[at, :], wo_ref[...], NT)
        do_ref[at, :] = mixed_back.astype(BF16)
        dot_ref[:, at] = mixed_back.T.astype(BF16)

    dks_ref[...] = jnp.zeros_like(dks_ref)
    dvs_ref[...] = jnp.zeros_like(dvs_ref)
    wide = 2 * HD
    head_of = lax.broadcasted_iota(jnp.int32, (BLOCK, wide), 1) // HD

    def stack(values):
        zero = jnp.zeros_like(values)
        return jnp.concatenate([jnp.where(head_of == e, values, zero) for e in range(2)], axis=0)

    def diagonal(values):
        return jnp.concatenate([values[e * HD : (e + 1) * HD, e * BLOCK : (e + 1) * BLOCK] for e in range(2)], axis=0)

    spot = lax.broadcasted_iota(jnp.int32, (BLOCK, 2 * BLOCK), 1) % BLOCK
    admitted = lax.broadcasted_iota(jnp.int32, (BLOCK, 2 * BLOCK), 0) <= spot

    def products_in(b, p):
        at, seen, own = pl.ds(b * BLOCK, BLOCK), pl.ds(0, (b + 1) * BLOCK), pl.ds(p * wide, wide)
        q, do = stack(q_ref[at, own]), stack(do_ref[at, own])
        return q, do, dot(k_ref[seen, own], q, NT), dot(v_ref[seen, own], do, NT)

    def softmax(b, scores, back):
        edge = jnp.where(admitted, scores[b * BLOCK :], -1e30)
        scores = edge if b == 0 else jnp.concatenate([scores[: b * BLOCK], edge], axis=0)
        top = jnp.max(scores, axis=0, keepdims=True)
        expo = jnp.exp(scores - top)
        probs = expo * (1.0 / jnp.sum(expo, axis=0, keepdims=True))
        share = jnp.sum(probs * back, axis=0, keepdims=True)
        return probs.astype(BF16), (probs * (back - share)).astype(BF16)

    def products_out(b, p, q, do, low, back):
        at, seen, own = pl.ds(b * BLOCK, BLOCK), pl.ds(0, (b + 1) * BLOCK), pl.ds(p * wide, wide)
        mixed = diagonal(dot(vt_ref[own, seen], low))
        ot_ref[own, at] = mixed.astype(BF16)
        o_ref[at, own] = mixed.T.astype(BF16)
        dqs_ref[at, own] = diagonal(dot(kt_ref[own, seen], back)).T * scale
        dks_ref[seen, own] += dot(back, q)
        dvs_ref[seen, own] += dot(low, do)

    units = [(b, p) for b in range(rows // BLOCK) for p in range(lanes // wide)]
    ready = products_in(*units[0])
    done = None
    for n, (b, p) in enumerate(units):
        q, do, scores, back = ready
        if n + 1 < len(units):
            ready = products_in(*units[n + 1])
        low, back = softmax(b, scores, back)
        if done is not None:
            products_out(*done)
        done = (b, p, q, do, low, back)
    products_out(*done)

    total = jnp.zeros((1, lanes), F32)
    for t in range(rows // tile):
        at = pl.ds(t * tile, tile)
        same, cross = turn(dqs_ref[at, :], at)
        dq = (same - cross).astype(BF16)
        same, cross = turn(dks_ref[at, :], at)
        dk = (same - cross).astype(BF16)
        dv = dvs_ref[at, :].astype(BF16)
        total += jnp.sum(dq.astype(F32), axis=0, keepdims=True)
        q_ref[at, :] = dq
        k_ref[at, :] = dk
        v_ref[at, :] = dv
        acc_ref[at, :] += dot(o_ref[at, :], wo_ref[...])
        da_ref[at, :] += dot(dq, wq_ref[...], NT) + dot(dk, wk_ref[...], NT) + dot(dv, wv_ref[...], NT)
    dbias_ref[...] = total
    dwo_ref[...] = dot(ot_ref[...], g_ref[...]).astype(BF16)
    dq_ref[...] = dot(at_ref[...], q_ref[...]).astype(BF16)
    dk_ref[...] = dot(at_ref[...], k_ref[...]).astype(BF16)
    dv_ref[...] = dot(at_ref[...], v_ref[...]).astype(BF16)

    @pl.when(step == last)
    def _():
        gain = jnp.zeros((1, width), F32)
        shift = jnp.zeros((1, width), F32)
        for s in range(blocks):
            at = pl.ds(s * BLOCK, BLOCK)
            sorted_at = pl.ds(order_ref[0, s] * BLOCK, BLOCK)
            xh, _ = normalized(stored(x_ref, s).astype(F32))
            da = da_ref[sorted_at, :]
            gain += jnp.sum(da * xh, axis=0, keepdims=True)
            shift += jnp.sum(da, axis=0, keepdims=True)
            h_ref[at, :] = (da * norm_ref[1:2, :]).astype(BF16)
            out_ref[at, :] = acc_ref[sorted_at, :].astype(BF16)
        small_ref[0:1, :] = gain
        small_ref[1:2, :] = shift


def attend(order, x, g, norms, bias_q, tables, weights):
    rows, width = x.shape
    lanes = QUAD * HD
    groups = width // lanes
    whole = lambda shape: pl.BlockSpec(shape, lambda i: (0,) * len(shape))
    column = pl.BlockSpec((width, lanes), lambda i: (0, i))
    once = lambda shape: pl.BlockSpec(shape, lambda i: (0,) * len(shape), pipeline_mode=pl.Buffered(1))
    small = jax.ShapeDtypeStruct((rows, width), BF16)
    return pl.pallas_call(
        attend_kernel,
        grid=(groups,),
        in_specs=[
            pl.BlockSpec(memory_space=pltpu.SMEM),
            once((rows, width)),
            once((rows, width)),
            once(norms.shape),
            pl.BlockSpec((8, lanes), lambda i: (0, i)),
            once(tables[0].shape),
            once(tables[0].shape),
            once(tables[0].shape),
            pl.BlockSpec((width, lanes), lambda i: (0, i)),
            pl.BlockSpec((width, lanes), lambda i: (0, groups + i)),
            pl.BlockSpec((width, lanes), lambda i: (0, 2 * groups + i)),
            pl.BlockSpec((lanes, width), lambda i: (i, 3)),
        ],
        out_specs=[
            whole((rows, width)),
            whole((rows, width)),
            column,
            column,
            column,
            pl.BlockSpec((lanes, width), lambda i: (i, 0)),
            pl.BlockSpec((1, lanes), lambda i: (0, i)),
            whole((8, width)),
        ],
        out_shape=[
            small,
            small,
            jax.ShapeDtypeStruct((width, width), BF16),
            jax.ShapeDtypeStruct((width, width), BF16),
            jax.ShapeDtypeStruct((width, width), BF16),
            jax.ShapeDtypeStruct((width, width), BF16),
            jax.ShapeDtypeStruct((1, width), F32),
            jax.ShapeDtypeStruct((8, width), F32),
        ],
        scratch_shapes=[
            pltpu.VMEM((rows, width), BF16),
            pltpu.VMEM((rows, width), BF16),
            pltpu.VMEM((width, rows), BF16),
            pltpu.VMEM((rows, width), F32),
            pltpu.VMEM((rows, width), F32),
        ]
        + [pltpu.VMEM((rows, lanes), BF16)] * 5
        + [pltpu.VMEM((lanes, rows), BF16)] * 4
        + [pltpu.VMEM((rows, lanes), F32)] * 3,
        compiler_params=pltpu.CompilerParams(vmem_limit_bytes=60 * MIB),
        cost_estimate=pl.CostEstimate(
            flops=24 * rows * width * width + 8 * rows * rows * width,
            bytes_accessed=16 * width * width + 8 * rows * width,
            transcendentals=HEADS * rows * rows // 2,
        ),
        name="attend",
    )(order, x, g, norms, bias_q, *tables, weights, weights, weights, weights)


def rotary_tables(length):
    half = ROT // 2
    frequency = ROPE_BASE ** (-(np.arange(half) * 2.0 / ROT))
    angle = np.arange(length)[:, None] * frequency[None, :]
    cosine, sine = np.cos(angle), np.sin(angle)
    rest = np.zeros((length, HD - ROT))
    none = np.zeros_like(sine)
    cos_full = np.concatenate([cosine, cosine, rest + 1.0], axis=1)
    low = np.concatenate([-sine, none, rest], axis=1)
    high = np.concatenate([none, sine, rest], axis=1)
    return tuple(jnp.asarray(np.tile(t, (1, 2)).astype(np.float32)) for t in (cos_full, low, high))


def adamw(weight, grad, first, second, rate, decay):
    first_new = BETA_ONE * first + (1.0 - BETA_ONE) * grad
    second_new = BETA_TWO * second + (1.0 - BETA_TWO) * grad * grad
    first_hat = first_new / (1.0 - BETA_ONE**STEP)
    second_hat = second_new / (1.0 - BETA_TWO**STEP)
    weight_new = weight - rate * (first_hat / (jnp.sqrt(second_hat) + EPS_ADAM) + decay * weight)
    return (first_new, second_new, weight_new)


def shards(
    tokens, out_grad, block_order, qkv_weight, out_weight, up_weight, down_weight, norm_params, bias_params,
    qkv_first, qkv_second, out_first, out_second, up_first, up_second, down_first, down_second,
    norm_first, norm_second, bias_first, bias_second,
):
    groups, ring = lax.axis_size("dp"), lax.axis_size("ctx")
    group, rank = lax.axis_index("dp"), lax.axis_index("ctx")
    batch, piece, width = tokens.shape
    length = piece * ring
    count = batch * piece
    ff = up_weight.shape[1]

    share = bias_params.shape[0]
    lanes = share + -share % 128
    small = jnp.concatenate([
        jnp.pad(bias_params[None, :], ((0, 0), (0, lanes - share))),
        jnp.pad(norm_params, ((0, 3), (0, lanes - norm_params.shape[1]))),
    ])
    x_rows, g_rows = tokens.reshape(count, width), out_grad.reshape(count, width)
    att_copy, biases, norms, home_x, home_g, feed_out, h_feed, dup, ddown, dbias_up, small_feed = gather_feed(
        up_weight, down_weight, qkv_weight, out_weight, small, x_rows, g_rows, piece, ring * share
    )

    odd = group % 2

    order = block_order[jnp.clip(rank - odd, 0, batch - 1)]
    spots = jnp.arange(order.shape[0])
    order = jnp.stack([order, jnp.sum(jnp.where(order[None, :] == spots[:, None], spots[None, :], 0), axis=1)])

    attend_out, h_attend, dq, dk, dv, dout, dbias_q, small_attend = attend(
        order, home_x, home_g, norms, biases, rotary_tables(length), att_copy
    )

    dqkv = jnp.concatenate([dq, dk, dv], axis=1)
    tail = jnp.concatenate(
        [small_attend[:2].reshape(-1), small_feed[:2].reshape(-1), dbias_q[0], small_feed[2], dbias_up[0], small_feed[2]]
    )
    entries = tail.shape[0]
    tail = jnp.pad(tail, (0, -entries % 1024)).reshape(-1, 128)
    *owned, tail, ret_mixed, ret_back = reduce_all((dup, ddown, dqkv, dout), tail, attend_out, h_attend, batch)
    up_grad, down_grad, qkv_grad, out_grads = (
        g.reshape(w.shape).astype(F32)
        for g, w in zip(owned, (up_weight, down_weight, qkv_weight, out_weight))
    )
    tail = tail.reshape(-1)[:entries]
    returned = [v.reshape(count, width).astype(F32) for v in (ret_mixed, ret_back)]

    rows = x_rows.astype(F32)
    bias_rows = biases[0:1, width : 2 * width] + biases[0:1, 2 * width + ff :]
    layer_out = (rows + returned[0] + feed_out + bias_rows).astype(BF16).reshape(batch, piece, width)
    xh, scale = normalized(rows)
    h = returned[1] + h_feed
    inner = jnp.mean(h * xh, axis=-1, keepdims=True)
    input_grad = g_rows.astype(F32) + scale * (h - jnp.mean(h, axis=-1, keepdims=True) - xh * inner)
    input_grad = input_grad.reshape(batch, piece, width)

    norm_grad = lax.dynamic_slice_in_dim(tail[: 4 * width].reshape(4, width), rank * (width // ring), width // ring, 1)
    bias_grad = lax.dynamic_slice_in_dim(tail[4 * width :], rank * share, share, 0)

    qkv_new = adamw(qkv_weight, qkv_grad, qkv_first, qkv_second, 0.1, DECAY)
    out_new = adamw(out_weight, out_grads, out_first, out_second, 0.6, DECAY)
    up_new = adamw(up_weight, up_grad, up_first, up_second, 0.1, DECAY)
    down_new = adamw(down_weight, down_grad, down_first, down_second, 0.05, DECAY)
    norm_new = adamw(norm_params, norm_grad, norm_first, norm_second, 0.6, 0.0)
    bias_new = adamw(bias_params, bias_grad, bias_first, bias_second, 0.6, 0.0)
    return (
        layer_out, input_grad, *qkv_new, *out_new, *up_new, *down_new,
        norm_new[0], norm_new[1][:2], norm_new[1][2:], norm_new[2], *bias_new,
    )


def solution(mesh):
    rows, columns, token = P("ctx", None), P(None, "ctx"), P("dp", "ctx", None)
    in_specs = (token, token, P("dp", None)) + (rows,) * 4 + (columns, P("ctx")) + (rows,) * 8
    in_specs += (columns, columns, P("ctx"), P("ctx"))
    out_specs = (token, token) + (rows,) * 12 + (columns,) * 4 + (P("ctx"),) * 3
    return jax.shard_map(shards, mesh=mesh, in_specs=in_specs, out_specs=out_specs, check_vma=False)
```

```python
import functools
import math
from types import SimpleNamespace

import jax
import jax.numpy as jnp
import numpy as np
from jax import lax
from jax.experimental import pallas as pl
from jax.experimental.pallas import tpu as pltpu
from jax.sharding import PartitionSpec as P

HEADS = 12
HD = 64
STEP = 10
ROT = 16
BLOCK = 128
QUAD = 4
MLP_LEVELS = (2, 1)
LEVELS = (3, 3, 0, 0)

EPS_NORM = 1e-05
BETA_ONE = 0.9
BETA_TWO = 0.95
EPS_ADAM = 1e-08
DECAY = 0.01
ROPE_BASE = 10000.0
F32 = jnp.float32
BF16 = jnp.bfloat16
MIB = 1024 * 1024


def dot(left, right, dims=((1,), (0,))):
    return lax.dot_general(left, right, (dims, ((), ())), preferred_element_type=F32)


NN = ((1,), (0,))
NT = ((1,), (1,))
TN = ((0,), (0,))


def normalized(values):
    mean = jnp.mean(values, axis=-1, keepdims=True)
    centred = values - mean
    variance = jnp.mean(centred * centred, axis=-1, keepdims=True)
    scale = lax.rsqrt(variance + EPS_NORM)
    return centred * scale, scale


MESH = pl.DeviceIdType.MESH


def plane(d):
    core, x, y = d % 2, d // 2 % 2, d // 4 % 2
    return core, x, y, d + 1 - 2 * core, d + 2 - 4 * x, d + 4 - 8 * y


def gather_kernel(
    up, down, qkv, out, small, tokens, cotangents,
    att_all, small_all, norm_all, home_x, home_g, out_ref, h_ref, up_part, down_part, dbias_ref, sums_ref,
    up_all, down_all, att_own, up_wide, down_wide, att_wide, small_in, x_ref, g_ref, m_ref, mt_ref, hid_ref, dup_in_ref,
    dup_ref, up_core, up_first, ddown_ref, down_core,
    z_send, z_recv, p_send, p_recv, s_send, s_recv, t_send, t_recv, local, out_sem, c_send, c_recv,
):
    ring = lax.axis_size("ctx")
    d, z = lax.axis_index("dp"), lax.axis_index("ctx")
    core, x, y, core_id, x_id, y_id = plane(d)
    own = x + 2 * y
    own_x, own_y, far = own + 1 - 2 * x, own + 2 - 4 * y, 3 - own
    count, width = tokens.shape
    piece = home_x.shape[0] // ring
    batch = count // piece
    arrays = ((up_wide, up_all, False), (down_wide, down_all, True), (att_own, att_all, False))

    def slot(a, base, place, half=None):
        source, whole, tall = arrays[a]
        ref = source if base is None else whole
        rows, columns = source.shape
        at = 0 if base is None else base * rows
        height, span = rows // 4, columns // 2
        at = at + place * height
        column = core * span
        if half is not None:
            if tall:
                height = height // 2
                at = at + half * height
            else:
                span = span // 2
                column = column + half * span
        return ref.at[pl.ds(pl.multiple_of(at, 16), height), pl.ds(pl.multiple_of(column, 128), span)]

    def other_slot(a, base, place):
        source, whole, tall = arrays[a]
        rows, columns = source.shape
        at = pl.multiple_of(base * rows + place * (rows // 4), 16)
        column = pl.multiple_of((1 - core) * (columns // 2), 128)
        return whole.at[pl.ds(at, rows // 4), pl.ds(column, columns // 2)]

    def remote(src, dst, send, recv, dp, ctx):
        return pltpu.make_async_remote_copy(
            src_ref=src, dst_ref=dst, send_sem=send, recv_sem=recv, device_id=(dp, ctx), device_id_type=MESH
        )

    columns = qkv.shape[1]
    wide_loads = [
        [pltpu.make_async_copy(up, up_wide, local.at[0])],
        [pltpu.make_async_copy(down, down_wide, local.at[1])],
        [
            pltpu.make_async_copy(qkv, att_wide.at[:, pl.ds(0, columns)], local.at[2]),
            pltpu.make_async_copy(out, att_wide.at[:, pl.ds(columns, out.shape[1])], local.at[8]),
        ],
    ]
    for loads in wide_loads:
        for copy in loads:
            copy.start()

    def cast_own(a):
        for copy in wide_loads[a]:
            copy.wait()
        wide, target = ((up_wide, up_all), (down_wide, down_all), (att_wide, att_own))[a]
        rows = wide.shape[0]
        tile = 64
        base = 0 if a == 2 else z * rows

        def body(t, _):
            value = wide[pl.ds(pl.multiple_of(t * tile, 16), tile), :].astype(BF16)
            target[pl.ds(pl.multiple_of(base + t * tile, 16), tile), :] = value
            return 0

        lax.fori_loop(0, rows // tile, body, 0)

    barrier = pltpu.get_barrier_semaphore()
    for k in range(1, ring):
        pl.semaphore_signal(barrier, inc=1, device_id=(d, (z + k) % ring), device_id_type=MESH)
    for other in (core_id, x_id, y_id):
        pl.semaphore_signal(barrier, inc=1, device_id=(other, z), device_id_type=MESH)
    cast_own(0)
    pl.semaphore_wait(barrier, ring + 2)

    def hop(a, way, h):
        shard = z - h if way == 0 else z + h
        target = z + 1 if way == 0 else z - 1
        src = slot(a, None, own) if h == 0 and a == 2 else slot(a, shard, own)
        return remote(src, slot(a, shard, own), z_send.at[a, way, h], z_recv.at[a, way, h], d, target)

    def can_send(way, h):
        shard = z - h if way == 0 else z + h
        target = z + 1 if way == 0 else z - 1
        return (shard >= 0) & (shard < ring) & (target >= 0) & (target < ring)

    def in_range(way, h):
        shard = z - h if way == 0 else z + h
        return (shard >= 0) & (shard < ring)

    def cast(a, shard, j):
        send, recv = p_send.at[a, shard, j], p_recv.at[a, shard, j]
        if j == 0:
            ref = slot(a, shard, own)
            return remote(ref, ref, send, recv, x_id, z)
        if j == 1:
            ref = slot(a, shard, own)
            return remote(ref, ref, send, recv, y_id, z)
        if j == 2:
            ref = slot(a, shard, own_x, 0)
            return remote(ref, ref, send, recv, y_id, z)
        if j == 3:
            ref = slot(a, shard, own_y, 1)
            return remote(ref, ref, send, recv, x_id, z)
        ref = slot(a, shard, (own, own_x, own_y, far)[j - 4])
        return remote(ref, ref, send, recv, core_id, z)

    def arrived(a, shard, j):
        send, recv = p_send.at[a, shard, j], p_recv.at[a, shard, j]
        ref = {0: lambda: slot(a, shard, own_x), 1: lambda: slot(a, shard, own_y),
               2: lambda: slot(a, shard, far, 0), 3: lambda: slot(a, shard, far, 1)}.get(
            j, lambda: other_slot(a, shard, (own, own_x, own_y, far)[j - 4]))()
        remote(ref, ref, send, recv, core_id, z).wait_recv()

    def start_hops(a):
        for way in range(2):
            @pl.when(can_send(way, 0))
            def _(way=way):
                hop(a, way, 0).start()

    def small_copy(k):
        return remote(small, small_in.at[z], s_send.at[k], s_recv.at[k], d, (z + k) % ring)

    def stage_a(a, h):
        for way in range(2):
            @pl.when(in_range(way, h))
            def _(way=way):
                shard = z - h if way == 0 else z + h
                ref = slot(a, shard, own)
                remote(ref, ref, z_send.at[a, way, h - 1], z_recv.at[a, way, h - 1], core_id, z).wait_recv()

                @pl.when(can_send(way, h))
                def _():
                    hop(a, way, h).start()

                cast(a, shard, 0).start()
                cast(a, shard, 1).start()
                cast(a, shard, 4).start()

    def stage_b(a, h):
        for way in range(2):
            @pl.when(in_range(way, h))
            def _(way=way):
                shard = z - h if way == 0 else z + h
                arrived(a, shard, 0)
                cast(a, shard, 2).start()
                cast(a, shard, 5).start()
                arrived(a, shard, 1)
                cast(a, shard, 3).start()
                cast(a, shard, 6).start()

    def stage_c(a, h):
        for way in range(2):
            @pl.when(in_range(way, h))
            def _(way=way):
                shard = z - h if way == 0 else z + h
                arrived(a, shard, 2)
                arrived(a, shard, 3)
                cast(a, shard, 7).start()

    def stage_d(a, h):
        for way in range(2):
            @pl.when(in_range(way, h))
            def _(way=way):
                shard = z - h if way == 0 else z + h
                for j in range(4, 8):
                    arrived(a, shard, j)

    pairs = ((tokens, home_x), (cotangents, home_g))

    def move(which, i):
        source, whole = pairs[which]
        src = source.at[pl.ds(i * piece, piece), :]
        dst = whole.at[pl.ds(pl.multiple_of(z * piece, 16), piece), :]
        return src, dst, i + core

    def start_moves(which):
        for i in range(batch):
            src, dst, target = move(which, i)

            @pl.when(target != z)
            def _(src=src, dst=dst, target=target, i=i):
                remote(src, dst, t_send.at[which, i], t_recv.at[which, z], d, target).start()

            @pl.when(target == z)
            def _(src=src, dst=dst):
                pltpu.make_async_copy(src, dst, local.at[6 + which]).start()

    own_rows = pl.ds(pl.multiple_of(z * att_own.shape[0], 16), att_own.shape[0])
    own_att = pltpu.make_async_copy(att_own, att_all.at[own_rows, :], local.at[9])
    x_load = pltpu.make_async_copy(tokens, x_ref, local.at[3])
    g_load = pltpu.make_async_copy(cotangents, g_ref, local.at[4])
    own_small = pltpu.make_async_copy(small, small_in.at[z], local.at[5])

    start_hops(0)
    cast_own(1)
    start_hops(1)
    cast_own(2)
    start_hops(2)
    for k in range(1, ring):
        small_copy(k).start()
    for copy in (own_att, x_load, g_load, own_small):
        copy.start()
    hops = range(1, ring)
    work = [(a, h) for a in range(3) for h in hops]
    early = 2 * (ring - 1)
    for n in range(len(work)):
        stage_a(*work[n])
        if 1 <= n <= early:
            stage_b(*work[n - 1])
        if 2 <= n <= early + 1:
            stage_c(*work[n - 2])
    start_moves(0)
    start_moves(1)

    own_small.wait()
    for k in range(1, ring):
        ref = small_in.at[(z + ring - k) % ring]
        remote(ref, ref, s_send.at[k], s_recv.at[k], core_id, z).wait_recv()
    x_load.wait()
    g_load.wait()
    entries = small_all.shape[1]
    biases = jnp.zeros((8, entries), F32)
    norms = jnp.zeros((8, width), F32)
    for r in range(ring):
        block = small_in[r].astype(BF16).astype(F32)
        full = jnp.concatenate([block, jnp.zeros((8, entries - block.shape[1]), F32)], axis=1)
        biases += pltpu.roll(full, r * (entries // ring), 1) if r else full
        norms += pltpu.roll(block[:, :width], r * (width // ring), 1) if r else block[:, :width]
    small_all[...] = biases
    norm_all[...] = norms
    ff = up_all.shape[1]
    gain_2, shift_2 = norm_all[3:4, :], norm_all[4:5, :]
    tile = 256
    tiles = count // tile
    for t in range(tiles):
        at = pl.ds(t * tile, tile)
        xh, _ = normalized(x_ref[at, :].astype(F32))
        m = xh * gain_2 + shift_2
        m_ref[at, :] = m.astype(BF16)
        mt_ref[:, at] = m.T.astype(BF16)
        out_ref[at, :] = jnp.zeros((tile, width), F32)
        h_ref[at, :] = jnp.zeros((tile, width), F32)
    for h in hops:
        stage_d(0, h)
        stage_d(1, h)

    strip = dup_ref.shape[3] // ring
    steps = ff // (ring * strip)
    half = ring // 2
    big, by_core = (dup_ref, ddown_ref), (up_core, down_core)
    bits, ids = ((x, y), (y, x)), ((x_id, y_id), (y_id, x_id))

    def sizes(a):
        return by_core[a].shape[2], by_core[a].shape[3]

    def slice_of(order):
        return 2 * bits[order][0] + bits[order][1]

    def core_copy(a, i):
        _, span = sizes(a)
        away = pl.ds(pl.multiple_of((1 - core) * span, 128), span)
        return remote(big[a].at[i, :, :, away], by_core[a].at[i], c_send.at[a, i, 0], c_recv.at[a, i, 0], core_id, z)

    def first_copy(a, i, order):
        height, _ = sizes(a)
        own = pl.ds(order * half, half)
        away = pl.ds(pl.multiple_of((1 - bits[order][0]) * (height // 2), 16), height // 2)
        return remote(
            by_core[a].at[i, own, away, :], up_first.at[i, own], c_send.at[a, i, 1 + order],
            c_recv.at[a, i, 1 + order], ids[order][0], z,
        )

    def add(into, at, term, owners):
        height = term(0).shape[0]
        tile = 32 if height % 48 else 48

        def body(n, _):
            o, t = n // (height // tile), n % (height // tile)
            spot = pl.ds(pl.multiple_of(at + t * tile, 16), tile)
            value = term(o)[pl.ds(pl.multiple_of(t * tile, 16), tile), :]
            into[o, spot, :] = (into[o, spot, :].astype(F32) + value.astype(F32)).astype(BF16)
            return 0

        lax.fori_loop(0, owners * (height // tile), body, 0)

    def chunk_1(i):
        for a in range(2):
            _, span = sizes(a)
            core_copy(a, i).wait_recv()
            keep = pl.ds(pl.multiple_of(core * span, 128), span)
            add(by_core[a].at[i], 0, lambda o: big[a].at[i, o, :, keep], ring)
        for order in range(2):
            first_copy(0, i, order).start()
        parts_out(1, i)[0].start()

    def chunk_2(i):
        height, _ = sizes(0)
        for order in range(2):
            own = pl.ds(order * half, half)
            first_copy(0, i, order).wait_recv()
            at = bits[order][0] * (height // 2)
            add(by_core[0].at[i, own], at, lambda o: up_first.at[i, order * half + o], half)
        for copy in parts_out(0, i):
            copy.start()

    def parts_out(a, i):
        height, span = sizes(a)
        if a == 1:
            return [pltpu.make_async_copy(by_core[1].at[i], down_part.at[:, i], out_sem.at[i, 2 * half])]
        copies = []
        for order in range(2):
            own = pl.ds(order * half, half)
            rows = pl.ds(pl.multiple_of(bits[order][0] * (height // 2), 16), height // 2)
            for n in range(half):
                copies.append(pltpu.make_async_copy(
                    by_core[0].at[i, own, rows, pl.ds(n * strip, strip)],
                    up_part.at[own, :, pl.ds(pl.multiple_of(n * steps * strip + i * strip, 128), strip)],
                    out_sem.at[i, half * order + n],
                ))
        return copies

    def feed_step(step, _):
        for h in hops:
            @pl.when(step == h - 1)
            def _(h=h):
                stage_b(2, h)

            @pl.when(step == h)
            def _(h=h):
                stage_c(2, h)

        @pl.when(step < steps)
        def _():
            spots = [pl.ds(pl.multiple_of(r * (ff // ring) + step * strip, 128), strip) for r in range(ring)]
            bias_spots = [
                pl.ds(pl.multiple_of(2 * width + r * (ff // ring) + step * strip, 128), strip) for r in range(ring)
            ]
            up_part_ = jnp.concatenate([up_all[:, at] for at in spots], axis=1)
            down_part_ = jnp.concatenate([down_all[at, :] for at in spots], axis=0)
            bias = jnp.concatenate([small_all[0:1, at] for at in bias_spots], axis=1)
            total = jnp.zeros((1, ring * strip), F32)
            for t in range(tiles):
                at = pl.ds(t * tile, tile)
                u = dot(m_ref[at, :], up_part_) + bias
                cdf = 0.5 * (1.0 + lax.erf(u * (1.0 / math.sqrt(2.0))))
                hidden = (u * cdf).astype(BF16)
                slope = cdf + u * jnp.exp(-0.5 * u * u) * (1.0 / math.sqrt(2.0 * math.pi))
                back = (dot(g_ref[at, :], down_part_, NT) * slope).astype(BF16)
                hid_ref[at, :] = hidden
                dup_in_ref[at, :] = back
                total += jnp.sum(back.astype(F32), axis=0, keepdims=True)
                out_ref[at, :] += dot(hidden, down_part_)
                h_ref[at, :] += dot(back, up_part_, NT)
            for r in range(ring):
                dbias_ref[0:1, spots[r]] = total[:, r * strip : (r + 1) * strip]
            ddown = dot(hid_ref[...], g_ref[...], TN).astype(BF16)
            dup = dot(mt_ref[...], dup_in_ref[...]).astype(BF16)
            for r in range(ring):
                ddown_ref[step, r] = ddown[r * strip : (r + 1) * strip, :]
                dup_ref[step, r] = dup[r * (width // ring) : (r + 1) * (width // ring), :]
            core_copy(0, step).start()
            core_copy(1, step).start()

        for lag, stage in ((1, chunk_1), (3, chunk_2)):
            @pl.when((step >= lag) & (step < steps + lag))
            def _(lag=lag, stage=stage):
                stage(step - lag)

        return 0

    lax.fori_loop(0, steps + 3, feed_step, 0)

    gain = jnp.zeros((1, width), F32)
    shift = jnp.zeros((1, width), F32)
    sums = jnp.zeros((1, width), F32)
    for t in range(tiles):
        at = pl.ds(t * tile, tile)
        xh, _ = normalized(x_ref[at, :].astype(F32))
        dm = h_ref[at, :]
        gain += jnp.sum(dm * xh, axis=0, keepdims=True)
        shift += jnp.sum(dm, axis=0, keepdims=True)
        sums += jnp.sum(g_ref[at, :].astype(F32), axis=0, keepdims=True)
        h_ref[at, :] = dm * gain_2
    sums_ref[...] = jnp.concatenate([gain, shift, sums, jnp.zeros((5, width), F32)], axis=0)

    mine = z - core
    for which in range(2):
        for k in range(1, ring):
            @pl.when((mine >= 0) & (mine < batch))
            def _(which=which, k=k):
                other = (z + k) % ring
                ref = pairs[which][1].at[pl.ds(pl.multiple_of(other * piece, 16), piece), :]
                remote(ref, ref, t_send.at[which, 0], t_recv.at[which, other], core_id, z).wait_recv()
    for h in hops:
        stage_d(2, h)
    for k in range(1, ring):
        small_copy(k).wait_send()
    for a in range(3):
        for way in range(2):
            for h in range(ring - 1):
                @pl.when(can_send(way, h))
                def _(a=a, way=way, h=h):
                    hop(a, way, h).wait_send()
        for h in hops:
            for way in range(2):
                @pl.when(in_range(way, h))
                def _(a=a, h=h, way=way):
                    shard = z - h if way == 0 else z + h
                    for j in range(8):
                        cast(a, shard, j).wait_send()
    for which in range(2):
        for i in range(batch):
            src, dst, target = move(which, i)

            @pl.when(target != z)
            def _(src=src, dst=dst, target=target, which=which, i=i):
                remote(src, dst, t_send.at[which, i], t_recv.at[which, z], d, target).wait_send()

            @pl.when(target == z)
            def _(src=src, dst=dst, which=which):
                pltpu.make_async_copy(src, dst, local.at[6 + which]).wait()
    own_att.wait()

    def close(i, _):
        for a in range(2):
            core_copy(a, i).wait_send()
            for copy in parts_out(a, i):
                copy.wait()
        for order in range(2):
            first_copy(0, i, order).wait_send()
        return 0

    lax.fori_loop(0, steps, close, 0)


def gather_feed(up, down, qkv, out, small, tokens, cotangents, piece, entries):
    ring = lax.axis_size("ctx")
    count, width = tokens.shape
    ff = up.shape[1]
    strip = 128
    chunk = ring * strip
    steps = ff // chunk
    shard = up.shape[0]
    columns = qkv.shape[1] + out.shape[1]
    home = jax.ShapeDtypeStruct((ring * piece, width), tokens.dtype)
    rows = jax.ShapeDtypeStruct((count, width), F32)
    dma = pltpu.SemaphoreType.DMA
    anywhere = pl.BlockSpec(memory_space=pl.ANY)
    vmem = pl.BlockSpec(memory_space=pltpu.VMEM)
    return pl.pallas_call(
        gather_kernel,
        in_specs=[anywhere] * 7,
        out_specs=[anywhere, vmem, vmem, anywhere, anywhere, vmem, vmem, anywhere, anywhere, vmem, vmem],
        out_shape=[
            jax.ShapeDtypeStruct((ring * shard, columns), BF16),
            jax.ShapeDtypeStruct((8, entries), F32), jax.ShapeDtypeStruct((8, width), F32), home, home, rows, rows,
            jax.ShapeDtypeStruct((ring, shard // 2, ff // 2), BF16),
            jax.ShapeDtypeStruct((ring, steps, strip, width // 2), BF16),
            jax.ShapeDtypeStruct((8, ff), F32), jax.ShapeDtypeStruct((8, width), F32),
        ],
        scratch_shapes=[
            pltpu.VMEM((ring * shard, ff), BF16), pltpu.VMEM((ring * down.shape[0], width), BF16),
            pltpu.VMEM((shard, columns), BF16),
            pltpu.VMEM(up.shape, F32), pltpu.VMEM(down.shape, F32), pltpu.VMEM((shard, columns), F32),
            pltpu.VMEM((ring, *small.shape), F32),
            pltpu.VMEM((count, width), BF16), pltpu.VMEM((count, width), BF16), pltpu.VMEM((count, width), BF16),
            pltpu.VMEM((width, count), BF16),
            pltpu.VMEM((count, chunk), BF16), pltpu.VMEM((count, chunk), BF16),
            pltpu.VMEM((steps, ring, shard, chunk), BF16), pltpu.VMEM((steps, ring, shard, chunk // 2), BF16),
            pltpu.VMEM((steps, ring, shard // 2, chunk // 2), BF16),
            pltpu.VMEM((steps, ring, strip, width), BF16), pltpu.VMEM((steps, ring, strip, width // 2), BF16),
            dma((3, 2, ring)), dma((3, 2, ring)), dma((3, ring, 8)), dma((3, ring, 8)),
            dma((ring,)), dma((ring,)), dma((2, count // piece)), dma((2, ring)), dma((10,)), dma((steps, ring + 1)),
            dma((2, steps, 3)), dma((2, steps, 3)),
        ],
        compiler_params=pltpu.CompilerParams(
            collective_id=0, has_side_effects=True, vmem_limit_bytes=60 * MIB
        ),
        cost_estimate=pl.CostEstimate(
            flops=12 * count * width * ff, bytes_accessed=60 * MIB, transcendentals=count * ff
        ),
        name="gather_feed",
    )(up, down, qkv, out, small, tokens, cotangents)


def remote(src, dst, send_sem, recv_sem, dp, ctx):
    return pltpu.make_async_remote_copy(
        src_ref=src, dst_ref=dst, send_sem=send_sem, recv_sem=recv_sem, device_id=(dp, ctx), device_id_type=MESH
    )


def team_id(d, t):
    return d + (8 << t) * (1 - 2 * (d // (8 << t) % 2))


def greet(teams):
    ring = lax.axis_size("ctx")
    d, z = lax.axis_index("dp"), lax.axis_index("ctx")
    core, x, y, core_id, x_id, y_id = plane(d)
    barrier = pltpu.get_barrier_semaphore()
    partners = [core_id, x_id, y_id, x_id + y_id - d] + [team_id(d, t) for t in range(teams)]
    for k in range(1, ring):
        pl.semaphore_signal(barrier, inc=1, device_id=(d, (z + k) % ring), device_id_type=MESH)
    for other in partners:
        pl.semaphore_signal(barrier, inc=1, device_id=(other, z), device_id_type=MESH)
    pl.semaphore_wait(barrier, ring - 1 + len(partners))


def reducer(teams, levels, ins, sums, bufs, send, recv, load):
    count = len(ins)
    ring = lax.axis_size("ctx")
    d, z = lax.axis_index("dp"), lax.axis_index("ctx")
    core, x, y, core_id, x_id, y_id = plane(d)
    far_id = x_id + y_id - d
    bits, ids = ((x, y), (y, x)), ((x_id, y_id), (y_id, x_id))
    spots = ((x, y), (1 - x, y), (x, 1 - y), (1 - x, 1 - y))

    def sizes(a):
        _, strips, quarter, span = bufs[a][-1].shape
        return strips, quarter, span

    def owners(a, order):
        strips = sizes(a)[0]
        return pl.ds(order * ring // 2 * strips, ring // 2 * strips)

    def rows_at(at, height):
        return pl.ds(pl.multiple_of(at, 16), height)

    def kept(a, order):
        return 0 if levels[a] == 2 else bits[order][0] * 2 * sizes(a)[1]

    def core_copy(a):
        span = sizes(a)[2]
        away = pl.ds(pl.multiple_of((1 - core) * span, 128), span)
        return remote(ins[a].at[:, :, away], bufs[a][1], send.at[a, 0], recv.at[a, 0], core_id, z)

    def own_load(a):
        if levels[a] == 3:
            return pltpu.make_async_copy(ins[a], bufs[a][5].at[0], load.at[a])
        span = sizes(a)[2]
        keep = pl.ds(pl.multiple_of(core * span, 128), span)
        src = ins[a].at[:, :, keep] if levels[a] == 0 else ins[a]
        return pltpu.make_async_copy(src, bufs[a][0], load.at[a])

    def first_copy(a, order):
        quarter = sizes(a)[1]
        away = rows_at((1 - bits[order][0]) * 2 * quarter, 2 * quarter)
        return remote(
            bufs[a][0].at[owners(a, order), away, :], bufs[a][2].at[owners(a, order)], send.at[a, 1 + order],
            recv.at[a, 1 + order], ids[order][0], z,
        )

    def second_copy(a, order):
        quarter = sizes(a)[1]
        away = rows_at(kept(a, order) + (1 - bits[order][1]) * quarter, quarter)
        return remote(
            bufs[a][0].at[owners(a, order), away, :], bufs[a][3].at[owners(a, order)], send.at[a, 3 + order],
            recv.at[a, 3 + order], ids[order][1], z,
        )

    def own_quarter(a, owner):
        strips, quarter, _ = sizes(a)
        order = owner // (ring // 2)
        first, second = (1 - order) * x + order * y, (1 - order) * y + order * x
        at = second * quarter if levels[a] == 2 else (2 * first + second) * quarter
        return bufs[a][0].at[pl.ds(owner * strips, strips), rows_at(at, quarter), :]

    def owner_copy(a, k):
        to = (z + k) % ring
        return remote(own_quarter(a, to), bufs[a][4].at[k - 1], send.at[a, 4 + k], recv.at[a, 4 + k], d, to)

    def team_copy(a, t):
        j = 4 + ring + 7 + t
        return remote(bufs[a][5].at[0], bufs[a][5].at[1 + t], send.at[a, j], recv.at[a, j], team_id(d, t), z)

    def final(a, spot, side):
        strips, quarter, span = sizes(a)
        order = z // (ring // 2)
        xx, yy = spots[spot]
        at = ((1 - order) * (2 * xx + yy) + order * (2 * yy + xx)) * quarter
        return sums[a].at[:, rows_at(at, quarter), pl.ds(pl.multiple_of(side * span, 128), span)]

    def spread(a, j):
        s, r = send.at[a, 4 + ring + j - 1], recv.at[a, 4 + ring + j - 1]
        if j < 4:
            return remote(bufs[a][5].at[0], final(a, 0, core), s, r, (x_id, y_id, far_id)[j - 1], z)
        src = bufs[a][5].at[0] if j == 4 else final(a, j - 4, core)
        return remote(src, final(a, j - 4, core), s, r, core_id, z)

    def spread_here(a, j):
        s, r = send.at[a, 4 + ring + j - 1], recv.at[a, 4 + ring + j - 1]
        ref = final(a, j, core) if j < 4 else final(a, j - 4, 1 - core)
        remote(ref, ref, s, r, core_id, z).wait_recv()

    def keep_own(a):
        return pltpu.make_async_copy(bufs[a][5].at[0], final(a, 0, core), load.at[count + a])

    def add(into, at, term, blocks):
        height = term.shape[1]
        tile = 32 if height % 48 else 48

        def body(n, _):
            o, t = n // (height // tile), n % (height // tile)
            spot = rows_at(at + t * tile, tile)
            value = term[o, rows_at(t * tile, tile), :]
            into[o, spot, :] = (into[o, spot, :].astype(F32) + value.astype(F32)).astype(BF16)
            return 0

        lax.fori_loop(0, blocks * (height // tile), body, 0)

    def enter(a):
        if levels[a] == 0:
            core_copy(a).start()
        own_load(a).start()

    def first(a):
        own_load(a).wait()
        if levels[a] == 0:
            core_copy(a).wait_recv()
            add(bufs[a][0], 0, bufs[a][1], bufs[a][0].shape[0])
        if levels[a] < 2:
            for order in range(2):
                first_copy(a, order).start()

    def second(a):
        for order in range(2):
            if levels[a] < 2:
                first_copy(a, order).wait_recv()
                own = owners(a, order)
                add(bufs[a][0].at[own], kept(a, order), bufs[a][2].at[own], ring // 2 * sizes(a)[0])
            second_copy(a, order).start()

    def to_owner(a):
        for order in range(2):
            second_copy(a, order).wait_recv()
            own = owners(a, order)
            at = kept(a, order) + bits[order][1] * sizes(a)[1]
            add(bufs[a][0].at[own], at, bufs[a][3].at[own], ring // 2 * sizes(a)[0])
        for k in range(1, ring):
            owner_copy(a, k).start()

    def add_up(a):
        for k in range(1, ring):
            owner_copy(a, k).wait_recv()
        mine = own_quarter(a, z)
        for s in range(sizes(a)[0]):
            terms = [mine[s]] + [bufs[a][4][k, s] for k in range(ring - 1)]
            bufs[a][5][0, s] = sum((t.astype(F32) for t in terms[1:]), terms[0].astype(F32)).astype(BF16)
        for t in range(teams):
            team_copy(a, t).start()
            team_copy(a, t).wait()
            bufs[a][5][0] = (bufs[a][5][0].astype(F32) + bufs[a][5][1 + t].astype(F32)).astype(BF16)

    def total(a):
        if levels[a] == 3:
            own_load(a).wait()
        else:
            add_up(a)
        keep_own(a).start()
        for j in range(1, 5):
            spread(a, j).start()

    def hand_on(a):
        add_up(a)
        out = pltpu.make_async_copy(bufs[a][5].at[0], sums[a], load.at[count + a])
        out.start()
        sent(a)
        out.wait()

    def share(a):
        for j in range(1, 4):
            spread_here(a, j)
            spread(a, 4 + j).start()

    def sent(a):
        if levels[a] == 0:
            core_copy(a).wait_send()
        for order in range(2):
            if levels[a] < 2:
                first_copy(a, order).wait_send()
            second_copy(a, order).wait_send()
        for k in range(1, ring):
            owner_copy(a, k).wait_send()

    def close(a):
        for j in range(4, 8):
            spread_here(a, j)
        if levels[a] < 3:
            sent(a)
        for j in range(1, 8):
            spread(a, j).wait_send()
        keep_own(a).wait()

    return SimpleNamespace(
        enter=enter, first=first, second=second, to_owner=to_owner, total=total, hand_on=hand_on, share=share, close=close
    )


def reducer_scratch(levels, shapes, teams, ring):
    scratch = []
    for level, (strips, rows, columns) in zip(levels, shapes):
        blocks, span = ring * strips, columns // 2
        none = (1, 16, 128)
        scratch += [
            pltpu.VMEM(none if level == 3 else (blocks, rows // 2 if level == 2 else rows, span), BF16),
            pltpu.VMEM((blocks, rows, span) if level == 0 else none, BF16),
            pltpu.VMEM((blocks, rows // 2, span) if level < 2 else none, BF16),
            pltpu.VMEM((blocks, rows // 4, span) if level < 3 else none, BF16),
            pltpu.VMEM((ring - 1, strips, rows // 4, span) if level < 3 else (1, *none), BF16),
            pltpu.VMEM((1 + teams, strips, rows // 4, span), BF16),
        ]
    copies = 4 + ring + 7 + teams
    dma = pltpu.SemaphoreType.DMA
    return scratch + [dma((len(levels), copies)), dma((len(levels), copies)), dma((2 * len(levels),))]


def reduce_kernel(
    teams, up_ref, down_ref, qkv_ref, small_att, small_mlp, small_up, back_ref, o_last, o_ref, g_ref, weights,
    up_sum, down_sum, qkv_sum, out_sum, small_out, attend_out, ret_back, *refs,
):
    ring = lax.axis_size("ctx")
    d, z = lax.axis_index("dp"), lax.axis_index("ctx")
    core, x, y, core_id, x_id, y_id = plane(d)
    bufs = [refs[6 * a : 6 * a + 6] for a in range(4)]
    send, recv, load, o_in, wo_ref, dwo_ref, small_acc, small_in = refs[24:32]
    s_send, s_recv, r_send, r_recv, r_local = refs[32:]
    batch, piece, width = ret_back.shape
    lanes = o_last.shape[1]
    up, down, qkv, out = range(4)
    ins, sums = (up_ref, down_ref, qkv_ref, dwo_ref), (up_sum, down_sum, qkv_sum, out_sum)
    do = reducer(teams, LEVELS, ins, sums, bufs, send, recv, load)

    pairs = ((o_last, o_in), (back_ref, ret_back))
    mine = z - core

    def returned(which, i, to):
        source, target = pairs[which]
        return source.at[pl.ds(pl.multiple_of(to * piece, 16), piece), :], target.at[i]

    def start_returns(which):
        for i in range(batch):
            @pl.when(mine == i)
            def _(i=i):
                for k in range(1, ring):
                    to = (z + k) % ring
                    src, dst = returned(which, i, to)
                    remote(src, dst, r_send.at[which, k], r_recv.at[which, i], d, to).start()
                src, dst = returned(which, i, z)
                pltpu.make_async_copy(src, dst, r_local.at[which]).start()

    def wait_returns(which):
        for i in range(batch):
            src, dst = returned(which, i, z)

            @pl.when(mine == i)
            def _(src=src, dst=dst):
                pltpu.make_async_copy(src, dst, r_local.at[which]).wait()

            @pl.when(mine != i)
            def _(i=i, src=src, dst=dst):
                remote(src, dst, r_send.at[which, 0], r_recv.at[which, i], core_id, z).wait_recv()

    def close_returns(which):
        for i in range(batch):
            @pl.when(mine == i)
            def _(i=i):
                for k in range(1, ring):
                    to = (z + k) % ring
                    remote(*returned(which, i, to), r_send.at[which, k], r_recv.at[which, i], d, to).wait_send()

    steps = [core_id, x_id, y_id] + [team_id(d, t) for t in range(teams)]

    def small_copy(n):
        return remote(small_acc, small_in.at[n], s_send.at[n], s_recv.at[n], steps[n], z)

    def small_owner(k):
        n = len(steps) + k - 1
        return remote(small_acc, small_in.at[n], s_send.at[n], s_recv.at[n], d, (z + k) % ring)

    def small_close(n):
        small_copy(n).wait()
        small_acc[...] += small_in[n]
        if n + 1 < len(steps):
            small_copy(n + 1).start()
        else:
            for k in range(1, ring):
                small_owner(k).start()

    columns = weights.shape[1] - width
    wo_load = pltpu.make_async_copy(weights.at[:, pl.ds(columns, width)], wo_ref, r_local.at[2])
    wo_load.start()
    small_acc[0:8, :] = small_att[...]
    small_acc[8:16, :] = small_mlp[...]
    for n in range(small_up.shape[1] // width):
        small_acc[16 + n : 17 + n, :] = small_up[0:1, n * width : (n + 1) * width]
    rest = 16 + small_up.shape[1] // width
    small_acc[rest:, :] = jnp.zeros((small_acc.shape[0] - rest, width), F32)
    greet(teams)
    do.enter(qkv)
    start_returns(0)
    start_returns(1)
    do.enter(up)
    do.enter(down)
    small_copy(0).start()
    do.total(up)
    do.total(down)
    do.first(qkv)
    small_close(0)
    do.share(up)
    do.share(down)

    wo_load.wait()
    wait_returns(0)
    split = o_ref.shape[1]
    for i in range(batch):
        at = pl.ds(i * piece, piece)
        attend_out[at, :] = dot(o_ref[at, :], wo_ref[:split, :]) + dot(o_in[i], wo_ref[split:, :])
    late = jnp.concatenate([o_in[i] for i in range(batch)], axis=0)
    dwo = jnp.concatenate([dot(o_ref[...], g_ref[...], TN), dot(late, g_ref[...], TN)], axis=0).astype(BF16)
    for r in range(ring):
        dwo_ref[r] = dwo[r * (width // ring) : (r + 1) * (width // ring), :]
    do.enter(out)
    do.second(qkv)
    do.first(out)
    small_close(1)
    do.to_owner(qkv)
    do.second(out)
    for n in range(2, len(steps)):
        small_close(n)
    do.total(qkv)
    do.to_owner(out)
    do.share(qkv)
    do.total(out)
    for k in range(1, ring):
        small_owner(k).wait()
    total = small_acc[...]
    for k in range(ring - 1):
        total += small_in[len(steps) + k]
    small_out[...] = total
    do.share(out)
    for a in range(4):
        do.close(a)
    wait_returns(1)
    close_returns(0)
    close_returns(1)


def reduce_all(up, down, qkv, small_att, small_mlp, small_up, back, o_last, o_first, g, weights, batch):
    ring, groups = lax.axis_size("ctx"), lax.axis_size("dp")
    teams = (groups // 8).bit_length() - 1
    width = g.shape[1]
    piece = g.shape[0] // batch
    shapes = [(n, 4 * rows, 2 * span) for n, rows, span in (up.shape, down.shape)]
    shapes += [(1, width // ring, qkv.shape[1]), (1, width // ring, width)]
    dma = pltpu.SemaphoreType.DMA
    anywhere = pl.BlockSpec(memory_space=pl.ANY)
    vmem = pl.BlockSpec(memory_space=pltpu.VMEM)
    rounds = 3 + teams + ring - 1
    small = (16 + -(-small_up.shape[1] // width // 8) * 8, width)
    scratch = reducer_scratch(LEVELS, shapes, teams, ring)
    scratch += [
        pltpu.VMEM((batch, piece, o_last.shape[1]), BF16), pltpu.VMEM((width, width), BF16),
        pltpu.VMEM((ring, width // ring, width), BF16), pltpu.VMEM(small, F32), pltpu.VMEM((rounds, *small), F32),
        dma((rounds,)), dma((rounds,)), dma((2, ring)), dma((2, batch)), dma((3,)),
    ]
    return pl.pallas_call(
        functools.partial(reduce_kernel, teams),
        in_specs=[anywhere] * 3 + [vmem] * 3 + [anywhere, anywhere, vmem, vmem, anywhere],
        out_specs=[anywhere] * 4 + [vmem, vmem, anywhere],
        out_shape=[jax.ShapeDtypeStruct(shape, BF16) for shape in shapes]
        + [
            jax.ShapeDtypeStruct(small, F32), jax.ShapeDtypeStruct(g.shape, F32),
            jax.ShapeDtypeStruct((batch, piece, width), BF16),
        ],
        scratch_shapes=scratch,
        compiler_params=pltpu.CompilerParams(collective_id=1, has_side_effects=True, vmem_limit_bytes=56 * MIB),
        cost_estimate=pl.CostEstimate(flops=4 * width * width * g.shape[0], bytes_accessed=60 * MIB, transcendentals=0),
        name="reduce",
    )(
        up, down, qkv.reshape(ring, width // ring, -1), small_att, small_mlp, small_up, back, o_last,
        o_first.reshape(batch * piece, -1), g, weights,
    )


def attend_kernel(
    teams, order_ref, x_ref, stored_g_ref, norm_ref, bias_ref, cos_ref, low_ref, high_ref, wq_ref, wk_ref, wv_ref,
    wo_ref, up_ref, down_ref, h_ref, dqkv_all, small_ref, o_last, ret_o, up_sum, down_sum,
    g_ref, a_ref, at_ref, da_ref, q_ref, k_ref, v_ref, do_ref, o_ref, kt_ref, vt_ref, dqs_ref, dks_ref, dvs_ref,
    grad_ref, stored_o_ref, o_send, o_recv, o_local, grad_sem, *reduce_refs,
):
    step = pl.program_id(0)
    last = grad_ref.shape[0] - 1
    rows, width = x_ref.shape
    lanes = QUAD * HD
    tile = 256
    half = ROT // 2
    scale = 1.0 / math.sqrt(HD)
    blocks = rows // BLOCK
    ring = lax.axis_size("ctx")
    d, z = lax.axis_index("dp"), lax.axis_index("ctx")
    core_id = plane(d)[3]
    batch, piece = ret_o.shape[:2]
    mine = z - d % 2
    is_home = (mine >= 0) & (mine < batch)
    up, down = 0, 1
    bufs = (reduce_refs[:6], reduce_refs[6:12])
    do_sum = reducer(teams, MLP_LEVELS, (up_ref, down_ref), (up_sum, down_sum), bufs, *reduce_refs[12:])

    @pl.when(step == 0)
    def _():
        do_sum.enter(down)
        do_sum.enter(up)
        greet(teams)
        do_sum.first(down)
        do_sum.first(up)
        do_sum.second(up)

    def o_copy(quad, k, i):
        to = (z + k) % ring
        src = stored_o_ref.at[quad, pl.ds(pl.multiple_of(to * piece, 16), piece), :]
        dst = ret_o.at[i, :, pl.ds(pl.multiple_of(quad * lanes, 128), lanes)]
        if k == 0:
            return pltpu.make_async_copy(src, dst, o_local.at[quad])
        return remote(src, dst, o_send.at[quad, k], o_recv.at[quad, i], d, to)

    def grad_copy(quad, j):
        at = pl.ds(pl.multiple_of(j * width + quad * lanes, 128), lanes)
        return pltpu.make_async_copy(grad_ref.at[quad, j], dqkv_all.at[:, at], grad_sem.at[quad, j])


    def stored(ref, at):
        values = ref[pl.ds(at * BLOCK, BLOCK), :]
        return jnp.where(is_home, values, jnp.zeros_like(values))

    @pl.when(step == 0)
    def _():
        for j in range(blocks):
            place = order_ref[1, j]
            at = pl.ds(j * BLOCK, BLOCK)
            xh, _ = normalized(stored(x_ref, place).astype(F32))
            a = xh * norm_ref[1:2, :] + norm_ref[2:3, :]
            a_ref[at, :] = a.astype(BF16)
            at_ref[:, at] = a.T.astype(BF16)
            g_ref[at, :] = stored(stored_g_ref, place)
        da_ref[...] = jnp.zeros_like(da_ref)

    def table(ref, at):
        values = ref[at, :]
        return jnp.concatenate([values] * (lanes // values.shape[1]), axis=1)

    def turn(values, at):
        low = pltpu.roll(values, lanes - half, 1) * table(low_ref, at)
        high = pltpu.roll(values, half, 1) * table(high_ref, at)
        return values * table(cos_ref, at), low + high

    for t in range(rows // tile):
        at = pl.ds(t * tile, tile)
        a = a_ref[at, :]
        same, cross = turn(dot(a, wq_ref[...]) + bias_ref[0:1, :], at)
        q_ref[at, :] = ((same + cross).astype(BF16) * scale).astype(BF16)
        same, cross = turn(dot(a, wk_ref[...]), at)
        keys = same + cross
        k_ref[at, :] = keys.astype(BF16)
        kt_ref[:, at] = keys.T.astype(BF16)
        values = dot(a, wv_ref[...])
        v_ref[at, :] = values.astype(BF16)
        vt_ref[:, at] = values.T.astype(BF16)
        mixed_back = dot(g_ref[at, :], wo_ref[...], NT)
        do_ref[at, :] = mixed_back.astype(BF16)

    dks_ref[...] = jnp.zeros_like(dks_ref)
    dvs_ref[...] = jnp.zeros_like(dvs_ref)
    wide = 2 * HD
    head_of = lax.broadcasted_iota(jnp.int32, (BLOCK, wide), 1) // HD

    def stack(values):
        zero = jnp.zeros_like(values)
        return jnp.concatenate([jnp.where(head_of == e, values, zero) for e in range(2)], axis=0)

    def diagonal(values):
        return jnp.concatenate([values[e * HD : (e + 1) * HD, e * BLOCK : (e + 1) * BLOCK] for e in range(2)], axis=0)

    spot = lax.broadcasted_iota(jnp.int32, (BLOCK, 2 * BLOCK), 1) % BLOCK
    admitted = lax.broadcasted_iota(jnp.int32, (BLOCK, 2 * BLOCK), 0) <= spot

    def products_in(b, p):
        at, seen, own = pl.ds(b * BLOCK, BLOCK), pl.ds(0, (b + 1) * BLOCK), pl.ds(p * wide, wide)
        q, do = stack(q_ref[at, own]), stack(do_ref[at, own])
        return q, do, dot(k_ref[seen, own], q, NT), dot(v_ref[seen, own], do, NT)

    def softmax(b, scores, back):
        edge = jnp.where(admitted, scores[b * BLOCK :], -1e30)
        scores = edge if b == 0 else jnp.concatenate([scores[: b * BLOCK], edge], axis=0)
        top = jnp.max(scores, axis=0, keepdims=True)
        expo = jnp.exp(scores - top)
        probs = expo * (1.0 / jnp.sum(expo, axis=0, keepdims=True))
        share = jnp.sum(probs * back, axis=0, keepdims=True)
        return probs.astype(BF16), (probs * (back - share)).astype(BF16)

    def products_out(b, p, q, do, low, back):
        at, seen, own = pl.ds(b * BLOCK, BLOCK), pl.ds(0, (b + 1) * BLOCK), pl.ds(p * wide, wide)
        mixed = diagonal(dot(vt_ref[own, seen], low))
        o_ref[at, own] = mixed.T.astype(BF16)
        dqs_ref[at, own] = diagonal(dot(kt_ref[own, seen], back)).T * scale
        dks_ref[seen, own] += dot(back, q)
        dvs_ref[seen, own] += dot(low, do)

    units = [(b, p) for b in range(rows // BLOCK) for p in range(lanes // wide)]
    ready = products_in(*units[0])
    done = None
    for n, (b, p) in enumerate(units):
        q, do, scores, back = ready
        if n + 1 < len(units):
            ready = products_in(*units[n + 1])
        low, back = softmax(b, scores, back)
        if done is not None:
            products_out(*done)
        done = (b, p, q, do, low, back)
    products_out(*done)

    total = jnp.zeros((1, lanes), F32)
    for t in range(rows // tile):
        at = pl.ds(t * tile, tile)
        same, cross = turn(dqs_ref[at, :], at)
        dq = (same - cross).astype(BF16)
        same, cross = turn(dks_ref[at, :], at)
        dk = (same - cross).astype(BF16)
        dv = dvs_ref[at, :].astype(BF16)
        total += jnp.sum(dq.astype(F32), axis=0, keepdims=True)
        q_ref[at, :] = dq
        k_ref[at, :] = dk
        v_ref[at, :] = dv
        da_ref[at, :] += dot(dq, wq_ref[...], NT) + dot(dk, wk_ref[...], NT) + dot(dv, wv_ref[...], NT)
    small_ref[2:3, pl.ds(pl.multiple_of(step * lanes, 128), lanes)] = total
    for j, ref in enumerate((q_ref, k_ref, v_ref)):
        grad_ref[step, j] = dot(at_ref[...], ref[...]).astype(BF16)
        grad_copy(step, j).start()
    for s in range(blocks):
        stored_o_ref[step, s * BLOCK : (s + 1) * BLOCK, :] = o_ref[pl.ds(order_ref[0, s] * BLOCK, BLOCK), :]

    for i in range(batch):
        @pl.when((mine == i) & (step < last))
        def _(i=i):
            for k in range(ring):
                o_copy(step, k, i).start()

    @pl.when(step == 0)
    def _():
        do_sum.second(down)
        do_sum.to_owner(up)

    @pl.when(step == 1)
    def _():
        do_sum.to_owner(down)

    @pl.when(step == last)
    def _():
        gain = jnp.zeros((1, width), F32)
        shift = jnp.zeros((1, width), F32)
        for s in range(blocks):
            at = pl.ds(s * BLOCK, BLOCK)
            sorted_at = pl.ds(order_ref[0, s] * BLOCK, BLOCK)
            xh, _ = normalized(stored(x_ref, s).astype(F32))
            da = da_ref[sorted_at, :]
            gain += jnp.sum(da * xh, axis=0, keepdims=True)
            shift += jnp.sum(da, axis=0, keepdims=True)
            h_ref[at, :] = (da * norm_ref[1:2, :]).astype(BF16)
        small_ref[0:1, :] = gain
        small_ref[1:2, :] = shift
        small_ref[3:8, :] = jnp.zeros((5, width), F32)
        out = pltpu.make_async_copy(stored_o_ref.at[last], o_last, o_local.at[last])
        out.start()
        do_sum.hand_on(up)
        do_sum.hand_on(down)
        for quad in range(last):
            for i in range(batch):
                @pl.when(mine != i)
                def _(quad=quad, i=i):
                    ref = ret_o.at[i, :, pl.ds(quad * lanes, lanes)]
                    remote(ref, ref, o_send.at[quad, 0], o_recv.at[quad, i], core_id, z).wait_recv()

                @pl.when(mine == i)
                def _(quad=quad, i=i):
                    o_copy(quad, 0, i).wait()
                    for k in range(1, ring):
                        o_copy(quad, k, i).wait_send()
        for quad in range(last + 1):
            for j in range(3):
                grad_copy(quad, j).wait()
        out.wait()


def attend(order, x, g, norms, bias_q, tables, weights, up, down, batch):
    ring, groups_dp = lax.axis_size("ctx"), lax.axis_size("dp")
    teams = (groups_dp // 8).bit_length() - 1
    shapes = ((1, 2 * up.shape[1], 2 * up.shape[2]), (down.shape[1], down.shape[2], 2 * down.shape[3]))
    down = down.reshape(-1, *down.shape[2:])
    rows, width = x.shape
    lanes = QUAD * HD
    groups = width // lanes
    anywhere = pl.BlockSpec(memory_space=pl.ANY)
    whole = lambda shape: pl.BlockSpec(shape, lambda i: (0,) * len(shape))
    once = lambda shape: pl.BlockSpec(shape, lambda i: (0,) * len(shape), pipeline_mode=pl.Buffered(1))
    dma = pltpu.SemaphoreType.DMA
    slices = [(n, r // 4, c // 2) for n, r, c in shapes]
    return pl.pallas_call(
        functools.partial(attend_kernel, teams),
        grid=(groups,),
        in_specs=[
            pl.BlockSpec(memory_space=pltpu.SMEM),
            once((rows, width)),
            once((rows, width)),
            once(norms.shape),
            pl.BlockSpec((8, lanes), lambda i: (0, i)),
            once(tables[0].shape),
            once(tables[0].shape),
            once(tables[0].shape),
            pl.BlockSpec((width, lanes), lambda i: (0, i)),
            pl.BlockSpec((width, lanes), lambda i: (0, groups + i)),
            pl.BlockSpec((width, lanes), lambda i: (0, 2 * groups + i)),
            pl.BlockSpec((lanes, width), lambda i: (i, 3)),
            anywhere,
            anywhere,
        ],
        out_specs=[once((rows, width)), anywhere, once((8, width))] + [anywhere] * 4,
        out_shape=[
            jax.ShapeDtypeStruct((rows, width), BF16),
            jax.ShapeDtypeStruct((width, 3 * width), BF16),
            jax.ShapeDtypeStruct((8, width), F32),
            jax.ShapeDtypeStruct((rows, lanes), BF16),
            jax.ShapeDtypeStruct((batch, rows // ring, width - lanes), BF16),
        ]
        + [jax.ShapeDtypeStruct(shape, BF16) for shape in slices],
        scratch_shapes=[
            pltpu.VMEM((rows, width), BF16),
            pltpu.VMEM((rows, width), BF16),
            pltpu.VMEM((width, rows), BF16),
            pltpu.VMEM((rows, width), F32),
        ]
        + [pltpu.VMEM((rows, lanes), BF16)] * 5
        + [pltpu.VMEM((lanes, rows), BF16)] * 2
        + [pltpu.VMEM((rows, lanes), F32)] * 3
        + [
            pltpu.VMEM((groups, 3, width, lanes), BF16), pltpu.VMEM((groups, rows, lanes), BF16),
            dma((groups, ring)), dma((groups, batch)), dma((groups,)), dma((groups, 3)),
        ]
        + reducer_scratch(MLP_LEVELS, shapes, teams, ring),
        compiler_params=pltpu.CompilerParams(
            collective_id=2, has_side_effects=True, vmem_limit_bytes=60 * MIB
        ),
        cost_estimate=pl.CostEstimate(
            flops=24 * rows * width * width + 8 * rows * rows * width,
            bytes_accessed=16 * width * width + 8 * rows * width,
            transcendentals=HEADS * rows * rows // 2,
        ),
        name="attend",
    )(order, x, g, norms, bias_q, *tables, weights, weights, weights, weights, up, down)


def rotary_tables(length):
    half = ROT // 2
    frequency = ROPE_BASE ** (-(np.arange(half) * 2.0 / ROT))
    angle = np.arange(length)[:, None] * frequency[None, :]
    cosine, sine = np.cos(angle), np.sin(angle)
    rest = np.zeros((length, HD - ROT))
    none = np.zeros_like(sine)
    cos_full = np.concatenate([cosine, cosine, rest + 1.0], axis=1)
    low = np.concatenate([-sine, none, rest], axis=1)
    high = np.concatenate([none, sine, rest], axis=1)
    return tuple(jnp.asarray(np.tile(t, (1, 2)).astype(np.float32)) for t in (cos_full, low, high))


def adamw(weight, grad, first, second, rate, decay):
    first_new = BETA_ONE * first + (1.0 - BETA_ONE) * grad
    second_new = BETA_TWO * second + (1.0 - BETA_TWO) * grad * grad
    first_hat = first_new / (1.0 - BETA_ONE**STEP)
    second_hat = second_new / (1.0 - BETA_TWO**STEP)
    weight_new = weight - rate * (first_hat / (jnp.sqrt(second_hat) + EPS_ADAM) + decay * weight)
    return (first_new, second_new, weight_new)


def shards(
    tokens, out_grad, block_order, qkv_weight, out_weight, up_weight, down_weight, norm_params, bias_params,
    qkv_first, qkv_second, out_first, out_second, up_first, up_second, down_first, down_second,
    norm_first, norm_second, bias_first, bias_second,
):
    groups, ring = lax.axis_size("dp"), lax.axis_size("ctx")
    group, rank = lax.axis_index("dp"), lax.axis_index("ctx")
    batch, piece, width = tokens.shape
    length = piece * ring
    count = batch * piece
    ff = up_weight.shape[1]

    share = bias_params.shape[0]
    lanes = share + -share % 128
    small = jnp.concatenate([
        jnp.pad(bias_params[None, :], ((0, 0), (0, lanes - share))),
        jnp.pad(norm_params, ((0, 3), (0, lanes - norm_params.shape[1]))),
    ])
    x_rows, g_rows = tokens.reshape(count, width), out_grad.reshape(count, width)
    att_copy, biases, norms, home_x, home_g, feed_out, h_feed, dup, ddown, dbias_up, small_feed = gather_feed(
        up_weight, down_weight, qkv_weight, out_weight, small, x_rows, g_rows, piece, ring * share
    )

    odd = group % 2

    order = block_order[jnp.clip(rank - odd, 0, batch - 1)]
    spots = jnp.arange(order.shape[0])
    order = jnp.stack([order, jnp.sum(jnp.where(order[None, :] == spots[:, None], spots[None, :], 0), axis=1)])

    h_attend, dqkv, small_attend, o_last, o_first, up_slice, down_slice = attend(
        order, home_x, home_g, norms, biases, rotary_tables(length), att_copy, dup, ddown, batch
    )
    *owned, tail, attend_out, ret_back = reduce_all(
        up_slice, down_slice, dqkv, small_attend, small_feed, dbias_up, h_attend, o_last, o_first, g_rows, att_copy, batch
    )
    up_grad, down_grad, qkv_grad, out_grads = (
        g.reshape(w.shape).astype(F32)
        for g, w in zip(owned, (up_weight, down_weight, qkv_weight, out_weight))
    )

    rows = x_rows.astype(F32)
    bias_rows = biases[0:1, width : 2 * width] + biases[0:1, 2 * width + ff :]
    layer_out = (rows + attend_out + feed_out + bias_rows).astype(BF16).reshape(batch, piece, width)
    xh, scale = normalized(rows)
    h = ret_back.reshape(count, width).astype(F32) + h_feed
    inner = jnp.mean(h * xh, axis=-1, keepdims=True)
    input_grad = g_rows.astype(F32) + scale * (h - jnp.mean(h, axis=-1, keepdims=True) - xh * inner)
    input_grad = input_grad.reshape(batch, piece, width)

    norm_grad = jnp.concatenate([tail[0:2], tail[8:10]])
    norm_grad = lax.dynamic_slice_in_dim(norm_grad, rank * (width // ring), width // ring, 1)
    bias_grad = jnp.concatenate([tail[2], tail[10], tail[16 : 16 + ff // width].reshape(-1), tail[10]])
    bias_grad = lax.dynamic_slice_in_dim(bias_grad, rank * share, share, 0)

    qkv_new = adamw(qkv_weight, qkv_grad, qkv_first, qkv_second, 0.1, DECAY)
    out_new = adamw(out_weight, out_grads, out_first, out_second, 0.6, DECAY)
    up_new = adamw(up_weight, up_grad, up_first, up_second, 0.1, DECAY)
    down_new = adamw(down_weight, down_grad, down_first, down_second, 0.05, DECAY)
    norm_new = adamw(norm_params, norm_grad, norm_first, norm_second, 0.6, 0.0)
    bias_new = adamw(bias_params, bias_grad, bias_first, bias_second, 0.6, 0.0)
    return (
        layer_out, input_grad, *qkv_new, *out_new, *up_new, *down_new,
        norm_new[0], norm_new[1][:2], norm_new[1][2:], norm_new[2], *bias_new,
    )


def solution(mesh):
    rows, columns, token = P("ctx", None), P(None, "ctx"), P("dp", "ctx", None)
    in_specs = (token, token, P("dp", None)) + (rows,) * 4 + (columns, P("ctx")) + (rows,) * 8
    in_specs += (columns, columns, P("ctx"), P("ctx"))
    out_specs = (token, token) + (rows,) * 12 + (columns,) * 4 + (P("ctx"),) * 3
    return jax.shard_map(shards, mesh=mesh, in_specs=in_specs, out_specs=out_specs, check_vma=False)
```

```python
import functools
import math
from types import SimpleNamespace

import jax
import jax.numpy as jnp
import numpy as np
from jax import lax
from jax.experimental import pallas as pl
from jax.experimental.pallas import tpu as pltpu
from jax.sharding import PartitionSpec as P

HEADS = 12
HD = 64
STEP = 10
ROT = 16
BLOCK = 128
QUAD = 4
MLP_LEVELS = (2, 1)
LEVELS = (3, 3, 0, 0)

EPS_NORM = 1e-05
BETA_ONE = 0.9
BETA_TWO = 0.95
EPS_ADAM = 1e-08
DECAY = 0.01
ROPE_BASE = 10000.0
F32 = jnp.float32
BF16 = jnp.bfloat16
MIB = 1024 * 1024


def dot(left, right, dims=((1,), (0,))):
    return lax.dot_general(left, right, (dims, ((), ())), preferred_element_type=F32)


NN = ((1,), (0,))
NT = ((1,), (1,))
TN = ((0,), (0,))


def normalized(values):
    mean = jnp.mean(values, axis=-1, keepdims=True)
    centred = values - mean
    variance = jnp.mean(centred * centred, axis=-1, keepdims=True)
    scale = lax.rsqrt(variance + EPS_NORM)
    return centred * scale, scale


MESH = pl.DeviceIdType.MESH


def plane(d):
    core, x, y = d % 2, d // 2 % 2, d // 4 % 2
    return core, x, y, d + 1 - 2 * core, d + 2 - 4 * x, d + 4 - 8 * y


def gather_kernel(
    up, down, qkv, out, small, tokens, cotangents,
    att_all, small_all, norm_all, home_x, home_g, out_ref, h_ref, up_part, down_part, dbias_ref, sums_ref,
    up_all, down_all, att_own, up_wide, down_wide, att_wide, small_in, x_ref, g_ref, m_ref, mt_ref, hid_ref, dup_in_ref,
    dup_ref, up_core, up_first, ddown_ref, down_core,
    z_send, z_recv, p_send, p_recv, s_send, s_recv, t_send, t_recv, local, out_sem, c_send, c_recv,
):
    ring = lax.axis_size("ctx")
    d, z = lax.axis_index("dp"), lax.axis_index("ctx")
    core, x, y, core_id, x_id, y_id = plane(d)
    own = x + 2 * y
    own_x, own_y, far = own + 1 - 2 * x, own + 2 - 4 * y, 3 - own
    count, width = tokens.shape
    piece = home_x.shape[0] // ring
    batch = count // piece
    arrays = ((up_wide, up_all, False), (down_wide, down_all, True), (att_own, att_all, False))

    def slot(a, base, place, half=None):
        source, whole, tall = arrays[a]
        ref = source if base is None else whole
        rows, columns = source.shape
        at = 0 if base is None else base * rows
        height, span = rows // 4, columns // 2
        at = at + place * height
        column = core * span
        if half is not None:
            if tall:
                height = height // 2
                at = at + half * height
            else:
                span = span // 2
                column = column + half * span
        return ref.at[pl.ds(pl.multiple_of(at, 16), height), pl.ds(pl.multiple_of(column, 128), span)]

    def other_slot(a, base, place):
        source, whole, tall = arrays[a]
        rows, columns = source.shape
        at = pl.multiple_of(base * rows + place * (rows // 4), 16)
        column = pl.multiple_of((1 - core) * (columns // 2), 128)
        return whole.at[pl.ds(at, rows // 4), pl.ds(column, columns // 2)]

    def remote(src, dst, send, recv, dp, ctx):
        return pltpu.make_async_remote_copy(
            src_ref=src, dst_ref=dst, send_sem=send, recv_sem=recv, device_id=(dp, ctx), device_id_type=MESH
        )

    columns = qkv.shape[1]
    wide_loads = [
        [pltpu.make_async_copy(up, up_wide, local.at[0])],
        [pltpu.make_async_copy(down, down_wide, local.at[1])],
        [
            pltpu.make_async_copy(qkv, att_wide.at[:, pl.ds(0, columns)], local.at[2]),
            pltpu.make_async_copy(out, att_wide.at[:, pl.ds(columns, out.shape[1])], local.at[8]),
        ],
    ]
    for loads in wide_loads:
        for copy in loads:
            copy.start()

    def cast_own(a):
        for copy in wide_loads[a]:
            copy.wait()
        wide, target = ((up_wide, up_all), (down_wide, down_all), (att_wide, att_own))[a]
        rows = wide.shape[0]
        tile = 64
        base = 0 if a == 2 else z * rows

        def body(t, _):
            value = wide[pl.ds(pl.multiple_of(t * tile, 16), tile), :].astype(BF16)
            target[pl.ds(pl.multiple_of(base + t * tile, 16), tile), :] = value
            return 0

        lax.fori_loop(0, rows // tile, body, 0)

    barrier = pltpu.get_barrier_semaphore()
    for k in range(1, ring):
        pl.semaphore_signal(barrier, inc=1, device_id=(d, (z + k) % ring), device_id_type=MESH)
    for other in (core_id, x_id, y_id):
        pl.semaphore_signal(barrier, inc=1, device_id=(other, z), device_id_type=MESH)
    cast_own(0)
    pl.semaphore_wait(barrier, ring + 2)

    def hop(a, way, h):
        shard = z - h if way == 0 else z + h
        target = z + 1 if way == 0 else z - 1
        src = slot(a, None, own) if h == 0 and a == 2 else slot(a, shard, own)
        return remote(src, slot(a, shard, own), z_send.at[a, way, h], z_recv.at[a, way, h], d, target)

    def can_send(way, h):
        shard = z - h if way == 0 else z + h
        target = z + 1 if way == 0 else z - 1
        return (shard >= 0) & (shard < ring) & (target >= 0) & (target < ring)

    def in_range(way, h):
        shard = z - h if way == 0 else z + h
        return (shard >= 0) & (shard < ring)

    def cast(a, shard, j):
        send, recv = p_send.at[a, shard, j], p_recv.at[a, shard, j]
        if j == 0:
            ref = slot(a, shard, own)
            return remote(ref, ref, send, recv, x_id, z)
        if j == 1:
            ref = slot(a, shard, own)
            return remote(ref, ref, send, recv, y_id, z)
        if j == 2:
            ref = slot(a, shard, own_x, 0)
            return remote(ref, ref, send, recv, y_id, z)
        if j == 3:
            ref = slot(a, shard, own_y, 1)
            return remote(ref, ref, send, recv, x_id, z)
        ref = slot(a, shard, (own, own_x, own_y, far)[j - 4])
        return remote(ref, ref, send, recv, core_id, z)

    def arrived(a, shard, j):
        send, recv = p_send.at[a, shard, j], p_recv.at[a, shard, j]
        ref = {0: lambda: slot(a, shard, own_x), 1: lambda: slot(a, shard, own_y),
               2: lambda: slot(a, shard, far, 0), 3: lambda: slot(a, shard, far, 1)}.get(
            j, lambda: other_slot(a, shard, (own, own_x, own_y, far)[j - 4]))()
        remote(ref, ref, send, recv, core_id, z).wait_recv()

    def start_hops(a):
        for way in range(2):
            @pl.when(can_send(way, 0))
            def _(way=way):
                hop(a, way, 0).start()

    def small_copy(k):
        return remote(small, small_in.at[z], s_send.at[k], s_recv.at[k], d, (z + k) % ring)

    def stage_a(a, h):
        for way in range(2):
            @pl.when(in_range(way, h))
            def _(way=way):
                shard = z - h if way == 0 else z + h
                ref = slot(a, shard, own)
                remote(ref, ref, z_send.at[a, way, h - 1], z_recv.at[a, way, h - 1], core_id, z).wait_recv()

                @pl.when(can_send(way, h))
                def _():
                    hop(a, way, h).start()

                cast(a, shard, 0).start()
                cast(a, shard, 1).start()
                cast(a, shard, 4).start()

    def stage_b(a, h):
        for way in range(2):
            @pl.when(in_range(way, h))
            def _(way=way):
                shard = z - h if way == 0 else z + h
                arrived(a, shard, 0)
                cast(a, shard, 2).start()
                cast(a, shard, 5).start()
                arrived(a, shard, 1)
                cast(a, shard, 3).start()
                cast(a, shard, 6).start()

    def stage_c(a, h):
        for way in range(2):
            @pl.when(in_range(way, h))
            def _(way=way):
                shard = z - h if way == 0 else z + h
                arrived(a, shard, 2)
                arrived(a, shard, 3)
                cast(a, shard, 7).start()

    def stage_d(a, h):
        for way in range(2):
            @pl.when(in_range(way, h))
            def _(way=way):
                shard = z - h if way == 0 else z + h
                for j in range(4, 8):
                    arrived(a, shard, j)

    pairs = ((tokens, home_x), (cotangents, home_g))

    def move(which, i):
        source, whole = pairs[which]
        src = source.at[pl.ds(i * piece, piece), :]
        dst = whole.at[pl.ds(pl.multiple_of(z * piece, 16), piece), :]
        return src, dst, i + core

    def start_moves(which):
        for i in range(batch):
            src, dst, target = move(which, i)

            @pl.when(target != z)
            def _(src=src, dst=dst, target=target, i=i):
                remote(src, dst, t_send.at[which, i], t_recv.at[which, z], d, target).start()

            @pl.when(target == z)
            def _(src=src, dst=dst):
                pltpu.make_async_copy(src, dst, local.at[6 + which]).start()

    own_rows = pl.ds(pl.multiple_of(z * att_own.shape[0], 16), att_own.shape[0])
    own_att = pltpu.make_async_copy(att_own, att_all.at[own_rows, :], local.at[9])
    x_load = pltpu.make_async_copy(tokens, x_ref, local.at[3])
    g_load = pltpu.make_async_copy(cotangents, g_ref, local.at[4])
    own_small = pltpu.make_async_copy(small, small_in.at[z], local.at[5])

    start_hops(0)
    cast_own(1)
    start_hops(1)
    cast_own(2)
    start_hops(2)
    for k in range(1, ring):
        small_copy(k).start()
    for copy in (own_att, x_load, g_load, own_small):
        copy.start()
    hops = range(1, ring)
    work = [(a, h) for a in range(2) for h in hops]
    for n in range(len(work) + 2):
        if n < len(work):
            stage_a(*work[n])
        if n == len(work) - 1:
            start_moves(0)
        if 1 <= n <= len(work):
            stage_b(*work[n - 1])
        if n >= 2:
            stage_c(*work[n - 2])
    stage_a(2, 1)

    own_small.wait()
    for k in range(1, ring):
        ref = small_in.at[(z + ring - k) % ring]
        remote(ref, ref, s_send.at[k], s_recv.at[k], core_id, z).wait_recv()
    x_load.wait()
    g_load.wait()
    entries = small_all.shape[1]
    biases = jnp.zeros((8, entries), F32)
    norms = jnp.zeros((8, width), F32)
    for r in range(ring):
        block = small_in[r].astype(BF16).astype(F32)
        full = jnp.concatenate([block, jnp.zeros((8, entries - block.shape[1]), F32)], axis=1)
        biases += pltpu.roll(full, r * (entries // ring), 1) if r else full
        norms += pltpu.roll(block[:, :width], r * (width // ring), 1) if r else block[:, :width]
    small_all[...] = biases
    norm_all[...] = norms
    ff = up_all.shape[1]
    gain_2, shift_2 = norm_all[3:4, :], norm_all[4:5, :]
    tile = 256
    tiles = count // tile
    for t in range(tiles):
        at = pl.ds(t * tile, tile)
        xh, _ = normalized(x_ref[at, :].astype(F32))
        m = xh * gain_2 + shift_2
        m_ref[at, :] = m.astype(BF16)
        mt_ref[:, at] = m.T.astype(BF16)
        out_ref[at, :] = jnp.zeros((tile, width), F32)
        h_ref[at, :] = jnp.zeros((tile, width), F32)
    for h in hops:
        stage_d(0, h)
        stage_d(1, h)

    strip = dup_ref.shape[3] // ring
    steps = ff // (ring * strip)
    half = ring // 2
    big, by_core = (dup_ref, ddown_ref), (up_core, down_core)
    bits, ids = ((x, y), (y, x)), ((x_id, y_id), (y_id, x_id))

    def sizes(a):
        return by_core[a].shape[2], by_core[a].shape[3]

    def slice_of(order):
        return 2 * bits[order][0] + bits[order][1]

    def core_copy(a, i):
        _, span = sizes(a)
        away = pl.ds(pl.multiple_of((1 - core) * span, 128), span)
        return remote(big[a].at[i, :, :, away], by_core[a].at[i], c_send.at[a, i, 0], c_recv.at[a, i, 0], core_id, z)

    def first_copy(a, i, order):
        height, _ = sizes(a)
        own = pl.ds(order * half, half)
        away = pl.ds(pl.multiple_of((1 - bits[order][0]) * (height // 2), 16), height // 2)
        return remote(
            by_core[a].at[i, own, away, :], up_first.at[i, own], c_send.at[a, i, 1 + order],
            c_recv.at[a, i, 1 + order], ids[order][0], z,
        )

    def add(into, at, term, owners):
        height = term(0).shape[0]
        tile = 32 if height % 48 else 48

        def body(n, _):
            o, t = n // (height // tile), n % (height // tile)
            spot = pl.ds(pl.multiple_of(at + t * tile, 16), tile)
            value = term(o)[pl.ds(pl.multiple_of(t * tile, 16), tile), :]
            into[o, spot, :] = (into[o, spot, :].astype(F32) + value.astype(F32)).astype(BF16)
            return 0

        lax.fori_loop(0, owners * (height // tile), body, 0)

    def chunk_1(i):
        for a in range(2):
            _, span = sizes(a)
            core_copy(a, i).wait_recv()
            keep = pl.ds(pl.multiple_of(core * span, 128), span)
            add(by_core[a].at[i], 0, lambda o: big[a].at[i, o, :, keep], ring)
        for order in range(2):
            first_copy(0, i, order).start()
        parts_out(1, i)[0].start()

    def chunk_2(i):
        height, _ = sizes(0)
        for order in range(2):
            own = pl.ds(order * half, half)
            first_copy(0, i, order).wait_recv()
            at = bits[order][0] * (height // 2)
            add(by_core[0].at[i, own], at, lambda o: up_first.at[i, order * half + o], half)
        for copy in parts_out(0, i):
            copy.start()

    def parts_out(a, i):
        height, span = sizes(a)
        if a == 1:
            return [pltpu.make_async_copy(by_core[1].at[i], down_part.at[:, i], out_sem.at[i, 2 * half])]
        copies = []
        for order in range(2):
            own = pl.ds(order * half, half)
            rows = pl.ds(pl.multiple_of(bits[order][0] * (height // 2), 16), height // 2)
            for n in range(half):
                copies.append(pltpu.make_async_copy(
                    by_core[0].at[i, own, rows, pl.ds(n * strip, strip)],
                    up_part.at[own, :, pl.ds(pl.multiple_of(n * steps * strip + i * strip, 128), strip)],
                    out_sem.at[i, half * order + n],
                ))
        return copies

    def feed_step(step, _):
        for h in hops:
            @pl.when(step == h - 1)
            def _(h=h):
                if h + 1 < ring:
                    stage_a(2, h + 1)
                if h == ring - 2:
                    start_moves(1)
                stage_b(2, h)

            @pl.when(step == h)
            def _(h=h):
                stage_c(2, h)

        @pl.when(step < steps)
        def _():
            spots = [pl.ds(pl.multiple_of(r * (ff // ring) + step * strip, 128), strip) for r in range(ring)]
            bias_spots = [
                pl.ds(pl.multiple_of(2 * width + r * (ff // ring) + step * strip, 128), strip) for r in range(ring)
            ]
            up_part_ = jnp.concatenate([up_all[:, at] for at in spots], axis=1)
            down_part_ = jnp.concatenate([down_all[at, :] for at in spots], axis=0)
            bias = jnp.concatenate([small_all[0:1, at] for at in bias_spots], axis=1)
            total = jnp.zeros((1, ring * strip), F32)
            for t in range(tiles):
                at = pl.ds(t * tile, tile)
                u = dot(m_ref[at, :], up_part_) + bias
                cdf = 0.5 * (1.0 + lax.erf(u * (1.0 / math.sqrt(2.0))))
                hidden = (u * cdf).astype(BF16)
                slope = cdf + u * jnp.exp(-0.5 * u * u) * (1.0 / math.sqrt(2.0 * math.pi))
                back = (dot(g_ref[at, :], down_part_, NT) * slope).astype(BF16)
                hid_ref[at, :] = hidden
                dup_in_ref[at, :] = back
                total += jnp.sum(back.astype(F32), axis=0, keepdims=True)
                out_ref[at, :] += dot(hidden, down_part_)
                h_ref[at, :] += dot(back, up_part_, NT)
            for r in range(ring):
                dbias_ref[0:1, spots[r]] = total[:, r * strip : (r + 1) * strip]
            ddown = dot(hid_ref[...], g_ref[...], TN).astype(BF16)
            dup = dot(mt_ref[...], dup_in_ref[...]).astype(BF16)
            for r in range(ring):
                ddown_ref[step, r] = ddown[r * strip : (r + 1) * strip, :]
                dup_ref[step, r] = dup[r * (width // ring) : (r + 1) * (width // ring), :]
            core_copy(0, step).start()
            core_copy(1, step).start()

        for lag, stage in ((1, chunk_1), (3, chunk_2)):
            @pl.when((step >= lag) & (step < steps + lag))
            def _(lag=lag, stage=stage):
                stage(step - lag)

        return 0

    lax.fori_loop(0, steps + 3, feed_step, 0)

    gain = jnp.zeros((1, width), F32)
    shift = jnp.zeros((1, width), F32)
    sums = jnp.zeros((1, width), F32)
    for t in range(tiles):
        at = pl.ds(t * tile, tile)
        xh, _ = normalized(x_ref[at, :].astype(F32))
        dm = h_ref[at, :]
        gain += jnp.sum(dm * xh, axis=0, keepdims=True)
        shift += jnp.sum(dm, axis=0, keepdims=True)
        sums += jnp.sum(g_ref[at, :].astype(F32), axis=0, keepdims=True)
        h_ref[at, :] = dm * gain_2
    sums_ref[...] = jnp.concatenate([gain, shift, sums, jnp.zeros((5, width), F32)], axis=0)

    mine = z - core
    for which in range(2):
        for k in range(1, ring):
            @pl.when((mine >= 0) & (mine < batch))
            def _(which=which, k=k):
                other = (z + k) % ring
                ref = pairs[which][1].at[pl.ds(pl.multiple_of(other * piece, 16), piece), :]
                remote(ref, ref, t_send.at[which, 0], t_recv.at[which, other], core_id, z).wait_recv()
    for h in hops:
        stage_d(2, h)
    for k in range(1, ring):
        small_copy(k).wait_send()
    for a in range(3):
        for way in range(2):
            for h in range(ring - 1):
                @pl.when(can_send(way, h))
                def _(a=a, way=way, h=h):
                    hop(a, way, h).wait_send()
        for h in hops:
            for way in range(2):
                @pl.when(in_range(way, h))
                def _(a=a, h=h, way=way):
                    shard = z - h if way == 0 else z + h
                    for j in range(8):
                        cast(a, shard, j).wait_send()
    for which in range(2):
        for i in range(batch):
            src, dst, target = move(which, i)

            @pl.when(target != z)
            def _(src=src, dst=dst, target=target, which=which, i=i):
                remote(src, dst, t_send.at[which, i], t_recv.at[which, z], d, target).wait_send()

            @pl.when(target == z)
            def _(src=src, dst=dst, which=which):
                pltpu.make_async_copy(src, dst, local.at[6 + which]).wait()
    own_att.wait()

    def close(i, _):
        for a in range(2):
            core_copy(a, i).wait_send()
            for copy in parts_out(a, i):
                copy.wait()
        for order in range(2):
            first_copy(0, i, order).wait_send()
        return 0

    lax.fori_loop(0, steps, close, 0)


def gather_feed(up, down, qkv, out, small, tokens, cotangents, piece, entries):
    ring = lax.axis_size("ctx")
    count, width = tokens.shape
    ff = up.shape[1]
    strip = 128
    chunk = ring * strip
    steps = ff // chunk
    shard = up.shape[0]
    columns = qkv.shape[1] + out.shape[1]
    home = jax.ShapeDtypeStruct((ring * piece, width), tokens.dtype)
    rows = jax.ShapeDtypeStruct((count, width), F32)
    dma = pltpu.SemaphoreType.DMA
    anywhere = pl.BlockSpec(memory_space=pl.ANY)
    vmem = pl.BlockSpec(memory_space=pltpu.VMEM)
    return pl.pallas_call(
        gather_kernel,
        in_specs=[anywhere] * 7,
        out_specs=[anywhere, vmem, vmem, anywhere, anywhere, vmem, vmem, anywhere, anywhere, vmem, vmem],
        out_shape=[
            jax.ShapeDtypeStruct((ring * shard, columns), BF16),
            jax.ShapeDtypeStruct((8, entries), F32), jax.ShapeDtypeStruct((8, width), F32), home, home, rows, rows,
            jax.ShapeDtypeStruct((ring, shard // 2, ff // 2), BF16),
            jax.ShapeDtypeStruct((ring, steps, strip, width // 2), BF16),
            jax.ShapeDtypeStruct((8, ff), F32), jax.ShapeDtypeStruct((8, width), F32),
        ],
        scratch_shapes=[
            pltpu.VMEM((ring * shard, ff), BF16), pltpu.VMEM((ring * down.shape[0], width), BF16),
            pltpu.VMEM((shard, columns), BF16),
            pltpu.VMEM(up.shape, F32), pltpu.VMEM(down.shape, F32), pltpu.VMEM((shard, columns), F32),
            pltpu.VMEM((ring, *small.shape), F32),
            pltpu.VMEM((count, width), BF16), pltpu.VMEM((count, width), BF16), pltpu.VMEM((count, width), BF16),
            pltpu.VMEM((width, count), BF16),
            pltpu.VMEM((count, chunk), BF16), pltpu.VMEM((count, chunk), BF16),
            pltpu.VMEM((steps, ring, shard, chunk), BF16), pltpu.VMEM((steps, ring, shard, chunk // 2), BF16),
            pltpu.VMEM((steps, ring, shard // 2, chunk // 2), BF16),
            pltpu.VMEM((steps, ring, strip, width), BF16), pltpu.VMEM((steps, ring, strip, width // 2), BF16),
            dma((3, 2, ring)), dma((3, 2, ring)), dma((3, ring, 8)), dma((3, ring, 8)),
            dma((ring,)), dma((ring,)), dma((2, count // piece)), dma((2, ring)), dma((10,)), dma((steps, ring + 1)),
            dma((2, steps, 3)), dma((2, steps, 3)),
        ],
        compiler_params=pltpu.CompilerParams(
            collective_id=0, has_side_effects=True, vmem_limit_bytes=60 * MIB
        ),
        cost_estimate=pl.CostEstimate(
            flops=12 * count * width * ff, bytes_accessed=60 * MIB, transcendentals=count * ff
        ),
        name="gather_feed",
    )(up, down, qkv, out, small, tokens, cotangents)


def remote(src, dst, send_sem, recv_sem, dp, ctx):
    return pltpu.make_async_remote_copy(
        src_ref=src, dst_ref=dst, send_sem=send_sem, recv_sem=recv_sem, device_id=(dp, ctx), device_id_type=MESH
    )


def team_id(d, t):
    return d + (8 << t) * (1 - 2 * (d // (8 << t) % 2))


def greet(teams):
    ring = lax.axis_size("ctx")
    d, z = lax.axis_index("dp"), lax.axis_index("ctx")
    core, x, y, core_id, x_id, y_id = plane(d)
    barrier = pltpu.get_barrier_semaphore()
    partners = [core_id, x_id, y_id, x_id + y_id - d] + [team_id(d, t) for t in range(teams)]
    for k in range(1, ring):
        pl.semaphore_signal(barrier, inc=1, device_id=(d, (z + k) % ring), device_id_type=MESH)
    for other in partners:
        pl.semaphore_signal(barrier, inc=1, device_id=(other, z), device_id_type=MESH)
    pl.semaphore_wait(barrier, ring - 1 + len(partners))


def reducer(teams, levels, ins, sums, bufs, send, recv, load):
    count = len(ins)
    ring = lax.axis_size("ctx")
    d, z = lax.axis_index("dp"), lax.axis_index("ctx")
    core, x, y, core_id, x_id, y_id = plane(d)
    far_id = x_id + y_id - d
    bits, ids = ((x, y), (y, x)), ((x_id, y_id), (y_id, x_id))
    spots = ((x, y), (1 - x, y), (x, 1 - y), (1 - x, 1 - y))

    def sizes(a):
        _, strips, quarter, span = bufs[a][-1].shape
        return strips, quarter, span

    def owners(a, order):
        strips = sizes(a)[0]
        return pl.ds(order * ring // 2 * strips, ring // 2 * strips)

    def rows_at(at, height):
        return pl.ds(pl.multiple_of(at, 16), height)

    def kept(a, order):
        return 0 if levels[a] == 2 else bits[order][0] * 2 * sizes(a)[1]

    def core_copy(a):
        span = sizes(a)[2]
        away = pl.ds(pl.multiple_of((1 - core) * span, 128), span)
        return remote(ins[a].at[:, :, away], bufs[a][1], send.at[a, 0], recv.at[a, 0], core_id, z)

    def own_load(a):
        if levels[a] == 3:
            return pltpu.make_async_copy(ins[a], bufs[a][5].at[0], load.at[a])
        span = sizes(a)[2]
        keep = pl.ds(pl.multiple_of(core * span, 128), span)
        src = ins[a].at[:, :, keep] if levels[a] == 0 else ins[a]
        return pltpu.make_async_copy(src, bufs[a][0], load.at[a])

    def first_copy(a, order):
        quarter = sizes(a)[1]
        away = rows_at((1 - bits[order][0]) * 2 * quarter, 2 * quarter)
        return remote(
            bufs[a][0].at[owners(a, order), away, :], bufs[a][2].at[owners(a, order)], send.at[a, 1 + order],
            recv.at[a, 1 + order], ids[order][0], z,
        )

    def second_copy(a, order):
        quarter = sizes(a)[1]
        away = rows_at(kept(a, order) + (1 - bits[order][1]) * quarter, quarter)
        return remote(
            bufs[a][0].at[owners(a, order), away, :], bufs[a][3].at[owners(a, order)], send.at[a, 3 + order],
            recv.at[a, 3 + order], ids[order][1], z,
        )

    def own_quarter(a, owner):
        strips, quarter, _ = sizes(a)
        order = owner // (ring // 2)
        first, second = (1 - order) * x + order * y, (1 - order) * y + order * x
        at = second * quarter if levels[a] == 2 else (2 * first + second) * quarter
        return bufs[a][0].at[pl.ds(owner * strips, strips), rows_at(at, quarter), :]

    def owner_copy(a, k):
        to = (z + k) % ring
        return remote(own_quarter(a, to), bufs[a][4].at[k - 1], send.at[a, 4 + k], recv.at[a, 4 + k], d, to)

    def team_copy(a, t):
        j = 4 + ring + 7 + t
        return remote(bufs[a][5].at[0], bufs[a][5].at[1 + t], send.at[a, j], recv.at[a, j], team_id(d, t), z)

    def final(a, spot, side):
        strips, quarter, span = sizes(a)
        order = z // (ring // 2)
        xx, yy = spots[spot]
        at = ((1 - order) * (2 * xx + yy) + order * (2 * yy + xx)) * quarter
        return sums[a].at[:, rows_at(at, quarter), pl.ds(pl.multiple_of(side * span, 128), span)]

    def spread(a, j):
        s, r = send.at[a, 4 + ring + j - 1], recv.at[a, 4 + ring + j - 1]
        if j < 4:
            return remote(bufs[a][5].at[0], final(a, 0, core), s, r, (x_id, y_id, far_id)[j - 1], z)
        src = bufs[a][5].at[0] if j == 4 else final(a, j - 4, core)
        return remote(src, final(a, j - 4, core), s, r, core_id, z)

    def spread_here(a, j):
        s, r = send.at[a, 4 + ring + j - 1], recv.at[a, 4 + ring + j - 1]
        ref = final(a, j, core) if j < 4 else final(a, j - 4, 1 - core)
        remote(ref, ref, s, r, core_id, z).wait_recv()

    def keep_own(a):
        return pltpu.make_async_copy(bufs[a][5].at[0], final(a, 0, core), load.at[count + a])

    def add(into, at, term, blocks):
        height = term.shape[1]
        tile = 32 if height % 48 else 48

        def body(n, _):
            o, t = n // (height // tile), n % (height // tile)
            spot = rows_at(at + t * tile, tile)
            value = term[o, rows_at(t * tile, tile), :]
            into[o, spot, :] = (into[o, spot, :].astype(F32) + value.astype(F32)).astype(BF16)
            return 0

        lax.fori_loop(0, blocks * (height // tile), body, 0)

    def enter(a):
        if levels[a] == 0:
            core_copy(a).start()
        own_load(a).start()

    def first(a):
        own_load(a).wait()
        if levels[a] == 0:
            core_copy(a).wait_recv()
            add(bufs[a][0], 0, bufs[a][1], bufs[a][0].shape[0])
        if levels[a] < 2:
            for order in range(2):
                first_copy(a, order).start()

    def second(a):
        for order in range(2):
            if levels[a] < 2:
                first_copy(a, order).wait_recv()
                own = owners(a, order)
                add(bufs[a][0].at[own], kept(a, order), bufs[a][2].at[own], ring // 2 * sizes(a)[0])
            second_copy(a, order).start()

    def to_owner(a):
        for order in range(2):
            second_copy(a, order).wait_recv()
            own = owners(a, order)
            at = kept(a, order) + bits[order][1] * sizes(a)[1]
            add(bufs[a][0].at[own], at, bufs[a][3].at[own], ring // 2 * sizes(a)[0])
        for k in range(1, ring):
            owner_copy(a, k).start()

    def add_up(a):
        for k in range(1, ring):
            owner_copy(a, k).wait_recv()
        mine = own_quarter(a, z)
        for s in range(sizes(a)[0]):
            terms = [mine[s]] + [bufs[a][4][k, s] for k in range(ring - 1)]
            bufs[a][5][0, s] = sum((t.astype(F32) for t in terms[1:]), terms[0].astype(F32)).astype(BF16)
        for t in range(teams):
            team_copy(a, t).start()
            team_copy(a, t).wait()
            bufs[a][5][0] = (bufs[a][5][0].astype(F32) + bufs[a][5][1 + t].astype(F32)).astype(BF16)

    def total(a):
        if levels[a] == 3:
            own_load(a).wait()
        else:
            add_up(a)
        keep_own(a).start()
        for j in range(1, 5):
            spread(a, j).start()

    def hand_on(a):
        add_up(a)
        out = pltpu.make_async_copy(bufs[a][5].at[0], sums[a], load.at[count + a])
        out.start()
        sent(a)
        out.wait()

    def share(a):
        for j in range(1, 4):
            spread_here(a, j)
            spread(a, 4 + j).start()

    def sent(a):
        if levels[a] == 0:
            core_copy(a).wait_send()
        for order in range(2):
            if levels[a] < 2:
                first_copy(a, order).wait_send()
            second_copy(a, order).wait_send()
        for k in range(1, ring):
            owner_copy(a, k).wait_send()

    def close(a):
        for j in range(4, 8):
            spread_here(a, j)
        if levels[a] < 3:
            sent(a)
        for j in range(1, 8):
            spread(a, j).wait_send()
        keep_own(a).wait()

    return SimpleNamespace(
        enter=enter, first=first, second=second, to_owner=to_owner, total=total, hand_on=hand_on, share=share, close=close
    )


def reducer_scratch(levels, shapes, teams, ring):
    scratch = []
    for level, (strips, rows, columns) in zip(levels, shapes):
        blocks, span = ring * strips, columns // 2
        none = (1, 16, 128)
        scratch += [
            pltpu.VMEM(none if level == 3 else (blocks, rows // 2 if level == 2 else rows, span), BF16),
            pltpu.VMEM((blocks, rows, span) if level == 0 else none, BF16),
            pltpu.VMEM((blocks, rows // 2, span) if level < 2 else none, BF16),
            pltpu.VMEM((blocks, rows // 4, span) if level < 3 else none, BF16),
            pltpu.VMEM((ring - 1, strips, rows // 4, span) if level < 3 else (1, *none), BF16),
            pltpu.VMEM((1 + teams, strips, rows // 4, span), BF16),
        ]
    copies = 4 + ring + 7 + teams
    dma = pltpu.SemaphoreType.DMA
    return scratch + [dma((len(levels), copies)), dma((len(levels), copies)), dma((2 * len(levels),))]


def reduce_kernel(
    teams, up_ref, down_ref, qkv_ref, small_att, small_mlp, small_up, back_ref, o_last, o_ref, g_ref, weights,
    up_sum, down_sum, qkv_sum, out_sum, norm_out, bias_out, attend_out, ret_back, *refs,
):
    ring = lax.axis_size("ctx")
    d, z = lax.axis_index("dp"), lax.axis_index("ctx")
    core, x, y, core_id, x_id, y_id = plane(d)
    bufs = [refs[6 * a : 6 * a + 6] for a in range(4)]
    send, recv, load, o_in, wo_ref, dwo_ref, small_acc, small_in = refs[24:32]
    s_send, s_recv, r_send, r_recv, r_local = refs[32:]
    batch, piece, width = ret_back.shape
    lanes = o_last.shape[1]
    up, down, qkv, out = range(4)
    ins, sums = (up_ref, down_ref, qkv_ref, dwo_ref), (up_sum, down_sum, qkv_sum, out_sum)
    do = reducer(teams, LEVELS, ins, sums, bufs, send, recv, load)

    pairs = ((o_last, o_in), (back_ref, ret_back))
    mine = z - core

    def returned(which, i, to):
        source, target = pairs[which]
        return source.at[pl.ds(pl.multiple_of(to * piece, 16), piece), :], target.at[i]

    def start_returns(which):
        for i in range(batch):
            @pl.when(mine == i)
            def _(i=i):
                for k in range(1, ring):
                    to = (z + k) % ring
                    src, dst = returned(which, i, to)
                    remote(src, dst, r_send.at[which, k], r_recv.at[which, i], d, to).start()
                src, dst = returned(which, i, z)
                pltpu.make_async_copy(src, dst, r_local.at[which]).start()

    def wait_returns(which):
        for i in range(batch):
            src, dst = returned(which, i, z)

            @pl.when(mine == i)
            def _(src=src, dst=dst):
                pltpu.make_async_copy(src, dst, r_local.at[which]).wait()

            @pl.when(mine != i)
            def _(i=i, src=src, dst=dst):
                remote(src, dst, r_send.at[which, 0], r_recv.at[which, i], core_id, z).wait_recv()

    def close_returns(which):
        for i in range(batch):
            @pl.when(mine == i)
            def _(i=i):
                for k in range(1, ring):
                    to = (z + k) % ring
                    remote(*returned(which, i, to), r_send.at[which, k], r_recv.at[which, i], d, to).wait_send()

    steps = [core_id, x_id, y_id] + [team_id(d, t) for t in range(teams)]

    def small_copy(n):
        return remote(small_acc, small_in.at[n], s_send.at[n], s_recv.at[n], steps[n], z)

    def small_owner(k):
        n = len(steps) + k - 1
        return remote(small_acc, small_in.at[n], s_send.at[n], s_recv.at[n], d, (z + k) % ring)

    def small_close(n):
        small_copy(n).wait()
        small_acc[...] += small_in[n]
        if n + 1 < len(steps):
            small_copy(n + 1).start()
        else:
            for k in range(1, ring):
                small_owner(k).start()

    columns = weights.shape[1] - width
    wo_load = pltpu.make_async_copy(weights.at[:, pl.ds(columns, width)], wo_ref, r_local.at[2])
    wo_load.start()
    small_acc[0:8, :] = small_att[...]
    small_acc[8:16, :] = small_mlp[...]
    for n in range(small_up.shape[1] // width):
        small_acc[16 + n : 17 + n, :] = small_up[0:1, n * width : (n + 1) * width]
    rest = 16 + small_up.shape[1] // width
    small_acc[rest:, :] = jnp.zeros((small_acc.shape[0] - rest, width), F32)
    greet(teams)
    do.enter(qkv)
    start_returns(0)
    start_returns(1)
    do.enter(up)
    do.enter(down)
    small_copy(0).start()
    do.total(up)
    do.total(down)
    do.first(qkv)
    small_close(0)
    do.share(up)
    do.share(down)

    wo_load.wait()
    wait_returns(0)
    split = o_ref.shape[1]
    for i in range(batch):
        at = pl.ds(i * piece, piece)
        attend_out[at, :] = dot(o_ref[at, :], wo_ref[:split, :]) + dot(o_in[i], wo_ref[split:, :])
    late = jnp.concatenate([o_in[i] for i in range(batch)], axis=0)
    dwo = jnp.concatenate([dot(o_ref[...], g_ref[...], TN), dot(late, g_ref[...], TN)], axis=0).astype(BF16)
    for r in range(ring):
        dwo_ref[r] = dwo[r * (width // ring) : (r + 1) * (width // ring), :]
    do.enter(out)
    do.second(qkv)
    do.first(out)
    small_close(1)
    do.to_owner(qkv)
    do.second(out)
    for n in range(2, len(steps)):
        small_close(n)
    do.total(qkv)
    do.to_owner(out)
    do.share(qkv)
    do.total(out)
    for k in range(1, ring):
        small_owner(k).wait()
    total = small_acc[...]
    for k in range(ring - 1):
        total += small_in[len(steps) + k]
    norm = jnp.concatenate([total[0:2], total[8:10], jnp.zeros((4, width), F32)], axis=0)
    norm_out[...] = pltpu.roll(norm, (ring - z) % ring * (width // ring), 1)
    ups = [total[16 + n : 17 + n] for n in range(small_up.shape[1] // width)]
    bias = jnp.concatenate([total[2:3], total[10:11], *ups, total[10:11]], axis=1)
    entries = bias.shape[1]
    bias = pltpu.roll(jnp.broadcast_to(bias, (8, entries)), (ring - z) % ring * (entries // ring), 1)
    bias_out[...] = bias[:, : bias_out.shape[1]]
    do.share(out)
    for a in range(4):
        do.close(a)
    wait_returns(1)
    close_returns(0)
    close_returns(1)


def reduce_all(up, down, qkv, small_att, small_mlp, small_up, back, o_last, o_first, g, weights, batch):
    ring, groups = lax.axis_size("ctx"), lax.axis_size("dp")
    teams = (groups // 8).bit_length() - 1
    width = g.shape[1]
    piece = g.shape[0] // batch
    shapes = [(n, 4 * rows, 2 * span) for n, rows, span in (up.shape, down.shape)]
    shapes += [(1, width // ring, qkv.shape[1]), (1, width // ring, width)]
    dma = pltpu.SemaphoreType.DMA
    anywhere = pl.BlockSpec(memory_space=pl.ANY)
    vmem = pl.BlockSpec(memory_space=pltpu.VMEM)
    rounds = 3 + teams + ring - 1
    small = (16 + -(-small_up.shape[1] // width // 8) * 8, width)
    share = (3 * width + small_up.shape[1]) // ring
    scratch = reducer_scratch(LEVELS, shapes, teams, ring)
    scratch += [
        pltpu.VMEM((batch, piece, o_last.shape[1]), BF16), pltpu.VMEM((width, width), BF16),
        pltpu.VMEM((ring, width // ring, width), BF16), pltpu.VMEM(small, F32), pltpu.VMEM((rounds, *small), F32),
        dma((rounds,)), dma((rounds,)), dma((2, ring)), dma((2, batch)), dma((3,)),
    ]
    return pl.pallas_call(
        functools.partial(reduce_kernel, teams),
        in_specs=[anywhere] * 3 + [vmem] * 3 + [anywhere, anywhere, vmem, vmem, anywhere],
        out_specs=[anywhere] * 4 + [vmem, vmem, vmem, anywhere],
        out_shape=[jax.ShapeDtypeStruct(shape, BF16) for shape in shapes]
        + [
            jax.ShapeDtypeStruct((8, width), F32), jax.ShapeDtypeStruct((8, share + -share % 128), F32),
            jax.ShapeDtypeStruct(g.shape, F32),
            jax.ShapeDtypeStruct((batch, piece, width), BF16),
        ],
        scratch_shapes=scratch,
        compiler_params=pltpu.CompilerParams(collective_id=1, has_side_effects=True, vmem_limit_bytes=56 * MIB),
        cost_estimate=pl.CostEstimate(flops=4 * width * width * g.shape[0], bytes_accessed=60 * MIB, transcendentals=0),
        name="reduce",
    )(
        up, down, qkv.reshape(ring, width // ring, -1), small_att, small_mlp, small_up, back, o_last,
        o_first.reshape(batch * piece, -1), g, weights,
    )


def attend_kernel(
    teams, order_ref, x_ref, stored_g_ref, norm_ref, bias_ref, cos_ref, low_ref, high_ref, wq_ref, wk_ref, wv_ref,
    wo_ref, up_ref, down_ref, h_ref, dqkv_all, small_ref, o_last, ret_o, up_sum, down_sum,
    g_ref, a_ref, at_ref, da_ref, q_ref, k_ref, v_ref, do_ref, o_ref, kt_ref, vt_ref, dqs_ref, dks_ref, dvs_ref,
    grad_ref, stored_o_ref, o_send, o_recv, o_local, grad_sem, *reduce_refs,
):
    step = pl.program_id(0)
    last = grad_ref.shape[0] - 1
    rows, width = x_ref.shape
    lanes = QUAD * HD
    tile = 256
    half = ROT // 2
    scale = 1.0 / math.sqrt(HD)
    blocks = rows // BLOCK
    ring = lax.axis_size("ctx")
    d, z = lax.axis_index("dp"), lax.axis_index("ctx")
    core_id = plane(d)[3]
    batch, piece = ret_o.shape[:2]
    mine = z - d % 2
    is_home = (mine >= 0) & (mine < batch)
    up, down = 0, 1
    bufs = (reduce_refs[:6], reduce_refs[6:12])
    do_sum = reducer(teams, MLP_LEVELS, (up_ref, down_ref), (up_sum, down_sum), bufs, *reduce_refs[12:])

    @pl.when(step == 0)
    def _():
        do_sum.enter(down)
        do_sum.enter(up)
        greet(teams)
        do_sum.first(down)
        do_sum.first(up)
        do_sum.second(up)

    def o_copy(quad, k, i):
        to = (z + k) % ring
        src = stored_o_ref.at[quad, pl.ds(pl.multiple_of(to * piece, 16), piece), :]
        dst = ret_o.at[i, :, pl.ds(pl.multiple_of(quad * lanes, 128), lanes)]
        if k == 0:
            return pltpu.make_async_copy(src, dst, o_local.at[quad])
        return remote(src, dst, o_send.at[quad, k], o_recv.at[quad, i], d, to)

    def grad_copy(quad, j):
        at = pl.ds(pl.multiple_of(j * width + quad * lanes, 128), lanes)
        return pltpu.make_async_copy(grad_ref.at[quad, j], dqkv_all.at[:, at], grad_sem.at[quad, j])


    def stored(ref, at):
        values = ref[pl.ds(at * BLOCK, BLOCK), :]
        return jnp.where(is_home, values, jnp.zeros_like(values))

    @pl.when(step == 0)
    def _():
        for j in range(blocks):
            place = order_ref[1, j]
            at = pl.ds(j * BLOCK, BLOCK)
            xh, _ = normalized(stored(x_ref, place).astype(F32))
            a = xh * norm_ref[1:2, :] + norm_ref[2:3, :]
            a_ref[at, :] = a.astype(BF16)
            at_ref[:, at] = a.T.astype(BF16)
            g_ref[at, :] = stored(stored_g_ref, place)
        da_ref[...] = jnp.zeros_like(da_ref)

    def table(ref, at):
        values = ref[at, :]
        return jnp.concatenate([values] * (lanes // values.shape[1]), axis=1)

    def turn(values, at):
        low = pltpu.roll(values, lanes - half, 1) * table(low_ref, at)
        high = pltpu.roll(values, half, 1) * table(high_ref, at)
        return values * table(cos_ref, at), low + high

    for t in range(rows // tile):
        at = pl.ds(t * tile, tile)
        a = a_ref[at, :]
        same, cross = turn(dot(a, wq_ref[...]) + bias_ref[0:1, :], at)
        q_ref[at, :] = ((same + cross).astype(BF16) * scale).astype(BF16)
        same, cross = turn(dot(a, wk_ref[...]), at)
        keys = same + cross
        k_ref[at, :] = keys.astype(BF16)
        kt_ref[:, at] = keys.T.astype(BF16)
        values = dot(a, wv_ref[...])
        v_ref[at, :] = values.astype(BF16)
        vt_ref[:, at] = values.T.astype(BF16)
        mixed_back = dot(g_ref[at, :], wo_ref[...], NT)
        do_ref[at, :] = mixed_back.astype(BF16)

    dks_ref[...] = jnp.zeros_like(dks_ref)
    dvs_ref[...] = jnp.zeros_like(dvs_ref)
    wide = 2 * HD
    head_of = lax.broadcasted_iota(jnp.int32, (BLOCK, wide), 1) // HD

    def stack(values):
        zero = jnp.zeros_like(values)
        return jnp.concatenate([jnp.where(head_of == e, values, zero) for e in range(2)], axis=0)

    def diagonal(values):
        return jnp.concatenate([values[e * HD : (e + 1) * HD, e * BLOCK : (e + 1) * BLOCK] for e in range(2)], axis=0)

    spot = lax.broadcasted_iota(jnp.int32, (BLOCK, 2 * BLOCK), 1) % BLOCK
    admitted = lax.broadcasted_iota(jnp.int32, (BLOCK, 2 * BLOCK), 0) <= spot

    def products_in(b, p):
        at, seen, own = pl.ds(b * BLOCK, BLOCK), pl.ds(0, (b + 1) * BLOCK), pl.ds(p * wide, wide)
        q, do = stack(q_ref[at, own]), stack(do_ref[at, own])
        return q, do, dot(k_ref[seen, own], q, NT), dot(v_ref[seen, own], do, NT)

    def softmax(b, scores, back):
        edge = jnp.where(admitted, scores[b * BLOCK :], -1e30)
        scores = edge if b == 0 else jnp.concatenate([scores[: b * BLOCK], edge], axis=0)
        top = jnp.max(scores, axis=0, keepdims=True)
        expo = jnp.exp(scores - top)
        probs = expo * (1.0 / jnp.sum(expo, axis=0, keepdims=True))
        share = jnp.sum(probs * back, axis=0, keepdims=True)
        return probs.astype(BF16), (probs * (back - share)).astype(BF16)

    def products_out(b, p, q, do, low, back):
        at, seen, own = pl.ds(b * BLOCK, BLOCK), pl.ds(0, (b + 1) * BLOCK), pl.ds(p * wide, wide)
        mixed = diagonal(dot(vt_ref[own, seen], low))
        o_ref[at, own] = mixed.T.astype(BF16)
        dqs_ref[at, own] = diagonal(dot(kt_ref[own, seen], back)).T * scale
        dks_ref[seen, own] += dot(back, q)
        dvs_ref[seen, own] += dot(low, do)

    units = [(b, p) for b in range(rows // BLOCK) for p in range(lanes // wide)]
    ready = products_in(*units[0])
    done = None
    for n, (b, p) in enumerate(units):
        q, do, scores, back = ready
        if n + 1 < len(units):
            ready = products_in(*units[n + 1])
        low, back = softmax(b, scores, back)
        if done is not None:
            products_out(*done)
        done = (b, p, q, do, low, back)
    products_out(*done)

    total = jnp.zeros((1, lanes), F32)
    for t in range(rows // tile):
        at = pl.ds(t * tile, tile)
        same, cross = turn(dqs_ref[at, :], at)
        dq = (same - cross).astype(BF16)
        same, cross = turn(dks_ref[at, :], at)
        dk = (same - cross).astype(BF16)
        dv = dvs_ref[at, :].astype(BF16)
        total += jnp.sum(dq.astype(F32), axis=0, keepdims=True)
        q_ref[at, :] = dq
        k_ref[at, :] = dk
        v_ref[at, :] = dv
        da_ref[at, :] += dot(dq, wq_ref[...], NT) + dot(dk, wk_ref[...], NT) + dot(dv, wv_ref[...], NT)
    small_ref[2:3, pl.ds(pl.multiple_of(step * lanes, 128), lanes)] = total
    for j, ref in enumerate((q_ref, k_ref, v_ref)):
        grad_ref[step, j] = dot(at_ref[...], ref[...]).astype(BF16)
        grad_copy(step, j).start()
    for s in range(blocks):
        stored_o_ref[step, s * BLOCK : (s + 1) * BLOCK, :] = o_ref[pl.ds(order_ref[0, s] * BLOCK, BLOCK), :]

    for i in range(batch):
        @pl.when((mine == i) & (step < last))
        def _(i=i):
            for k in range(ring):
                o_copy(step, k, i).start()

    @pl.when(step == 0)
    def _():
        do_sum.second(down)
        do_sum.to_owner(up)

    @pl.when(step == 1)
    def _():
        do_sum.to_owner(down)

    @pl.when(step == last)
    def _():
        gain = jnp.zeros((1, width), F32)
        shift = jnp.zeros((1, width), F32)
        for s in range(blocks):
            at = pl.ds(s * BLOCK, BLOCK)
            sorted_at = pl.ds(order_ref[0, s] * BLOCK, BLOCK)
            xh, _ = normalized(stored(x_ref, s).astype(F32))
            da = da_ref[sorted_at, :]
            gain += jnp.sum(da * xh, axis=0, keepdims=True)
            shift += jnp.sum(da, axis=0, keepdims=True)
            h_ref[at, :] = (da * norm_ref[1:2, :]).astype(BF16)
        small_ref[0:1, :] = gain
        small_ref[1:2, :] = shift
        small_ref[3:8, :] = jnp.zeros((5, width), F32)
        out = pltpu.make_async_copy(stored_o_ref.at[last], o_last, o_local.at[last])
        out.start()
        do_sum.hand_on(up)
        do_sum.hand_on(down)
        for quad in range(last):
            for i in range(batch):
                @pl.when(mine != i)
                def _(quad=quad, i=i):
                    ref = ret_o.at[i, :, pl.ds(quad * lanes, lanes)]
                    remote(ref, ref, o_send.at[quad, 0], o_recv.at[quad, i], core_id, z).wait_recv()

                @pl.when(mine == i)
                def _(quad=quad, i=i):
                    o_copy(quad, 0, i).wait()
                    for k in range(1, ring):
                        o_copy(quad, k, i).wait_send()
        for quad in range(last + 1):
            for j in range(3):
                grad_copy(quad, j).wait()
        out.wait()


def attend(order, x, g, norms, bias_q, tables, weights, up, down, batch):
    ring, groups_dp = lax.axis_size("ctx"), lax.axis_size("dp")
    teams = (groups_dp // 8).bit_length() - 1
    shapes = ((1, 2 * up.shape[1], 2 * up.shape[2]), (down.shape[1], down.shape[2], 2 * down.shape[3]))
    down = down.reshape(-1, *down.shape[2:])
    rows, width = x.shape
    lanes = QUAD * HD
    groups = width // lanes
    anywhere = pl.BlockSpec(memory_space=pl.ANY)
    whole = lambda shape: pl.BlockSpec(shape, lambda i: (0,) * len(shape))
    once = lambda shape: pl.BlockSpec(shape, lambda i: (0,) * len(shape), pipeline_mode=pl.Buffered(1))
    dma = pltpu.SemaphoreType.DMA
    slices = [(n, r // 4, c // 2) for n, r, c in shapes]
    return pl.pallas_call(
        functools.partial(attend_kernel, teams),
        grid=(groups,),
        in_specs=[
            pl.BlockSpec(memory_space=pltpu.SMEM),
            once((rows, width)),
            once((rows, width)),
            once(norms.shape),
            pl.BlockSpec((8, lanes), lambda i: (0, i)),
            once(tables[0].shape),
            once(tables[0].shape),
            once(tables[0].shape),
            pl.BlockSpec((width, lanes), lambda i: (0, i)),
            pl.BlockSpec((width, lanes), lambda i: (0, groups + i)),
            pl.BlockSpec((width, lanes), lambda i: (0, 2 * groups + i)),
            pl.BlockSpec((lanes, width), lambda i: (i, 3)),
            anywhere,
            anywhere,
        ],
        out_specs=[once((rows, width)), anywhere, once((8, width))] + [anywhere] * 4,
        out_shape=[
            jax.ShapeDtypeStruct((rows, width), BF16),
            jax.ShapeDtypeStruct((width, 3 * width), BF16),
            jax.ShapeDtypeStruct((8, width), F32),
            jax.ShapeDtypeStruct((rows, lanes), BF16),
            jax.ShapeDtypeStruct((batch, rows // ring, width - lanes), BF16),
        ]
        + [jax.ShapeDtypeStruct(shape, BF16) for shape in slices],
        scratch_shapes=[
            pltpu.VMEM((rows, width), BF16),
            pltpu.VMEM((rows, width), BF16),
            pltpu.VMEM((width, rows), BF16),
            pltpu.VMEM((rows, width), F32),
        ]
        + [pltpu.VMEM((rows, lanes), BF16)] * 5
        + [pltpu.VMEM((lanes, rows), BF16)] * 2
        + [pltpu.VMEM((rows, lanes), F32)] * 3
        + [
            pltpu.VMEM((groups, 3, width, lanes), BF16), pltpu.VMEM((groups, rows, lanes), BF16),
            dma((groups, ring)), dma((groups, batch)), dma((groups,)), dma((groups, 3)),
        ]
        + reducer_scratch(MLP_LEVELS, shapes, teams, ring),
        compiler_params=pltpu.CompilerParams(
            collective_id=2, has_side_effects=True, vmem_limit_bytes=60 * MIB
        ),
        cost_estimate=pl.CostEstimate(
            flops=24 * rows * width * width + 8 * rows * rows * width,
            bytes_accessed=16 * width * width + 8 * rows * width,
            transcendentals=HEADS * rows * rows // 2,
        ),
        name="attend",
    )(order, x, g, norms, bias_q, *tables, weights, weights, weights, weights, up, down)


def rotary_tables(length):
    half = ROT // 2
    frequency = ROPE_BASE ** (-(np.arange(half) * 2.0 / ROT))
    angle = np.arange(length)[:, None] * frequency[None, :]
    cosine, sine = np.cos(angle), np.sin(angle)
    rest = np.zeros((length, HD - ROT))
    none = np.zeros_like(sine)
    cos_full = np.concatenate([cosine, cosine, rest + 1.0], axis=1)
    low = np.concatenate([-sine, none, rest], axis=1)
    high = np.concatenate([none, sine, rest], axis=1)
    return tuple(jnp.asarray(np.tile(t, (1, 2)).astype(np.float32)) for t in (cos_full, low, high))


def adamw(weight, grad, first, second, rate, decay):
    first_new = BETA_ONE * first + (1.0 - BETA_ONE) * grad
    second_new = BETA_TWO * second + (1.0 - BETA_TWO) * grad * grad
    first_hat = first_new / (1.0 - BETA_ONE**STEP)
    second_hat = second_new / (1.0 - BETA_TWO**STEP)
    weight_new = weight - rate * (first_hat / (jnp.sqrt(second_hat) + EPS_ADAM) + decay * weight)
    return (first_new, second_new, weight_new)


RATES = (0.1, 0.6, 0.1, 0.05)


def finish_kernel(*refs):
    x_ref, g_ref, attend_ref, feed_ref, h_ref, back_ref, bias_ref, norm_grad = refs[:8]
    norm, norm_first, norm_second = refs[8:11]
    inputs, outputs = refs[11:27], refs[27:]
    layer_out, input_grad = outputs[:2]
    for n, rate in enumerate(RATES):
        weight, grad, first, second = (ref[...] for ref in inputs[4 * n : 4 * n + 4])
        new = adamw(weight, grad.astype(F32), first, second, rate, DECAY)
        for ref, value in zip(outputs[2 + 3 * n : 5 + 3 * n], new):
            ref[...] = value
    width = x_ref.shape[1]
    bias = bias_ref[0:1, width : 2 * width] + bias_ref[0:1, bias_ref.shape[1] - width :]
    rows = x_ref[...].astype(F32)
    layer_out[...] = (rows + attend_ref[...] + feed_ref[...] + bias).astype(BF16)
    xh, scale = normalized(rows)
    h = back_ref[...].astype(F32) + h_ref[...]
    inner = jnp.mean(h * xh, axis=-1, keepdims=True)
    input_grad[...] = g_ref[...].astype(F32) + scale * (h - jnp.mean(h, axis=-1, keepdims=True) - xh * inner)

    @pl.when(pl.program_id(0) == 0)
    def _():
        grad = norm_grad[0:4, : norm.shape[1]]
        first, second, new = adamw(norm[...], grad, norm_first[...], norm_second[...], 0.6, 0.0)
        outputs[14][...] = first
        outputs[15][...] = second[0:2]
        outputs[16][...] = second[2:4]
        outputs[17][...] = new


def finish(rows, biases, norm_grad, norm_args, weights):
    steps = 12
    whole = lambda v: pl.BlockSpec(v.shape, lambda i: (0,) * len(v.shape))
    part = lambda v: pl.BlockSpec((v.shape[0] // steps, v.shape[1]), lambda i: (i, 0))
    like = lambda v, dtype: jax.ShapeDtypeStruct(v.shape, dtype)
    count, width = rows[0].shape
    args = [*rows, biases, norm_grad, *norm_args] + [v for group in weights for v in group]
    specs = [part(v) for v in rows] + [whole(v) for v in (biases, norm_grad, *norm_args)]
    specs += [part(v) for group in weights for v in group]
    outs = [like(rows[0], BF16), like(rows[0], F32)] + [like(group[0], F32) for group in weights for _ in range(3)]
    out_specs = [part(v) for v in outs]
    own = norm_args[0].shape[1]
    norm_outs = [jax.ShapeDtypeStruct((n, own), F32) for n in (4, 2, 2, 4)]
    return pl.pallas_call(
        finish_kernel,
        grid=(steps,),
        in_specs=specs,
        out_specs=out_specs + [whole(v) for v in norm_outs],
        out_shape=outs + norm_outs,
        compiler_params=pltpu.CompilerParams(vmem_limit_bytes=56 * MIB),
        cost_estimate=pl.CostEstimate(flops=0, bytes_accessed=64 * MIB, transcendentals=0),
        name="finish",
    )(*args)


def shards(
    tokens, out_grad, block_order, qkv_weight, out_weight, up_weight, down_weight, norm_params, bias_params,
    qkv_first, qkv_second, out_first, out_second, up_first, up_second, down_first, down_second,
    norm_first, norm_second, bias_first, bias_second,
):
    groups, ring = lax.axis_size("dp"), lax.axis_size("ctx")
    group, rank = lax.axis_index("dp"), lax.axis_index("ctx")
    batch, piece, width = tokens.shape
    length = piece * ring
    count = batch * piece
    ff = up_weight.shape[1]

    share = bias_params.shape[0]
    lanes = share + -share % 128
    small = jnp.concatenate([
        jnp.pad(bias_params[None, :], ((0, 0), (0, lanes - share))),
        jnp.pad(norm_params, ((0, 3), (0, lanes - norm_params.shape[1]))),
    ])
    x_rows, g_rows = tokens.reshape(count, width), out_grad.reshape(count, width)
    att_copy, biases, norms, home_x, home_g, feed_out, h_feed, dup, ddown, dbias_up, small_feed = gather_feed(
        up_weight, down_weight, qkv_weight, out_weight, small, x_rows, g_rows, piece, ring * share
    )

    odd = group % 2

    order = block_order[jnp.clip(rank - odd, 0, batch - 1)]
    spots = jnp.arange(order.shape[0])
    order = jnp.stack([order, jnp.sum(jnp.where(order[None, :] == spots[:, None], spots[None, :], 0), axis=1)])

    h_attend, dqkv, small_attend, o_last, o_first, up_slice, down_slice = attend(
        order, home_x, home_g, norms, biases, rotary_tables(length), att_copy, dup, ddown, batch
    )
    *owned, norm_grad, bias_grad, attend_out, ret_back = reduce_all(
        up_slice, down_slice, dqkv, small_attend, small_feed, dbias_up, h_attend, o_last, o_first, g_rows, att_copy, batch
    )
    up_grad, down_grad, qkv_grad, out_grads = (
        g.reshape(w.shape) for g, w in zip(owned, (up_weight, down_weight, qkv_weight, out_weight))
    )
    layer_out, input_grad, *new, norm_a, norm_b, norm_c, norm_d = finish(
        (x_rows, g_rows, attend_out, feed_out, h_feed, ret_back.reshape(count, width)),
        biases,
        norm_grad,
        (norm_params, norm_first, norm_second),
        (
            (qkv_weight, qkv_grad, qkv_first, qkv_second),
            (out_weight, out_grads, out_first, out_second),
            (up_weight, up_grad, up_first, up_second),
            (down_weight, down_grad, down_first, down_second),
        ),
    )
    bias_new = adamw(bias_params, bias_grad[0, :share], bias_first, bias_second, 0.6, 0.0)
    return (
        layer_out.reshape(tokens.shape), input_grad.reshape(tokens.shape), *new,
        norm_a, norm_b, norm_c, norm_d, *bias_new,
    )


def solution(mesh):
    rows, columns, token = P("ctx", None), P(None, "ctx"), P("dp", "ctx", None)
    in_specs = (token, token, P("dp", None)) + (rows,) * 4 + (columns, P("ctx")) + (rows,) * 8
    in_specs += (columns, columns, P("ctx"), P("ctx"))
    out_specs = (token, token) + (rows,) * 12 + (columns,) * 4 + (P("ctx"),) * 3
    return jax.shard_map(shards, mesh=mesh, in_specs=in_specs, out_specs=out_specs, check_vma=False)
```

```python
import functools
import math
from types import SimpleNamespace

import jax
import jax.numpy as jnp
import numpy as np
from jax import lax
from jax.experimental import pallas as pl
from jax.experimental.pallas import tpu as pltpu
from jax.sharding import PartitionSpec as P

HEADS = 12
HD = 64
STEP = 10
ROT = 16
BLOCK = 128
QUAD = 4
MLP_LEVELS = (2, 1)
LEVELS = (3, 3, 0, 0)

EPS_NORM = 1e-05
BETA_ONE = 0.9
BETA_TWO = 0.95
EPS_ADAM = 1e-08
DECAY = 0.01
ROPE_BASE = 10000.0
F32 = jnp.float32
BF16 = jnp.bfloat16
MIB = 1024 * 1024


def dot(left, right, dims=((1,), (0,))):
    return lax.dot_general(left, right, (dims, ((), ())), preferred_element_type=F32)


NN = ((1,), (0,))
NT = ((1,), (1,))
TN = ((0,), (0,))


def normalized(values):
    mean = jnp.mean(values, axis=-1, keepdims=True)
    centred = values - mean
    variance = jnp.mean(centred * centred, axis=-1, keepdims=True)
    scale = lax.rsqrt(variance + EPS_NORM)
    return centred * scale, scale


MESH = pl.DeviceIdType.MESH


def plane(d):
    core, x, y = d % 2, d // 2 % 2, d // 4 % 2
    return core, x, y, d + 1 - 2 * core, d + 2 - 4 * x, d + 4 - 8 * y


def gather_kernel(
    up, down, qkv, out, small, tokens, cotangents,
    att_all, small_all, norm_all, home_x, home_g, out_ref, h_ref, up_part, down_part, dbias_ref, sums_ref,
    up_all, down_all, att_own, up_wide, down_wide, att_wide, small_in, x_ref, g_ref, m_ref, mt_ref, hid_ref, dup_in_ref,
    dup_ref, up_core, up_first, ddown_ref, down_core,
    z_send, z_recv, p_send, p_recv, s_send, s_recv, t_send, t_recv, local, out_sem, c_send, c_recv,
):
    ring = lax.axis_size("ctx")
    d, z = lax.axis_index("dp"), lax.axis_index("ctx")
    core, x, y, core_id, x_id, y_id = plane(d)
    own = x + 2 * y
    own_x, own_y, far = own + 1 - 2 * x, own + 2 - 4 * y, 3 - own
    count, width = tokens.shape
    piece = home_x.shape[0] // ring
    batch = count // piece
    att = 4
    height, span = att_own.shape[0] // 4, att_own.shape[1] // 2
    strips = ring // 2

    def part(a, base, place, side, half):
        if a == att:
            at = pl.multiple_of(base * att_own.shape[0] + place * height, 16)
            first, wide = side * span, span
            if half is not None:
                first, wide = side * span + half * (span // 2), span // 2
            return att_all.at[pl.ds(at, height), pl.ds(pl.multiple_of(first, 128), wide)]
        n = a // 2
        if a % 2 == 0:
            columns = up_all.shape[2] // 2
            first, count_ = side * strips, strips
            if half is not None:
                first, count_ = side * strips + half * (strips // 2), strips // 2
            at = pl.multiple_of(base * height + base * 3 * height + place * height, 16)
            return up_all.at[pl.ds(first, count_), pl.ds(at, height), pl.ds(n * columns, columns)]
        rows = down_wide.shape[0]
        tall = rows // 8
        at = base * rows + n * (rows // 2) + place * tall
        if half is not None:
            at, tall = at + half * (tall // 2), tall // 2
        return down_all.at[
            pl.ds(pl.multiple_of(at, 16), tall), pl.ds(pl.multiple_of(side * (width // 2), 128), width // 2)
        ]

    def slot(a, base, place, half=None):
        return part(a, base, place, core, half)

    def other_slot(a, base, place):
        return part(a, base, place, 1 - core, None)

    def own_att_slot():
        return att_own.at[
            pl.ds(pl.multiple_of(own * height, 16), height), pl.ds(pl.multiple_of(core * span, 128), span)
        ]

    def remote(src, dst, send, recv, dp, ctx):
        return pltpu.make_async_remote_copy(
            src_ref=src, dst_ref=dst, send_sem=send, recv_sem=recv, device_id=(dp, ctx), device_id_type=MESH
        )

    columns = qkv.shape[1]
    wide_loads = [
        [pltpu.make_async_copy(up, up_wide, local.at[0])],
        [pltpu.make_async_copy(down, down_wide, local.at[1])],
        [
            pltpu.make_async_copy(qkv, att_wide.at[:, pl.ds(0, columns)], local.at[2]),
            pltpu.make_async_copy(out, att_wide.at[:, pl.ds(columns, out.shape[1])], local.at[8]),
        ],
    ]
    for loads in wide_loads:
        for copy in loads:
            copy.start()

    def cast_own(a):
        for copy in wide_loads[a]:
            copy.wait()
        wide, target = ((up_wide, up_all), (down_wide, down_all), (att_wide, att_own))[a]
        rows = wide.shape[0]
        tile = 64
        base = 0 if a == 2 else z * rows

        def body(t, _):
            value = wide[pl.ds(pl.multiple_of(t * tile, 16), tile), :].astype(BF16)
            at = pl.ds(pl.multiple_of(base + t * tile, 16), tile)
            if a == 0:
                columns = target.shape[2]
                for r in range(ring):
                    target[r, at, :] = value[:, r * columns : (r + 1) * columns]
            else:
                target[at, :] = value
            return 0

        lax.fori_loop(0, rows // tile, body, 0)

    barrier = pltpu.get_barrier_semaphore()
    for k in range(1, ring):
        pl.semaphore_signal(barrier, inc=1, device_id=(d, (z + k) % ring), device_id_type=MESH)
    for other in (core_id, x_id, y_id):
        pl.semaphore_signal(barrier, inc=1, device_id=(other, z), device_id_type=MESH)
    cast_own(0)
    pl.semaphore_wait(barrier, ring + 2)

    def hop(a, way, h):
        shard = z - h if way == 0 else z + h
        target = z + 1 if way == 0 else z - 1
        src = own_att_slot() if h == 0 and a == att else slot(a, shard, own)
        return remote(src, slot(a, shard, own), z_send.at[a, way, h], z_recv.at[a, way, h], d, target)

    def can_send(way, h):
        shard = z - h if way == 0 else z + h
        target = z + 1 if way == 0 else z - 1
        return (shard >= 0) & (shard < ring) & (target >= 0) & (target < ring)

    def in_range(way, h):
        shard = z - h if way == 0 else z + h
        return (shard >= 0) & (shard < ring)

    def cast(a, shard, j):
        send, recv = p_send.at[a, shard, j], p_recv.at[a, shard, j]
        if j == 0:
            ref = slot(a, shard, own)
            return remote(ref, ref, send, recv, x_id, z)
        if j == 1:
            ref = slot(a, shard, own)
            return remote(ref, ref, send, recv, y_id, z)
        if j == 2:
            ref = slot(a, shard, own_x, 0)
            return remote(ref, ref, send, recv, y_id, z)
        if j == 3:
            ref = slot(a, shard, own_y, 1)
            return remote(ref, ref, send, recv, x_id, z)
        ref = slot(a, shard, (own, own_x, own_y, far)[j - 4])
        return remote(ref, ref, send, recv, core_id, z)

    def arrived(a, shard, j):
        send, recv = p_send.at[a, shard, j], p_recv.at[a, shard, j]
        ref = {0: lambda: slot(a, shard, own_x), 1: lambda: slot(a, shard, own_y),
               2: lambda: slot(a, shard, far, 0), 3: lambda: slot(a, shard, far, 1)}.get(
            j, lambda: other_slot(a, shard, (own, own_x, own_y, far)[j - 4]))()
        remote(ref, ref, send, recv, core_id, z).wait_recv()

    def start_hops(a):
        for way in range(2):
            @pl.when(can_send(way, 0))
            def _(way=way):
                hop(a, way, 0).start()

    def small_copy(k):
        return remote(small, small_in.at[z], s_send.at[k], s_recv.at[k], d, (z + k) % ring)

    def stage_a(a, h):
        for way in range(2):
            @pl.when(in_range(way, h))
            def _(way=way):
                shard = z - h if way == 0 else z + h
                ref = slot(a, shard, own)
                remote(ref, ref, z_send.at[a, way, h - 1], z_recv.at[a, way, h - 1], core_id, z).wait_recv()

                @pl.when(can_send(way, h))
                def _():
                    hop(a, way, h).start()

                cast(a, shard, 0).start()
                cast(a, shard, 1).start()
                cast(a, shard, 4).start()

    def stage_b(a, h):
        for way in range(2):
            @pl.when(in_range(way, h))
            def _(way=way):
                shard = z - h if way == 0 else z + h
                arrived(a, shard, 0)
                cast(a, shard, 2).start()
                cast(a, shard, 5).start()
                arrived(a, shard, 1)
                cast(a, shard, 3).start()
                cast(a, shard, 6).start()

    def stage_c(a, h):
        for way in range(2):
            @pl.when(in_range(way, h))
            def _(way=way):
                shard = z - h if way == 0 else z + h
                arrived(a, shard, 2)
                arrived(a, shard, 3)
                cast(a, shard, 7).start()

    def stage_d(a, h):
        for way in range(2):
            @pl.when(in_range(way, h))
            def _(way=way):
                shard = z - h if way == 0 else z + h
                for j in range(4, 8):
                    arrived(a, shard, j)

    pairs = ((tokens, home_x), (cotangents, home_g))

    def move(which, i):
        source, whole = pairs[which]
        src = source.at[pl.ds(i * piece, piece), :]
        dst = whole.at[pl.ds(pl.multiple_of(z * piece, 16), piece), :]
        return src, dst, i + core

    def start_moves(which):
        for i in range(batch):
            src, dst, target = move(which, i)

            @pl.when(target != z)
            def _(src=src, dst=dst, target=target, i=i):
                remote(src, dst, t_send.at[which, i], t_recv.at[which, z], d, target).start()

            @pl.when(target == z)
            def _(src=src, dst=dst):
                pltpu.make_async_copy(src, dst, local.at[6 + which]).start()

    own_rows = pl.ds(pl.multiple_of(z * att_own.shape[0], 16), att_own.shape[0])
    own_att = pltpu.make_async_copy(att_own, att_all.at[own_rows, :], local.at[9])
    x_load = pltpu.make_async_copy(tokens, x_ref, local.at[3])
    g_load = pltpu.make_async_copy(cotangents, g_ref, local.at[4])
    own_small = pltpu.make_async_copy(small, small_in.at[z], local.at[5])

    start_hops(0)
    cast_own(1)
    start_hops(1)
    start_hops(2)
    start_hops(3)
    cast_own(2)
    start_hops(att)
    for k in range(1, ring):
        small_copy(k).start()
    for copy in (own_att, x_load, g_load, own_small):
        copy.start()
    hops = range(1, ring)
    work = [(a, h) for n in range(2) for h in hops for a in (2 * n, 2 * n + 1)]
    early = len(work) // 2
    for n in range(len(work)):
        stage_a(*work[n])
        if 1 <= n <= early:
            stage_b(*work[n - 1])
        if 2 <= n <= early + 1:
            stage_c(*work[n - 2])
    start_moves(0)
    stage_a(att, 1)

    own_small.wait()
    for k in range(1, ring):
        ref = small_in.at[(z + ring - k) % ring]
        remote(ref, ref, s_send.at[k], s_recv.at[k], core_id, z).wait_recv()
    x_load.wait()
    g_load.wait()
    entries = small_all.shape[1]
    biases = jnp.zeros((8, entries), F32)
    norms = jnp.zeros((8, width), F32)
    for r in range(ring):
        block = small_in[r].astype(BF16).astype(F32)
        full = jnp.concatenate([block, jnp.zeros((8, entries - block.shape[1]), F32)], axis=1)
        biases += pltpu.roll(full, r * (entries // ring), 1) if r else full
        norms += pltpu.roll(block[:, :width], r * (width // ring), 1) if r else block[:, :width]
    small_all[...] = biases
    norm_all[...] = norms
    ff = ring * up_all.shape[2]
    gain_2, shift_2 = norm_all[3:4, :], norm_all[4:5, :]
    tile = 256
    tiles = count // tile
    for t in range(tiles):
        at = pl.ds(t * tile, tile)
        xh, _ = normalized(x_ref[at, :].astype(F32))
        m = xh * gain_2 + shift_2
        m_ref[at, :] = m.astype(BF16)
        mt_ref[:, at] = m.T.astype(BF16)
        out_ref[at, :] = jnp.zeros((tile, width), F32)
        h_ref[at, :] = jnp.zeros((tile, width), F32)
    for h in hops:
        stage_d(0, h)
        stage_d(1, h)

    strip = dup_ref.shape[3] // ring
    steps = ff // (ring * strip)
    half = ring // 2
    big, by_core = (dup_ref, ddown_ref), (up_core, down_core)
    bits, ids = ((x, y), (y, x)), ((x_id, y_id), (y_id, x_id))

    def sizes(a):
        return by_core[a].shape[2], by_core[a].shape[3]

    def slice_of(order):
        return 2 * bits[order][0] + bits[order][1]

    def core_copy(a, i):
        _, span = sizes(a)
        away = pl.ds(pl.multiple_of((1 - core) * span, 128), span)
        return remote(big[a].at[i, :, :, away], by_core[a].at[i], c_send.at[a, i, 0], c_recv.at[a, i, 0], core_id, z)

    def first_copy(a, i, order):
        height, _ = sizes(a)
        own = pl.ds(order * half, half)
        away = pl.ds(pl.multiple_of((1 - bits[order][0]) * (height // 2), 16), height // 2)
        return remote(
            by_core[a].at[i, own, away, :], up_first.at[i, own], c_send.at[a, i, 1 + order],
            c_recv.at[a, i, 1 + order], ids[order][0], z,
        )

    def add(into, at, term, owners):
        height = term(0).shape[0]
        tile = 32 if height % 48 else 48

        def body(n, _):
            o, t = n // (height // tile), n % (height // tile)
            spot = pl.ds(pl.multiple_of(at + t * tile, 16), tile)
            value = term(o)[pl.ds(pl.multiple_of(t * tile, 16), tile), :]
            into[o, spot, :] = (into[o, spot, :].astype(F32) + value.astype(F32)).astype(BF16)
            return 0

        lax.fori_loop(0, owners * (height // tile), body, 0)

    def chunk_1(i):
        for a in range(2):
            _, span = sizes(a)
            core_copy(a, i).wait_recv()
            keep = pl.ds(pl.multiple_of(core * span, 128), span)
            add(by_core[a].at[i], 0, lambda o: big[a].at[i, o, :, keep], ring)
        for order in range(2):
            first_copy(0, i, order).start()
        parts_out(1, i)[0].start()

    def chunk_2(i):
        height, _ = sizes(0)
        for order in range(2):
            own = pl.ds(order * half, half)
            first_copy(0, i, order).wait_recv()
            at = bits[order][0] * (height // 2)
            add(by_core[0].at[i, own], at, lambda o: up_first.at[i, order * half + o], half)
        for copy in parts_out(0, i):
            copy.start()

    def parts_out(a, i):
        height, span = sizes(a)
        if a == 1:
            return [pltpu.make_async_copy(by_core[1].at[i], down_part.at[:, i], out_sem.at[i, 2 * half])]
        copies = []
        for order in range(2):
            own = pl.ds(order * half, half)
            rows = pl.ds(pl.multiple_of(bits[order][0] * (height // 2), 16), height // 2)
            for n in range(half):
                copies.append(pltpu.make_async_copy(
                    by_core[0].at[i, own, rows, pl.ds(n * strip, strip)],
                    up_part.at[own, :, pl.ds(pl.multiple_of(n * steps * strip + i * strip, 128), strip)],
                    out_sem.at[i, half * order + n],
                ))
        return copies

    def feed_step(step, _):
        def at_step(n, stage, which):
            @pl.when(step == n)
            def _():
                for h in hops:
                    for a in which:
                        stage(a, h)

        at_step(1, stage_b, (2, 3))
        at_step(2, stage_c, (2, 3))
        at_step(3, stage_d, (2, 3))
        for h in hops:
            @pl.when((step == 2 * h - 2) & (h > 1))
            def _(h=h):
                stage_a(att, h)

            @pl.when(step == 2 * h + 1)
            def _(h=h):
                stage_b(att, h)

            @pl.when(step == 2 * h + 2)
            def _(h=h):
                stage_c(att, h)

        @pl.when(step == 3)
        def _():
            start_moves(1)

        @pl.when(step < steps)
        def _():
            spots = [pl.ds(pl.multiple_of(r * (ff // ring) + step * strip, 128), strip) for r in range(ring)]
            bias_spots = [
                pl.ds(pl.multiple_of(2 * width + r * (ff // ring) + step * strip, 128), strip) for r in range(ring)
            ]
            inner = pl.ds(pl.multiple_of(step * strip, 128), strip)
            up_part_ = jnp.concatenate([up_all[r, :, inner] for r in range(ring)], axis=1)
            down_part_ = jnp.concatenate([down_all[at, :] for at in spots], axis=0)
            bias = jnp.concatenate([small_all[0:1, at] for at in bias_spots], axis=1)
            total = jnp.zeros((1, ring * strip), F32)
            for t in range(tiles):
                at = pl.ds(t * tile, tile)
                u = dot(m_ref[at, :], up_part_) + bias
                cdf = 0.5 * (1.0 + lax.erf(u * (1.0 / math.sqrt(2.0))))
                hidden = (u * cdf).astype(BF16)
                slope = cdf + u * jnp.exp(-0.5 * u * u) * (1.0 / math.sqrt(2.0 * math.pi))
                back = (dot(g_ref[at, :], down_part_, NT) * slope).astype(BF16)
                hid_ref[at, :] = hidden
                dup_in_ref[at, :] = back
                total += jnp.sum(back.astype(F32), axis=0, keepdims=True)
                out_ref[at, :] += dot(hidden, down_part_)
                h_ref[at, :] += dot(back, up_part_, NT)
            for r in range(ring):
                dbias_ref[0:1, spots[r]] = total[:, r * strip : (r + 1) * strip]
            ddown = dot(hid_ref[...], g_ref[...], TN).astype(BF16)
            dup = dot(mt_ref[...], dup_in_ref[...]).astype(BF16)
            for r in range(ring):
                ddown_ref[step, r] = ddown[r * strip : (r + 1) * strip, :]
                dup_ref[step, r] = dup[r * (width // ring) : (r + 1) * (width // ring), :]
            core_copy(0, step).start()
            core_copy(1, step).start()

        for lag, stage in ((1, chunk_1), (3, chunk_2)):
            @pl.when((step >= lag) & (step < steps + lag))
            def _(lag=lag, stage=stage):
                stage(step - lag)

        return 0

    lax.fori_loop(0, steps + 3, feed_step, 0)

    gain = jnp.zeros((1, width), F32)
    shift = jnp.zeros((1, width), F32)
    sums = jnp.zeros((1, width), F32)
    for t in range(tiles):
        at = pl.ds(t * tile, tile)
        xh, _ = normalized(x_ref[at, :].astype(F32))
        dm = h_ref[at, :]
        gain += jnp.sum(dm * xh, axis=0, keepdims=True)
        shift += jnp.sum(dm, axis=0, keepdims=True)
        sums += jnp.sum(g_ref[at, :].astype(F32), axis=0, keepdims=True)
        h_ref[at, :] = dm * gain_2
    sums_ref[...] = jnp.concatenate([gain, shift, sums, jnp.zeros((5, width), F32)], axis=0)

    mine = z - core
    for which in range(2):
        for k in range(1, ring):
            @pl.when((mine >= 0) & (mine < batch))
            def _(which=which, k=k):
                other = (z + k) % ring
                ref = pairs[which][1].at[pl.ds(pl.multiple_of(other * piece, 16), piece), :]
                remote(ref, ref, t_send.at[which, 0], t_recv.at[which, other], core_id, z).wait_recv()
    for h in hops:
        stage_d(att, h)
    for k in range(1, ring):
        small_copy(k).wait_send()
    for a in range(5):
        for way in range(2):
            for h in range(ring - 1):
                @pl.when(can_send(way, h))
                def _(a=a, way=way, h=h):
                    hop(a, way, h).wait_send()
        for h in hops:
            for way in range(2):
                @pl.when(in_range(way, h))
                def _(a=a, h=h, way=way):
                    shard = z - h if way == 0 else z + h
                    for j in range(8):
                        cast(a, shard, j).wait_send()
    for which in range(2):
        for i in range(batch):
            src, dst, target = move(which, i)

            @pl.when(target != z)
            def _(src=src, dst=dst, target=target, which=which, i=i):
                remote(src, dst, t_send.at[which, i], t_recv.at[which, z], d, target).wait_send()

            @pl.when(target == z)
            def _(src=src, dst=dst, which=which):
                pltpu.make_async_copy(src, dst, local.at[6 + which]).wait()
    own_att.wait()

    def close(i, _):
        for a in range(2):
            core_copy(a, i).wait_send()
            for copy in parts_out(a, i):
                copy.wait()
        for order in range(2):
            first_copy(0, i, order).wait_send()
        return 0

    lax.fori_loop(0, steps, close, 0)


def gather_feed(up, down, qkv, out, small, tokens, cotangents, piece, entries):
    ring = lax.axis_size("ctx")
    count, width = tokens.shape
    ff = up.shape[1]
    strip = 128
    chunk = ring * strip
    steps = ff // chunk
    shard = up.shape[0]
    columns = qkv.shape[1] + out.shape[1]
    home = jax.ShapeDtypeStruct((ring * piece, width), tokens.dtype)
    rows = jax.ShapeDtypeStruct((count, width), F32)
    dma = pltpu.SemaphoreType.DMA
    anywhere = pl.BlockSpec(memory_space=pl.ANY)
    vmem = pl.BlockSpec(memory_space=pltpu.VMEM)
    return pl.pallas_call(
        gather_kernel,
        in_specs=[anywhere] * 7,
        out_specs=[anywhere, vmem, vmem, anywhere, anywhere, vmem, vmem, anywhere, anywhere, vmem, vmem],
        out_shape=[
            jax.ShapeDtypeStruct((ring * shard, columns), BF16),
            jax.ShapeDtypeStruct((8, entries), F32), jax.ShapeDtypeStruct((8, width), F32), home, home, rows, rows,
            jax.ShapeDtypeStruct((ring, shard // 2, ff // 2), BF16),
            jax.ShapeDtypeStruct((ring, steps, strip, width // 2), BF16),
            jax.ShapeDtypeStruct((8, ff), F32), jax.ShapeDtypeStruct((8, width), F32),
        ],
        scratch_shapes=[
            pltpu.VMEM((ring, ring * shard, ff // ring), BF16), pltpu.VMEM((ring * down.shape[0], width), BF16),
            pltpu.VMEM((shard, columns), BF16),
            pltpu.VMEM(up.shape, F32), pltpu.VMEM(down.shape, F32), pltpu.VMEM((shard, columns), F32),
            pltpu.VMEM((ring, *small.shape), F32),
            pltpu.VMEM((count, width), BF16), pltpu.VMEM((count, width), BF16), pltpu.VMEM((count, width), BF16),
            pltpu.VMEM((width, count), BF16),
            pltpu.VMEM((count, chunk), BF16), pltpu.VMEM((count, chunk), BF16),
            pltpu.VMEM((steps, ring, shard, chunk), BF16), pltpu.VMEM((steps, ring, shard, chunk // 2), BF16),
            pltpu.VMEM((steps, ring, shard // 2, chunk // 2), BF16),
            pltpu.VMEM((steps, ring, strip, width), BF16), pltpu.VMEM((steps, ring, strip, width // 2), BF16),
            dma((5, 2, ring)), dma((5, 2, ring)), dma((5, ring, 8)), dma((5, ring, 8)),
            dma((ring,)), dma((ring,)), dma((2, count // piece)), dma((2, ring)), dma((10,)), dma((steps, ring + 1)),
            dma((2, steps, 3)), dma((2, steps, 3)),
        ],
        compiler_params=pltpu.CompilerParams(
            collective_id=0, has_side_effects=True, vmem_limit_bytes=60 * MIB
        ),
        cost_estimate=pl.CostEstimate(
            flops=12 * count * width * ff, bytes_accessed=60 * MIB, transcendentals=count * ff
        ),
        name="gather_feed",
    )(up, down, qkv, out, small, tokens, cotangents)


def remote(src, dst, send_sem, recv_sem, dp, ctx):
    return pltpu.make_async_remote_copy(
        src_ref=src, dst_ref=dst, send_sem=send_sem, recv_sem=recv_sem, device_id=(dp, ctx), device_id_type=MESH
    )


def team_id(d, t):
    return d + (8 << t) * (1 - 2 * (d // (8 << t) % 2))


def greet(teams):
    ring = lax.axis_size("ctx")
    d, z = lax.axis_index("dp"), lax.axis_index("ctx")
    core, x, y, core_id, x_id, y_id = plane(d)
    barrier = pltpu.get_barrier_semaphore()
    partners = [core_id, x_id, y_id, x_id + y_id - d] + [team_id(d, t) for t in range(teams)]
    for k in range(1, ring):
        pl.semaphore_signal(barrier, inc=1, device_id=(d, (z + k) % ring), device_id_type=MESH)
    for other in partners:
        pl.semaphore_signal(barrier, inc=1, device_id=(other, z), device_id_type=MESH)
    pl.semaphore_wait(barrier, ring - 1 + len(partners))


def reducer(teams, levels, ins, sums, bufs, send, recv, load):
    count = len(ins)
    ring = lax.axis_size("ctx")
    d, z = lax.axis_index("dp"), lax.axis_index("ctx")
    core, x, y, core_id, x_id, y_id = plane(d)
    far_id = x_id + y_id - d
    bits, ids = ((x, y), (y, x)), ((x_id, y_id), (y_id, x_id))
    spots = ((x, y), (1 - x, y), (x, 1 - y), (1 - x, 1 - y))

    def sizes(a):
        _, strips, quarter, span = bufs[a][-1].shape
        return strips, quarter, span

    def owners(a, order):
        strips = sizes(a)[0]
        return pl.ds(order * ring // 2 * strips, ring // 2 * strips)

    def rows_at(at, height):
        return pl.ds(pl.multiple_of(at, 16), height)

    def kept(a, order):
        return 0 if levels[a] == 2 else bits[order][0] * 2 * sizes(a)[1]

    def core_copy(a):
        span = sizes(a)[2]
        away = pl.ds(pl.multiple_of((1 - core) * span, 128), span)
        return remote(ins[a].at[:, :, away], bufs[a][1], send.at[a, 0], recv.at[a, 0], core_id, z)

    def own_load(a):
        if levels[a] == 3:
            return pltpu.make_async_copy(ins[a], bufs[a][5].at[0], load.at[a])
        span = sizes(a)[2]
        keep = pl.ds(pl.multiple_of(core * span, 128), span)
        src = ins[a].at[:, :, keep] if levels[a] == 0 else ins[a]
        return pltpu.make_async_copy(src, bufs[a][0], load.at[a])

    def first_copy(a, order):
        quarter = sizes(a)[1]
        away = rows_at((1 - bits[order][0]) * 2 * quarter, 2 * quarter)
        return remote(
            bufs[a][0].at[owners(a, order), away, :], bufs[a][2].at[owners(a, order)], send.at[a, 1 + order],
            recv.at[a, 1 + order], ids[order][0], z,
        )

    def second_copy(a, order):
        quarter = sizes(a)[1]
        away = rows_at(kept(a, order) + (1 - bits[order][1]) * quarter, quarter)
        return remote(
            bufs[a][0].at[owners(a, order), away, :], bufs[a][3].at[owners(a, order)], send.at[a, 3 + order],
            recv.at[a, 3 + order], ids[order][1], z,
        )

    def own_quarter(a, owner):
        strips, quarter, _ = sizes(a)
        order = owner // (ring // 2)
        first, second = (1 - order) * x + order * y, (1 - order) * y + order * x
        at = second * quarter if levels[a] == 2 else (2 * first + second) * quarter
        return bufs[a][0].at[pl.ds(owner * strips, strips), rows_at(at, quarter), :]

    def owner_copy(a, k):
        to = (z + k) % ring
        return remote(own_quarter(a, to), bufs[a][4].at[k - 1], send.at[a, 4 + k], recv.at[a, 4 + k], d, to)

    def team_copy(a, t):
        j = 4 + ring + 7 + t
        return remote(bufs[a][5].at[0], bufs[a][5].at[1 + t], send.at[a, j], recv.at[a, j], team_id(d, t), z)

    def final(a, spot, side):
        strips, quarter, span = sizes(a)
        order = z // (ring // 2)
        xx, yy = spots[spot]
        at = ((1 - order) * (2 * xx + yy) + order * (2 * yy + xx)) * quarter
        return sums[a].at[:, rows_at(at, quarter), pl.ds(pl.multiple_of(side * span, 128), span)]

    def spread(a, j):
        s, r = send.at[a, 4 + ring + j - 1], recv.at[a, 4 + ring + j - 1]
        if j < 4:
            return remote(bufs[a][5].at[0], final(a, 0, core), s, r, (x_id, y_id, far_id)[j - 1], z)
        src = bufs[a][5].at[0] if j == 4 else final(a, j - 4, core)
        return remote(src, final(a, j - 4, core), s, r, core_id, z)

    def spread_here(a, j):
        s, r = send.at[a, 4 + ring + j - 1], recv.at[a, 4 + ring + j - 1]
        ref = final(a, j, core) if j < 4 else final(a, j - 4, 1 - core)
        remote(ref, ref, s, r, core_id, z).wait_recv()

    def keep_own(a):
        return pltpu.make_async_copy(bufs[a][5].at[0], final(a, 0, core), load.at[count + a])

    def add(into, at, term, blocks):
        height = term.shape[1]
        tile = 32 if height % 48 else 48

        def body(n, _):
            o, t = n // (height // tile), n % (height // tile)
            spot = rows_at(at + t * tile, tile)
            value = term[o, rows_at(t * tile, tile), :]
            into[o, spot, :] = (into[o, spot, :].astype(F32) + value.astype(F32)).astype(BF16)
            return 0

        lax.fori_loop(0, blocks * (height // tile), body, 0)

    def enter(a):
        if levels[a] == 0:
            core_copy(a).start()
        own_load(a).start()

    def first(a):
        own_load(a).wait()
        if levels[a] == 0:
            core_copy(a).wait_recv()
            add(bufs[a][0], 0, bufs[a][1], bufs[a][0].shape[0])
        if levels[a] < 2:
            for order in range(2):
                first_copy(a, order).start()

    def second(a):
        for order in range(2):
            if levels[a] < 2:
                first_copy(a, order).wait_recv()
                own = owners(a, order)
                add(bufs[a][0].at[own], kept(a, order), bufs[a][2].at[own], ring // 2 * sizes(a)[0])
            second_copy(a, order).start()

    def to_owner(a):
        for order in range(2):
            second_copy(a, order).wait_recv()
            own = owners(a, order)
            at = kept(a, order) + bits[order][1] * sizes(a)[1]
            add(bufs[a][0].at[own], at, bufs[a][3].at[own], ring // 2 * sizes(a)[0])
        for k in range(1, ring):
            owner_copy(a, k).start()

    def add_up(a):
        for k in range(1, ring):
            owner_copy(a, k).wait_recv()
        mine = own_quarter(a, z)
        for s in range(sizes(a)[0]):
            terms = [mine[s]] + [bufs[a][4][k, s] for k in range(ring - 1)]
            bufs[a][5][0, s] = sum((t.astype(F32) for t in terms[1:]), terms[0].astype(F32)).astype(BF16)
        for t in range(teams):
            team_copy(a, t).start()
            team_copy(a, t).wait()
            bufs[a][5][0] = (bufs[a][5][0].astype(F32) + bufs[a][5][1 + t].astype(F32)).astype(BF16)

    def total(a):
        if levels[a] == 3:
            own_load(a).wait()
        else:
            add_up(a)
        keep_own(a).start()
        for j in range(1, 5):
            spread(a, j).start()

    def hand_on(a):
        add_up(a)
        out = pltpu.make_async_copy(bufs[a][5].at[0], sums[a], load.at[count + a])
        out.start()
        sent(a)
        out.wait()

    def share(a):
        for j in range(1, 4):
            spread_here(a, j)
            spread(a, 4 + j).start()

    def sent(a):
        if levels[a] == 0:
            core_copy(a).wait_send()
        for order in range(2):
            if levels[a] < 2:
                first_copy(a, order).wait_send()
            second_copy(a, order).wait_send()
        for k in range(1, ring):
            owner_copy(a, k).wait_send()

    def close(a):
        for j in range(4, 8):
            spread_here(a, j)
        if levels[a] < 3:
            sent(a)
        for j in range(1, 8):
            spread(a, j).wait_send()
        keep_own(a).wait()

    return SimpleNamespace(
        enter=enter, first=first, second=second, to_owner=to_owner, total=total, hand_on=hand_on, share=share, close=close
    )


def reducer_scratch(levels, shapes, teams, ring):
    scratch = []
    for level, (strips, rows, columns) in zip(levels, shapes):
        blocks, span = ring * strips, columns // 2
        none = (1, 16, 128)
        scratch += [
            pltpu.VMEM(none if level == 3 else (blocks, rows // 2 if level == 2 else rows, span), BF16),
            pltpu.VMEM((blocks, rows, span) if level == 0 else none, BF16),
            pltpu.VMEM((blocks, rows // 2, span) if level < 2 else none, BF16),
            pltpu.VMEM((blocks, rows // 4, span) if level < 3 else none, BF16),
            pltpu.VMEM((ring - 1, strips, rows // 4, span) if level < 3 else (1, *none), BF16),
            pltpu.VMEM((1 + teams, strips, rows // 4, span), BF16),
        ]
    copies = 4 + ring + 7 + teams
    dma = pltpu.SemaphoreType.DMA
    return scratch + [dma((len(levels), copies)), dma((len(levels), copies)), dma((2 * len(levels),))]


def reduce_kernel(
    teams, up_ref, down_ref, qkv_ref, small_att, small_mlp, small_up, back_ref, o_last, o_ref, g_ref, weights,
    up_sum, down_sum, qkv_sum, out_sum, norm_out, bias_out, attend_out, ret_back, *refs,
):
    ring = lax.axis_size("ctx")
    d, z = lax.axis_index("dp"), lax.axis_index("ctx")
    core, x, y, core_id, x_id, y_id = plane(d)
    bufs = [refs[6 * a : 6 * a + 6] for a in range(4)]
    send, recv, load, o_in, wo_ref, dwo_ref, small_acc, small_in = refs[24:32]
    s_send, s_recv, r_send, r_recv, r_local = refs[32:]
    batch, piece, width = ret_back.shape
    lanes = o_last.shape[1]
    up, down, qkv, out = range(4)
    ins, sums = (up_ref, down_ref, qkv_ref, dwo_ref), (up_sum, down_sum, qkv_sum, out_sum)
    do = reducer(teams, LEVELS, ins, sums, bufs, send, recv, load)

    pairs = ((o_last, o_in), (back_ref, ret_back))
    mine = z - core

    def returned(which, i, to):
        source, target = pairs[which]
        return source.at[pl.ds(pl.multiple_of(to * piece, 16), piece), :], target.at[i]

    def start_returns(which):
        for i in range(batch):
            @pl.when(mine == i)
            def _(i=i):
                for k in range(1, ring):
                    to = (z + k) % ring
                    src, dst = returned(which, i, to)
                    remote(src, dst, r_send.at[which, k], r_recv.at[which, i], d, to).start()
                src, dst = returned(which, i, z)
                pltpu.make_async_copy(src, dst, r_local.at[which]).start()

    def wait_returns(which):
        for i in range(batch):
            src, dst = returned(which, i, z)

            @pl.when(mine == i)
            def _(src=src, dst=dst):
                pltpu.make_async_copy(src, dst, r_local.at[which]).wait()

            @pl.when(mine != i)
            def _(i=i, src=src, dst=dst):
                remote(src, dst, r_send.at[which, 0], r_recv.at[which, i], core_id, z).wait_recv()

    def close_returns(which):
        for i in range(batch):
            @pl.when(mine == i)
            def _(i=i):
                for k in range(1, ring):
                    to = (z + k) % ring
                    remote(*returned(which, i, to), r_send.at[which, k], r_recv.at[which, i], d, to).wait_send()

    steps = [core_id, x_id, y_id] + [team_id(d, t) for t in range(teams)]

    def small_copy(n):
        return remote(small_acc, small_in.at[n], s_send.at[n], s_recv.at[n], steps[n], z)

    def small_owner(k):
        n = len(steps) + k - 1
        return remote(small_acc, small_in.at[n], s_send.at[n], s_recv.at[n], d, (z + k) % ring)

    def small_close(n):
        small_copy(n).wait()
        small_acc[...] += small_in[n]
        if n + 1 < len(steps):
            small_copy(n + 1).start()
        else:
            for k in range(1, ring):
                small_owner(k).start()

    columns = weights.shape[1] - width
    wo_load = pltpu.make_async_copy(weights.at[:, pl.ds(columns, width)], wo_ref, r_local.at[2])
    wo_load.start()
    small_acc[0:8, :] = small_att[...]
    small_acc[8:16, :] = small_mlp[...]
    for n in range(small_up.shape[1] // width):
        small_acc[16 + n : 17 + n, :] = small_up[0:1, n * width : (n + 1) * width]
    rest = 16 + small_up.shape[1] // width
    small_acc[rest:, :] = jnp.zeros((small_acc.shape[0] - rest, width), F32)
    greet(teams)
    do.enter(qkv)
    start_returns(0)
    start_returns(1)
    do.enter(up)
    do.enter(down)
    small_copy(0).start()
    do.total(up)
    do.total(down)
    do.first(qkv)
    small_close(0)
    do.share(up)
    do.share(down)

    wo_load.wait()
    wait_returns(0)
    split = o_ref.shape[1]
    for i in range(batch):
        at = pl.ds(i * piece, piece)
        attend_out[at, :] = dot(o_ref[at, :], wo_ref[:split, :]) + dot(o_in[i], wo_ref[split:, :])
    late = jnp.concatenate([o_in[i] for i in range(batch)], axis=0)
    dwo = jnp.concatenate([dot(o_ref[...], g_ref[...], TN), dot(late, g_ref[...], TN)], axis=0).astype(BF16)
    for r in range(ring):
        dwo_ref[r] = dwo[r * (width // ring) : (r + 1) * (width // ring), :]
    do.enter(out)
    do.second(qkv)
    do.first(out)
    small_close(1)
    do.to_owner(qkv)
    do.second(out)
    for n in range(2, len(steps)):
        small_close(n)
    do.total(qkv)
    do.to_owner(out)
    do.share(qkv)
    do.total(out)
    for k in range(1, ring):
        small_owner(k).wait()
    total = small_acc[...]
    for k in range(ring - 1):
        total += small_in[len(steps) + k]
    norm = jnp.concatenate([total[0:2], total[8:10], jnp.zeros((4, width), F32)], axis=0)
    norm_out[...] = pltpu.roll(norm, (ring - z) % ring * (width // ring), 1)
    ups = [total[16 + n : 17 + n] for n in range(small_up.shape[1] // width)]
    bias = jnp.concatenate([total[2:3], total[10:11], *ups, total[10:11]], axis=1)
    entries = bias.shape[1]
    bias = pltpu.roll(jnp.broadcast_to(bias, (8, entries)), (ring - z) % ring * (entries // ring), 1)
    bias_out[...] = bias[:, : bias_out.shape[1]]
    do.share(out)
    for a in range(4):
        do.close(a)
    wait_returns(1)
    close_returns(0)
    close_returns(1)


def reduce_all(up, down, qkv, small_att, small_mlp, small_up, back, o_last, o_first, g, weights, batch):
    ring, groups = lax.axis_size("ctx"), lax.axis_size("dp")
    teams = (groups // 8).bit_length() - 1
    width = g.shape[1]
    piece = g.shape[0] // batch
    shapes = [(n, 4 * rows, 2 * span) for n, rows, span in (up.shape, down.shape)]
    shapes += [(1, width // ring, qkv.shape[1]), (1, width // ring, width)]
    dma = pltpu.SemaphoreType.DMA
    anywhere = pl.BlockSpec(memory_space=pl.ANY)
    vmem = pl.BlockSpec(memory_space=pltpu.VMEM)
    rounds = 3 + teams + ring - 1
    small = (16 + -(-small_up.shape[1] // width // 8) * 8, width)
    share = (3 * width + small_up.shape[1]) // ring
    scratch = reducer_scratch(LEVELS, shapes, teams, ring)
    scratch += [
        pltpu.VMEM((batch, piece, o_last.shape[1]), BF16), pltpu.VMEM((width, width), BF16),
        pltpu.VMEM((ring, width // ring, width), BF16), pltpu.VMEM(small, F32), pltpu.VMEM((rounds, *small), F32),
        dma((rounds,)), dma((rounds,)), dma((2, ring)), dma((2, batch)), dma((3,)),
    ]
    return pl.pallas_call(
        functools.partial(reduce_kernel, teams),
        in_specs=[anywhere] * 3 + [vmem] * 3 + [anywhere, anywhere, vmem, vmem, anywhere],
        out_specs=[anywhere] * 4 + [vmem, vmem, vmem, anywhere],
        out_shape=[jax.ShapeDtypeStruct(shape, BF16) for shape in shapes]
        + [
            jax.ShapeDtypeStruct((8, width), F32), jax.ShapeDtypeStruct((8, share + -share % 128), F32),
            jax.ShapeDtypeStruct(g.shape, F32),
            jax.ShapeDtypeStruct((batch, piece, width), BF16),
        ],
        scratch_shapes=scratch,
        compiler_params=pltpu.CompilerParams(collective_id=1, has_side_effects=True, vmem_limit_bytes=56 * MIB),
        cost_estimate=pl.CostEstimate(flops=4 * width * width * g.shape[0], bytes_accessed=60 * MIB, transcendentals=0),
        name="reduce",
    )(
        up, down, qkv.reshape(ring, width // ring, -1), small_att, small_mlp, small_up, back, o_last,
        o_first.reshape(batch * piece, -1), g, weights,
    )


def attend_kernel(
    teams, order_ref, x_ref, stored_g_ref, norm_ref, bias_ref, cos_ref, low_ref, high_ref, wq_ref, wk_ref, wv_ref,
    wo_ref, up_ref, down_ref, h_ref, dqkv_all, small_ref, o_last, ret_o, up_sum, down_sum,
    g_ref, a_ref, at_ref, da_ref, q_ref, k_ref, v_ref, do_ref, o_ref, kt_ref, vt_ref, dqs_ref, dks_ref, dvs_ref,
    grad_ref, stored_o_ref, o_send, o_recv, o_local, grad_sem, *reduce_refs,
):
    step = pl.program_id(0)
    last = grad_ref.shape[0] - 1
    rows, width = x_ref.shape
    lanes = QUAD * HD
    tile = 256
    half = ROT // 2
    scale = 1.0 / math.sqrt(HD)
    blocks = rows // BLOCK
    ring = lax.axis_size("ctx")
    d, z = lax.axis_index("dp"), lax.axis_index("ctx")
    core_id = plane(d)[3]
    batch, piece = ret_o.shape[:2]
    mine = z - d % 2
    is_home = (mine >= 0) & (mine < batch)
    up, down = 0, 1
    bufs = (reduce_refs[:6], reduce_refs[6:12])
    do_sum = reducer(teams, MLP_LEVELS, (up_ref, down_ref), (up_sum, down_sum), bufs, *reduce_refs[12:])

    @pl.when(step == 0)
    def _():
        do_sum.enter(down)
        do_sum.enter(up)
        greet(teams)
        do_sum.first(down)
        do_sum.first(up)
        do_sum.second(up)

    def o_copy(quad, k, i):
        to = (z + k) % ring
        src = stored_o_ref.at[quad, pl.ds(pl.multiple_of(to * piece, 16), piece), :]
        dst = ret_o.at[i, :, pl.ds(pl.multiple_of(quad * lanes, 128), lanes)]
        if k == 0:
            return pltpu.make_async_copy(src, dst, o_local.at[quad])
        return remote(src, dst, o_send.at[quad, k], o_recv.at[quad, i], d, to)

    def grad_copy(quad, j):
        at = pl.ds(pl.multiple_of(j * width + quad * lanes, 128), lanes)
        return pltpu.make_async_copy(grad_ref.at[quad, j], dqkv_all.at[:, at], grad_sem.at[quad, j])


    def stored(ref, at):
        values = ref[pl.ds(at * BLOCK, BLOCK), :]
        return jnp.where(is_home, values, jnp.zeros_like(values))

    @pl.when(step == 0)
    def _():
        for j in range(blocks):
            place = order_ref[1, j]
            at = pl.ds(j * BLOCK, BLOCK)
            xh, _ = normalized(stored(x_ref, place).astype(F32))
            a = xh * norm_ref[1:2, :] + norm_ref[2:3, :]
            a_ref[at, :] = a.astype(BF16)
            at_ref[:, at] = a.T.astype(BF16)
            g_ref[at, :] = stored(stored_g_ref, place)
        da_ref[...] = jnp.zeros_like(da_ref)

    def table(ref, at):
        values = ref[at, :]
        return jnp.concatenate([values] * (lanes // values.shape[1]), axis=1)

    def turn(values, at):
        low = pltpu.roll(values, lanes - half, 1) * table(low_ref, at)
        high = pltpu.roll(values, half, 1) * table(high_ref, at)
        return values * table(cos_ref, at), low + high

    for t in range(rows // tile):
        at = pl.ds(t * tile, tile)
        a = a_ref[at, :]
        same, cross = turn(dot(a, wq_ref[...]) + bias_ref[0:1, :], at)
        q_ref[at, :] = ((same + cross).astype(BF16) * scale).astype(BF16)
        same, cross = turn(dot(a, wk_ref[...]), at)
        keys = same + cross
        k_ref[at, :] = keys.astype(BF16)
        kt_ref[:, at] = keys.T.astype(BF16)
        values = dot(a, wv_ref[...])
        v_ref[at, :] = values.astype(BF16)
        vt_ref[:, at] = values.T.astype(BF16)
        mixed_back = dot(g_ref[at, :], wo_ref[...], NT)
        do_ref[at, :] = mixed_back.astype(BF16)

    dks_ref[...] = jnp.zeros_like(dks_ref)
    dvs_ref[...] = jnp.zeros_like(dvs_ref)
    wide = 2 * HD
    head_of = lax.broadcasted_iota(jnp.int32, (BLOCK, wide), 1) // HD

    def stack(values):
        zero = jnp.zeros_like(values)
        return jnp.concatenate([jnp.where(head_of == e, values, zero) for e in range(2)], axis=0)

    def diagonal(values):
        return jnp.concatenate([values[e * HD : (e + 1) * HD, e * BLOCK : (e + 1) * BLOCK] for e in range(2)], axis=0)

    spot = lax.broadcasted_iota(jnp.int32, (BLOCK, 2 * BLOCK), 1) % BLOCK
    admitted = lax.broadcasted_iota(jnp.int32, (BLOCK, 2 * BLOCK), 0) <= spot

    def products_in(b, p):
        at, seen, own = pl.ds(b * BLOCK, BLOCK), pl.ds(0, (b + 1) * BLOCK), pl.ds(p * wide, wide)
        q, do = stack(q_ref[at, own]), stack(do_ref[at, own])
        return q, do, dot(k_ref[seen, own], q, NT), dot(v_ref[seen, own], do, NT)

    def softmax(b, scores, back):
        edge = jnp.where(admitted, scores[b * BLOCK :], -1e30)
        scores = edge if b == 0 else jnp.concatenate([scores[: b * BLOCK], edge], axis=0)
        top = jnp.max(scores, axis=0, keepdims=True)
        expo = jnp.exp(scores - top)
        probs = expo * (1.0 / jnp.sum(expo, axis=0, keepdims=True))
        share = jnp.sum(probs * back, axis=0, keepdims=True)
        return probs.astype(BF16), (probs * (back - share)).astype(BF16)

    def products_out(b, p, q, do, low, back):
        at, seen, own = pl.ds(b * BLOCK, BLOCK), pl.ds(0, (b + 1) * BLOCK), pl.ds(p * wide, wide)
        mixed = diagonal(dot(vt_ref[own, seen], low))
        o_ref[at, own] = mixed.T.astype(BF16)
        dqs_ref[at, own] = diagonal(dot(kt_ref[own, seen], back)).T * scale
        dks_ref[seen, own] += dot(back, q)
        dvs_ref[seen, own] += dot(low, do)

    units = [(b, p) for b in range(rows // BLOCK) for p in range(lanes // wide)]
    ready = products_in(*units[0])
    done = None
    for n, (b, p) in enumerate(units):
        q, do, scores, back = ready
        if n + 1 < len(units):
            ready = products_in(*units[n + 1])
        low, back = softmax(b, scores, back)
        if done is not None:
            products_out(*done)
        done = (b, p, q, do, low, back)
    products_out(*done)

    total = jnp.zeros((1, lanes), F32)
    for t in range(rows // tile):
        at = pl.ds(t * tile, tile)
        same, cross = turn(dqs_ref[at, :], at)
        dq = (same - cross).astype(BF16)
        same, cross = turn(dks_ref[at, :], at)
        dk = (same - cross).astype(BF16)
        dv = dvs_ref[at, :].astype(BF16)
        total += jnp.sum(dq.astype(F32), axis=0, keepdims=True)
        q_ref[at, :] = dq
        k_ref[at, :] = dk
        v_ref[at, :] = dv
        da_ref[at, :] += dot(dq, wq_ref[...], NT) + dot(dk, wk_ref[...], NT) + dot(dv, wv_ref[...], NT)
    small_ref[2:3, pl.ds(pl.multiple_of(step * lanes, 128), lanes)] = total
    for j, ref in enumerate((q_ref, k_ref, v_ref)):
        grad_ref[step, j] = dot(at_ref[...], ref[...]).astype(BF16)
        grad_copy(step, j).start()
    for s in range(blocks):
        stored_o_ref[step, s * BLOCK : (s + 1) * BLOCK, :] = o_ref[pl.ds(order_ref[0, s] * BLOCK, BLOCK), :]

    for i in range(batch):
        @pl.when((mine == i) & (step < last))
        def _(i=i):
            for k in range(ring):
                o_copy(step, k, i).start()

    @pl.when(step == 0)
    def _():
        do_sum.second(down)
        do_sum.to_owner(up)

    @pl.when(step == 1)
    def _():
        do_sum.to_owner(down)

    @pl.when(step == last)
    def _():
        gain = jnp.zeros((1, width), F32)
        shift = jnp.zeros((1, width), F32)
        for s in range(blocks):
            at = pl.ds(s * BLOCK, BLOCK)
            sorted_at = pl.ds(order_ref[0, s] * BLOCK, BLOCK)
            xh, _ = normalized(stored(x_ref, s).astype(F32))
            da = da_ref[sorted_at, :]
            gain += jnp.sum(da * xh, axis=0, keepdims=True)
            shift += jnp.sum(da, axis=0, keepdims=True)
            h_ref[at, :] = (da * norm_ref[1:2, :]).astype(BF16)
        small_ref[0:1, :] = gain
        small_ref[1:2, :] = shift
        small_ref[3:8, :] = jnp.zeros((5, width), F32)
        out = pltpu.make_async_copy(stored_o_ref.at[last], o_last, o_local.at[last])
        out.start()
        do_sum.hand_on(up)
        do_sum.hand_on(down)
        for quad in range(last):
            for i in range(batch):
                @pl.when(mine != i)
                def _(quad=quad, i=i):
                    ref = ret_o.at[i, :, pl.ds(quad * lanes, lanes)]
                    remote(ref, ref, o_send.at[quad, 0], o_recv.at[quad, i], core_id, z).wait_recv()

                @pl.when(mine == i)
                def _(quad=quad, i=i):
                    o_copy(quad, 0, i).wait()
                    for k in range(1, ring):
                        o_copy(quad, k, i).wait_send()
        for quad in range(last + 1):
            for j in range(3):
                grad_copy(quad, j).wait()
        out.wait()


def attend(order, x, g, norms, bias_q, tables, weights, up, down, batch):
    ring, groups_dp = lax.axis_size("ctx"), lax.axis_size("dp")
    teams = (groups_dp // 8).bit_length() - 1
    shapes = ((1, 2 * up.shape[1], 2 * up.shape[2]), (down.shape[1], down.shape[2], 2 * down.shape[3]))
    down = down.reshape(-1, *down.shape[2:])
    rows, width = x.shape
    lanes = QUAD * HD
    groups = width // lanes
    anywhere = pl.BlockSpec(memory_space=pl.ANY)
    whole = lambda shape: pl.BlockSpec(shape, lambda i: (0,) * len(shape))
    once = lambda shape: pl.BlockSpec(shape, lambda i: (0,) * len(shape), pipeline_mode=pl.Buffered(1))
    dma = pltpu.SemaphoreType.DMA
    slices = [(n, r // 4, c // 2) for n, r, c in shapes]
    return pl.pallas_call(
        functools.partial(attend_kernel, teams),
        grid=(groups,),
        in_specs=[
            pl.BlockSpec(memory_space=pltpu.SMEM),
            once((rows, width)),
            once((rows, width)),
            once(norms.shape),
            pl.BlockSpec((8, lanes), lambda i: (0, i)),
            once(tables[0].shape),
            once(tables[0].shape),
            once(tables[0].shape),
            pl.BlockSpec((width, lanes), lambda i: (0, i)),
            pl.BlockSpec((width, lanes), lambda i: (0, groups + i)),
            pl.BlockSpec((width, lanes), lambda i: (0, 2 * groups + i)),
            pl.BlockSpec((lanes, width), lambda i: (i, 3)),
            anywhere,
            anywhere,
        ],
        out_specs=[once((rows, width)), anywhere, once((8, width))] + [anywhere] * 4,
        out_shape=[
            jax.ShapeDtypeStruct((rows, width), BF16),
            jax.ShapeDtypeStruct((width, 3 * width), BF16),
            jax.ShapeDtypeStruct((8, width), F32),
            jax.ShapeDtypeStruct((rows, lanes), BF16),
            jax.ShapeDtypeStruct((batch, rows // ring, width - lanes), BF16),
        ]
        + [jax.ShapeDtypeStruct(shape, BF16) for shape in slices],
        scratch_shapes=[
            pltpu.VMEM((rows, width), BF16),
            pltpu.VMEM((rows, width), BF16),
            pltpu.VMEM((width, rows), BF16),
            pltpu.VMEM((rows, width), F32),
        ]
        + [pltpu.VMEM((rows, lanes), BF16)] * 5
        + [pltpu.VMEM((lanes, rows), BF16)] * 2
        + [pltpu.VMEM((rows, lanes), F32)] * 3
        + [
            pltpu.VMEM((groups, 3, width, lanes), BF16), pltpu.VMEM((groups, rows, lanes), BF16),
            dma((groups, ring)), dma((groups, batch)), dma((groups,)), dma((groups, 3)),
        ]
        + reducer_scratch(MLP_LEVELS, shapes, teams, ring),
        compiler_params=pltpu.CompilerParams(
            collective_id=2, has_side_effects=True, vmem_limit_bytes=60 * MIB
        ),
        cost_estimate=pl.CostEstimate(
            flops=24 * rows * width * width + 8 * rows * rows * width,
            bytes_accessed=16 * width * width + 8 * rows * width,
            transcendentals=HEADS * rows * rows // 2,
        ),
        name="attend",
    )(order, x, g, norms, bias_q, *tables, weights, weights, weights, weights, up, down)


def rotary_tables(length):
    half = ROT // 2
    frequency = ROPE_BASE ** (-(np.arange(half) * 2.0 / ROT))
    angle = np.arange(length)[:, None] * frequency[None, :]
    cosine, sine = np.cos(angle), np.sin(angle)
    rest = np.zeros((length, HD - ROT))
    none = np.zeros_like(sine)
    cos_full = np.concatenate([cosine, cosine, rest + 1.0], axis=1)
    low = np.concatenate([-sine, none, rest], axis=1)
    high = np.concatenate([none, sine, rest], axis=1)
    return tuple(jnp.asarray(np.tile(t, (1, 2)).astype(np.float32)) for t in (cos_full, low, high))


def adamw(weight, grad, first, second, rate, decay):
    first_new = BETA_ONE * first + (1.0 - BETA_ONE) * grad
    second_new = BETA_TWO * second + (1.0 - BETA_TWO) * grad * grad
    first_hat = first_new / (1.0 - BETA_ONE**STEP)
    second_hat = second_new / (1.0 - BETA_TWO**STEP)
    weight_new = weight - rate * (first_hat / (jnp.sqrt(second_hat) + EPS_ADAM) + decay * weight)
    return (first_new, second_new, weight_new)


RATES = (0.1, 0.6, 0.1, 0.05)


def finish_kernel(*refs):
    x_ref, g_ref, attend_ref, feed_ref, h_ref, back_ref, bias_ref, norm_grad = refs[:8]
    norm, norm_first, norm_second = refs[8:11]
    inputs, outputs = refs[11:27], refs[27:]
    layer_out, input_grad = outputs[:2]
    for n, rate in enumerate(RATES):
        weight, grad, first, second = (ref[...] for ref in inputs[4 * n : 4 * n + 4])
        new = adamw(weight, grad.astype(F32), first, second, rate, DECAY)
        for ref, value in zip(outputs[2 + 3 * n : 5 + 3 * n], new):
            ref[...] = value
    width = x_ref.shape[1]
    bias = bias_ref[0:1, width : 2 * width] + bias_ref[0:1, bias_ref.shape[1] - width :]
    rows = x_ref[...].astype(F32)
    layer_out[...] = (rows + attend_ref[...] + feed_ref[...] + bias).astype(BF16)
    xh, scale = normalized(rows)
    h = back_ref[...].astype(F32) + h_ref[...]
    inner = jnp.mean(h * xh, axis=-1, keepdims=True)
    input_grad[...] = g_ref[...].astype(F32) + scale * (h - jnp.mean(h, axis=-1, keepdims=True) - xh * inner)

    @pl.when(pl.program_id(0) == 0)
    def _():
        grad = norm_grad[0:4, : norm.shape[1]]
        first, second, new = adamw(norm[...], grad, norm_first[...], norm_second[...], 0.6, 0.0)
        outputs[14][...] = first
        outputs[15][...] = second[0:2]
        outputs[16][...] = second[2:4]
        outputs[17][...] = new


def finish(rows, biases, norm_grad, norm_args, weights):
    steps = 4
    whole = lambda v: pl.BlockSpec(v.shape, lambda i: (0,) * len(v.shape))
    part = lambda v: pl.BlockSpec((v.shape[0] // steps, v.shape[1]), lambda i: (i, 0))
    like = lambda v, dtype: jax.ShapeDtypeStruct(v.shape, dtype)
    count, width = rows[0].shape
    args = [*rows, biases, norm_grad, *norm_args] + [v for group in weights for v in group]
    specs = [part(v) for v in rows] + [whole(v) for v in (biases, norm_grad, *norm_args)]
    specs += [part(v) for group in weights for v in group]
    outs = [like(rows[0], BF16), like(rows[0], F32)] + [like(group[0], F32) for group in weights for _ in range(3)]
    out_specs = [part(v) for v in outs]
    own = norm_args[0].shape[1]
    norm_outs = [jax.ShapeDtypeStruct((n, own), F32) for n in (4, 2, 2, 4)]
    return pl.pallas_call(
        finish_kernel,
        grid=(steps,),
        in_specs=specs,
        out_specs=out_specs + [whole(v) for v in norm_outs],
        out_shape=outs + norm_outs,
        compiler_params=pltpu.CompilerParams(vmem_limit_bytes=56 * MIB),
        cost_estimate=pl.CostEstimate(flops=0, bytes_accessed=64 * MIB, transcendentals=0),
        name="finish",
    )(*args)


def shards(
    tokens, out_grad, block_order, qkv_weight, out_weight, up_weight, down_weight, norm_params, bias_params,
    qkv_first, qkv_second, out_first, out_second, up_first, up_second, down_first, down_second,
    norm_first, norm_second, bias_first, bias_second,
):
    groups, ring = lax.axis_size("dp"), lax.axis_size("ctx")
    group, rank = lax.axis_index("dp"), lax.axis_index("ctx")
    batch, piece, width = tokens.shape
    length = piece * ring
    count = batch * piece
    ff = up_weight.shape[1]

    share = bias_params.shape[0]
    lanes = share + -share % 128
    small = jnp.concatenate([
        jnp.pad(bias_params[None, :], ((0, 0), (0, lanes - share))),
        jnp.pad(norm_params, ((0, 3), (0, lanes - norm_params.shape[1]))),
    ])
    x_rows, g_rows = tokens.reshape(count, width), out_grad.reshape(count, width)
    att_copy, biases, norms, home_x, home_g, feed_out, h_feed, dup, ddown, dbias_up, small_feed = gather_feed(
        up_weight, down_weight, qkv_weight, out_weight, small, x_rows, g_rows, piece, ring * share
    )

    odd = group % 2

    order = block_order[jnp.clip(rank - odd, 0, batch - 1)]
    spots = jnp.arange(order.shape[0])
    order = jnp.stack([order, jnp.sum(jnp.where(order[None, :] == spots[:, None], spots[None, :], 0), axis=1)])

    h_attend, dqkv, small_attend, o_last, o_first, up_slice, down_slice = attend(
        order, home_x, home_g, norms, biases, rotary_tables(length), att_copy, dup, ddown, batch
    )
    *owned, norm_grad, bias_grad, attend_out, ret_back = reduce_all(
        up_slice, down_slice, dqkv, small_attend, small_feed, dbias_up, h_attend, o_last, o_first, g_rows, att_copy, batch
    )
    up_grad, down_grad, qkv_grad, out_grads = (
        g.reshape(w.shape) for g, w in zip(owned, (up_weight, down_weight, qkv_weight, out_weight))
    )
    layer_out, input_grad, *new, norm_a, norm_b, norm_c, norm_d = finish(
        (x_rows, g_rows, attend_out, feed_out, h_feed, ret_back.reshape(count, width)),
        biases,
        norm_grad,
        (norm_params, norm_first, norm_second),
        (
            (qkv_weight, qkv_grad, qkv_first, qkv_second),
            (out_weight, out_grads, out_first, out_second),
            (up_weight, up_grad, up_first, up_second),
            (down_weight, down_grad, down_first, down_second),
        ),
    )
    bias_new = adamw(bias_params, bias_grad[0, :share], bias_first, bias_second, 0.6, 0.0)
    return (
        layer_out.reshape(tokens.shape), input_grad.reshape(tokens.shape), *new,
        norm_a, norm_b, norm_c, norm_d, *bias_new,
    )


def solution(mesh):
    rows, columns, token = P("ctx", None), P(None, "ctx"), P("dp", "ctx", None)
    in_specs = (token, token, P("dp", None)) + (rows,) * 4 + (columns, P("ctx")) + (rows,) * 8
    in_specs += (columns, columns, P("ctx"), P("ctx"))
    out_specs = (token, token) + (rows,) * 12 + (columns,) * 4 + (P("ctx"),) * 3
    return jax.shard_map(shards, mesh=mesh, in_specs=in_specs, out_specs=out_specs, check_vma=False)
```

```python
import functools
import math
from types import SimpleNamespace

import jax
import jax.numpy as jnp
import numpy as np
from jax import lax
from jax.experimental import pallas as pl
from jax.experimental.pallas import tpu as pltpu
from jax.sharding import PartitionSpec as P

HEADS = 12
HD = 64
STEP = 10
ROT = 16
BLOCK = 128
QUAD = 4
MLP_LEVELS = (2, 1)
LEVELS = (3, 3, 0, 0)

EPS_NORM = 1e-05
BETA_ONE = 0.9
BETA_TWO = 0.95
EPS_ADAM = 1e-08
DECAY = 0.01
ROPE_BASE = 10000.0
F32 = jnp.float32
BF16 = jnp.bfloat16
MIB = 1024 * 1024


def dot(left, right, dims=((1,), (0,))):
    return lax.dot_general(left, right, (dims, ((), ())), preferred_element_type=F32)


NN = ((1,), (0,))
NT = ((1,), (1,))
TN = ((0,), (0,))


def normalized(values):
    mean = jnp.mean(values, axis=-1, keepdims=True)
    centred = values - mean
    variance = jnp.mean(centred * centred, axis=-1, keepdims=True)
    scale = lax.rsqrt(variance + EPS_NORM)
    return centred * scale, scale


MESH = pl.DeviceIdType.MESH


def plane(d):
    core, x, y = d % 2, d // 2 % 2, d // 4 % 2
    return core, x, y, d + 1 - 2 * core, d + 2 - 4 * x, d + 4 - 8 * y


def gather_kernel(
    up, down, qkv, out, small, tokens, cotangents,
    att_all, small_all, norm_all, home_x, home_g, out_ref, h_ref, up_part, down_part, dbias_ref, sums_ref,
    up_all, down_all, att_own, up_wide, down_wide, att_wide, small_in, x_ref, g_ref, m_ref, mt_ref, hid_ref, dup_in_ref,
    dup_ref, up_core, up_first, ddown_ref, down_core,
    z_send, z_recv, p_send, p_recv, s_send, s_recv, t_send, t_recv, local, out_sem, c_send, c_recv,
):
    ring = lax.axis_size("ctx")
    d, z = lax.axis_index("dp"), lax.axis_index("ctx")
    core, x, y, core_id, x_id, y_id = plane(d)
    own = x + 2 * y
    own_x, own_y, far = own + 1 - 2 * x, own + 2 - 4 * y, 3 - own
    count, width = tokens.shape
    piece = home_x.shape[0] // ring
    batch = count // piece
    att = 4
    height, span = att_own.shape[0] // 4, att_own.shape[1] // 2
    strips = ring // 2

    def part(a, base, place, side, half):
        if a == att:
            at = pl.multiple_of(base * att_own.shape[0] + place * height, 16)
            first, wide = side * span, span
            if half is not None:
                first, wide = side * span + half * (span // 2), span // 2
            return att_all.at[pl.ds(at, height), pl.ds(pl.multiple_of(first, 128), wide)]
        n = a // 2
        if a % 2 == 0:
            columns = up_all.shape[2] // 2
            first, count_ = side * strips, strips
            if half is not None:
                first, count_ = side * strips + half * (strips // 2), strips // 2
            at = pl.multiple_of(base * height + base * 3 * height + place * height, 16)
            return up_all.at[pl.ds(first, count_), pl.ds(at, height), pl.ds(n * columns, columns)]
        rows = down_wide.shape[0]
        tall = rows // 8
        at = base * rows + n * (rows // 2) + place * tall
        if half is not None:
            at, tall = at + half * (tall // 2), tall // 2
        return down_all.at[
            pl.ds(pl.multiple_of(at, 16), tall), pl.ds(pl.multiple_of(side * (width // 2), 128), width // 2)
        ]

    def slot(a, base, place, half=None):
        return part(a, base, place, core, half)

    def other_slot(a, base, place):
        return part(a, base, place, 1 - core, None)

    def own_att_slot():
        return att_own.at[
            pl.ds(pl.multiple_of(own * height, 16), height), pl.ds(pl.multiple_of(core * span, 128), span)
        ]

    def remote(src, dst, send, recv, dp, ctx):
        return pltpu.make_async_remote_copy(
            src_ref=src, dst_ref=dst, send_sem=send, recv_sem=recv, device_id=(dp, ctx), device_id_type=MESH
        )

    columns = qkv.shape[1]
    wide_loads = [
        [pltpu.make_async_copy(up, up_wide, local.at[0])],
        [pltpu.make_async_copy(down, down_wide, local.at[1])],
        [
            pltpu.make_async_copy(qkv, att_wide.at[:, pl.ds(0, columns)], local.at[2]),
            pltpu.make_async_copy(out, att_wide.at[:, pl.ds(columns, out.shape[1])], local.at[8]),
        ],
    ]
    for loads in wide_loads:
        for copy in loads:
            copy.start()

    def cast_own(a):
        for copy in wide_loads[a]:
            copy.wait()
        wide, target = ((up_wide, up_all), (down_wide, down_all), (att_wide, att_own))[a]
        rows = wide.shape[0]
        tile = 64
        base = 0 if a == 2 else z * rows

        def body(t, _):
            value = wide[pl.ds(pl.multiple_of(t * tile, 16), tile), :].astype(BF16)
            at = pl.ds(pl.multiple_of(base + t * tile, 16), tile)
            if a == 0:
                columns = target.shape[2]
                for r in range(ring):
                    target[r, at, :] = value[:, r * columns : (r + 1) * columns]
            else:
                target[at, :] = value
            return 0

        lax.fori_loop(0, rows // tile, body, 0)

    barrier = pltpu.get_barrier_semaphore()
    for k in range(1, ring):
        pl.semaphore_signal(barrier, inc=1, device_id=(d, (z + k) % ring), device_id_type=MESH)
    for other in (core_id, x_id, y_id):
        pl.semaphore_signal(barrier, inc=1, device_id=(other, z), device_id_type=MESH)
    cast_own(0)
    pl.semaphore_wait(barrier, ring + 2)

    def hop(a, way, h):
        shard = z - h if way == 0 else z + h
        target = z + 1 if way == 0 else z - 1
        src = own_att_slot() if h == 0 and a == att else slot(a, shard, own)
        return remote(src, slot(a, shard, own), z_send.at[a, way, h], z_recv.at[a, way, h], d, target)

    def can_send(way, h):
        shard = z - h if way == 0 else z + h
        target = z + 1 if way == 0 else z - 1
        return (shard >= 0) & (shard < ring) & (target >= 0) & (target < ring)

    def in_range(way, h):
        shard = z - h if way == 0 else z + h
        return (shard >= 0) & (shard < ring)

    def cast(a, shard, j):
        send, recv = p_send.at[a, shard, j], p_recv.at[a, shard, j]
        if j == 0:
            ref = slot(a, shard, own)
            return remote(ref, ref, send, recv, x_id, z)
        if j == 1:
            ref = slot(a, shard, own)
            return remote(ref, ref, send, recv, y_id, z)
        if j == 2:
            ref = slot(a, shard, own_x, 0)
            return remote(ref, ref, send, recv, y_id, z)
        if j == 3:
            ref = slot(a, shard, own_y, 1)
            return remote(ref, ref, send, recv, x_id, z)
        ref = slot(a, shard, (own, own_x, own_y, far)[j - 4])
        return remote(ref, ref, send, recv, core_id, z)

    def arrived(a, shard, j):
        send, recv = p_send.at[a, shard, j], p_recv.at[a, shard, j]
        ref = {0: lambda: slot(a, shard, own_x), 1: lambda: slot(a, shard, own_y),
               2: lambda: slot(a, shard, far, 0), 3: lambda: slot(a, shard, far, 1)}.get(
            j, lambda: other_slot(a, shard, (own, own_x, own_y, far)[j - 4]))()
        remote(ref, ref, send, recv, core_id, z).wait_recv()

    def start_hops(a):
        for way in range(2):
            @pl.when(can_send(way, 0))
            def _(way=way):
                hop(a, way, 0).start()

    def small_copy(k):
        return remote(small, small_in.at[z], s_send.at[k], s_recv.at[k], d, (z + k) % ring)

    def stage_a(a, h):
        for way in range(2):
            @pl.when(in_range(way, h))
            def _(way=way):
                shard = z - h if way == 0 else z + h
                ref = slot(a, shard, own)
                remote(ref, ref, z_send.at[a, way, h - 1], z_recv.at[a, way, h - 1], core_id, z).wait_recv()

                @pl.when(can_send(way, h))
                def _():
                    hop(a, way, h).start()

                cast(a, shard, 0).start()
                cast(a, shard, 1).start()
                cast(a, shard, 4).start()

    def stage_b(a, h):
        for way in range(2):
            @pl.when(in_range(way, h))
            def _(way=way):
                shard = z - h if way == 0 else z + h
                arrived(a, shard, 0)
                cast(a, shard, 2).start()
                cast(a, shard, 5).start()
                arrived(a, shard, 1)
                cast(a, shard, 3).start()
                cast(a, shard, 6).start()

    def stage_c(a, h):
        for way in range(2):
            @pl.when(in_range(way, h))
            def _(way=way):
                shard = z - h if way == 0 else z + h
                arrived(a, shard, 2)
                arrived(a, shard, 3)
                cast(a, shard, 7).start()

    def stage_d(a, h):
        for way in range(2):
            @pl.when(in_range(way, h))
            def _(way=way):
                shard = z - h if way == 0 else z + h
                for j in range(4, 8):
                    arrived(a, shard, j)

    pairs = ((tokens, home_x), (cotangents, home_g))

    def move(which, i):
        source, whole = pairs[which]
        i = i + core * (batch - 1 - 2 * i)
        src = source.at[pl.ds(pl.multiple_of(i * piece, 16), piece), :]
        dst = whole.at[pl.ds(pl.multiple_of(z * piece, 16), piece), :]
        return src, dst, i + core

    def start_moves(which):
        for i in range(batch):
            src, dst, target = move(which, i)

            @pl.when(target != z)
            def _(src=src, dst=dst, target=target, i=i):
                remote(src, dst, t_send.at[which, i], t_recv.at[which, z], d, target).start()

            @pl.when(target == z)
            def _(src=src, dst=dst):
                pltpu.make_async_copy(src, dst, local.at[6 + which]).start()

    own_rows = pl.ds(pl.multiple_of(z * att_own.shape[0], 16), att_own.shape[0])
    own_att = pltpu.make_async_copy(att_own, att_all.at[own_rows, :], local.at[9])
    x_load = pltpu.make_async_copy(tokens, x_ref, local.at[3])
    g_load = pltpu.make_async_copy(cotangents, g_ref, local.at[4])
    own_small = pltpu.make_async_copy(small, small_in.at[z], local.at[5])

    start_hops(0)
    cast_own(1)
    start_hops(1)
    start_hops(2)
    start_hops(3)
    cast_own(2)
    start_hops(att)
    for k in range(1, ring):
        small_copy(k).start()
    for copy in (own_att, x_load, g_load, own_small):
        copy.start()
    hops = range(1, ring)
    work = [(a, h) for n in range(2) for h in hops for a in (2 * n, 2 * n + 1)]
    early = len(work) // 2
    for n in range(len(work)):
        stage_a(*work[n])
        if 1 <= n <= early:
            stage_b(*work[n - 1])
        if 2 <= n <= early + 1:
            stage_c(*work[n - 2])
    start_moves(0)
    start_moves(1)
    stage_a(att, 1)

    own_small.wait()
    for k in range(1, ring):
        ref = small_in.at[(z + ring - k) % ring]
        remote(ref, ref, s_send.at[k], s_recv.at[k], core_id, z).wait_recv()
    x_load.wait()
    g_load.wait()
    entries = small_all.shape[1]
    biases = jnp.zeros((8, entries), F32)
    norms = jnp.zeros((8, width), F32)
    for r in range(ring):
        block = small_in[r].astype(BF16).astype(F32)
        full = jnp.concatenate([block, jnp.zeros((8, entries - block.shape[1]), F32)], axis=1)
        biases += pltpu.roll(full, r * (entries // ring), 1) if r else full
        norms += pltpu.roll(block[:, :width], r * (width // ring), 1) if r else block[:, :width]
    small_all[...] = biases
    norm_all[...] = norms
    ff = ring * up_all.shape[2]
    gain_2, shift_2 = norm_all[3:4, :], norm_all[4:5, :]
    tile = 256
    tiles = count // tile
    for t in range(tiles):
        at = pl.ds(t * tile, tile)
        xh, _ = normalized(x_ref[at, :].astype(F32))
        m = xh * gain_2 + shift_2
        m_ref[at, :] = m.astype(BF16)
        mt_ref[:, at] = m.T.astype(BF16)
        out_ref[at, :] = jnp.zeros((tile, width), F32)
        h_ref[at, :] = jnp.zeros((tile, width), F32)
    for h in hops:
        stage_d(0, h)
        stage_d(1, h)

    strip = dup_ref.shape[3] // ring
    steps = ff // (ring * strip)
    half = ring // 2
    big, by_core = (dup_ref, ddown_ref), (up_core, down_core)
    bits, ids = ((x, y), (y, x)), ((x_id, y_id), (y_id, x_id))

    def sizes(a):
        return by_core[a].shape[2], by_core[a].shape[3]

    def slice_of(order):
        return 2 * bits[order][0] + bits[order][1]

    def core_copy(a, i):
        _, span = sizes(a)
        away = pl.ds(pl.multiple_of((1 - core) * span, 128), span)
        return remote(big[a].at[i, :, :, away], by_core[a].at[i], c_send.at[a, i, 0], c_recv.at[a, i, 0], core_id, z)

    def first_copy(a, i, order):
        height, _ = sizes(a)
        own = pl.ds(order * half, half)
        away = pl.ds(pl.multiple_of((1 - bits[order][0]) * (height // 2), 16), height // 2)
        return remote(
            by_core[a].at[i, own, away, :], up_first.at[i, own], c_send.at[a, i, 1 + order],
            c_recv.at[a, i, 1 + order], ids[order][0], z,
        )

    def add(into, at, term, owners):
        height = term(0).shape[0]
        tile = 32 if height % 48 else 48

        def body(n, _):
            o, t = n // (height // tile), n % (height // tile)
            spot = pl.ds(pl.multiple_of(at + t * tile, 16), tile)
            value = term(o)[pl.ds(pl.multiple_of(t * tile, 16), tile), :]
            into[o, spot, :] = (into[o, spot, :].astype(F32) + value.astype(F32)).astype(BF16)
            return 0

        lax.fori_loop(0, owners * (height // tile), body, 0)

    def chunk_1(i):
        for a in range(2):
            _, span = sizes(a)
            core_copy(a, i).wait_recv()
            keep = pl.ds(pl.multiple_of(core * span, 128), span)
            add(by_core[a].at[i], 0, lambda o: big[a].at[i, o, :, keep], ring)
        for order in range(2):
            first_copy(0, i, order).start()
        parts_out(1, i)[0].start()

    def chunk_2(i):
        height, _ = sizes(0)
        for order in range(2):
            own = pl.ds(order * half, half)
            first_copy(0, i, order).wait_recv()
            at = bits[order][0] * (height // 2)
            add(by_core[0].at[i, own], at, lambda o: up_first.at[i, order * half + o], half)
        for copy in parts_out(0, i):
            copy.start()

    def parts_out(a, i):
        height, span = sizes(a)
        if a == 1:
            return [pltpu.make_async_copy(by_core[1].at[i], down_part.at[:, i], out_sem.at[i, 2 * half])]
        copies = []
        for order in range(2):
            own = pl.ds(order * half, half)
            rows = pl.ds(pl.multiple_of(bits[order][0] * (height // 2), 16), height // 2)
            for n in range(half):
                copies.append(pltpu.make_async_copy(
                    by_core[0].at[i, own, rows, pl.ds(n * strip, strip)],
                    up_part.at[own, :, pl.ds(pl.multiple_of(n * steps * strip + i * strip, 128), strip)],
                    out_sem.at[i, half * order + n],
                ))
        return copies

    def feed_step(step, _):
        def at_step(n, stage, which):
            @pl.when(step == n)
            def _():
                for h in hops:
                    for a in which:
                        stage(a, h)

        at_step(1, stage_b, (2, 3))
        at_step(2, stage_c, (2, 3))
        at_step(3, stage_d, (2, 3))
        for h in hops:
            @pl.when((step == 2 * h - 2) & (h > 1))
            def _(h=h):
                stage_a(att, h)

            @pl.when(step == 2 * h + 1)
            def _(h=h):
                stage_b(att, h)

            @pl.when(step == 2 * h + 2)
            def _(h=h):
                stage_c(att, h)

        @pl.when(step < steps)
        def _():
            spots = [pl.ds(pl.multiple_of(r * (ff // ring) + step * strip, 128), strip) for r in range(ring)]
            bias_spots = [
                pl.ds(pl.multiple_of(2 * width + r * (ff // ring) + step * strip, 128), strip) for r in range(ring)
            ]
            inner = pl.ds(pl.multiple_of(step * strip, 128), strip)
            up_part_ = jnp.concatenate([up_all[r, :, inner] for r in range(ring)], axis=1)
            down_part_ = jnp.concatenate([down_all[at, :] for at in spots], axis=0)
            bias = jnp.concatenate([small_all[0:1, at] for at in bias_spots], axis=1)
            total = jnp.zeros((1, ring * strip), F32)
            for t in range(tiles):
                at = pl.ds(t * tile, tile)
                u = dot(m_ref[at, :], up_part_) + bias
                cdf = 0.5 * (1.0 + lax.erf(u * (1.0 / math.sqrt(2.0))))
                hidden = (u * cdf).astype(BF16)
                slope = cdf + u * jnp.exp(-0.5 * u * u) * (1.0 / math.sqrt(2.0 * math.pi))
                back = (dot(g_ref[at, :], down_part_, NT) * slope).astype(BF16)
                hid_ref[at, :] = hidden
                dup_in_ref[at, :] = back
                total += jnp.sum(back.astype(F32), axis=0, keepdims=True)
                out_ref[at, :] += dot(hidden, down_part_)
                h_ref[at, :] += dot(back, up_part_, NT)
            for r in range(ring):
                dbias_ref[0:1, spots[r]] = total[:, r * strip : (r + 1) * strip]
            ddown = dot(hid_ref[...], g_ref[...], TN).astype(BF16)
            dup = dot(mt_ref[...], dup_in_ref[...]).astype(BF16)
            for r in range(ring):
                ddown_ref[step, r] = ddown[r * strip : (r + 1) * strip, :]
                dup_ref[step, r] = dup[r * (width // ring) : (r + 1) * (width // ring), :]
            core_copy(0, step).start()
            core_copy(1, step).start()

        for lag, stage in ((1, chunk_1), (3, chunk_2)):
            @pl.when((step >= lag) & (step < steps + lag))
            def _(lag=lag, stage=stage):
                stage(step - lag)

        return 0

    lax.fori_loop(0, steps + 3, feed_step, 0)

    gain = jnp.zeros((1, width), F32)
    shift = jnp.zeros((1, width), F32)
    sums = jnp.zeros((1, width), F32)
    for t in range(tiles):
        at = pl.ds(t * tile, tile)
        xh, _ = normalized(x_ref[at, :].astype(F32))
        dm = h_ref[at, :]
        gain += jnp.sum(dm * xh, axis=0, keepdims=True)
        shift += jnp.sum(dm, axis=0, keepdims=True)
        sums += jnp.sum(g_ref[at, :].astype(F32), axis=0, keepdims=True)
        h_ref[at, :] = dm * gain_2
    sums_ref[...] = jnp.concatenate([gain, shift, sums, jnp.zeros((5, width), F32)], axis=0)

    mine = z - core
    for which in range(2):
        for k in range(1, ring):
            @pl.when((mine >= 0) & (mine < batch))
            def _(which=which, k=k):
                other = (z + k) % ring
                ref = pairs[which][1].at[pl.ds(pl.multiple_of(other * piece, 16), piece), :]
                remote(ref, ref, t_send.at[which, 0], t_recv.at[which, other], core_id, z).wait_recv()
    for h in hops:
        stage_d(att, h)
    for k in range(1, ring):
        small_copy(k).wait_send()
    for a in range(5):
        for way in range(2):
            for h in range(ring - 1):
                @pl.when(can_send(way, h))
                def _(a=a, way=way, h=h):
                    hop(a, way, h).wait_send()
        for h in hops:
            for way in range(2):
                @pl.when(in_range(way, h))
                def _(a=a, h=h, way=way):
                    shard = z - h if way == 0 else z + h
                    for j in range(8):
                        cast(a, shard, j).wait_send()
    for which in range(2):
        for i in range(batch):
            src, dst, target = move(which, i)

            @pl.when(target != z)
            def _(src=src, dst=dst, target=target, which=which, i=i):
                remote(src, dst, t_send.at[which, i], t_recv.at[which, z], d, target).wait_send()

            @pl.when(target == z)
            def _(src=src, dst=dst, which=which):
                pltpu.make_async_copy(src, dst, local.at[6 + which]).wait()
    own_att.wait()

    def close(i, _):
        for a in range(2):
            core_copy(a, i).wait_send()
            for copy in parts_out(a, i):
                copy.wait()
        for order in range(2):
            first_copy(0, i, order).wait_send()
        return 0

    lax.fori_loop(0, steps, close, 0)


def gather_feed(up, down, qkv, out, small, tokens, cotangents, piece, entries):
    ring = lax.axis_size("ctx")
    count, width = tokens.shape
    ff = up.shape[1]
    strip = 128
    chunk = ring * strip
    steps = ff // chunk
    shard = up.shape[0]
    columns = qkv.shape[1] + out.shape[1]
    home = jax.ShapeDtypeStruct((ring * piece, width), tokens.dtype)
    rows = jax.ShapeDtypeStruct((count, width), F32)
    dma = pltpu.SemaphoreType.DMA
    anywhere = pl.BlockSpec(memory_space=pl.ANY)
    vmem = pl.BlockSpec(memory_space=pltpu.VMEM)
    return pl.pallas_call(
        gather_kernel,
        in_specs=[anywhere] * 7,
        out_specs=[anywhere, vmem, vmem, anywhere, anywhere, vmem, vmem, anywhere, anywhere, vmem, vmem],
        out_shape=[
            jax.ShapeDtypeStruct((ring * shard, columns), BF16),
            jax.ShapeDtypeStruct((8, entries), F32), jax.ShapeDtypeStruct((8, width), F32), home, home, rows, rows,
            jax.ShapeDtypeStruct((ring, shard // 2, ff // 2), BF16),
            jax.ShapeDtypeStruct((ring, steps, strip, width // 2), BF16),
            jax.ShapeDtypeStruct((8, ff), F32), jax.ShapeDtypeStruct((8, width), F32),
        ],
        scratch_shapes=[
            pltpu.VMEM((ring, ring * shard, ff // ring), BF16), pltpu.VMEM((ring * down.shape[0], width), BF16),
            pltpu.VMEM((shard, columns), BF16),
            pltpu.VMEM(up.shape, F32), pltpu.VMEM(down.shape, F32), pltpu.VMEM((shard, columns), F32),
            pltpu.VMEM((ring, *small.shape), F32),
            pltpu.VMEM((count, width), BF16), pltpu.VMEM((count, width), BF16), pltpu.VMEM((count, width), BF16),
            pltpu.VMEM((width, count), BF16),
            pltpu.VMEM((count, chunk), BF16), pltpu.VMEM((count, chunk), BF16),
            pltpu.VMEM((steps, ring, shard, chunk), BF16), pltpu.VMEM((steps, ring, shard, chunk // 2), BF16),
            pltpu.VMEM((steps, ring, shard // 2, chunk // 2), BF16),
            pltpu.VMEM((steps, ring, strip, width), BF16), pltpu.VMEM((steps, ring, strip, width // 2), BF16),
            dma((5, 2, ring)), dma((5, 2, ring)), dma((5, ring, 8)), dma((5, ring, 8)),
            dma((ring,)), dma((ring,)), dma((2, count // piece)), dma((2, ring)), dma((10,)), dma((steps, ring + 1)),
            dma((2, steps, 3)), dma((2, steps, 3)),
        ],
        compiler_params=pltpu.CompilerParams(
            collective_id=0, has_side_effects=True, vmem_limit_bytes=60 * MIB
        ),
        cost_estimate=pl.CostEstimate(
            flops=12 * count * width * ff, bytes_accessed=60 * MIB, transcendentals=count * ff
        ),
        name="gather_feed",
    )(up, down, qkv, out, small, tokens, cotangents)


def remote(src, dst, send_sem, recv_sem, dp, ctx):
    return pltpu.make_async_remote_copy(
        src_ref=src, dst_ref=dst, send_sem=send_sem, recv_sem=recv_sem, device_id=(dp, ctx), device_id_type=MESH
    )


def team_id(d, t):
    return d + (8 << t) * (1 - 2 * (d // (8 << t) % 2))


def greet(teams):
    ring = lax.axis_size("ctx")
    d, z = lax.axis_index("dp"), lax.axis_index("ctx")
    core, x, y, core_id, x_id, y_id = plane(d)
    barrier = pltpu.get_barrier_semaphore()
    partners = [core_id, x_id, y_id, x_id + y_id - d] + [team_id(d, t) for t in range(teams)]
    for k in range(1, ring):
        pl.semaphore_signal(barrier, inc=1, device_id=(d, (z + k) % ring), device_id_type=MESH)
    for other in partners:
        pl.semaphore_signal(barrier, inc=1, device_id=(other, z), device_id_type=MESH)
    pl.semaphore_wait(barrier, ring - 1 + len(partners))


def reducer(teams, levels, ins, sums, bufs, send, recv, load):
    count = len(ins)
    ring = lax.axis_size("ctx")
    d, z = lax.axis_index("dp"), lax.axis_index("ctx")
    core, x, y, core_id, x_id, y_id = plane(d)
    far_id = x_id + y_id - d
    bits, ids = ((x, y), (y, x)), ((x_id, y_id), (y_id, x_id))
    spots = ((x, y), (1 - x, y), (x, 1 - y), (1 - x, 1 - y))

    def sizes(a):
        _, strips, quarter, span = bufs[a][-1].shape
        return strips, quarter, span

    def owners(a, order):
        strips = sizes(a)[0]
        return pl.ds(order * ring // 2 * strips, ring // 2 * strips)

    def rows_at(at, height):
        return pl.ds(pl.multiple_of(at, 16), height)

    def kept(a, order):
        return 0 if levels[a] == 2 else bits[order][0] * 2 * sizes(a)[1]

    def core_copy(a):
        span = sizes(a)[2]
        away = pl.ds(pl.multiple_of((1 - core) * span, 128), span)
        return remote(ins[a].at[:, :, away], bufs[a][1], send.at[a, 0], recv.at[a, 0], core_id, z)

    def own_load(a):
        if levels[a] == 3:
            return pltpu.make_async_copy(ins[a], bufs[a][5].at[0], load.at[a])
        span = sizes(a)[2]
        keep = pl.ds(pl.multiple_of(core * span, 128), span)
        src = ins[a].at[:, :, keep] if levels[a] == 0 else ins[a]
        return pltpu.make_async_copy(src, bufs[a][0], load.at[a])

    def first_copy(a, order):
        quarter = sizes(a)[1]
        away = rows_at((1 - bits[order][0]) * 2 * quarter, 2 * quarter)
        return remote(
            bufs[a][0].at[owners(a, order), away, :], bufs[a][2].at[owners(a, order)], send.at[a, 1 + order],
            recv.at[a, 1 + order], ids[order][0], z,
        )

    def second_copy(a, order):
        quarter = sizes(a)[1]
        away = rows_at(kept(a, order) + (1 - bits[order][1]) * quarter, quarter)
        return remote(
            bufs[a][0].at[owners(a, order), away, :], bufs[a][3].at[owners(a, order)], send.at[a, 3 + order],
            recv.at[a, 3 + order], ids[order][1], z,
        )

    def own_quarter(a, owner):
        strips, quarter, _ = sizes(a)
        order = owner // (ring // 2)
        first, second = (1 - order) * x + order * y, (1 - order) * y + order * x
        at = second * quarter if levels[a] == 2 else (2 * first + second) * quarter
        return bufs[a][0].at[pl.ds(owner * strips, strips), rows_at(at, quarter), :]

    def owner_copy(a, k):
        to = (z + k) % ring
        return remote(own_quarter(a, to), bufs[a][4].at[k - 1], send.at[a, 4 + k], recv.at[a, 4 + k], d, to)

    def team_copy(a, t):
        j = 4 + ring + 7 + t
        return remote(bufs[a][5].at[0], bufs[a][5].at[1 + t], send.at[a, j], recv.at[a, j], team_id(d, t), z)

    def final(a, spot, side):
        strips, quarter, span = sizes(a)
        order = z // (ring // 2)
        xx, yy = spots[spot]
        at = ((1 - order) * (2 * xx + yy) + order * (2 * yy + xx)) * quarter
        return sums[a].at[:, rows_at(at, quarter), pl.ds(pl.multiple_of(side * span, 128), span)]

    def spread(a, j):
        s, r = send.at[a, 4 + ring + j - 1], recv.at[a, 4 + ring + j - 1]
        if j < 4:
            return remote(bufs[a][5].at[0], final(a, 0, core), s, r, (x_id, y_id, far_id)[j - 1], z)
        src = bufs[a][5].at[0] if j == 4 else final(a, j - 4, core)
        return remote(src, final(a, j - 4, core), s, r, core_id, z)

    def spread_here(a, j):
        s, r = send.at[a, 4 + ring + j - 1], recv.at[a, 4 + ring + j - 1]
        ref = final(a, j, core) if j < 4 else final(a, j - 4, 1 - core)
        remote(ref, ref, s, r, core_id, z).wait_recv()

    def keep_own(a):
        return pltpu.make_async_copy(bufs[a][5].at[0], final(a, 0, core), load.at[count + a])

    def add(into, at, term, blocks):
        height = term.shape[1]
        tile = 32 if height % 48 else 48

        def body(n, _):
            o, t = n // (height // tile), n % (height // tile)
            spot = rows_at(at + t * tile, tile)
            value = term[o, rows_at(t * tile, tile), :]
            into[o, spot, :] = (into[o, spot, :].astype(F32) + value.astype(F32)).astype(BF16)
            return 0

        lax.fori_loop(0, blocks * (height // tile), body, 0)

    def enter(a):
        if levels[a] == 0:
            core_copy(a).start()
        own_load(a).start()

    def first(a):
        own_load(a).wait()
        if levels[a] == 0:
            core_copy(a).wait_recv()
            add(bufs[a][0], 0, bufs[a][1], bufs[a][0].shape[0])
        if levels[a] < 2:
            for order in range(2):
                first_copy(a, order).start()

    def second(a):
        for order in range(2):
            if levels[a] < 2:
                first_copy(a, order).wait_recv()
                own = owners(a, order)
                add(bufs[a][0].at[own], kept(a, order), bufs[a][2].at[own], ring // 2 * sizes(a)[0])
            second_copy(a, order).start()

    def to_owner(a):
        for order in range(2):
            second_copy(a, order).wait_recv()
            own = owners(a, order)
            at = kept(a, order) + bits[order][1] * sizes(a)[1]
            add(bufs[a][0].at[own], at, bufs[a][3].at[own], ring // 2 * sizes(a)[0])
        for k in range(1, ring):
            owner_copy(a, k).start()

    def add_up(a):
        for k in range(1, ring):
            owner_copy(a, k).wait_recv()
        mine = own_quarter(a, z)
        for s in range(sizes(a)[0]):
            terms = [mine[s]] + [bufs[a][4][k, s] for k in range(ring - 1)]
            bufs[a][5][0, s] = sum((t.astype(F32) for t in terms[1:]), terms[0].astype(F32)).astype(BF16)
        for t in range(teams):
            team_copy(a, t).start()
            team_copy(a, t).wait()
            bufs[a][5][0] = (bufs[a][5][0].astype(F32) + bufs[a][5][1 + t].astype(F32)).astype(BF16)

    def total(a):
        if levels[a] == 3:
            own_load(a).wait()
        else:
            add_up(a)
        keep_own(a).start()
        for j in range(1, 5):
            spread(a, j).start()

    def hand_on(a):
        add_up(a)
        out = pltpu.make_async_copy(bufs[a][5].at[0], sums[a], load.at[count + a])
        out.start()
        sent(a)
        out.wait()

    def share(a):
        for j in range(1, 4):
            spread_here(a, j)
            spread(a, 4 + j).start()

    def sent(a):
        if levels[a] == 0:
            core_copy(a).wait_send()
        for order in range(2):
            if levels[a] < 2:
                first_copy(a, order).wait_send()
            second_copy(a, order).wait_send()
        for k in range(1, ring):
            owner_copy(a, k).wait_send()

    def close(a):
        for j in range(4, 8):
            spread_here(a, j)
        if levels[a] < 3:
            sent(a)
        for j in range(1, 8):
            spread(a, j).wait_send()
        keep_own(a).wait()

    return SimpleNamespace(
        enter=enter, first=first, second=second, to_owner=to_owner, total=total, hand_on=hand_on, share=share, close=close
    )


def reducer_scratch(levels, shapes, teams, ring):
    scratch = []
    for level, (strips, rows, columns) in zip(levels, shapes):
        blocks, span = ring * strips, columns // 2
        none = (1, 16, 128)
        scratch += [
            pltpu.VMEM(none if level == 3 else (blocks, rows // 2 if level == 2 else rows, span), BF16),
            pltpu.VMEM((blocks, rows, span) if level == 0 else none, BF16),
            pltpu.VMEM((blocks, rows // 2, span) if level < 2 else none, BF16),
            pltpu.VMEM((blocks, rows // 4, span) if level < 3 else none, BF16),
            pltpu.VMEM((ring - 1, strips, rows // 4, span) if level < 3 else (1, *none), BF16),
            pltpu.VMEM((1 + teams, strips, rows // 4, span), BF16),
        ]
    copies = 4 + ring + 7 + teams
    dma = pltpu.SemaphoreType.DMA
    return scratch + [dma((len(levels), copies)), dma((len(levels), copies)), dma((2 * len(levels),))]


def reduce_kernel(
    teams, up_ref, down_ref, qkv_ref, small_att, small_mlp, small_up, back_ref, o_ref, g_ref, weights,
    up_sum, down_sum, qkv_sum, out_sum, norm_out, bias_out, attend_out, ret_back, *refs,
):
    ring = lax.axis_size("ctx")
    d, z = lax.axis_index("dp"), lax.axis_index("ctx")
    core, x, y, core_id, x_id, y_id = plane(d)
    bufs = [refs[6 * a : 6 * a + 6] for a in range(4)]
    send, recv, load, wo_ref, dwo_ref, small_acc, small_in = refs[24:31]
    s_send, s_recv, r_send, r_recv, r_local = refs[31:]
    batch, piece, width = ret_back.shape
    up, down, qkv, out = range(4)
    ins, sums = (up_ref, down_ref, qkv_ref, dwo_ref), (up_sum, down_sum, qkv_sum, out_sum)
    do = reducer(teams, LEVELS, ins, sums, bufs, send, recv, load)

    pairs = ((back_ref, ret_back),)
    mine = z - core

    def returned(which, i, to):
        source, target = pairs[which]
        return source.at[pl.ds(pl.multiple_of(to * piece, 16), piece), :], target.at[i]

    def start_returns(which):
        for i in range(batch):
            @pl.when(mine == i)
            def _(i=i):
                for k in range(1, ring):
                    to = (z + k) % ring
                    src, dst = returned(which, i, to)
                    remote(src, dst, r_send.at[which, k], r_recv.at[which, i], d, to).start()
                src, dst = returned(which, i, z)
                pltpu.make_async_copy(src, dst, r_local.at[which]).start()

    def wait_returns(which):
        for i in range(batch):
            src, dst = returned(which, i, z)

            @pl.when(mine == i)
            def _(src=src, dst=dst):
                pltpu.make_async_copy(src, dst, r_local.at[which]).wait()

            @pl.when(mine != i)
            def _(i=i, src=src, dst=dst):
                remote(src, dst, r_send.at[which, 0], r_recv.at[which, i], core_id, z).wait_recv()

    def close_returns(which):
        for i in range(batch):
            @pl.when(mine == i)
            def _(i=i):
                for k in range(1, ring):
                    to = (z + k) % ring
                    remote(*returned(which, i, to), r_send.at[which, k], r_recv.at[which, i], d, to).wait_send()

    steps = [core_id, x_id, y_id] + [team_id(d, t) for t in range(teams)]

    def small_copy(n):
        return remote(small_acc, small_in.at[n], s_send.at[n], s_recv.at[n], steps[n], z)

    def small_owner(k):
        n = len(steps) + k - 1
        return remote(small_acc, small_in.at[n], s_send.at[n], s_recv.at[n], d, (z + k) % ring)

    def small_close(n):
        small_copy(n).wait()
        small_acc[...] += small_in[n]
        if n + 1 < len(steps):
            small_copy(n + 1).start()
        else:
            for k in range(1, ring):
                small_owner(k).start()

    columns = weights.shape[1] - width
    wo_load = pltpu.make_async_copy(weights.at[:, pl.ds(columns, width)], wo_ref, r_local.at[2])
    wo_load.start()
    small_acc[0:8, :] = small_att[...]
    small_acc[8:16, :] = small_mlp[...]
    for n in range(small_up.shape[1] // width):
        small_acc[16 + n : 17 + n, :] = small_up[0:1, n * width : (n + 1) * width]
    rest = 16 + small_up.shape[1] // width
    small_acc[rest:, :] = jnp.zeros((small_acc.shape[0] - rest, width), F32)
    greet(teams)
    do.enter(qkv)
    start_returns(0)
    do.enter(up)
    do.enter(down)
    small_copy(0).start()
    do.total(up)
    do.total(down)
    dwo = dot(o_ref[...], g_ref[...], TN).astype(BF16)
    for r in range(ring):
        dwo_ref[r] = dwo[r * (width // ring) : (r + 1) * (width // ring), :]
    do.enter(out)
    do.first(qkv)
    do.first(out)
    small_close(0)
    do.share(up)
    do.share(down)
    wo_load.wait()
    for i in range(batch):
        at = pl.ds(i * piece, piece)
        attend_out[at, :] = dot(o_ref[at, :], wo_ref[...])
    do.second(qkv)
    do.second(out)
    small_close(1)
    do.to_owner(qkv)
    do.to_owner(out)
    for n in range(2, len(steps)):
        small_close(n)
    do.total(qkv)
    do.total(out)
    for k in range(1, ring):
        small_owner(k).wait()
    total = small_acc[...]
    for k in range(ring - 1):
        total += small_in[len(steps) + k]
    norm = jnp.concatenate([total[0:2], total[8:10], jnp.zeros((4, width), F32)], axis=0)
    norm_out[...] = pltpu.roll(norm, (ring - z) % ring * (width // ring), 1)
    ups = [total[16 + n : 17 + n] for n in range(small_up.shape[1] // width)]
    bias = jnp.concatenate([total[2:3], total[10:11], *ups, total[10:11]], axis=1)
    entries = bias.shape[1]
    bias = pltpu.roll(jnp.broadcast_to(bias, (8, entries)), (ring - z) % ring * (entries // ring), 1)
    bias_out[...] = bias[:, : bias_out.shape[1]]
    do.share(qkv)
    do.share(out)
    for a in range(4):
        do.close(a)
    wait_returns(0)
    close_returns(0)


def reduce_all(up, down, qkv, small_att, small_mlp, small_up, back, o, g, weights, batch):
    ring, groups = lax.axis_size("ctx"), lax.axis_size("dp")
    teams = (groups // 8).bit_length() - 1
    width = g.shape[1]
    piece = g.shape[0] // batch
    shapes = [(n, 4 * rows, 2 * span) for n, rows, span in (up.shape, down.shape)]
    shapes += [(1, width // ring, qkv.shape[1]), (1, width // ring, width)]
    dma = pltpu.SemaphoreType.DMA
    anywhere = pl.BlockSpec(memory_space=pl.ANY)
    vmem = pl.BlockSpec(memory_space=pltpu.VMEM)
    rounds = 3 + teams + ring - 1
    small = (16 + -(-small_up.shape[1] // width // 8) * 8, width)
    share = (3 * width + small_up.shape[1]) // ring
    scratch = reducer_scratch(LEVELS, shapes, teams, ring)
    scratch += [
        pltpu.VMEM((width, width), BF16),
        pltpu.VMEM((ring, width // ring, width), BF16), pltpu.VMEM(small, F32), pltpu.VMEM((rounds, *small), F32),
        dma((rounds,)), dma((rounds,)), dma((1, ring)), dma((1, batch)), dma((3,)),
    ]
    return pl.pallas_call(
        functools.partial(reduce_kernel, teams),
        in_specs=[anywhere] * 3 + [vmem] * 3 + [anywhere, vmem, vmem, anywhere],
        out_specs=[anywhere] * 4 + [vmem, vmem, vmem, anywhere],
        out_shape=[jax.ShapeDtypeStruct(shape, BF16) for shape in shapes]
        + [
            jax.ShapeDtypeStruct((8, width), F32), jax.ShapeDtypeStruct((8, share + -share % 128), F32),
            jax.ShapeDtypeStruct(g.shape, F32),
            jax.ShapeDtypeStruct((batch, piece, width), BF16),
        ],
        scratch_shapes=scratch,
        compiler_params=pltpu.CompilerParams(collective_id=1, has_side_effects=True, vmem_limit_bytes=26 * MIB),
        cost_estimate=pl.CostEstimate(flops=4 * width * width * g.shape[0], bytes_accessed=60 * MIB, transcendentals=0),
        name="reduce",
    )(
        up, down, qkv.reshape(ring, width // ring, -1), small_att, small_mlp, small_up, back,
        o.reshape(batch * piece, -1), g, weights,
    )


def attend_kernel(
    teams, order_ref, x_ref, stored_g_ref, norm_ref, bias_ref, cos_ref, low_ref, high_ref, wq_ref, wk_ref, wv_ref,
    wo_ref, up_ref, down_ref, h_ref, dqkv_all, small_ref, ret_o, up_sum, down_sum,
    g_ref, a_ref, at_ref, da_ref, q_ref, k_ref, v_ref, do_ref, o_ref, kt_ref, vt_ref, dqs_ref, dks_ref, dvs_ref,
    grad_ref, stored_o_ref, o_send, o_recv, o_local, grad_sem, *reduce_refs,
):
    step = pl.program_id(0)
    last = grad_ref.shape[0] - 1
    rows, width = x_ref.shape
    lanes = QUAD * HD
    tile = 256
    half = ROT // 2
    scale = 1.0 / math.sqrt(HD)
    blocks = rows // BLOCK
    ring = lax.axis_size("ctx")
    d, z = lax.axis_index("dp"), lax.axis_index("ctx")
    core_id = plane(d)[3]
    batch, piece = ret_o.shape[:2]
    mine = z - d % 2
    is_home = (mine >= 0) & (mine < batch)
    up, down = 0, 1
    bufs = (reduce_refs[:6], reduce_refs[6:12])
    do_sum = reducer(teams, MLP_LEVELS, (up_ref, down_ref), (up_sum, down_sum), bufs, *reduce_refs[12:])

    @pl.when(step == 0)
    def _():
        do_sum.enter(down)
        do_sum.enter(up)
        greet(teams)
        do_sum.first(down)
        do_sum.first(up)
        do_sum.second(up)

    def o_copy(quad, k, i):
        to = (z + k) % ring
        src = stored_o_ref.at[quad, pl.ds(pl.multiple_of(to * piece, 16), piece), :]
        dst = ret_o.at[i, :, pl.ds(pl.multiple_of(quad * lanes, 128), lanes)]
        if k == 0:
            return pltpu.make_async_copy(src, dst, o_local.at[quad])
        return remote(src, dst, o_send.at[quad, k], o_recv.at[quad, i], d, to)

    def grad_copy(quad, j):
        at = pl.ds(pl.multiple_of(j * width + quad * lanes, 128), lanes)
        return pltpu.make_async_copy(grad_ref.at[quad, j], dqkv_all.at[:, at], grad_sem.at[quad, j])


    def stored(ref, at):
        values = ref[pl.ds(at * BLOCK, BLOCK), :]
        return jnp.where(is_home, values, jnp.zeros_like(values))

    @pl.when(step == 0)
    def _():
        for j in range(blocks):
            place = order_ref[1, j]
            at = pl.ds(j * BLOCK, BLOCK)
            xh, _ = normalized(stored(x_ref, place).astype(F32))
            a = xh * norm_ref[1:2, :] + norm_ref[2:3, :]
            a_ref[at, :] = a.astype(BF16)
            at_ref[:, at] = a.T.astype(BF16)
            g_ref[at, :] = stored(stored_g_ref, place)
        da_ref[...] = jnp.zeros_like(da_ref)

    def table(ref, at):
        values = ref[at, :]
        return jnp.concatenate([values] * (lanes // values.shape[1]), axis=1)

    def turn(values, at):
        low = pltpu.roll(values, lanes - half, 1) * table(low_ref, at)
        high = pltpu.roll(values, half, 1) * table(high_ref, at)
        return values * table(cos_ref, at), low + high

    for t in range(rows // tile):
        at = pl.ds(t * tile, tile)
        a = a_ref[at, :]
        same, cross = turn(dot(a, wq_ref[...]) + bias_ref[0:1, :], at)
        q_ref[at, :] = ((same + cross).astype(BF16) * scale).astype(BF16)
        same, cross = turn(dot(a, wk_ref[...]), at)
        keys = same + cross
        k_ref[at, :] = keys.astype(BF16)
        kt_ref[:, at] = keys.T.astype(BF16)
        values = dot(a, wv_ref[...])
        v_ref[at, :] = values.astype(BF16)
        vt_ref[:, at] = values.T.astype(BF16)
        mixed_back = dot(g_ref[at, :], wo_ref[...], NT)
        do_ref[at, :] = mixed_back.astype(BF16)

    dks_ref[...] = jnp.zeros_like(dks_ref)
    dvs_ref[...] = jnp.zeros_like(dvs_ref)
    wide = 2 * HD
    head_of = lax.broadcasted_iota(jnp.int32, (BLOCK, wide), 1) // HD

    def stack(values):
        zero = jnp.zeros_like(values)
        return jnp.concatenate([jnp.where(head_of == e, values, zero) for e in range(2)], axis=0)

    def diagonal(values):
        return jnp.concatenate([values[e * HD : (e + 1) * HD, e * BLOCK : (e + 1) * BLOCK] for e in range(2)], axis=0)

    spot = lax.broadcasted_iota(jnp.int32, (BLOCK, 2 * BLOCK), 1) % BLOCK
    admitted = lax.broadcasted_iota(jnp.int32, (BLOCK, 2 * BLOCK), 0) <= spot

    def products_in(b, p):
        at, seen, own = pl.ds(b * BLOCK, BLOCK), pl.ds(0, (b + 1) * BLOCK), pl.ds(p * wide, wide)
        q, do = stack(q_ref[at, own]), stack(do_ref[at, own])
        return q, do, dot(k_ref[seen, own], q, NT), dot(v_ref[seen, own], do, NT)

    def softmax(b, scores, back):
        edge = jnp.where(admitted, scores[b * BLOCK :], -1e30)
        scores = edge if b == 0 else jnp.concatenate([scores[: b * BLOCK], edge], axis=0)
        top = jnp.max(scores, axis=0, keepdims=True)
        expo = jnp.exp(scores - top)
        probs = expo * (1.0 / jnp.sum(expo, axis=0, keepdims=True))
        share = jnp.sum(probs * back, axis=0, keepdims=True)
        return probs.astype(BF16), (probs * (back - share)).astype(BF16)

    def products_out(b, p, q, do, low, back):
        at, seen, own = pl.ds(b * BLOCK, BLOCK), pl.ds(0, (b + 1) * BLOCK), pl.ds(p * wide, wide)
        mixed = diagonal(dot(vt_ref[own, seen], low))
        o_ref[at, own] = mixed.T.astype(BF16)
        dqs_ref[at, own] = diagonal(dot(kt_ref[own, seen], back)).T * scale
        dks_ref[seen, own] += dot(back, q)
        dvs_ref[seen, own] += dot(low, do)

    units = [(b, p) for b in range(rows // BLOCK) for p in range(lanes // wide)]
    ready = products_in(*units[0])
    done = None
    for n, (b, p) in enumerate(units):
        q, do, scores, back = ready
        if n + 1 < len(units):
            ready = products_in(*units[n + 1])
        low, back = softmax(b, scores, back)
        if done is not None:
            products_out(*done)
        done = (b, p, q, do, low, back)
    products_out(*done)

    for s in range(blocks):
        stored_o_ref[step, s * BLOCK : (s + 1) * BLOCK, :] = o_ref[pl.ds(order_ref[0, s] * BLOCK, BLOCK), :]

    for i in range(batch):
        @pl.when(mine == i)
        def _(i=i):
            for k in range(ring):
                o_copy(step, k, i).start()

    total = jnp.zeros((1, lanes), F32)
    for t in range(rows // tile):
        at = pl.ds(t * tile, tile)
        same, cross = turn(dqs_ref[at, :], at)
        dq = (same - cross).astype(BF16)
        same, cross = turn(dks_ref[at, :], at)
        dk = (same - cross).astype(BF16)
        dv = dvs_ref[at, :].astype(BF16)
        total += jnp.sum(dq.astype(F32), axis=0, keepdims=True)
        q_ref[at, :] = dq
        k_ref[at, :] = dk
        v_ref[at, :] = dv
        da_ref[at, :] += dot(dq, wq_ref[...], NT) + dot(dk, wk_ref[...], NT) + dot(dv, wv_ref[...], NT)
    small_ref[2:3, pl.ds(pl.multiple_of(step * lanes, 128), lanes)] = total
    for j, ref in enumerate((q_ref, k_ref, v_ref)):
        grad_ref[step, j] = dot(at_ref[...], ref[...]).astype(BF16)
        grad_copy(step, j).start()
    @pl.when(step == 0)
    def _():
        do_sum.second(down)
        do_sum.to_owner(up)

    @pl.when(step == 1)
    def _():
        do_sum.to_owner(down)

    @pl.when(step == last)
    def _():
        gain = jnp.zeros((1, width), F32)
        shift = jnp.zeros((1, width), F32)
        for s in range(blocks):
            at = pl.ds(s * BLOCK, BLOCK)
            sorted_at = pl.ds(order_ref[0, s] * BLOCK, BLOCK)
            xh, _ = normalized(stored(x_ref, s).astype(F32))
            da = da_ref[sorted_at, :]
            gain += jnp.sum(da * xh, axis=0, keepdims=True)
            shift += jnp.sum(da, axis=0, keepdims=True)
            h_ref[at, :] = (da * norm_ref[1:2, :]).astype(BF16)
        small_ref[0:1, :] = gain
        small_ref[1:2, :] = shift
        small_ref[3:8, :] = jnp.zeros((5, width), F32)
        do_sum.hand_on(up)
        do_sum.hand_on(down)
        for quad in range(last + 1):
            for i in range(batch):
                @pl.when(mine != i)
                def _(quad=quad, i=i):
                    ref = ret_o.at[i, :, pl.ds(quad * lanes, lanes)]
                    remote(ref, ref, o_send.at[quad, 0], o_recv.at[quad, i], core_id, z).wait_recv()

                @pl.when(mine == i)
                def _(quad=quad, i=i):
                    o_copy(quad, 0, i).wait()
                    for k in range(1, ring):
                        o_copy(quad, k, i).wait_send()
        for quad in range(last + 1):
            for j in range(3):
                grad_copy(quad, j).wait()


def attend(order, x, g, norms, bias_q, tables, weights, up, down, batch):
    ring, groups_dp = lax.axis_size("ctx"), lax.axis_size("dp")
    teams = (groups_dp // 8).bit_length() - 1
    shapes = ((1, 2 * up.shape[1], 2 * up.shape[2]), (down.shape[1], down.shape[2], 2 * down.shape[3]))
    down = down.reshape(-1, *down.shape[2:])
    rows, width = x.shape
    lanes = QUAD * HD
    groups = width // lanes
    anywhere = pl.BlockSpec(memory_space=pl.ANY)
    whole = lambda shape: pl.BlockSpec(shape, lambda i: (0,) * len(shape))
    once = lambda shape: pl.BlockSpec(shape, lambda i: (0,) * len(shape), pipeline_mode=pl.Buffered(1))
    dma = pltpu.SemaphoreType.DMA
    slices = [(n, r // 4, c // 2) for n, r, c in shapes]
    return pl.pallas_call(
        functools.partial(attend_kernel, teams),
        grid=(groups,),
        in_specs=[
            pl.BlockSpec(memory_space=pltpu.SMEM),
            once((rows, width)),
            once((rows, width)),
            once(norms.shape),
            pl.BlockSpec((8, lanes), lambda i: (0, i)),
            once(tables[0].shape),
            once(tables[0].shape),
            once(tables[0].shape),
            pl.BlockSpec((width, lanes), lambda i: (0, i)),
            pl.BlockSpec((width, lanes), lambda i: (0, groups + i)),
            pl.BlockSpec((width, lanes), lambda i: (0, 2 * groups + i)),
            pl.BlockSpec((lanes, width), lambda i: (i, 3)),
            anywhere,
            anywhere,
        ],
        out_specs=[once((rows, width)), anywhere, once((8, width))] + [anywhere] * 3,
        out_shape=[
            jax.ShapeDtypeStruct((rows, width), BF16),
            jax.ShapeDtypeStruct((width, 3 * width), BF16),
            jax.ShapeDtypeStruct((8, width), F32),
            jax.ShapeDtypeStruct((batch, rows // ring, width), BF16),
        ]
        + [jax.ShapeDtypeStruct(shape, BF16) for shape in slices],
        scratch_shapes=[
            pltpu.VMEM((rows, width), BF16),
            pltpu.VMEM((rows, width), BF16),
            pltpu.VMEM((width, rows), BF16),
            pltpu.VMEM((rows, width), F32),
        ]
        + [pltpu.VMEM((rows, lanes), BF16)] * 5
        + [pltpu.VMEM((lanes, rows), BF16)] * 2
        + [pltpu.VMEM((rows, lanes), F32)] * 3
        + [
            pltpu.VMEM((groups, 3, width, lanes), BF16), pltpu.VMEM((groups, rows, lanes), BF16),
            dma((groups, ring)), dma((groups, batch)), dma((groups,)), dma((groups, 3)),
        ]
        + reducer_scratch(MLP_LEVELS, shapes, teams, ring),
        compiler_params=pltpu.CompilerParams(
            collective_id=2, has_side_effects=True, vmem_limit_bytes=60 * MIB
        ),
        cost_estimate=pl.CostEstimate(
            flops=24 * rows * width * width + 8 * rows * rows * width,
            bytes_accessed=16 * width * width + 8 * rows * width,
            transcendentals=HEADS * rows * rows // 2,
        ),
        name="attend",
    )(order, x, g, norms, bias_q, *tables, weights, weights, weights, weights, up, down)


def rotary_tables(length):
    half = ROT // 2
    frequency = ROPE_BASE ** (-(np.arange(half) * 2.0 / ROT))
    angle = np.arange(length)[:, None] * frequency[None, :]
    cosine, sine = np.cos(angle), np.sin(angle)
    rest = np.zeros((length, HD - ROT))
    none = np.zeros_like(sine)
    cos_full = np.concatenate([cosine, cosine, rest + 1.0], axis=1)
    low = np.concatenate([-sine, none, rest], axis=1)
    high = np.concatenate([none, sine, rest], axis=1)
    return tuple(jnp.asarray(np.tile(t, (1, 2)).astype(np.float32)) for t in (cos_full, low, high))


def adamw(weight, grad, first, second, rate, decay):
    first_new = BETA_ONE * first + (1.0 - BETA_ONE) * grad
    second_new = BETA_TWO * second + (1.0 - BETA_TWO) * grad * grad
    first_hat = first_new / (1.0 - BETA_ONE**STEP)
    second_hat = second_new / (1.0 - BETA_TWO**STEP)
    weight_new = weight - rate * (first_hat / (jnp.sqrt(second_hat) + EPS_ADAM) + decay * weight)
    return (first_new, second_new, weight_new)


RATES = (0.1, 0.6, 0.1, 0.05)


def finish_kernel(*refs):
    x_ref, g_ref, attend_ref, feed_ref, h_ref, back_ref, bias_ref, norm_grad = refs[:8]
    norm, norm_first, norm_second = refs[8:11]
    inputs, outputs = refs[11:27], refs[27:]
    layer_out, input_grad = outputs[:2]
    for n, rate in enumerate(RATES):
        weight, grad, first, second = (ref[...] for ref in inputs[4 * n : 4 * n + 4])
        new = adamw(weight, grad.astype(F32), first, second, rate, DECAY)
        for ref, value in zip(outputs[2 + 3 * n : 5 + 3 * n], new):
            ref[...] = value
    width = x_ref.shape[1]
    bias = bias_ref[0:1, width : 2 * width] + bias_ref[0:1, bias_ref.shape[1] - width :]
    rows = x_ref[...].astype(F32)
    layer_out[...] = (rows + attend_ref[...] + feed_ref[...] + bias).astype(BF16)
    xh, scale = normalized(rows)
    h = back_ref[...].astype(F32) + h_ref[...]
    inner = jnp.mean(h * xh, axis=-1, keepdims=True)
    input_grad[...] = g_ref[...].astype(F32) + scale * (h - jnp.mean(h, axis=-1, keepdims=True) - xh * inner)

    @pl.when(pl.program_id(0) == 0)
    def _():
        grad = norm_grad[0:4, : norm.shape[1]]
        first, second, new = adamw(norm[...], grad, norm_first[...], norm_second[...], 0.6, 0.0)
        outputs[14][...] = first
        outputs[15][...] = second[0:2]
        outputs[16][...] = second[2:4]
        outputs[17][...] = new


def finish(rows, biases, norm_grad, norm_args, weights):
    steps = 4
    whole = lambda v: pl.BlockSpec(v.shape, lambda i: (0,) * len(v.shape))
    part = lambda v: pl.BlockSpec((v.shape[0] // steps, v.shape[1]), lambda i: (i, 0))
    like = lambda v, dtype: jax.ShapeDtypeStruct(v.shape, dtype)
    count, width = rows[0].shape
    args = [*rows, biases, norm_grad, *norm_args] + [v for group in weights for v in group]
    specs = [part(v) for v in rows] + [whole(v) for v in (biases, norm_grad, *norm_args)]
    specs += [part(v) for group in weights for v in group]
    outs = [like(rows[0], BF16), like(rows[0], F32)] + [like(group[0], F32) for group in weights for _ in range(3)]
    out_specs = [part(v) for v in outs]
    own = norm_args[0].shape[1]
    norm_outs = [jax.ShapeDtypeStruct((n, own), F32) for n in (4, 2, 2, 4)]
    return pl.pallas_call(
        finish_kernel,
        grid=(steps,),
        in_specs=specs,
        out_specs=out_specs + [whole(v) for v in norm_outs],
        out_shape=outs + norm_outs,
        compiler_params=pltpu.CompilerParams(vmem_limit_bytes=56 * MIB),
        cost_estimate=pl.CostEstimate(flops=0, bytes_accessed=64 * MIB, transcendentals=0),
        name="finish",
    )(*args)


def shards(
    tokens, out_grad, block_order, qkv_weight, out_weight, up_weight, down_weight, norm_params, bias_params,
    qkv_first, qkv_second, out_first, out_second, up_first, up_second, down_first, down_second,
    norm_first, norm_second, bias_first, bias_second,
):
    groups, ring = lax.axis_size("dp"), lax.axis_size("ctx")
    group, rank = lax.axis_index("dp"), lax.axis_index("ctx")
    batch, piece, width = tokens.shape
    length = piece * ring
    count = batch * piece
    ff = up_weight.shape[1]

    share = bias_params.shape[0]
    lanes = share + -share % 128
    small = jnp.concatenate([
        jnp.pad(bias_params[None, :], ((0, 0), (0, lanes - share))),
        jnp.pad(norm_params, ((0, 3), (0, lanes - norm_params.shape[1]))),
    ])
    x_rows, g_rows = tokens.reshape(count, width), out_grad.reshape(count, width)
    att_copy, biases, norms, home_x, home_g, feed_out, h_feed, dup, ddown, dbias_up, small_feed = gather_feed(
        up_weight, down_weight, qkv_weight, out_weight, small, x_rows, g_rows, piece, ring * share
    )

    odd = group % 2

    order = block_order[jnp.clip(rank - odd, 0, batch - 1)]
    spots = jnp.arange(order.shape[0])
    order = jnp.stack([order, jnp.sum(jnp.where(order[None, :] == spots[:, None], spots[None, :], 0), axis=1)])

    h_attend, dqkv, small_attend, o_rows, up_slice, down_slice = attend(
        order, home_x, home_g, norms, biases, rotary_tables(length), att_copy, dup, ddown, batch
    )
    *owned, norm_grad, bias_grad, attend_out, ret_back = reduce_all(
        up_slice, down_slice, dqkv, small_attend, small_feed, dbias_up, h_attend, o_rows, g_rows, att_copy, batch
    )
    up_grad, down_grad, qkv_grad, out_grads = (
        g.reshape(w.shape) for g, w in zip(owned, (up_weight, down_weight, qkv_weight, out_weight))
    )
    layer_out, input_grad, *new, norm_a, norm_b, norm_c, norm_d = finish(
        (x_rows, g_rows, attend_out, feed_out, h_feed, ret_back.reshape(count, width)),
        biases,
        norm_grad,
        (norm_params, norm_first, norm_second),
        (
            (qkv_weight, qkv_grad, qkv_first, qkv_second),
            (out_weight, out_grads, out_first, out_second),
            (up_weight, up_grad, up_first, up_second),
            (down_weight, down_grad, down_first, down_second),
        ),
    )
    bias_new = adamw(bias_params, bias_grad[0, :share], bias_first, bias_second, 0.6, 0.0)
    return (
        layer_out.reshape(tokens.shape), input_grad.reshape(tokens.shape), *new,
        norm_a, norm_b, norm_c, norm_d, *bias_new,
    )


def solution(mesh):
    rows, columns, token = P("ctx", None), P(None, "ctx"), P("dp", "ctx", None)
    in_specs = (token, token, P("dp", None)) + (rows,) * 4 + (columns, P("ctx")) + (rows,) * 8
    in_specs += (columns, columns, P("ctx"), P("ctx"))
    out_specs = (token, token) + (rows,) * 12 + (columns,) * 4 + (P("ctx"),) * 3
    return jax.shard_map(shards, mesh=mesh, in_specs=in_specs, out_specs=out_specs, check_vma=False)
```

```python
import functools
import math
from types import SimpleNamespace

import jax
import jax.numpy as jnp
import numpy as np
from jax import lax
from jax.experimental import pallas as pl
from jax.experimental.pallas import tpu as pltpu
from jax.sharding import PartitionSpec as P

HEADS = 12
HD = 64
STEP = 10
ROT = 16
BLOCK = 128
QUAD = 4
MLP_LEVELS = (2, 1)
LEVELS = (3, 3, 0, 0)

EPS_NORM = 1e-05
BETA_ONE = 0.9
BETA_TWO = 0.95
EPS_ADAM = 1e-08
DECAY = 0.01
ROPE_BASE = 10000.0
F32 = jnp.float32
BF16 = jnp.bfloat16
MIB = 1024 * 1024


def dot(left, right, dims=((1,), (0,))):
    return lax.dot_general(left, right, (dims, ((), ())), preferred_element_type=F32)


NN = ((1,), (0,))
NT = ((1,), (1,))
TN = ((0,), (0,))


def normalized(values):
    mean = jnp.mean(values, axis=-1, keepdims=True)
    centred = values - mean
    variance = jnp.mean(centred * centred, axis=-1, keepdims=True)
    scale = lax.rsqrt(variance + EPS_NORM)
    return centred * scale, scale


MESH = pl.DeviceIdType.MESH


def plane(d):
    core, x, y = d % 2, d // 2 % 2, d // 4 % 2
    return core, x, y, d + 1 - 2 * core, d + 2 - 4 * x, d + 4 - 8 * y


def gather_kernel(
    up, down, qkv, out, small, tokens, cotangents,
    att_all, small_all, norm_all, home_x, home_g, out_ref, h_ref, up_part, down_part, dbias_ref, sums_ref,
    up_all, down_all, att_own, up_wide, down_wide, att_wide, small_in, x_ref, g_ref, m_ref, mt_ref, hid_ref, dup_in_ref,
    dup_ref, up_core, up_first, ddown_ref, down_core,
    z_send, z_recv, p_send, p_recv, s_send, s_recv, t_send, t_recv, local, out_sem, c_send, c_recv,
):
    ring = lax.axis_size("ctx")
    d, z = lax.axis_index("dp"), lax.axis_index("ctx")
    core, x, y, core_id, x_id, y_id = plane(d)
    own = x + 2 * y
    own_x, own_y, far = own + 1 - 2 * x, own + 2 - 4 * y, 3 - own
    count, width = tokens.shape
    piece = home_x.shape[0] // ring
    batch = count // piece
    arrays = ((up_wide, up_all, False), (down_wide, down_all, True), (att_own, att_all, False))

    def slot(a, base, place, half=None):
        source, whole, tall = arrays[a]
        ref = source if base is None else whole
        rows, columns = source.shape
        at = 0 if base is None else base * rows
        height, span = rows // 4, columns // 2
        at = at + place * height
        column = core * span
        if half is not None:
            if tall:
                height = height // 2
                at = at + half * height
            else:
                span = span // 2
                column = column + half * span
        return ref.at[pl.ds(pl.multiple_of(at, 16), height), pl.ds(pl.multiple_of(column, 128), span)]

    def side(a, base, of):
        source, whole, tall = arrays[a]
        rows, columns = source.shape
        at = pl.multiple_of(base * rows, 16)
        return whole.at[pl.ds(at, rows), pl.ds(pl.multiple_of(of * (columns // 2), 128), columns // 2)]

    def remote(src, dst, send, recv, dp, ctx):
        return pltpu.make_async_remote_copy(
            src_ref=src, dst_ref=dst, send_sem=send, recv_sem=recv, device_id=(dp, ctx), device_id_type=MESH
        )

    columns = qkv.shape[1]
    wide_loads = [
        [pltpu.make_async_copy(up, up_wide, local.at[0])],
        [pltpu.make_async_copy(down, down_wide, local.at[1])],
        [
            pltpu.make_async_copy(qkv, att_wide.at[:, pl.ds(0, columns)], local.at[2]),
            pltpu.make_async_copy(out, att_wide.at[:, pl.ds(columns, out.shape[1])], local.at[8]),
        ],
    ]
    for loads in wide_loads:
        for copy in loads:
            copy.start()

    def cast_own(a):
        for copy in wide_loads[a]:
            copy.wait()
        wide, target = ((up_wide, up_all), (down_wide, down_all), (att_wide, att_own))[a]
        rows = wide.shape[0]
        tile = 64
        base = 0 if a == 2 else z * rows

        def body(t, _):
            value = wide[pl.ds(pl.multiple_of(t * tile, 16), tile), :].astype(BF16)
            target[pl.ds(pl.multiple_of(base + t * tile, 16), tile), :] = value
            return 0

        lax.fori_loop(0, rows // tile, body, 0)

    barrier = pltpu.get_barrier_semaphore()
    for k in range(1, ring):
        pl.semaphore_signal(barrier, inc=1, device_id=(d, (z + k) % ring), device_id_type=MESH)
    for other in (core_id, x_id, y_id):
        pl.semaphore_signal(barrier, inc=1, device_id=(other, z), device_id_type=MESH)
    cast_own(0)
    pl.semaphore_wait(barrier, ring + 2)

    def hop(a, way, h):
        shard = z - h if way == 0 else z + h
        target = z + 1 if way == 0 else z - 1
        src = slot(a, None, own) if h == 0 and a == 2 else slot(a, shard, own)
        return remote(src, slot(a, shard, own), z_send.at[a, way, h], z_recv.at[a, way, h], d, target)

    def can_send(way, h):
        shard = z - h if way == 0 else z + h
        target = z + 1 if way == 0 else z - 1
        return (shard >= 0) & (shard < ring) & (target >= 0) & (target < ring)

    def in_range(way, h):
        shard = z - h if way == 0 else z + h
        return (shard >= 0) & (shard < ring)

    def cast(a, shard, j, via_x):
        send, recv = p_send.at[a, shard, j], p_recv.at[a, shard, j]
        if j == 3:
            ref = side(a, shard, core)
            return remote(ref, ref, send, recv, core_id, z)
        ref = slot(a, shard, own if j < 2 else (own_y if via_x else own_x))
        return remote(ref, ref, send, recv, x_id if (j == 0 or j == 2 and via_x) else y_id, z)

    def arrived(a, shard, j):
        send, recv = p_send.at[a, shard, j], p_recv.at[a, shard, j]
        ref = side(a, shard, 1 - core) if j == 3 else slot(a, shard, (own_x, own_y, far)[j])
        remote(ref, ref, send, recv, core_id, z).wait_recv()

    def via(a, h):
        return (a + h) % 2 == 0

    def start_hops(a):
        for way in range(2):
            @pl.when(can_send(way, 0))
            def _(way=way):
                hop(a, way, 0).start()

    def small_copy(k):
        return remote(small, small_in.at[z], s_send.at[k], s_recv.at[k], d, (z + k) % ring)

    def stage_a(a, h):
        for way in range(2):
            @pl.when(in_range(way, h))
            def _(way=way):
                shard = z - h if way == 0 else z + h
                ref = slot(a, shard, own)
                remote(ref, ref, z_send.at[a, way, h - 1], z_recv.at[a, way, h - 1], core_id, z).wait_recv()

                @pl.when(can_send(way, h))
                def _():
                    hop(a, way, h).start()

                cast(a, shard, 0, via(a, h)).start()
                cast(a, shard, 1, via(a, h)).start()

    def stage_b(a, h):
        for way in range(2):
            @pl.when(in_range(way, h))
            def _(way=way):
                shard = z - h if way == 0 else z + h
                first = 1 if via(a, h) else 0
                arrived(a, shard, first)
                cast(a, shard, 2, via(a, h)).start()
                arrived(a, shard, 1 - first)

    def stage_c(a, h):
        for way in range(2):
            @pl.when(in_range(way, h))
            def _(way=way):
                shard = z - h if way == 0 else z + h
                arrived(a, shard, 2)
                cast(a, shard, 3, via(a, h)).start()

    def stage_d(a, h):
        for way in range(2):
            @pl.when(in_range(way, h))
            def _(way=way):
                shard = z - h if way == 0 else z + h
                arrived(a, shard, 3)

    pairs = ((tokens, home_x), (cotangents, home_g))

    def move(which, i):
        source, whole = pairs[which]
        src = source.at[pl.ds(i * piece, piece), :]
        dst = whole.at[pl.ds(pl.multiple_of(z * piece, 16), piece), :]
        return src, dst, i + core

    def start_moves(which):
        for i in range(batch):
            src, dst, target = move(which, i)

            @pl.when(target != z)
            def _(src=src, dst=dst, target=target, i=i):
                remote(src, dst, t_send.at[which, i], t_recv.at[which, z], d, target).start()

            @pl.when(target == z)
            def _(src=src, dst=dst):
                pltpu.make_async_copy(src, dst, local.at[6 + which]).start()

    own_rows = pl.ds(pl.multiple_of(z * att_own.shape[0], 16), att_own.shape[0])
    own_att = pltpu.make_async_copy(att_own, att_all.at[own_rows, :], local.at[9])
    x_load = pltpu.make_async_copy(tokens, x_ref, local.at[3])
    g_load = pltpu.make_async_copy(cotangents, g_ref, local.at[4])
    own_small = pltpu.make_async_copy(small, small_in.at[z], local.at[5])

    start_hops(0)
    cast_own(1)
    start_hops(1)
    cast_own(2)
    start_hops(2)
    for k in range(1, ring):
        small_copy(k).start()
    for copy in (own_att, x_load, g_load, own_small):
        copy.start()
    hops = range(1, ring)
    work = [(a, h) for a in range(2) for h in hops]
    for n in range(len(work) + 2):
        if n < len(work):
            stage_a(*work[n])
        if n == len(work) - 1:
            start_moves(0)
        if 1 <= n <= len(work):
            stage_b(*work[n - 1])
        if n >= 2:
            stage_c(*work[n - 2])
    stage_a(2, 1)

    own_small.wait()
    for k in range(1, ring):
        ref = small_in.at[(z + ring - k) % ring]
        remote(ref, ref, s_send.at[k], s_recv.at[k], core_id, z).wait_recv()
    x_load.wait()
    g_load.wait()
    entries = small_all.shape[1]
    biases = jnp.zeros((8, entries), F32)
    norms = jnp.zeros((8, width), F32)
    for r in range(ring):
        block = small_in[r].astype(BF16).astype(F32)
        full = jnp.concatenate([block, jnp.zeros((8, entries - block.shape[1]), F32)], axis=1)
        biases += pltpu.roll(full, r * (entries // ring), 1) if r else full
        norms += pltpu.roll(block[:, :width], r * (width // ring), 1) if r else block[:, :width]
    small_all[...] = biases
    norm_all[...] = norms
    ff = up_all.shape[1]
    gain_2, shift_2 = norm_all[3:4, :], norm_all[4:5, :]
    tile = 256
    tiles = count // tile
    for t in range(tiles):
        at = pl.ds(t * tile, tile)
        xh, _ = normalized(x_ref[at, :].astype(F32))
        m = xh * gain_2 + shift_2
        m_ref[at, :] = m.astype(BF16)
        mt_ref[:, at] = m.T.astype(BF16)
        out_ref[at, :] = jnp.zeros((tile, width), F32)
        h_ref[at, :] = jnp.zeros((tile, width), F32)
    for h in hops:
        stage_d(0, h)
        stage_d(1, h)

    strip = dup_ref.shape[3] // ring
    steps = ff // (ring * strip)
    half = ring // 2
    big, by_core = (dup_ref, ddown_ref), (up_core, down_core)
    bits, ids = ((x, y), (y, x)), ((x_id, y_id), (y_id, x_id))

    def sizes(a):
        return by_core[a].shape[2], by_core[a].shape[3]

    def slice_of(order):
        return 2 * bits[order][0] + bits[order][1]

    def core_copy(a, i):
        _, span = sizes(a)
        away = pl.ds(pl.multiple_of((1 - core) * span, 128), span)
        return remote(big[a].at[i, :, :, away], by_core[a].at[i], c_send.at[a, i, 0], c_recv.at[a, i, 0], core_id, z)

    def first_copy(a, i, order):
        height, _ = sizes(a)
        own = pl.ds(order * half, half)
        away = pl.ds(pl.multiple_of((1 - bits[order][0]) * (height // 2), 16), height // 2)
        return remote(
            by_core[a].at[i, own, away, :], up_first.at[i, own], c_send.at[a, i, 1 + order],
            c_recv.at[a, i, 1 + order], ids[order][0], z,
        )

    def add(into, at, term, owners):
        height = term(0).shape[0]
        tile = 32 if height % 48 else 48

        def body(n, _):
            o, t = n // (height // tile), n % (height // tile)
            spot = pl.ds(pl.multiple_of(at + t * tile, 16), tile)
            value = term(o)[pl.ds(pl.multiple_of(t * tile, 16), tile), :]
            into[o, spot, :] = (into[o, spot, :].astype(F32) + value.astype(F32)).astype(BF16)
            return 0

        lax.fori_loop(0, owners * (height // tile), body, 0)

    def chunk_1(i):
        for a in range(2):
            _, span = sizes(a)
            core_copy(a, i).wait_recv()
            keep = pl.ds(pl.multiple_of(core * span, 128), span)
            add(by_core[a].at[i], 0, lambda o: big[a].at[i, o, :, keep], ring)
        for order in range(2):
            first_copy(0, i, order).start()
        parts_out(1, i)[0].start()

    def chunk_2(i):
        height, _ = sizes(0)
        for order in range(2):
            own = pl.ds(order * half, half)
            first_copy(0, i, order).wait_recv()
            at = bits[order][0] * (height // 2)
            add(by_core[0].at[i, own], at, lambda o: up_first.at[i, order * half + o], half)
        for copy in parts_out(0, i):
            copy.start()

    def parts_out(a, i):
        height, span = sizes(a)
        if a == 1:
            return [pltpu.make_async_copy(by_core[1].at[i], down_part.at[:, i], out_sem.at[i, 2 * half])]
        copies = []
        for order in range(2):
            own = pl.ds(order * half, half)
            rows = pl.ds(pl.multiple_of(bits[order][0] * (height // 2), 16), height // 2)
            for n in range(half):
                copies.append(pltpu.make_async_copy(
                    by_core[0].at[i, own, rows, pl.ds(n * strip, strip)],
                    up_part.at[own, :, pl.ds(pl.multiple_of(n * steps * strip + i * strip, 128), strip)],
                    out_sem.at[i, half * order + n],
                ))
        return copies

    def feed_step(step, _):
        for h in hops:
            @pl.when(step == h - 1)
            def _(h=h):
                if h + 1 < ring:
                    stage_a(2, h + 1)
                if h == ring - 2:
                    start_moves(1)
                stage_b(2, h)

            @pl.when(step == h)
            def _(h=h):
                stage_c(2, h)

        @pl.when(step < steps)
        def _():
            spots = [pl.ds(pl.multiple_of(r * (ff // ring) + step * strip, 128), strip) for r in range(ring)]
            bias_spots = [
                pl.ds(pl.multiple_of(2 * width + r * (ff // ring) + step * strip, 128), strip) for r in range(ring)
            ]
            up_part_ = jnp.concatenate([up_all[:, at] for at in spots], axis=1)
            down_part_ = jnp.concatenate([down_all[at, :] for at in spots], axis=0)
            bias = jnp.concatenate([small_all[0:1, at] for at in bias_spots], axis=1)
            total = jnp.zeros((1, ring * strip), F32)
            for t in range(tiles):
                at = pl.ds(t * tile, tile)
                u = dot(m_ref[at, :], up_part_) + bias
                cdf = 0.5 * (1.0 + lax.erf(u * (1.0 / math.sqrt(2.0))))
                hidden = (u * cdf).astype(BF16)
                slope = cdf + u * jnp.exp(-0.5 * u * u) * (1.0 / math.sqrt(2.0 * math.pi))
                back = (dot(g_ref[at, :], down_part_, NT) * slope).astype(BF16)
                hid_ref[at, :] = hidden
                dup_in_ref[at, :] = back
                total += jnp.sum(back.astype(F32), axis=0, keepdims=True)
                out_ref[at, :] += dot(hidden, down_part_)
                h_ref[at, :] += dot(back, up_part_, NT)
            for r in range(ring):
                dbias_ref[0:1, spots[r]] = total[:, r * strip : (r + 1) * strip]
            ddown = dot(hid_ref[...], g_ref[...], TN).astype(BF16)
            dup = dot(mt_ref[...], dup_in_ref[...]).astype(BF16)
            for r in range(ring):
                ddown_ref[step, r] = ddown[r * strip : (r + 1) * strip, :]
                dup_ref[step, r] = dup[r * (width // ring) : (r + 1) * (width // ring), :]
            core_copy(0, step).start()
            core_copy(1, step).start()

        for lag, stage in ((1, chunk_1), (3, chunk_2)):
            @pl.when((step >= lag) & (step < steps + lag))
            def _(lag=lag, stage=stage):
                stage(step - lag)

        return 0

    lax.fori_loop(0, steps + 3, feed_step, 0)

    gain = jnp.zeros((1, width), F32)
    shift = jnp.zeros((1, width), F32)
    sums = jnp.zeros((1, width), F32)
    for t in range(tiles):
        at = pl.ds(t * tile, tile)
        xh, _ = normalized(x_ref[at, :].astype(F32))
        dm = h_ref[at, :]
        gain += jnp.sum(dm * xh, axis=0, keepdims=True)
        shift += jnp.sum(dm, axis=0, keepdims=True)
        sums += jnp.sum(g_ref[at, :].astype(F32), axis=0, keepdims=True)
        h_ref[at, :] = dm * gain_2
    sums_ref[...] = jnp.concatenate([gain, shift, sums, jnp.zeros((5, width), F32)], axis=0)

    mine = z - core
    for which in range(2):
        for k in range(1, ring):
            @pl.when((mine >= 0) & (mine < batch))
            def _(which=which, k=k):
                other = (z + k) % ring
                ref = pairs[which][1].at[pl.ds(pl.multiple_of(other * piece, 16), piece), :]
                remote(ref, ref, t_send.at[which, 0], t_recv.at[which, other], core_id, z).wait_recv()
    for h in hops:
        stage_d(2, h)
    for k in range(1, ring):
        small_copy(k).wait_send()
    for a in range(3):
        for way in range(2):
            for h in range(ring - 1):
                @pl.when(can_send(way, h))
                def _(a=a, way=way, h=h):
                    hop(a, way, h).wait_send()
        for h in hops:
            for way in range(2):
                @pl.when(in_range(way, h))
                def _(a=a, h=h, way=way):
                    shard = z - h if way == 0 else z + h
                    for j in range(4):
                        cast(a, shard, j, via(a, h)).wait_send()
    for which in range(2):
        for i in range(batch):
            src, dst, target = move(which, i)

            @pl.when(target != z)
            def _(src=src, dst=dst, target=target, which=which, i=i):
                remote(src, dst, t_send.at[which, i], t_recv.at[which, z], d, target).wait_send()

            @pl.when(target == z)
            def _(src=src, dst=dst, which=which):
                pltpu.make_async_copy(src, dst, local.at[6 + which]).wait()
    own_att.wait()

    def close(i, _):
        for a in range(2):
            core_copy(a, i).wait_send()
            for copy in parts_out(a, i):
                copy.wait()
        for order in range(2):
            first_copy(0, i, order).wait_send()
        return 0

    lax.fori_loop(0, steps, close, 0)


def gather_feed(up, down, qkv, out, small, tokens, cotangents, piece, entries):
    ring = lax.axis_size("ctx")
    count, width = tokens.shape
    ff = up.shape[1]
    strip = 128
    chunk = ring * strip
    steps = ff // chunk
    shard = up.shape[0]
    columns = qkv.shape[1] + out.shape[1]
    home = jax.ShapeDtypeStruct((ring * piece, width), tokens.dtype)
    rows = jax.ShapeDtypeStruct((count, width), F32)
    dma = pltpu.SemaphoreType.DMA
    anywhere = pl.BlockSpec(memory_space=pl.ANY)
    vmem = pl.BlockSpec(memory_space=pltpu.VMEM)
    return pl.pallas_call(
        gather_kernel,
        in_specs=[anywhere] * 7,
        out_specs=[anywhere, vmem, vmem, anywhere, anywhere, vmem, vmem, anywhere, anywhere, vmem, vmem],
        out_shape=[
            jax.ShapeDtypeStruct((ring * shard, columns), BF16),
            jax.ShapeDtypeStruct((8, entries), F32), jax.ShapeDtypeStruct((8, width), F32), home, home, rows, rows,
            jax.ShapeDtypeStruct((ring, shard // 2, ff // 2), BF16),
            jax.ShapeDtypeStruct((ring, steps, strip, width // 2), BF16),
            jax.ShapeDtypeStruct((8, ff), F32), jax.ShapeDtypeStruct((8, width), F32),
        ],
        scratch_shapes=[
            pltpu.VMEM((ring * shard, ff), BF16), pltpu.VMEM((ring * down.shape[0], width), BF16),
            pltpu.VMEM((shard, columns), BF16),
            pltpu.VMEM(up.shape, F32), pltpu.VMEM(down.shape, F32), pltpu.VMEM((shard, columns), F32),
            pltpu.VMEM((ring, *small.shape), F32),
            pltpu.VMEM((count, width), BF16), pltpu.VMEM((count, width), BF16), pltpu.VMEM((count, width), BF16),
            pltpu.VMEM((width, count), BF16),
            pltpu.VMEM((count, chunk), BF16), pltpu.VMEM((count, chunk), BF16),
            pltpu.VMEM((steps, ring, shard, chunk), BF16), pltpu.VMEM((steps, ring, shard, chunk // 2), BF16),
            pltpu.VMEM((steps, ring, shard // 2, chunk // 2), BF16),
            pltpu.VMEM((steps, ring, strip, width), BF16), pltpu.VMEM((steps, ring, strip, width // 2), BF16),
            dma((3, 2, ring)), dma((3, 2, ring)), dma((3, ring, 4)), dma((3, ring, 4)),
            dma((ring,)), dma((ring,)), dma((2, count // piece)), dma((2, ring)), dma((10,)), dma((steps, ring + 1)),
            dma((2, steps, 3)), dma((2, steps, 3)),
        ],
        compiler_params=pltpu.CompilerParams(
            collective_id=0, has_side_effects=True, vmem_limit_bytes=60 * MIB
        ),
        cost_estimate=pl.CostEstimate(
            flops=12 * count * width * ff, bytes_accessed=60 * MIB, transcendentals=count * ff
        ),
        name="gather_feed",
    )(up, down, qkv, out, small, tokens, cotangents)


def remote(src, dst, send_sem, recv_sem, dp, ctx):
    return pltpu.make_async_remote_copy(
        src_ref=src, dst_ref=dst, send_sem=send_sem, recv_sem=recv_sem, device_id=(dp, ctx), device_id_type=MESH
    )


def team_id(d, t):
    return d + (8 << t) * (1 - 2 * (d // (8 << t) % 2))


def greet(teams):
    ring = lax.axis_size("ctx")
    d, z = lax.axis_index("dp"), lax.axis_index("ctx")
    core, x, y, core_id, x_id, y_id = plane(d)
    barrier = pltpu.get_barrier_semaphore()
    partners = [core_id, x_id, y_id, x_id + y_id - d] + [team_id(d, t) for t in range(teams)]
    for k in range(1, ring):
        pl.semaphore_signal(barrier, inc=1, device_id=(d, (z + k) % ring), device_id_type=MESH)
    for other in partners:
        pl.semaphore_signal(barrier, inc=1, device_id=(other, z), device_id_type=MESH)
    pl.semaphore_wait(barrier, ring - 1 + len(partners))


def reducer(teams, levels, ins, sums, bufs, send, recv, load):
    count = len(ins)
    ring = lax.axis_size("ctx")
    d, z = lax.axis_index("dp"), lax.axis_index("ctx")
    core, x, y, core_id, x_id, y_id = plane(d)
    far_id = x_id + y_id - d
    bits, ids = ((x, y), (y, x)), ((x_id, y_id), (y_id, x_id))
    spots = ((x, y), (1 - x, y), (x, 1 - y), (1 - x, 1 - y))

    def sizes(a):
        _, strips, quarter, span = bufs[a][-1].shape
        return strips, quarter, span

    def owners(a, order):
        strips = sizes(a)[0]
        return pl.ds(order * ring // 2 * strips, ring // 2 * strips)

    def rows_at(at, height):
        return pl.ds(pl.multiple_of(at, 16), height)

    def kept(a, order):
        return 0 if levels[a] == 2 else bits[order][0] * 2 * sizes(a)[1]

    def core_copy(a):
        span = sizes(a)[2]
        away = pl.ds(pl.multiple_of((1 - core) * span, 128), span)
        return remote(ins[a].at[:, :, away], bufs[a][1], send.at[a, 0], recv.at[a, 0], core_id, z)

    def own_load(a):
        if levels[a] == 3:
            return pltpu.make_async_copy(ins[a], bufs[a][5].at[0], load.at[a])
        span = sizes(a)[2]
        keep = pl.ds(pl.multiple_of(core * span, 128), span)
        src = ins[a].at[:, :, keep] if levels[a] == 0 else ins[a]
        return pltpu.make_async_copy(src, bufs[a][0], load.at[a])

    def first_copy(a, order):
        quarter = sizes(a)[1]
        away = rows_at((1 - bits[order][0]) * 2 * quarter, 2 * quarter)
        return remote(
            bufs[a][0].at[owners(a, order), away, :], bufs[a][2].at[owners(a, order)], send.at[a, 1 + order],
            recv.at[a, 1 + order], ids[order][0], z,
        )

    def second_copy(a, order):
        quarter = sizes(a)[1]
        away = rows_at(kept(a, order) + (1 - bits[order][1]) * quarter, quarter)
        return remote(
            bufs[a][0].at[owners(a, order), away, :], bufs[a][3].at[owners(a, order)], send.at[a, 3 + order],
            recv.at[a, 3 + order], ids[order][1], z,
        )

    def own_quarter(a, owner):
        strips, quarter, _ = sizes(a)
        order = owner // (ring // 2)
        first, second = (1 - order) * x + order * y, (1 - order) * y + order * x
        at = second * quarter if levels[a] == 2 else (2 * first + second) * quarter
        return bufs[a][0].at[pl.ds(owner * strips, strips), rows_at(at, quarter), :]

    def owner_copy(a, k):
        to = (z + k) % ring
        return remote(own_quarter(a, to), bufs[a][4].at[k - 1], send.at[a, 4 + k], recv.at[a, 4 + k], d, to)

    def team_copy(a, t):
        j = 4 + ring + 7 + t
        return remote(bufs[a][5].at[0], bufs[a][5].at[1 + t], send.at[a, j], recv.at[a, j], team_id(d, t), z)

    def final(a, spot, side):
        strips, quarter, span = sizes(a)
        order = z // (ring // 2)
        xx, yy = spots[spot]
        at = ((1 - order) * (2 * xx + yy) + order * (2 * yy + xx)) * quarter
        return sums[a].at[:, rows_at(at, quarter), pl.ds(pl.multiple_of(side * span, 128), span)]

    def spread(a, j):
        s, r = send.at[a, 4 + ring + j - 1], recv.at[a, 4 + ring + j - 1]
        if j < 4:
            return remote(bufs[a][5].at[0], final(a, 0, core), s, r, (x_id, y_id, far_id)[j - 1], z)
        src = bufs[a][5].at[0] if j == 4 else final(a, j - 4, core)
        return remote(src, final(a, j - 4, core), s, r, core_id, z)

    def spread_here(a, j):
        s, r = send.at[a, 4 + ring + j - 1], recv.at[a, 4 + ring + j - 1]
        ref = final(a, j, core) if j < 4 else final(a, j - 4, 1 - core)
        remote(ref, ref, s, r, core_id, z).wait_recv()

    def keep_own(a):
        return pltpu.make_async_copy(bufs[a][5].at[0], final(a, 0, core), load.at[count + a])

    def add(into, at, term, blocks):
        height = term.shape[1]
        tile = 32 if height % 48 else 48

        def body(n, _):
            o, t = n // (height // tile), n % (height // tile)
            spot = rows_at(at + t * tile, tile)
            value = term[o, rows_at(t * tile, tile), :]
            into[o, spot, :] = (into[o, spot, :].astype(F32) + value.astype(F32)).astype(BF16)
            return 0

        lax.fori_loop(0, blocks * (height // tile), body, 0)

    def enter(a):
        if levels[a] == 0:
            core_copy(a).start()
        own_load(a).start()

    def first(a):
        own_load(a).wait()
        if levels[a] == 0:
            core_copy(a).wait_recv()
            add(bufs[a][0], 0, bufs[a][1], bufs[a][0].shape[0])
        if levels[a] < 2:
            for order in range(2):
                first_copy(a, order).start()

    def second(a):
        for order in range(2):
            if levels[a] < 2:
                first_copy(a, order).wait_recv()
                own = owners(a, order)
                add(bufs[a][0].at[own], kept(a, order), bufs[a][2].at[own], ring // 2 * sizes(a)[0])
            second_copy(a, order).start()

    def to_owner(a):
        for order in range(2):
            second_copy(a, order).wait_recv()
            own = owners(a, order)
            at = kept(a, order) + bits[order][1] * sizes(a)[1]
            add(bufs[a][0].at[own], at, bufs[a][3].at[own], ring // 2 * sizes(a)[0])
        for k in range(1, ring):
            owner_copy(a, k).start()

    def add_up(a):
        for k in range(1, ring):
            owner_copy(a, k).wait_recv()
        mine = own_quarter(a, z)
        for s in range(sizes(a)[0]):
            terms = [mine[s]] + [bufs[a][4][k, s] for k in range(ring - 1)]
            bufs[a][5][0, s] = sum((t.astype(F32) for t in terms[1:]), terms[0].astype(F32)).astype(BF16)
        for t in range(teams):
            team_copy(a, t).start()
            team_copy(a, t).wait()
            bufs[a][5][0] = (bufs[a][5][0].astype(F32) + bufs[a][5][1 + t].astype(F32)).astype(BF16)

    def total(a):
        if levels[a] == 3:
            own_load(a).wait()
        else:
            add_up(a)
        keep_own(a).start()
        for j in range(1, 5):
            spread(a, j).start()

    def hand_on(a):
        add_up(a)
        out = pltpu.make_async_copy(bufs[a][5].at[0], sums[a], load.at[count + a])
        out.start()
        sent(a)
        out.wait()

    def share(a):
        for j in range(1, 4):
            spread_here(a, j)
            spread(a, 4 + j).start()

    def sent(a):
        if levels[a] == 0:
            core_copy(a).wait_send()
        for order in range(2):
            if levels[a] < 2:
                first_copy(a, order).wait_send()
            second_copy(a, order).wait_send()
        for k in range(1, ring):
            owner_copy(a, k).wait_send()

    def close(a):
        for j in range(4, 8):
            spread_here(a, j)
        if levels[a] < 3:
            sent(a)
        for j in range(1, 8):
            spread(a, j).wait_send()
        keep_own(a).wait()

    return SimpleNamespace(
        enter=enter, first=first, second=second, to_owner=to_owner, total=total, hand_on=hand_on, share=share, close=close
    )


def reducer_scratch(levels, shapes, teams, ring):
    scratch = []
    for level, (strips, rows, columns) in zip(levels, shapes):
        blocks, span = ring * strips, columns // 2
        none = (1, 16, 128)
        scratch += [
            pltpu.VMEM(none if level == 3 else (blocks, rows // 2 if level == 2 else rows, span), BF16),
            pltpu.VMEM((blocks, rows, span) if level == 0 else none, BF16),
            pltpu.VMEM((blocks, rows // 2, span) if level < 2 else none, BF16),
            pltpu.VMEM((blocks, rows // 4, span) if level < 3 else none, BF16),
            pltpu.VMEM((ring - 1, strips, rows // 4, span) if level < 3 else (1, *none), BF16),
            pltpu.VMEM((1 + teams, strips, rows // 4, span), BF16),
        ]
    copies = 4 + ring + 7 + teams
    dma = pltpu.SemaphoreType.DMA
    return scratch + [dma((len(levels), copies)), dma((len(levels), copies)), dma((2 * len(levels),))]


def reduce_kernel(
    teams, up_ref, down_ref, qkv_ref, small_att, small_mlp, small_up, back_ref, o_ref, g_ref, weights,
    up_sum, down_sum, qkv_sum, out_sum, norm_out, bias_out, attend_out, ret_back, *refs,
):
    ring = lax.axis_size("ctx")
    d, z = lax.axis_index("dp"), lax.axis_index("ctx")
    core, x, y, core_id, x_id, y_id = plane(d)
    bufs = [refs[6 * a : 6 * a + 6] for a in range(4)]
    send, recv, load, wo_ref, dwo_ref, small_acc, small_in = refs[24:31]
    s_send, s_recv, r_send, r_recv, r_local = refs[31:]
    batch, piece, width = ret_back.shape
    up, down, qkv, out = range(4)
    ins, sums = (up_ref, down_ref, qkv_ref, dwo_ref), (up_sum, down_sum, qkv_sum, out_sum)
    do = reducer(teams, LEVELS, ins, sums, bufs, send, recv, load)

    pairs = ((back_ref, ret_back),)
    mine = z - core

    def returned(which, i, to):
        source, target = pairs[which]
        return source.at[pl.ds(pl.multiple_of(to * piece, 16), piece), :], target.at[i]

    def start_returns(which):
        for i in range(batch):
            @pl.when(mine == i)
            def _(i=i):
                for k in range(1, ring):
                    to = (z + k) % ring
                    src, dst = returned(which, i, to)
                    remote(src, dst, r_send.at[which, k], r_recv.at[which, i], d, to).start()
                src, dst = returned(which, i, z)
                pltpu.make_async_copy(src, dst, r_local.at[which]).start()

    def wait_returns(which):
        for i in range(batch):
            src, dst = returned(which, i, z)

            @pl.when(mine == i)
            def _(src=src, dst=dst):
                pltpu.make_async_copy(src, dst, r_local.at[which]).wait()

            @pl.when(mine != i)
            def _(i=i, src=src, dst=dst):
                remote(src, dst, r_send.at[which, 0], r_recv.at[which, i], core_id, z).wait_recv()

    def close_returns(which):
        for i in range(batch):
            @pl.when(mine == i)
            def _(i=i):
                for k in range(1, ring):
                    to = (z + k) % ring
                    remote(*returned(which, i, to), r_send.at[which, k], r_recv.at[which, i], d, to).wait_send()

    steps = [core_id, x_id, y_id] + [team_id(d, t) for t in range(teams)]

    def small_copy(n):
        return remote(small_acc, small_in.at[n], s_send.at[n], s_recv.at[n], steps[n], z)

    def small_owner(k):
        n = len(steps) + k - 1
        return remote(small_acc, small_in.at[n], s_send.at[n], s_recv.at[n], d, (z + k) % ring)

    def small_close(n):
        small_copy(n).wait()
        small_acc[...] += small_in[n]
        if n + 1 < len(steps):
            small_copy(n + 1).start()
        else:
            for k in range(1, ring):
                small_owner(k).start()

    columns = weights.shape[1] - width
    wo_load = pltpu.make_async_copy(weights.at[:, pl.ds(columns, width)], wo_ref, r_local.at[2])
    wo_load.start()
    small_acc[0:8, :] = small_att[...]
    small_acc[8:16, :] = small_mlp[...]
    for n in range(small_up.shape[1] // width):
        small_acc[16 + n : 17 + n, :] = small_up[0:1, n * width : (n + 1) * width]
    rest = 16 + small_up.shape[1] // width
    small_acc[rest:, :] = jnp.zeros((small_acc.shape[0] - rest, width), F32)
    greet(teams)
    do.enter(qkv)
    start_returns(0)
    do.enter(up)
    do.enter(down)
    small_copy(0).start()
    do.total(up)
    do.total(down)
    dwo = dot(o_ref[...], g_ref[...], TN).astype(BF16)
    for r in range(ring):
        dwo_ref[r] = dwo[r * (width // ring) : (r + 1) * (width // ring), :]
    do.enter(out)
    do.first(qkv)
    do.first(out)
    small_close(0)
    do.share(up)
    do.share(down)
    wo_load.wait()
    for i in range(batch):
        at = pl.ds(i * piece, piece)
        attend_out[at, :] = dot(o_ref[at, :], wo_ref[...])
    do.second(qkv)
    do.second(out)
    small_close(1)
    do.to_owner(qkv)
    do.to_owner(out)
    for n in range(2, len(steps)):
        small_close(n)
    do.total(qkv)
    do.total(out)
    for k in range(1, ring):
        small_owner(k).wait()
    total = small_acc[...]
    for k in range(ring - 1):
        total += small_in[len(steps) + k]
    norm = jnp.concatenate([total[0:2], total[8:10], jnp.zeros((4, width), F32)], axis=0)
    norm_out[...] = pltpu.roll(norm, (ring - z) % ring * (width // ring), 1)
    ups = [total[16 + n : 17 + n] for n in range(small_up.shape[1] // width)]
    bias = jnp.concatenate([total[2:3], total[10:11], *ups, total[10:11]], axis=1)
    entries = bias.shape[1]
    bias = pltpu.roll(jnp.broadcast_to(bias, (8, entries)), (ring - z) % ring * (entries // ring), 1)
    bias_out[...] = bias[:, : bias_out.shape[1]]
    do.share(qkv)
    do.share(out)
    for a in range(4):
        do.close(a)
    wait_returns(0)
    close_returns(0)


def reduce_all(up, down, qkv, small_att, small_mlp, small_up, back, o, g, weights, batch):
    ring, groups = lax.axis_size("ctx"), lax.axis_size("dp")
    teams = (groups // 8).bit_length() - 1
    width = g.shape[1]
    piece = g.shape[0] // batch
    shapes = [(n, 4 * rows, 2 * span) for n, rows, span in (up.shape, down.shape)]
    shapes += [(1, width // ring, qkv.shape[1]), (1, width // ring, width)]
    dma = pltpu.SemaphoreType.DMA
    anywhere = pl.BlockSpec(memory_space=pl.ANY)
    vmem = pl.BlockSpec(memory_space=pltpu.VMEM)
    rounds = 3 + teams + ring - 1
    small = (16 + -(-small_up.shape[1] // width // 8) * 8, width)
    share = (3 * width + small_up.shape[1]) // ring
    scratch = reducer_scratch(LEVELS, shapes, teams, ring)
    scratch += [
        pltpu.VMEM((width, width), BF16),
        pltpu.VMEM((ring, width // ring, width), BF16), pltpu.VMEM(small, F32), pltpu.VMEM((rounds, *small), F32),
        dma((rounds,)), dma((rounds,)), dma((1, ring)), dma((1, batch)), dma((3,)),
    ]
    return pl.pallas_call(
        functools.partial(reduce_kernel, teams),
        in_specs=[anywhere] * 3 + [vmem] * 3 + [anywhere, vmem, vmem, anywhere],
        out_specs=[anywhere] * 4 + [vmem, vmem, vmem, anywhere],
        out_shape=[jax.ShapeDtypeStruct(shape, BF16) for shape in shapes]
        + [
            jax.ShapeDtypeStruct((8, width), F32), jax.ShapeDtypeStruct((8, share + -share % 128), F32),
            jax.ShapeDtypeStruct(g.shape, F32),
            jax.ShapeDtypeStruct((batch, piece, width), BF16),
        ],
        scratch_shapes=scratch,
        compiler_params=pltpu.CompilerParams(collective_id=1, has_side_effects=True, vmem_limit_bytes=56 * MIB),
        cost_estimate=pl.CostEstimate(flops=4 * width * width * g.shape[0], bytes_accessed=60 * MIB, transcendentals=0),
        name="reduce",
    )(
        up, down, qkv.reshape(ring, width // ring, -1), small_att, small_mlp, small_up, back,
        o.reshape(batch * piece, -1), g, weights,
    )


def attend_kernel(
    teams, order_ref, x_ref, stored_g_ref, norm_ref, bias_ref, cos_ref, low_ref, high_ref, wq_ref, wk_ref, wv_ref,
    wo_ref, up_ref, down_ref, h_ref, dqkv_all, small_ref, ret_o, up_sum, down_sum,
    g_ref, a_ref, at_ref, da_ref, q_ref, k_ref, v_ref, do_ref, o_ref, kt_ref, vt_ref, dqs_ref, dks_ref, dvs_ref,
    grad_ref, stored_o_ref, o_send, o_recv, o_local, grad_sem, *reduce_refs,
):
    step = pl.program_id(0)
    last = grad_ref.shape[0] - 1
    rows, width = x_ref.shape
    lanes = QUAD * HD
    tile = 256
    half = ROT // 2
    scale = 1.0 / math.sqrt(HD)
    blocks = rows // BLOCK
    ring = lax.axis_size("ctx")
    d, z = lax.axis_index("dp"), lax.axis_index("ctx")
    core_id = plane(d)[3]
    batch, piece = ret_o.shape[:2]
    mine = z - d % 2
    is_home = (mine >= 0) & (mine < batch)
    up, down = 0, 1
    bufs = (reduce_refs[:6], reduce_refs[6:12])
    do_sum = reducer(teams, MLP_LEVELS, (up_ref, down_ref), (up_sum, down_sum), bufs, *reduce_refs[12:])

    @pl.when(step == 0)
    def _():
        do_sum.enter(down)
        do_sum.enter(up)
        greet(teams)
        do_sum.first(down)
        do_sum.first(up)
        do_sum.second(up)

    def o_copy(quad, k, i):
        to = (z + k) % ring
        src = stored_o_ref.at[quad, pl.ds(pl.multiple_of(to * piece, 16), piece), :]
        dst = ret_o.at[i, :, pl.ds(pl.multiple_of(quad * lanes, 128), lanes)]
        if k == 0:
            return pltpu.make_async_copy(src, dst, o_local.at[quad])
        return remote(src, dst, o_send.at[quad, k], o_recv.at[quad, i], d, to)

    def grad_copy(quad, j):
        at = pl.ds(pl.multiple_of(j * width + quad * lanes, 128), lanes)
        return pltpu.make_async_copy(grad_ref.at[quad, j], dqkv_all.at[:, at], grad_sem.at[quad, j])


    def stored(ref, at):
        values = ref[pl.ds(at * BLOCK, BLOCK), :]
        return jnp.where(is_home, values, jnp.zeros_like(values))

    @pl.when(step == 0)
    def _():
        for j in range(blocks):
            place = order_ref[1, j]
            at = pl.ds(j * BLOCK, BLOCK)
            xh, _ = normalized(stored(x_ref, place).astype(F32))
            a = xh * norm_ref[1:2, :] + norm_ref[2:3, :]
            a_ref[at, :] = a.astype(BF16)
            at_ref[:, at] = a.T.astype(BF16)
            g_ref[at, :] = stored(stored_g_ref, place)
        da_ref[...] = jnp.zeros_like(da_ref)

    def table(ref, at):
        values = ref[at, :]
        return jnp.concatenate([values] * (lanes // values.shape[1]), axis=1)

    def turn(values, at):
        low = pltpu.roll(values, lanes - half, 1) * table(low_ref, at)
        high = pltpu.roll(values, half, 1) * table(high_ref, at)
        return values * table(cos_ref, at), low + high

    for t in range(rows // tile):
        at = pl.ds(t * tile, tile)
        a = a_ref[at, :]
        same, cross = turn(dot(a, wq_ref[...]) + bias_ref[0:1, :], at)
        q_ref[at, :] = ((same + cross).astype(BF16) * scale).astype(BF16)
        same, cross = turn(dot(a, wk_ref[...]), at)
        keys = same + cross
        k_ref[at, :] = keys.astype(BF16)
        kt_ref[:, at] = keys.T.astype(BF16)
        values = dot(a, wv_ref[...])
        v_ref[at, :] = values.astype(BF16)
        vt_ref[:, at] = values.T.astype(BF16)
        mixed_back = dot(g_ref[at, :], wo_ref[...], NT)
        do_ref[at, :] = mixed_back.astype(BF16)

    dks_ref[...] = jnp.zeros_like(dks_ref)
    dvs_ref[...] = jnp.zeros_like(dvs_ref)
    wide = 2 * HD
    head_of = lax.broadcasted_iota(jnp.int32, (BLOCK, wide), 1) // HD

    def stack(values):
        zero = jnp.zeros_like(values)
        return jnp.concatenate([jnp.where(head_of == e, values, zero) for e in range(2)], axis=0)

    def diagonal(values):
        return jnp.concatenate([values[e * HD : (e + 1) * HD, e * BLOCK : (e + 1) * BLOCK] for e in range(2)], axis=0)

    spot = lax.broadcasted_iota(jnp.int32, (BLOCK, 2 * BLOCK), 1) % BLOCK
    admitted = lax.broadcasted_iota(jnp.int32, (BLOCK, 2 * BLOCK), 0) <= spot

    def products_in(b, p):
        at, seen, own = pl.ds(b * BLOCK, BLOCK), pl.ds(0, (b + 1) * BLOCK), pl.ds(p * wide, wide)
        q, do = stack(q_ref[at, own]), stack(do_ref[at, own])
        return q, do, dot(k_ref[seen, own], q, NT), dot(v_ref[seen, own], do, NT)

    def softmax(b, scores, back):
        edge = jnp.where(admitted, scores[b * BLOCK :], -1e30)
        scores = edge if b == 0 else jnp.concatenate([scores[: b * BLOCK], edge], axis=0)
        top = jnp.max(scores, axis=0, keepdims=True)
        expo = jnp.exp(scores - top)
        probs = expo * (1.0 / jnp.sum(expo, axis=0, keepdims=True))
        share = jnp.sum(probs * back, axis=0, keepdims=True)
        return probs.astype(BF16), (probs * (back - share)).astype(BF16)

    def products_out(b, p, q, do, low, back):
        at, seen, own = pl.ds(b * BLOCK, BLOCK), pl.ds(0, (b + 1) * BLOCK), pl.ds(p * wide, wide)
        mixed = diagonal(dot(vt_ref[own, seen], low))
        o_ref[at, own] = mixed.T.astype(BF16)
        dqs_ref[at, own] = diagonal(dot(kt_ref[own, seen], back)).T * scale
        dks_ref[seen, own] += dot(back, q)
        dvs_ref[seen, own] += dot(low, do)

    units = [(b, p) for b in range(rows // BLOCK) for p in range(lanes // wide)]
    ready = products_in(*units[0])
    done = None
    for n, (b, p) in enumerate(units):
        q, do, scores, back = ready
        if n + 1 < len(units):
            ready = products_in(*units[n + 1])
        low, back = softmax(b, scores, back)
        if done is not None:
            products_out(*done)
        done = (b, p, q, do, low, back)
    products_out(*done)

    for s in range(blocks):
        stored_o_ref[step, s * BLOCK : (s + 1) * BLOCK, :] = o_ref[pl.ds(order_ref[0, s] * BLOCK, BLOCK), :]

    for i in range(batch):
        @pl.when(mine == i)
        def _(i=i):
            for k in range(ring):
                o_copy(step, k, i).start()

    total = jnp.zeros((1, lanes), F32)
    for t in range(rows // tile):
        at = pl.ds(t * tile, tile)
        same, cross = turn(dqs_ref[at, :], at)
        dq = (same - cross).astype(BF16)
        same, cross = turn(dks_ref[at, :], at)
        dk = (same - cross).astype(BF16)
        dv = dvs_ref[at, :].astype(BF16)
        total += jnp.sum(dq.astype(F32), axis=0, keepdims=True)
        q_ref[at, :] = dq
        k_ref[at, :] = dk
        v_ref[at, :] = dv
        da_ref[at, :] += dot(dq, wq_ref[...], NT) + dot(dk, wk_ref[...], NT) + dot(dv, wv_ref[...], NT)
    small_ref[2:3, pl.ds(pl.multiple_of(step * lanes, 128), lanes)] = total
    for j, ref in enumerate((q_ref, k_ref, v_ref)):
        grad_ref[step, j] = dot(at_ref[...], ref[...]).astype(BF16)
        grad_copy(step, j).start()
    @pl.when(step == 0)
    def _():
        do_sum.second(down)
        do_sum.to_owner(up)

    @pl.when(step == 1)
    def _():
        do_sum.to_owner(down)

    @pl.when(step == last)
    def _():
        gain = jnp.zeros((1, width), F32)
        shift = jnp.zeros((1, width), F32)
        for s in range(blocks):
            at = pl.ds(s * BLOCK, BLOCK)
            sorted_at = pl.ds(order_ref[0, s] * BLOCK, BLOCK)
            xh, _ = normalized(stored(x_ref, s).astype(F32))
            da = da_ref[sorted_at, :]
            gain += jnp.sum(da * xh, axis=0, keepdims=True)
            shift += jnp.sum(da, axis=0, keepdims=True)
            h_ref[at, :] = (da * norm_ref[1:2, :]).astype(BF16)
        small_ref[0:1, :] = gain
        small_ref[1:2, :] = shift
        small_ref[3:8, :] = jnp.zeros((5, width), F32)
        do_sum.hand_on(up)
        do_sum.hand_on(down)
        for quad in range(last + 1):
            for i in range(batch):
                @pl.when(mine != i)
                def _(quad=quad, i=i):
                    ref = ret_o.at[i, :, pl.ds(quad * lanes, lanes)]
                    remote(ref, ref, o_send.at[quad, 0], o_recv.at[quad, i], core_id, z).wait_recv()

                @pl.when(mine == i)
                def _(quad=quad, i=i):
                    o_copy(quad, 0, i).wait()
                    for k in range(1, ring):
                        o_copy(quad, k, i).wait_send()
        for quad in range(last + 1):
            for j in range(3):
                grad_copy(quad, j).wait()


def attend(order, x, g, norms, bias_q, tables, weights, up, down, batch):
    ring, groups_dp = lax.axis_size("ctx"), lax.axis_size("dp")
    teams = (groups_dp // 8).bit_length() - 1
    shapes = ((1, 2 * up.shape[1], 2 * up.shape[2]), (down.shape[1], down.shape[2], 2 * down.shape[3]))
    down = down.reshape(-1, *down.shape[2:])
    rows, width = x.shape
    lanes = QUAD * HD
    groups = width // lanes
    anywhere = pl.BlockSpec(memory_space=pl.ANY)
    whole = lambda shape: pl.BlockSpec(shape, lambda i: (0,) * len(shape))
    once = lambda shape: pl.BlockSpec(shape, lambda i: (0,) * len(shape), pipeline_mode=pl.Buffered(1))
    dma = pltpu.SemaphoreType.DMA
    slices = [(n, r // 4, c // 2) for n, r, c in shapes]
    return pl.pallas_call(
        functools.partial(attend_kernel, teams),
        grid=(groups,),
        in_specs=[
            pl.BlockSpec(memory_space=pltpu.SMEM),
            once((rows, width)),
            once((rows, width)),
            once(norms.shape),
            pl.BlockSpec((8, lanes), lambda i: (0, i)),
            once(tables[0].shape),
            once(tables[0].shape),
            once(tables[0].shape),
            pl.BlockSpec((width, lanes), lambda i: (0, i)),
            pl.BlockSpec((width, lanes), lambda i: (0, groups + i)),
            pl.BlockSpec((width, lanes), lambda i: (0, 2 * groups + i)),
            pl.BlockSpec((lanes, width), lambda i: (i, 3)),
            anywhere,
            anywhere,
        ],
        out_specs=[once((rows, width)), anywhere, once((8, width))] + [anywhere] * 3,
        out_shape=[
            jax.ShapeDtypeStruct((rows, width), BF16),
            jax.ShapeDtypeStruct((width, 3 * width), BF16),
            jax.ShapeDtypeStruct((8, width), F32),
            jax.ShapeDtypeStruct((batch, rows // ring, width), BF16),
        ]
        + [jax.ShapeDtypeStruct(shape, BF16) for shape in slices],
        scratch_shapes=[
            pltpu.VMEM((rows, width), BF16),
            pltpu.VMEM((rows, width), BF16),
            pltpu.VMEM((width, rows), BF16),
            pltpu.VMEM((rows, width), F32),
        ]
        + [pltpu.VMEM((rows, lanes), BF16)] * 5
        + [pltpu.VMEM((lanes, rows), BF16)] * 2
        + [pltpu.VMEM((rows, lanes), F32)] * 3
        + [
            pltpu.VMEM((groups, 3, width, lanes), BF16), pltpu.VMEM((groups, rows, lanes), BF16),
            dma((groups, ring)), dma((groups, batch)), dma((groups,)), dma((groups, 3)),
        ]
        + reducer_scratch(MLP_LEVELS, shapes, teams, ring),
        compiler_params=pltpu.CompilerParams(
            collective_id=2, has_side_effects=True, vmem_limit_bytes=60 * MIB
        ),
        cost_estimate=pl.CostEstimate(
            flops=24 * rows * width * width + 8 * rows * rows * width,
            bytes_accessed=16 * width * width + 8 * rows * width,
            transcendentals=HEADS * rows * rows // 2,
        ),
        name="attend",
    )(order, x, g, norms, bias_q, *tables, weights, weights, weights, weights, up, down)


def rotary_tables(length):
    half = ROT // 2
    frequency = ROPE_BASE ** (-(np.arange(half) * 2.0 / ROT))
    angle = np.arange(length)[:, None] * frequency[None, :]
    cosine, sine = np.cos(angle), np.sin(angle)
    rest = np.zeros((length, HD - ROT))
    none = np.zeros_like(sine)
    cos_full = np.concatenate([cosine, cosine, rest + 1.0], axis=1)
    low = np.concatenate([-sine, none, rest], axis=1)
    high = np.concatenate([none, sine, rest], axis=1)
    return tuple(jnp.asarray(np.tile(t, (1, 2)).astype(np.float32)) for t in (cos_full, low, high))


def adamw(weight, grad, first, second, rate, decay):
    first_new = BETA_ONE * first + (1.0 - BETA_ONE) * grad
    second_new = BETA_TWO * second + (1.0 - BETA_TWO) * grad * grad
    first_hat = first_new / (1.0 - BETA_ONE**STEP)
    second_hat = second_new / (1.0 - BETA_TWO**STEP)
    weight_new = weight - rate * (first_hat / (jnp.sqrt(second_hat) + EPS_ADAM) + decay * weight)
    return (first_new, second_new, weight_new)


RATES = (0.1, 0.6, 0.1, 0.05)


def finish_kernel(*refs):
    x_ref, g_ref, attend_ref, feed_ref, h_ref, back_ref, bias_ref, norm_grad = refs[:8]
    norm, norm_first, norm_second = refs[8:11]
    inputs, outputs = refs[11:27], refs[27:]
    layer_out, input_grad = outputs[:2]
    for n, rate in enumerate(RATES):
        weight, grad, first, second = (ref[...] for ref in inputs[4 * n : 4 * n + 4])
        new = adamw(weight, grad.astype(F32), first, second, rate, DECAY)
        for ref, value in zip(outputs[2 + 3 * n : 5 + 3 * n], new):
            ref[...] = value
    width = x_ref.shape[1]
    bias = bias_ref[0:1, width : 2 * width] + bias_ref[0:1, bias_ref.shape[1] - width :]
    rows = x_ref[...].astype(F32)
    layer_out[...] = (rows + attend_ref[...] + feed_ref[...] + bias).astype(BF16)
    xh, scale = normalized(rows)
    h = back_ref[...].astype(F32) + h_ref[...]
    inner = jnp.mean(h * xh, axis=-1, keepdims=True)
    input_grad[...] = g_ref[...].astype(F32) + scale * (h - jnp.mean(h, axis=-1, keepdims=True) - xh * inner)

    @pl.when(pl.program_id(0) == 0)
    def _():
        grad = norm_grad[0:4, : norm.shape[1]]
        first, second, new = adamw(norm[...], grad, norm_first[...], norm_second[...], 0.6, 0.0)
        outputs[14][...] = first
        outputs[15][...] = second[0:2]
        outputs[16][...] = second[2:4]
        outputs[17][...] = new


def finish(rows, biases, norm_grad, norm_args, weights):
    steps = 4
    whole = lambda v: pl.BlockSpec(v.shape, lambda i: (0,) * len(v.shape))
    part = lambda v: pl.BlockSpec((v.shape[0] // steps, v.shape[1]), lambda i: (i, 0))
    like = lambda v, dtype: jax.ShapeDtypeStruct(v.shape, dtype)
    count, width = rows[0].shape
    args = [*rows, biases, norm_grad, *norm_args] + [v for group in weights for v in group]
    specs = [part(v) for v in rows] + [whole(v) for v in (biases, norm_grad, *norm_args)]
    specs += [part(v) for group in weights for v in group]
    outs = [like(rows[0], BF16), like(rows[0], F32)] + [like(group[0], F32) for group in weights for _ in range(3)]
    out_specs = [part(v) for v in outs]
    own = norm_args[0].shape[1]
    norm_outs = [jax.ShapeDtypeStruct((n, own), F32) for n in (4, 2, 2, 4)]
    return pl.pallas_call(
        finish_kernel,
        grid=(steps,),
        in_specs=specs,
        out_specs=out_specs + [whole(v) for v in norm_outs],
        out_shape=outs + norm_outs,
        compiler_params=pltpu.CompilerParams(vmem_limit_bytes=56 * MIB),
        cost_estimate=pl.CostEstimate(flops=0, bytes_accessed=64 * MIB, transcendentals=0),
        name="finish",
    )(*args)


def shards(
    tokens, out_grad, block_order, qkv_weight, out_weight, up_weight, down_weight, norm_params, bias_params,
    qkv_first, qkv_second, out_first, out_second, up_first, up_second, down_first, down_second,
    norm_first, norm_second, bias_first, bias_second,
):
    groups, ring = lax.axis_size("dp"), lax.axis_size("ctx")
    group, rank = lax.axis_index("dp"), lax.axis_index("ctx")
    batch, piece, width = tokens.shape
    length = piece * ring
    count = batch * piece
    ff = up_weight.shape[1]

    share = bias_params.shape[0]
    lanes = share + -share % 128
    small = jnp.concatenate([
        jnp.pad(bias_params[None, :], ((0, 0), (0, lanes - share))),
        jnp.pad(norm_params, ((0, 3), (0, lanes - norm_params.shape[1]))),
    ])
    x_rows, g_rows = tokens.reshape(count, width), out_grad.reshape(count, width)
    att_copy, biases, norms, home_x, home_g, feed_out, h_feed, dup, ddown, dbias_up, small_feed = gather_feed(
        up_weight, down_weight, qkv_weight, out_weight, small, x_rows, g_rows, piece, ring * share
    )

    odd = group % 2

    order = block_order[jnp.clip(rank - odd, 0, batch - 1)]
    spots = jnp.arange(order.shape[0])
    order = jnp.stack([order, jnp.sum(jnp.where(order[None, :] == spots[:, None], spots[None, :], 0), axis=1)])

    h_attend, dqkv, small_attend, o_rows, up_slice, down_slice = attend(
        order, home_x, home_g, norms, biases, rotary_tables(length), att_copy, dup, ddown, batch
    )
    *owned, norm_grad, bias_grad, attend_out, ret_back = reduce_all(
        up_slice, down_slice, dqkv, small_attend, small_feed, dbias_up, h_attend, o_rows, g_rows, att_copy, batch
    )
    up_grad, down_grad, qkv_grad, out_grads = (
        g.reshape(w.shape) for g, w in zip(owned, (up_weight, down_weight, qkv_weight, out_weight))
    )
    layer_out, input_grad, *new, norm_a, norm_b, norm_c, norm_d = finish(
        (x_rows, g_rows, attend_out, feed_out, h_feed, ret_back.reshape(count, width)),
        biases,
        norm_grad,
        (norm_params, norm_first, norm_second),
        (
            (qkv_weight, qkv_grad, qkv_first, qkv_second),
            (out_weight, out_grads, out_first, out_second),
            (up_weight, up_grad, up_first, up_second),
            (down_weight, down_grad, down_first, down_second),
        ),
    )
    bias_new = adamw(bias_params, bias_grad[0, :share], bias_first, bias_second, 0.6, 0.0)
    return (
        layer_out.reshape(tokens.shape), input_grad.reshape(tokens.shape), *new,
        norm_a, norm_b, norm_c, norm_d, *bias_new,
    )


def solution(mesh):
    rows, columns, token = P("ctx", None), P(None, "ctx"), P("dp", "ctx", None)
    in_specs = (token, token, P("dp", None)) + (rows,) * 4 + (columns, P("ctx")) + (rows,) * 8
    in_specs += (columns, columns, P("ctx"), P("ctx"))
    out_specs = (token, token) + (rows,) * 12 + (columns,) * 4 + (P("ctx"),) * 3
    return jax.shard_map(shards, mesh=mesh, in_specs=in_specs, out_specs=out_specs, check_vma=False)
```

```python
import functools
import math
from types import SimpleNamespace

import jax
import jax.numpy as jnp
import numpy as np
from jax import lax
from jax.experimental import pallas as pl
from jax.experimental.pallas import tpu as pltpu
from jax.sharding import PartitionSpec as P

HEADS = 12
HD = 64
STEP = 10
ROT = 16
BLOCK = 128
QUAD = 4
MLP_LEVELS = (2, 1)
LEVELS = (3, 3, 0, 0)

EPS_NORM = 1e-05
BETA_ONE = 0.9
BETA_TWO = 0.95
EPS_ADAM = 1e-08
DECAY = 0.01
ROPE_BASE = 10000.0
F32 = jnp.float32
BF16 = jnp.bfloat16
MIB = 1024 * 1024


def dot(left, right, dims=((1,), (0,))):
    return lax.dot_general(left, right, (dims, ((), ())), preferred_element_type=F32)


NN = ((1,), (0,))
NT = ((1,), (1,))
TN = ((0,), (0,))


def normalized(values):
    mean = jnp.mean(values, axis=-1, keepdims=True)
    centred = values - mean
    variance = jnp.mean(centred * centred, axis=-1, keepdims=True)
    scale = lax.rsqrt(variance + EPS_NORM)
    return centred * scale, scale


MESH = pl.DeviceIdType.MESH


def plane(d):
    core, x, y = d % 2, d // 2 % 2, d // 4 % 2
    return core, x, y, d + 1 - 2 * core, d + 2 - 4 * x, d + 4 - 8 * y


def gather_kernel(
    up, down, qkv, out, small, tokens, cotangents,
    att_all, small_all, norm_all, home_x, home_g, out_ref, h_ref, up_part, down_part, dbias_ref, sums_ref,
    up_all, down_all, att_own, up_wide, down_wide, att_wide, small_in, x_ref, g_ref, m_ref, mt_ref, hid_ref, dup_in_ref,
    dup_ref, up_core, up_first, ddown_ref, down_core,
    z_send, z_recv, p_send, p_recv, s_send, s_recv, t_send, t_recv, local, out_sem, c_send, c_recv,
):
    ring = lax.axis_size("ctx")
    d, z = lax.axis_index("dp"), lax.axis_index("ctx")
    core, x, y, core_id, x_id, y_id = plane(d)
    own = x + 2 * y
    own_x, own_y, far = own + 1 - 2 * x, own + 2 - 4 * y, 3 - own
    count, width = tokens.shape
    piece = home_x.shape[0] // ring
    batch = count // piece
    arrays = ((up_wide, up_all, False), (down_wide, down_all, True), (att_own, att_all, False))

    def slot(a, base, place, half=None):
        source, whole, tall = arrays[a]
        ref = source if base is None else whole
        rows, columns = source.shape
        at = 0 if base is None else base * rows
        height, span = rows // 4, columns // 2
        at = at + place * height
        column = core * span
        if half is not None:
            if tall:
                height = height // 2
                at = at + half * height
            else:
                span = span // 2
                column = column + half * span
        return ref.at[pl.ds(pl.multiple_of(at, 16), height), pl.ds(pl.multiple_of(column, 128), span)]

    def other_slot(a, base, place):
        source, whole, tall = arrays[a]
        rows, columns = source.shape
        at = pl.multiple_of(base * rows + place * (rows // 4), 16)
        column = pl.multiple_of((1 - core) * (columns // 2), 128)
        return whole.at[pl.ds(at, rows // 4), pl.ds(column, columns // 2)]

    def remote(src, dst, send, recv, dp, ctx):
        return pltpu.make_async_remote_copy(
            src_ref=src, dst_ref=dst, send_sem=send, recv_sem=recv, device_id=(dp, ctx), device_id_type=MESH
        )

    columns = qkv.shape[1]
    wide_loads = [
        [pltpu.make_async_copy(up, up_wide, local.at[0])],
        [pltpu.make_async_copy(down, down_wide, local.at[1])],
        [
            pltpu.make_async_copy(qkv, att_wide.at[:, pl.ds(0, columns)], local.at[2]),
            pltpu.make_async_copy(out, att_wide.at[:, pl.ds(columns, out.shape[1])], local.at[8]),
        ],
    ]
    for loads in wide_loads:
        for copy in loads:
            copy.start()

    def cast_own(a):
        for copy in wide_loads[a]:
            copy.wait()
        wide, target = ((up_wide, up_all), (down_wide, down_all), (att_wide, att_own))[a]
        rows = wide.shape[0]
        tile = 64
        base = 0 if a == 2 else z * rows

        def body(t, _):
            value = wide[pl.ds(pl.multiple_of(t * tile, 16), tile), :].astype(BF16)
            target[pl.ds(pl.multiple_of(base + t * tile, 16), tile), :] = value
            return 0

        lax.fori_loop(0, rows // tile, body, 0)

    barrier = pltpu.get_barrier_semaphore()
    for k in range(1, ring):
        pl.semaphore_signal(barrier, inc=1, device_id=(d, (z + k) % ring), device_id_type=MESH)
    for other in (core_id, x_id, y_id):
        pl.semaphore_signal(barrier, inc=1, device_id=(other, z), device_id_type=MESH)
    cast_own(0)
    pl.semaphore_wait(barrier, ring + 2)

    def hop(a, way, h):
        shard = z - h if way == 0 else z + h
        target = z + 1 if way == 0 else z - 1
        src = slot(a, None, own) if h == 0 and a == 2 else slot(a, shard, own)
        return remote(src, slot(a, shard, own), z_send.at[a, way, h], z_recv.at[a, way, h], d, target)

    def can_send(way, h):
        shard = z - h if way == 0 else z + h
        target = z + 1 if way == 0 else z - 1
        return (shard >= 0) & (shard < ring) & (target >= 0) & (target < ring)

    def in_range(way, h):
        shard = z - h if way == 0 else z + h
        return (shard >= 0) & (shard < ring)

    def cast(a, shard, j):
        send, recv = p_send.at[a, shard, j], p_recv.at[a, shard, j]
        if j == 0:
            ref = slot(a, shard, own)
            return remote(ref, ref, send, recv, x_id, z)
        if j == 1:
            ref = slot(a, shard, own)
            return remote(ref, ref, send, recv, y_id, z)
        if j == 2:
            ref = slot(a, shard, own_x, 0)
            return remote(ref, ref, send, recv, y_id, z)
        if j == 3:
            ref = slot(a, shard, own_y, 1)
            return remote(ref, ref, send, recv, x_id, z)
        ref = slot(a, shard, (own, own_x, own_y, far)[j - 4])
        return remote(ref, ref, send, recv, core_id, z)

    def arrived(a, shard, j):
        send, recv = p_send.at[a, shard, j], p_recv.at[a, shard, j]
        ref = {0: lambda: slot(a, shard, own_x), 1: lambda: slot(a, shard, own_y),
               2: lambda: slot(a, shard, far, 0), 3: lambda: slot(a, shard, far, 1)}.get(
            j, lambda: other_slot(a, shard, (own, own_x, own_y, far)[j - 4]))()
        remote(ref, ref, send, recv, core_id, z).wait_recv()

    def start_hops(a):
        for way in range(2):
            @pl.when(can_send(way, 0))
            def _(way=way):
                hop(a, way, 0).start()

    def small_copy(k):
        return remote(small, small_in.at[z], s_send.at[k], s_recv.at[k], d, (z + k) % ring)

    def stage_a(a, h):
        for way in range(2):
            @pl.when(in_range(way, h))
            def _(way=way):
                shard = z - h if way == 0 else z + h
                ref = slot(a, shard, own)
                remote(ref, ref, z_send.at[a, way, h - 1], z_recv.at[a, way, h - 1], core_id, z).wait_recv()

                @pl.when(can_send(way, h))
                def _():
                    hop(a, way, h).start()

                cast(a, shard, 0).start()
                cast(a, shard, 1).start()
                cast(a, shard, 4).start()

    def stage_b(a, h):
        for way in range(2):
            @pl.when(in_range(way, h))
            def _(way=way):
                shard = z - h if way == 0 else z + h
                arrived(a, shard, 0)
                cast(a, shard, 2).start()
                cast(a, shard, 5).start()
                arrived(a, shard, 1)
                cast(a, shard, 3).start()
                cast(a, shard, 6).start()

    def stage_c(a, h):
        for way in range(2):
            @pl.when(in_range(way, h))
            def _(way=way):
                shard = z - h if way == 0 else z + h
                arrived(a, shard, 2)
                arrived(a, shard, 3)
                cast(a, shard, 7).start()

    def stage_d(a, h):
        for way in range(2):
            @pl.when(in_range(way, h))
            def _(way=way):
                shard = z - h if way == 0 else z + h
                for j in range(4, 8):
                    arrived(a, shard, j)

    pairs = ((tokens, home_x), (cotangents, home_g))

    def move(which, i):
        source, whole = pairs[which]
        src = source.at[pl.ds(i * piece, piece), :]
        dst = whole.at[pl.ds(pl.multiple_of(z * piece, 16), piece), :]
        return src, dst, i + core

    def start_moves(which):
        for i in range(batch):
            src, dst, target = move(which, i)

            @pl.when(target != z)
            def _(src=src, dst=dst, target=target, i=i):
                remote(src, dst, t_send.at[which, i], t_recv.at[which, z], d, target).start()

            @pl.when(target == z)
            def _(src=src, dst=dst):
                pltpu.make_async_copy(src, dst, local.at[6 + which]).start()

    own_rows = pl.ds(pl.multiple_of(z * att_own.shape[0], 16), att_own.shape[0])
    own_att = pltpu.make_async_copy(att_own, att_all.at[own_rows, :], local.at[9])
    x_load = pltpu.make_async_copy(tokens, x_ref, local.at[3])
    g_load = pltpu.make_async_copy(cotangents, g_ref, local.at[4])
    own_small = pltpu.make_async_copy(small, small_in.at[z], local.at[5])

    start_hops(0)
    cast_own(1)
    start_hops(1)
    cast_own(2)
    start_hops(2)
    for k in range(1, ring):
        small_copy(k).start()
    for copy in (own_att, x_load, g_load, own_small):
        copy.start()
    hops = range(1, ring)
    work = [(a, h) for a in range(2) for h in hops]
    for n in range(len(work) + 2):
        if n < len(work):
            stage_a(*work[n])
        if n == len(work) - 1:
            start_moves(0)
        if 1 <= n <= len(work):
            stage_b(*work[n - 1])
        if n >= 2:
            stage_c(*work[n - 2])
    stage_a(2, 1)

    own_small.wait()
    for k in range(1, ring):
        ref = small_in.at[(z + ring - k) % ring]
        remote(ref, ref, s_send.at[k], s_recv.at[k], core_id, z).wait_recv()
    x_load.wait()
    g_load.wait()
    entries = small_all.shape[1]
    biases = jnp.zeros((8, entries), F32)
    norms = jnp.zeros((8, width), F32)
    for r in range(ring):
        block = small_in[r].astype(BF16).astype(F32)
        full = jnp.concatenate([block, jnp.zeros((8, entries - block.shape[1]), F32)], axis=1)
        biases += pltpu.roll(full, r * (entries // ring), 1) if r else full
        norms += pltpu.roll(block[:, :width], r * (width // ring), 1) if r else block[:, :width]
    small_all[...] = biases
    norm_all[...] = norms
    ff = up_all.shape[1]
    gain_2, shift_2 = norm_all[3:4, :], norm_all[4:5, :]
    tile = 256
    tiles = count // tile
    for t in range(tiles):
        at = pl.ds(t * tile, tile)
        xh, _ = normalized(x_ref[at, :].astype(F32))
        m = xh * gain_2 + shift_2
        m_ref[at, :] = m.astype(BF16)
        mt_ref[:, at] = m.T.astype(BF16)
        out_ref[at, :] = jnp.zeros((tile, width), F32)
        h_ref[at, :] = jnp.zeros((tile, width), F32)
    for h in hops:
        stage_d(0, h)
        stage_d(1, h)

    strip = dup_ref.shape[3] // ring
    steps = ff // (ring * strip)
    half = ring // 2
    big, by_core = (dup_ref, ddown_ref), (up_core, down_core)
    bits, ids = ((x, y), (y, x)), ((x_id, y_id), (y_id, x_id))

    def sizes(a):
        return by_core[a].shape[2], by_core[a].shape[3]

    def slice_of(order):
        return 2 * bits[order][0] + bits[order][1]

    def core_copy(a, i):
        _, span = sizes(a)
        away = pl.ds(pl.multiple_of((1 - core) * span, 128), span)
        return remote(big[a].at[i, :, :, away], by_core[a].at[i], c_send.at[a, i, 0], c_recv.at[a, i, 0], core_id, z)

    def first_copy(a, i, order):
        height, _ = sizes(a)
        own = pl.ds(order * half, half)
        away = pl.ds(pl.multiple_of((1 - bits[order][0]) * (height // 2), 16), height // 2)
        return remote(
            by_core[a].at[i, own, away, :], up_first.at[i, own], c_send.at[a, i, 1 + order],
            c_recv.at[a, i, 1 + order], ids[order][0], z,
        )

    def add(into, at, term, owners):
        height = term(0).shape[0]
        tile = 32 if height % 48 else 48

        def body(n, _):
            o, t = n // (height // tile), n % (height // tile)
            spot = pl.ds(pl.multiple_of(at + t * tile, 16), tile)
            value = term(o)[pl.ds(pl.multiple_of(t * tile, 16), tile), :]
            into[o, spot, :] = (into[o, spot, :].astype(F32) + value.astype(F32)).astype(BF16)
            return 0

        lax.fori_loop(0, owners * (height // tile), body, 0)

    def chunk_1(i):
        for a in range(2):
            _, span = sizes(a)
            core_copy(a, i).wait_recv()
            keep = pl.ds(pl.multiple_of(core * span, 128), span)
            add(by_core[a].at[i], 0, lambda o: big[a].at[i, o, :, keep], ring)
        for order in range(2):
            first_copy(0, i, order).start()
        parts_out(1, i)[0].start()

    def chunk_2(i):
        height, _ = sizes(0)
        for order in range(2):
            own = pl.ds(order * half, half)
            first_copy(0, i, order).wait_recv()
            at = bits[order][0] * (height // 2)
            add(by_core[0].at[i, own], at, lambda o: up_first.at[i, order * half + o], half)
        for copy in parts_out(0, i):
            copy.start()

    def parts_out(a, i):
        height, span = sizes(a)
        if a == 1:
            return [pltpu.make_async_copy(by_core[1].at[i], down_part.at[:, i], out_sem.at[i, 2 * half])]
        copies = []
        for order in range(2):
            own = pl.ds(order * half, half)
            rows = pl.ds(pl.multiple_of(bits[order][0] * (height // 2), 16), height // 2)
            for n in range(half):
                copies.append(pltpu.make_async_copy(
                    by_core[0].at[i, own, rows, pl.ds(n * strip, strip)],
                    up_part.at[own, :, pl.ds(pl.multiple_of(n * steps * strip + i * strip, 128), strip)],
                    out_sem.at[i, half * order + n],
                ))
        return copies

    def feed_step(step, _):
        @pl.when(step == 1)
        def _():
            start_moves(1)

        for h in hops:
            @pl.when((step == 2 * h - 2) & (h > 1))
            def _(h=h):
                stage_a(2, h)

            @pl.when(step == 2 * h)
            def _(h=h):
                stage_b(2, h)

            @pl.when(step == 2 * h + 1)
            def _(h=h):
                stage_c(2, h)

        @pl.when(step < steps)
        def _():
            spots = [pl.ds(pl.multiple_of(r * (ff // ring) + step * strip, 128), strip) for r in range(ring)]
            bias_spots = [
                pl.ds(pl.multiple_of(2 * width + r * (ff // ring) + step * strip, 128), strip) for r in range(ring)
            ]
            up_part_ = jnp.concatenate([up_all[:, at] for at in spots], axis=1)
            down_part_ = jnp.concatenate([down_all[at, :] for at in spots], axis=0)
            bias = jnp.concatenate([small_all[0:1, at] for at in bias_spots], axis=1)
            total = jnp.zeros((1, ring * strip), F32)
            for t in range(tiles):
                at = pl.ds(t * tile, tile)
                u = dot(m_ref[at, :], up_part_) + bias
                cdf = 0.5 * (1.0 + lax.erf(u * (1.0 / math.sqrt(2.0))))
                hidden = (u * cdf).astype(BF16)
                slope = cdf + u * jnp.exp(-0.5 * u * u) * (1.0 / math.sqrt(2.0 * math.pi))
                back = (dot(g_ref[at, :], down_part_, NT) * slope).astype(BF16)
                hid_ref[at, :] = hidden
                dup_in_ref[at, :] = back
                total += jnp.sum(back.astype(F32), axis=0, keepdims=True)
                out_ref[at, :] += dot(hidden, down_part_)
                h_ref[at, :] += dot(back, up_part_, NT)
            for r in range(ring):
                dbias_ref[0:1, spots[r]] = total[:, r * strip : (r + 1) * strip]
            ddown = dot(hid_ref[...], g_ref[...], TN).astype(BF16)
            dup = dot(mt_ref[...], dup_in_ref[...]).astype(BF16)
            for r in range(ring):
                ddown_ref[step, r] = ddown[r * strip : (r + 1) * strip, :]
                dup_ref[step, r] = dup[r * (width // ring) : (r + 1) * (width // ring), :]
            core_copy(0, step).start()
            core_copy(1, step).start()

        for lag, stage in ((1, chunk_1), (3, chunk_2)):
            @pl.when((step >= lag) & (step < steps + lag))
            def _(lag=lag, stage=stage):
                stage(step - lag)

        return 0

    lax.fori_loop(0, steps + 3, feed_step, 0)

    gain = jnp.zeros((1, width), F32)
    shift = jnp.zeros((1, width), F32)
    sums = jnp.zeros((1, width), F32)
    for t in range(tiles):
        at = pl.ds(t * tile, tile)
        xh, _ = normalized(x_ref[at, :].astype(F32))
        dm = h_ref[at, :]
        gain += jnp.sum(dm * xh, axis=0, keepdims=True)
        shift += jnp.sum(dm, axis=0, keepdims=True)
        sums += jnp.sum(g_ref[at, :].astype(F32), axis=0, keepdims=True)
        h_ref[at, :] = dm * gain_2
    sums_ref[...] = jnp.concatenate([gain, shift, sums, jnp.zeros((5, width), F32)], axis=0)

    mine = z - core
    for which in range(2):
        for k in range(1, ring):
            @pl.when((mine >= 0) & (mine < batch))
            def _(which=which, k=k):
                other = (z + k) % ring
                ref = pairs[which][1].at[pl.ds(pl.multiple_of(other * piece, 16), piece), :]
                remote(ref, ref, t_send.at[which, 0], t_recv.at[which, other], core_id, z).wait_recv()
    for h in hops:
        stage_d(2, h)
    for k in range(1, ring):
        small_copy(k).wait_send()
    for a in range(3):
        for way in range(2):
            for h in range(ring - 1):
                @pl.when(can_send(way, h))
                def _(a=a, way=way, h=h):
                    hop(a, way, h).wait_send()
        for h in hops:
            for way in range(2):
                @pl.when(in_range(way, h))
                def _(a=a, h=h, way=way):
                    shard = z - h if way == 0 else z + h
                    for j in range(8):
                        cast(a, shard, j).wait_send()
    for which in range(2):
        for i in range(batch):
            src, dst, target = move(which, i)

            @pl.when(target != z)
            def _(src=src, dst=dst, target=target, which=which, i=i):
                remote(src, dst, t_send.at[which, i], t_recv.at[which, z], d, target).wait_send()

            @pl.when(target == z)
            def _(src=src, dst=dst, which=which):
                pltpu.make_async_copy(src, dst, local.at[6 + which]).wait()
    own_att.wait()

    def close(i, _):
        for a in range(2):
            core_copy(a, i).wait_send()
            for copy in parts_out(a, i):
                copy.wait()
        for order in range(2):
            first_copy(0, i, order).wait_send()
        return 0

    lax.fori_loop(0, steps, close, 0)


def gather_feed(up, down, qkv, out, small, tokens, cotangents, piece, entries):
    ring = lax.axis_size("ctx")
    count, width = tokens.shape
    ff = up.shape[1]
    strip = 128
    chunk = ring * strip
    steps = ff // chunk
    shard = up.shape[0]
    columns = qkv.shape[1] + out.shape[1]
    home = jax.ShapeDtypeStruct((ring * piece, width), tokens.dtype)
    rows = jax.ShapeDtypeStruct((count, width), F32)
    dma = pltpu.SemaphoreType.DMA
    anywhere = pl.BlockSpec(memory_space=pl.ANY)
    vmem = pl.BlockSpec(memory_space=pltpu.VMEM)
    return pl.pallas_call(
        gather_kernel,
        in_specs=[anywhere] * 7,
        out_specs=[anywhere, vmem, vmem, anywhere, anywhere, vmem, vmem, anywhere, anywhere, vmem, vmem],
        out_shape=[
            jax.ShapeDtypeStruct((ring * shard, columns), BF16),
            jax.ShapeDtypeStruct((8, entries), F32), jax.ShapeDtypeStruct((8, width), F32), home, home, rows, rows,
            jax.ShapeDtypeStruct((ring, shard // 2, ff // 2), BF16),
            jax.ShapeDtypeStruct((ring, steps, strip, width // 2), BF16),
            jax.ShapeDtypeStruct((8, ff), F32), jax.ShapeDtypeStruct((8, width), F32),
        ],
        scratch_shapes=[
            pltpu.VMEM((ring * shard, ff), BF16), pltpu.VMEM((ring * down.shape[0], width), BF16),
            pltpu.VMEM((shard, columns), BF16),
            pltpu.VMEM(up.shape, F32), pltpu.VMEM(down.shape, F32), pltpu.VMEM((shard, columns), F32),
            pltpu.VMEM((ring, *small.shape), F32),
            pltpu.VMEM((count, width), BF16), pltpu.VMEM((count, width), BF16), pltpu.VMEM((count, width), BF16),
            pltpu.VMEM((width, count), BF16),
            pltpu.VMEM((count, chunk), BF16), pltpu.VMEM((count, chunk), BF16),
            pltpu.VMEM((steps, ring, shard, chunk), BF16), pltpu.VMEM((steps, ring, shard, chunk // 2), BF16),
            pltpu.VMEM((steps, ring, shard // 2, chunk // 2), BF16),
            pltpu.VMEM((steps, ring, strip, width), BF16), pltpu.VMEM((steps, ring, strip, width // 2), BF16),
            dma((3, 2, ring)), dma((3, 2, ring)), dma((3, ring, 8)), dma((3, ring, 8)),
            dma((ring,)), dma((ring,)), dma((2, count // piece)), dma((2, ring)), dma((10,)), dma((steps, ring + 1)),
            dma((2, steps, 3)), dma((2, steps, 3)),
        ],
        compiler_params=pltpu.CompilerParams(
            collective_id=0, has_side_effects=True, vmem_limit_bytes=60 * MIB
        ),
        cost_estimate=pl.CostEstimate(
            flops=12 * count * width * ff, bytes_accessed=60 * MIB, transcendentals=count * ff
        ),
        name="gather_feed",
    )(up, down, qkv, out, small, tokens, cotangents)


def remote(src, dst, send_sem, recv_sem, dp, ctx):
    return pltpu.make_async_remote_copy(
        src_ref=src, dst_ref=dst, send_sem=send_sem, recv_sem=recv_sem, device_id=(dp, ctx), device_id_type=MESH
    )


def team_id(d, t):
    return d + (8 << t) * (1 - 2 * (d // (8 << t) % 2))


def greet(teams):
    ring = lax.axis_size("ctx")
    d, z = lax.axis_index("dp"), lax.axis_index("ctx")
    core, x, y, core_id, x_id, y_id = plane(d)
    barrier = pltpu.get_barrier_semaphore()
    partners = [core_id, x_id, y_id, x_id + y_id - d] + [team_id(d, t) for t in range(teams)]
    for k in range(1, ring):
        pl.semaphore_signal(barrier, inc=1, device_id=(d, (z + k) % ring), device_id_type=MESH)
    for other in partners:
        pl.semaphore_signal(barrier, inc=1, device_id=(other, z), device_id_type=MESH)
    pl.semaphore_wait(barrier, ring - 1 + len(partners))


def reducer(teams, levels, ins, sums, bufs, send, recv, load):
    count = len(ins)
    ring = lax.axis_size("ctx")
    d, z = lax.axis_index("dp"), lax.axis_index("ctx")
    core, x, y, core_id, x_id, y_id = plane(d)
    far_id = x_id + y_id - d
    bits, ids = ((x, y), (y, x)), ((x_id, y_id), (y_id, x_id))
    spots = ((x, y), (1 - x, y), (x, 1 - y), (1 - x, 1 - y))

    def sizes(a):
        _, strips, quarter, span = bufs[a][-1].shape
        return strips, quarter, span

    def owners(a, order):
        strips = sizes(a)[0]
        return pl.ds(order * ring // 2 * strips, ring // 2 * strips)

    def rows_at(at, height):
        return pl.ds(pl.multiple_of(at, 16), height)

    def kept(a, order):
        return 0 if levels[a] == 2 else bits[order][0] * 2 * sizes(a)[1]

    def core_copy(a):
        span = sizes(a)[2]
        away = pl.ds(pl.multiple_of((1 - core) * span, 128), span)
        return remote(ins[a].at[:, :, away], bufs[a][1], send.at[a, 0], recv.at[a, 0], core_id, z)

    def own_load(a):
        if levels[a] == 3:
            return pltpu.make_async_copy(ins[a], bufs[a][5].at[0], load.at[a])
        span = sizes(a)[2]
        keep = pl.ds(pl.multiple_of(core * span, 128), span)
        src = ins[a].at[:, :, keep] if levels[a] == 0 else ins[a]
        return pltpu.make_async_copy(src, bufs[a][0], load.at[a])

    def first_copy(a, order):
        quarter = sizes(a)[1]
        away = rows_at((1 - bits[order][0]) * 2 * quarter, 2 * quarter)
        return remote(
            bufs[a][0].at[owners(a, order), away, :], bufs[a][2].at[owners(a, order)], send.at[a, 1 + order],
            recv.at[a, 1 + order], ids[order][0], z,
        )

    def second_copy(a, order):
        quarter = sizes(a)[1]
        away = rows_at(kept(a, order) + (1 - bits[order][1]) * quarter, quarter)
        return remote(
            bufs[a][0].at[owners(a, order), away, :], bufs[a][3].at[owners(a, order)], send.at[a, 3 + order],
            recv.at[a, 3 + order], ids[order][1], z,
        )

    def own_quarter(a, owner):
        strips, quarter, _ = sizes(a)
        order = owner // (ring // 2)
        first, second = (1 - order) * x + order * y, (1 - order) * y + order * x
        at = second * quarter if levels[a] == 2 else (2 * first + second) * quarter
        return bufs[a][0].at[pl.ds(owner * strips, strips), rows_at(at, quarter), :]

    def owner_copy(a, k):
        to = (z + k) % ring
        return remote(own_quarter(a, to), bufs[a][4].at[k - 1], send.at[a, 4 + k], recv.at[a, 4 + k], d, to)

    def team_copy(a, t):
        j = 4 + ring + 7 + t
        return remote(bufs[a][5].at[0], bufs[a][5].at[1 + t], send.at[a, j], recv.at[a, j], team_id(d, t), z)

    def final(a, spot, side):
        strips, quarter, span = sizes(a)
        order = z // (ring // 2)
        xx, yy = spots[spot]
        at = ((1 - order) * (2 * xx + yy) + order * (2 * yy + xx)) * quarter
        return sums[a].at[:, rows_at(at, quarter), pl.ds(pl.multiple_of(side * span, 128), span)]

    def spread(a, j):
        s, r = send.at[a, 4 + ring + j - 1], recv.at[a, 4 + ring + j - 1]
        if j < 4:
            return remote(bufs[a][5].at[0], final(a, 0, core), s, r, (x_id, y_id, far_id)[j - 1], z)
        src = bufs[a][5].at[0] if j == 4 else final(a, j - 4, core)
        return remote(src, final(a, j - 4, core), s, r, core_id, z)

    def spread_here(a, j):
        s, r = send.at[a, 4 + ring + j - 1], recv.at[a, 4 + ring + j - 1]
        ref = final(a, j, core) if j < 4 else final(a, j - 4, 1 - core)
        remote(ref, ref, s, r, core_id, z).wait_recv()

    def keep_own(a):
        return pltpu.make_async_copy(bufs[a][5].at[0], final(a, 0, core), load.at[count + a])

    def add(into, at, term, blocks):
        height = term.shape[1]
        tile = 32 if height % 48 else 48

        def body(n, _):
            o, t = n // (height // tile), n % (height // tile)
            spot = rows_at(at + t * tile, tile)
            value = term[o, rows_at(t * tile, tile), :]
            into[o, spot, :] = (into[o, spot, :].astype(F32) + value.astype(F32)).astype(BF16)
            return 0

        lax.fori_loop(0, blocks * (height // tile), body, 0)

    def enter(a):
        if levels[a] == 0:
            core_copy(a).start()
        own_load(a).start()

    def first(a):
        own_load(a).wait()
        if levels[a] == 0:
            core_copy(a).wait_recv()
            add(bufs[a][0], 0, bufs[a][1], bufs[a][0].shape[0])
        if levels[a] < 2:
            for order in range(2):
                first_copy(a, order).start()

    def second(a):
        for order in range(2):
            if levels[a] < 2:
                first_copy(a, order).wait_recv()
                own = owners(a, order)
                add(bufs[a][0].at[own], kept(a, order), bufs[a][2].at[own], ring // 2 * sizes(a)[0])
            second_copy(a, order).start()

    def to_owner(a):
        for order in range(2):
            second_copy(a, order).wait_recv()
            own = owners(a, order)
            at = kept(a, order) + bits[order][1] * sizes(a)[1]
            add(bufs[a][0].at[own], at, bufs[a][3].at[own], ring // 2 * sizes(a)[0])
        for k in range(1, ring):
            owner_copy(a, k).start()

    def add_up(a):
        for k in range(1, ring):
            owner_copy(a, k).wait_recv()
        mine = own_quarter(a, z)
        for s in range(sizes(a)[0]):
            terms = [mine[s]] + [bufs[a][4][k, s] for k in range(ring - 1)]
            bufs[a][5][0, s] = sum((t.astype(F32) for t in terms[1:]), terms[0].astype(F32)).astype(BF16)
        for t in range(teams):
            team_copy(a, t).start()
            team_copy(a, t).wait()
            bufs[a][5][0] = (bufs[a][5][0].astype(F32) + bufs[a][5][1 + t].astype(F32)).astype(BF16)

    def total(a):
        if levels[a] == 3:
            own_load(a).wait()
        else:
            add_up(a)
        keep_own(a).start()
        for j in range(1, 5):
            spread(a, j).start()

    def hand_on(a):
        add_up(a)
        out = pltpu.make_async_copy(bufs[a][5].at[0], sums[a], load.at[count + a])
        out.start()
        sent(a)
        out.wait()

    def share(a):
        for j in range(1, 4):
            spread_here(a, j)
            spread(a, 4 + j).start()

    def sent(a):
        if levels[a] == 0:
            core_copy(a).wait_send()
        for order in range(2):
            if levels[a] < 2:
                first_copy(a, order).wait_send()
            second_copy(a, order).wait_send()
        for k in range(1, ring):
            owner_copy(a, k).wait_send()

    def close(a):
        for j in range(4, 8):
            spread_here(a, j)
        if levels[a] < 3:
            sent(a)
        for j in range(1, 8):
            spread(a, j).wait_send()
        keep_own(a).wait()

    return SimpleNamespace(
        enter=enter, first=first, second=second, to_owner=to_owner, total=total, hand_on=hand_on, share=share, close=close
    )


def reducer_scratch(levels, shapes, teams, ring):
    scratch = []
    for level, (strips, rows, columns) in zip(levels, shapes):
        blocks, span = ring * strips, columns // 2
        none = (1, 16, 128)
        scratch += [
            pltpu.VMEM(none if level == 3 else (blocks, rows // 2 if level == 2 else rows, span), BF16),
            pltpu.VMEM((blocks, rows, span) if level == 0 else none, BF16),
            pltpu.VMEM((blocks, rows // 2, span) if level < 2 else none, BF16),
            pltpu.VMEM((blocks, rows // 4, span) if level < 3 else none, BF16),
            pltpu.VMEM((ring - 1, strips, rows // 4, span) if level < 3 else (1, *none), BF16),
            pltpu.VMEM((1 + teams, strips, rows // 4, span), BF16),
        ]
    copies = 4 + ring + 7 + teams
    dma = pltpu.SemaphoreType.DMA
    return scratch + [dma((len(levels), copies)), dma((len(levels), copies)), dma((2 * len(levels),))]


def reduce_kernel(
    teams, up_ref, down_ref, qkv_ref, small_att, small_mlp, small_up, back_ref, o_last, o_ref, g_ref, weights,
    up_sum, down_sum, qkv_sum, out_sum, norm_out, bias_out, attend_out, ret_back, *refs,
):
    ring = lax.axis_size("ctx")
    d, z = lax.axis_index("dp"), lax.axis_index("ctx")
    core, x, y, core_id, x_id, y_id = plane(d)
    bufs = [refs[6 * a : 6 * a + 6] for a in range(4)]
    send, recv, load, o_in, wo_ref, dwo_ref, small_acc, small_in = refs[24:32]
    s_send, s_recv, r_send, r_recv, r_local = refs[32:]
    batch, piece, width = ret_back.shape
    lanes = o_last.shape[1]
    up, down, qkv, out = range(4)
    ins, sums = (up_ref, down_ref, qkv_ref, dwo_ref), (up_sum, down_sum, qkv_sum, out_sum)
    do = reducer(teams, LEVELS, ins, sums, bufs, send, recv, load)

    pairs = ((o_last, o_in), (back_ref, ret_back))
    mine = z - core

    def returned(which, i, to):
        source, target = pairs[which]
        return source.at[pl.ds(pl.multiple_of(to * piece, 16), piece), :], target.at[i]

    def start_returns(which):
        for i in range(batch):
            @pl.when(mine == i)
            def _(i=i):
                for k in range(1, ring):
                    to = (z + k) % ring
                    src, dst = returned(which, i, to)
                    remote(src, dst, r_send.at[which, k], r_recv.at[which, i], d, to).start()
                src, dst = returned(which, i, z)
                pltpu.make_async_copy(src, dst, r_local.at[which]).start()

    def wait_returns(which):
        for i in range(batch):
            src, dst = returned(which, i, z)

            @pl.when(mine == i)
            def _(src=src, dst=dst):
                pltpu.make_async_copy(src, dst, r_local.at[which]).wait()

            @pl.when(mine != i)
            def _(i=i, src=src, dst=dst):
                remote(src, dst, r_send.at[which, 0], r_recv.at[which, i], core_id, z).wait_recv()

    def close_returns(which):
        for i in range(batch):
            @pl.when(mine == i)
            def _(i=i):
                for k in range(1, ring):
                    to = (z + k) % ring
                    remote(*returned(which, i, to), r_send.at[which, k], r_recv.at[which, i], d, to).wait_send()

    steps = [core_id, x_id, y_id] + [team_id(d, t) for t in range(teams)]

    def small_copy(n):
        return remote(small_acc, small_in.at[n], s_send.at[n], s_recv.at[n], steps[n], z)

    def small_owner(k):
        n = len(steps) + k - 1
        return remote(small_acc, small_in.at[n], s_send.at[n], s_recv.at[n], d, (z + k) % ring)

    def small_close(n):
        small_copy(n).wait()
        small_acc[...] += small_in[n]
        if n + 1 < len(steps):
            small_copy(n + 1).start()
        else:
            for k in range(1, ring):
                small_owner(k).start()

    columns = weights.shape[1] - width
    wo_load = pltpu.make_async_copy(weights.at[:, pl.ds(columns, width)], wo_ref, r_local.at[2])
    wo_load.start()
    small_acc[0:8, :] = small_att[...]
    small_acc[8:16, :] = small_mlp[...]
    for n in range(small_up.shape[1] // width):
        small_acc[16 + n : 17 + n, :] = small_up[0:1, n * width : (n + 1) * width]
    rest = 16 + small_up.shape[1] // width
    small_acc[rest:, :] = jnp.zeros((small_acc.shape[0] - rest, width), F32)
    greet(teams)
    do.enter(qkv)
    start_returns(0)
    do.enter(up)
    do.enter(down)
    small_copy(0).start()
    do.total(up)
    do.total(down)
    do.first(qkv)
    small_close(0)
    do.share(up)
    do.share(down)

    wo_load.wait()
    wait_returns(0)
    start_returns(1)
    split = o_ref.shape[1]
    for i in range(batch):
        at = pl.ds(i * piece, piece)
        attend_out[at, :] = dot(o_ref[at, :], wo_ref[:split, :]) + dot(o_in[i], wo_ref[split:, :])
    late = jnp.concatenate([o_in[i] for i in range(batch)], axis=0)
    dwo = jnp.concatenate([dot(o_ref[...], g_ref[...], TN), dot(late, g_ref[...], TN)], axis=0).astype(BF16)
    for r in range(ring):
        dwo_ref[r] = dwo[r * (width // ring) : (r + 1) * (width // ring), :]
    do.enter(out)
    do.second(qkv)
    do.first(out)
    small_close(1)
    do.to_owner(qkv)
    do.second(out)
    for n in range(2, len(steps)):
        small_close(n)
    do.total(qkv)
    do.to_owner(out)
    do.share(qkv)
    do.total(out)
    for k in range(1, ring):
        small_owner(k).wait()
    total = small_acc[...]
    for k in range(ring - 1):
        total += small_in[len(steps) + k]
    norm = jnp.concatenate([total[0:2], total[8:10], jnp.zeros((4, width), F32)], axis=0)
    norm_out[...] = pltpu.roll(norm, (ring - z) % ring * (width // ring), 1)
    ups = [total[16 + n : 17 + n] for n in range(small_up.shape[1] // width)]
    bias = jnp.concatenate([total[2:3], total[10:11], *ups, total[10:11]], axis=1)
    entries = bias.shape[1]
    bias = pltpu.roll(jnp.broadcast_to(bias, (8, entries)), (ring - z) % ring * (entries // ring), 1)
    bias_out[...] = bias[:, : bias_out.shape[1]]
    do.share(out)
    for a in range(4):
        do.close(a)
    wait_returns(1)
    close_returns(0)
    close_returns(1)


def reduce_all(up, down, qkv, small_att, small_mlp, small_up, back, o_last, o_first, g, weights, batch):
    ring, groups = lax.axis_size("ctx"), lax.axis_size("dp")
    teams = (groups // 8).bit_length() - 1
    width = g.shape[1]
    piece = g.shape[0] // batch
    shapes = [(n, 4 * rows, 2 * span) for n, rows, span in (up.shape, down.shape)]
    shapes += [(1, width // ring, qkv.shape[1]), (1, width // ring, width)]
    dma = pltpu.SemaphoreType.DMA
    anywhere = pl.BlockSpec(memory_space=pl.ANY)
    vmem = pl.BlockSpec(memory_space=pltpu.VMEM)
    rounds = 3 + teams + ring - 1
    small = (16 + -(-small_up.shape[1] // width // 8) * 8, width)
    share = (3 * width + small_up.shape[1]) // ring
    scratch = reducer_scratch(LEVELS, shapes, teams, ring)
    scratch += [
        pltpu.VMEM((batch, piece, o_last.shape[1]), BF16), pltpu.VMEM((width, width), BF16),
        pltpu.VMEM((ring, width // ring, width), BF16), pltpu.VMEM(small, F32), pltpu.VMEM((rounds, *small), F32),
        dma((rounds,)), dma((rounds,)), dma((2, ring)), dma((2, batch)), dma((3,)),
    ]
    return pl.pallas_call(
        functools.partial(reduce_kernel, teams),
        in_specs=[anywhere] * 3 + [vmem] * 3 + [anywhere, anywhere, vmem, vmem, anywhere],
        out_specs=[anywhere] * 4 + [vmem, vmem, vmem, anywhere],
        out_shape=[jax.ShapeDtypeStruct(shape, BF16) for shape in shapes]
        + [
            jax.ShapeDtypeStruct((8, width), F32), jax.ShapeDtypeStruct((8, share + -share % 128), F32),
            jax.ShapeDtypeStruct(g.shape, F32),
            jax.ShapeDtypeStruct((batch, piece, width), BF16),
        ],
        scratch_shapes=scratch,
        compiler_params=pltpu.CompilerParams(collective_id=1, has_side_effects=True, vmem_limit_bytes=56 * MIB),
        cost_estimate=pl.CostEstimate(flops=4 * width * width * g.shape[0], bytes_accessed=60 * MIB, transcendentals=0),
        name="reduce",
    )(
        up, down, qkv.reshape(ring, width // ring, -1), small_att, small_mlp, small_up, back, o_last,
        o_first.reshape(batch * piece, -1), g, weights,
    )


def attend_kernel(
    teams, order_ref, x_ref, stored_g_ref, norm_ref, bias_ref, cos_ref, low_ref, high_ref, wq_ref, wk_ref, wv_ref,
    wo_ref, up_ref, down_ref, h_ref, dqkv_all, small_ref, o_last, ret_o, up_sum, down_sum,
    g_ref, a_ref, at_ref, da_ref, q_ref, k_ref, v_ref, do_ref, o_ref, kt_ref, vt_ref, dqs_ref, dks_ref, dvs_ref,
    grad_ref, stored_o_ref, o_send, o_recv, o_local, grad_sem, *reduce_refs,
):
    step = pl.program_id(0)
    last = grad_ref.shape[0] - 1
    rows, width = x_ref.shape
    lanes = QUAD * HD
    tile = 256
    half = ROT // 2
    scale = 1.0 / math.sqrt(HD)
    blocks = rows // BLOCK
    ring = lax.axis_size("ctx")
    d, z = lax.axis_index("dp"), lax.axis_index("ctx")
    core_id = plane(d)[3]
    batch, piece = ret_o.shape[:2]
    mine = z - d % 2
    is_home = (mine >= 0) & (mine < batch)
    up, down = 0, 1
    bufs = (reduce_refs[:6], reduce_refs[6:12])
    do_sum = reducer(teams, MLP_LEVELS, (up_ref, down_ref), (up_sum, down_sum), bufs, *reduce_refs[12:])

    @pl.when(step == 0)
    def _():
        do_sum.enter(down)
        do_sum.enter(up)
        greet(teams)
        do_sum.first(down)
        do_sum.first(up)
        do_sum.second(up)

    def o_copy(quad, k, i):
        to = (z + k) % ring
        src = stored_o_ref.at[quad, pl.ds(pl.multiple_of(to * piece, 16), piece), :]
        dst = ret_o.at[i, :, pl.ds(pl.multiple_of(quad * lanes, 128), lanes)]
        if k == 0:
            return pltpu.make_async_copy(src, dst, o_local.at[quad])
        return remote(src, dst, o_send.at[quad, k], o_recv.at[quad, i], d, to)

    def grad_copy(quad, j):
        at = pl.ds(pl.multiple_of(j * width + quad * lanes, 128), lanes)
        return pltpu.make_async_copy(grad_ref.at[quad, j], dqkv_all.at[:, at], grad_sem.at[quad, j])


    def stored(ref, at):
        values = ref[pl.ds(at * BLOCK, BLOCK), :]
        return jnp.where(is_home, values, jnp.zeros_like(values))

    @pl.when(step == 0)
    def _():
        for j in range(blocks):
            place = order_ref[1, j]
            at = pl.ds(j * BLOCK, BLOCK)
            xh, _ = normalized(stored(x_ref, place).astype(F32))
            a = xh * norm_ref[1:2, :] + norm_ref[2:3, :]
            a_ref[at, :] = a.astype(BF16)
            at_ref[:, at] = a.T.astype(BF16)
            g_ref[at, :] = stored(stored_g_ref, place)
        da_ref[...] = jnp.zeros_like(da_ref)

    def table(ref, at):
        values = ref[at, :]
        return jnp.concatenate([values] * (lanes // values.shape[1]), axis=1)

    def turn(values, at):
        low = pltpu.roll(values, lanes - half, 1) * table(low_ref, at)
        high = pltpu.roll(values, half, 1) * table(high_ref, at)
        return values * table(cos_ref, at), low + high

    for t in range(rows // tile):
        at = pl.ds(t * tile, tile)
        a = a_ref[at, :]
        same, cross = turn(dot(a, wq_ref[...]) + bias_ref[0:1, :], at)
        q_ref[at, :] = ((same + cross).astype(BF16) * scale).astype(BF16)
        same, cross = turn(dot(a, wk_ref[...]), at)
        keys = same + cross
        k_ref[at, :] = keys.astype(BF16)
        kt_ref[:, at] = keys.T.astype(BF16)
        values = dot(a, wv_ref[...])
        v_ref[at, :] = values.astype(BF16)
        vt_ref[:, at] = values.T.astype(BF16)
        mixed_back = dot(g_ref[at, :], wo_ref[...], NT)
        do_ref[at, :] = mixed_back.astype(BF16)

    dks_ref[...] = jnp.zeros_like(dks_ref)
    dvs_ref[...] = jnp.zeros_like(dvs_ref)
    wide = 2 * HD
    head_of = lax.broadcasted_iota(jnp.int32, (BLOCK, wide), 1) // HD

    def stack(values):
        zero = jnp.zeros_like(values)
        return jnp.concatenate([jnp.where(head_of == e, values, zero) for e in range(2)], axis=0)

    def diagonal(values):
        return jnp.concatenate([values[e * HD : (e + 1) * HD, e * BLOCK : (e + 1) * BLOCK] for e in range(2)], axis=0)

    spot = lax.broadcasted_iota(jnp.int32, (BLOCK, 2 * BLOCK), 1) % BLOCK
    admitted = lax.broadcasted_iota(jnp.int32, (BLOCK, 2 * BLOCK), 0) <= spot

    def products_in(b, p):
        at, seen, own = pl.ds(b * BLOCK, BLOCK), pl.ds(0, (b + 1) * BLOCK), pl.ds(p * wide, wide)
        q, do = stack(q_ref[at, own]), stack(do_ref[at, own])
        return q, do, dot(k_ref[seen, own], q, NT), dot(v_ref[seen, own], do, NT)

    def softmax(b, scores, back):
        edge = jnp.where(admitted, scores[b * BLOCK :], -1e30)
        scores = edge if b == 0 else jnp.concatenate([scores[: b * BLOCK], edge], axis=0)
        top = jnp.max(scores, axis=0, keepdims=True)
        expo = jnp.exp(scores - top)
        probs = expo * (1.0 / jnp.sum(expo, axis=0, keepdims=True))
        share = jnp.sum(probs * back, axis=0, keepdims=True)
        return probs.astype(BF16), (probs * (back - share)).astype(BF16)

    def products_out(b, p, q, do, low, back):
        at, seen, own = pl.ds(b * BLOCK, BLOCK), pl.ds(0, (b + 1) * BLOCK), pl.ds(p * wide, wide)
        mixed = diagonal(dot(vt_ref[own, seen], low))
        o_ref[at, own] = mixed.T.astype(BF16)
        dqs_ref[at, own] = diagonal(dot(kt_ref[own, seen], back)).T * scale
        dks_ref[seen, own] += dot(back, q)
        dvs_ref[seen, own] += dot(low, do)

    units = [(b, p) for b in range(rows // BLOCK) for p in range(lanes // wide)]
    ready = products_in(*units[0])
    done = None
    for n, (b, p) in enumerate(units):
        q, do, scores, back = ready
        if n + 1 < len(units):
            ready = products_in(*units[n + 1])
        low, back = softmax(b, scores, back)
        if done is not None:
            products_out(*done)
        done = (b, p, q, do, low, back)
    products_out(*done)

    total = jnp.zeros((1, lanes), F32)
    for t in range(rows // tile):
        at = pl.ds(t * tile, tile)
        same, cross = turn(dqs_ref[at, :], at)
        dq = (same - cross).astype(BF16)
        same, cross = turn(dks_ref[at, :], at)
        dk = (same - cross).astype(BF16)
        dv = dvs_ref[at, :].astype(BF16)
        total += jnp.sum(dq.astype(F32), axis=0, keepdims=True)
        q_ref[at, :] = dq
        k_ref[at, :] = dk
        v_ref[at, :] = dv
        da_ref[at, :] += dot(dq, wq_ref[...], NT) + dot(dk, wk_ref[...], NT) + dot(dv, wv_ref[...], NT)
    small_ref[2:3, pl.ds(pl.multiple_of(step * lanes, 128), lanes)] = total
    for j, ref in enumerate((q_ref, k_ref, v_ref)):
        grad_ref[step, j] = dot(at_ref[...], ref[...]).astype(BF16)
        grad_copy(step, j).start()
    for s in range(blocks):
        stored_o_ref[step, s * BLOCK : (s + 1) * BLOCK, :] = o_ref[pl.ds(order_ref[0, s] * BLOCK, BLOCK), :]

    for i in range(batch):
        @pl.when((mine == i) & (step < last))
        def _(i=i):
            for k in range(ring):
                o_copy(step, k, i).start()

    @pl.when(step == 0)
    def _():
        do_sum.second(down)
        do_sum.to_owner(up)

    @pl.when(step == 1)
    def _():
        do_sum.to_owner(down)

    @pl.when(step == last)
    def _():
        gain = jnp.zeros((1, width), F32)
        shift = jnp.zeros((1, width), F32)
        for s in range(blocks):
            at = pl.ds(s * BLOCK, BLOCK)
            sorted_at = pl.ds(order_ref[0, s] * BLOCK, BLOCK)
            xh, _ = normalized(stored(x_ref, s).astype(F32))
            da = da_ref[sorted_at, :]
            gain += jnp.sum(da * xh, axis=0, keepdims=True)
            shift += jnp.sum(da, axis=0, keepdims=True)
            h_ref[at, :] = (da * norm_ref[1:2, :]).astype(BF16)
        small_ref[0:1, :] = gain
        small_ref[1:2, :] = shift
        small_ref[3:8, :] = jnp.zeros((5, width), F32)
        out = pltpu.make_async_copy(stored_o_ref.at[last], o_last, o_local.at[last])
        out.start()
        do_sum.hand_on(up)
        do_sum.hand_on(down)
        for quad in range(last):
            for i in range(batch):
                @pl.when(mine != i)
                def _(quad=quad, i=i):
                    ref = ret_o.at[i, :, pl.ds(quad * lanes, lanes)]
                    remote(ref, ref, o_send.at[quad, 0], o_recv.at[quad, i], core_id, z).wait_recv()

                @pl.when(mine == i)
                def _(quad=quad, i=i):
                    o_copy(quad, 0, i).wait()
                    for k in range(1, ring):
                        o_copy(quad, k, i).wait_send()
        for quad in range(last + 1):
            for j in range(3):
                grad_copy(quad, j).wait()
        out.wait()


def attend(order, x, g, norms, bias_q, tables, weights, up, down, batch):
    ring, groups_dp = lax.axis_size("ctx"), lax.axis_size("dp")
    teams = (groups_dp // 8).bit_length() - 1
    shapes = ((1, 2 * up.shape[1], 2 * up.shape[2]), (down.shape[1], down.shape[2], 2 * down.shape[3]))
    down = down.reshape(-1, *down.shape[2:])
    rows, width = x.shape
    lanes = QUAD * HD
    groups = width // lanes
    anywhere = pl.BlockSpec(memory_space=pl.ANY)
    whole = lambda shape: pl.BlockSpec(shape, lambda i: (0,) * len(shape))
    once = lambda shape: pl.BlockSpec(shape, lambda i: (0,) * len(shape), pipeline_mode=pl.Buffered(1))
    dma = pltpu.SemaphoreType.DMA
    slices = [(n, r // 4, c // 2) for n, r, c in shapes]
    return pl.pallas_call(
        functools.partial(attend_kernel, teams),
        grid=(groups,),
        in_specs=[
            pl.BlockSpec(memory_space=pltpu.SMEM),
            once((rows, width)),
            once((rows, width)),
            once(norms.shape),
            pl.BlockSpec((8, lanes), lambda i: (0, i)),
            once(tables[0].shape),
            once(tables[0].shape),
            once(tables[0].shape),
            pl.BlockSpec((width, lanes), lambda i: (0, i)),
            pl.BlockSpec((width, lanes), lambda i: (0, groups + i)),
            pl.BlockSpec((width, lanes), lambda i: (0, 2 * groups + i)),
            pl.BlockSpec((lanes, width), lambda i: (i, 3)),
            anywhere,
            anywhere,
        ],
        out_specs=[once((rows, width)), anywhere, once((8, width))] + [anywhere] * 4,
        out_shape=[
            jax.ShapeDtypeStruct((rows, width), BF16),
            jax.ShapeDtypeStruct((width, 3 * width), BF16),
            jax.ShapeDtypeStruct((8, width), F32),
            jax.ShapeDtypeStruct((rows, lanes), BF16),
            jax.ShapeDtypeStruct((batch, rows // ring, width - lanes), BF16),
        ]
        + [jax.ShapeDtypeStruct(shape, BF16) for shape in slices],
        scratch_shapes=[
            pltpu.VMEM((rows, width), BF16),
            pltpu.VMEM((rows, width), BF16),
            pltpu.VMEM((width, rows), BF16),
            pltpu.VMEM((rows, width), F32),
        ]
        + [pltpu.VMEM((rows, lanes), BF16)] * 5
        + [pltpu.VMEM((lanes, rows), BF16)] * 2
        + [pltpu.VMEM((rows, lanes), F32)] * 3
        + [
            pltpu.VMEM((groups, 3, width, lanes), BF16), pltpu.VMEM((groups, rows, lanes), BF16),
            dma((groups, ring)), dma((groups, batch)), dma((groups,)), dma((groups, 3)),
        ]
        + reducer_scratch(MLP_LEVELS, shapes, teams, ring),
        compiler_params=pltpu.CompilerParams(
            collective_id=2, has_side_effects=True, vmem_limit_bytes=60 * MIB
        ),
        cost_estimate=pl.CostEstimate(
            flops=24 * rows * width * width + 8 * rows * rows * width,
            bytes_accessed=16 * width * width + 8 * rows * width,
            transcendentals=HEADS * rows * rows // 2,
        ),
        name="attend",
    )(order, x, g, norms, bias_q, *tables, weights, weights, weights, weights, up, down)


def rotary_tables(length):
    half = ROT // 2
    frequency = ROPE_BASE ** (-(np.arange(half) * 2.0 / ROT))
    angle = np.arange(length)[:, None] * frequency[None, :]
    cosine, sine = np.cos(angle), np.sin(angle)
    rest = np.zeros((length, HD - ROT))
    none = np.zeros_like(sine)
    cos_full = np.concatenate([cosine, cosine, rest + 1.0], axis=1)
    low = np.concatenate([-sine, none, rest], axis=1)
    high = np.concatenate([none, sine, rest], axis=1)
    return tuple(jnp.asarray(np.tile(t, (1, 2)).astype(np.float32)) for t in (cos_full, low, high))


def adamw(weight, grad, first, second, rate, decay):
    first_new = BETA_ONE * first + (1.0 - BETA_ONE) * grad
    second_new = BETA_TWO * second + (1.0 - BETA_TWO) * grad * grad
    first_hat = first_new / (1.0 - BETA_ONE**STEP)
    second_hat = second_new / (1.0 - BETA_TWO**STEP)
    weight_new = weight - rate * (first_hat / (jnp.sqrt(second_hat) + EPS_ADAM) + decay * weight)
    return (first_new, second_new, weight_new)


RATES = (0.1, 0.6, 0.1, 0.05)


def finish_kernel(*refs):
    x_ref, g_ref, attend_ref, feed_ref, h_ref, back_ref, bias_ref, norm_grad = refs[:8]
    norm, norm_first, norm_second = refs[8:11]
    inputs, outputs = refs[11:27], refs[27:]
    layer_out, input_grad = outputs[:2]
    for n, rate in enumerate(RATES):
        weight, grad, first, second = (ref[...] for ref in inputs[4 * n : 4 * n + 4])
        new = adamw(weight, grad.astype(F32), first, second, rate, DECAY)
        for ref, value in zip(outputs[2 + 3 * n : 5 + 3 * n], new):
            ref[...] = value
    width = x_ref.shape[1]
    bias = bias_ref[0:1, width : 2 * width] + bias_ref[0:1, bias_ref.shape[1] - width :]
    rows = x_ref[...].astype(F32)
    layer_out[...] = (rows + attend_ref[...] + feed_ref[...] + bias).astype(BF16)
    xh, scale = normalized(rows)
    h = back_ref[...].astype(F32) + h_ref[...]
    inner = jnp.mean(h * xh, axis=-1, keepdims=True)
    input_grad[...] = g_ref[...].astype(F32) + scale * (h - jnp.mean(h, axis=-1, keepdims=True) - xh * inner)

    @pl.when(pl.program_id(0) == 0)
    def _():
        grad = norm_grad[0:4, : norm.shape[1]]
        first, second, new = adamw(norm[...], grad, norm_first[...], norm_second[...], 0.6, 0.0)
        outputs[14][...] = first
        outputs[15][...] = second[0:2]
        outputs[16][...] = second[2:4]
        outputs[17][...] = new


def finish(rows, biases, norm_grad, norm_args, weights):
    steps = 4
    whole = lambda v: pl.BlockSpec(v.shape, lambda i: (0,) * len(v.shape))
    part = lambda v: pl.BlockSpec((v.shape[0] // steps, v.shape[1]), lambda i: (i, 0))
    like = lambda v, dtype: jax.ShapeDtypeStruct(v.shape, dtype)
    count, width = rows[0].shape
    args = [*rows, biases, norm_grad, *norm_args] + [v for group in weights for v in group]
    specs = [part(v) for v in rows] + [whole(v) for v in (biases, norm_grad, *norm_args)]
    specs += [part(v) for group in weights for v in group]
    outs = [like(rows[0], BF16), like(rows[0], F32)] + [like(group[0], F32) for group in weights for _ in range(3)]
    out_specs = [part(v) for v in outs]
    own = norm_args[0].shape[1]
    norm_outs = [jax.ShapeDtypeStruct((n, own), F32) for n in (4, 2, 2, 4)]
    return pl.pallas_call(
        finish_kernel,
        grid=(steps,),
        in_specs=specs,
        out_specs=out_specs + [whole(v) for v in norm_outs],
        out_shape=outs + norm_outs,
        compiler_params=pltpu.CompilerParams(vmem_limit_bytes=56 * MIB),
        cost_estimate=pl.CostEstimate(flops=0, bytes_accessed=64 * MIB, transcendentals=0),
        name="finish",
    )(*args)


def shards(
    tokens, out_grad, block_order, qkv_weight, out_weight, up_weight, down_weight, norm_params, bias_params,
    qkv_first, qkv_second, out_first, out_second, up_first, up_second, down_first, down_second,
    norm_first, norm_second, bias_first, bias_second,
):
    groups, ring = lax.axis_size("dp"), lax.axis_size("ctx")
    group, rank = lax.axis_index("dp"), lax.axis_index("ctx")
    batch, piece, width = tokens.shape
    length = piece * ring
    count = batch * piece
    ff = up_weight.shape[1]

    share = bias_params.shape[0]
    lanes = share + -share % 128
    small = jnp.concatenate([
        jnp.pad(bias_params[None, :], ((0, 0), (0, lanes - share))),
        jnp.pad(norm_params, ((0, 3), (0, lanes - norm_params.shape[1]))),
    ])
    x_rows, g_rows = tokens.reshape(count, width), out_grad.reshape(count, width)
    att_copy, biases, norms, home_x, home_g, feed_out, h_feed, dup, ddown, dbias_up, small_feed = gather_feed(
        up_weight, down_weight, qkv_weight, out_weight, small, x_rows, g_rows, piece, ring * share
    )

    odd = group % 2

    order = block_order[jnp.clip(rank - odd, 0, batch - 1)]
    spots = jnp.arange(order.shape[0])
    order = jnp.stack([order, jnp.sum(jnp.where(order[None, :] == spots[:, None], spots[None, :], 0), axis=1)])

    h_attend, dqkv, small_attend, o_last, o_first, up_slice, down_slice = attend(
        order, home_x, home_g, norms, biases, rotary_tables(length), att_copy, dup, ddown, batch
    )
    *owned, norm_grad, bias_grad, attend_out, ret_back = reduce_all(
        up_slice, down_slice, dqkv, small_attend, small_feed, dbias_up, h_attend, o_last, o_first, g_rows, att_copy, batch
    )
    up_grad, down_grad, qkv_grad, out_grads = (
        g.reshape(w.shape) for g, w in zip(owned, (up_weight, down_weight, qkv_weight, out_weight))
    )
    layer_out, input_grad, *new, norm_a, norm_b, norm_c, norm_d = finish(
        (x_rows, g_rows, attend_out, feed_out, h_feed, ret_back.reshape(count, width)),
        biases,
        norm_grad,
        (norm_params, norm_first, norm_second),
        (
            (qkv_weight, qkv_grad, qkv_first, qkv_second),
            (out_weight, out_grads, out_first, out_second),
            (up_weight, up_grad, up_first, up_second),
            (down_weight, down_grad, down_first, down_second),
        ),
    )
    bias_new = adamw(bias_params, bias_grad[0, :share], bias_first, bias_second, 0.6, 0.0)
    return (
        layer_out.reshape(tokens.shape), input_grad.reshape(tokens.shape), *new,
        norm_a, norm_b, norm_c, norm_d, *bias_new,
    )


def solution(mesh):
    rows, columns, token = P("ctx", None), P(None, "ctx"), P("dp", "ctx", None)
    in_specs = (token, token, P("dp", None)) + (rows,) * 4 + (columns, P("ctx")) + (rows,) * 8
    in_specs += (columns, columns, P("ctx"), P("ctx"))
    out_specs = (token, token) + (rows,) * 12 + (columns,) * 4 + (P("ctx"),) * 3
    return jax.shard_map(shards, mesh=mesh, in_specs=in_specs, out_specs=out_specs, check_vma=False)
```

```python
import functools
import math
from types import SimpleNamespace

import jax
import jax.numpy as jnp
import numpy as np
from jax import lax
from jax.experimental import pallas as pl
from jax.experimental.pallas import tpu as pltpu
from jax.sharding import PartitionSpec as P

HEADS = 12
HD = 64
STEP = 10
ROT = 16
BLOCK = 128
QUAD = 4
MLP_LEVELS = (2, 1)
LEVELS = (3, 3, 0, 0)

EPS_NORM = 1e-05
BETA_ONE = 0.9
BETA_TWO = 0.95
EPS_ADAM = 1e-08
DECAY = 0.01
ROPE_BASE = 10000.0
F32 = jnp.float32
BF16 = jnp.bfloat16
MIB = 1024 * 1024


def dot(left, right, dims=((1,), (0,))):
    return lax.dot_general(left, right, (dims, ((), ())), preferred_element_type=F32)


NN = ((1,), (0,))
NT = ((1,), (1,))
TN = ((0,), (0,))


def normalized(values):
    mean = jnp.mean(values, axis=-1, keepdims=True)
    centred = values - mean
    variance = jnp.mean(centred * centred, axis=-1, keepdims=True)
    scale = lax.rsqrt(variance + EPS_NORM)
    return centred * scale, scale


MESH = pl.DeviceIdType.MESH


def plane(d):
    core, x, y = d % 2, d // 2 % 2, d // 4 % 2
    return core, x, y, d + 1 - 2 * core, d + 2 - 4 * x, d + 4 - 8 * y


def gather_kernel(
    up, down, qkv, out, small, tokens, cotangents,
    att_all, small_all, norm_all, home_x, home_g, out_ref, h_ref, up_part, down_part, dbias_ref, sums_ref,
    up_all, down_all, att_own, up_wide, down_wide, att_wide, small_in, x_ref, g_ref, m_ref, mt_ref, hid_ref, dup_in_ref,
    dup_ref, up_core, up_first, ddown_ref, down_core,
    z_send, z_recv, p_send, p_recv, s_send, s_recv, t_send, t_recv, local, out_sem, c_send, c_recv,
):
    ring = lax.axis_size("ctx")
    d, z = lax.axis_index("dp"), lax.axis_index("ctx")
    core, x, y, core_id, x_id, y_id = plane(d)
    own = x + 2 * y
    own_x, own_y, far = own + 1 - 2 * x, own + 2 - 4 * y, 3 - own
    count, width = tokens.shape
    piece = home_x.shape[0] // ring
    batch = count // piece
    arrays = ((up_wide, up_all, False), (down_wide, down_all, True), (att_own, att_all, False))

    def slot(a, base, place, half=None):
        source, whole, tall = arrays[a]
        ref = source if base is None else whole
        rows, columns = source.shape
        at = 0 if base is None else base * rows
        height, span = rows // 4, columns // 2
        at = at + place * height
        column = core * span
        if half is not None:
            if tall:
                height = height // 2
                at = at + half * height
            else:
                span = span // 2
                column = column + half * span
        return ref.at[pl.ds(pl.multiple_of(at, 16), height), pl.ds(pl.multiple_of(column, 128), span)]

    def other_slot(a, base, place):
        source, whole, tall = arrays[a]
        rows, columns = source.shape
        at = pl.multiple_of(base * rows + place * (rows // 4), 16)
        column = pl.multiple_of((1 - core) * (columns // 2), 128)
        return whole.at[pl.ds(at, rows // 4), pl.ds(column, columns // 2)]

    def remote(src, dst, send, recv, dp, ctx):
        return pltpu.make_async_remote_copy(
            src_ref=src, dst_ref=dst, send_sem=send, recv_sem=recv, device_id=(dp, ctx), device_id_type=MESH
        )

    columns = qkv.shape[1]
    wide_loads = [
        [pltpu.make_async_copy(up, up_wide, local.at[0])],
        [pltpu.make_async_copy(down, down_wide, local.at[1])],
        [
            pltpu.make_async_copy(qkv, att_wide.at[:, pl.ds(0, columns)], local.at[2]),
            pltpu.make_async_copy(out, att_wide.at[:, pl.ds(columns, out.shape[1])], local.at[8]),
        ],
    ]
    for loads in wide_loads:
        for copy in loads:
            copy.start()

    def cast_own(a):
        for copy in wide_loads[a]:
            copy.wait()
        wide, target = ((up_wide, up_all), (down_wide, down_all), (att_wide, att_own))[a]
        rows = wide.shape[0]
        tile = 64
        base = 0 if a == 2 else z * rows

        def body(t, _):
            value = wide[pl.ds(pl.multiple_of(t * tile, 16), tile), :].astype(BF16)
            target[pl.ds(pl.multiple_of(base + t * tile, 16), tile), :] = value
            return 0

        lax.fori_loop(0, rows // tile, body, 0)

    barrier = pltpu.get_barrier_semaphore()
    for k in range(1, ring):
        pl.semaphore_signal(barrier, inc=1, device_id=(d, (z + k) % ring), device_id_type=MESH)
    for other in (core_id, x_id, y_id):
        pl.semaphore_signal(barrier, inc=1, device_id=(other, z), device_id_type=MESH)
    cast_own(0)
    pl.semaphore_wait(barrier, ring + 2)

    def hop(a, way, h):
        shard = z - h if way == 0 else z + h
        target = z + 1 if way == 0 else z - 1
        src = slot(a, None, own) if h == 0 and a == 2 else slot(a, shard, own)
        return remote(src, slot(a, shard, own), z_send.at[a, way, h], z_recv.at[a, way, h], d, target)

    def can_send(way, h):
        shard = z - h if way == 0 else z + h
        target = z + 1 if way == 0 else z - 1
        return (shard >= 0) & (shard < ring) & (target >= 0) & (target < ring)

    def in_range(way, h):
        shard = z - h if way == 0 else z + h
        return (shard >= 0) & (shard < ring)

    def cast(a, shard, j):
        send, recv = p_send.at[a, shard, j], p_recv.at[a, shard, j]
        if j == 0:
            ref = slot(a, shard, own)
            return remote(ref, ref, send, recv, x_id, z)
        if j == 1:
            ref = slot(a, shard, own)
            return remote(ref, ref, send, recv, y_id, z)
        if j == 2:
            ref = slot(a, shard, own_x, 0)
            return remote(ref, ref, send, recv, y_id, z)
        if j == 3:
            ref = slot(a, shard, own_y, 1)
            return remote(ref, ref, send, recv, x_id, z)
        ref = slot(a, shard, (own, own_x, own_y, far)[j - 4])
        return remote(ref, ref, send, recv, core_id, z)

    def arrived(a, shard, j):
        send, recv = p_send.at[a, shard, j], p_recv.at[a, shard, j]
        ref = {0: lambda: slot(a, shard, own_x), 1: lambda: slot(a, shard, own_y),
               2: lambda: slot(a, shard, far, 0), 3: lambda: slot(a, shard, far, 1)}.get(
            j, lambda: other_slot(a, shard, (own, own_x, own_y, far)[j - 4]))()
        remote(ref, ref, send, recv, core_id, z).wait_recv()

    def start_hops(a):
        for way in range(2):
            @pl.when(can_send(way, 0))
            def _(way=way):
                hop(a, way, 0).start()

    def small_copy(k):
        return remote(small, small_in.at[z], s_send.at[k], s_recv.at[k], d, (z + k) % ring)

    def stage_a(a, h):
        for way in range(2):
            @pl.when(in_range(way, h))
            def _(way=way):
                shard = z - h if way == 0 else z + h
                ref = slot(a, shard, own)
                remote(ref, ref, z_send.at[a, way, h - 1], z_recv.at[a, way, h - 1], core_id, z).wait_recv()

                @pl.when(can_send(way, h))
                def _():
                    hop(a, way, h).start()

                cast(a, shard, 0).start()
                cast(a, shard, 1).start()
                cast(a, shard, 4).start()

    def stage_b(a, h):
        for way in range(2):
            @pl.when(in_range(way, h))
            def _(way=way):
                shard = z - h if way == 0 else z + h
                arrived(a, shard, 0)
                cast(a, shard, 2).start()
                cast(a, shard, 5).start()
                arrived(a, shard, 1)
                cast(a, shard, 3).start()
                cast(a, shard, 6).start()

    def stage_c(a, h):
        for way in range(2):
            @pl.when(in_range(way, h))
            def _(way=way):
                shard = z - h if way == 0 else z + h
                arrived(a, shard, 2)
                arrived(a, shard, 3)
                cast(a, shard, 7).start()

    def stage_d(a, h):
        for way in range(2):
            @pl.when(in_range(way, h))
            def _(way=way):
                shard = z - h if way == 0 else z + h
                for j in range(4, 8):
                    arrived(a, shard, j)

    pairs = ((tokens, home_x), (cotangents, home_g))

    def move(which, i):
        source, whole = pairs[which]
        src = source.at[pl.ds(i * piece, piece), :]
        dst = whole.at[pl.ds(pl.multiple_of(z * piece, 16), piece), :]
        return src, dst, i + core

    def start_moves(which):
        for i in range(batch):
            src, dst, target = move(which, i)

            @pl.when(target != z)
            def _(src=src, dst=dst, target=target, i=i):
                remote(src, dst, t_send.at[which, i], t_recv.at[which, z], d, target).start()

            @pl.when(target == z)
            def _(src=src, dst=dst):
                pltpu.make_async_copy(src, dst, local.at[6 + which]).start()

    own_rows = pl.ds(pl.multiple_of(z * att_own.shape[0], 16), att_own.shape[0])
    own_att = pltpu.make_async_copy(att_own, att_all.at[own_rows, :], local.at[9])
    x_load = pltpu.make_async_copy(tokens, x_ref, local.at[3])
    g_load = pltpu.make_async_copy(cotangents, g_ref, local.at[4])
    own_small = pltpu.make_async_copy(small, small_in.at[z], local.at[5])

    start_hops(0)
    cast_own(1)
    start_hops(1)
    cast_own(2)
    start_hops(2)
    for k in range(1, ring):
        small_copy(k).start()
    for copy in (own_att, x_load, g_load, own_small):
        copy.start()
    hops = range(1, ring)
    work = [(a, h) for a in range(2) for h in hops]
    for n in range(len(work) + 2):
        if n < len(work):
            stage_a(*work[n])
        if n == len(work) - 1:
            start_moves(0)
        if 1 <= n <= len(work):
            stage_b(*work[n - 1])
        if n >= 2:
            stage_c(*work[n - 2])
    start_moves(1)
    stage_a(2, 1)

    own_small.wait()
    for k in range(1, ring):
        ref = small_in.at[(z + ring - k) % ring]
        remote(ref, ref, s_send.at[k], s_recv.at[k], core_id, z).wait_recv()
    x_load.wait()
    g_load.wait()
    entries = small_all.shape[1]
    biases = jnp.zeros((8, entries), F32)
    norms = jnp.zeros((8, width), F32)
    for r in range(ring):
        block = small_in[r].astype(BF16).astype(F32)
        full = jnp.concatenate([block, jnp.zeros((8, entries - block.shape[1]), F32)], axis=1)
        biases += pltpu.roll(full, r * (entries // ring), 1) if r else full
        norms += pltpu.roll(block[:, :width], r * (width // ring), 1) if r else block[:, :width]
    small_all[...] = biases
    norm_all[...] = norms
    ff = up_all.shape[1]
    gain_2, shift_2 = norm_all[3:4, :], norm_all[4:5, :]
    tile = 256
    tiles = count // tile
    for t in range(tiles):
        at = pl.ds(t * tile, tile)
        xh, _ = normalized(x_ref[at, :].astype(F32))
        m = xh * gain_2 + shift_2
        m_ref[at, :] = m.astype(BF16)
        mt_ref[:, at] = m.T.astype(BF16)
        out_ref[at, :] = jnp.zeros((tile, width), F32)
        h_ref[at, :] = jnp.zeros((tile, width), F32)
    for h in hops:
        stage_d(0, h)
        stage_d(1, h)

    strip = dup_ref.shape[3] // ring
    steps = ff // (ring * strip)
    half = ring // 2
    big, by_core = (dup_ref, ddown_ref), (up_core, down_core)
    bits, ids = ((x, y), (y, x)), ((x_id, y_id), (y_id, x_id))

    def sizes(a):
        return by_core[a].shape[2], by_core[a].shape[3]

    def slice_of(order):
        return 2 * bits[order][0] + bits[order][1]

    def core_copy(a, i):
        _, span = sizes(a)
        away = pl.ds(pl.multiple_of((1 - core) * span, 128), span)
        return remote(big[a].at[i, :, :, away], by_core[a].at[i], c_send.at[a, i, 0], c_recv.at[a, i, 0], core_id, z)

    def first_copy(a, i, order):
        height, _ = sizes(a)
        own = pl.ds(order * half, half)
        away = pl.ds(pl.multiple_of((1 - bits[order][0]) * (height // 2), 16), height // 2)
        return remote(
            by_core[a].at[i, own, away, :], up_first.at[i, own], c_send.at[a, i, 1 + order],
            c_recv.at[a, i, 1 + order], ids[order][0], z,
        )

    def add(into, at, term, owners):
        height = term(0).shape[0]
        tile = 32 if height % 48 else 48

        def body(n, _):
            o, t = n // (height // tile), n % (height // tile)
            spot = pl.ds(pl.multiple_of(at + t * tile, 16), tile)
            value = term(o)[pl.ds(pl.multiple_of(t * tile, 16), tile), :]
            into[o, spot, :] = (into[o, spot, :].astype(F32) + value.astype(F32)).astype(BF16)
            return 0

        lax.fori_loop(0, owners * (height // tile), body, 0)

    def chunk_1(i):
        for a in range(2):
            _, span = sizes(a)
            core_copy(a, i).wait_recv()
            keep = pl.ds(pl.multiple_of(core * span, 128), span)
            add(by_core[a].at[i], 0, lambda o: big[a].at[i, o, :, keep], ring)
        for order in range(2):
            first_copy(0, i, order).start()
        parts_out(1, i)[0].start()

    def chunk_2(i):
        height, _ = sizes(0)
        for order in range(2):
            own = pl.ds(order * half, half)
            first_copy(0, i, order).wait_recv()
            at = bits[order][0] * (height // 2)
            add(by_core[0].at[i, own], at, lambda o: up_first.at[i, order * half + o], half)
        for copy in parts_out(0, i):
            copy.start()

    def parts_out(a, i):
        height, span = sizes(a)
        if a == 1:
            return [pltpu.make_async_copy(by_core[1].at[i], down_part.at[:, i], out_sem.at[i, 2 * half])]
        copies = []
        for order in range(2):
            own = pl.ds(order * half, half)
            rows = pl.ds(pl.multiple_of(bits[order][0] * (height // 2), 16), height // 2)
            for n in range(half):
                copies.append(pltpu.make_async_copy(
                    by_core[0].at[i, own, rows, pl.ds(n * strip, strip)],
                    up_part.at[own, :, pl.ds(pl.multiple_of(n * steps * strip + i * strip, 128), strip)],
                    out_sem.at[i, half * order + n],
                ))
        return copies

    def feed_step(step, _):
        for h in hops:
            @pl.when((step == 2 * h - 2) & (h > 1))
            def _(h=h):
                stage_a(2, h)

            @pl.when(step == 2 * h)
            def _(h=h):
                stage_b(2, h)

            @pl.when(step == 2 * h + 1)
            def _(h=h):
                stage_c(2, h)

        @pl.when(step < steps)
        def _():
            spots = [pl.ds(pl.multiple_of(r * (ff // ring) + step * strip, 128), strip) for r in range(ring)]
            bias_spots = [
                pl.ds(pl.multiple_of(2 * width + r * (ff // ring) + step * strip, 128), strip) for r in range(ring)
            ]
            up_part_ = jnp.concatenate([up_all[:, at] for at in spots], axis=1)
            down_part_ = jnp.concatenate([down_all[at, :] for at in spots], axis=0)
            bias = jnp.concatenate([small_all[0:1, at] for at in bias_spots], axis=1)
            total = jnp.zeros((1, ring * strip), F32)
            for t in range(tiles):
                at = pl.ds(t * tile, tile)
                u = dot(m_ref[at, :], up_part_) + bias
                cdf = 0.5 * (1.0 + lax.erf(u * (1.0 / math.sqrt(2.0))))
                hidden = (u * cdf).astype(BF16)
                slope = cdf + u * jnp.exp(-0.5 * u * u) * (1.0 / math.sqrt(2.0 * math.pi))
                back = (dot(g_ref[at, :], down_part_, NT) * slope).astype(BF16)
                hid_ref[at, :] = hidden
                dup_in_ref[at, :] = back
                total += jnp.sum(back.astype(F32), axis=0, keepdims=True)
                out_ref[at, :] += dot(hidden, down_part_)
                h_ref[at, :] += dot(back, up_part_, NT)
            for r in range(ring):
                dbias_ref[0:1, spots[r]] = total[:, r * strip : (r + 1) * strip]
            ddown = dot(hid_ref[...], g_ref[...], TN).astype(BF16)
            dup = dot(mt_ref[...], dup_in_ref[...]).astype(BF16)
            for r in range(ring):
                ddown_ref[step, r] = ddown[r * strip : (r + 1) * strip, :]
                dup_ref[step, r] = dup[r * (width // ring) : (r + 1) * (width // ring), :]
            core_copy(0, step).start()
            core_copy(1, step).start()

        for lag, stage in ((1, chunk_1), (3, chunk_2)):
            @pl.when((step >= lag) & (step < steps + lag))
            def _(lag=lag, stage=stage):
                stage(step - lag)

        return 0

    lax.fori_loop(0, steps + 3, feed_step, 0)

    gain = jnp.zeros((1, width), F32)
    shift = jnp.zeros((1, width), F32)
    sums = jnp.zeros((1, width), F32)
    for t in range(tiles):
        at = pl.ds(t * tile, tile)
        xh, _ = normalized(x_ref[at, :].astype(F32))
        dm = h_ref[at, :]
        gain += jnp.sum(dm * xh, axis=0, keepdims=True)
        shift += jnp.sum(dm, axis=0, keepdims=True)
        sums += jnp.sum(g_ref[at, :].astype(F32), axis=0, keepdims=True)
        h_ref[at, :] = dm * gain_2
    sums_ref[...] = jnp.concatenate([gain, shift, sums, jnp.zeros((5, width), F32)], axis=0)

    mine = z - core
    for which in range(2):
        for k in range(1, ring):
            @pl.when((mine >= 0) & (mine < batch))
            def _(which=which, k=k):
                other = (z + k) % ring
                ref = pairs[which][1].at[pl.ds(pl.multiple_of(other * piece, 16), piece), :]
                remote(ref, ref, t_send.at[which, 0], t_recv.at[which, other], core_id, z).wait_recv()
    for h in hops:
        stage_d(2, h)
    for k in range(1, ring):
        small_copy(k).wait_send()
    for a in range(3):
        for way in range(2):
            for h in range(ring - 1):
                @pl.when(can_send(way, h))
                def _(a=a, way=way, h=h):
                    hop(a, way, h).wait_send()
        for h in hops:
            for way in range(2):
                @pl.when(in_range(way, h))
                def _(a=a, h=h, way=way):
                    shard = z - h if way == 0 else z + h
                    for j in range(8):
                        cast(a, shard, j).wait_send()
    for which in range(2):
        for i in range(batch):
            src, dst, target = move(which, i)

            @pl.when(target != z)
            def _(src=src, dst=dst, target=target, which=which, i=i):
                remote(src, dst, t_send.at[which, i], t_recv.at[which, z], d, target).wait_send()

            @pl.when(target == z)
            def _(src=src, dst=dst, which=which):
                pltpu.make_async_copy(src, dst, local.at[6 + which]).wait()
    own_att.wait()

    def close(i, _):
        for a in range(2):
            core_copy(a, i).wait_send()
            for copy in parts_out(a, i):
                copy.wait()
        for order in range(2):
            first_copy(0, i, order).wait_send()
        return 0

    lax.fori_loop(0, steps, close, 0)


def gather_feed(up, down, qkv, out, small, tokens, cotangents, piece, entries):
    ring = lax.axis_size("ctx")
    count, width = tokens.shape
    ff = up.shape[1]
    strip = 128
    chunk = ring * strip
    steps = ff // chunk
    shard = up.shape[0]
    columns = qkv.shape[1] + out.shape[1]
    home = jax.ShapeDtypeStruct((ring * piece, width), tokens.dtype)
    rows = jax.ShapeDtypeStruct((count, width), F32)
    dma = pltpu.SemaphoreType.DMA
    anywhere = pl.BlockSpec(memory_space=pl.ANY)
    vmem = pl.BlockSpec(memory_space=pltpu.VMEM)
    return pl.pallas_call(
        gather_kernel,
        in_specs=[anywhere] * 7,
        out_specs=[anywhere, vmem, vmem, anywhere, anywhere, vmem, vmem, anywhere, anywhere, vmem, vmem],
        out_shape=[
            jax.ShapeDtypeStruct((ring * shard, columns), BF16),
            jax.ShapeDtypeStruct((8, entries), F32), jax.ShapeDtypeStruct((8, width), F32), home, home, rows, rows,
            jax.ShapeDtypeStruct((ring, shard // 2, ff // 2), BF16),
            jax.ShapeDtypeStruct((ring, steps, strip, width // 2), BF16),
            jax.ShapeDtypeStruct((8, ff), F32), jax.ShapeDtypeStruct((8, width), F32),
        ],
        scratch_shapes=[
            pltpu.VMEM((ring * shard, ff), BF16), pltpu.VMEM((ring * down.shape[0], width), BF16),
            pltpu.VMEM((shard, columns), BF16),
            pltpu.VMEM(up.shape, F32), pltpu.VMEM(down.shape, F32), pltpu.VMEM((shard, columns), F32),
            pltpu.VMEM((ring, *small.shape), F32),
            pltpu.VMEM((count, width), BF16), pltpu.VMEM((count, width), BF16), pltpu.VMEM((count, width), BF16),
            pltpu.VMEM((width, count), BF16),
            pltpu.VMEM((count, chunk), BF16), pltpu.VMEM((count, chunk), BF16),
            pltpu.VMEM((steps, ring, shard, chunk), BF16), pltpu.VMEM((steps, ring, shard, chunk // 2), BF16),
            pltpu.VMEM((steps, ring, shard // 2, chunk // 2), BF16),
            pltpu.VMEM((steps, ring, strip, width), BF16), pltpu.VMEM((steps, ring, strip, width // 2), BF16),
            dma((3, 2, ring)), dma((3, 2, ring)), dma((3, ring, 8)), dma((3, ring, 8)),
            dma((ring,)), dma((ring,)), dma((2, count // piece)), dma((2, ring)), dma((10,)), dma((steps, ring + 1)),
            dma((2, steps, 3)), dma((2, steps, 3)),
        ],
        compiler_params=pltpu.CompilerParams(
            collective_id=0, has_side_effects=True, vmem_limit_bytes=60 * MIB
        ),
        cost_estimate=pl.CostEstimate(
            flops=12 * count * width * ff, bytes_accessed=60 * MIB, transcendentals=count * ff
        ),
        name="gather_feed",
    )(up, down, qkv, out, small, tokens, cotangents)


def remote(src, dst, send_sem, recv_sem, dp, ctx):
    return pltpu.make_async_remote_copy(
        src_ref=src, dst_ref=dst, send_sem=send_sem, recv_sem=recv_sem, device_id=(dp, ctx), device_id_type=MESH
    )


def team_id(d, t):
    return d + (8 << t) * (1 - 2 * (d // (8 << t) % 2))


def greet(teams):
    ring = lax.axis_size("ctx")
    d, z = lax.axis_index("dp"), lax.axis_index("ctx")
    core, x, y, core_id, x_id, y_id = plane(d)
    barrier = pltpu.get_barrier_semaphore()
    partners = [core_id, x_id, y_id, x_id + y_id - d] + [team_id(d, t) for t in range(teams)]
    for k in range(1, ring):
        pl.semaphore_signal(barrier, inc=1, device_id=(d, (z + k) % ring), device_id_type=MESH)
    for other in partners:
        pl.semaphore_signal(barrier, inc=1, device_id=(other, z), device_id_type=MESH)
    pl.semaphore_wait(barrier, ring - 1 + len(partners))


def reducer(teams, levels, ins, sums, bufs, send, recv, load):
    count = len(ins)
    ring = lax.axis_size("ctx")
    d, z = lax.axis_index("dp"), lax.axis_index("ctx")
    core, x, y, core_id, x_id, y_id = plane(d)
    far_id = x_id + y_id - d
    bits, ids = ((x, y), (y, x)), ((x_id, y_id), (y_id, x_id))
    spots = ((x, y), (1 - x, y), (x, 1 - y), (1 - x, 1 - y))

    def sizes(a):
        _, strips, quarter, span = bufs[a][-1].shape
        return strips, quarter, span

    def owners(a, order):
        strips = sizes(a)[0]
        return pl.ds(order * ring // 2 * strips, ring // 2 * strips)

    def rows_at(at, height):
        return pl.ds(pl.multiple_of(at, 16), height)

    def kept(a, order):
        return 0 if levels[a] == 2 else bits[order][0] * 2 * sizes(a)[1]

    def core_copy(a):
        span = sizes(a)[2]
        away = pl.ds(pl.multiple_of((1 - core) * span, 128), span)
        return remote(ins[a].at[:, :, away], bufs[a][1], send.at[a, 0], recv.at[a, 0], core_id, z)

    def own_load(a):
        if levels[a] == 3:
            return pltpu.make_async_copy(ins[a], bufs[a][5].at[0], load.at[a])
        span = sizes(a)[2]
        keep = pl.ds(pl.multiple_of(core * span, 128), span)
        src = ins[a].at[:, :, keep] if levels[a] == 0 else ins[a]
        return pltpu.make_async_copy(src, bufs[a][0], load.at[a])

    def first_copy(a, order):
        quarter = sizes(a)[1]
        away = rows_at((1 - bits[order][0]) * 2 * quarter, 2 * quarter)
        return remote(
            bufs[a][0].at[owners(a, order), away, :], bufs[a][2].at[owners(a, order)], send.at[a, 1 + order],
            recv.at[a, 1 + order], ids[order][0], z,
        )

    def second_copy(a, order):
        quarter = sizes(a)[1]
        away = rows_at(kept(a, order) + (1 - bits[order][1]) * quarter, quarter)
        return remote(
            bufs[a][0].at[owners(a, order), away, :], bufs[a][3].at[owners(a, order)], send.at[a, 3 + order],
            recv.at[a, 3 + order], ids[order][1], z,
        )

    def own_quarter(a, owner):
        strips, quarter, _ = sizes(a)
        order = owner // (ring // 2)
        first, second = (1 - order) * x + order * y, (1 - order) * y + order * x
        at = second * quarter if levels[a] == 2 else (2 * first + second) * quarter
        return bufs[a][0].at[pl.ds(owner * strips, strips), rows_at(at, quarter), :]

    def owner_copy(a, k):
        to = (z + k) % ring
        return remote(own_quarter(a, to), bufs[a][4].at[k - 1], send.at[a, 4 + k], recv.at[a, 4 + k], d, to)

    def team_copy(a, t):
        j = 4 + ring + 7 + t
        return remote(bufs[a][5].at[0], bufs[a][5].at[1 + t], send.at[a, j], recv.at[a, j], team_id(d, t), z)

    def final(a, spot, side):
        strips, quarter, span = sizes(a)
        order = z // (ring // 2)
        xx, yy = spots[spot]
        at = ((1 - order) * (2 * xx + yy) + order * (2 * yy + xx)) * quarter
        return sums[a].at[:, rows_at(at, quarter), pl.ds(pl.multiple_of(side * span, 128), span)]

    def spread(a, j):
        s, r = send.at[a, 4 + ring + j - 1], recv.at[a, 4 + ring + j - 1]
        if j < 4:
            return remote(bufs[a][5].at[0], final(a, 0, core), s, r, (x_id, y_id, far_id)[j - 1], z)
        src = bufs[a][5].at[0] if j == 4 else final(a, j - 4, core)
        return remote(src, final(a, j - 4, core), s, r, core_id, z)

    def spread_here(a, j):
        s, r = send.at[a, 4 + ring + j - 1], recv.at[a, 4 + ring + j - 1]
        ref = final(a, j, core) if j < 4 else final(a, j - 4, 1 - core)
        remote(ref, ref, s, r, core_id, z).wait_recv()

    def keep_own(a):
        return pltpu.make_async_copy(bufs[a][5].at[0], final(a, 0, core), load.at[count + a])

    def add(into, at, term, blocks):
        height = term.shape[1]
        tile = 32 if height % 48 else 48

        def body(n, _):
            o, t = n // (height // tile), n % (height // tile)
            spot = rows_at(at + t * tile, tile)
            value = term[o, rows_at(t * tile, tile), :]
            into[o, spot, :] = (into[o, spot, :].astype(F32) + value.astype(F32)).astype(BF16)
            return 0

        lax.fori_loop(0, blocks * (height // tile), body, 0)

    def enter(a):
        if levels[a] == 0:
            core_copy(a).start()
        own_load(a).start()

    def first(a):
        own_load(a).wait()
        if levels[a] == 0:
            core_copy(a).wait_recv()
            add(bufs[a][0], 0, bufs[a][1], bufs[a][0].shape[0])
        if levels[a] < 2:
            for order in range(2):
                first_copy(a, order).start()

    def second(a):
        for order in range(2):
            if levels[a] < 2:
                first_copy(a, order).wait_recv()
                own = owners(a, order)
                add(bufs[a][0].at[own], kept(a, order), bufs[a][2].at[own], ring // 2 * sizes(a)[0])
            second_copy(a, order).start()

    def to_owner(a):
        for order in range(2):
            second_copy(a, order).wait_recv()
            own = owners(a, order)
            at = kept(a, order) + bits[order][1] * sizes(a)[1]
            add(bufs[a][0].at[own], at, bufs[a][3].at[own], ring // 2 * sizes(a)[0])
        for k in range(1, ring):
            owner_copy(a, k).start()

    def add_up(a):
        for k in range(1, ring):
            owner_copy(a, k).wait_recv()
        mine = own_quarter(a, z)
        for s in range(sizes(a)[0]):
            terms = [mine[s]] + [bufs[a][4][k, s] for k in range(ring - 1)]
            bufs[a][5][0, s] = sum((t.astype(F32) for t in terms[1:]), terms[0].astype(F32)).astype(BF16)
        for t in range(teams):
            team_copy(a, t).start()
            team_copy(a, t).wait()
            bufs[a][5][0] = (bufs[a][5][0].astype(F32) + bufs[a][5][1 + t].astype(F32)).astype(BF16)

    def total(a):
        if levels[a] == 3:
            own_load(a).wait()
        else:
            add_up(a)
        keep_own(a).start()
        for j in range(1, 5):
            spread(a, j).start()

    def hand_on(a):
        add_up(a)
        out = pltpu.make_async_copy(bufs[a][5].at[0], sums[a], load.at[count + a])
        out.start()
        sent(a)
        out.wait()

    def share(a):
        for j in range(1, 4):
            spread_here(a, j)
            spread(a, 4 + j).start()

    def sent(a):
        if levels[a] == 0:
            core_copy(a).wait_send()
        for order in range(2):
            if levels[a] < 2:
                first_copy(a, order).wait_send()
            second_copy(a, order).wait_send()
        for k in range(1, ring):
            owner_copy(a, k).wait_send()

    def close(a):
        for j in range(4, 8):
            spread_here(a, j)
        if levels[a] < 3:
            sent(a)
        for j in range(1, 8):
            spread(a, j).wait_send()
        keep_own(a).wait()

    return SimpleNamespace(
        enter=enter, first=first, second=second, to_owner=to_owner, total=total, hand_on=hand_on, share=share, close=close
    )


def reducer_scratch(levels, shapes, teams, ring):
    scratch = []
    for level, (strips, rows, columns) in zip(levels, shapes):
        blocks, span = ring * strips, columns // 2
        none = (1, 16, 128)
        scratch += [
            pltpu.VMEM(none if level == 3 else (blocks, rows // 2 if level == 2 else rows, span), BF16),
            pltpu.VMEM((blocks, rows, span) if level == 0 else none, BF16),
            pltpu.VMEM((blocks, rows // 2, span) if level < 2 else none, BF16),
            pltpu.VMEM((blocks, rows // 4, span) if level < 3 else none, BF16),
            pltpu.VMEM((ring - 1, strips, rows // 4, span) if level < 3 else (1, *none), BF16),
            pltpu.VMEM((1 + teams, strips, rows // 4, span), BF16),
        ]
    copies = 4 + ring + 7 + teams
    dma = pltpu.SemaphoreType.DMA
    return scratch + [dma((len(levels), copies)), dma((len(levels), copies)), dma((2 * len(levels),))]


def reduce_kernel(
    teams, up_ref, down_ref, qkv_ref, small_att, small_mlp, small_up, back_ref, o_last, o_ref, g_ref, weights,
    up_sum, down_sum, qkv_sum, out_sum, norm_out, bias_out, attend_out, ret_back, *refs,
):
    ring = lax.axis_size("ctx")
    d, z = lax.axis_index("dp"), lax.axis_index("ctx")
    core, x, y, core_id, x_id, y_id = plane(d)
    bufs = [refs[6 * a : 6 * a + 6] for a in range(4)]
    send, recv, load, o_in, wo_ref, dwo_ref, small_acc, small_in = refs[24:32]
    s_send, s_recv, r_send, r_recv, r_local = refs[32:]
    batch, piece, width = ret_back.shape
    lanes = o_last.shape[1]
    up, down, qkv, out = range(4)
    ins, sums = (up_ref, down_ref, qkv_ref, dwo_ref), (up_sum, down_sum, qkv_sum, out_sum)
    do = reducer(teams, LEVELS, ins, sums, bufs, send, recv, load)

    pairs = ((o_last, o_in), (back_ref, ret_back))
    mine = z - core

    def returned(which, i, to):
        source, target = pairs[which]
        return source.at[pl.ds(pl.multiple_of(to * piece, 16), piece), :], target.at[i]

    def start_returns(which):
        for i in range(batch):
            @pl.when(mine == i)
            def _(i=i):
                for k in range(1, ring):
                    to = (z + k) % ring
                    src, dst = returned(which, i, to)
                    remote(src, dst, r_send.at[which, k], r_recv.at[which, i], d, to).start()
                src, dst = returned(which, i, z)
                pltpu.make_async_copy(src, dst, r_local.at[which]).start()

    def wait_returns(which):
        for i in range(batch):
            src, dst = returned(which, i, z)

            @pl.when(mine == i)
            def _(src=src, dst=dst):
                pltpu.make_async_copy(src, dst, r_local.at[which]).wait()

            @pl.when(mine != i)
            def _(i=i, src=src, dst=dst):
                remote(src, dst, r_send.at[which, 0], r_recv.at[which, i], core_id, z).wait_recv()

    def close_returns(which):
        for i in range(batch):
            @pl.when(mine == i)
            def _(i=i):
                for k in range(1, ring):
                    to = (z + k) % ring
                    remote(*returned(which, i, to), r_send.at[which, k], r_recv.at[which, i], d, to).wait_send()

    steps = [core_id, x_id, y_id] + [team_id(d, t) for t in range(teams)]

    def small_copy(n):
        return remote(small_acc, small_in.at[n], s_send.at[n], s_recv.at[n], steps[n], z)

    def small_owner(k):
        n = len(steps) + k - 1
        return remote(small_acc, small_in.at[n], s_send.at[n], s_recv.at[n], d, (z + k) % ring)

    def small_close(n):
        small_copy(n).wait()
        small_acc[...] += small_in[n]
        if n + 1 < len(steps):
            small_copy(n + 1).start()
        else:
            for k in range(1, ring):
                small_owner(k).start()

    columns = weights.shape[1] - width
    wo_load = pltpu.make_async_copy(weights.at[:, pl.ds(columns, width)], wo_ref, r_local.at[2])
    wo_load.start()
    small_acc[0:8, :] = small_att[...]
    small_acc[8:16, :] = small_mlp[...]
    for n in range(small_up.shape[1] // width):
        small_acc[16 + n : 17 + n, :] = small_up[0:1, n * width : (n + 1) * width]
    rest = 16 + small_up.shape[1] // width
    small_acc[rest:, :] = jnp.zeros((small_acc.shape[0] - rest, width), F32)
    greet(teams)
    do.enter(qkv)
    start_returns(0)
    start_returns(1)
    do.enter(up)
    do.enter(down)
    small_copy(0).start()
    do.total(up)
    do.total(down)
    do.first(qkv)
    small_close(0)
    do.share(up)
    do.share(down)

    wo_load.wait()
    wait_returns(0)
    split = o_ref.shape[1]
    for i in range(batch):
        at = pl.ds(i * piece, piece)
        attend_out[at, :] = dot(o_ref[at, :], wo_ref[:split, :]) + dot(o_in[i], wo_ref[split:, :])
    late = jnp.concatenate([o_in[i] for i in range(batch)], axis=0)
    dwo = jnp.concatenate([dot(o_ref[...], g_ref[...], TN), dot(late, g_ref[...], TN)], axis=0).astype(BF16)
    for r in range(ring):
        dwo_ref[r] = dwo[r * (width // ring) : (r + 1) * (width // ring), :]
    do.enter(out)
    do.second(qkv)
    do.first(out)
    small_close(1)
    do.to_owner(qkv)
    do.second(out)
    for n in range(2, len(steps)):
        small_close(n)
    do.total(qkv)
    do.to_owner(out)
    do.share(qkv)
    do.total(out)
    for k in range(1, ring):
        small_owner(k).wait()
    total = small_acc[...]
    for k in range(ring - 1):
        total += small_in[len(steps) + k]
    norm = jnp.concatenate([total[0:2], total[8:10], jnp.zeros((4, width), F32)], axis=0)
    norm_out[...] = pltpu.roll(norm, (ring - z) % ring * (width // ring), 1)
    ups = [total[16 + n : 17 + n] for n in range(small_up.shape[1] // width)]
    bias = jnp.concatenate([total[2:3], total[10:11], *ups, total[10:11]], axis=1)
    entries = bias.shape[1]
    bias = pltpu.roll(jnp.broadcast_to(bias, (8, entries)), (ring - z) % ring * (entries // ring), 1)
    bias_out[...] = bias[:, : bias_out.shape[1]]
    do.share(out)
    for a in range(4):
        do.close(a)
    wait_returns(1)
    close_returns(0)
    close_returns(1)


def reduce_all(up, down, qkv, small_att, small_mlp, small_up, back, o_last, o_first, g, weights, batch):
    ring, groups = lax.axis_size("ctx"), lax.axis_size("dp")
    teams = (groups // 8).bit_length() - 1
    width = g.shape[1]
    piece = g.shape[0] // batch
    shapes = [(n, 4 * rows, 2 * span) for n, rows, span in (up.shape, down.shape)]
    shapes += [(1, width // ring, qkv.shape[1]), (1, width // ring, width)]
    dma = pltpu.SemaphoreType.DMA
    anywhere = pl.BlockSpec(memory_space=pl.ANY)
    vmem = pl.BlockSpec(memory_space=pltpu.VMEM)
    rounds = 3 + teams + ring - 1
    small = (16 + -(-small_up.shape[1] // width // 8) * 8, width)
    share = (3 * width + small_up.shape[1]) // ring
    scratch = reducer_scratch(LEVELS, shapes, teams, ring)
    scratch += [
        pltpu.VMEM((batch, piece, o_last.shape[1]), BF16), pltpu.VMEM((width, width), BF16),
        pltpu.VMEM((ring, width // ring, width), BF16), pltpu.VMEM(small, F32), pltpu.VMEM((rounds, *small), F32),
        dma((rounds,)), dma((rounds,)), dma((2, ring)), dma((2, batch)), dma((3,)),
    ]
    return pl.pallas_call(
        functools.partial(reduce_kernel, teams),
        in_specs=[anywhere] * 3 + [vmem] * 3 + [anywhere, anywhere, vmem, vmem, anywhere],
        out_specs=[anywhere] * 4 + [vmem, vmem, vmem, anywhere],
        out_shape=[jax.ShapeDtypeStruct(shape, BF16) for shape in shapes]
        + [
            jax.ShapeDtypeStruct((8, width), F32), jax.ShapeDtypeStruct((8, share + -share % 128), F32),
            jax.ShapeDtypeStruct(g.shape, F32),
            jax.ShapeDtypeStruct((batch, piece, width), BF16),
        ],
        scratch_shapes=scratch,
        compiler_params=pltpu.CompilerParams(collective_id=1, has_side_effects=True, vmem_limit_bytes=56 * MIB),
        cost_estimate=pl.CostEstimate(flops=4 * width * width * g.shape[0], bytes_accessed=60 * MIB, transcendentals=0),
        name="reduce",
    )(
        up, down, qkv.reshape(ring, width // ring, -1), small_att, small_mlp, small_up, back, o_last,
        o_first.reshape(batch * piece, -1), g, weights,
    )


def attend_kernel(
    teams, order_ref, x_ref, stored_g_ref, norm_ref, bias_ref, cos_ref, low_ref, high_ref, wq_ref, wk_ref, wv_ref,
    wo_ref, up_ref, down_ref, h_ref, dqkv_all, small_ref, o_last, ret_o, up_sum, down_sum,
    g_ref, a_ref, at_ref, da_ref, q_ref, k_ref, v_ref, do_ref, o_ref, kt_ref, vt_ref, dqs_ref, dks_ref, dvs_ref,
    grad_ref, stored_o_ref, o_send, o_recv, o_local, grad_sem, *reduce_refs,
):
    step = pl.program_id(0)
    last = grad_ref.shape[0] - 1
    rows, width = x_ref.shape
    lanes = QUAD * HD
    tile = 256
    half = ROT // 2
    scale = 1.0 / math.sqrt(HD)
    blocks = rows // BLOCK
    ring = lax.axis_size("ctx")
    d, z = lax.axis_index("dp"), lax.axis_index("ctx")
    core_id = plane(d)[3]
    batch, piece = ret_o.shape[:2]
    mine = z - d % 2
    is_home = (mine >= 0) & (mine < batch)
    up, down = 0, 1
    bufs = (reduce_refs[:6], reduce_refs[6:12])
    do_sum = reducer(teams, MLP_LEVELS, (up_ref, down_ref), (up_sum, down_sum), bufs, *reduce_refs[12:])

    @pl.when(step == 0)
    def _():
        do_sum.enter(down)
        do_sum.enter(up)
        greet(teams)
        do_sum.first(down)
        do_sum.first(up)
        do_sum.second(up)

    def o_copy(quad, k, i):
        to = (z + k) % ring
        src = stored_o_ref.at[quad, pl.ds(pl.multiple_of(to * piece, 16), piece), :]
        dst = ret_o.at[i, :, pl.ds(pl.multiple_of(quad * lanes, 128), lanes)]
        if k == 0:
            return pltpu.make_async_copy(src, dst, o_local.at[quad])
        return remote(src, dst, o_send.at[quad, k], o_recv.at[quad, i], d, to)

    def grad_copy(quad, j):
        at = pl.ds(pl.multiple_of(j * width + quad * lanes, 128), lanes)
        return pltpu.make_async_copy(grad_ref.at[quad, j], dqkv_all.at[:, at], grad_sem.at[quad, j])


    def stored(ref, at):
        values = ref[pl.ds(at * BLOCK, BLOCK), :]
        return jnp.where(is_home, values, jnp.zeros_like(values))

    @pl.when(step == 0)
    def _():
        for j in range(blocks):
            place = order_ref[1, j]
            at = pl.ds(j * BLOCK, BLOCK)
            xh, _ = normalized(stored(x_ref, place).astype(F32))
            a = xh * norm_ref[1:2, :] + norm_ref[2:3, :]
            a_ref[at, :] = a.astype(BF16)
            at_ref[:, at] = a.T.astype(BF16)
            g_ref[at, :] = stored(stored_g_ref, place)
        da_ref[...] = jnp.zeros_like(da_ref)

    def table(ref, at):
        values = ref[at, :]
        return jnp.concatenate([values] * (lanes // values.shape[1]), axis=1)

    def turn(values, at):
        low = pltpu.roll(values, lanes - half, 1) * table(low_ref, at)
        high = pltpu.roll(values, half, 1) * table(high_ref, at)
        return values * table(cos_ref, at), low + high

    for t in range(rows // tile):
        at = pl.ds(t * tile, tile)
        a = a_ref[at, :]
        same, cross = turn(dot(a, wq_ref[...]) + bias_ref[0:1, :], at)
        q_ref[at, :] = ((same + cross).astype(BF16) * scale).astype(BF16)
        same, cross = turn(dot(a, wk_ref[...]), at)
        keys = same + cross
        k_ref[at, :] = keys.astype(BF16)
        kt_ref[:, at] = keys.T.astype(BF16)
        values = dot(a, wv_ref[...])
        v_ref[at, :] = values.astype(BF16)
        vt_ref[:, at] = values.T.astype(BF16)
        mixed_back = dot(g_ref[at, :], wo_ref[...], NT)
        do_ref[at, :] = mixed_back.astype(BF16)

    dks_ref[...] = jnp.zeros_like(dks_ref)
    dvs_ref[...] = jnp.zeros_like(dvs_ref)
    wide = 2 * HD
    head_of = lax.broadcasted_iota(jnp.int32, (BLOCK, wide), 1) // HD

    def stack(values):
        zero = jnp.zeros_like(values)
        return jnp.concatenate([jnp.where(head_of == e, values, zero) for e in range(2)], axis=0)

    def diagonal(values):
        return jnp.concatenate([values[e * HD : (e + 1) * HD, e * BLOCK : (e + 1) * BLOCK] for e in range(2)], axis=0)

    spot = lax.broadcasted_iota(jnp.int32, (BLOCK, 2 * BLOCK), 1) % BLOCK
    admitted = lax.broadcasted_iota(jnp.int32, (BLOCK, 2 * BLOCK), 0) <= spot

    def products_in(b, p):
        at, seen, own = pl.ds(b * BLOCK, BLOCK), pl.ds(0, (b + 1) * BLOCK), pl.ds(p * wide, wide)
        q, do = stack(q_ref[at, own]), stack(do_ref[at, own])
        return q, do, dot(k_ref[seen, own], q, NT), dot(v_ref[seen, own], do, NT)

    def softmax(b, scores, back):
        edge = jnp.where(admitted, scores[b * BLOCK :], -1e30)
        scores = edge if b == 0 else jnp.concatenate([scores[: b * BLOCK], edge], axis=0)
        top = jnp.max(scores, axis=0, keepdims=True)
        expo = jnp.exp(scores - top)
        probs = expo * (1.0 / jnp.sum(expo, axis=0, keepdims=True))
        share = jnp.sum(probs * back, axis=0, keepdims=True)
        return probs.astype(BF16), (probs * (back - share)).astype(BF16)

    def products_out(b, p, q, do, low, back):
        at, seen, own = pl.ds(b * BLOCK, BLOCK), pl.ds(0, (b + 1) * BLOCK), pl.ds(p * wide, wide)
        mixed = diagonal(dot(vt_ref[own, seen], low))
        o_ref[at, own] = mixed.T.astype(BF16)
        dqs_ref[at, own] = diagonal(dot(kt_ref[own, seen], back)).T * scale
        dks_ref[seen, own] += dot(back, q)
        dvs_ref[seen, own] += dot(low, do)

    units = [(b, p) for b in range(rows // BLOCK) for p in range(lanes // wide)]
    ready = products_in(*units[0])
    done = None
    for n, (b, p) in enumerate(units):
        q, do, scores, back = ready
        if n + 1 < len(units):
            ready = products_in(*units[n + 1])
        low, back = softmax(b, scores, back)
        if done is not None:
            products_out(*done)
        done = (b, p, q, do, low, back)
    products_out(*done)

    total = jnp.zeros((1, lanes), F32)
    for t in range(rows // tile):
        at = pl.ds(t * tile, tile)
        same, cross = turn(dqs_ref[at, :], at)
        dq = (same - cross).astype(BF16)
        same, cross = turn(dks_ref[at, :], at)
        dk = (same - cross).astype(BF16)
        dv = dvs_ref[at, :].astype(BF16)
        total += jnp.sum(dq.astype(F32), axis=0, keepdims=True)
        q_ref[at, :] = dq
        k_ref[at, :] = dk
        v_ref[at, :] = dv
        da_ref[at, :] += dot(dq, wq_ref[...], NT) + dot(dk, wk_ref[...], NT) + dot(dv, wv_ref[...], NT)
    small_ref[2:3, pl.ds(pl.multiple_of(step * lanes, 128), lanes)] = total
    for j, ref in enumerate((q_ref, k_ref, v_ref)):
        grad_ref[step, j] = dot(at_ref[...], ref[...]).astype(BF16)
        grad_copy(step, j).start()
    for s in range(blocks):
        stored_o_ref[step, s * BLOCK : (s + 1) * BLOCK, :] = o_ref[pl.ds(order_ref[0, s] * BLOCK, BLOCK), :]

    for i in range(batch):
        @pl.when((mine == i) & (step < last))
        def _(i=i):
            for k in range(ring):
                o_copy(step, k, i).start()

    @pl.when(step == 0)
    def _():
        do_sum.second(down)
        do_sum.to_owner(up)

    @pl.when(step == 1)
    def _():
        do_sum.to_owner(down)

    @pl.when(step == last)
    def _():
        gain = jnp.zeros((1, width), F32)
        shift = jnp.zeros((1, width), F32)
        for s in range(blocks):
            at = pl.ds(s * BLOCK, BLOCK)
            sorted_at = pl.ds(order_ref[0, s] * BLOCK, BLOCK)
            xh, _ = normalized(stored(x_ref, s).astype(F32))
            da = da_ref[sorted_at, :]
            gain += jnp.sum(da * xh, axis=0, keepdims=True)
            shift += jnp.sum(da, axis=0, keepdims=True)
            h_ref[at, :] = (da * norm_ref[1:2, :]).astype(BF16)
        small_ref[0:1, :] = gain
        small_ref[1:2, :] = shift
        small_ref[3:8, :] = jnp.zeros((5, width), F32)
        out = pltpu.make_async_copy(stored_o_ref.at[last], o_last, o_local.at[last])
        out.start()
        do_sum.hand_on(up)
        do_sum.hand_on(down)
        for quad in range(last):
            for i in range(batch):
                @pl.when(mine != i)
                def _(quad=quad, i=i):
                    ref = ret_o.at[i, :, pl.ds(quad * lanes, lanes)]
                    remote(ref, ref, o_send.at[quad, 0], o_recv.at[quad, i], core_id, z).wait_recv()

                @pl.when(mine == i)
                def _(quad=quad, i=i):
                    o_copy(quad, 0, i).wait()
                    for k in range(1, ring):
                        o_copy(quad, k, i).wait_send()
        for quad in range(last + 1):
            for j in range(3):
                grad_copy(quad, j).wait()
        out.wait()


def attend(order, x, g, norms, bias_q, tables, weights, up, down, batch):
    ring, groups_dp = lax.axis_size("ctx"), lax.axis_size("dp")
    teams = (groups_dp // 8).bit_length() - 1
    shapes = ((1, 2 * up.shape[1], 2 * up.shape[2]), (down.shape[1], down.shape[2], 2 * down.shape[3]))
    down = down.reshape(-1, *down.shape[2:])
    rows, width = x.shape
    lanes = QUAD * HD
    groups = width // lanes
    anywhere = pl.BlockSpec(memory_space=pl.ANY)
    whole = lambda shape: pl.BlockSpec(shape, lambda i: (0,) * len(shape))
    once = lambda shape: pl.BlockSpec(shape, lambda i: (0,) * len(shape), pipeline_mode=pl.Buffered(1))
    dma = pltpu.SemaphoreType.DMA
    slices = [(n, r // 4, c // 2) for n, r, c in shapes]
    return pl.pallas_call(
        functools.partial(attend_kernel, teams),
        grid=(groups,),
        in_specs=[
            pl.BlockSpec(memory_space=pltpu.SMEM),
            once((rows, width)),
            once((rows, width)),
            once(norms.shape),
            pl.BlockSpec((8, lanes), lambda i: (0, i)),
            once(tables[0].shape),
            once(tables[0].shape),
            once(tables[0].shape),
            pl.BlockSpec((width, lanes), lambda i: (0, i)),
            pl.BlockSpec((width, lanes), lambda i: (0, groups + i)),
            pl.BlockSpec((width, lanes), lambda i: (0, 2 * groups + i)),
            pl.BlockSpec((lanes, width), lambda i: (i, 3)),
            anywhere,
            anywhere,
        ],
        out_specs=[once((rows, width)), anywhere, once((8, width))] + [anywhere] * 4,
        out_shape=[
            jax.ShapeDtypeStruct((rows, width), BF16),
            jax.ShapeDtypeStruct((width, 3 * width), BF16),
            jax.ShapeDtypeStruct((8, width), F32),
            jax.ShapeDtypeStruct((rows, lanes), BF16),
            jax.ShapeDtypeStruct((batch, rows // ring, width - lanes), BF16),
        ]
        + [jax.ShapeDtypeStruct(shape, BF16) for shape in slices],
        scratch_shapes=[
            pltpu.VMEM((rows, width), BF16),
            pltpu.VMEM((rows, width), BF16),
            pltpu.VMEM((width, rows), BF16),
            pltpu.VMEM((rows, width), F32),
        ]
        + [pltpu.VMEM((rows, lanes), BF16)] * 5
        + [pltpu.VMEM((lanes, rows), BF16)] * 2
        + [pltpu.VMEM((rows, lanes), F32)] * 3
        + [
            pltpu.VMEM((groups, 3, width, lanes), BF16), pltpu.VMEM((groups, rows, lanes), BF16),
            dma((groups, ring)), dma((groups, batch)), dma((groups,)), dma((groups, 3)),
        ]
        + reducer_scratch(MLP_LEVELS, shapes, teams, ring),
        compiler_params=pltpu.CompilerParams(
            collective_id=2, has_side_effects=True, vmem_limit_bytes=60 * MIB
        ),
        cost_estimate=pl.CostEstimate(
            flops=24 * rows * width * width + 8 * rows * rows * width,
            bytes_accessed=16 * width * width + 8 * rows * width,
            transcendentals=HEADS * rows * rows // 2,
        ),
        name="attend",
    )(order, x, g, norms, bias_q, *tables, weights, weights, weights, weights, up, down)


def rotary_tables(length):
    half = ROT // 2
    frequency = ROPE_BASE ** (-(np.arange(half) * 2.0 / ROT))
    angle = np.arange(length)[:, None] * frequency[None, :]
    cosine, sine = np.cos(angle), np.sin(angle)
    rest = np.zeros((length, HD - ROT))
    none = np.zeros_like(sine)
    cos_full = np.concatenate([cosine, cosine, rest + 1.0], axis=1)
    low = np.concatenate([-sine, none, rest], axis=1)
    high = np.concatenate([none, sine, rest], axis=1)
    return tuple(jnp.asarray(np.tile(t, (1, 2)).astype(np.float32)) for t in (cos_full, low, high))


def adamw(weight, grad, first, second, rate, decay):
    first_new = BETA_ONE * first + (1.0 - BETA_ONE) * grad
    second_new = BETA_TWO * second + (1.0 - BETA_TWO) * grad * grad
    first_hat = first_new / (1.0 - BETA_ONE**STEP)
    second_hat = second_new / (1.0 - BETA_TWO**STEP)
    weight_new = weight - rate * (first_hat / (jnp.sqrt(second_hat) + EPS_ADAM) + decay * weight)
    return (first_new, second_new, weight_new)


RATES = (0.1, 0.6, 0.1, 0.05)


def finish_kernel(*refs):
    x_ref, g_ref, attend_ref, feed_ref, h_ref, back_ref, bias_ref, norm_grad = refs[:8]
    norm, norm_first, norm_second = refs[8:11]
    inputs, outputs = refs[11:27], refs[27:]
    layer_out, input_grad = outputs[:2]
    for n, rate in enumerate(RATES):
        weight, grad, first, second = (ref[...] for ref in inputs[4 * n : 4 * n + 4])
        new = adamw(weight, grad.astype(F32), first, second, rate, DECAY)
        for ref, value in zip(outputs[2 + 3 * n : 5 + 3 * n], new):
            ref[...] = value
    width = x_ref.shape[1]
    bias = bias_ref[0:1, width : 2 * width] + bias_ref[0:1, bias_ref.shape[1] - width :]
    rows = x_ref[...].astype(F32)
    layer_out[...] = (rows + attend_ref[...] + feed_ref[...] + bias).astype(BF16)
    xh, scale = normalized(rows)
    h = back_ref[...].astype(F32) + h_ref[...]
    inner = jnp.mean(h * xh, axis=-1, keepdims=True)
    input_grad[...] = g_ref[...].astype(F32) + scale * (h - jnp.mean(h, axis=-1, keepdims=True) - xh * inner)

    @pl.when(pl.program_id(0) == 0)
    def _():
        grad = norm_grad[0:4, : norm.shape[1]]
        first, second, new = adamw(norm[...], grad, norm_first[...], norm_second[...], 0.6, 0.0)
        outputs[14][...] = first
        outputs[15][...] = second[0:2]
        outputs[16][...] = second[2:4]
        outputs[17][...] = new


def finish(rows, biases, norm_grad, norm_args, weights):
    steps = 4
    whole = lambda v: pl.BlockSpec(v.shape, lambda i: (0,) * len(v.shape))
    part = lambda v: pl.BlockSpec((v.shape[0] // steps, v.shape[1]), lambda i: (i, 0))
    like = lambda v, dtype: jax.ShapeDtypeStruct(v.shape, dtype)
    count, width = rows[0].shape
    args = [*rows, biases, norm_grad, *norm_args] + [v for group in weights for v in group]
    specs = [part(v) for v in rows] + [whole(v) for v in (biases, norm_grad, *norm_args)]
    specs += [part(v) for group in weights for v in group]
    outs = [like(rows[0], BF16), like(rows[0], F32)] + [like(group[0], F32) for group in weights for _ in range(3)]
    out_specs = [part(v) for v in outs]
    own = norm_args[0].shape[1]
    norm_outs = [jax.ShapeDtypeStruct((n, own), F32) for n in (4, 2, 2, 4)]
    return pl.pallas_call(
        finish_kernel,
        grid=(steps,),
        in_specs=specs,
        out_specs=out_specs + [whole(v) for v in norm_outs],
        out_shape=outs + norm_outs,
        compiler_params=pltpu.CompilerParams(vmem_limit_bytes=56 * MIB),
        cost_estimate=pl.CostEstimate(flops=0, bytes_accessed=64 * MIB, transcendentals=0),
        name="finish",
    )(*args)


def shards(
    tokens, out_grad, block_order, qkv_weight, out_weight, up_weight, down_weight, norm_params, bias_params,
    qkv_first, qkv_second, out_first, out_second, up_first, up_second, down_first, down_second,
    norm_first, norm_second, bias_first, bias_second,
):
    groups, ring = lax.axis_size("dp"), lax.axis_size("ctx")
    group, rank = lax.axis_index("dp"), lax.axis_index("ctx")
    batch, piece, width = tokens.shape
    length = piece * ring
    count = batch * piece
    ff = up_weight.shape[1]

    share = bias_params.shape[0]
    lanes = share + -share % 128
    small = jnp.concatenate([
        jnp.pad(bias_params[None, :], ((0, 0), (0, lanes - share))),
        jnp.pad(norm_params, ((0, 3), (0, lanes - norm_params.shape[1]))),
    ])
    x_rows, g_rows = tokens.reshape(count, width), out_grad.reshape(count, width)
    att_copy, biases, norms, home_x, home_g, feed_out, h_feed, dup, ddown, dbias_up, small_feed = gather_feed(
        up_weight, down_weight, qkv_weight, out_weight, small, x_rows, g_rows, piece, ring * share
    )

    odd = group % 2

    order = block_order[jnp.clip(rank - odd, 0, batch - 1)]
    spots = jnp.arange(order.shape[0])
    order = jnp.stack([order, jnp.sum(jnp.where(order[None, :] == spots[:, None], spots[None, :], 0), axis=1)])

    h_attend, dqkv, small_attend, o_last, o_first, up_slice, down_slice = attend(
        order, home_x, home_g, norms, biases, rotary_tables(length), att_copy, dup, ddown, batch
    )
    *owned, norm_grad, bias_grad, attend_out, ret_back = reduce_all(
        up_slice, down_slice, dqkv, small_attend, small_feed, dbias_up, h_attend, o_last, o_first, g_rows, att_copy, batch
    )
    up_grad, down_grad, qkv_grad, out_grads = (
        g.reshape(w.shape) for g, w in zip(owned, (up_weight, down_weight, qkv_weight, out_weight))
    )
    layer_out, input_grad, *new, norm_a, norm_b, norm_c, norm_d = finish(
        (x_rows, g_rows, attend_out, feed_out, h_feed, ret_back.reshape(count, width)),
        biases,
        norm_grad,
        (norm_params, norm_first, norm_second),
        (
            (qkv_weight, qkv_grad, qkv_first, qkv_second),
            (out_weight, out_grads, out_first, out_second),
            (up_weight, up_grad, up_first, up_second),
            (down_weight, down_grad, down_first, down_second),
        ),
    )
    bias_new = adamw(bias_params, bias_grad[0, :share], bias_first, bias_second, 0.6, 0.0)
    return (
        layer_out.reshape(tokens.shape), input_grad.reshape(tokens.shape), *new,
        norm_a, norm_b, norm_c, norm_d, *bias_new,
    )


def solution(mesh):
    rows, columns, token = P("ctx", None), P(None, "ctx"), P("dp", "ctx", None)
    in_specs = (token, token, P("dp", None)) + (rows,) * 4 + (columns, P("ctx")) + (rows,) * 8
    in_specs += (columns, columns, P("ctx"), P("ctx"))
    out_specs = (token, token) + (rows,) * 12 + (columns,) * 4 + (P("ctx"),) * 3
    return jax.shard_map(shards, mesh=mesh, in_specs=in_specs, out_specs=out_specs, check_vma=False)
```

```python
import functools
import math
from types import SimpleNamespace

import jax
import jax.numpy as jnp
import numpy as np
from jax import lax
from jax.experimental import pallas as pl
from jax.experimental.pallas import tpu as pltpu
from jax.sharding import PartitionSpec as P

HEADS = 12
HD = 64
STEP = 10
ROT = 16
BLOCK = 128
QUAD = 4
MLP_LEVELS = (2, 1)
LEVELS = (3, 3, 0, 0)

EPS_NORM = 1e-05
BETA_ONE = 0.9
BETA_TWO = 0.95
EPS_ADAM = 1e-08
DECAY = 0.01
ROPE_BASE = 10000.0
F32 = jnp.float32
BF16 = jnp.bfloat16
MIB = 1024 * 1024


def dot(left, right, dims=((1,), (0,))):
    return lax.dot_general(left, right, (dims, ((), ())), preferred_element_type=F32)


NN = ((1,), (0,))
NT = ((1,), (1,))
TN = ((0,), (0,))


def normalized(values):
    mean = jnp.mean(values, axis=-1, keepdims=True)
    centred = values - mean
    variance = jnp.mean(centred * centred, axis=-1, keepdims=True)
    scale = lax.rsqrt(variance + EPS_NORM)
    return centred * scale, scale


MESH = pl.DeviceIdType.MESH


def plane(d):
    core, x, y = d % 2, d // 2 % 2, d // 4 % 2
    return core, x, y, d + 1 - 2 * core, d + 2 - 4 * x, d + 4 - 8 * y


def gather_kernel(
    up, down, qkv, out, small, tokens, cotangents,
    att_all, small_all, norm_all, home_x, home_g, out_ref, h_ref, up_part, down_part, dbias_ref, sums_ref,
    up_all, down_all, att_own, up_wide, down_wide, att_wide, small_in, x_ref, g_ref, m_ref, mt_ref, hid_ref, dup_in_ref,
    dup_ref, up_core, up_first, ddown_ref, down_core,
    z_send, z_recv, p_send, p_recv, s_send, s_recv, t_send, t_recv, local, out_sem, c_send, c_recv,
):
    ring = lax.axis_size("ctx")
    d, z = lax.axis_index("dp"), lax.axis_index("ctx")
    core, x, y, core_id, x_id, y_id = plane(d)
    own = x + 2 * y
    own_x, own_y, far = own + 1 - 2 * x, own + 2 - 4 * y, 3 - own
    count, width = tokens.shape
    piece = home_x.shape[0] // ring
    batch = count // piece
    arrays = ((up_wide, up_all, False), (down_wide, down_all, True), (att_own, att_all, False))

    def slot(a, base, place, half=None):
        source, whole, tall = arrays[a]
        ref = source if base is None else whole
        rows, columns = source.shape
        at = 0 if base is None else base * rows
        height, span = rows // 4, columns // 2
        at = at + place * height
        column = core * span
        if half is not None:
            if tall:
                height = height // 2
                at = at + half * height
            else:
                span = span // 2
                column = column + half * span
        return ref.at[pl.ds(pl.multiple_of(at, 16), height), pl.ds(pl.multiple_of(column, 128), span)]

    def other_slot(a, base, place):
        source, whole, tall = arrays[a]
        rows, columns = source.shape
        at = pl.multiple_of(base * rows + place * (rows // 4), 16)
        column = pl.multiple_of((1 - core) * (columns // 2), 128)
        return whole.at[pl.ds(at, rows // 4), pl.ds(column, columns // 2)]

    def remote(src, dst, send, recv, dp, ctx):
        return pltpu.make_async_remote_copy(
            src_ref=src, dst_ref=dst, send_sem=send, recv_sem=recv, device_id=(dp, ctx), device_id_type=MESH
        )

    columns = qkv.shape[1]
    wide_loads = [
        [pltpu.make_async_copy(up, up_wide, local.at[0])],
        [pltpu.make_async_copy(down, down_wide, local.at[1])],
        [
            pltpu.make_async_copy(qkv, att_wide.at[:, pl.ds(0, columns)], local.at[2]),
            pltpu.make_async_copy(out, att_wide.at[:, pl.ds(columns, out.shape[1])], local.at[8]),
        ],
    ]
    for loads in wide_loads:
        for copy in loads:
            copy.start()

    def cast_own(a):
        for copy in wide_loads[a]:
            copy.wait()
        wide, target = ((up_wide, up_all), (down_wide, down_all), (att_wide, att_own))[a]
        rows = wide.shape[0]
        tile = 64
        base = 0 if a == 2 else z * rows

        def body(t, _):
            value = wide[pl.ds(pl.multiple_of(t * tile, 16), tile), :].astype(BF16)
            target[pl.ds(pl.multiple_of(base + t * tile, 16), tile), :] = value
            return 0

        lax.fori_loop(0, rows // tile, body, 0)

    barrier = pltpu.get_barrier_semaphore()
    for k in range(1, ring):
        pl.semaphore_signal(barrier, inc=1, device_id=(d, (z + k) % ring), device_id_type=MESH)
    for other in (core_id, x_id, y_id):
        pl.semaphore_signal(barrier, inc=1, device_id=(other, z), device_id_type=MESH)
    cast_own(0)
    pl.semaphore_wait(barrier, ring + 2)

    def hop(a, way, h):
        shard = z - h if way == 0 else z + h
        target = z + 1 if way == 0 else z - 1
        src = slot(a, None, own) if h == 0 and a == 2 else slot(a, shard, own)
        return remote(src, slot(a, shard, own), z_send.at[a, way, h], z_recv.at[a, way, h], d, target)

    def can_send(way, h):
        shard = z - h if way == 0 else z + h
        target = z + 1 if way == 0 else z - 1
        return (shard >= 0) & (shard < ring) & (target >= 0) & (target < ring)

    def in_range(way, h):
        shard = z - h if way == 0 else z + h
        return (shard >= 0) & (shard < ring)

    def cast(a, shard, j):
        send, recv = p_send.at[a, shard, j], p_recv.at[a, shard, j]
        if j == 0:
            ref = slot(a, shard, own)
            return remote(ref, ref, send, recv, x_id, z)
        if j == 1:
            ref = slot(a, shard, own)
            return remote(ref, ref, send, recv, y_id, z)
        if j == 2:
            ref = slot(a, shard, own_x, 0)
            return remote(ref, ref, send, recv, y_id, z)
        if j == 3:
            ref = slot(a, shard, own_y, 1)
            return remote(ref, ref, send, recv, x_id, z)
        ref = slot(a, shard, (own, own_x, own_y, far)[j - 4])
        return remote(ref, ref, send, recv, core_id, z)

    def arrived(a, shard, j):
        send, recv = p_send.at[a, shard, j], p_recv.at[a, shard, j]
        ref = {0: lambda: slot(a, shard, own_x), 1: lambda: slot(a, shard, own_y),
               2: lambda: slot(a, shard, far, 0), 3: lambda: slot(a, shard, far, 1)}.get(
            j, lambda: other_slot(a, shard, (own, own_x, own_y, far)[j - 4]))()
        remote(ref, ref, send, recv, core_id, z).wait_recv()

    def start_hops(a):
        for way in range(2):
            @pl.when(can_send(way, 0))
            def _(way=way):
                hop(a, way, 0).start()

    def small_copy(k):
        return remote(small, small_in.at[z], s_send.at[k], s_recv.at[k], d, (z + k) % ring)

    def stage_a(a, h):
        for way in range(2):
            @pl.when(in_range(way, h))
            def _(way=way):
                shard = z - h if way == 0 else z + h
                ref = slot(a, shard, own)
                remote(ref, ref, z_send.at[a, way, h - 1], z_recv.at[a, way, h - 1], core_id, z).wait_recv()

                @pl.when(can_send(way, h))
                def _():
                    hop(a, way, h).start()

                cast(a, shard, 0).start()
                cast(a, shard, 1).start()
                cast(a, shard, 4).start()

    def stage_b(a, h):
        for way in range(2):
            @pl.when(in_range(way, h))
            def _(way=way):
                shard = z - h if way == 0 else z + h
                arrived(a, shard, 0)
                cast(a, shard, 2).start()
                cast(a, shard, 5).start()
                arrived(a, shard, 1)
                cast(a, shard, 3).start()
                cast(a, shard, 6).start()

    def stage_c(a, h):
        for way in range(2):
            @pl.when(in_range(way, h))
            def _(way=way):
                shard = z - h if way == 0 else z + h
                arrived(a, shard, 2)
                arrived(a, shard, 3)
                cast(a, shard, 7).start()

    def stage_d(a, h):
        for way in range(2):
            @pl.when(in_range(way, h))
            def _(way=way):
                shard = z - h if way == 0 else z + h
                for j in range(4, 8):
                    arrived(a, shard, j)

    pairs = ((tokens, home_x), (cotangents, home_g))

    def move(which, i):
        source, whole = pairs[which]
        src = source.at[pl.ds(i * piece, piece), :]
        dst = whole.at[pl.ds(pl.multiple_of(z * piece, 16), piece), :]
        return src, dst, i + core

    def start_moves(which):
        for i in range(batch):
            src, dst, target = move(which, i)

            @pl.when(target != z)
            def _(src=src, dst=dst, target=target, i=i):
                remote(src, dst, t_send.at[which, i], t_recv.at[which, z], d, target).start()

            @pl.when(target == z)
            def _(src=src, dst=dst):
                pltpu.make_async_copy(src, dst, local.at[6 + which]).start()

    own_rows = pl.ds(pl.multiple_of(z * att_own.shape[0], 16), att_own.shape[0])
    own_att = pltpu.make_async_copy(att_own, att_all.at[own_rows, :], local.at[9])
    x_load = pltpu.make_async_copy(tokens, x_ref, local.at[3])
    g_load = pltpu.make_async_copy(cotangents, g_ref, local.at[4])
    own_small = pltpu.make_async_copy(small, small_in.at[z], local.at[5])

    start_hops(0)
    cast_own(1)
    start_hops(1)
    cast_own(2)
    start_hops(2)
    for k in range(1, ring):
        small_copy(k).start()
    for copy in (own_att, x_load, g_load, own_small):
        copy.start()
    hops = range(1, ring)
    work = [(a, h) for a in range(2) for h in hops]
    for n in range(len(work) + 2):
        if n < len(work):
            stage_a(*work[n])
        if n == len(work) - 1:
            start_moves(0)
        if 1 <= n <= len(work):
            stage_b(*work[n - 1])
        if n >= 2:
            stage_c(*work[n - 2])
    stage_a(2, 1)

    own_small.wait()
    for k in range(1, ring):
        ref = small_in.at[(z + ring - k) % ring]
        remote(ref, ref, s_send.at[k], s_recv.at[k], core_id, z).wait_recv()
    x_load.wait()
    g_load.wait()
    entries = small_all.shape[1]
    biases = jnp.zeros((8, entries), F32)
    norms = jnp.zeros((8, width), F32)
    for r in range(ring):
        block = small_in[r].astype(BF16).astype(F32)
        full = jnp.concatenate([block, jnp.zeros((8, entries - block.shape[1]), F32)], axis=1)
        biases += pltpu.roll(full, r * (entries // ring), 1) if r else full
        norms += pltpu.roll(block[:, :width], r * (width // ring), 1) if r else block[:, :width]
    small_all[...] = biases
    norm_all[...] = norms
    ff = up_all.shape[1]
    gain_2, shift_2 = norm_all[3:4, :], norm_all[4:5, :]
    tile = 256
    tiles = count // tile
    for t in range(tiles):
        at = pl.ds(t * tile, tile)
        xh, _ = normalized(x_ref[at, :].astype(F32))
        m = xh * gain_2 + shift_2
        m_ref[at, :] = m.astype(BF16)
        mt_ref[:, at] = m.T.astype(BF16)
        out_ref[at, :] = jnp.zeros((tile, width), F32)
        h_ref[at, :] = jnp.zeros((tile, width), F32)
    for h in hops:
        stage_d(0, h)
        stage_d(1, h)

    strip = dup_ref.shape[3] // ring
    steps = ff // (ring * strip)
    half = ring // 2
    big, by_core = (dup_ref, ddown_ref), (up_core, down_core)
    bits, ids = ((x, y), (y, x)), ((x_id, y_id), (y_id, x_id))

    def sizes(a):
        return by_core[a].shape[2], by_core[a].shape[3]

    def slice_of(order):
        return 2 * bits[order][0] + bits[order][1]

    def core_copy(a, i):
        _, span = sizes(a)
        away = pl.ds(pl.multiple_of((1 - core) * span, 128), span)
        return remote(big[a].at[i, :, :, away], by_core[a].at[i], c_send.at[a, i, 0], c_recv.at[a, i, 0], core_id, z)

    def first_copy(a, i, order):
        height, _ = sizes(a)
        own = pl.ds(order * half, half)
        away = pl.ds(pl.multiple_of((1 - bits[order][0]) * (height // 2), 16), height // 2)
        return remote(
            by_core[a].at[i, own, away, :], up_first.at[i, own], c_send.at[a, i, 1 + order],
            c_recv.at[a, i, 1 + order], ids[order][0], z,
        )

    def add(into, at, term, owners):
        height = term(0).shape[0]
        tile = 32 if height % 48 else 48

        def body(n, _):
            o, t = n // (height // tile), n % (height // tile)
            spot = pl.ds(pl.multiple_of(at + t * tile, 16), tile)
            value = term(o)[pl.ds(pl.multiple_of(t * tile, 16), tile), :]
            into[o, spot, :] = (into[o, spot, :].astype(F32) + value.astype(F32)).astype(BF16)
            return 0

        lax.fori_loop(0, owners * (height // tile), body, 0)

    def chunk_1(i):
        for a in range(2):
            _, span = sizes(a)
            core_copy(a, i).wait_recv()
            keep = pl.ds(pl.multiple_of(core * span, 128), span)
            add(by_core[a].at[i], 0, lambda o: big[a].at[i, o, :, keep], ring)
        for order in range(2):
            first_copy(0, i, order).start()
        parts_out(1, i)[0].start()

    def chunk_2(i):
        height, _ = sizes(0)
        for order in range(2):
            own = pl.ds(order * half, half)
            first_copy(0, i, order).wait_recv()
            at = bits[order][0] * (height // 2)
            add(by_core[0].at[i, own], at, lambda o: up_first.at[i, order * half + o], half)
        for copy in parts_out(0, i):
            copy.start()

    def parts_out(a, i):
        height, span = sizes(a)
        if a == 1:
            return [pltpu.make_async_copy(by_core[1].at[i], down_part.at[:, i], out_sem.at[i, 2 * half])]
        copies = []
        for order in range(2):
            own = pl.ds(order * half, half)
            rows = pl.ds(pl.multiple_of(bits[order][0] * (height // 2), 16), height // 2)
            for n in range(half):
                copies.append(pltpu.make_async_copy(
                    by_core[0].at[i, own, rows, pl.ds(n * strip, strip)],
                    up_part.at[own, :, pl.ds(pl.multiple_of(n * steps * strip + i * strip, 128), strip)],
                    out_sem.at[i, half * order + n],
                ))
        return copies

    def feed_step(step, _):
        for h in hops:
            @pl.when(step == h - 1)
            def _(h=h):
                if h + 1 < ring:
                    stage_a(2, h + 1)
                if h == ring - 2:
                    start_moves(1)
                stage_b(2, h)

            @pl.when(step == h)
            def _(h=h):
                stage_c(2, h)

        @pl.when(step < steps)
        def _():
            spots = [pl.ds(pl.multiple_of(r * (ff // ring) + step * strip, 128), strip) for r in range(ring)]
            bias_spots = [
                pl.ds(pl.multiple_of(2 * width + r * (ff // ring) + step * strip, 128), strip) for r in range(ring)
            ]
            up_part_ = jnp.concatenate([up_all[:, at] for at in spots], axis=1)
            down_part_ = jnp.concatenate([down_all[at, :] for at in spots], axis=0)
            bias = jnp.concatenate([small_all[0:1, at] for at in bias_spots], axis=1)
            total = jnp.zeros((1, ring * strip), F32)
            for t in range(tiles):
                at = pl.ds(t * tile, tile)
                u = dot(m_ref[at, :], up_part_) + bias
                cdf = 0.5 * (1.0 + lax.erf(u * (1.0 / math.sqrt(2.0))))
                hidden = (u * cdf).astype(BF16)
                slope = cdf + u * jnp.exp(-0.5 * u * u) * (1.0 / math.sqrt(2.0 * math.pi))
                back = (dot(g_ref[at, :], down_part_, NT) * slope).astype(BF16)
                hid_ref[at, :] = hidden
                dup_in_ref[at, :] = back
                total += jnp.sum(back.astype(F32), axis=0, keepdims=True)
                out_ref[at, :] += dot(hidden, down_part_)
                h_ref[at, :] += dot(back, up_part_, NT)
            for r in range(ring):
                dbias_ref[0:1, spots[r]] = total[:, r * strip : (r + 1) * strip]
            ddown = dot(hid_ref[...], g_ref[...], TN).astype(BF16)
            dup = dot(mt_ref[...], dup_in_ref[...]).astype(BF16)
            for r in range(ring):
                ddown_ref[step, r] = ddown[r * strip : (r + 1) * strip, :]
                dup_ref[step, r] = dup[r * (width // ring) : (r + 1) * (width // ring), :]
            core_copy(0, step).start()
            core_copy(1, step).start()

        for lag, stage in ((1, chunk_1), (3, chunk_2)):
            @pl.when((step >= lag) & (step < steps + lag))
            def _(lag=lag, stage=stage):
                stage(step - lag)

        return 0

    lax.fori_loop(0, steps + 3, feed_step, 0)

    gain = jnp.zeros((1, width), F32)
    shift = jnp.zeros((1, width), F32)
    sums = jnp.zeros((1, width), F32)
    for t in range(tiles):
        at = pl.ds(t * tile, tile)
        xh, _ = normalized(x_ref[at, :].astype(F32))
        dm = h_ref[at, :]
        gain += jnp.sum(dm * xh, axis=0, keepdims=True)
        shift += jnp.sum(dm, axis=0, keepdims=True)
        sums += jnp.sum(g_ref[at, :].astype(F32), axis=0, keepdims=True)
        h_ref[at, :] = dm * gain_2
    sums_ref[...] = jnp.concatenate([gain, shift, sums, jnp.zeros((5, width), F32)], axis=0)

    mine = z - core
    for which in range(2):
        for k in range(1, ring):
            @pl.when((mine >= 0) & (mine < batch))
            def _(which=which, k=k):
                other = (z + k) % ring
                ref = pairs[which][1].at[pl.ds(pl.multiple_of(other * piece, 16), piece), :]
                remote(ref, ref, t_send.at[which, 0], t_recv.at[which, other], core_id, z).wait_recv()
    for h in hops:
        stage_d(2, h)
    for k in range(1, ring):
        small_copy(k).wait_send()
    for a in range(3):
        for way in range(2):
            for h in range(ring - 1):
                @pl.when(can_send(way, h))
                def _(a=a, way=way, h=h):
                    hop(a, way, h).wait_send()
        for h in hops:
            for way in range(2):
                @pl.when(in_range(way, h))
                def _(a=a, h=h, way=way):
                    shard = z - h if way == 0 else z + h
                    for j in range(8):
                        cast(a, shard, j).wait_send()
    for which in range(2):
        for i in range(batch):
            src, dst, target = move(which, i)

            @pl.when(target != z)
            def _(src=src, dst=dst, target=target, which=which, i=i):
                remote(src, dst, t_send.at[which, i], t_recv.at[which, z], d, target).wait_send()

            @pl.when(target == z)
            def _(src=src, dst=dst, which=which):
                pltpu.make_async_copy(src, dst, local.at[6 + which]).wait()
    own_att.wait()

    def close(i, _):
        for a in range(2):
            core_copy(a, i).wait_send()
            for copy in parts_out(a, i):
                copy.wait()
        for order in range(2):
            first_copy(0, i, order).wait_send()
        return 0

    lax.fori_loop(0, steps, close, 0)


def gather_feed(up, down, qkv, out, small, tokens, cotangents, piece, entries):
    ring = lax.axis_size("ctx")
    count, width = tokens.shape
    ff = up.shape[1]
    strip = 128
    chunk = ring * strip
    steps = ff // chunk
    shard = up.shape[0]
    columns = qkv.shape[1] + out.shape[1]
    home = jax.ShapeDtypeStruct((ring * piece, width), tokens.dtype)
    rows = jax.ShapeDtypeStruct((count, width), F32)
    dma = pltpu.SemaphoreType.DMA
    anywhere = pl.BlockSpec(memory_space=pl.ANY)
    vmem = pl.BlockSpec(memory_space=pltpu.VMEM)
    return pl.pallas_call(
        gather_kernel,
        in_specs=[anywhere] * 7,
        out_specs=[anywhere, vmem, vmem, anywhere, anywhere, vmem, vmem, anywhere, anywhere, vmem, vmem],
        out_shape=[
            jax.ShapeDtypeStruct((ring * shard, columns), BF16),
            jax.ShapeDtypeStruct((8, entries), F32), jax.ShapeDtypeStruct((8, width), F32), home, home, rows, rows,
            jax.ShapeDtypeStruct((ring, shard // 2, ff // 2), BF16),
            jax.ShapeDtypeStruct((ring, steps, strip, width // 2), BF16),
            jax.ShapeDtypeStruct((8, ff), F32), jax.ShapeDtypeStruct((8, width), F32),
        ],
        scratch_shapes=[
            pltpu.VMEM((ring * shard, ff), BF16), pltpu.VMEM((ring * down.shape[0], width), BF16),
            pltpu.VMEM((shard, columns), BF16),
            pltpu.VMEM(up.shape, F32), pltpu.VMEM(down.shape, F32), pltpu.VMEM((shard, columns), F32),
            pltpu.VMEM((ring, *small.shape), F32),
            pltpu.VMEM((count, width), BF16), pltpu.VMEM((count, width), BF16), pltpu.VMEM((count, width), BF16),
            pltpu.VMEM((width, count), BF16),
            pltpu.VMEM((count, chunk), BF16), pltpu.VMEM((count, chunk), BF16),
            pltpu.VMEM((steps, ring, shard, chunk), BF16), pltpu.VMEM((steps, ring, shard, chunk // 2), BF16),
            pltpu.VMEM((steps, ring, shard // 2, chunk // 2), BF16),
            pltpu.VMEM((steps, ring, strip, width), BF16), pltpu.VMEM((steps, ring, strip, width // 2), BF16),
            dma((3, 2, ring)), dma((3, 2, ring)), dma((3, ring, 8)), dma((3, ring, 8)),
            dma((ring,)), dma((ring,)), dma((2, count // piece)), dma((2, ring)), dma((10,)), dma((steps, ring + 1)),
            dma((2, steps, 3)), dma((2, steps, 3)),
        ],
        compiler_params=pltpu.CompilerParams(
            collective_id=0, has_side_effects=True, vmem_limit_bytes=60 * MIB
        ),
        cost_estimate=pl.CostEstimate(
            flops=12 * count * width * ff, bytes_accessed=60 * MIB, transcendentals=count * ff
        ),
        name="gather_feed",
    )(up, down, qkv, out, small, tokens, cotangents)


def remote(src, dst, send_sem, recv_sem, dp, ctx):
    return pltpu.make_async_remote_copy(
        src_ref=src, dst_ref=dst, send_sem=send_sem, recv_sem=recv_sem, device_id=(dp, ctx), device_id_type=MESH
    )


def team_id(d, t):
    return d + (8 << t) * (1 - 2 * (d // (8 << t) % 2))


def greet(teams):
    ring = lax.axis_size("ctx")
    d, z = lax.axis_index("dp"), lax.axis_index("ctx")
    core, x, y, core_id, x_id, y_id = plane(d)
    barrier = pltpu.get_barrier_semaphore()
    partners = [core_id, x_id, y_id, x_id + y_id - d] + [team_id(d, t) for t in range(teams)]
    for k in range(1, ring):
        pl.semaphore_signal(barrier, inc=1, device_id=(d, (z + k) % ring), device_id_type=MESH)
    for other in partners:
        pl.semaphore_signal(barrier, inc=1, device_id=(other, z), device_id_type=MESH)
    pl.semaphore_wait(barrier, ring - 1 + len(partners))


def reducer(teams, levels, ins, sums, bufs, send, recv, load):
    count = len(ins)
    ring = lax.axis_size("ctx")
    d, z = lax.axis_index("dp"), lax.axis_index("ctx")
    core, x, y, core_id, x_id, y_id = plane(d)
    far_id = x_id + y_id - d
    bits, ids = ((x, y), (y, x)), ((x_id, y_id), (y_id, x_id))
    spots = ((x, y), (1 - x, y), (x, 1 - y), (1 - x, 1 - y))

    def sizes(a):
        _, strips, quarter, span = bufs[a][-1].shape
        return strips, quarter, span

    def owners(a, order):
        strips = sizes(a)[0]
        return pl.ds(order * ring // 2 * strips, ring // 2 * strips)

    def rows_at(at, height):
        return pl.ds(pl.multiple_of(at, 16), height)

    def kept(a, order):
        return 0 if levels[a] == 2 else bits[order][0] * 2 * sizes(a)[1]

    def core_copy(a):
        span = sizes(a)[2]
        away = pl.ds(pl.multiple_of((1 - core) * span, 128), span)
        return remote(ins[a].at[:, :, away], bufs[a][1], send.at[a, 0], recv.at[a, 0], core_id, z)

    def own_load(a):
        if levels[a] == 3:
            return pltpu.make_async_copy(ins[a], bufs[a][5].at[0], load.at[a])
        span = sizes(a)[2]
        keep = pl.ds(pl.multiple_of(core * span, 128), span)
        src = ins[a].at[:, :, keep] if levels[a] == 0 else ins[a]
        return pltpu.make_async_copy(src, bufs[a][0], load.at[a])

    def first_copy(a, order):
        quarter = sizes(a)[1]
        away = rows_at((1 - bits[order][0]) * 2 * quarter, 2 * quarter)
        return remote(
            bufs[a][0].at[owners(a, order), away, :], bufs[a][2].at[owners(a, order)], send.at[a, 1 + order],
            recv.at[a, 1 + order], ids[order][0], z,
        )

    def second_copy(a, order):
        quarter = sizes(a)[1]
        away = rows_at(kept(a, order) + (1 - bits[order][1]) * quarter, quarter)
        return remote(
            bufs[a][0].at[owners(a, order), away, :], bufs[a][3].at[owners(a, order)], send.at[a, 3 + order],
            recv.at[a, 3 + order], ids[order][1], z,
        )

    def own_quarter(a, owner):
        strips, quarter, _ = sizes(a)
        order = owner // (ring // 2)
        first, second = (1 - order) * x + order * y, (1 - order) * y + order * x
        at = second * quarter if levels[a] == 2 else (2 * first + second) * quarter
        return bufs[a][0].at[pl.ds(owner * strips, strips), rows_at(at, quarter), :]

    def owner_copy(a, k):
        to = (z + k) % ring
        return remote(own_quarter(a, to), bufs[a][4].at[k - 1], send.at[a, 4 + k], recv.at[a, 4 + k], d, to)

    def team_copy(a, t):
        j = 4 + ring + 7 + t
        return remote(bufs[a][5].at[0], bufs[a][5].at[1 + t], send.at[a, j], recv.at[a, j], team_id(d, t), z)

    def final(a, spot, side):
        strips, quarter, span = sizes(a)
        order = z // (ring // 2)
        xx, yy = spots[spot]
        at = ((1 - order) * (2 * xx + yy) + order * (2 * yy + xx)) * quarter
        return sums[a].at[:, rows_at(at, quarter), pl.ds(pl.multiple_of(side * span, 128), span)]

    def spread(a, j):
        s, r = send.at[a, 4 + ring + j - 1], recv.at[a, 4 + ring + j - 1]
        if j < 4:
            return remote(bufs[a][5].at[0], final(a, 0, core), s, r, (x_id, y_id, far_id)[j - 1], z)
        src = bufs[a][5].at[0] if j == 4 else final(a, j - 4, core)
        return remote(src, final(a, j - 4, core), s, r, core_id, z)

    def spread_here(a, j):
        s, r = send.at[a, 4 + ring + j - 1], recv.at[a, 4 + ring + j - 1]
        ref = final(a, j, core) if j < 4 else final(a, j - 4, 1 - core)
        remote(ref, ref, s, r, core_id, z).wait_recv()

    def keep_own(a):
        return pltpu.make_async_copy(bufs[a][5].at[0], final(a, 0, core), load.at[count + a])

    def add(into, at, term, blocks):
        height = term.shape[1]
        tile = 32 if height % 48 else 48

        def body(n, _):
            o, t = n // (height // tile), n % (height // tile)
            spot = rows_at(at + t * tile, tile)
            value = term[o, rows_at(t * tile, tile), :]
            into[o, spot, :] = (into[o, spot, :].astype(F32) + value.astype(F32)).astype(BF16)
            return 0

        lax.fori_loop(0, blocks * (height // tile), body, 0)

    def enter(a):
        if levels[a] == 0:
            core_copy(a).start()
        own_load(a).start()

    def first(a):
        own_load(a).wait()
        if levels[a] == 0:
            core_copy(a).wait_recv()
            add(bufs[a][0], 0, bufs[a][1], bufs[a][0].shape[0])
        if levels[a] < 2:
            for order in range(2):
                first_copy(a, order).start()

    def second(a):
        for order in range(2):
            if levels[a] < 2:
                first_copy(a, order).wait_recv()
                own = owners(a, order)
                add(bufs[a][0].at[own], kept(a, order), bufs[a][2].at[own], ring // 2 * sizes(a)[0])
            second_copy(a, order).start()

    def to_owner(a):
        for order in range(2):
            second_copy(a, order).wait_recv()
            own = owners(a, order)
            at = kept(a, order) + bits[order][1] * sizes(a)[1]
            add(bufs[a][0].at[own], at, bufs[a][3].at[own], ring // 2 * sizes(a)[0])
        for k in range(1, ring):
            owner_copy(a, k).start()

    def add_up(a):
        for k in range(1, ring):
            owner_copy(a, k).wait_recv()
        mine = own_quarter(a, z)
        for s in range(sizes(a)[0]):
            terms = [mine[s]] + [bufs[a][4][k, s] for k in range(ring - 1)]
            bufs[a][5][0, s] = sum((t.astype(F32) for t in terms[1:]), terms[0].astype(F32)).astype(BF16)
        for t in range(teams):
            team_copy(a, t).start()
            team_copy(a, t).wait()
            bufs[a][5][0] = (bufs[a][5][0].astype(F32) + bufs[a][5][1 + t].astype(F32)).astype(BF16)

    def total(a):
        if levels[a] == 3:
            own_load(a).wait()
        else:
            add_up(a)
        keep_own(a).start()
        for j in range(1, 5):
            spread(a, j).start()

    def hand_on(a):
        add_up(a)
        out = pltpu.make_async_copy(bufs[a][5].at[0], sums[a], load.at[count + a])
        out.start()
        sent(a)
        out.wait()

    def share(a):
        for j in range(1, 4):
            spread_here(a, j)
            spread(a, 4 + j).start()

    def sent(a):
        if levels[a] == 0:
            core_copy(a).wait_send()
        for order in range(2):
            if levels[a] < 2:
                first_copy(a, order).wait_send()
            second_copy(a, order).wait_send()
        for k in range(1, ring):
            owner_copy(a, k).wait_send()

    def close(a):
        for j in range(4, 8):
            spread_here(a, j)
        if levels[a] < 3:
            sent(a)
        for j in range(1, 8):
            spread(a, j).wait_send()
        keep_own(a).wait()

    return SimpleNamespace(
        enter=enter, first=first, second=second, to_owner=to_owner, total=total, hand_on=hand_on, share=share, close=close
    )


def reducer_scratch(levels, shapes, teams, ring):
    scratch = []
    for level, (strips, rows, columns) in zip(levels, shapes):
        blocks, span = ring * strips, columns // 2
        none = (1, 16, 128)
        scratch += [
            pltpu.VMEM(none if level == 3 else (blocks, rows // 2 if level == 2 else rows, span), BF16),
            pltpu.VMEM((blocks, rows, span) if level == 0 else none, BF16),
            pltpu.VMEM((blocks, rows // 2, span) if level < 2 else none, BF16),
            pltpu.VMEM((blocks, rows // 4, span) if level < 3 else none, BF16),
            pltpu.VMEM((ring - 1, strips, rows // 4, span) if level < 3 else (1, *none), BF16),
            pltpu.VMEM((1 + teams, strips, rows // 4, span), BF16),
        ]
    copies = 4 + ring + 7 + teams
    dma = pltpu.SemaphoreType.DMA
    return scratch + [dma((len(levels), copies)), dma((len(levels), copies)), dma((2 * len(levels),))]


def reduce_kernel(
    teams, up_ref, down_ref, qkv_ref, small_att, small_mlp, small_up, back_ref, o_last, o_ref, g_ref, weights,
    up_sum, down_sum, qkv_sum, out_sum, norm_out, bias_out, attend_out, ret_back, *refs,
):
    ring = lax.axis_size("ctx")
    d, z = lax.axis_index("dp"), lax.axis_index("ctx")
    core, x, y, core_id, x_id, y_id = plane(d)
    bufs = [refs[6 * a : 6 * a + 6] for a in range(4)]
    send, recv, load, o_in, wo_ref, dwo_ref, small_acc, small_in = refs[24:32]
    s_send, s_recv, r_send, r_recv, r_local = refs[32:]
    batch, piece, width = ret_back.shape
    lanes = o_last.shape[1]
    up, down, qkv, out = range(4)
    ins, sums = (up_ref, down_ref, qkv_ref, dwo_ref), (up_sum, down_sum, qkv_sum, out_sum)
    do = reducer(teams, LEVELS, ins, sums, bufs, send, recv, load)

    pairs = ((o_last, o_in), (back_ref, ret_back))
    mine = z - core

    def returned(which, i, to):
        source, target = pairs[which]
        return source.at[pl.ds(pl.multiple_of(to * piece, 16), piece), :], target.at[i]

    def start_returns(which):
        for i in range(batch):
            @pl.when(mine == i)
            def _(i=i):
                for k in range(1, ring):
                    to = (z + k) % ring
                    src, dst = returned(which, i, to)
                    remote(src, dst, r_send.at[which, k], r_recv.at[which, i], d, to).start()
                src, dst = returned(which, i, z)
                pltpu.make_async_copy(src, dst, r_local.at[which]).start()

    def wait_returns(which):
        for i in range(batch):
            src, dst = returned(which, i, z)

            @pl.when(mine == i)
            def _(src=src, dst=dst):
                pltpu.make_async_copy(src, dst, r_local.at[which]).wait()

            @pl.when(mine != i)
            def _(i=i, src=src, dst=dst):
                remote(src, dst, r_send.at[which, 0], r_recv.at[which, i], core_id, z).wait_recv()

    def close_returns(which):
        for i in range(batch):
            @pl.when(mine == i)
            def _(i=i):
                for k in range(1, ring):
                    to = (z + k) % ring
                    remote(*returned(which, i, to), r_send.at[which, k], r_recv.at[which, i], d, to).wait_send()

    steps = [core_id, x_id, y_id] + [team_id(d, t) for t in range(teams)]

    def small_copy(n):
        return remote(small_acc, small_in.at[n], s_send.at[n], s_recv.at[n], steps[n], z)

    def small_owner(k):
        n = len(steps) + k - 1
        return remote(small_acc, small_in.at[n], s_send.at[n], s_recv.at[n], d, (z + k) % ring)

    def small_close(n):
        small_copy(n).wait()
        small_acc[...] += small_in[n]
        if n + 1 < len(steps):
            small_copy(n + 1).start()
        else:
            for k in range(1, ring):
                small_owner(k).start()

    columns = weights.shape[1] - width
    wo_load = pltpu.make_async_copy(weights.at[:, pl.ds(columns, width)], wo_ref, r_local.at[2])
    wo_load.start()
    small_acc[0:8, :] = small_att[...]
    small_acc[8:16, :] = small_mlp[...]
    for n in range(small_up.shape[1] // width):
        small_acc[16 + n : 17 + n, :] = small_up[0:1, n * width : (n + 1) * width]
    rest = 16 + small_up.shape[1] // width
    small_acc[rest:, :] = jnp.zeros((small_acc.shape[0] - rest, width), F32)
    greet(teams)
    do.enter(qkv)
    start_returns(0)
    start_returns(1)
    do.enter(up)
    do.enter(down)
    small_copy(0).start()
    do.total(up)
    do.total(down)
    do.first(qkv)
    small_close(0)
    do.share(up)
    do.share(down)

    wo_load.wait()
    wait_returns(0)
    split = o_ref.shape[1]
    for i in range(batch):
        at = pl.ds(i * piece, piece)
        attend_out[at, :] = dot(o_ref[at, :], wo_ref[:split, :]) + dot(o_in[i], wo_ref[split:, :])
    late = jnp.concatenate([o_in[i] for i in range(batch)], axis=0)
    dwo = jnp.concatenate([dot(o_ref[...], g_ref[...], TN), dot(late, g_ref[...], TN)], axis=0).astype(BF16)
    for r in range(ring):
        dwo_ref[r] = dwo[r * (width // ring) : (r + 1) * (width // ring), :]
    do.enter(out)
    do.second(qkv)
    do.first(out)
    small_close(1)
    do.to_owner(qkv)
    do.second(out)
    for n in range(2, len(steps)):
        small_close(n)
    do.total(qkv)
    do.to_owner(out)
    do.share(qkv)
    do.total(out)
    for k in range(1, ring):
        small_owner(k).wait()
    total = small_acc[...]
    for k in range(ring - 1):
        total += small_in[len(steps) + k]
    norm = jnp.concatenate([total[0:2], total[8:10], jnp.zeros((4, width), F32)], axis=0)
    norm_out[...] = pltpu.roll(norm, (ring - z) % ring * (width // ring), 1)
    ups = [total[16 + n : 17 + n] for n in range(small_up.shape[1] // width)]
    bias = jnp.concatenate([total[2:3], total[10:11], *ups, total[10:11]], axis=1)
    entries = bias.shape[1]
    bias = pltpu.roll(jnp.broadcast_to(bias, (8, entries)), (ring - z) % ring * (entries // ring), 1)
    bias_out[...] = bias[:, : bias_out.shape[1]]
    do.share(out)
    for a in range(4):
        do.close(a)
    wait_returns(1)
    close_returns(0)
    close_returns(1)


def reduce_all(up, down, qkv, small_att, small_mlp, small_up, back, o_last, o_first, g, weights, batch):
    ring, groups = lax.axis_size("ctx"), lax.axis_size("dp")
    teams = (groups // 8).bit_length() - 1
    width = g.shape[1]
    piece = g.shape[0] // batch
    shapes = [(n, 4 * rows, 2 * span) for n, rows, span in (up.shape, down.shape)]
    shapes += [(1, width // ring, qkv.shape[1]), (1, width // ring, width)]
    dma = pltpu.SemaphoreType.DMA
    anywhere = pl.BlockSpec(memory_space=pl.ANY)
    vmem = pl.BlockSpec(memory_space=pltpu.VMEM)
    rounds = 3 + teams + ring - 1
    small = (16 + -(-small_up.shape[1] // width // 8) * 8, width)
    share = (3 * width + small_up.shape[1]) // ring
    scratch = reducer_scratch(LEVELS, shapes, teams, ring)
    scratch += [
        pltpu.VMEM((batch, piece, o_last.shape[1]), BF16), pltpu.VMEM((width, width), BF16),
        pltpu.VMEM((ring, width // ring, width), BF16), pltpu.VMEM(small, F32), pltpu.VMEM((rounds, *small), F32),
        dma((rounds,)), dma((rounds,)), dma((2, ring)), dma((2, batch)), dma((3,)),
    ]
    return pl.pallas_call(
        functools.partial(reduce_kernel, teams),
        in_specs=[anywhere] * 3 + [vmem] * 3 + [anywhere, anywhere, vmem, vmem, anywhere],
        out_specs=[anywhere] * 4 + [vmem, vmem, vmem, anywhere],
        out_shape=[jax.ShapeDtypeStruct(shape, BF16) for shape in shapes]
        + [
            jax.ShapeDtypeStruct((8, width), F32), jax.ShapeDtypeStruct((8, share + -share % 128), F32),
            jax.ShapeDtypeStruct(g.shape, F32),
            jax.ShapeDtypeStruct((batch, piece, width), BF16),
        ],
        scratch_shapes=scratch,
        compiler_params=pltpu.CompilerParams(collective_id=1, has_side_effects=True, vmem_limit_bytes=56 * MIB),
        cost_estimate=pl.CostEstimate(flops=4 * width * width * g.shape[0], bytes_accessed=60 * MIB, transcendentals=0),
        name="reduce",
    )(
        up, down, qkv.reshape(ring, width // ring, -1), small_att, small_mlp, small_up, back, o_last,
        o_first.reshape(batch * piece, -1), g, weights,
    )


def attend_kernel(
    teams, order_ref, x_ref, stored_g_ref, norm_ref, bias_ref, cos_ref, low_ref, high_ref, wq_ref, wk_ref, wv_ref,
    wo_ref, up_ref, down_ref, h_ref, dqkv_all, small_ref, o_last, ret_o, up_sum, down_sum,
    g_ref, a_ref, at_ref, da_ref, q_ref, k_ref, v_ref, do_ref, o_ref, kt_ref, vt_ref, dqs_ref, dks_ref, dvs_ref,
    grad_ref, stored_o_ref, o_send, o_recv, o_local, grad_sem, *reduce_refs,
):
    step = pl.program_id(0)
    last = grad_ref.shape[0] - 1
    rows, width = x_ref.shape
    lanes = QUAD * HD
    tile = 256
    half = ROT // 2
    scale = 1.0 / math.sqrt(HD)
    blocks = rows // BLOCK
    ring = lax.axis_size("ctx")
    d, z = lax.axis_index("dp"), lax.axis_index("ctx")
    core_id = plane(d)[3]
    batch, piece = ret_o.shape[:2]
    mine = z - d % 2
    is_home = (mine >= 0) & (mine < batch)
    up, down = 0, 1
    bufs = (reduce_refs[:6], reduce_refs[6:12])
    do_sum = reducer(teams, MLP_LEVELS, (up_ref, down_ref), (up_sum, down_sum), bufs, *reduce_refs[12:])

    @pl.when(step == 0)
    def _():
        do_sum.enter(down)
        do_sum.enter(up)
        greet(teams)
        do_sum.first(down)
        do_sum.first(up)
        do_sum.second(up)

    def o_copy(quad, k, i):
        to = (z + k) % ring
        src = stored_o_ref.at[quad, pl.ds(pl.multiple_of(to * piece, 16), piece), :]
        dst = ret_o.at[i, :, pl.ds(pl.multiple_of(quad * lanes, 128), lanes)]
        if k == 0:
            return pltpu.make_async_copy(src, dst, o_local.at[quad])
        return remote(src, dst, o_send.at[quad, k], o_recv.at[quad, i], d, to)

    def grad_copy(quad, j):
        at = pl.ds(pl.multiple_of(j * width + quad * lanes, 128), lanes)
        return pltpu.make_async_copy(grad_ref.at[quad, j], dqkv_all.at[:, at], grad_sem.at[quad, j])


    def stored(ref, at):
        values = ref[pl.ds(at * BLOCK, BLOCK), :]
        return jnp.where(is_home, values, jnp.zeros_like(values))

    @pl.when(step == 0)
    def _():
        for j in range(blocks):
            place = order_ref[1, j]
            at = pl.ds(j * BLOCK, BLOCK)
            xh, _ = normalized(stored(x_ref, place).astype(F32))
            a = xh * norm_ref[1:2, :] + norm_ref[2:3, :]
            a_ref[at, :] = a.astype(BF16)
            at_ref[:, at] = a.T.astype(BF16)
            g_ref[at, :] = stored(stored_g_ref, place)
        da_ref[...] = jnp.zeros_like(da_ref)

    def table(ref, at):
        values = ref[at, :]
        return jnp.concatenate([values] * (lanes // values.shape[1]), axis=1)

    def turn(values, at):
        low = pltpu.roll(values, lanes - half, 1) * table(low_ref, at)
        high = pltpu.roll(values, half, 1) * table(high_ref, at)
        return values * table(cos_ref, at), low + high

    for t in range(rows // tile):
        at = pl.ds(t * tile, tile)
        a = a_ref[at, :]
        same, cross = turn(dot(a, wq_ref[...]) + bias_ref[0:1, :], at)
        q_ref[at, :] = ((same + cross).astype(BF16) * scale).astype(BF16)
        same, cross = turn(dot(a, wk_ref[...]), at)
        keys = same + cross
        k_ref[at, :] = keys.astype(BF16)
        kt_ref[:, at] = keys.T.astype(BF16)
        values = dot(a, wv_ref[...])
        v_ref[at, :] = values.astype(BF16)
        vt_ref[:, at] = values.T.astype(BF16)
        mixed_back = dot(g_ref[at, :], wo_ref[...], NT)
        do_ref[at, :] = mixed_back.astype(BF16)

    dks_ref[...] = jnp.zeros_like(dks_ref)
    dvs_ref[...] = jnp.zeros_like(dvs_ref)
    wide = 2 * HD
    head_of = lax.broadcasted_iota(jnp.int32, (BLOCK, wide), 1) // HD

    def stack(values):
        zero = jnp.zeros_like(values)
        return jnp.concatenate([jnp.where(head_of == e, values, zero) for e in range(2)], axis=0)

    def diagonal(values):
        return jnp.concatenate([values[e * HD : (e + 1) * HD, e * BLOCK : (e + 1) * BLOCK] for e in range(2)], axis=0)

    spot = lax.broadcasted_iota(jnp.int32, (BLOCK, 2 * BLOCK), 1) % BLOCK
    admitted = lax.broadcasted_iota(jnp.int32, (BLOCK, 2 * BLOCK), 0) <= spot

    def products_in(b, p):
        at, seen, own = pl.ds(b * BLOCK, BLOCK), pl.ds(0, (b + 1) * BLOCK), pl.ds(p * wide, wide)
        q, do = stack(q_ref[at, own]), stack(do_ref[at, own])
        return q, do, dot(k_ref[seen, own], q, NT), dot(v_ref[seen, own], do, NT)

    def softmax(b, scores, back):
        edge = jnp.where(admitted, scores[b * BLOCK :], -1e30)
        scores = edge if b == 0 else jnp.concatenate([scores[: b * BLOCK], edge], axis=0)
        top = jnp.max(scores, axis=0, keepdims=True)
        expo = jnp.exp(scores - top)
        probs = expo * (1.0 / jnp.sum(expo, axis=0, keepdims=True))
        share = jnp.sum(probs * back, axis=0, keepdims=True)
        return probs.astype(BF16), (probs * (back - share)).astype(BF16)

    def products_out(b, p, q, do, low, back):
        at, seen, own = pl.ds(b * BLOCK, BLOCK), pl.ds(0, (b + 1) * BLOCK), pl.ds(p * wide, wide)
        mixed = diagonal(dot(vt_ref[own, seen], low))
        o_ref[at, own] = mixed.T.astype(BF16)
        dqs_ref[at, own] = diagonal(dot(kt_ref[own, seen], back)).T * scale
        dks_ref[seen, own] += dot(back, q)
        dvs_ref[seen, own] += dot(low, do)

    units = [(b, p) for b in range(rows // BLOCK) for p in range(lanes // wide)]
    ready = products_in(*units[0])
    done = None
    for n, (b, p) in enumerate(units):
        q, do, scores, back = ready
        if n + 1 < len(units):
            ready = products_in(*units[n + 1])
        low, back = softmax(b, scores, back)
        if done is not None:
            products_out(*done)
        done = (b, p, q, do, low, back)
    products_out(*done)

    total = jnp.zeros((1, lanes), F32)
    for t in range(rows // tile):
        at = pl.ds(t * tile, tile)
        same, cross = turn(dqs_ref[at, :], at)
        dq = (same - cross).astype(BF16)
        same, cross = turn(dks_ref[at, :], at)
        dk = (same - cross).astype(BF16)
        dv = dvs_ref[at, :].astype(BF16)
        total += jnp.sum(dq.astype(F32), axis=0, keepdims=True)
        q_ref[at, :] = dq
        k_ref[at, :] = dk
        v_ref[at, :] = dv
        da_ref[at, :] += dot(dq, wq_ref[...], NT) + dot(dk, wk_ref[...], NT) + dot(dv, wv_ref[...], NT)
    small_ref[2:3, pl.ds(pl.multiple_of(step * lanes, 128), lanes)] = total
    for j, ref in enumerate((q_ref, k_ref, v_ref)):
        grad_ref[step, j] = dot(at_ref[...], ref[...]).astype(BF16)
        grad_copy(step, j).start()
    for s in range(blocks):
        stored_o_ref[step, s * BLOCK : (s + 1) * BLOCK, :] = o_ref[pl.ds(order_ref[0, s] * BLOCK, BLOCK), :]

    for i in range(batch):
        @pl.when((mine == i) & (step < last))
        def _(i=i):
            for k in range(ring):
                o_copy(step, k, i).start()

    @pl.when(step == 0)
    def _():
        do_sum.second(down)
        do_sum.to_owner(up)

    @pl.when(step == 1)
    def _():
        do_sum.to_owner(down)

    @pl.when(step == last)
    def _():
        gain = jnp.zeros((1, width), F32)
        shift = jnp.zeros((1, width), F32)
        for s in range(blocks):
            at = pl.ds(s * BLOCK, BLOCK)
            sorted_at = pl.ds(order_ref[0, s] * BLOCK, BLOCK)
            xh, _ = normalized(stored(x_ref, s).astype(F32))
            da = da_ref[sorted_at, :]
            gain += jnp.sum(da * xh, axis=0, keepdims=True)
            shift += jnp.sum(da, axis=0, keepdims=True)
            h_ref[at, :] = (da * norm_ref[1:2, :]).astype(BF16)
        small_ref[0:1, :] = gain
        small_ref[1:2, :] = shift
        small_ref[3:8, :] = jnp.zeros((5, width), F32)
        out = pltpu.make_async_copy(stored_o_ref.at[last], o_last, o_local.at[last])
        out.start()
        do_sum.hand_on(up)
        do_sum.hand_on(down)
        for quad in range(last):
            for i in range(batch):
                @pl.when(mine != i)
                def _(quad=quad, i=i):
                    ref = ret_o.at[i, :, pl.ds(quad * lanes, lanes)]
                    remote(ref, ref, o_send.at[quad, 0], o_recv.at[quad, i], core_id, z).wait_recv()

                @pl.when(mine == i)
                def _(quad=quad, i=i):
                    o_copy(quad, 0, i).wait()
                    for k in range(1, ring):
                        o_copy(quad, k, i).wait_send()
        for quad in range(last + 1):
            for j in range(3):
                grad_copy(quad, j).wait()
        out.wait()


def attend(order, x, g, norms, bias_q, tables, weights, up, down, batch):
    ring, groups_dp = lax.axis_size("ctx"), lax.axis_size("dp")
    teams = (groups_dp // 8).bit_length() - 1
    shapes = ((1, 2 * up.shape[1], 2 * up.shape[2]), (down.shape[1], down.shape[2], 2 * down.shape[3]))
    down = down.reshape(-1, *down.shape[2:])
    rows, width = x.shape
    lanes = QUAD * HD
    groups = width // lanes
    anywhere = pl.BlockSpec(memory_space=pl.ANY)
    whole = lambda shape: pl.BlockSpec(shape, lambda i: (0,) * len(shape))
    once = lambda shape: pl.BlockSpec(shape, lambda i: (0,) * len(shape), pipeline_mode=pl.Buffered(1))
    dma = pltpu.SemaphoreType.DMA
    slices = [(n, r // 4, c // 2) for n, r, c in shapes]
    return pl.pallas_call(
        functools.partial(attend_kernel, teams),
        grid=(groups,),
        in_specs=[
            pl.BlockSpec(memory_space=pltpu.SMEM),
            once((rows, width)),
            once((rows, width)),
            once(norms.shape),
            pl.BlockSpec((8, lanes), lambda i: (0, i)),
            once(tables[0].shape),
            once(tables[0].shape),
            once(tables[0].shape),
            pl.BlockSpec((width, lanes), lambda i: (0, i)),
            pl.BlockSpec((width, lanes), lambda i: (0, groups + i)),
            pl.BlockSpec((width, lanes), lambda i: (0, 2 * groups + i)),
            pl.BlockSpec((lanes, width), lambda i: (i, 3)),
            anywhere,
            anywhere,
        ],
        out_specs=[once((rows, width)), anywhere, once((8, width))] + [anywhere] * 4,
        out_shape=[
            jax.ShapeDtypeStruct((rows, width), BF16),
            jax.ShapeDtypeStruct((width, 3 * width), BF16),
            jax.ShapeDtypeStruct((8, width), F32),
            jax.ShapeDtypeStruct((rows, lanes), BF16),
            jax.ShapeDtypeStruct((batch, rows // ring, width - lanes), BF16),
        ]
        + [jax.ShapeDtypeStruct(shape, BF16) for shape in slices],
        scratch_shapes=[
            pltpu.VMEM((rows, width), BF16),
            pltpu.VMEM((rows, width), BF16),
            pltpu.VMEM((width, rows), BF16),
            pltpu.VMEM((rows, width), F32),
        ]
        + [pltpu.VMEM((rows, lanes), BF16)] * 5
        + [pltpu.VMEM((lanes, rows), BF16)] * 2
        + [pltpu.VMEM((rows, lanes), F32)] * 3
        + [
            pltpu.VMEM((groups, 3, width, lanes), BF16), pltpu.VMEM((groups, rows, lanes), BF16),
            dma((groups, ring)), dma((groups, batch)), dma((groups,)), dma((groups, 3)),
        ]
        + reducer_scratch(MLP_LEVELS, shapes, teams, ring),
        compiler_params=pltpu.CompilerParams(
            collective_id=2, has_side_effects=True, vmem_limit_bytes=60 * MIB
        ),
        cost_estimate=pl.CostEstimate(
            flops=24 * rows * width * width + 8 * rows * rows * width,
            bytes_accessed=16 * width * width + 8 * rows * width,
            transcendentals=HEADS * rows * rows // 2,
        ),
        name="attend",
    )(order, x, g, norms, bias_q, *tables, weights, weights, weights, weights, up, down)


def rotary_tables(length):
    half = ROT // 2
    frequency = ROPE_BASE ** (-(np.arange(half) * 2.0 / ROT))
    angle = np.arange(length)[:, None] * frequency[None, :]
    cosine, sine = np.cos(angle), np.sin(angle)
    rest = np.zeros((length, HD - ROT))
    none = np.zeros_like(sine)
    cos_full = np.concatenate([cosine, cosine, rest + 1.0], axis=1)
    low = np.concatenate([-sine, none, rest], axis=1)
    high = np.concatenate([none, sine, rest], axis=1)
    return tuple(jnp.asarray(np.tile(t, (1, 2)).astype(np.float32)) for t in (cos_full, low, high))


def adamw(weight, grad, first, second, rate, decay):
    first_new = BETA_ONE * first + (1.0 - BETA_ONE) * grad
    second_new = BETA_TWO * second + (1.0 - BETA_TWO) * grad * grad
    first_hat = first_new / (1.0 - BETA_ONE**STEP)
    second_hat = second_new / (1.0 - BETA_TWO**STEP)
    weight_new = weight - rate * (first_hat / (jnp.sqrt(second_hat) + EPS_ADAM) + decay * weight)
    return (first_new, second_new, weight_new)


RATES = (0.1, 0.6, 0.1, 0.05)


def finish_kernel(*refs):
    x_ref, g_ref, attend_ref, feed_ref, h_ref, back_ref, bias_ref, norm_grad = refs[:8]
    norm, norm_first, norm_second = refs[8:11]
    inputs, outputs = refs[11:27], refs[27:]
    layer_out, input_grad = outputs[:2]
    for n, rate in enumerate(RATES):
        weight, grad, first, second = (ref[...] for ref in inputs[4 * n : 4 * n + 4])
        new = adamw(weight, grad.astype(F32), first, second, rate, DECAY)
        for ref, value in zip(outputs[2 + 3 * n : 5 + 3 * n], new):
            ref[...] = value
    width = x_ref.shape[1]
    bias = bias_ref[0:1, width : 2 * width] + bias_ref[0:1, bias_ref.shape[1] - width :]
    rows = x_ref[...].astype(F32)
    layer_out[...] = (rows + attend_ref[...] + feed_ref[...] + bias).astype(BF16)
    xh, scale = normalized(rows)
    h = back_ref[...].astype(F32) + h_ref[...]
    inner = jnp.mean(h * xh, axis=-1, keepdims=True)
    input_grad[...] = g_ref[...].astype(F32) + scale * (h - jnp.mean(h, axis=-1, keepdims=True) - xh * inner)

    @pl.when(pl.program_id(0) == 0)
    def _():
        grad = norm_grad[0:4, : norm.shape[1]]
        first, second, new = adamw(norm[...], grad, norm_first[...], norm_second[...], 0.6, 0.0)
        outputs[14][...] = first
        outputs[15][...] = second[0:2]
        outputs[16][...] = second[2:4]
        outputs[17][...] = new


def finish(rows, biases, norm_grad, norm_args, weights):
    steps = 4
    whole = lambda v: pl.BlockSpec(v.shape, lambda i: (0,) * len(v.shape))
    part = lambda v: pl.BlockSpec((v.shape[0] // steps, v.shape[1]), lambda i: (i, 0))
    like = lambda v, dtype: jax.ShapeDtypeStruct(v.shape, dtype)
    count, width = rows[0].shape
    args = [*rows, biases, norm_grad, *norm_args] + [v for group in weights for v in group]
    specs = [part(v) for v in rows] + [whole(v) for v in (biases, norm_grad, *norm_args)]
    specs += [part(v) for group in weights for v in group]
    outs = [like(rows[0], BF16), like(rows[0], F32)] + [like(group[0], F32) for group in weights for _ in range(3)]
    out_specs = [part(v) for v in outs]
    own = norm_args[0].shape[1]
    norm_outs = [jax.ShapeDtypeStruct((n, own), F32) for n in (4, 2, 2, 4)]
    return pl.pallas_call(
        finish_kernel,
        grid=(steps,),
        in_specs=specs,
        out_specs=out_specs + [whole(v) for v in norm_outs],
        out_shape=outs + norm_outs,
        compiler_params=pltpu.CompilerParams(vmem_limit_bytes=56 * MIB),
        cost_estimate=pl.CostEstimate(flops=0, bytes_accessed=64 * MIB, transcendentals=0),
        name="finish",
    )(*args)


def shards(
    tokens, out_grad, block_order, qkv_weight, out_weight, up_weight, down_weight, norm_params, bias_params,
    qkv_first, qkv_second, out_first, out_second, up_first, up_second, down_first, down_second,
    norm_first, norm_second, bias_first, bias_second,
):
    groups, ring = lax.axis_size("dp"), lax.axis_size("ctx")
    group, rank = lax.axis_index("dp"), lax.axis_index("ctx")
    batch, piece, width = tokens.shape
    length = piece * ring
    count = batch * piece
    ff = up_weight.shape[1]

    share = bias_params.shape[0]
    lanes = share + -share % 128
    small = jnp.concatenate([
        jnp.pad(bias_params[None, :], ((0, 0), (0, lanes - share))),
        jnp.pad(norm_params, ((0, 3), (0, lanes - norm_params.shape[1]))),
    ])
    x_rows, g_rows = tokens.reshape(count, width), out_grad.reshape(count, width)
    att_copy, biases, norms, home_x, home_g, feed_out, h_feed, dup, ddown, dbias_up, small_feed = gather_feed(
        up_weight, down_weight, qkv_weight, out_weight, small, x_rows, g_rows, piece, ring * share
    )

    odd = group % 2

    order = block_order[jnp.clip(rank - odd, 0, batch - 1)]
    spots = jnp.arange(order.shape[0])
    order = jnp.stack([order, jnp.sum(jnp.where(order[None, :] == spots[:, None], spots[None, :], 0), axis=1)])

    h_attend, dqkv, small_attend, o_last, o_first, up_slice, down_slice = attend(
        order, home_x, home_g, norms, biases, rotary_tables(length), att_copy, dup, ddown, batch
    )
    *owned, norm_grad, bias_grad, attend_out, ret_back = reduce_all(
        up_slice, down_slice, dqkv, small_attend, small_feed, dbias_up, h_attend, o_last, o_first, g_rows, att_copy, batch
    )
    up_grad, down_grad, qkv_grad, out_grads = (
        g.reshape(w.shape) for g, w in zip(owned, (up_weight, down_weight, qkv_weight, out_weight))
    )
    layer_out, input_grad, *new, norm_a, norm_b, norm_c, norm_d = finish(
        (x_rows, g_rows, attend_out, feed_out, h_feed, ret_back.reshape(count, width)),
        biases,
        norm_grad,
        (norm_params, norm_first, norm_second),
        (
            (qkv_weight, qkv_grad, qkv_first, qkv_second),
            (out_weight, out_grads, out_first, out_second),
            (up_weight, up_grad, up_first, up_second),
            (down_weight, down_grad, down_first, down_second),
        ),
    )
    bias_new = adamw(bias_params, bias_grad[0, :share], bias_first, bias_second, 0.6, 0.0)
    return (
        layer_out.reshape(tokens.shape), input_grad.reshape(tokens.shape), *new,
        norm_a, norm_b, norm_c, norm_d, *bias_new,
    )


def solution(mesh):
    rows, columns, token = P("ctx", None), P(None, "ctx"), P("dp", "ctx", None)
    in_specs = (token, token, P("dp", None)) + (rows,) * 4 + (columns, P("ctx")) + (rows,) * 8
    in_specs += (columns, columns, P("ctx"), P("ctx"))
    out_specs = (token, token) + (rows,) * 12 + (columns,) * 4 + (P("ctx"),) * 3
    return jax.shard_map(shards, mesh=mesh, in_specs=in_specs, out_specs=out_specs, check_vma=False)
```
